32 devices in a mesh: blk: 32 (over z, y, x, core).
Axes of the slice: x: 2, y: 2, z: 4, core: 2. Of those that a mesh axis runs over, the one named last changes fastest.
Arguments:
- images: bfloat16 [12800, 768], P('blk'), may hold values from -6 to 6
- captions: bfloat16 [20480, 768], P('blk'), may hold values from -6 to 6
- img_gain1: bfloat16 [768], replicated, may hold values from 0.5 to 1.5
- img_bias1: bfloat16 [768], replicated, may hold values from -3 to 3
- img_qkv: bfloat16 [1769472], P('blk'), may hold values from -0.21875 to 0.21875
- img_out: bfloat16 [589824], P('blk'), may hold values from -0.5 to 0.5
- img_gain2: bfloat16 [768], replicated, may hold values from 0.5 to 1.5
- img_bias2: bfloat16 [768], replicated, may hold values from -3 to 3
- img_up: bfloat16 [2359296], P('blk'), may hold values from -0.21875 to 0.21875
- img_down: bfloat16 [2359296], P('blk'), may hold values from -0.109375 to 0.109375
- txt_gain1: float32 [768], replicated, may hold values from 0.5 to 1.5
- txt_bias1: float32 [768], replicated, may hold values from -3 to 3
- txt_qkv: bfloat16 [768, 2304], replicated, may hold values from -0.21875 to 0.21875
- txt_out: bfloat16 [768, 768], replicated, may hold values from -0.4375 to 0.4375
- txt_gain2: float32 [768], replicated, may hold values from 0.5 to 1.5
- txt_bias2: float32 [768], replicated, may hold values from -3 to 3
- txt_up: bfloat16 [768, 3072], replicated, may hold values from -0.21875 to 0.21875
- txt_down: bfloat16 [3072, 768], replicated, may hold values from -0.109375 to 0.109375
- counts: int32 [256], P('blk'), may hold values from 1 to 5, as said below
- matches: int32 [1280, 256], P('blk'), may hold values 0 or 1
Outputs:
- loss: float32 [], replicated
- caption_grad: float32 [20480, 768], P('blk')
- grad_gain1: float32 [768], replicated
- grad_bias1: float32 [768], replicated
- grad_qkv: float32 [1769472], P('blk')
- grad_out: float32 [589824], P('blk')
- grad_gain2: float32 [768], replicated
- grad_bias2: float32 [768], replicated
- grad_up: float32 [2359296], P('blk')
- grad_down: float32 [2359296], P('blk')
The draws below stay inside these ranges and needn't reach their ends.
Inputs may be any that keep to these rules, and one draw needn't show every extreme that they name: `counts`: each image has 1 to 5 captions; in every draw all 8 images of one block have 5, so that block's 40 caption slots are all live.
All inputs are finite; a program needn't handle non-finite values. No bound on the sum of `matches` on one device may be relied on, other than what follows from the above.
Results may differ from the reference program's by a relative error of at most 0.015.
Values may be sent and summed in bfloat16 or wider, within the bound.
No kernel may reach another device: no remote copies, remote signals or barrier semaphores. Data moves between devices by JAX's collectives and lax.ppermute only.
A program may use at most 192 MiB of HBM per device.

```python
import jax
import jax.numpy as jnp
from jax import lax

D = 768
FF = 3072
HEAD = 64
IMG_LEN = 50
TXT_LEN = 16
IMG_DEV = 8
CAP_DEV = 40
IMAGES = 256
CAPTIONS = 1280
N_BLK = 32


def draw_counts(key, part):
    key = jax.random.fold_in(key, 7)
    first_key, second_key = jax.random.split(key)
    base_counts = jax.random.randint(first_key, (IMAGES,), 1, 6)
    chosen = jax.random.randint(second_key, (), 0, IMAGES // IMG_DEV)
    device_ids = jnp.arange(IMAGES) // IMG_DEV
    return jnp.where(device_ids == chosen, 5, base_counts).astype(jnp.int32)


def with_ends(drawn, own_key, least, high):
    longest = drawn.shape.index(max(drawn.shape))
    spots = []
    for shift in (0, 1):
        where = [jax.random.randint(jax.random.fold_in(own_key, axis), (), 0, length) for axis, length in enumerate(drawn.shape)]
        where[longest] = (where[longest] + shift) % drawn.shape[longest]
        spots.append(tuple(where))
    return drawn.at[spots[0]].set(least).at[spots[1]].set(high)


def block_levels(own_key, dims, shards, smallest, largest):
    level, own = 1.0, jax.random.fold_in(own_key, 6)
    for dim, shards_of in shards:
        steps = jnp.exp(jax.random.uniform(jax.random.fold_in(own, dim), (shards_of,), jnp.float32, smallest / len(shards), largest / len(shards)))
        level = level * jnp.repeat(steps, dims[dim] // shards_of).reshape([-1 if axis == dim else 1 for axis in range(len(dims))])
    return level


def scatter_about(own_key, shape, spread, bound, cuts=(), held_as=jnp.bfloat16):
    values = jax.random.normal(own_key, shape, jnp.float32) * spread
    if len(cuts) > 0:
        values = block_levels(own_key, shape, cuts, -0.22, 0.18) * values
    return jnp.clip(values, min=-bound, max=bound).astype(held_as)


def setup_inputs(seed: int = 0) -> dict:
    keys = jax.random.split(jax.random.key(seed), 21)
    return {
        "images": scatter_about(keys[0], (IMAGES * IMG_LEN, D), 1.0, 6.0, ((0, 32),)),
        "captions": scatter_about(keys[1], (CAPTIONS * TXT_LEN, D), 1.0, 6.0, ((0, 32),)),
        "img_gain1": jnp.clip(1.0 + 0.1 * jax.random.normal(keys[2], (D,), jnp.float32), 0.5, 1.5).astype(jnp.bfloat16),
        "img_bias1": scatter_about(keys[3], (D,), 0.5, 3.0),
        "img_qkv": scatter_about(keys[4], (3 * D * D,), D ** -0.5, 0.21875, ((0, 32),)),
        "img_out": scatter_about(keys[5], (D * D,), (D // 7) ** -0.5, 0.5, ((0, 32),)),
        "img_gain2": jnp.clip(1.0 + 0.1 * jax.random.normal(keys[6], (D,), jnp.float32), 0.5, 1.5).astype(jnp.bfloat16),
        "img_bias2": scatter_about(keys[7], (D,), 0.5, 3.0),
        "img_up": scatter_about(keys[8], (D * FF,), D ** -0.5, 0.21875, ((0, 32),)),
        "img_down": scatter_about(keys[9], (FF * D,), FF ** -0.5, 0.109375, ((0, 32),)),
        "txt_gain1": jnp.clip(1.0 + 0.1 * jax.random.normal(keys[10], (D,), jnp.float32), 0.5, 1.5),
        "txt_bias1": scatter_about(keys[11], (D,), 0.5, 3.0, (), jnp.float32),
        "txt_qkv": scatter_about(keys[12], (D, 3 * D), D ** -0.5, 0.21875),
        "txt_out": scatter_about(keys[13], (D, D), (D // 4) ** -0.5, 0.4375),
        "txt_gain2": jnp.clip(1.0 + 0.1 * jax.random.normal(keys[14], (D,), jnp.float32), 0.5, 1.5),
        "txt_bias2": scatter_about(keys[15], (D,), 0.5, 3.0, (), jnp.float32),
        "txt_up": scatter_about(keys[16], (D, FF), D ** -0.5, 0.21875),
        "txt_down": scatter_about(keys[17], (FF, D), FF ** -0.5, 0.109375),
        "counts": draw_counts(jax.random.fold_in(keys[20], 71), 0),
        "matches": with_ends((jax.random.randint(keys[19], (CAPTIONS, IMAGES), 0, IMAGES) < 2).astype(jnp.int32), jax.random.fold_in(keys[19], 1), 0, 1),
    }


@jax.custom_vjp
def low(v):
    return lax.optimization_barrier(v.astype(jnp.bfloat16)).astype(jnp.float32)

@jax.custom_vjp
def low_back(v):
    return v

def low_keep(v):
    return (low(v), None)

def low_pass(kept, grad):
    return (grad,)

def back_keep(v):
    return (v, None)

def back_low(kept, grad):
    return (low(grad),)
low.defvjp(low_keep, low_pass)
low_back.defvjp(back_keep, back_low)
norm_eps = 1e-06
logit_scale = 50.0
highest = lax.Precision.HIGHEST

def layer_norm(values, norm_gain, norm_bias):
    average = lax.optimization_barrier(jnp.mean(values, axis=-1, keepdims=True))
    centred = values - average
    variance = lax.optimization_barrier(jnp.mean(centred * centred, axis=-1, keepdims=True))
    return centred * lax.rsqrt(variance + norm_eps) * norm_gain + norm_bias

def block_forward(values, norm_gain1, norm_bias1, w_qkv, w_out, norm_gain2, norm_bias2, w_up, w_down, seq_len):
    row_total = values.shape[0]
    model_width = values.shape[1]
    seq_count = row_total // seq_len
    head_count = model_width // HEAD
    normed = low(layer_norm(values, norm_gain1, norm_bias1))
    project = low_back(low(jnp.dot(normed, w_qkv, precision=highest)))
    heads_split = project.reshape(seq_count, seq_len, 3, head_count, HEAD)
    queries = heads_split[:, :, 0]
    key_part = heads_split[:, :, 1]
    val_part = heads_split[:, :, 2]
    scores = low_back(HEAD ** (-0.5) * jnp.einsum('cqhe,ckhe->chqk', queries, key_part, precision=highest))
    soft_probs = low(jax.nn.softmax(scores, axis=-1))
    attended = jnp.einsum('chqk,ckhe->cqhe', soft_probs, val_part, precision=highest).reshape(row_total, model_width)
    attended = low_back(low(attended))
    middle = values + low_back(jnp.dot(attended, w_out, precision=highest))
    normed_two = low(layer_norm(middle, norm_gain2, norm_bias2))
    pre_act = low_back(jnp.dot(normed_two, w_up, precision=highest))
    activated = low(jax.nn.gelu(pre_act, approximate=False))
    return middle + low_back(jnp.dot(activated, w_down, precision=highest))

def embed(output_rows, seq_len):
    model_width = output_rows.shape[1]
    pooled = lax.optimization_barrier(jnp.mean(output_rows.reshape(-1, seq_len, model_width), axis=1))
    return low(pooled * lax.rsqrt(lax.optimization_barrier(jnp.sum(pooled * pooled, axis=-1, keepdims=True)) + norm_eps))

def reference(images, captions, img_gain1, img_bias1, img_qkv, img_out, img_gain2, img_bias2, img_up, img_down, txt_gain1, txt_bias1, txt_qkv, txt_out, txt_gain2, txt_bias2, txt_up, txt_down, counts, matches):
    image_params = (img_gain1.astype(jnp.float32), img_bias1.astype(jnp.float32), img_qkv.astype(jnp.float32).reshape(D, 3 * D), img_out.astype(jnp.float32).reshape(D, D), img_gain2.astype(jnp.float32), img_bias2.astype(jnp.float32), img_up.astype(jnp.float32).reshape(D, FF), img_down.astype(jnp.float32).reshape(FF, D))
    image_rows = images.astype(jnp.float32).reshape(N_BLK, IMG_DEV * IMG_LEN, D)

    def image_step(row_block):
        return embed(block_forward(row_block, *image_params, IMG_LEN), IMG_LEN)
    image_embed = lax.map(image_step, image_rows).reshape(IMAGES, D)
    block_counts = counts.reshape(N_BLK, IMG_DEV)
    ends_at = jnp.cumsum(block_counts, axis=1).astype(jnp.int32)
    slot_ids = jnp.arange(CAP_DEV, dtype=jnp.int32)
    owner_local = lax.optimization_barrier(jnp.sum((ends_at[:, None, :] <= slot_ids[None, :, None]).astype(jnp.int32), axis=2))
    live_mask = (slot_ids[None, :] < ends_at[:, -1:]).astype(jnp.float32).reshape(CAPTIONS)
    owner_ids = (owner_local + jnp.arange(N_BLK, dtype=jnp.int32)[:, None] * IMG_DEV).reshape(CAPTIONS)
    columns = jnp.arange(IMAGES, dtype=jnp.int32)
    positive = jnp.where((matches > 0) | (owner_ids[:, None] == columns[None, :]), 1.0, 0.0).astype(jnp.float32) * live_mask[:, None]

    def loss_of(caption_rows, norm_gain1, norm_bias1, w_qkv, w_out, norm_gain2, norm_bias2, w_up, w_down):
        grouped = caption_rows.reshape(N_BLK, CAP_DEV * TXT_LEN, D)

        def text_step(row_block):
            return embed(block_forward(row_block, norm_gain1, norm_bias1, w_qkv, w_out, norm_gain2, norm_bias2, w_up, w_down, TXT_LEN), TXT_LEN)
        text_embed = lax.map(jax.checkpoint(text_step), grouped).reshape(CAPTIONS, D)
        similar = low_back(logit_scale * jnp.dot(text_embed, image_embed.T, precision=highest))
        shifted = jnp.exp(similar - logit_scale)
        row_lse = logit_scale + jnp.log(lax.optimization_barrier(jnp.sum(shifted, axis=1)))
        row_count = jnp.maximum(lax.optimization_barrier(jnp.sum(positive, axis=1)), 1.0)
        cap_term = live_mask * (row_lse - lax.optimization_barrier(jnp.sum(positive * similar, axis=1)) / row_count)
        col_lse = logit_scale + jnp.log(lax.optimization_barrier(jnp.sum(live_mask[:, None] * shifted, axis=0)))
        col_count = lax.optimization_barrier(jnp.sum(positive, axis=0))
        img_term = col_lse - lax.optimization_barrier(jnp.sum(positive * similar, axis=0)) / col_count
        return 0.5 * jnp.sum(cap_term) / jnp.sum(live_mask) + 0.5 * jnp.mean(img_term)
    text_params = tuple((item.astype(jnp.float32) for item in (txt_gain1, txt_bias1, txt_qkv, txt_out, txt_gain2, txt_bias2, txt_up, txt_down)))
    loss_value, pull_back = jax.vjp(loss_of, captions.astype(jnp.float32), *text_params)
    grads = pull_back(jnp.ones_like(loss_value))
    return (loss_value, grads[0], grads[1], grads[2], grads[3].reshape(-1), grads[4].reshape(-1), grads[5], grads[6], grads[7].reshape(-1), grads[8].reshape(-1))
```

```python
import jax
import jax.numpy as jnp
from jax import lax
from jax.sharding import PartitionSpec as P

D = 768
FF = 3072
HEAD = 64
HEADS = D // HEAD
IMG_LEN = 50
TXT_LEN = 16
AXIS = "blk"

norm_eps = 1e-06
logit_scale = 50.0
f32 = jnp.float32
bf16 = jnp.bfloat16


def swapped(value, mask):
    peers = lax.axis_size(AXIS)
    return lax.ppermute(value, AXIS, [(i, i ^ mask) for i in range(peers)])


def bit_masks():
    peers = lax.axis_size(AXIS)
    return [1 << k for k in range(peers.bit_length() - 1)]


def gathered(block):
    own = lax.axis_index(AXIS)
    held = block[None]
    for mask in reversed(bit_masks()):
        other = swapped(held, mask)
        upper = (own & mask) > 0
        first = jnp.where(upper, other, held)
        second = jnp.where(upper, held, other)
        held = jnp.stack([first, second], axis=1).reshape((-1,) + block.shape)
    return held


def spread(block):
    peers = lax.axis_size(AXIS)
    copies = jnp.broadcast_to(block[None], (peers,) + block.shape)
    return lax.all_to_all(copies, AXIS, split_axis=0, concat_axis=0, tiled=True)


def stage_orders():
    masks = bit_masks()
    head, tail = masks[:-2], masks[-2:]
    order_a = list(head)
    order_b = list(head)
    for k in range(1, len(head) - 1, 2):
        order_b[k], order_b[k + 1] = order_b[k + 1], order_b[k]
    return order_a, order_b, tail


def row_order(order, tail):
    peers = lax.axis_size(AXIS)
    own = lax.axis_index(AXIS)
    per = D // peers
    bits = list(order) + list(reversed(tail))
    places = lax.iota(jnp.int32, D)
    block = places // per
    target = jnp.zeros_like(block) + own
    for k, mask in enumerate(bits):
        target = target ^ (((block >> (len(bits) - 1 - k)) & 1) * mask)
    source = target * per + places % per
    return (lax.iota(jnp.int32, D)[:, None] == source[None, :]).astype(bf16)


def scattered(part_a, part_b):
    order_a, order_b, tail = stage_orders()
    for mask_a, mask_b in zip(order_a, order_b):
        half = part_a.shape[0] // 2
        got_a = swapped(part_a[half:], mask_a)
        got_b = swapped(part_b[half:], mask_b)
        part_a = (part_a[:half].astype(f32) + got_a.astype(f32)).astype(bf16)
        part_b = (part_b[:half].astype(f32) + got_b.astype(f32)).astype(bf16)
    both = jnp.concatenate([part_a, part_b], axis=1)
    rows = both.shape[0] // 4
    low, high = tail
    total = both[:rows].astype(f32)
    for k, mask in ((1, low), (2, high), (3, low | high)):
        total = total + swapped(both[k * rows : (k + 1) * rows], mask).astype(f32)
    return total


def norm_parts(values):
    average = jnp.mean(values, axis=-1, keepdims=True)
    centred = values - average
    variance = jnp.mean(centred * centred, axis=-1, keepdims=True)
    scale = lax.rsqrt(variance + norm_eps)
    return centred * scale, scale


def norm_back(unit, scale, gain, grad):
    inner = grad * gain
    shift = jnp.mean(inner, axis=-1, keepdims=True)
    along = jnp.mean(inner * unit, axis=-1, keepdims=True)
    return scale * (inner - shift - unit * along)


def attention(project, seq_len):
    rows = project.shape[0]
    split = project.reshape(rows // seq_len, seq_len, 3, HEADS, HEAD)
    queries, keys, vals = split[:, :, 0], split[:, :, 1], split[:, :, 2]
    scores = jnp.einsum("cqhe,ckhe->chqk", queries, keys, preferred_element_type=f32)
    probs = jax.nn.softmax(scores * HEAD ** (-0.5), axis=-1)
    mixed = jnp.einsum("chqk,ckhe->cqhe", probs.astype(bf16), vals, preferred_element_type=f32)
    return queries, keys, vals, probs, mixed.reshape(rows, D).astype(bf16)


def pooled_down(summed, seq_len, weight_parts):
    mean = summed * (1.0 / seq_len)
    high = mean.astype(bf16)
    low = (mean - high.astype(f32)).astype(bf16)
    out = 0.0
    for k, weight in weight_parts:
        out = out + jnp.dot(high[:, k], weight, preferred_element_type=f32)
        out = out + jnp.dot(low[:, k], weight, preferred_element_type=f32)
    return out


def local(
    images,
    captions,
    img_gain1,
    img_bias1,
    img_qkv,
    img_out,
    img_gain2,
    img_bias2,
    img_up,
    img_down,
    txt_gain1,
    txt_bias1,
    txt_qkv,
    txt_out,
    txt_gain2,
    txt_bias2,
    txt_up,
    txt_down,
    counts,
    matches,
):
    peers = lax.axis_size(AXIS)
    own = lax.axis_index(AXIS)
    per = D // peers
    img_local = counts.shape[0]
    cap_local = matches.shape[0]
    total_images = matches.shape[1]

    shard = jnp.concatenate(
        [
            img_qkv.reshape(per, 3 * D),
            img_out.reshape(per, D),
            img_up.reshape(per, FF),
            img_down.reshape(per, FF),
        ],
        axis=1,
    )
    whole = lax.all_gather(shard, AXIS, axis=0, tiled=True)

    rows_in = captions.astype(f32)
    unit1, scale1 = norm_parts(rows_in)
    normed1 = (unit1 * txt_gain1 + txt_bias1).astype(bf16)
    project = jnp.dot(normed1, txt_qkv, preferred_element_type=f32).astype(bf16)
    queries, keys, vals, probs, attended = attention(project, TXT_LEN)
    middle = rows_in + jnp.dot(attended, txt_out, preferred_element_type=f32)
    unit2, scale2 = norm_parts(middle)
    normed2 = (unit2 * txt_gain2 + txt_bias2).astype(bf16)
    inner = jnp.dot(normed2, txt_up, preferred_element_type=f32)
    half_erf = 0.5 * (1.0 + lax.erf(inner * (0.5**0.5)))
    hidden = (inner * half_erf).astype(bf16)
    slope = (half_erf + inner * jnp.exp(-0.5 * inner * inner) * 0.3989422804014327).astype(bf16)
    hidden_sum = jnp.sum(hidden.astype(f32).reshape(cap_local, TXT_LEN, FF), axis=1)
    pooled = jnp.mean(middle.reshape(cap_local, TXT_LEN, D), axis=1) + pooled_down(
        hidden_sum, TXT_LEN, [(slice(None), txt_down)]
    )
    inverse = lax.rsqrt(jnp.sum(pooled * pooled, axis=-1, keepdims=True) + norm_eps)
    text_unit = pooled * inverse
    text_low = text_unit.astype(bf16)

    ends_at = jnp.cumsum(counts)
    slot_ids = lax.iota(jnp.int32, cap_local)
    owner = jnp.sum((ends_at[None, :] <= slot_ids[:, None]).astype(jnp.int32), axis=1)
    owner = owner + own * img_local
    live = slot_ids < ends_at[-1]
    columns = lax.iota(jnp.int32, total_images)
    positive = ((matches > 0) | (owner[:, None] == columns[None, :])) & live[:, None]

    own_pack = jnp.concatenate([text_low, positive.astype(bf16)], axis=1)
    small = peers * cap_local * total_images <= 1 << 20
    if small:
        text_pack = gathered(own_pack).reshape(-1, D + total_images)
        hidden_cols = lax.all_to_all(
            (hidden_sum * inverse).astype(bf16), AXIS, split_axis=1, concat_axis=0, tiled=True
        )

    img_rows = images.astype(f32)
    unit, _ = norm_parts(img_rows)
    normed = (unit * img_gain1.astype(f32) + img_bias1.astype(f32)).astype(bf16)
    project_img = jnp.dot(normed, whole[:, : 3 * D], preferred_element_type=f32).astype(bf16)
    attended_img = attention(project_img, IMG_LEN)[-1]
    middle_img = img_rows + jnp.dot(
        attended_img, whole[:, 3 * D : 4 * D], preferred_element_type=f32
    )
    unit, _ = norm_parts(middle_img)
    normed = (unit * img_gain2.astype(f32) + img_bias2.astype(f32)).astype(bf16)
    inner_img = jnp.dot(normed, whole[:, 4 * D : 4 * D + FF], preferred_element_type=f32)
    hidden_img = (inner_img * (0.5 * (1.0 + lax.erf(inner_img * (0.5**0.5))))).astype(bf16)
    sum_img = jnp.sum(hidden_img.astype(f32).reshape(img_local, IMG_LEN, FF), axis=1)
    fold = FF // D
    sum_img = sum_img.reshape(img_local, D, fold).transpose(0, 2, 1).reshape(img_local, FF)
    pooled_img = jnp.mean(middle_img.reshape(img_local, IMG_LEN, D), axis=1) + pooled_down(
        sum_img,
        IMG_LEN,
        [
            (slice(k * D, (k + 1) * D), whole[:, 4 * D + FF + k * D : 4 * D + FF + (k + 1) * D])
            for k in range(fold)
        ],
    )
    image_low = (
        pooled_img * lax.rsqrt(jnp.sum(pooled_img * pooled_img, axis=-1, keepdims=True) + norm_eps)
    ).astype(bf16)
    image_all = spread(image_low).reshape(total_images, D)

    def similarities(text_rows):
        return logit_scale * lax.dot_general(
            text_rows, image_all, (((1,), (1,)), ((), ())), preferred_element_type=f32
        )

    def first_pass(pack):
        similar = similarities(pack[:, :D])
        pos = pack[:, D:].astype(f32)
        alive = jnp.max(pos, axis=1, keepdims=True)
        shifted = jnp.exp(similar - logit_scale)
        row_sum = jnp.sum(shifted, axis=1, keepdims=True)
        row_count = jnp.maximum(jnp.sum(pos, axis=1, keepdims=True), 1.0)
        pos_similar = pos * similar
        cap_term = alive * (
            logit_scale + jnp.log(row_sum) - jnp.sum(pos_similar, axis=1, keepdims=True) / row_count
        )
        return (
            jnp.sum(alive * shifted, axis=0, keepdims=True),
            jnp.sum(pos, axis=0, keepdims=True),
            jnp.sum(pos_similar, axis=0, keepdims=True),
            jnp.sum(cap_term),
            jnp.sum(alive),
        )

    sums = first_pass(text_pack) if small else lax.psum(first_pass(own_pack), AXIS)
    col_sum, col_count, col_pos, cap_total, live_total = sums
    img_term = logit_scale + jnp.log(col_sum) - col_pos / col_count
    loss_value = 0.5 * cap_total / live_total + 0.5 * jnp.mean(img_term)
    cap_share, img_share = 0.5 / live_total, 0.5 / total_images

    def second_pass(pack):
        shifted = jnp.exp(similarities(pack[:, :D]) - logit_scale)
        pos = pack[:, D:].astype(f32)
        alive = jnp.max(pos, axis=1, keepdims=True)
        row_sum = jnp.sum(shifted, axis=1, keepdims=True)
        row_count = jnp.maximum(jnp.sum(pos, axis=1, keepdims=True), 1.0)
        grad_sims = (
            alive * shifted * (cap_share / row_sum + img_share / col_sum)
            - pos * (cap_share / row_count + img_share / col_count)
        ).astype(bf16)
        return jnp.dot(grad_sims, image_all, preferred_element_type=f32) * logit_scale

    own_grad = second_pass(own_pack)
    grad_pool = inverse * (
        own_grad - text_unit * jnp.sum(own_grad * text_unit, axis=-1, keepdims=True)
    )
    grad_row = grad_pool * (1.0 / TXT_LEN)
    grad_hidden = lax.dot_general(
        grad_row.astype(bf16), txt_down, (((1,), (1,)), ((), ())), preferred_element_type=f32
    )
    grad_inner = (
        (grad_hidden[:, None, :] * slope.astype(f32).reshape(cap_local, TXT_LEN, FF))
        .astype(bf16)
        .reshape(cap_local * TXT_LEN, FF)
    )
    if small:
        grad_all, text_all = second_pass(text_pack), text_pack[:, :D].astype(f32)
        along = jnp.sum(grad_all * text_all, axis=-1, keepdims=True)
        turned = ((grad_all - text_all * along) * (1.0 / TXT_LEN)).astype(bf16)
        grad_down = lax.dot_general(
            hidden_cols, turned, (((0,), (0,)), ((), ())), preferred_element_type=f32
        )
    else:
        grad_down = lax.psum_scatter(
            lax.dot_general(
                hidden_sum.astype(bf16),
                grad_row.astype(bf16),
                (((0,), (0,)), ((), ())),
                preferred_element_type=f32,
            ),
            AXIS,
            scatter_dimension=0,
            tiled=True,
        )
    order_a, order_b, tail = stage_orders()
    perm_a, perm_b = row_order(order_a, tail), row_order(order_b, tail)

    def weight_grad(lhs, rhs):
        return lax.dot_general(
            lhs, rhs, (((0,), (0,)), ((), ())), preferred_element_type=f32
        ).astype(bf16)

    def placed(values, perm):
        return jnp.dot(values, perm, preferred_element_type=f32).astype(bf16)

    up_share = scattered(
        weight_grad(placed(normed2, perm_a), grad_inner[:, : FF // 2]),
        weight_grad(placed(normed2, perm_b), grad_inner[:, FF // 2 :]),
    )
    grad_normed2 = lax.dot_general(
        grad_inner, txt_up, (((1,), (1,)), ((), ())), preferred_element_type=f32
    )
    gain_two = jnp.sum(grad_normed2 * unit2, axis=0)
    bias_two = jnp.sum(grad_normed2, axis=0)
    row_wide = jnp.broadcast_to(grad_row[:, None, :], (cap_local, TXT_LEN, D)).reshape(-1, D)
    grad_middle = row_wide + norm_back(unit2, scale2, txt_gain2, grad_normed2)
    grad_branch = grad_middle.astype(bf16)
    grad_out = weight_grad(placed(attended, perm_b), grad_branch)
    grad_att = (
        lax.dot_general(
            grad_branch, txt_out, (((1,), (1,)), ((), ())), preferred_element_type=f32
        )
        .astype(bf16)
        .reshape(queries.shape)
    )
    grad_probs = jnp.einsum("cqhe,ckhe->chqk", grad_att, vals, preferred_element_type=f32)
    grad_val = jnp.einsum(
        "chqk,cqhe->ckhe", probs.astype(bf16), grad_att, preferred_element_type=f32
    )
    grad_scores = (
        probs * (grad_probs - jnp.sum(grad_probs * probs, axis=-1, keepdims=True))
    ).astype(bf16)
    grad_query = jnp.einsum("chqk,ckhe->cqhe", grad_scores, keys, preferred_element_type=f32)
    grad_key = jnp.einsum("chqk,cqhe->ckhe", grad_scores, queries, preferred_element_type=f32)
    grad_proj = (
        jnp.stack([grad_query * HEAD ** (-0.5), grad_key * HEAD ** (-0.5), grad_val], axis=2)
        .reshape(cap_local * TXT_LEN, 3 * D)
        .astype(bf16)
    )
    placed1 = placed(normed1, perm_b)
    rest_share = scattered(
        weight_grad(placed(normed1, perm_a), grad_proj[:, : 2 * D]),
        jnp.concatenate([weight_grad(placed1, grad_proj[:, 2 * D :]), grad_out], axis=1),
    )
    grad_normed1 = lax.dot_general(
        grad_proj, txt_qkv, (((1,), (1,)), ((), ())), preferred_element_type=f32
    )
    gain_one = jnp.sum(grad_normed1 * unit1, axis=0)
    bias_one = jnp.sum(grad_normed1, axis=0)
    caption_grad = grad_middle + norm_back(unit1, scale1, txt_gain1, grad_normed1)
    norms = jnp.sum(spread(jnp.stack([gain_one, bias_one, gain_two, bias_two])[None]), axis=0)
    norms = norms.reshape(4, D)
    return (
        loss_value,
        caption_grad,
        norms[0],
        norms[1],
        rest_share[:, : 3 * D].reshape(-1),
        rest_share[:, 3 * D :].reshape(-1),
        norms[2],
        norms[3],
        up_share.reshape(-1),
        grad_down.reshape(-1),
    )


def solution(mesh):
    split, flat, whole = P("blk", None), P("blk"), P()
    image_block = (whole, whole, flat, flat, whole, whole, flat, flat)
    return jax.shard_map(
        local,
        mesh=mesh,
        in_specs=(split, split) + image_block + (whole,) * 8 + (flat, split),
        out_specs=(whole, split, whole, whole, flat, flat, whole, whole, flat, flat),
        check_vma=False,
    )
```

```python
import functools

import jax
import jax.numpy as jnp
from jax import lax
from jax.experimental import pallas as pl
from jax.experimental.pallas import tpu as pltpu
from jax.sharding import PartitionSpec as P

D = 768
FF = 3072
HEAD = 64
HEADS = D // HEAD
IMG_LEN = 50
TXT_LEN = 16
AXIS = "blk"

norm_eps = 1e-06
logit_scale = 50.0
f32 = jnp.float32
bf16 = jnp.bfloat16


def swapped(value, mask):
    peers = lax.axis_size(AXIS)
    return lax.ppermute(value, AXIS, [(i, i ^ mask) for i in range(peers)])


def bit_masks():
    peers = lax.axis_size(AXIS)
    return [1 << k for k in range(peers.bit_length() - 1)]


def gathered(block):
    own = lax.axis_index(AXIS)
    held = block[None]
    for mask in reversed(bit_masks()):
        other = swapped(held, mask)
        upper = (own & mask) > 0
        first = jnp.where(upper, other, held)
        second = jnp.where(upper, held, other)
        held = jnp.stack([first, second], axis=1).reshape((-1,) + block.shape)
    return held


def spread(block):
    peers = lax.axis_size(AXIS)
    copies = jnp.broadcast_to(block[None], (peers,) + block.shape)
    return lax.all_to_all(copies, AXIS, split_axis=0, concat_axis=0, tiled=True)


def stage_orders():
    masks = bit_masks()
    head, tail = masks[:-2], masks[-2:]
    order_a = list(head)
    order_b = list(head)
    for k in range(1, len(head) - 1, 2):
        order_b[k], order_b[k + 1] = order_b[k + 1], order_b[k]
    return order_a, order_b, tail


def row_order(order, tail):
    peers = lax.axis_size(AXIS)
    own = lax.axis_index(AXIS)
    per = D // peers
    bits = list(order) + list(reversed(tail))
    places = lax.iota(jnp.int32, D)
    block = places // per
    target = jnp.zeros_like(block) + own
    for k, mask in enumerate(bits):
        target = target ^ (((block >> (len(bits) - 1 - k)) & 1) * mask)
    source = target * per + places % per
    return (source[:, None] == lax.iota(jnp.int32, D)[None, :]).astype(bf16)


def placed(order, values):
    return mul_bt(order, values).astype(bf16)


def summed_pair(kept, got):
    return (kept.astype(f32) + got.astype(f32)).astype(bf16)


def scattered(keep_a, send_a, keep_b, send_b):
    order_a, order_b, tail = stage_orders()
    for k, (mask_a, mask_b) in enumerate(zip(order_a, order_b)):
        got_a = swapped(send_a, mask_a)
        got_b = swapped(send_b, mask_b)
        half = keep_a.shape[0] // 2
        if k + 1 < len(order_a):
            send_a = summed_pair(keep_a[half:], got_a[half:])
            send_b = summed_pair(keep_b[half:], got_b[half:])
            keep_a = summed_pair(keep_a[:half], got_a[:half])
            keep_b = summed_pair(keep_b[:half], got_b[:half])
        else:
            keep_a, keep_b = summed_pair(keep_a, got_a), summed_pair(keep_b, got_b)
    both = jnp.concatenate([keep_a, keep_b], axis=1)
    rows = both.shape[0] // 4
    low, high = tail
    total = both[:rows].astype(f32)
    for k, mask in ((1, low), (2, high), (3, low | high)):
        total = total + swapped(both[k * rows : (k + 1) * rows], mask).astype(f32)
    return total


VMEM_BYTES = 56 << 20
TILE = 512


def norm_parts(values):
    average = jnp.mean(values, axis=-1, keepdims=True)
    centred = values - average
    variance = jnp.mean(centred * centred, axis=-1, keepdims=True)
    scale = lax.rsqrt(variance + norm_eps)
    return centred * scale, scale


def norm_back(unit, scale, gain, grad):
    inner = grad * gain
    shift = jnp.mean(inner, axis=-1, keepdims=True)
    along = jnp.mean(inner * unit, axis=-1, keepdims=True)
    return scale * (inner - shift - unit * along)


def mul(lhs, rhs):
    return jnp.dot(lhs, rhs, preferred_element_type=f32)


def mul_bt(lhs, rhs):
    return lax.dot_general(lhs, rhs, (((1,), (1,)), ((), ())), preferred_element_type=f32)


def mul_at(lhs, rhs):
    return lax.dot_general(lhs, rhs, (((0,), (0,)), ((), ())), preferred_element_type=f32)


def params(**more):
    return pltpu.CompilerParams(vmem_limit_bytes=VMEM_BYTES, **more)


def cost(flops, moved, transcendentals=0):
    return pl.CostEstimate(flops=flops, bytes_accessed=moved, transcendentals=transcendentals)


def lane_halves(dtype):
    lane = lax.broadcasted_iota(jnp.int32, (1, 2 * HEAD), 1)
    low = jnp.where(lane < HEAD, 1.0, 0.0)
    return low.astype(dtype), (1.0 - low).astype(dtype)


def two_heads(pair):
    low, high = lane_halves(bf16)
    return jnp.concatenate([pair * low, pair * high], axis=0)


def same_sequence(rows, row0, cols, col0, seq_len):
    row = (lax.broadcasted_iota(jnp.int32, (rows, cols), 0) + row0) // seq_len
    col = (lax.broadcasted_iota(jnp.int32, (rows, cols), 1) + col0) // seq_len
    return row == col


def masked_softmax(scores, mask):
    scores = jnp.where(mask, scores, -1e30)
    raised = jnp.exp(scores - jnp.max(scores, axis=-1, keepdims=True))
    return raised * (1.0 / jnp.sum(raised, axis=-1, keepdims=True))


def pair_cols(part, pair):
    start = part * D + pair * 2 * HEAD
    return slice(start, start + 2 * HEAD)


def front_kernel(
    seq_len, windows, ln_rows, x_ref, g1_ref, b1_ref, wqkv_ref, wo_ref, g2_ref, b2_ref, h1_ref,
    qkv_ref, att_ref, mid_ref, h2_ref, sum_ref
):
    rows = x_ref.shape[0]
    gain1, bias1 = g1_ref[...].astype(f32), b1_ref[...].astype(f32)
    gain2, bias2 = g2_ref[...].astype(f32), b2_ref[...].astype(f32)

    @pl.loop(0, rows // ln_rows)
    def _(step):
        at = pl.ds(pl.multiple_of(step * ln_rows, ln_rows), ln_rows)
        unit, _ = norm_parts(x_ref[at, :].astype(f32))
        h1_ref[at, :] = (unit * gain1 + bias1).astype(bf16)

    @pl.loop(0, 3 * D // 256)
    def _(step):
        at = pl.ds(pl.multiple_of(step * 256, 256), 256)
        qkv_ref[:, at] = mul(h1_ref[...], wqkv_ref[:, at]).astype(bf16)

    def attend(q_rows, k_rows, mask):
        for pair in range(HEADS // 2):
            queries = two_heads(qkv_ref[q_rows, pair_cols(0, pair)] * bf16(HEAD ** (-0.5)))
            scores = mul_bt(queries, qkv_ref[k_rows, pair_cols(1, pair)])
            probs = masked_softmax(scores, mask).astype(bf16)
            half = probs.shape[0] // 2
            vals = qkv_ref[k_rows, pair_cols(2, pair)]
            low, high = lane_halves(f32)
            mixed = mul(probs, vals)
            att_ref[q_rows, pair_cols(0, pair)] = (
                mixed[:half] * low + mixed[half:] * high
            ).astype(bf16)

    if len(windows) == 1:
        size = windows[0]
        one = same_sequence(size, 0, size, 0, seq_len)
        mask = jnp.concatenate([one, one], axis=0)

        @pl.loop(0, rows // size)
        def _(step):
            at = pl.ds(pl.multiple_of(step * size, size), size)
            attend(at, at, mask)
    else:
        for row0, count, key0, keys in windows:
            one = same_sequence(count, row0, keys, key0, seq_len)
            attend(pl.ds(row0, count), pl.ds(key0, keys), jnp.concatenate([one, one], axis=0))

    @pl.loop(0, D // 256)
    def _(step):
        at = pl.ds(pl.multiple_of(step * 256, 256), 256)
        mid_ref[:, at] = x_ref[:, at].astype(f32) + mul(att_ref[...], wo_ref[:, at])

    @pl.loop(0, rows // ln_rows)
    def _(step):
        at = pl.ds(pl.multiple_of(step * ln_rows, ln_rows), ln_rows)
        unit, _ = norm_parts(mid_ref[at, :])
        h2_ref[at, :] = (unit * gain2 + bias2).astype(bf16)

    if seq_len % 8 == 0:
        per = ln_rows // seq_len

        @pl.loop(0, rows // ln_rows)
        def _(step):
            values = mid_ref[pl.ds(pl.multiple_of(step * ln_rows, ln_rows), ln_rows), :]
            sum_ref[pl.ds(pl.multiple_of(step * per, per), per), :] = jnp.sum(
                values.reshape(per, seq_len, D), axis=1
            )
    else:
        for k in range(rows // seq_len):
            first, last = k * seq_len, (k + 1) * seq_len
            at8, end8 = first // 8 * 8, -(-last // 8) * 8
            values = mid_ref[at8:end8, :]
            place = lax.broadcasted_iota(jnp.int32, values.shape, 0) + at8
            inside = (place >= first) & (place < last)
            sum_ref[k : k + 1, :] = jnp.sum(
                jnp.where(inside, values, 0.0), axis=0, keepdims=True
            )


def front(seq_len, windows, ln_rows, rows_in, gain1, bias1, wqkv, wo, wo_col, gain2, bias2):
    rows = rows_in.shape[0]
    shapes = [
        ((rows, D), bf16),
        ((rows, 3 * D), bf16),
        ((rows, D), bf16),
        ((rows, D), f32),
        ((rows, D), bf16),
        ((rows // seq_len, D), f32),
    ]
    whole = lambda shape: pl.BlockSpec(shape, lambda i: (0, 0))
    row = whole((1, D))
    return pl.pallas_call(
        functools.partial(front_kernel, seq_len, windows, ln_rows),
        grid=(1,),
        out_shape=[jax.ShapeDtypeStruct(*item) for item in shapes],
        in_specs=[
            whole((rows, D)), row, row, whole((D, 3 * D)),
            pl.BlockSpec((D, D), lambda i: (0, wo_col)), row, row,
        ],
        out_specs=[whole(item[0]) for item in shapes],
        compiler_params=params(),
        cost_estimate=cost(rows * D * D * 8, 14 * D * rows + 8 * D * D, rows * 128 * HEADS),
        name="front",
    )(rows_in, gain1[None], bias1[None], wqkv, wo, gain2[None], bias2[None])


def gelu_parts(inner):
    half = 0.5 * (1.0 + lax.erf(inner * (0.5**0.5)))
    return inner * half, half


def pool_matrix(count, rows, row0, seq_len):
    row = (lax.broadcasted_iota(jnp.int32, (count, rows), 1) + row0) // seq_len
    return jnp.where(row == lax.broadcasted_iota(jnp.int32, (count, rows), 0), 1.0, 0.0).astype(bf16)


def two_terms(mean):
    high = mean.astype(bf16)
    low = (mean - high.astype(f32)).astype(bf16)
    return jnp.concatenate([high, low], axis=0)


def unit_rows(pooled):
    inverse = lax.rsqrt(jnp.sum(pooled * pooled, axis=-1, keepdims=True) + norm_eps)
    return pooled * inverse, inverse


def text_up_kernel(h2_ref, wu_ref, wd_ref, sum_ref, slope_ref, hid_ref, unit_ref, inv_ref, acc):
    step = pl.program_id(0)
    chunk = 128
    per = chunk // TXT_LEN
    pool = pool_matrix(per, chunk, 0, TXT_LEN)
    for k in range(h2_ref.shape[0] // chunk):
        inner = mul(h2_ref[k * chunk : (k + 1) * chunk, :], wu_ref[...])
        value, half = gelu_parts(inner)
        slope = half + inner * (jnp.exp(-0.5 * inner * inner) * 0.3989422804014327)
        slope_ref[k * chunk : (k + 1) * chunk, :] = slope.astype(bf16)
        hid_ref[k * per : (k + 1) * per, :] = mul(pool, value.astype(bf16))
    terms = mul(two_terms(hid_ref[...] * (1.0 / TXT_LEN)), wd_ref[...])
    count = hid_ref.shape[0]
    added = terms[:count] + terms[count:]

    @pl.when(step == 0)
    def _():
        acc[...] = sum_ref[...] * (1.0 / TXT_LEN) + added

    @pl.when(step > 0)
    def _():
        acc[...] += added

    @pl.when(step == pl.num_programs(0) - 1)
    def _():
        unit, inverse = unit_rows(acc[...])
        unit_ref[...] = unit
        inv_ref[...] = jnp.broadcast_to(inverse, inv_ref.shape)


def text_up(normed2, weight_up, weight_down, middle_sum):
    rows, count = normed2.shape[0], middle_sum.shape[0]
    fixed = lambda shape: pl.BlockSpec(shape, lambda i: (0, 0))
    return pl.pallas_call(
        text_up_kernel,
        grid=(FF // TILE,),
        out_shape=[
            jax.ShapeDtypeStruct((rows, FF), bf16),
            jax.ShapeDtypeStruct((count, FF), f32),
            jax.ShapeDtypeStruct((count, D), f32),
            jax.ShapeDtypeStruct((count, 128), f32),
        ],
        in_specs=[
            fixed((rows, D)),
            pl.BlockSpec((D, TILE), lambda i: (0, i)),
            pl.BlockSpec((TILE, D), lambda i: (i, 0)),
            fixed((count, D)),
        ],
        out_specs=[
            pl.BlockSpec((rows, TILE), lambda i: (0, i)),
            pl.BlockSpec((count, TILE), lambda i: (0, i)),
            fixed((count, D)),
            fixed((count, 128)),
        ],
        scratch_shapes=[pltpu.VMEM((count, D), f32)],
        compiler_params=params(),
        cost_estimate=cost(2 * rows * D * FF, 4 * D * FF + 2 * rows * FF, 20 * rows * FF),
        name="text_up",
    )(normed2, weight_up, weight_down, middle_sum)


def image_up_kernel(fold, h2_ref, wu_ref, wd_ref, sum_ref, out_ref, acc):
    step = pl.program_id(0)
    rows, count = h2_ref.shape[0], sum_ref.shape[0]
    chunk = 80
    summed = jnp.zeros((count, TILE), f32)
    for k in range(rows // chunk):
        inner = mul(h2_ref[k * chunk : (k + 1) * chunk, :], wu_ref[...])
        value, _ = gelu_parts(inner)
        pool = pool_matrix(count, chunk, k * chunk, IMG_LEN)
        summed = summed + mul(pool, value.astype(bf16))
    mean = two_terms(summed * (1.0 / IMG_LEN))
    place = lax.broadcasted_iota(jnp.int32, (TILE, TILE // fold), 0)
    picked = lax.broadcasted_iota(jnp.int32, (TILE, TILE // fold), 1) * fold
    terms = jnp.zeros((2 * count, D), f32)
    for k in range(fold):
        chosen = jnp.where(place == picked + k, 1.0, 0.0).astype(bf16)
        part = mul(mean, chosen).astype(bf16)
        terms = terms + mul(part, wd_ref[:, k * D : (k + 1) * D])
    added = terms[:count] + terms[count:]

    @pl.when(step == 0)
    def _():
        acc[...] = sum_ref[...] * (1.0 / IMG_LEN) + added

    @pl.when(step > 0)
    def _():
        acc[...] += added

    @pl.when(step == pl.num_programs(0) - 1)
    def _():
        out_ref[...] = unit_rows(acc[...])[0].astype(bf16)


def image_up(normed2, whole, up_col, down_col, middle_sum):
    rows, count = normed2.shape[0], middle_sum.shape[0]
    fold = FF // D
    fixed = lambda shape: pl.BlockSpec(shape, lambda i: (0, 0))
    return pl.pallas_call(
        functools.partial(image_up_kernel, fold),
        grid=(FF // TILE,),
        out_shape=jax.ShapeDtypeStruct((count, D), bf16),
        in_specs=[
            fixed((rows, D)),
            pl.BlockSpec((D, TILE), lambda i: (0, up_col // TILE + i)),
            pl.BlockSpec((TILE // fold, fold * D), lambda i: (i, down_col // (fold * D))),
            fixed((count, D)),
        ],
        out_specs=fixed((count, D)),
        scratch_shapes=[pltpu.VMEM((count, D), f32)],
        compiler_params=params(),
        cost_estimate=cost(2 * rows * D * FF, 4 * D * FF, 15 * rows * FF),
        name="image_up",
    )(normed2, whole, whole, middle_sum)


def loss_parts(text_rows, pos, image_all):
    similar = mul_bt(text_rows, image_all) * logit_scale
    shifted = jnp.exp(similar - logit_scale)
    alive = jnp.max(pos, axis=1, keepdims=True)
    row_sum = jnp.sum(shifted, axis=1, keepdims=True)
    row_count = jnp.maximum(jnp.sum(pos, axis=1, keepdims=True), 1.0)
    return similar, shifted, alive, row_sum, row_count


def sums_over_captions(text_rows, pos, image_all):
    similar, shifted, alive, row_sum, row_count = loss_parts(text_rows, pos, image_all)
    pos_similar = pos * similar
    cap_term = alive * (
        logit_scale + jnp.log(row_sum) - jnp.sum(pos_similar, axis=1, keepdims=True) / row_count
    )
    return (
        jnp.sum(alive * shifted, axis=0, keepdims=True),
        jnp.sum(pos, axis=0, keepdims=True),
        jnp.sum(pos_similar, axis=0, keepdims=True),
        jnp.sum(cap_term, axis=0, keepdims=True),
        jnp.sum(alive, axis=0, keepdims=True),
    )


def loss_from(sums):
    col_sum, col_count, col_pos, cap_total, live_total = sums
    img_term = logit_scale + jnp.log(col_sum) - col_pos / col_count
    return 0.5 * cap_total / live_total + 0.5 * jnp.mean(img_term, axis=1, keepdims=True)


def grad_of_unit(text_rows, pos, image_all, col_sum, col_count, live_total):
    _, shifted, alive, row_sum, row_count = loss_parts(text_rows, pos, image_all)
    cap_share, img_share = 0.5 / live_total, 0.5 / image_all.shape[0]
    grad_sims = alive * shifted * (cap_share / row_sum + img_share / col_sum) - pos * (
        cap_share / row_count + img_share / col_count
    )
    return mul(grad_sims.astype(bf16), image_all) * logit_scale


def turned(grad, unit):
    return grad - unit * jnp.sum(grad * unit, axis=-1, keepdims=True)


def loss_kernel(
    pack_ref, image_ref, own_ref, unit_ref, inv_ref, loss_ref, row_ref, col_sum_ref, col_count_ref,
    live_ref
):
    image_all = image_ref[...]
    chunk = 256
    total = None
    for k in range(pack_ref.shape[0] // chunk):
        at = slice(k * chunk, (k + 1) * chunk)
        part = sums_over_captions(pack_ref[at, :D], pack_ref[at, D:].astype(f32), image_all)
        total = part if total is None else [a + b for a, b in zip(total, part)]
    loss_ref[...] = jnp.broadcast_to(loss_from(total), loss_ref.shape)
    col_sum, col_count, _, _, live_total = total
    col_sum_ref[...] = col_sum
    col_count_ref[...] = col_count
    live_ref[...] = jnp.broadcast_to(live_total, live_ref.shape)
    grad = grad_of_unit(
        own_ref[:, :D], own_ref[:, D:].astype(f32), image_all, col_sum, col_count, live_total
    )
    row_ref[...] = inv_ref[:, :1] * turned(grad, unit_ref[...]) * (1.0 / TXT_LEN)


def loss_and_rows(pack, image_all, own_pack, unit, inverse):
    images, count = image_all.shape[0], own_pack.shape[0]
    shapes = [(1, 128), (count, D), (1, images), (1, images), (1, 128)]
    return pl.pallas_call(
        loss_kernel,
        out_shape=[jax.ShapeDtypeStruct(shape, f32) for shape in shapes],
        compiler_params=params(),
        cost_estimate=cost(2 * pack.shape[0] * images * D, 2 * pack.size, pack.shape[0] * images),
        name="loss_and_rows",
    )(pack, image_all, own_pack, unit, inverse)


def down_kernel(pack_ref, image_ref, col_sum_ref, col_count_ref, live_ref, hid_ref, out_ref):
    step = pl.program_id(0)
    text_rows = pack_ref[:, :D]
    grad = grad_of_unit(
        text_rows, pack_ref[:, D:].astype(f32), image_ref[...], col_sum_ref[...],
        col_count_ref[...], live_ref[:, :1]
    )
    rows = (turned(grad, text_rows.astype(f32)) * (1.0 / TXT_LEN)).astype(bf16)
    part = mul_at(hid_ref[...], rows)

    @pl.when(step == 0)
    def _():
        out_ref[...] = part

    @pl.when(step > 0)
    def _():
        out_ref[...] += part


def grad_of_down(pack, image_all, col_sum, col_count, live_total, hidden_cols):
    images, chunk = image_all.shape[0], 256
    fixed = lambda shape: pl.BlockSpec(shape, lambda i: (0, 0))
    per = hidden_cols.shape[1]
    return pl.pallas_call(
        down_kernel,
        grid=(pack.shape[0] // chunk,),
        out_shape=jax.ShapeDtypeStruct((per, D), f32),
        in_specs=[
            pl.BlockSpec((chunk, pack.shape[1]), lambda i: (i, 0)),
            fixed((images, D)), fixed((1, images)), fixed((1, images)), fixed((1, 128)),
            pl.BlockSpec((chunk, per), lambda i: (i, 0)),
        ],
        out_specs=fixed((per, D)),
        compiler_params=params(),
        cost_estimate=cost(4 * pack.shape[0] * images * D, 2 * pack.size, pack.shape[0] * images),
        name="grad_of_down",
    )(pack, image_all, col_sum, col_count, live_total, hidden_cols)


def mlp_back_kernel(
    low_ref, wd_ref, slope_ref, wu_ref, lhs_ref, mid_ref, gain_ref, row_ref, keep_a, send_a, keep_b,
    send_b, out_ref, gain_out, bias_out, acc
):
    step = pl.program_id(0)
    count, rows = low_ref.shape[0], slope_ref.shape[0]
    half = D // 2
    hidden = mul_bt(low_ref[...], wd_ref[...])
    wide = jnp.broadcast_to(hidden[:, None, :], (count, TXT_LEN, TILE)).reshape(rows, TILE)
    inner = (wide * slope_ref[...].astype(f32)).astype(bf16)
    weight = mul(lhs_ref[0], inner).astype(bf16)

    @pl.when(step < pl.num_programs(0) // 2)
    def _():
        keep_a[...] = weight[:half]
        send_a[...] = weight[half:]

    @pl.when(step >= pl.num_programs(0) // 2)
    def _():
        keep_b[...] = weight[:half]
        send_b[...] = weight[half:]

    added = mul_bt(inner, wu_ref[...])

    @pl.when(step == 0)
    def _():
        acc[...] = added

    @pl.when(step > 0)
    def _():
        acc[...] += added

    @pl.when(step == pl.num_programs(0) - 1)
    def _():
        chunk = 128
        per = chunk // TXT_LEN
        gain = gain_ref[...]
        gain_out[...] = jnp.zeros_like(gain_out)
        bias_out[...] = jnp.zeros_like(bias_out)

        @pl.loop(0, rows // chunk)
        def _(k):
            at = pl.ds(pl.multiple_of(k * chunk, chunk), chunk)
            unit, scale = norm_parts(mid_ref[at, :])
            grad = acc[at, :]
            gain_out[...] += jnp.sum(grad * unit, axis=0, keepdims=True)
            bias_out[...] += jnp.sum(grad, axis=0, keepdims=True)
            row = row_ref[pl.ds(pl.multiple_of(k * per, per), per), :]
            row = jnp.broadcast_to(row[:, None, :], (per, TXT_LEN, D)).reshape(chunk, D)
            out_ref[at, :] = row + norm_back(unit, scale, gain, grad)


def mlp_back(grad_row, weight_down, slope, weight_up, lhs, middle, gain):
    rows, count = slope.shape[0], grad_row.shape[0]
    steps = FF // TILE
    fixed = lambda shape: pl.BlockSpec(shape, lambda i: (0, 0))
    first = pl.BlockSpec((D // 2, TILE), lambda i: (0, jnp.minimum(i, steps // 2 - 1)))
    second = pl.BlockSpec((D // 2, TILE), lambda i: (0, jnp.maximum(i - steps // 2, 0)))
    part = jax.ShapeDtypeStruct((D // 2, FF // 2), bf16)
    line = jax.ShapeDtypeStruct((1, D), f32)
    return pl.pallas_call(
        mlp_back_kernel,
        grid=(steps,),
        out_shape=[part] * 4 + [jax.ShapeDtypeStruct((rows, D), f32), line, line],
        in_specs=[
            fixed((count, D)),
            pl.BlockSpec((TILE, D), lambda i: (i, 0)),
            pl.BlockSpec((rows, TILE), lambda i: (0, i)),
            pl.BlockSpec((D, TILE), lambda i: (0, i)),
            pl.BlockSpec((1, D, rows), lambda i: (i // (steps // 2), 0, 0)),
            fixed((rows, D)),
            fixed((1, D)),
            fixed((count, D)),
        ],
        out_specs=[first, first, second, second, fixed((rows, D)), fixed((1, D)), fixed((1, D))],
        scratch_shapes=[pltpu.VMEM((rows, D), f32)],
        compiler_params=params(),
        cost_estimate=cost(4 * rows * D * FF, 4 * D * FF + 2 * rows * FF + 2 * D * FF, rows * FF),
        name="mlp_back",
    )(grad_row.astype(bf16), weight_down, slope, weight_up, lhs, middle, gain[None], grad_row)


def attention_back_kernel(grad_ref, wo_ref, qkv_ref, low_ref, out_ref):
    rows, chunk = grad_ref.shape[0], 128
    one = same_sequence(chunk, 0, chunk, 0, TXT_LEN)
    mask = jnp.concatenate([one, one], axis=0)

    @pl.loop(0, rows // chunk)
    def _(step):
        at = pl.ds(pl.multiple_of(step * chunk, chunk), chunk)
        low_ref[at, :] = grad_ref[at, :].astype(bf16)

    @pl.loop(0, rows // chunk)
    def _(step):
        at = pl.ds(pl.multiple_of(step * chunk, chunk), chunk)
        grad_att = mul_bt(low_ref[at, :], wo_ref[...]).astype(bf16)
        for pair in range(HEADS // 2):
            queries = two_heads(qkv_ref[at, pair_cols(0, pair)] * bf16(HEAD ** (-0.5)))
            keys = qkv_ref[at, pair_cols(1, pair)]
            vals = qkv_ref[at, pair_cols(2, pair)]
            grads = two_heads(grad_att[:, pair_cols(0, pair)])
            probs = masked_softmax(mul_bt(queries, keys), mask)
            grad_probs = mul_bt(grads, vals)
            along = jnp.sum(grad_probs * probs, axis=-1, keepdims=True)
            grad_scores = (probs * (grad_probs - along)).astype(bf16)
            side = jnp.concatenate([grad_scores[:chunk], grad_scores[chunk:]], axis=1)
            grad_q = mul(side, two_heads(keys)) * HEAD ** (-0.5)
            grad_k = mul_at(grad_scores, queries)
            grad_v = mul_at(probs.astype(bf16), grads)
            out_ref[at, pair_cols(0, pair)] = grad_q.astype(bf16)
            out_ref[at, pair_cols(1, pair)] = grad_k.astype(bf16)
            out_ref[at, pair_cols(2, pair)] = grad_v.astype(bf16)


def attention_back(grad_middle, weight_out, project):
    rows = project.shape[0]
    return pl.pallas_call(
        attention_back_kernel,
        out_shape=[
            jax.ShapeDtypeStruct((rows, D), bf16),
            jax.ShapeDtypeStruct((rows, 3 * D), bf16),
        ],
        compiler_params=params(),
        cost_estimate=cost(2 * rows * D * D, 16 * rows * D + 2 * D * D, rows * 128 * HEADS),
        name="attention_back",
    )(grad_middle, weight_out, project)


def weight_back_kernel(lhs_ref, proj_ref, low_ref, keep_a, send_a, keep_b, send_b):
    step = pl.program_id(0)
    half = D // 2

    @pl.when(step < 2)
    def _():
        weight = mul(lhs_ref[0], proj_ref[...]).astype(bf16)
        keep_a[...] = weight[:half]
        send_a[...] = weight[half:]

    @pl.when(step == 2)
    def _():
        weight = mul(lhs_ref[0], proj_ref[...]).astype(bf16)
        keep_b[...] = weight[:half]
        send_b[...] = weight[half:]

    @pl.when(step == 3)
    def _():
        weight = mul(lhs_ref[0], low_ref[...]).astype(bf16)
        keep_b[...] = weight[:half]
        send_b[...] = weight[half:]


def weight_back(lhs, grad_proj, grad_low):
    rows = grad_proj.shape[0]
    first = pl.BlockSpec((D // 2, D), lambda i: (0, jnp.minimum(i, 1)))
    second = pl.BlockSpec((D // 2, D), lambda i: (0, jnp.maximum(i - 2, 0)))
    return pl.pallas_call(
        weight_back_kernel,
        grid=(4,),
        out_shape=[jax.ShapeDtypeStruct((D // 2, 2 * D), bf16)] * 4,
        in_specs=[
            pl.BlockSpec((1, D, rows), lambda i: (jnp.maximum(i - 1, 0), 0, 0)),
            pl.BlockSpec((rows, D), lambda i: (0, jnp.minimum(i, 2))),
            pl.BlockSpec((rows, D), lambda i: (0, 0)),
        ],
        out_specs=[first, first, second, second],
        compiler_params=params(),
        cost_estimate=cost(8 * rows * D * D, 8 * rows * D + 14 * D * D),
        name="weight_back",
    )(lhs, grad_proj, grad_low)


def input_back_kernel(proj_ref, w_ref, x_ref, gain_ref, mid_ref, out_ref, gain_out, bias_out, acc):
    step = pl.program_id(0)
    rows, chunk = x_ref.shape[0], 128
    added = mul_bt(proj_ref[...], w_ref[...])

    @pl.when(step == 0)
    def _():
        acc[...] = added

    @pl.when(step > 0)
    def _():
        acc[...] += added

    @pl.when(step == pl.num_programs(0) - 1)
    def _():
        gain = gain_ref[...]
        gain_out[...] = jnp.zeros_like(gain_out)
        bias_out[...] = jnp.zeros_like(bias_out)

        @pl.loop(0, rows // chunk)
        def _(k):
            at = pl.ds(pl.multiple_of(k * chunk, chunk), chunk)
            unit, scale = norm_parts(x_ref[at, :].astype(f32))
            grad = acc[at, :]
            gain_out[...] += jnp.sum(grad * unit, axis=0, keepdims=True)
            bias_out[...] += jnp.sum(grad, axis=0, keepdims=True)
            out_ref[at, :] = mid_ref[at, :] + norm_back(unit, scale, gain, grad)


def input_back(grad_proj, weight, rows_in, gain, grad_middle):
    rows = rows_in.shape[0]
    fixed = lambda shape: pl.BlockSpec(shape, lambda i: (0, 0))
    line = jax.ShapeDtypeStruct((1, D), f32)
    return pl.pallas_call(
        input_back_kernel,
        grid=(3,),
        out_shape=[jax.ShapeDtypeStruct((rows, D), f32), line, line],
        in_specs=[
            pl.BlockSpec((rows, D), lambda i: (0, i)),
            pl.BlockSpec((D, D), lambda i: (0, i)),
            fixed((rows, D)), fixed((1, D)), fixed((rows, D)),
        ],
        out_specs=[fixed((rows, D)), fixed((1, D)), fixed((1, D))],
        scratch_shapes=[pltpu.VMEM((rows, D), f32)],
        compiler_params=params(),
        cost_estimate=cost(6 * rows * D * D, 14 * rows * D + 6 * D * D),
        name="input_back",
    )(grad_proj, weight, rows_in, gain[None], grad_middle)


def local(
    images,
    captions,
    img_gain1,
    img_bias1,
    img_qkv,
    img_out,
    img_gain2,
    img_bias2,
    img_up,
    img_down,
    txt_gain1,
    txt_bias1,
    txt_qkv,
    txt_out,
    txt_gain2,
    txt_bias2,
    txt_up,
    txt_down,
    counts,
    matches,
):
    peers = lax.axis_size(AXIS)
    own = lax.axis_index(AXIS)
    per = D // peers
    img_local = counts.shape[0]
    cap_local = matches.shape[0]
    total_images = matches.shape[1]

    shard = jnp.concatenate(
        [
            img_qkv.reshape(per, 3 * D),
            img_out.reshape(per, D),
            img_up.reshape(per, FF),
            img_down.reshape(per, FF),
        ],
        axis=1,
    )
    whole = lax.all_gather(shard, AXIS, axis=0, tiled=True)

    normed1, project, attended, middle, normed2, middle_sum = front(
        TXT_LEN, (128,), 128, captions, txt_gain1, txt_bias1, txt_qkv, txt_out, 0, txt_gain2, txt_bias2
    )
    slope, hidden_sum, text_unit, inverse = text_up(normed2, txt_up, txt_down, middle_sum)
    text_low = text_unit.astype(bf16)

    ends_at = jnp.cumsum(counts)
    slot_ids = lax.iota(jnp.int32, cap_local)
    owner = jnp.sum((ends_at[None, :] <= slot_ids[:, None]).astype(jnp.int32), axis=1)
    owner = owner + own * img_local
    live = slot_ids < ends_at[-1]
    columns = lax.iota(jnp.int32, total_images)
    positive = ((matches > 0) | (owner[:, None] == columns[None, :])) & live[:, None]

    own_pack = jnp.concatenate([text_low, positive.astype(bf16)], axis=1)
    small = peers * cap_local * total_images <= 1 << 20
    if small:
        text_pack = gathered(own_pack).reshape(-1, D + total_images)
        hidden_cols = lax.all_to_all(
            (hidden_sum * inverse[:, :1]).astype(bf16), AXIS, split_axis=1, concat_axis=0, tiled=True
        )

    windows = ((0, 208, 0, 256), (208, 192, 192, 208))
    image_front = front(
        IMG_LEN, windows, 80, images, img_gain1, img_bias1, whole, whole, 3, img_gain2, img_bias2
    )
    image_low = image_up(image_front[4], whole, 4 * D, 4 * D + FF, image_front[5])
    image_all = spread(image_low).reshape(total_images, D)

    order_a, order_b, tail = stage_orders()
    matrix_a, matrix_b = row_order(order_a, tail), row_order(order_b, tail)
    lhs_up = jnp.stack([placed(matrix_a, normed2), placed(matrix_b, normed2)])
    lhs_rest = jnp.stack(
        [placed(matrix_a, normed1), placed(matrix_b, normed1), placed(matrix_b, attended)]
    )

    if small:
        loss_value, grad_row, col_sum, col_count, live_total = loss_and_rows(
            text_pack, image_all, own_pack, text_unit, inverse
        )
        loss_value = loss_value[0, 0]
    else:
        pos = own_pack[:, D:].astype(f32)
        sums = lax.psum(sums_over_captions(text_low, pos, image_all), AXIS)
        loss_value = loss_from(sums)[0, 0]
        grad = grad_of_unit(text_low, pos, image_all, sums[0], sums[1], sums[4])
        grad_row = inverse[:, :1] * turned(grad, text_unit) * (1.0 / TXT_LEN)

    *up_parts, grad_middle, gain_two, bias_two = mlp_back(
        grad_row, txt_down, slope, txt_up, lhs_up, middle, txt_gain2
    )
    up_share = scattered(*up_parts)
    if small:
        grad_down = grad_of_down(text_pack, image_all, col_sum, col_count, live_total, hidden_cols)
    else:
        grad_down = lax.psum_scatter(
            mul_at(hidden_sum.astype(bf16), grad_row.astype(bf16)),
            AXIS,
            scatter_dimension=0,
            tiled=True,
        )
    grad_low, grad_proj = attention_back(grad_middle, txt_out, project)
    rest_share = scattered(*weight_back(lhs_rest, grad_proj, grad_low))
    caption_grad, gain_one, bias_one = input_back(
        grad_proj, txt_qkv, captions, txt_gain1, grad_middle
    )
    norms = jnp.concatenate([gain_one, bias_one, gain_two, bias_two], axis=0)
    norms = jnp.sum(spread(norms[None]), axis=0).reshape(4, D)
    return (
        loss_value,
        caption_grad,
        norms[0],
        norms[1],
        rest_share[:, : 3 * D].reshape(-1),
        rest_share[:, 3 * D :].reshape(-1),
        norms[2],
        norms[3],
        up_share.reshape(-1),
        grad_down.reshape(-1),
    )


def solution(mesh):
    split, flat, whole = P("blk", None), P("blk"), P()
    image_block = (whole, whole, flat, flat, whole, whole, flat, flat)
    return jax.shard_map(
        local,
        mesh=mesh,
        in_specs=(split, split) + image_block + (whole,) * 8 + (flat, split),
        out_specs=(whole, split, whole, whole, flat, flat, whole, whole, flat, flat),
        check_vma=False,
    )
```

```python
import functools

import jax
import jax.numpy as jnp
from jax import lax
from jax.experimental import pallas as pl
from jax.experimental.pallas import tpu as pltpu
from jax.sharding import PartitionSpec as P

D = 768
FF = 3072
HEAD = 64
HEADS = D // HEAD
IMG_LEN = 50
TXT_LEN = 16
AXIS = "blk"

norm_eps = 1e-06
logit_scale = 50.0
f32 = jnp.float32
bf16 = jnp.bfloat16


def swapped(value, mask):
    peers = lax.axis_size(AXIS)
    return lax.ppermute(value, AXIS, [(i, i ^ mask) for i in range(peers)])


def bit_masks():
    peers = lax.axis_size(AXIS)
    return [1 << k for k in range(peers.bit_length() - 1)]


def gathered(block):
    own = lax.axis_index(AXIS)
    held = block[None]
    for mask in reversed(bit_masks()):
        other = swapped(held, mask)
        upper = (own & mask) > 0
        first = jnp.where(upper, other, held)
        second = jnp.where(upper, held, other)
        held = jnp.stack([first, second], axis=1).reshape((-1,) + block.shape)
    return held


def spread(block):
    peers = lax.axis_size(AXIS)
    copies = jnp.broadcast_to(block[None], (peers,) + block.shape)
    return lax.all_to_all(copies, AXIS, split_axis=0, concat_axis=0, tiled=True)


def stage_orders():
    masks = bit_masks()
    head, tail = masks[:-2], masks[-2:]
    order_a = list(head)
    order_b = list(head)
    for k in range(1, len(head) - 1, 2):
        order_b[k], order_b[k + 1] = order_b[k + 1], order_b[k]
    return order_a, order_b, tail


def row_order(order, tail):
    peers = lax.axis_size(AXIS)
    own = lax.axis_index(AXIS)
    per = D // peers
    bits = list(order) + list(reversed(tail))
    places = lax.iota(jnp.int32, D)
    block = places // per
    target = jnp.zeros_like(block) + own
    for k, mask in enumerate(bits):
        target = target ^ (((block >> (len(bits) - 1 - k)) & 1) * mask)
    source = target * per + places % per
    return (source[:, None] == lax.iota(jnp.int32, D)[None, :]).astype(bf16)


def placed(order, values):
    return mul_bt(order, values).astype(bf16)


def hand_on(parts, stage):
    order_a, order_b, _ = stage_orders()
    keep_a, send_a, keep_b, send_b = parts
    return keep_a, swapped(send_a, order_a[stage]), keep_b, swapped(send_b, order_b[stage])


def hand_on_last(blocks):
    low, high = stage_orders()[2]
    own, *others = blocks
    return own, [swapped(block, mask) for block, mask in zip(others, (low, high, low | high))]


def sum_last(own, others):
    total = own
    for other in others:
        total = total + other.astype(f32)
    return total


VMEM_BYTES = 56 << 20
TILE = 512


def norm_parts(values):
    average = jnp.mean(values, axis=-1, keepdims=True)
    centred = values - average
    variance = jnp.mean(centred * centred, axis=-1, keepdims=True)
    scale = lax.rsqrt(variance + norm_eps)
    return centred * scale, scale


def norm_back(unit, scale, gain, grad):
    inner = grad * gain
    shift = jnp.mean(inner, axis=-1, keepdims=True)
    along = jnp.mean(inner * unit, axis=-1, keepdims=True)
    return scale * (inner - shift - unit * along)


def mul(lhs, rhs):
    return jnp.dot(lhs, rhs, preferred_element_type=f32)


def mul_bt(lhs, rhs):
    return lax.dot_general(lhs, rhs, (((1,), (1,)), ((), ())), preferred_element_type=f32)


def mul_at(lhs, rhs):
    return lax.dot_general(lhs, rhs, (((0,), (0,)), ((), ())), preferred_element_type=f32)


def params(**more):
    return pltpu.CompilerParams(vmem_limit_bytes=VMEM_BYTES, **more)


def cost(flops, moved, transcendentals=0):
    return pl.CostEstimate(flops=flops, bytes_accessed=moved, transcendentals=transcendentals)


def lane_halves(dtype):
    lane = lax.broadcasted_iota(jnp.int32, (1, 2 * HEAD), 1)
    low = jnp.where(lane < HEAD, 1.0, 0.0)
    return low.astype(dtype), (1.0 - low).astype(dtype)


def two_heads(pair):
    low, high = lane_halves(bf16)
    return jnp.concatenate([pair * low, pair * high], axis=0)


def same_sequence(rows, row0, cols, col0, seq_len):
    row = (lax.broadcasted_iota(jnp.int32, (rows, cols), 0) + row0) // seq_len
    col = (lax.broadcasted_iota(jnp.int32, (rows, cols), 1) + col0) // seq_len
    return row == col


def masked_softmax(scores, mask):
    scores = jnp.where(mask, scores, -1e30)
    raised = jnp.exp(scores - jnp.max(scores, axis=-1, keepdims=True))
    return raised * (1.0 / jnp.sum(raised, axis=-1, keepdims=True))


def fold_kernel(keep_a, got_a, keep_b, got_b, *refs):
    outs = refs[-4:]
    half = outs[0].shape[0]
    for k, (kept, got) in enumerate(((keep_a, got_a), (keep_b, got_b))):
        for j in range(2):
            at = slice(j * half, (j + 1) * half)
            outs[2 * k + j][...] = (kept[at, :].astype(f32) + got[at, :].astype(f32)).astype(bf16)


def fold(parts, after=()):
    rows, cols = parts[0].shape
    if rows % 32:
        whole = [
            (kept.astype(f32) + got.astype(f32)).astype(bf16)
            for kept, got in (parts[:2], parts[2:])
        ]
        return [part for one in whole for part in (one[: rows // 2], one[rows // 2 :])]
    tile = 512
    return pl.pallas_call(
        fold_kernel,
        grid=(cols // tile,),
        out_shape=[jax.ShapeDtypeStruct((rows // 2, cols), bf16)] * 4,
        in_specs=[pl.BlockSpec((rows, tile), lambda i: (0, i))] * 4 + anywhere(after),
        out_specs=[pl.BlockSpec((rows // 2, tile), lambda i: (0, i))] * 4,
        compiler_params=params(),
        cost_estimate=cost(2 * rows * cols, 12 * rows * cols),
        name="fold",
    )(*parts, *after)


def fold_last_kernel(keep_a, got_a, keep_b, got_b, own_ref, *outs):
    rows = own_ref.shape[0]
    cols = keep_a.shape[1]
    for k, (kept, got) in enumerate(((keep_a, got_a), (keep_b, got_b))):
        total = kept[...].astype(f32) + got[...].astype(f32)
        at = slice(k * cols, (k + 1) * cols)
        own_ref[:, at] = total[:rows]
        for j, out in enumerate(outs):
            out[:, at] = total[(j + 1) * rows : (j + 2) * rows].astype(bf16)


def fold_last(parts):
    rows, cols = parts[0].shape
    shape = (rows // 4, 2 * cols)
    if rows % 32:
        pairs = (parts[:2], parts[2:])
        both = [kept.astype(f32) + got.astype(f32) for kept, got in pairs]
        own, *others = jnp.split(jnp.concatenate(both, axis=1), 4)
        return [own] + [other.astype(bf16) for other in others]
    return pl.pallas_call(
        fold_last_kernel,
        out_shape=[jax.ShapeDtypeStruct(shape, f32)] + [jax.ShapeDtypeStruct(shape, bf16)] * 3,
        compiler_params=params(),
        cost_estimate=cost(2 * rows * cols, 12 * rows * cols),
        name="fold_last",
    )(*parts)


def anywhere(after):
    return [pl.BlockSpec(memory_space=pl.ANY)] * len(after)


def pair_cols(part, pair):
    start = part * D + pair * 2 * HEAD
    return slice(start, start + 2 * HEAD)


def front_kernel(
    seq_len, windows, ln_rows, x_ref, g1_ref, b1_ref, wqkv_ref, wo_ref, g2_ref, b2_ref, h1_ref,
    qkv_ref, att_ref, mid_ref, h2_ref, sum_ref
):
    rows = x_ref.shape[0]
    gain1, bias1 = g1_ref[...].astype(f32), b1_ref[...].astype(f32)
    gain2, bias2 = g2_ref[...].astype(f32), b2_ref[...].astype(f32)

    @pl.loop(0, rows // ln_rows)
    def _(step):
        at = pl.ds(pl.multiple_of(step * ln_rows, ln_rows), ln_rows)
        unit, _ = norm_parts(x_ref[at, :].astype(f32))
        h1_ref[at, :] = (unit * gain1 + bias1).astype(bf16)

    @pl.loop(0, 3 * D // 256)
    def _(step):
        at = pl.ds(pl.multiple_of(step * 256, 256), 256)
        qkv_ref[:, at] = mul(h1_ref[...], wqkv_ref[:, at]).astype(bf16)

    def attend(q_rows, k_rows, mask):
        for pair in range(HEADS // 2):
            queries = two_heads(qkv_ref[q_rows, pair_cols(0, pair)] * bf16(HEAD ** (-0.5)))
            scores = mul_bt(queries, qkv_ref[k_rows, pair_cols(1, pair)])
            probs = masked_softmax(scores, mask).astype(bf16)
            half = probs.shape[0] // 2
            vals = qkv_ref[k_rows, pair_cols(2, pair)]
            low, high = lane_halves(f32)
            mixed = mul(probs, vals)
            att_ref[q_rows, pair_cols(0, pair)] = (
                mixed[:half] * low + mixed[half:] * high
            ).astype(bf16)

    if len(windows) == 1:
        size = windows[0]
        one = same_sequence(size, 0, size, 0, seq_len)
        mask = jnp.concatenate([one, one], axis=0)

        @pl.loop(0, rows // size)
        def _(step):
            at = pl.ds(pl.multiple_of(step * size, size), size)
            attend(at, at, mask)
    else:
        for row0, count, key0, keys in windows:
            one = same_sequence(count, row0, keys, key0, seq_len)
            attend(pl.ds(row0, count), pl.ds(key0, keys), jnp.concatenate([one, one], axis=0))

    @pl.loop(0, D // 256)
    def _(step):
        at = pl.ds(pl.multiple_of(step * 256, 256), 256)
        mid_ref[:, at] = x_ref[:, at].astype(f32) + mul(att_ref[...], wo_ref[:, at])

    @pl.loop(0, rows // ln_rows)
    def _(step):
        at = pl.ds(pl.multiple_of(step * ln_rows, ln_rows), ln_rows)
        unit, _ = norm_parts(mid_ref[at, :])
        h2_ref[at, :] = (unit * gain2 + bias2).astype(bf16)

    if seq_len % 8 == 0:
        per = ln_rows // seq_len

        @pl.loop(0, rows // ln_rows)
        def _(step):
            values = mid_ref[pl.ds(pl.multiple_of(step * ln_rows, ln_rows), ln_rows), :]
            sum_ref[pl.ds(pl.multiple_of(step * per, per), per), :] = jnp.sum(
                values.reshape(per, seq_len, D), axis=1
            )
    else:
        for k in range(rows // seq_len):
            first, last = k * seq_len, (k + 1) * seq_len
            at8, end8 = first // 8 * 8, -(-last // 8) * 8
            values = mid_ref[at8:end8, :]
            place = lax.broadcasted_iota(jnp.int32, values.shape, 0) + at8
            inside = (place >= first) & (place < last)
            sum_ref[k : k + 1, :] = jnp.sum(
                jnp.where(inside, values, 0.0), axis=0, keepdims=True
            )


def front(seq_len, windows, ln_rows, rows_in, gain1, bias1, wqkv, wo, wo_col, gain2, bias2):
    rows = rows_in.shape[0]
    shapes = [
        ((rows, D), bf16),
        ((rows, 3 * D), bf16),
        ((rows, D), bf16),
        ((rows, D), f32),
        ((rows, D), bf16),
        ((rows // seq_len, D), f32),
    ]
    whole = lambda shape: pl.BlockSpec(shape, lambda i: (0, 0))
    row = whole((1, D))
    return pl.pallas_call(
        functools.partial(front_kernel, seq_len, windows, ln_rows),
        grid=(1,),
        out_shape=[jax.ShapeDtypeStruct(*item) for item in shapes],
        in_specs=[
            whole((rows, D)), row, row, whole((D, 3 * D)),
            pl.BlockSpec((D, D), lambda i: (0, wo_col)), row, row,
        ],
        out_specs=[whole(item[0]) for item in shapes],
        compiler_params=params(),
        cost_estimate=cost(rows * D * D * 8, 14 * D * rows + 8 * D * D, rows * 128 * HEADS),
        name="front",
    )(rows_in, gain1[None], bias1[None], wqkv, wo, gain2[None], bias2[None])


def gelu_parts(inner):
    half = 0.5 * (1.0 + lax.erf(inner * (0.5**0.5)))
    return inner * half, half


def pool_matrix(count, rows, row0, seq_len):
    row = (lax.broadcasted_iota(jnp.int32, (count, rows), 1) + row0) // seq_len
    return jnp.where(row == lax.broadcasted_iota(jnp.int32, (count, rows), 0), 1.0, 0.0).astype(bf16)


def two_terms(mean):
    high = mean.astype(bf16)
    low = (mean - high.astype(f32)).astype(bf16)
    return jnp.concatenate([high, low], axis=0)


def unit_rows(pooled):
    inverse = lax.rsqrt(jnp.sum(pooled * pooled, axis=-1, keepdims=True) + norm_eps)
    return pooled * inverse, inverse


def text_up_kernel(h2_ref, wu_ref, wd_ref, sum_ref, slope_ref, hid_ref, unit_ref, inv_ref, acc):
    step = pl.program_id(0)
    chunk = 128
    per = chunk // TXT_LEN
    pool = pool_matrix(per, chunk, 0, TXT_LEN)
    for k in range(h2_ref.shape[0] // chunk):
        inner = mul(h2_ref[k * chunk : (k + 1) * chunk, :], wu_ref[...])
        value, half = gelu_parts(inner)
        slope = half + inner * (jnp.exp(-0.5 * inner * inner) * 0.3989422804014327)
        slope_ref[k * chunk : (k + 1) * chunk, :] = slope.astype(bf16)
        hid_ref[k * per : (k + 1) * per, :] = mul(pool, value.astype(bf16))
    terms = mul(two_terms(hid_ref[...] * (1.0 / TXT_LEN)), wd_ref[...])
    count = hid_ref.shape[0]
    added = terms[:count] + terms[count:]

    @pl.when(step == 0)
    def _():
        acc[...] = sum_ref[...] * (1.0 / TXT_LEN) + added

    @pl.when(step > 0)
    def _():
        acc[...] += added

    @pl.when(step == pl.num_programs(0) - 1)
    def _():
        unit, inverse = unit_rows(acc[...])
        unit_ref[...] = unit
        inv_ref[...] = jnp.broadcast_to(inverse, inv_ref.shape)


def text_up(normed2, weight_up, weight_down, middle_sum):
    rows, count = normed2.shape[0], middle_sum.shape[0]
    fixed = lambda shape: pl.BlockSpec(shape, lambda i: (0, 0))
    return pl.pallas_call(
        text_up_kernel,
        grid=(FF // TILE,),
        out_shape=[
            jax.ShapeDtypeStruct((rows, FF), bf16),
            jax.ShapeDtypeStruct((count, FF), f32),
            jax.ShapeDtypeStruct((count, D), f32),
            jax.ShapeDtypeStruct((count, 128), f32),
        ],
        in_specs=[
            fixed((rows, D)),
            pl.BlockSpec((D, TILE), lambda i: (0, i)),
            pl.BlockSpec((TILE, D), lambda i: (i, 0)),
            fixed((count, D)),
        ],
        out_specs=[
            pl.BlockSpec((rows, TILE), lambda i: (0, i)),
            pl.BlockSpec((count, TILE), lambda i: (0, i)),
            fixed((count, D)),
            fixed((count, 128)),
        ],
        scratch_shapes=[pltpu.VMEM((count, D), f32)],
        compiler_params=params(),
        cost_estimate=cost(2 * rows * D * FF, 4 * D * FF + 2 * rows * FF, 20 * rows * FF),
        name="text_up",
    )(normed2, weight_up, weight_down, middle_sum)


def image_up_kernel(fold, h2_ref, wu_ref, wd_ref, sum_ref, out_ref, acc):
    step = pl.program_id(0)
    rows, count = h2_ref.shape[0], sum_ref.shape[0]
    chunk = 80
    summed = jnp.zeros((count, TILE), f32)
    for k in range(rows // chunk):
        inner = mul(h2_ref[k * chunk : (k + 1) * chunk, :], wu_ref[...])
        value, _ = gelu_parts(inner)
        pool = pool_matrix(count, chunk, k * chunk, IMG_LEN)
        summed = summed + mul(pool, value.astype(bf16))
    mean = two_terms(summed * (1.0 / IMG_LEN))
    place = lax.broadcasted_iota(jnp.int32, (TILE, TILE // fold), 0)
    picked = lax.broadcasted_iota(jnp.int32, (TILE, TILE // fold), 1) * fold
    terms = jnp.zeros((2 * count, D), f32)
    for k in range(fold):
        chosen = jnp.where(place == picked + k, 1.0, 0.0).astype(bf16)
        part = mul(mean, chosen).astype(bf16)
        terms = terms + mul(part, wd_ref[:, k * D : (k + 1) * D])
    added = terms[:count] + terms[count:]

    @pl.when(step == 0)
    def _():
        acc[...] = sum_ref[...] * (1.0 / IMG_LEN) + added

    @pl.when(step > 0)
    def _():
        acc[...] += added

    @pl.when(step == pl.num_programs(0) - 1)
    def _():
        out_ref[...] = unit_rows(acc[...])[0].astype(bf16)


def image_up(normed2, whole, up_col, down_col, middle_sum):
    rows, count = normed2.shape[0], middle_sum.shape[0]
    fold = FF // D
    fixed = lambda shape: pl.BlockSpec(shape, lambda i: (0, 0))
    return pl.pallas_call(
        functools.partial(image_up_kernel, fold),
        grid=(FF // TILE,),
        out_shape=jax.ShapeDtypeStruct((count, D), bf16),
        in_specs=[
            fixed((rows, D)),
            pl.BlockSpec((D, TILE), lambda i: (0, up_col // TILE + i)),
            pl.BlockSpec((TILE // fold, fold * D), lambda i: (i, down_col // (fold * D))),
            fixed((count, D)),
        ],
        out_specs=fixed((count, D)),
        scratch_shapes=[pltpu.VMEM((count, D), f32)],
        compiler_params=params(),
        cost_estimate=cost(2 * rows * D * FF, 4 * D * FF, 15 * rows * FF),
        name="image_up",
    )(normed2, whole, whole, middle_sum)


def loss_parts(text_rows, pos, image_all):
    similar = mul_bt(text_rows, image_all) * logit_scale
    shifted = jnp.exp(similar - logit_scale)
    alive = jnp.max(pos, axis=1, keepdims=True)
    row_sum = jnp.sum(shifted, axis=1, keepdims=True)
    row_count = jnp.maximum(jnp.sum(pos, axis=1, keepdims=True), 1.0)
    return similar, shifted, alive, row_sum, row_count


def sums_over_captions(text_rows, pos, image_all):
    similar, shifted, alive, row_sum, row_count = loss_parts(text_rows, pos, image_all)
    pos_similar = pos * similar
    cap_term = alive * (
        logit_scale + jnp.log(row_sum) - jnp.sum(pos_similar, axis=1, keepdims=True) / row_count
    )
    return (
        jnp.sum(alive * shifted, axis=0, keepdims=True),
        jnp.sum(pos, axis=0, keepdims=True),
        jnp.sum(pos_similar, axis=0, keepdims=True),
        jnp.sum(cap_term, axis=0, keepdims=True),
        jnp.sum(alive, axis=0, keepdims=True),
    )


def loss_from(sums):
    col_sum, col_count, col_pos, cap_total, live_total = sums
    img_term = logit_scale + jnp.log(col_sum) - col_pos / col_count
    return 0.5 * cap_total / live_total + 0.5 * jnp.mean(img_term, axis=1, keepdims=True)


def grad_of_unit(text_rows, pos, image_all, col_sum, col_count, live_total):
    _, shifted, alive, row_sum, row_count = loss_parts(text_rows, pos, image_all)
    cap_share, img_share = 0.5 / live_total, 0.5 / image_all.shape[0]
    grad_sims = alive * shifted * (cap_share / row_sum + img_share / col_sum) - pos * (
        cap_share / row_count + img_share / col_count
    )
    return mul(grad_sims.astype(bf16), image_all) * logit_scale


def turned(grad, unit):
    return grad - unit * jnp.sum(grad * unit, axis=-1, keepdims=True)


def loss_kernel(
    pack_ref, image_ref, own_ref, unit_ref, inv_ref, loss_ref, row_ref, low_ref, col_sum_ref,
    col_count_ref, live_ref
):
    image_all = image_ref[...]
    chunk = 256
    total = None
    for k in range(pack_ref.shape[0] // chunk):
        at = slice(k * chunk, (k + 1) * chunk)
        part = sums_over_captions(pack_ref[at, :D], pack_ref[at, D:].astype(f32), image_all)
        total = part if total is None else [a + b for a, b in zip(total, part)]
    loss_ref[...] = jnp.broadcast_to(loss_from(total), loss_ref.shape)
    col_sum, col_count, _, _, live_total = total
    col_sum_ref[...] = col_sum
    col_count_ref[...] = col_count
    live_ref[...] = jnp.broadcast_to(live_total, live_ref.shape)
    grad = grad_of_unit(
        own_ref[:, :D], own_ref[:, D:].astype(f32), image_all, col_sum, col_count, live_total
    )
    row = inv_ref[:, :1] * turned(grad, unit_ref[...]) * (1.0 / TXT_LEN)
    row_ref[...] = row
    low_ref[...] = row.astype(bf16)


def loss_and_rows(pack, image_all, own_pack, unit, inverse):
    images, count = image_all.shape[0], own_pack.shape[0]
    shapes = [(1, 128), (count, D), (count, D), (1, images), (1, images), (1, 128)]
    kinds = [f32, f32, bf16, f32, f32, f32]
    return pl.pallas_call(
        loss_kernel,
        out_shape=[jax.ShapeDtypeStruct(*item) for item in zip(shapes, kinds)],
        compiler_params=params(),
        cost_estimate=cost(2 * pack.shape[0] * images * D, 2 * pack.size, pack.shape[0] * images),
        name="loss_and_rows",
    )(pack, image_all, own_pack, unit, inverse)


def down_kernel(pack_ref, image_ref, col_sum_ref, col_count_ref, live_ref, hid_ref, *refs):
    step, out_ref = pl.program_id(0), refs[-1]
    text_rows = pack_ref[:, :D]
    grad = grad_of_unit(
        text_rows, pack_ref[:, D:].astype(f32), image_ref[...], col_sum_ref[...],
        col_count_ref[...], live_ref[:, :1]
    )
    rows = (turned(grad, text_rows.astype(f32)) * (1.0 / TXT_LEN)).astype(bf16)
    part = mul_at(hid_ref[...], rows)

    @pl.when(step == 0)
    def _():
        out_ref[...] = part

    @pl.when(step > 0)
    def _():
        out_ref[...] += part


def grad_of_down(pack, image_all, col_sum, col_count, live_total, hidden_cols, after):
    images, chunk = image_all.shape[0], 256
    fixed = lambda shape: pl.BlockSpec(shape, lambda i: (0, 0))
    per = hidden_cols.shape[1]
    return pl.pallas_call(
        down_kernel,
        grid=(pack.shape[0] // chunk,),
        out_shape=jax.ShapeDtypeStruct((per, D), f32),
        in_specs=[
            pl.BlockSpec((chunk, pack.shape[1]), lambda i: (i, 0)),
            fixed((images, D)), fixed((1, images)), fixed((1, images)), fixed((1, 128)),
            pl.BlockSpec((chunk, per), lambda i: (i, 0)),
        ]
        + anywhere(after),
        out_specs=fixed((per, D)),
        compiler_params=params(),
        cost_estimate=cost(4 * pack.shape[0] * images * D, 2 * pack.size, pack.shape[0] * images),
        name="grad_of_down",
    )(pack, image_all, col_sum, col_count, live_total, hidden_cols, *after)


def mlp_back_kernel(
    low_ref, wd_ref, slope_ref, wu_ref, lhs_ref, mid_ref, gain_ref, row_ref, keep_a, send_a, keep_b,
    send_b, out_ref, gain_out, bias_out, acc
):
    step = pl.program_id(0)
    count, rows = low_ref.shape[0], slope_ref.shape[0]
    half = D // 2
    hidden = mul_bt(low_ref[...], wd_ref[...])
    wide = jnp.broadcast_to(hidden[:, None, :], (count, TXT_LEN, TILE)).reshape(rows, TILE)
    inner = (wide * slope_ref[...].astype(f32)).astype(bf16)
    weight = mul(lhs_ref[0], inner).astype(bf16)

    @pl.when(step < pl.num_programs(0) // 2)
    def _():
        keep_a[...] = weight[:half]
        send_a[...] = weight[half:]

    @pl.when(step >= pl.num_programs(0) // 2)
    def _():
        keep_b[...] = weight[:half]
        send_b[...] = weight[half:]

    added = mul_bt(inner, wu_ref[...])

    @pl.when(step == 0)
    def _():
        acc[...] = added

    @pl.when(step > 0)
    def _():
        acc[...] += added

    @pl.when(step == pl.num_programs(0) - 1)
    def _():
        chunk = 128
        per = chunk // TXT_LEN
        gain = gain_ref[...]
        gain_out[...] = jnp.zeros_like(gain_out)
        bias_out[...] = jnp.zeros_like(bias_out)

        @pl.loop(0, rows // chunk)
        def _(k):
            at = pl.ds(pl.multiple_of(k * chunk, chunk), chunk)
            unit, scale = norm_parts(mid_ref[at, :])
            grad = acc[at, :]
            gain_out[...] += jnp.sum(grad * unit, axis=0, keepdims=True)
            bias_out[...] += jnp.sum(grad, axis=0, keepdims=True)
            row = row_ref[pl.ds(pl.multiple_of(k * per, per), per), :]
            row = jnp.broadcast_to(row[:, None, :], (per, TXT_LEN, D)).reshape(chunk, D)
            out_ref[at, :] = row + norm_back(unit, scale, gain, grad)


def mlp_back(grad_row, grad_low, weight_down, slope, weight_up, lhs, middle, gain):
    rows, count = slope.shape[0], grad_row.shape[0]
    steps = FF // TILE
    fixed = lambda shape: pl.BlockSpec(shape, lambda i: (0, 0))
    first = pl.BlockSpec((D // 2, TILE), lambda i: (0, jnp.minimum(i, steps // 2 - 1)))
    second = pl.BlockSpec((D // 2, TILE), lambda i: (0, jnp.maximum(i - steps // 2, 0)))
    part = jax.ShapeDtypeStruct((D // 2, FF // 2), bf16)
    line = jax.ShapeDtypeStruct((1, D), f32)
    return pl.pallas_call(
        mlp_back_kernel,
        grid=(steps,),
        out_shape=[part] * 4 + [jax.ShapeDtypeStruct((rows, D), f32), line, line],
        in_specs=[
            fixed((count, D)),
            pl.BlockSpec((TILE, D), lambda i: (i, 0)),
            pl.BlockSpec((rows, TILE), lambda i: (0, i)),
            pl.BlockSpec((D, TILE), lambda i: (0, i)),
            pl.BlockSpec((1, D, rows), lambda i: (i // (steps // 2), 0, 0)),
            fixed((rows, D)),
            fixed((1, D)),
            fixed((count, D)),
        ],
        out_specs=[first, first, second, second, fixed((rows, D)), fixed((1, D)), fixed((1, D))],
        scratch_shapes=[pltpu.VMEM((rows, D), f32)],
        compiler_params=params(),
        cost_estimate=cost(4 * rows * D * FF, 4 * D * FF + 2 * rows * FF + 2 * D * FF, rows * FF),
        name="mlp_back",
    )(grad_low, weight_down, slope, weight_up, lhs, middle, gain[None], grad_row)


def attention_back_kernel(grad_ref, wo_ref, qkv_ref, *refs):
    low_ref, out_ref = refs[-2:]
    chunk = grad_ref.shape[0]
    one = same_sequence(chunk, 0, chunk, 0, TXT_LEN)
    mask = jnp.concatenate([one, one], axis=0)
    low = grad_ref[...].astype(bf16)
    low_ref[...] = low
    grad_att = mul_bt(low, wo_ref[...]).astype(bf16)
    for pair in range(HEADS // 2):
        queries = two_heads(qkv_ref[:, pair_cols(0, pair)] * bf16(HEAD ** (-0.5)))
        keys = qkv_ref[:, pair_cols(1, pair)]
        vals = qkv_ref[:, pair_cols(2, pair)]
        grads = two_heads(grad_att[:, pair_cols(0, pair)])
        probs = masked_softmax(mul_bt(queries, keys), mask)
        grad_probs = mul_bt(grads, vals)
        along = jnp.sum(grad_probs * probs, axis=-1, keepdims=True)
        grad_scores = (probs * (grad_probs - along)).astype(bf16)
        side = jnp.concatenate([grad_scores[:chunk], grad_scores[chunk:]], axis=1)
        grad_q = mul(side, two_heads(keys)) * HEAD ** (-0.5)
        grad_k = mul_at(grad_scores, queries)
        grad_v = mul_at(probs.astype(bf16), grads)
        out_ref[:, pair_cols(0, pair)] = grad_q.astype(bf16)
        out_ref[:, pair_cols(1, pair)] = grad_k.astype(bf16)
        out_ref[:, pair_cols(2, pair)] = grad_v.astype(bf16)


def attention_back(grad_middle, weight_out, project, first, count, after=()):
    chunk = 128
    rows = count * chunk
    return pl.pallas_call(
        attention_back_kernel,
        grid=(count,),
        out_shape=[
            jax.ShapeDtypeStruct((rows, D), bf16),
            jax.ShapeDtypeStruct((rows, 3 * D), bf16),
        ],
        in_specs=[
            pl.BlockSpec((chunk, D), lambda i: (i + first, 0)),
            pl.BlockSpec((D, D), lambda i: (0, 0)),
            pl.BlockSpec((chunk, 3 * D), lambda i: (i + first, 0)),
        ]
        + anywhere(after),
        out_specs=[
            pl.BlockSpec((chunk, D), lambda i: (i, 0)),
            pl.BlockSpec((chunk, 3 * D), lambda i: (i, 0)),
        ],
        compiler_params=params(),
        cost_estimate=cost(10 * rows * D * D, 16 * rows * D + 2 * D * D, rows * 128 * HEADS),
        name="attention_back",
    )(grad_middle, weight_out, project, *after)


def mul_rows(lhs, parts):
    total, row = 0.0, 0
    for part in parts:
        total = total + mul(lhs[:, row : row + part.shape[0]], part[...])
        row += part.shape[0]
    return total


def weight_back_kernel(count, lhs_ref, *refs):
    step = pl.program_id(0)
    half = D // 2
    projs, lows = refs[:count], refs[count : 2 * count]
    keep_a, send_a, keep_b, send_b = refs[-4:]

    @pl.when(step < 2)
    def _():
        weight = mul_rows(lhs_ref[0], projs).astype(bf16)
        keep_a[...] = weight[:half]
        send_a[...] = weight[half:]

    @pl.when(step == 2)
    def _():
        weight = mul_rows(lhs_ref[0], projs).astype(bf16)
        keep_b[...] = weight[:half]
        send_b[...] = weight[half:]

    @pl.when(step == 3)
    def _():
        weight = mul_rows(lhs_ref[0], lows).astype(bf16)
        keep_b[...] = weight[:half]
        send_b[...] = weight[half:]


def weight_back(lhs, grad_projs, grad_lows, after=()):
    rows = lhs.shape[2]
    first = pl.BlockSpec((D // 2, D), lambda i: (0, jnp.minimum(i, 1)))
    second = pl.BlockSpec((D // 2, D), lambda i: (0, jnp.maximum(i - 2, 0)))
    return pl.pallas_call(
        functools.partial(weight_back_kernel, len(grad_projs)),
        grid=(4,),
        out_shape=[jax.ShapeDtypeStruct((D // 2, 2 * D), bf16)] * 4,
        in_specs=[pl.BlockSpec((1, D, rows), lambda i: (jnp.maximum(i - 1, 0), 0, 0))]
        + [
            pl.BlockSpec((part.shape[0], D), lambda i: (0, jnp.minimum(i, 2)))
            for part in grad_projs
        ]
        + [pl.BlockSpec((part.shape[0], D), lambda i: (0, 0)) for part in grad_lows]
        + anywhere(after),
        out_specs=[first, first, second, second],
        compiler_params=params(),
        cost_estimate=cost(8 * rows * D * D, 8 * rows * D + 14 * D * D),
        name="weight_back",
    )(lhs, *grad_projs, *grad_lows, *after)


def input_back_kernel(count, *refs):
    projs = refs[:count]
    w_ref, x_ref, gain_ref, mid_ref = refs[count : count + 4]
    out_ref, gain_out, bias_out, acc = refs[-4:]
    step = pl.program_id(0)
    rows, chunk = x_ref.shape[0], 128
    row = 0
    for part in projs:
        at = slice(row, row + part.shape[0])
        row += part.shape[0]
        added = mul_bt(part[...], w_ref[...])

        @pl.when(step == 0)
        def _(at=at, added=added):
            acc[at, :] = added

        @pl.when(step > 0)
        def _(at=at, added=added):
            acc[at, :] += added

    @pl.when(step == pl.num_programs(0) - 1)
    def _():
        gain = gain_ref[...]
        gain_out[...] = jnp.zeros_like(gain_out)
        bias_out[...] = jnp.zeros_like(bias_out)

        @pl.loop(0, rows // chunk)
        def _(k):
            at = pl.ds(pl.multiple_of(k * chunk, chunk), chunk)
            unit, scale = norm_parts(x_ref[at, :].astype(f32))
            grad = acc[at, :]
            gain_out[...] += jnp.sum(grad * unit, axis=0, keepdims=True)
            bias_out[...] += jnp.sum(grad, axis=0, keepdims=True)
            out_ref[at, :] = mid_ref[at, :] + norm_back(unit, scale, gain, grad)


def input_back(grad_projs, weight, rows_in, gain, grad_middle, after=()):
    rows = rows_in.shape[0]
    fixed = lambda shape: pl.BlockSpec(shape, lambda i: (0, 0))
    line = jax.ShapeDtypeStruct((1, D), f32)
    return pl.pallas_call(
        functools.partial(input_back_kernel, len(grad_projs)),
        grid=(3,),
        out_shape=[jax.ShapeDtypeStruct((rows, D), f32), line, line],
        in_specs=[pl.BlockSpec((part.shape[0], D), lambda i: (0, i)) for part in grad_projs]
        + [
            pl.BlockSpec((D, D), lambda i: (0, i)),
            fixed((rows, D)), fixed((1, D)), fixed((rows, D)),
        ]
        + anywhere(after),
        out_specs=[fixed((rows, D)), fixed((1, D)), fixed((1, D))],
        scratch_shapes=[pltpu.VMEM((rows, D), f32)],
        compiler_params=params(),
        cost_estimate=cost(6 * rows * D * D, 14 * rows * D + 6 * D * D),
        name="input_back",
    )(*grad_projs, weight, rows_in, gain[None], grad_middle, *after)


def local(
    images,
    captions,
    img_gain1,
    img_bias1,
    img_qkv,
    img_out,
    img_gain2,
    img_bias2,
    img_up,
    img_down,
    txt_gain1,
    txt_bias1,
    txt_qkv,
    txt_out,
    txt_gain2,
    txt_bias2,
    txt_up,
    txt_down,
    counts,
    matches,
):
    peers = lax.axis_size(AXIS)
    own = lax.axis_index(AXIS)
    per = D // peers
    img_local = counts.shape[0]
    cap_local = matches.shape[0]
    total_images = matches.shape[1]

    shard = jnp.concatenate(
        [
            img_qkv.reshape(per, 3 * D),
            img_out.reshape(per, D),
            img_up.reshape(per, FF),
            img_down.reshape(per, FF),
        ],
        axis=1,
    )
    whole = lax.all_gather(shard, AXIS, axis=0, tiled=True)

    normed1, project, attended, middle, normed2, middle_sum = front(
        TXT_LEN, (128,), 128, captions, txt_gain1, txt_bias1, txt_qkv, txt_out, 0, txt_gain2, txt_bias2
    )
    slope, hidden_sum, text_unit, inverse = text_up(normed2, txt_up, txt_down, middle_sum)
    text_low = text_unit.astype(bf16)

    ends_at = jnp.cumsum(counts)
    slot_ids = lax.iota(jnp.int32, cap_local)
    owner = jnp.sum((ends_at[None, :] <= slot_ids[:, None]).astype(jnp.int32), axis=1)
    owner = owner + own * img_local
    live = slot_ids < ends_at[-1]
    columns = lax.iota(jnp.int32, total_images)
    positive = ((matches > 0) | (owner[:, None] == columns[None, :])) & live[:, None]

    own_pack = jnp.concatenate([text_low, positive.astype(bf16)], axis=1)
    small = peers * cap_local * total_images <= 1 << 20
    if small:
        text_pack = gathered(own_pack).reshape(-1, D + total_images)
        hidden_cols = lax.all_to_all(
            (hidden_sum * inverse[:, :1]).astype(bf16), AXIS, split_axis=1, concat_axis=0, tiled=True
        )

    windows = ((0, 208, 0, 256), (208, 192, 192, 208))
    image_front = front(
        IMG_LEN, windows, 80, images, img_gain1, img_bias1, whole, whole, 3, img_gain2, img_bias2
    )
    image_low = image_up(image_front[4], whole, 4 * D, 4 * D + FF, image_front[5])
    image_all = spread(image_low).reshape(total_images, D)

    order_a, order_b, tail = stage_orders()
    matrix_a, matrix_b = row_order(order_a, tail), row_order(order_b, tail)
    lhs_up = jnp.stack([placed(matrix_a, normed2), placed(matrix_b, normed2)])
    lhs_rest = jnp.stack(
        [placed(matrix_a, normed1), placed(matrix_b, normed1), placed(matrix_b, attended)]
    )

    if small:
        loss_value, grad_row, row_low, col_sum, col_count, live_total = loss_and_rows(
            text_pack, image_all, own_pack, text_unit, inverse
        )
        loss_value = loss_value[0, 0]
    else:
        pos = own_pack[:, D:].astype(f32)
        sums = lax.psum(sums_over_captions(text_low, pos, image_all), AXIS)
        loss_value = loss_from(sums)[0, 0]
        grad = grad_of_unit(text_low, pos, image_all, sums[0], sums[1], sums[4])
        grad_row = inverse[:, :1] * turned(grad, text_unit) * (1.0 / TXT_LEN)
        row_low = grad_row.astype(bf16)

    *up, grad_middle, gain_two, bias_two = mlp_back(
        grad_row, row_low, txt_down, slope, txt_up, lhs_up, middle, txt_gain2
    )
    stages = len(order_a)
    low_one, proj_one = attention_back(grad_middle, txt_out, project, 0, 2)
    for stage in range(stages - 2):
        up = fold(hand_on(up, stage), (proj_one,))
    low_two, proj_two = attention_back(grad_middle, txt_out, project, 2, 3, up)
    up = fold(hand_on(up, stages - 2), (proj_two,))
    rest = weight_back(lhs_rest, (proj_one, proj_two), (low_one, low_two), up)
    up = fold_last(hand_on(up, stages - 1))
    caption_grad, gain_one, bias_one = input_back(
        (proj_one, proj_two), txt_qkv, captions, txt_gain1, grad_middle, [*up, rest[0]]
    )
    for stage in range(stages - 2):
        rest = fold(hand_on(rest, stage), (caption_grad,))
    up_share = sum_last(*hand_on_last(up))
    if small:
        grad_down = grad_of_down(
            text_pack, image_all, col_sum, col_count, live_total, hidden_cols, rest
        )
        rest = fold(hand_on(rest, stages - 2), (grad_down,))
    else:
        grad_down = lax.psum_scatter(
            mul_at(hidden_sum.astype(bf16), row_low), AXIS, scatter_dimension=0, tiled=True
        )
        rest = fold(hand_on(rest, stages - 2))
    rest_share = sum_last(*hand_on_last(fold_last(hand_on(rest, stages - 1))))
    norms = jnp.concatenate([gain_one, bias_one, gain_two, bias_two], axis=0)
    norms = jnp.sum(spread(norms[None]), axis=0).reshape(4, D)
    return (
        loss_value,
        caption_grad,
        norms[0],
        norms[1],
        rest_share[:, : 3 * D].reshape(-1),
        rest_share[:, 3 * D :].reshape(-1),
        norms[2],
        norms[3],
        up_share.reshape(-1),
        grad_down.reshape(-1),
    )


def solution(mesh):
    split, flat, whole = P("blk", None), P("blk"), P()
    image_block = (whole, whole, flat, flat, whole, whole, flat, flat)
    return jax.shard_map(
        local,
        mesh=mesh,
        in_specs=(split, split) + image_block + (whole,) * 8 + (flat, split),
        out_specs=(whole, split, whole, whole, flat, flat, whole, whole, flat, flat),
        check_vma=False,
    )
```

```python
import functools

import jax
import jax.numpy as jnp
from jax import lax
from jax.experimental import pallas as pl
from jax.experimental.pallas import tpu as pltpu
from jax.sharding import PartitionSpec as P

D = 768
FF = 3072
HEAD = 64
HEADS = D // HEAD
IMG_LEN = 50
TXT_LEN = 16
AXIS = "blk"

norm_eps = 1e-06
logit_scale = 50.0
f32 = jnp.float32
bf16 = jnp.bfloat16


def swapped(value, mask):
    peers = lax.axis_size(AXIS)
    return lax.ppermute(value, AXIS, [(i, i ^ mask) for i in range(peers)])


def bit_masks():
    peers = lax.axis_size(AXIS)
    return [1 << k for k in range(peers.bit_length() - 1)]


def gathered(block):
    own = lax.axis_index(AXIS)
    held = block[None]
    for mask in reversed(bit_masks()):
        other = swapped(held, mask)
        upper = (own & mask) > 0
        first = jnp.where(upper, other, held)
        second = jnp.where(upper, held, other)
        held = jnp.stack([first, second], axis=1).reshape((-1,) + block.shape)
    return held


def spread(block):
    peers = lax.axis_size(AXIS)
    copies = jnp.broadcast_to(block[None], (peers,) + block.shape)
    return lax.all_to_all(copies, AXIS, split_axis=0, concat_axis=0, tiled=True)


def stage_orders():
    masks = bit_masks()
    head, tail = masks[:-2], masks[-2:]
    order_a = list(head)
    order_b = list(head)
    for k in range(1, len(head) - 1, 2):
        order_b[k], order_b[k + 1] = order_b[k + 1], order_b[k]
    return order_a, order_b, tail


def row_order(bits):
    peers = lax.axis_size(AXIS)
    own = lax.axis_index(AXIS)
    per = D // peers
    places = lax.iota(jnp.int32, D)
    block = places // per
    target = jnp.zeros_like(block) + own
    for k, mask in enumerate(bits):
        target = target ^ (((block >> (len(bits) - 1 - k)) & 1) * mask)
    source = target * per + places % per
    return (source[:, None] == lax.iota(jnp.int32, D)[None, :]).astype(bf16)


def gathered_line(shard):
    return jnp.concatenate([shard] + [swapped(shard, mask) for mask in (8, 16, 24)], axis=0)


def gathered_rows(line, beside, above):
    half = line.shape[0] // 2
    pieces = [line, beside, above, swapped(beside[:half], 4), swapped(above[half:], 2)]
    return pieces + [swapped(piece, 1) for piece in pieces]


def in_turn(first, then):
    return lax.optimization_barrier((first, then))


def placed(order, values):
    return mul_bt(order, values).astype(bf16)


def hand_on(parts, stage):
    order_a, order_b, _ = stage_orders()
    keep_a, send_a, keep_b, send_b = parts
    return keep_a, swapped(send_a, order_a[stage]), keep_b, swapped(send_b, order_b[stage])


def hand_on_last(blocks):
    low, high = stage_orders()[2]
    own, *others = blocks
    return own, [swapped(block, mask) for block, mask in zip(others, (low, high, low | high))]


def sum_last(own, others):
    total = own
    for other in others:
        total = total + other.astype(f32)
    return total


VMEM_BYTES = 56 << 20
TILE = 512


def norm_parts(values):
    average = jnp.mean(values, axis=-1, keepdims=True)
    centred = values - average
    variance = jnp.mean(centred * centred, axis=-1, keepdims=True)
    scale = lax.rsqrt(variance + norm_eps)
    return centred * scale, scale


def norm_back(unit, scale, gain, grad):
    inner = grad * gain
    shift = jnp.mean(inner, axis=-1, keepdims=True)
    along = jnp.mean(inner * unit, axis=-1, keepdims=True)
    return scale * (inner - shift - unit * along)


def mul(lhs, rhs):
    return jnp.dot(lhs, rhs, preferred_element_type=f32)


def mul_bt(lhs, rhs):
    return lax.dot_general(lhs, rhs, (((1,), (1,)), ((), ())), preferred_element_type=f32)


def mul_at(lhs, rhs):
    return lax.dot_general(lhs, rhs, (((0,), (0,)), ((), ())), preferred_element_type=f32)


def params(**more):
    return pltpu.CompilerParams(vmem_limit_bytes=VMEM_BYTES, **more)


def cost(flops, moved, transcendentals=0):
    return pl.CostEstimate(flops=flops, bytes_accessed=moved, transcendentals=transcendentals)


def lane_halves(dtype):
    lane = lax.broadcasted_iota(jnp.int32, (1, 2 * HEAD), 1)
    low = jnp.where(lane < HEAD, 1.0, 0.0)
    return low.astype(dtype), (1.0 - low).astype(dtype)


def two_heads(pair):
    low, high = lane_halves(bf16)
    return jnp.concatenate([pair * low, pair * high], axis=0)


def same_sequence(rows, row0, cols, col0, seq_len):
    row = (lax.broadcasted_iota(jnp.int32, (rows, cols), 0) + row0) // seq_len
    col = (lax.broadcasted_iota(jnp.int32, (rows, cols), 1) + col0) // seq_len
    return row == col


def masked_softmax(scores, mask):
    scores = jnp.where(mask, scores, -1e30)
    raised = jnp.exp(scores - jnp.max(scores, axis=-1, keepdims=True))
    return raised * (1.0 / jnp.sum(raised, axis=-1, keepdims=True))


def fold_kernel(keep_a, got_a, keep_b, got_b, *refs):
    outs = refs[-4:]
    half = outs[0].shape[0]
    for k, (kept, got) in enumerate(((keep_a, got_a), (keep_b, got_b))):
        for j in range(2):
            at = slice(j * half, (j + 1) * half)
            outs[2 * k + j][...] = (kept[at, :].astype(f32) + got[at, :].astype(f32)).astype(bf16)


def fold(parts, after=()):
    rows, cols = parts[0].shape
    if rows % 32:
        whole = [
            (kept.astype(f32) + got.astype(f32)).astype(bf16)
            for kept, got in (parts[:2], parts[2:])
        ]
        return [part for one in whole for part in (one[: rows // 2], one[rows // 2 :])]
    tile = 512
    return pl.pallas_call(
        fold_kernel,
        grid=(cols // tile,),
        out_shape=[jax.ShapeDtypeStruct((rows // 2, cols), bf16)] * 4,
        in_specs=[pl.BlockSpec((rows, tile), lambda i: (0, i))] * 4 + anywhere(after),
        out_specs=[pl.BlockSpec((rows // 2, tile), lambda i: (0, i))] * 4,
        compiler_params=params(),
        cost_estimate=cost(2 * rows * cols, 12 * rows * cols),
        name="fold",
    )(*parts, *after)


def fold_last_kernel(keep_a, got_a, keep_b, got_b, *refs):
    own_ref, *outs = refs[-4:]
    rows = own_ref.shape[0]
    cols = keep_a.shape[1]
    for k, (kept, got) in enumerate(((keep_a, got_a), (keep_b, got_b))):
        total = kept[...].astype(f32) + got[...].astype(f32)
        at = slice(k * cols, (k + 1) * cols)
        own_ref[:, at] = total[:rows]
        for j, out in enumerate(outs):
            out[:, at] = total[(j + 1) * rows : (j + 2) * rows].astype(bf16)


def fold_last(parts, after=()):
    rows, cols = parts[0].shape
    shape = (rows // 4, 2 * cols)
    if rows % 32:
        pairs = (parts[:2], parts[2:])
        both = [kept.astype(f32) + got.astype(f32) for kept, got in pairs]
        own, *others = jnp.split(jnp.concatenate(both, axis=1), 4)
        return [own] + [other.astype(bf16) for other in others]
    return pl.pallas_call(
        fold_last_kernel,
        out_shape=[jax.ShapeDtypeStruct(shape, f32)] + [jax.ShapeDtypeStruct(shape, bf16)] * 3,
        in_specs=[pl.BlockSpec(memory_space=pltpu.VMEM)] * 4 + anywhere(after),
        compiler_params=params(),
        cost_estimate=cost(2 * rows * cols, 12 * rows * cols),
        name="fold_last",
    )(*parts, *after)


def anywhere(after):
    return [pl.BlockSpec(memory_space=pl.ANY)] * len(after)


def pair_cols(part, pair):
    start = part * D + pair * 2 * HEAD
    return slice(start, start + 2 * HEAD)


def norm_rows(src, dst, gain, bias, step_rows):
    @pl.loop(0, src.shape[0] // step_rows)
    def _(step):
        at = pl.ds(pl.multiple_of(step * step_rows, step_rows), step_rows)
        unit, _ = norm_parts(src[at, :].astype(f32))
        dst[at, :] = (unit * gain + bias).astype(bf16)


def attend(qkv_ref, att_ref, q_rows, k_rows, mask):
    low, high = lane_halves(f32)
    for pair in range(HEADS // 2):
        queries = two_heads(qkv_ref[q_rows, pair_cols(0, pair)] * bf16(HEAD ** (-0.5)))
        scores = mul_bt(queries, qkv_ref[k_rows, pair_cols(1, pair)])
        probs = masked_softmax(scores, mask).astype(bf16)
        half = probs.shape[0] // 2
        mixed = mul(probs, qkv_ref[k_rows, pair_cols(2, pair)])
        att_ref[q_rows, pair_cols(0, pair)] = (mixed[:half] * low + mixed[half:] * high).astype(bf16)


def twice(mask):
    return jnp.concatenate([mask, mask], axis=0)


def text_front_kernel(
    x_ref, g1_ref, b1_ref, wqkv_ref, wo_ref, g2_ref, b2_ref, h1_ref, qkv_ref, att_ref, mid_ref,
    h2_ref, sum_ref
):
    rows, chunk = x_ref.shape[0], 128
    norm_rows(x_ref, h1_ref, g1_ref[...], b1_ref[...], chunk)

    @pl.loop(0, 3 * D // 256)
    def _(step):
        at = pl.ds(pl.multiple_of(step * 256, 256), 256)
        qkv_ref[:, at] = mul(h1_ref[...], wqkv_ref[:, at]).astype(bf16)

    mask = twice(same_sequence(chunk, 0, chunk, 0, TXT_LEN))

    @pl.loop(0, rows // chunk)
    def _(step):
        at = pl.ds(pl.multiple_of(step * chunk, chunk), chunk)
        attend(qkv_ref, att_ref, at, at, mask)

    @pl.loop(0, D // 256)
    def _(step):
        at = pl.ds(pl.multiple_of(step * 256, 256), 256)
        mid_ref[:, at] = x_ref[:, at].astype(f32) + mul(att_ref[...], wo_ref[:, at])

    norm_rows(mid_ref, h2_ref, g2_ref[...], b2_ref[...], chunk)
    per = chunk // TXT_LEN

    @pl.loop(0, rows // chunk)
    def _(step):
        values = mid_ref[pl.ds(pl.multiple_of(step * chunk, chunk), chunk), :]
        sum_ref[pl.ds(pl.multiple_of(step * per, per), per), :] = jnp.sum(
            values.reshape(per, TXT_LEN, D), axis=1
        )


def text_front(rows_in, gain1, bias1, wqkv, wo, gain2, bias2):
    rows = rows_in.shape[0]
    shapes = [
        ((rows, D), bf16),
        ((rows, 3 * D), bf16),
        ((rows, D), bf16),
        ((rows, D), f32),
        ((rows, D), bf16),
        ((rows // TXT_LEN, D), f32),
    ]
    return pl.pallas_call(
        text_front_kernel,
        out_shape=[jax.ShapeDtypeStruct(*item) for item in shapes],
        compiler_params=params(),
        cost_estimate=cost(rows * D * D * 8, 14 * D * rows + 8 * D * D, rows * 128 * HEADS),
        name="text_front",
    )(rows_in, gain1[None], bias1[None], wqkv, wo, gain2[None], bias2[None])


def image_front_kernel(
    windows, x_ref, perm_ref, g1_ref, b1_ref, g2_ref, b2_ref, *refs
):
    h2_ref, sum_ref, w_ref, h1_ref, placed_ref, qkv_ref, att_ref, mid_ref, sems = refs[-9:]
    rows, chunk = x_ref.shape[0], 80
    copies, row = [], 0
    for k, piece in enumerate(refs[:-9]):
        place = w_ref.at[pl.ds(row, piece.shape[0]), :]
        copies.append(pltpu.make_async_copy(piece, place, sems.at[k]))
        row += piece.shape[0]
    for copy in copies:
        copy.start()

    def place_columns(src):
        @pl.loop(0, D // 256)
        def _(step):
            at = pl.ds(pl.multiple_of(step * 256, 256), 256)
            placed_ref[:, at] = mul_bt(src[...], perm_ref[at, :]).astype(bf16)

    norm_rows(x_ref, h1_ref, g1_ref[...].astype(f32), b1_ref[...].astype(f32), chunk)
    place_columns(h1_ref)
    for copy in copies:
        copy.wait()

    @pl.loop(0, 3 * D // 256)
    def _(step):
        at = pl.ds(pl.multiple_of(step * 256, 256), 256)
        qkv_ref[:, at] = mul(placed_ref[...], w_ref[:, at]).astype(bf16)

    for row0, count, key0, keys in windows:
        mask = twice(same_sequence(count, row0, keys, key0, IMG_LEN))
        attend(qkv_ref, att_ref, pl.ds(row0, count), pl.ds(key0, keys), mask)
    place_columns(att_ref)

    @pl.loop(0, D // 256)
    def _(step):
        at = pl.ds(pl.multiple_of(step * 256, 256), 256)
        there = pl.ds(pl.multiple_of(step * 256 + 3 * D, 256), 256)
        mid_ref[:, at] = x_ref[:, at].astype(f32) + mul(placed_ref[...], w_ref[:, there])

    norm_rows(mid_ref, h2_ref, g2_ref[...].astype(f32), b2_ref[...].astype(f32), chunk)
    for k in range(rows // IMG_LEN):
        first, last = k * IMG_LEN, (k + 1) * IMG_LEN
        start, end = first // 8 * 8, -(-last // 8) * 8
        values = mid_ref[start:end, :]
        place = lax.broadcasted_iota(jnp.int32, values.shape, 0) + start
        inside = (place >= first) & (place < last)
        sum_ref[k : k + 1, :] = jnp.sum(jnp.where(inside, values, 0.0), axis=0, keepdims=True)


def image_front(rows_in, pieces, perm, gain1, bias1, gain2, bias2):
    rows = rows_in.shape[0]
    windows = ((0, 208, 0, 256), (208, 192, 192, 208))
    vmem = pl.BlockSpec(memory_space=pltpu.VMEM)
    return pl.pallas_call(
        functools.partial(image_front_kernel, windows),
        out_shape=[
            jax.ShapeDtypeStruct((rows, D), bf16),
            jax.ShapeDtypeStruct((rows // IMG_LEN, D), f32),
        ],
        in_specs=[vmem] * 6 + anywhere(pieces),
        out_specs=[vmem] * 2,
        scratch_shapes=[
            pltpu.VMEM((D, 4 * D), bf16),
            pltpu.VMEM((rows, D), bf16),
            pltpu.VMEM((rows, D), bf16),
            pltpu.VMEM((rows, 3 * D), bf16),
            pltpu.VMEM((rows, D), bf16),
            pltpu.VMEM((rows, D), f32),
            pltpu.SemaphoreType.DMA((len(pieces),)),
        ],
        compiler_params=params(),
        cost_estimate=cost(rows * D * D * 12, 8 * D * D, rows * 256 * HEADS),
        name="image_front",
    )(rows_in, perm, gain1[None], bias1[None], gain2[None], bias2[None], *pieces)


def gelu_parts(inner):
    half = 0.5 * (1.0 + lax.erf(inner * (0.5**0.5)))
    return inner * half, half


def pack_kernel(unit_ref, pos_ref, *refs):
    refs[-1][:, :D] = unit_ref[...].astype(bf16)
    refs[-1][:, D:] = pos_ref[...]


def packed(unit, positive, after):
    shape = (unit.shape[0], D + positive.shape[1])
    return pl.pallas_call(
        pack_kernel,
        out_shape=jax.ShapeDtypeStruct(shape, bf16),
        in_specs=[pl.BlockSpec(memory_space=pltpu.VMEM)] * 2 + anywhere(after),
        compiler_params=params(),
        cost_estimate=cost(shape[0] * shape[1], 4 * shape[0] * shape[1]),
        name="packed",
    )(unit, positive, *after)


def pool_matrix(count, rows, row0, seq_len):
    row = (lax.broadcasted_iota(jnp.int32, (count, rows), 1) + row0) // seq_len
    return jnp.where(row == lax.broadcasted_iota(jnp.int32, (count, rows), 0), 1.0, 0.0).astype(bf16)


def two_terms(mean):
    high = mean.astype(bf16)
    low = (mean - high.astype(f32)).astype(bf16)
    return jnp.concatenate([high, low], axis=0)


def unit_rows(pooled):
    inverse = lax.rsqrt(jnp.sum(pooled * pooled, axis=-1, keepdims=True) + norm_eps)
    return pooled * inverse, inverse


def text_up_kernel(h2_ref, wu_ref, wd_ref, sum_ref, *refs):
    slope_ref, hid_ref, unit_ref, inv_ref, acc = refs[-5:]
    step = pl.program_id(0)
    chunk = 128
    per = chunk // TXT_LEN
    pool = pool_matrix(per, chunk, 0, TXT_LEN)
    for k in range(h2_ref.shape[0] // chunk):
        inner = mul(h2_ref[k * chunk : (k + 1) * chunk, :], wu_ref[...])
        value, half = gelu_parts(inner)
        slope = half + inner * (jnp.exp(-0.5 * inner * inner) * 0.3989422804014327)
        slope_ref[k * chunk : (k + 1) * chunk, :] = slope.astype(bf16)
        hid_ref[k * per : (k + 1) * per, :] = mul(pool, value.astype(bf16))
    terms = mul(two_terms(hid_ref[...] * (1.0 / TXT_LEN)), wd_ref[...])
    count = hid_ref.shape[0]
    added = terms[:count] + terms[count:]

    @pl.when(step == 0)
    def _():
        acc[...] = sum_ref[...] * (1.0 / TXT_LEN) + added

    @pl.when(step > 0)
    def _():
        acc[...] += added

    @pl.when(step == pl.num_programs(0) - 1)
    def _():
        unit, inverse = unit_rows(acc[...])
        unit_ref[...] = unit
        inv_ref[...] = jnp.broadcast_to(inverse, inv_ref.shape)


def text_up(normed2, weight_up, weight_down, middle_sum, after=()):
    rows, count = normed2.shape[0], middle_sum.shape[0]
    fixed = lambda shape: pl.BlockSpec(shape, lambda i: (0, 0))
    return pl.pallas_call(
        text_up_kernel,
        grid=(FF // TILE,),
        out_shape=[
            jax.ShapeDtypeStruct((rows, FF), bf16),
            jax.ShapeDtypeStruct((count, FF), f32),
            jax.ShapeDtypeStruct((count, D), f32),
            jax.ShapeDtypeStruct((count, 128), f32),
        ],
        in_specs=[
            fixed((rows, D)),
            pl.BlockSpec((D, TILE), lambda i: (0, i)),
            pl.BlockSpec((TILE, D), lambda i: (i, 0)),
            fixed((count, D)),
        ]
        + anywhere(after),
        out_specs=[
            pl.BlockSpec((rows, TILE), lambda i: (0, i)),
            pl.BlockSpec((count, TILE), lambda i: (0, i)),
            fixed((count, D)),
            fixed((count, 128)),
        ],
        scratch_shapes=[pltpu.VMEM((count, D), f32)],
        compiler_params=params(),
        cost_estimate=cost(2 * rows * D * FF, 4 * D * FF + 2 * rows * FF, 20 * rows * FF),
        name="text_up",
    )(normed2, weight_up, weight_down, middle_sum, *after)


def image_up_kernel(fold, h2_ref, wu_ref, wd_ref, sum_ref, *refs):
    out_ref, acc = refs[-2:]
    step = pl.program_id(0)
    rows, count = h2_ref.shape[0], sum_ref.shape[0]
    chunk = 80
    summed = jnp.zeros((count, TILE), f32)
    for k in range(rows // chunk):
        inner = mul(h2_ref[k * chunk : (k + 1) * chunk, :], wu_ref[...])
        value, _ = gelu_parts(inner)
        pool = pool_matrix(count, chunk, k * chunk, IMG_LEN)
        summed = summed + mul(pool, value.astype(bf16))
    mean = two_terms(summed * (1.0 / IMG_LEN))
    place = lax.broadcasted_iota(jnp.int32, (TILE, TILE // fold), 0)
    picked = lax.broadcasted_iota(jnp.int32, (TILE, TILE // fold), 1) * fold
    terms = jnp.zeros((2 * count, D), f32)
    for k in range(fold):
        chosen = jnp.where(place == picked + k, 1.0, 0.0).astype(bf16)
        part = mul(mean, chosen).astype(bf16)
        terms = terms + mul(part, wd_ref[:, k * D : (k + 1) * D])
    added = terms[:count] + terms[count:]

    @pl.when(step == 0)
    def _():
        acc[...] = sum_ref[...] * (1.0 / IMG_LEN) + added

    @pl.when(step > 0)
    def _():
        acc[...] += added

    @pl.when(step == pl.num_programs(0) - 1)
    def _():
        out_ref[...] = unit_rows(acc[...])[0].astype(bf16)


def image_up(normed2, whole, up_col, down_col, middle_sum, after=()):
    rows, count = normed2.shape[0], middle_sum.shape[0]
    fold = FF // D
    fixed = lambda shape: pl.BlockSpec(shape, lambda i: (0, 0))
    return pl.pallas_call(
        functools.partial(image_up_kernel, fold),
        grid=(FF // TILE,),
        out_shape=jax.ShapeDtypeStruct((count, D), bf16),
        in_specs=[
            fixed((rows, D)),
            pl.BlockSpec((D, TILE), lambda i: (0, up_col // TILE + i)),
            pl.BlockSpec((TILE // fold, fold * D), lambda i: (i, down_col // (fold * D))),
            fixed((count, D)),
        ]
        + anywhere(after),
        out_specs=fixed((count, D)),
        scratch_shapes=[pltpu.VMEM((count, D), f32)],
        compiler_params=params(),
        cost_estimate=cost(2 * rows * D * FF, 4 * D * FF, 15 * rows * FF),
        name="image_up",
    )(normed2, whole, whole, middle_sum, *after)


def loss_parts(text_rows, pos, image_all):
    similar = mul_bt(text_rows, image_all) * logit_scale
    shifted = jnp.exp(similar - logit_scale)
    alive = jnp.max(pos, axis=1, keepdims=True)
    row_sum = jnp.sum(shifted, axis=1, keepdims=True)
    row_count = jnp.maximum(jnp.sum(pos, axis=1, keepdims=True), 1.0)
    return similar, shifted, alive, row_sum, row_count


def sums_over_captions(text_rows, pos, image_all):
    similar, shifted, alive, row_sum, row_count = loss_parts(text_rows, pos, image_all)
    pos_similar = pos * similar
    cap_term = alive * (
        logit_scale + jnp.log(row_sum) - jnp.sum(pos_similar, axis=1, keepdims=True) / row_count
    )
    return (
        jnp.sum(alive * shifted, axis=0, keepdims=True),
        jnp.sum(pos, axis=0, keepdims=True),
        jnp.sum(pos_similar, axis=0, keepdims=True),
        jnp.sum(cap_term, axis=0, keepdims=True),
        jnp.sum(alive, axis=0, keepdims=True),
    )


def loss_from(sums):
    col_sum, col_count, col_pos, cap_total, live_total = sums
    img_term = logit_scale + jnp.log(col_sum) - col_pos / col_count
    return 0.5 * cap_total / live_total + 0.5 * jnp.mean(img_term, axis=1, keepdims=True)


def grad_of_unit(text_rows, pos, image_all, col_sum, col_count, live_total):
    _, shifted, alive, row_sum, row_count = loss_parts(text_rows, pos, image_all)
    cap_share, img_share = 0.5 / live_total, 0.5 / image_all.shape[0]
    grad_sims = alive * shifted * (cap_share / row_sum + img_share / col_sum) - pos * (
        cap_share / row_count + img_share / col_count
    )
    return mul(grad_sims.astype(bf16), image_all) * logit_scale


def turned(grad, unit):
    return grad - unit * jnp.sum(grad * unit, axis=-1, keepdims=True)


def loss_kernel(
    pack_ref, image_ref, own_ref, unit_ref, inv_ref, loss_ref, row_ref, low_ref, col_sum_ref,
    col_count_ref, live_ref
):
    image_all = image_ref[...]
    chunk = 256
    total = None
    for k in range(pack_ref.shape[0] // chunk):
        at = slice(k * chunk, (k + 1) * chunk)
        part = sums_over_captions(pack_ref[at, :D], pack_ref[at, D:].astype(f32), image_all)
        total = part if total is None else [a + b for a, b in zip(total, part)]
    loss_ref[...] = jnp.broadcast_to(loss_from(total), loss_ref.shape)
    col_sum, col_count, _, _, live_total = total
    col_sum_ref[...] = col_sum
    col_count_ref[...] = col_count
    live_ref[...] = jnp.broadcast_to(live_total, live_ref.shape)
    grad = grad_of_unit(
        own_ref[:, :D], own_ref[:, D:].astype(f32), image_all, col_sum, col_count, live_total
    )
    row = inv_ref[:, :1] * turned(grad, unit_ref[...]) * (1.0 / TXT_LEN)
    row_ref[...] = row
    low_ref[...] = row.astype(bf16)


def loss_and_rows(pack, image_all, own_pack, unit, inverse):
    images, count = image_all.shape[0], own_pack.shape[0]
    shapes = [(1, 128), (count, D), (count, D), (1, images), (1, images), (1, 128)]
    kinds = [f32, f32, bf16, f32, f32, f32]
    return pl.pallas_call(
        loss_kernel,
        out_shape=[jax.ShapeDtypeStruct(*item) for item in zip(shapes, kinds)],
        compiler_params=params(),
        cost_estimate=cost(2 * pack.shape[0] * images * D, 2 * pack.size, pack.shape[0] * images),
        name="loss_and_rows",
    )(pack, image_all, own_pack, unit, inverse)


def down_kernel(pack_ref, image_ref, col_sum_ref, col_count_ref, live_ref, hid_ref, *refs):
    step, out_ref = pl.program_id(0), refs[-1]
    text_rows = pack_ref[:, :D]
    grad = grad_of_unit(
        text_rows, pack_ref[:, D:].astype(f32), image_ref[...], col_sum_ref[...],
        col_count_ref[...], live_ref[:, :1]
    )
    rows = (turned(grad, text_rows.astype(f32)) * (1.0 / TXT_LEN)).astype(bf16)
    part = mul_at(hid_ref[...], rows)

    @pl.when(step == 0)
    def _():
        out_ref[...] = part

    @pl.when(step > 0)
    def _():
        out_ref[...] += part


def grad_of_down(pack, image_all, col_sum, col_count, live_total, hidden_cols, after):
    images, chunk = image_all.shape[0], 256
    fixed = lambda shape: pl.BlockSpec(shape, lambda i: (0, 0))
    per = hidden_cols.shape[1]
    return pl.pallas_call(
        down_kernel,
        grid=(pack.shape[0] // chunk,),
        out_shape=jax.ShapeDtypeStruct((per, D), f32),
        in_specs=[
            pl.BlockSpec((chunk, pack.shape[1]), lambda i: (i, 0)),
            fixed((images, D)), fixed((1, images)), fixed((1, images)), fixed((1, 128)),
            pl.BlockSpec((chunk, per), lambda i: (i, 0)),
        ]
        + anywhere(after),
        out_specs=fixed((per, D)),
        compiler_params=params(),
        cost_estimate=cost(4 * pack.shape[0] * images * D, 2 * pack.size, pack.shape[0] * images),
        name="grad_of_down",
    )(pack, image_all, col_sum, col_count, live_total, hidden_cols, *after)


def mlp_back_kernel(
    low_ref, wd_ref, slope_ref, wu_ref, lhs_ref, mid_ref, gain_ref, row_ref, keep_a, send_a, keep_b,
    send_b, out_ref, gain_out, bias_out, acc
):
    step = pl.program_id(0)
    count, rows = low_ref.shape[0], slope_ref.shape[0]
    half = D // 2
    hidden = mul_bt(low_ref[...], wd_ref[...])
    wide = jnp.broadcast_to(hidden[:, None, :], (count, TXT_LEN, TILE)).reshape(rows, TILE)
    inner = (wide * slope_ref[...].astype(f32)).astype(bf16)
    weight = mul(lhs_ref[0], inner).astype(bf16)

    @pl.when(step < pl.num_programs(0) // 2)
    def _():
        keep_a[...] = weight[:half]
        send_a[...] = weight[half:]

    @pl.when(step >= pl.num_programs(0) // 2)
    def _():
        keep_b[...] = weight[:half]
        send_b[...] = weight[half:]

    added = mul_bt(inner, wu_ref[...])

    @pl.when(step == 0)
    def _():
        acc[...] = added

    @pl.when(step > 0)
    def _():
        acc[...] += added

    @pl.when(step == pl.num_programs(0) - 1)
    def _():
        chunk = 128
        per = chunk // TXT_LEN
        gain = gain_ref[...]
        gain_out[...] = jnp.zeros_like(gain_out)
        bias_out[...] = jnp.zeros_like(bias_out)

        @pl.loop(0, rows // chunk)
        def _(k):
            at = pl.ds(pl.multiple_of(k * chunk, chunk), chunk)
            unit, scale = norm_parts(mid_ref[at, :])
            grad = acc[at, :]
            gain_out[...] += jnp.sum(grad * unit, axis=0, keepdims=True)
            bias_out[...] += jnp.sum(grad, axis=0, keepdims=True)
            row = row_ref[pl.ds(pl.multiple_of(k * per, per), per), :]
            row = jnp.broadcast_to(row[:, None, :], (per, TXT_LEN, D)).reshape(chunk, D)
            out_ref[at, :] = row + norm_back(unit, scale, gain, grad)


def mlp_back(grad_row, grad_low, weight_down, slope, weight_up, lhs, middle, gain):
    rows, count = slope.shape[0], grad_row.shape[0]
    steps = FF // TILE
    fixed = lambda shape: pl.BlockSpec(shape, lambda i: (0, 0))
    first = pl.BlockSpec((D // 2, TILE), lambda i: (0, jnp.minimum(i, steps // 2 - 1)))
    second = pl.BlockSpec((D // 2, TILE), lambda i: (0, jnp.maximum(i - steps // 2, 0)))
    part = jax.ShapeDtypeStruct((D // 2, FF // 2), bf16)
    line = jax.ShapeDtypeStruct((1, D), f32)
    return pl.pallas_call(
        mlp_back_kernel,
        grid=(steps,),
        out_shape=[part] * 4 + [jax.ShapeDtypeStruct((rows, D), f32), line, line],
        in_specs=[
            fixed((count, D)),
            pl.BlockSpec((TILE, D), lambda i: (i, 0)),
            pl.BlockSpec((rows, TILE), lambda i: (0, i)),
            pl.BlockSpec((D, TILE), lambda i: (0, i)),
            pl.BlockSpec((1, D, rows), lambda i: (i // (steps // 2), 0, 0)),
            fixed((rows, D)),
            fixed((1, D)),
            fixed((count, D)),
        ],
        out_specs=[first, first, second, second, fixed((rows, D)), fixed((1, D)), fixed((1, D))],
        scratch_shapes=[pltpu.VMEM((rows, D), f32)],
        compiler_params=params(),
        cost_estimate=cost(4 * rows * D * FF, 4 * D * FF + 2 * rows * FF + 2 * D * FF, rows * FF),
        name="mlp_back",
    )(grad_low, weight_down, slope, weight_up, lhs, middle, gain[None], grad_row)


def attention_back_kernel(grad_ref, wo_ref, qkv_ref, *refs):
    low_ref, out_ref = refs[-2:]
    chunk = grad_ref.shape[0]
    one = same_sequence(chunk, 0, chunk, 0, TXT_LEN)
    mask = jnp.concatenate([one, one], axis=0)
    low = grad_ref[...].astype(bf16)
    low_ref[...] = low
    grad_att = mul_bt(low, wo_ref[...]).astype(bf16)
    for pair in range(HEADS // 2):
        queries = two_heads(qkv_ref[:, pair_cols(0, pair)] * bf16(HEAD ** (-0.5)))
        keys = qkv_ref[:, pair_cols(1, pair)]
        vals = qkv_ref[:, pair_cols(2, pair)]
        grads = two_heads(grad_att[:, pair_cols(0, pair)])
        probs = masked_softmax(mul_bt(queries, keys), mask)
        grad_probs = mul_bt(grads, vals)
        along = jnp.sum(grad_probs * probs, axis=-1, keepdims=True)
        grad_scores = (probs * (grad_probs - along)).astype(bf16)
        side = jnp.concatenate([grad_scores[:chunk], grad_scores[chunk:]], axis=1)
        grad_q = mul(side, two_heads(keys)) * HEAD ** (-0.5)
        grad_k = mul_at(grad_scores, queries)
        grad_v = mul_at(probs.astype(bf16), grads)
        out_ref[:, pair_cols(0, pair)] = grad_q.astype(bf16)
        out_ref[:, pair_cols(1, pair)] = grad_k.astype(bf16)
        out_ref[:, pair_cols(2, pair)] = grad_v.astype(bf16)


def attention_back(grad_middle, weight_out, project, first, count, after=()):
    chunk = 128
    rows = count * chunk
    return pl.pallas_call(
        attention_back_kernel,
        grid=(count,),
        out_shape=[
            jax.ShapeDtypeStruct((rows, D), bf16),
            jax.ShapeDtypeStruct((rows, 3 * D), bf16),
        ],
        in_specs=[
            pl.BlockSpec((chunk, D), lambda i: (i + first, 0)),
            pl.BlockSpec((D, D), lambda i: (0, 0)),
            pl.BlockSpec((chunk, 3 * D), lambda i: (i + first, 0)),
        ]
        + anywhere(after),
        out_specs=[
            pl.BlockSpec((chunk, D), lambda i: (i, 0)),
            pl.BlockSpec((chunk, 3 * D), lambda i: (i, 0)),
        ],
        compiler_params=params(),
        cost_estimate=cost(10 * rows * D * D, 16 * rows * D + 2 * D * D, rows * 128 * HEADS),
        name="attention_back",
    )(grad_middle, weight_out, project, *after)


def mul_rows(lhs, parts):
    total, row = 0.0, 0
    for part in parts:
        total = total + mul(lhs[:, row : row + part.shape[0]], part[...])
        row += part.shape[0]
    return total


def weight_back_kernel(counts, lhs_ref, *refs):
    step, half = pl.program_id(0), D // 2
    keep, send = refs[-2:]
    row = 0
    for k, count in enumerate(counts):
        parts = refs[row : row + count]
        row += count

        @pl.when(step == k if len(counts) > 1 else step >= 0)
        def _(parts=parts):
            weight = mul_rows(lhs_ref[0], parts).astype(bf16)
            keep[...] = weight[:half]
            send[...] = weight[half:]


def weight_back(lhs, first, groups, blocks, after=()):
    rows = lhs.shape[2]
    steps = 2
    many = len(groups) > 1
    given = [part for group in groups for part in group]
    return pl.pallas_call(
        functools.partial(weight_back_kernel, [len(group) for group in groups]),
        grid=(steps,),
        out_shape=[jax.ShapeDtypeStruct((D // 2, steps * D), bf16)] * 2,
        in_specs=[pl.BlockSpec((1, D, rows), lambda i: (first + (i if many else 0), 0, 0))]
        + [
            pl.BlockSpec((part.shape[0], D), lambda i, col=col: (0, col + (0 if many else i)))
            for group, col in zip(groups, blocks)
            for part in group
        ]
        + anywhere(after),
        out_specs=[pl.BlockSpec((D // 2, D), lambda i: (0, i))] * 2,
        compiler_params=params(),
        cost_estimate=cost(4 * rows * D * D, 4 * rows * D + 7 * D * D),
        name="weight_back",
    )(lhs, *given, *after)


def input_back_kernel(count, *refs):
    projs = refs[:count]
    w_ref, x_ref, gain_ref, mid_ref = refs[count : count + 4]
    out_ref, gain_out, bias_out, acc = refs[-4:]
    step = pl.program_id(0)
    rows, chunk = x_ref.shape[0], 128
    row = 0
    for part in projs:
        at = slice(row, row + part.shape[0])
        row += part.shape[0]
        added = mul_bt(part[...], w_ref[...])

        @pl.when(step == 0)
        def _(at=at, added=added):
            acc[at, :] = added

        @pl.when(step > 0)
        def _(at=at, added=added):
            acc[at, :] += added

    @pl.when(step == pl.num_programs(0) - 1)
    def _():
        gain = gain_ref[...]
        gain_out[...] = jnp.zeros_like(gain_out)
        bias_out[...] = jnp.zeros_like(bias_out)

        @pl.loop(0, rows // chunk)
        def _(k):
            at = pl.ds(pl.multiple_of(k * chunk, chunk), chunk)
            unit, scale = norm_parts(x_ref[at, :].astype(f32))
            grad = acc[at, :]
            gain_out[...] += jnp.sum(grad * unit, axis=0, keepdims=True)
            bias_out[...] += jnp.sum(grad, axis=0, keepdims=True)
            out_ref[at, :] = mid_ref[at, :] + norm_back(unit, scale, gain, grad)


def input_back(grad_projs, weight, rows_in, gain, grad_middle, after=()):
    rows = rows_in.shape[0]
    fixed = lambda shape: pl.BlockSpec(shape, lambda i: (0, 0))
    line = jax.ShapeDtypeStruct((1, D), f32)
    return pl.pallas_call(
        functools.partial(input_back_kernel, len(grad_projs)),
        grid=(3,),
        out_shape=[jax.ShapeDtypeStruct((rows, D), f32), line, line],
        in_specs=[pl.BlockSpec((part.shape[0], D), lambda i: (0, i)) for part in grad_projs]
        + [
            pl.BlockSpec((D, D), lambda i: (0, i)),
            fixed((rows, D)), fixed((1, D)), fixed((rows, D)),
        ]
        + anywhere(after),
        out_specs=[fixed((rows, D)), fixed((1, D)), fixed((1, D))],
        scratch_shapes=[pltpu.VMEM((rows, D), f32)],
        compiler_params=params(),
        cost_estimate=cost(6 * rows * D * D, 14 * rows * D + 6 * D * D),
        name="input_back",
    )(*grad_projs, weight, rows_in, gain[None], grad_middle, *after)


def local(
    images,
    captions,
    img_gain1,
    img_bias1,
    img_qkv,
    img_out,
    img_gain2,
    img_bias2,
    img_up,
    img_down,
    txt_gain1,
    txt_bias1,
    txt_qkv,
    txt_out,
    txt_gain2,
    txt_bias2,
    txt_up,
    txt_down,
    counts,
    matches,
):
    peers = lax.axis_size(AXIS)
    own = lax.axis_index(AXIS)
    per = D // peers
    img_local = counts.shape[0]
    cap_local = matches.shape[0]
    total_images = matches.shape[1]

    whole = lax.all_gather(
        jnp.concatenate([img_up.reshape(per, FF), img_down.reshape(per, FF)], axis=1),
        AXIS,
        axis=0,
        tiled=True,
    )
    small = peers == 32
    shard = jnp.concatenate([img_qkv.reshape(per, 3 * D), img_out.reshape(per, D)], axis=1)
    if small:
        line, perm = gathered_line(shard), row_order((1, 4, 2, 16, 8))
    else:
        line, perm = lax.all_gather(shard, AXIS, axis=0, tiled=True), jnp.eye(D, dtype=bf16)

    normed1, project, attended, middle, normed2, middle_sum = text_front(
        captions, txt_gain1, txt_bias1, txt_qkv, txt_out, txt_gain2, txt_bias2
    )
    middle_sum, line = in_turn(middle_sum, line)
    beside, above = (swapped(line, 2), swapped(line, 4)) if small else (line, line)
    slope, hidden_sum, text_unit, inverse = text_up(
        normed2, txt_up, txt_down, middle_sum, (line,)
    )
    text_unit, (beside, above) = in_turn(text_unit, (beside, above))
    pieces = gathered_rows(line, beside, above) if small else [line]

    ends_at = jnp.cumsum(counts)
    slot_ids = lax.iota(jnp.int32, cap_local)
    owner = jnp.sum((ends_at[None, :] <= slot_ids[:, None]).astype(jnp.int32), axis=1)
    owner = owner + own * img_local
    live = slot_ids < ends_at[-1]
    columns = lax.iota(jnp.int32, total_images)
    positive = ((matches > 0) | (owner[:, None] == columns[None, :])) & live[:, None]

    own_pack = packed(text_unit, positive.astype(bf16), pieces[1:5])
    if small:
        text_pack = gathered(own_pack).reshape(-1, D + total_images)
        hidden_cols = lax.all_to_all(
            (hidden_sum * inverse[:, :1]).astype(bf16), AXIS, split_axis=1, concat_axis=0, tiled=True
        )

    normed_img, middle_img = image_front(
        images, pieces, perm, img_gain1, img_bias1, img_gain2, img_bias2
    )
    image_low = image_up(
        normed_img, whole, 0, FF, middle_img, (hidden_cols,) if small else ()
    )
    image_all = spread(image_low).reshape(total_images, D)

    order_a, order_b, tail = stage_orders()
    matrix_a, matrix_b = row_order(order_a + tail[::-1]), row_order(order_b + tail[::-1])
    lhs_up = jnp.stack([placed(matrix_a, normed2), placed(matrix_b, normed2)])
    lhs_rest = jnp.stack(
        [placed(matrix_a, normed1), placed(matrix_b, normed1), placed(matrix_b, attended)]
    )

    if small:
        loss_value, grad_row, row_low, col_sum, col_count, live_total = loss_and_rows(
            text_pack, image_all, own_pack, text_unit, inverse
        )
        loss_value = loss_value[0, 0]
    else:
        text_low, pos = own_pack[:, :D], own_pack[:, D:].astype(f32)
        sums = lax.psum(sums_over_captions(text_low, pos, image_all), AXIS)
        loss_value = loss_from(sums)[0, 0]
        grad = grad_of_unit(text_low, pos, image_all, sums[0], sums[1], sums[4])
        grad_row = inverse[:, :1] * turned(grad, text_unit) * (1.0 / TXT_LEN)
        row_low = grad_row.astype(bf16)

    *up, grad_middle, gain_two, bias_two = mlp_back(
        grad_row, row_low, txt_down, slope, txt_up, lhs_up, middle, txt_gain2
    )
    stages = len(order_a)
    low_one, proj_one = attention_back(grad_middle, txt_out, project, 0, 2)
    for stage in range(stages - 2):
        up = fold(hand_on(up, stage), (proj_one,))
    low_two, proj_two = attention_back(grad_middle, txt_out, project, 2, 3, up)
    up = fold(hand_on(up, stages - 2), (proj_two,))
    projs, lows = (proj_one, proj_two), (low_one, low_two)
    rest_a = weight_back(lhs_rest, 0, [projs], [0], up)
    up = fold_last(hand_on(up, stages - 1), rest_a[1:])
    rest_b = weight_back(lhs_rest, 1, [projs, lows], [2, 0], up)
    rest = [*rest_a, *rest_b]
    caption_grad, gain_one, bias_one = input_back(
        projs, txt_qkv, captions, txt_gain1, grad_middle, rest[3:]
    )
    for stage in range(stages - 2):
        rest = fold(hand_on(rest, stage), (caption_grad,))
    up_share = sum_last(*hand_on_last(up))
    if small:
        grad_down = grad_of_down(
            text_pack, image_all, col_sum, col_count, live_total, hidden_cols, rest
        )
        rest = fold(hand_on(rest, stages - 2), (grad_down,))
    else:
        grad_down = lax.psum_scatter(
            mul_at(hidden_sum.astype(bf16), row_low), AXIS, scatter_dimension=0, tiled=True
        )
        rest = fold(hand_on(rest, stages - 2))
    rest_share = sum_last(*hand_on_last(fold_last(hand_on(rest, stages - 1))))
    norms = jnp.concatenate([gain_one, bias_one, gain_two, bias_two], axis=0)
    norms = jnp.sum(spread(norms[None]), axis=0).reshape(4, D)
    return (
        loss_value,
        caption_grad,
        norms[0],
        norms[1],
        rest_share[:, : 3 * D].reshape(-1),
        rest_share[:, 3 * D :].reshape(-1),
        norms[2],
        norms[3],
        up_share.reshape(-1),
        grad_down.reshape(-1),
    )


def solution(mesh):
    split, flat, whole = P("blk", None), P("blk"), P()
    image_block = (whole, whole, flat, flat, whole, whole, flat, flat)
    return jax.shard_map(
        local,
        mesh=mesh,
        in_specs=(split, split) + image_block + (whole,) * 8 + (flat, split),
        out_specs=(whole, split, whole, whole, flat, flat, whole, whole, flat, flat),
        check_vma=False,
    )
```

```python
import functools

import jax
import jax.numpy as jnp
from jax import lax
from jax.experimental import pallas as pl
from jax.experimental.pallas import tpu as pltpu
from jax.sharding import PartitionSpec as P

D = 768
FF = 3072
HEAD = 64
HEADS = D // HEAD
IMG_LEN = 50
TXT_LEN = 16
AXIS = "blk"

norm_eps = 1e-06
logit_scale = 50.0
f32 = jnp.float32
bf16 = jnp.bfloat16


def swapped(value, mask):
    peers = lax.axis_size(AXIS)
    return lax.ppermute(value, AXIS, [(i, i ^ mask) for i in range(peers)])


def bit_masks():
    peers = lax.axis_size(AXIS)
    return [1 << k for k in range(peers.bit_length() - 1)]


def gathered_with(held, mask):
    upper = (lax.axis_index(AXIS) & mask) > 0
    other = swapped(held, mask)
    first = jnp.where(upper, other, held)
    second = jnp.where(upper, held, other)
    return jnp.stack([first, second], axis=1).reshape((-1,) + held.shape[1:])


def spread(block):
    peers = lax.axis_size(AXIS)
    copies = jnp.broadcast_to(block[None], (peers,) + block.shape)
    return lax.all_to_all(copies, AXIS, split_axis=0, concat_axis=0, tiled=True)


def stage_orders():
    masks = bit_masks()
    head, tail = masks[:-2], masks[-2:]
    order_a = list(head)
    order_b = list(head)
    for k in range(1, len(head) - 1, 2):
        order_b[k], order_b[k + 1] = order_b[k + 1], order_b[k]
    return order_a, order_b, tail


def row_order(bits):
    peers = lax.axis_size(AXIS)
    own = lax.axis_index(AXIS)
    per = D // peers
    places = lax.iota(jnp.int32, D)
    block = places // per
    target = jnp.zeros_like(block) + own
    for k, mask in enumerate(bits):
        target = target ^ (((block >> (len(bits) - 1 - k)) & 1) * mask)
    source = target * per + places % per
    return (source[:, None] == lax.iota(jnp.int32, D)[None, :]).astype(bf16)


def gathered_line(shard):
    return jnp.concatenate([shard] + [swapped(shard, mask) for mask in (8, 16, 24)], axis=0)


def gathered_rows(line, beside, above):
    half = line.shape[0] // 2
    pieces = [line, beside, above, swapped(beside[:half], 4), swapped(above[half:], 2)]
    return pieces + [swapped(piece, 1) for piece in pieces]


def in_turn(first, then):
    return lax.optimization_barrier((first, then))


def placed(order, values):
    return mul_bt(order, values).astype(bf16)


def hand_on(parts, stage):
    order_a, order_b, _ = stage_orders()
    keep_a, send_a, keep_b, send_b = parts
    return keep_a, swapped(send_a, order_a[stage]), keep_b, swapped(send_b, order_b[stage])


def hand_on_last(blocks):
    low, high = stage_orders()[2]
    own, *others = blocks
    return own, [swapped(block, mask) for block, mask in zip(others, (low, high, low | high))]


def sum_last(own, others):
    total = own
    for other in others:
        total = total + other.astype(f32)
    return total


VMEM_BYTES = 56 << 20
TILE = 512


def norm_parts(values):
    average = jnp.mean(values, axis=-1, keepdims=True)
    centred = values - average
    variance = jnp.mean(centred * centred, axis=-1, keepdims=True)
    scale = lax.rsqrt(variance + norm_eps)
    return centred * scale, scale


def norm_back(unit, scale, gain, grad):
    inner = grad * gain
    shift = jnp.mean(inner, axis=-1, keepdims=True)
    along = jnp.mean(inner * unit, axis=-1, keepdims=True)
    return scale * (inner - shift - unit * along)


def mul(lhs, rhs):
    return jnp.dot(lhs, rhs, preferred_element_type=f32)


def mul_bt(lhs, rhs):
    return lax.dot_general(lhs, rhs, (((1,), (1,)), ((), ())), preferred_element_type=f32)


def mul_at(lhs, rhs):
    return lax.dot_general(lhs, rhs, (((0,), (0,)), ((), ())), preferred_element_type=f32)


def params(**more):
    return pltpu.CompilerParams(vmem_limit_bytes=VMEM_BYTES, **more)


def cost(flops, moved, transcendentals=0):
    return pl.CostEstimate(flops=flops, bytes_accessed=moved, transcendentals=transcendentals)


def lane_halves(dtype):
    lane = lax.broadcasted_iota(jnp.int32, (1, 2 * HEAD), 1)
    low = jnp.where(lane < HEAD, 1.0, 0.0)
    return low.astype(dtype), (1.0 - low).astype(dtype)


def two_heads(pair):
    low, high = lane_halves(bf16)
    return jnp.concatenate([pair * low, pair * high], axis=0)


def same_sequence(rows, row0, cols, col0, seq_len):
    row = (lax.broadcasted_iota(jnp.int32, (rows, cols), 0) + row0) // seq_len
    col = (lax.broadcasted_iota(jnp.int32, (rows, cols), 1) + col0) // seq_len
    return row == col


def masked_softmax(scores, mask):
    scores = jnp.where(mask, scores, -1e30)
    raised = jnp.exp(scores - jnp.max(scores, axis=-1, keepdims=True))
    return raised * (1.0 / jnp.sum(raised, axis=-1, keepdims=True))


def fold_kernel(keep_a, got_a, keep_b, got_b, *refs):
    outs = refs[-4:]
    half = outs[0].shape[0]
    for k, (kept, got) in enumerate(((keep_a, got_a), (keep_b, got_b))):
        for j in range(2):
            at = slice(j * half, (j + 1) * half)
            outs[2 * k + j][...] = (kept[at, :].astype(f32) + got[at, :].astype(f32)).astype(bf16)


def fold(parts, after=()):
    rows, cols = parts[0].shape
    if rows % 32:
        whole = [
            (kept.astype(f32) + got.astype(f32)).astype(bf16)
            for kept, got in (parts[:2], parts[2:])
        ]
        return [part for one in whole for part in (one[: rows // 2], one[rows // 2 :])]
    tile = 512
    return pl.pallas_call(
        fold_kernel,
        grid=(cols // tile,),
        out_shape=[jax.ShapeDtypeStruct((rows // 2, cols), bf16)] * 4,
        in_specs=[pl.BlockSpec((rows, tile), lambda i: (0, i))] * 4 + anywhere(after),
        out_specs=[pl.BlockSpec((rows // 2, tile), lambda i: (0, i))] * 4,
        compiler_params=params(),
        cost_estimate=cost(2 * rows * cols, 12 * rows * cols),
        name="fold",
    )(*parts, *after)


def fold_last_kernel(keep_a, got_a, keep_b, got_b, *refs):
    own_ref, *outs = refs[-4:]
    rows = own_ref.shape[0]
    cols = keep_a.shape[1]
    for k, (kept, got) in enumerate(((keep_a, got_a), (keep_b, got_b))):
        total = kept[...].astype(f32) + got[...].astype(f32)
        at = slice(k * cols, (k + 1) * cols)
        own_ref[:, at] = total[:rows]
        for j, out in enumerate(outs):
            out[:, at] = total[(j + 1) * rows : (j + 2) * rows].astype(bf16)


def fold_last(parts, after=()):
    rows, cols = parts[0].shape
    shape = (rows // 4, 2 * cols)
    if rows % 32:
        pairs = (parts[:2], parts[2:])
        both = [kept.astype(f32) + got.astype(f32) for kept, got in pairs]
        own, *others = jnp.split(jnp.concatenate(both, axis=1), 4)
        return [own] + [other.astype(bf16) for other in others]
    return pl.pallas_call(
        fold_last_kernel,
        out_shape=[jax.ShapeDtypeStruct(shape, f32)] + [jax.ShapeDtypeStruct(shape, bf16)] * 3,
        in_specs=[pl.BlockSpec(memory_space=pltpu.VMEM)] * 4 + anywhere(after),
        compiler_params=params(),
        cost_estimate=cost(2 * rows * cols, 12 * rows * cols),
        name="fold_last",
    )(*parts, *after)


def anywhere(after):
    return [pl.BlockSpec(memory_space=pl.ANY)] * len(after)


def pair_cols(part, pair):
    start = part * D + pair * 2 * HEAD
    return slice(start, start + 2 * HEAD)


def norm_rows(src, dst, gain, bias, step_rows):
    @pl.loop(0, src.shape[0] // step_rows)
    def _(step):
        at = pl.ds(pl.multiple_of(step * step_rows, step_rows), step_rows)
        unit, _ = norm_parts(src[at, :].astype(f32))
        dst[at, :] = (unit * gain + bias).astype(bf16)


def attend(qkv_ref, att_ref, q_rows, k_rows, mask):
    low, high = lane_halves(f32)
    for pair in range(HEADS // 2):
        queries = two_heads(qkv_ref[q_rows, pair_cols(0, pair)] * bf16(HEAD ** (-0.5)))
        scores = mul_bt(queries, qkv_ref[k_rows, pair_cols(1, pair)])
        probs = masked_softmax(scores, mask).astype(bf16)
        half = probs.shape[0] // 2
        mixed = mul(probs, qkv_ref[k_rows, pair_cols(2, pair)])
        att_ref[q_rows, pair_cols(0, pair)] = (mixed[:half] * low + mixed[half:] * high).astype(bf16)


def twice(mask):
    return jnp.concatenate([mask, mask], axis=0)


def text_front_kernel(
    x_ref, g1_ref, b1_ref, wqkv_ref, wo_ref, g2_ref, b2_ref, h1_ref, qkv_ref, att_ref, mid_ref,
    h2_ref, sum_ref
):
    rows, chunk = x_ref.shape[0], 128
    norm_rows(x_ref, h1_ref, g1_ref[...], b1_ref[...], chunk)

    @pl.loop(0, 3 * D // 256)
    def _(step):
        at = pl.ds(pl.multiple_of(step * 256, 256), 256)
        qkv_ref[:, at] = mul(h1_ref[...], wqkv_ref[:, at]).astype(bf16)

    mask = twice(same_sequence(chunk, 0, chunk, 0, TXT_LEN))

    @pl.loop(0, rows // chunk)
    def _(step):
        at = pl.ds(pl.multiple_of(step * chunk, chunk), chunk)
        attend(qkv_ref, att_ref, at, at, mask)

    @pl.loop(0, D // 256)
    def _(step):
        at = pl.ds(pl.multiple_of(step * 256, 256), 256)
        mid_ref[:, at] = x_ref[:, at].astype(f32) + mul(att_ref[...], wo_ref[:, at])

    norm_rows(mid_ref, h2_ref, g2_ref[...], b2_ref[...], chunk)
    per = chunk // TXT_LEN

    @pl.loop(0, rows // chunk)
    def _(step):
        values = mid_ref[pl.ds(pl.multiple_of(step * chunk, chunk), chunk), :]
        sum_ref[pl.ds(pl.multiple_of(step * per, per), per), :] = jnp.sum(
            values.reshape(per, TXT_LEN, D), axis=1
        )


def text_front(rows_in, gain1, bias1, wqkv, wo, gain2, bias2):
    rows = rows_in.shape[0]
    shapes = [
        ((rows, D), bf16),
        ((rows, 3 * D), bf16),
        ((rows, D), bf16),
        ((rows, D), f32),
        ((rows, D), bf16),
        ((rows // TXT_LEN, D), f32),
    ]
    return pl.pallas_call(
        text_front_kernel,
        out_shape=[jax.ShapeDtypeStruct(*item) for item in shapes],
        compiler_params=params(),
        cost_estimate=cost(rows * D * D * 8, 14 * D * rows + 8 * D * D, rows * 128 * HEADS),
        name="text_front",
    )(rows_in, gain1[None], bias1[None], wqkv, wo, gain2[None], bias2[None])


def image_front_kernel(
    windows, x_ref, perm_ref, g1_ref, b1_ref, g2_ref, b2_ref, *refs
):
    h2_ref, sum_ref, w_ref, h1_ref, placed_ref, qkv_ref, att_ref, mid_ref, sems = refs[-9:]
    rows, chunk = x_ref.shape[0], 80
    copies, row = [], 0
    for k, piece in enumerate(refs[:-9]):
        place = w_ref.at[pl.ds(row, piece.shape[0]), :]
        copies.append(pltpu.make_async_copy(piece, place, sems.at[k]))
        row += piece.shape[0]
    for copy in copies:
        copy.start()

    def place_columns(src):
        @pl.loop(0, D // 256)
        def _(step):
            at = pl.ds(pl.multiple_of(step * 256, 256), 256)
            placed_ref[:, at] = mul_bt(src[...], perm_ref[at, :]).astype(bf16)

    norm_rows(x_ref, h1_ref, g1_ref[...].astype(f32), b1_ref[...].astype(f32), chunk)
    place_columns(h1_ref)
    for copy in copies:
        copy.wait()

    @pl.loop(0, 3 * D // 256)
    def _(step):
        at = pl.ds(pl.multiple_of(step * 256, 256), 256)
        qkv_ref[:, at] = mul(placed_ref[...], w_ref[:, at]).astype(bf16)

    for row0, count, key0, keys in windows:
        mask = twice(same_sequence(count, row0, keys, key0, IMG_LEN))
        attend(qkv_ref, att_ref, pl.ds(row0, count), pl.ds(key0, keys), mask)
    place_columns(att_ref)

    @pl.loop(0, D // 256)
    def _(step):
        at = pl.ds(pl.multiple_of(step * 256, 256), 256)
        there = pl.ds(pl.multiple_of(step * 256 + 3 * D, 256), 256)
        mid_ref[:, at] = x_ref[:, at].astype(f32) + mul(placed_ref[...], w_ref[:, there])

    norm_rows(mid_ref, h2_ref, g2_ref[...].astype(f32), b2_ref[...].astype(f32), chunk)
    for k in range(rows // IMG_LEN):
        first, last = k * IMG_LEN, (k + 1) * IMG_LEN
        start, end = first // 8 * 8, -(-last // 8) * 8
        values = mid_ref[start:end, :]
        place = lax.broadcasted_iota(jnp.int32, values.shape, 0) + start
        inside = (place >= first) & (place < last)
        sum_ref[k : k + 1, :] = jnp.sum(jnp.where(inside, values, 0.0), axis=0, keepdims=True)


def image_front(rows_in, pieces, perm, gain1, bias1, gain2, bias2):
    rows = rows_in.shape[0]
    windows = ((0, 208, 0, 256), (208, 192, 192, 208))
    vmem = pl.BlockSpec(memory_space=pltpu.VMEM)
    return pl.pallas_call(
        functools.partial(image_front_kernel, windows),
        out_shape=[
            jax.ShapeDtypeStruct((rows, D), bf16),
            jax.ShapeDtypeStruct((rows // IMG_LEN, D), f32),
        ],
        in_specs=[vmem] * 6 + anywhere(pieces),
        out_specs=[vmem] * 2,
        scratch_shapes=[
            pltpu.VMEM((D, 4 * D), bf16),
            pltpu.VMEM((rows, D), bf16),
            pltpu.VMEM((rows, D), bf16),
            pltpu.VMEM((rows, 3 * D), bf16),
            pltpu.VMEM((rows, D), bf16),
            pltpu.VMEM((rows, D), f32),
            pltpu.SemaphoreType.DMA((len(pieces),)),
        ],
        compiler_params=params(),
        cost_estimate=cost(rows * D * D * 12, 8 * D * D, rows * 256 * HEADS),
        name="image_front",
    )(rows_in, perm, gain1[None], bias1[None], gain2[None], bias2[None], *pieces)


def gelu_parts(inner):
    half = 0.5 * (1.0 + lax.erf(inner * (0.5**0.5)))
    return inner * half, half


def pack_kernel(unit_ref, pos_ref, *refs):
    refs[-1][:, :D] = unit_ref[...].astype(bf16)
    refs[-1][:, D:] = pos_ref[...]


def packed(unit, positive, after):
    shape = (unit.shape[0], D + positive.shape[1])
    return pl.pallas_call(
        pack_kernel,
        out_shape=jax.ShapeDtypeStruct(shape, bf16),
        in_specs=[pl.BlockSpec(memory_space=pltpu.VMEM)] * 2 + anywhere(after),
        compiler_params=params(),
        cost_estimate=cost(shape[0] * shape[1], 4 * shape[0] * shape[1]),
        name="packed",
    )(unit, positive, *after)


def pool_matrix(count, rows, row0, seq_len):
    row = (lax.broadcasted_iota(jnp.int32, (count, rows), 1) + row0) // seq_len
    return jnp.where(row == lax.broadcasted_iota(jnp.int32, (count, rows), 0), 1.0, 0.0).astype(bf16)


def two_terms(mean):
    high = mean.astype(bf16)
    low = (mean - high.astype(f32)).astype(bf16)
    return jnp.concatenate([high, low], axis=0)


def unit_rows(pooled):
    inverse = lax.rsqrt(jnp.sum(pooled * pooled, axis=-1, keepdims=True) + norm_eps)
    return pooled * inverse, inverse


def text_up_kernel(h2_ref, wu_ref, wd_ref, sum_ref, *refs):
    slope_ref, hid_ref, unit_ref, inv_ref, acc = refs[-5:]
    step = pl.program_id(0)
    chunk = 128
    per = chunk // TXT_LEN
    pool = pool_matrix(per, chunk, 0, TXT_LEN)
    for k in range(h2_ref.shape[0] // chunk):
        inner = mul(h2_ref[k * chunk : (k + 1) * chunk, :], wu_ref[...])
        value, half = gelu_parts(inner)
        slope = half + inner * (jnp.exp(-0.5 * inner * inner) * 0.3989422804014327)
        slope_ref[k * chunk : (k + 1) * chunk, :] = slope.astype(bf16)
        hid_ref[k * per : (k + 1) * per, :] = mul(pool, value.astype(bf16))
    terms = mul(two_terms(hid_ref[...] * (1.0 / TXT_LEN)), wd_ref[...])
    count = hid_ref.shape[0]
    added = terms[:count] + terms[count:]

    @pl.when(step == 0)
    def _():
        acc[...] = sum_ref[...] * (1.0 / TXT_LEN) + added

    @pl.when(step > 0)
    def _():
        acc[...] += added

    @pl.when(step == pl.num_programs(0) - 1)
    def _():
        unit, inverse = unit_rows(acc[...])
        unit_ref[...] = unit
        inv_ref[...] = jnp.broadcast_to(inverse, inv_ref.shape)


def text_up(normed2, weight_up, weight_down, middle_sum, after=()):
    rows, count = normed2.shape[0], middle_sum.shape[0]
    fixed = lambda shape: pl.BlockSpec(shape, lambda i: (0, 0))
    return pl.pallas_call(
        text_up_kernel,
        grid=(FF // TILE,),
        out_shape=[
            jax.ShapeDtypeStruct((rows, FF), bf16),
            jax.ShapeDtypeStruct((count, FF), f32),
            jax.ShapeDtypeStruct((count, D), f32),
            jax.ShapeDtypeStruct((count, 128), f32),
        ],
        in_specs=[
            fixed((rows, D)),
            pl.BlockSpec((D, TILE), lambda i: (0, i)),
            pl.BlockSpec((TILE, D), lambda i: (i, 0)),
            fixed((count, D)),
        ]
        + anywhere(after),
        out_specs=[
            pl.BlockSpec((rows, TILE), lambda i: (0, i)),
            pl.BlockSpec((count, TILE), lambda i: (0, i)),
            fixed((count, D)),
            fixed((count, 128)),
        ],
        scratch_shapes=[pltpu.VMEM((count, D), f32)],
        compiler_params=params(),
        cost_estimate=cost(2 * rows * D * FF, 4 * D * FF + 2 * rows * FF, 20 * rows * FF),
        name="text_up",
    )(normed2, weight_up, weight_down, middle_sum, *after)


def image_up_kernel(fold, h2_ref, wu_ref, wd_ref, sum_ref, *refs):
    out_ref, acc = refs[-2:]
    step = pl.program_id(0)
    rows, count = h2_ref.shape[0], sum_ref.shape[0]
    chunk = 80
    summed = jnp.zeros((count, TILE), f32)
    for k in range(rows // chunk):
        inner = mul(h2_ref[k * chunk : (k + 1) * chunk, :], wu_ref[...])
        value, _ = gelu_parts(inner)
        pool = pool_matrix(count, chunk, k * chunk, IMG_LEN)
        summed = summed + mul(pool, value.astype(bf16))
    mean = two_terms(summed * (1.0 / IMG_LEN))
    place = lax.broadcasted_iota(jnp.int32, (TILE, TILE // fold), 0)
    picked = lax.broadcasted_iota(jnp.int32, (TILE, TILE // fold), 1) * fold
    terms = jnp.zeros((2 * count, D), f32)
    for k in range(fold):
        chosen = jnp.where(place == picked + k, 1.0, 0.0).astype(bf16)
        part = mul(mean, chosen).astype(bf16)
        terms = terms + mul(part, wd_ref[:, k * D : (k + 1) * D])
    added = terms[:count] + terms[count:]

    @pl.when(step == 0)
    def _():
        acc[...] = sum_ref[...] * (1.0 / IMG_LEN) + added

    @pl.when(step > 0)
    def _():
        acc[...] += added

    @pl.when(step == pl.num_programs(0) - 1)
    def _():
        out_ref[...] = unit_rows(acc[...])[0].astype(bf16)


def image_up(normed2, whole, up_col, down_col, middle_sum, after=()):
    rows, count = normed2.shape[0], middle_sum.shape[0]
    fold = FF // D
    fixed = lambda shape: pl.BlockSpec(shape, lambda i: (0, 0))
    return pl.pallas_call(
        functools.partial(image_up_kernel, fold),
        grid=(FF // TILE,),
        out_shape=jax.ShapeDtypeStruct((count, D), bf16),
        in_specs=[
            fixed((rows, D)),
            pl.BlockSpec((D, TILE), lambda i: (0, up_col // TILE + i)),
            pl.BlockSpec((TILE // fold, fold * D), lambda i: (i, down_col // (fold * D))),
            fixed((count, D)),
        ]
        + anywhere(after),
        out_specs=fixed((count, D)),
        scratch_shapes=[pltpu.VMEM((count, D), f32)],
        compiler_params=params(),
        cost_estimate=cost(2 * rows * D * FF, 4 * D * FF, 15 * rows * FF),
        name="image_up",
    )(normed2, whole, whole, middle_sum, *after)


def loss_parts(text_rows, pos, image_all):
    similar = mul_bt(text_rows, image_all) * logit_scale
    shifted = jnp.exp(similar - logit_scale)
    alive = jnp.max(pos, axis=1, keepdims=True)
    row_sum = jnp.sum(shifted, axis=1, keepdims=True)
    row_count = jnp.maximum(jnp.sum(pos, axis=1, keepdims=True), 1.0)
    return similar, shifted, alive, row_sum, row_count


def sums_over_captions(text_rows, pos, image_all):
    similar, shifted, alive, row_sum, row_count = loss_parts(text_rows, pos, image_all)
    pos_similar = pos * similar
    cap_term = alive * (
        logit_scale + jnp.log(row_sum) - jnp.sum(pos_similar, axis=1, keepdims=True) / row_count
    )
    return (
        jnp.sum(alive * shifted, axis=0, keepdims=True),
        jnp.sum(pos, axis=0, keepdims=True),
        jnp.sum(pos_similar, axis=0, keepdims=True),
        jnp.sum(cap_term, axis=0, keepdims=True),
        jnp.sum(alive, axis=0, keepdims=True),
    )


def loss_from(sums):
    col_sum, col_count, col_pos, cap_total, live_total = sums
    img_term = logit_scale + jnp.log(col_sum) - col_pos / col_count
    return 0.5 * cap_total / live_total + 0.5 * jnp.mean(img_term, axis=1, keepdims=True)


def grad_of_unit(text_rows, pos, image_all, col_sum, col_count, live_total):
    _, shifted, alive, row_sum, row_count = loss_parts(text_rows, pos, image_all)
    cap_share, img_share = 0.5 / live_total, 0.5 / image_all.shape[0]
    grad_sims = alive * shifted * (cap_share / row_sum + img_share / col_sum) - pos * (
        cap_share / row_count + img_share / col_count
    )
    return mul(grad_sims.astype(bf16), image_all) * logit_scale


def turned(grad, unit):
    return grad - unit * jnp.sum(grad * unit, axis=-1, keepdims=True)


def loss_kernel(
    pack_ref, image_ref, own_ref, unit_ref, inv_ref, loss_ref, row_ref, low_ref, col_sum_ref,
    col_count_ref, live_ref
):
    image_all = image_ref[...]
    chunk = 256
    total = None
    for k in range(pack_ref.shape[0] // chunk):
        at = slice(k * chunk, (k + 1) * chunk)
        part = sums_over_captions(pack_ref[at, :D], pack_ref[at, D:].astype(f32), image_all)
        total = part if total is None else [a + b for a, b in zip(total, part)]
    loss_ref[...] = jnp.broadcast_to(loss_from(total), loss_ref.shape)
    col_sum, col_count, _, _, live_total = total
    col_sum_ref[...] = col_sum
    col_count_ref[...] = col_count
    live_ref[...] = jnp.broadcast_to(live_total, live_ref.shape)
    grad = grad_of_unit(
        own_ref[:, :D], own_ref[:, D:].astype(f32), image_all, col_sum, col_count, live_total
    )
    row = inv_ref[:, :1] * turned(grad, unit_ref[...]) * (1.0 / TXT_LEN)
    row_ref[...] = row
    low_ref[...] = row.astype(bf16)


def loss_and_rows(pack, image_all, own_pack, unit, inverse):
    images, count = image_all.shape[0], own_pack.shape[0]
    shapes = [(1, 128), (count, D), (count, D), (1, images), (1, images), (1, 128)]
    kinds = [f32, f32, bf16, f32, f32, f32]
    return pl.pallas_call(
        loss_kernel,
        out_shape=[jax.ShapeDtypeStruct(*item) for item in zip(shapes, kinds)],
        compiler_params=params(),
        cost_estimate=cost(2 * pack.shape[0] * images * D, 2 * pack.size, pack.shape[0] * images),
        name="loss_and_rows",
    )(pack, image_all, own_pack, unit, inverse)


def down_kernel(pack_ref, image_ref, col_sum_ref, col_count_ref, live_ref, hid_ref, *refs):
    step, out_ref = pl.program_id(0), refs[-1]
    text_rows = pack_ref[:, :D]
    grad = grad_of_unit(
        text_rows, pack_ref[:, D:].astype(f32), image_ref[...], col_sum_ref[...],
        col_count_ref[...], live_ref[:, :1]
    )
    rows = (turned(grad, text_rows.astype(f32)) * (1.0 / TXT_LEN)).astype(bf16)
    part = mul_at(hid_ref[...], rows)

    @pl.when(step == 0)
    def _():
        out_ref[...] = part

    @pl.when(step > 0)
    def _():
        out_ref[...] += part


def grad_of_down(pack, image_all, col_sum, col_count, live_total, hidden_cols, after):
    images, chunk = image_all.shape[0], 256
    fixed = lambda shape: pl.BlockSpec(shape, lambda i: (0, 0))
    per = hidden_cols.shape[1]
    return pl.pallas_call(
        down_kernel,
        grid=(pack.shape[0] // chunk,),
        out_shape=jax.ShapeDtypeStruct((per, D), f32),
        in_specs=[
            pl.BlockSpec((chunk, pack.shape[1]), lambda i: (i, 0)),
            fixed((images, D)), fixed((1, images)), fixed((1, images)), fixed((1, 128)),
            pl.BlockSpec((chunk, per), lambda i: (i, 0)),
        ]
        + anywhere(after),
        out_specs=fixed((per, D)),
        compiler_params=params(),
        cost_estimate=cost(4 * pack.shape[0] * images * D, 2 * pack.size, pack.shape[0] * images),
        name="grad_of_down",
    )(pack, image_all, col_sum, col_count, live_total, hidden_cols, *after)


def mlp_back_kernel(
    low_ref, wd_ref, slope_ref, wu_ref, lhs_ref, mid_ref, gain_ref, row_ref, keep_a, send_a, keep_b,
    send_b, out_ref, gain_out, bias_out, acc
):
    step = pl.program_id(0)
    count, rows = low_ref.shape[0], slope_ref.shape[0]
    half = D // 2
    hidden = mul_bt(low_ref[...], wd_ref[...])
    wide = jnp.broadcast_to(hidden[:, None, :], (count, TXT_LEN, TILE)).reshape(rows, TILE)
    inner = (wide * slope_ref[...].astype(f32)).astype(bf16)
    weight = mul(lhs_ref[0], inner).astype(bf16)

    @pl.when(step < pl.num_programs(0) // 2)
    def _():
        keep_a[...] = weight[:half]
        send_a[...] = weight[half:]

    @pl.when(step >= pl.num_programs(0) // 2)
    def _():
        keep_b[...] = weight[:half]
        send_b[...] = weight[half:]

    added = mul_bt(inner, wu_ref[...])

    @pl.when(step == 0)
    def _():
        acc[...] = added

    @pl.when(step > 0)
    def _():
        acc[...] += added

    @pl.when(step == pl.num_programs(0) - 1)
    def _():
        chunk = 128
        per = chunk // TXT_LEN
        gain = gain_ref[...]
        gain_out[...] = jnp.zeros_like(gain_out)
        bias_out[...] = jnp.zeros_like(bias_out)

        @pl.loop(0, rows // chunk)
        def _(k):
            at = pl.ds(pl.multiple_of(k * chunk, chunk), chunk)
            unit, scale = norm_parts(mid_ref[at, :])
            grad = acc[at, :]
            gain_out[...] += jnp.sum(grad * unit, axis=0, keepdims=True)
            bias_out[...] += jnp.sum(grad, axis=0, keepdims=True)
            row = row_ref[pl.ds(pl.multiple_of(k * per, per), per), :]
            row = jnp.broadcast_to(row[:, None, :], (per, TXT_LEN, D)).reshape(chunk, D)
            out_ref[at, :] = row + norm_back(unit, scale, gain, grad)


def mlp_back(grad_row, grad_low, weight_down, slope, weight_up, lhs, middle, gain):
    rows, count = slope.shape[0], grad_row.shape[0]
    steps = FF // TILE
    fixed = lambda shape: pl.BlockSpec(shape, lambda i: (0, 0))
    first = pl.BlockSpec((D // 2, TILE), lambda i: (0, jnp.minimum(i, steps // 2 - 1)))
    second = pl.BlockSpec((D // 2, TILE), lambda i: (0, jnp.maximum(i - steps // 2, 0)))
    part = jax.ShapeDtypeStruct((D // 2, FF // 2), bf16)
    line = jax.ShapeDtypeStruct((1, D), f32)
    return pl.pallas_call(
        mlp_back_kernel,
        grid=(steps,),
        out_shape=[part] * 4 + [jax.ShapeDtypeStruct((rows, D), f32), line, line],
        in_specs=[
            fixed((count, D)),
            pl.BlockSpec((TILE, D), lambda i: (i, 0)),
            pl.BlockSpec((rows, TILE), lambda i: (0, i)),
            pl.BlockSpec((D, TILE), lambda i: (0, i)),
            pl.BlockSpec((1, D, rows), lambda i: (i // (steps // 2), 0, 0)),
            fixed((rows, D)),
            fixed((1, D)),
            fixed((count, D)),
        ],
        out_specs=[first, first, second, second, fixed((rows, D)), fixed((1, D)), fixed((1, D))],
        scratch_shapes=[pltpu.VMEM((rows, D), f32)],
        compiler_params=params(),
        cost_estimate=cost(4 * rows * D * FF, 4 * D * FF + 2 * rows * FF + 2 * D * FF, rows * FF),
        name="mlp_back",
    )(grad_low, weight_down, slope, weight_up, lhs, middle, gain[None], grad_row)


def attention_back_kernel(grad_ref, wo_ref, qkv_ref, *refs):
    low_ref, out_ref = refs[-2:]
    chunk = grad_ref.shape[0]
    one = same_sequence(chunk, 0, chunk, 0, TXT_LEN)
    mask = jnp.concatenate([one, one], axis=0)
    low = grad_ref[...].astype(bf16)
    low_ref[...] = low
    grad_att = mul_bt(low, wo_ref[...]).astype(bf16)
    for pair in range(HEADS // 2):
        queries = two_heads(qkv_ref[:, pair_cols(0, pair)] * bf16(HEAD ** (-0.5)))
        keys = qkv_ref[:, pair_cols(1, pair)]
        vals = qkv_ref[:, pair_cols(2, pair)]
        grads = two_heads(grad_att[:, pair_cols(0, pair)])
        probs = masked_softmax(mul_bt(queries, keys), mask)
        grad_probs = mul_bt(grads, vals)
        along = jnp.sum(grad_probs * probs, axis=-1, keepdims=True)
        grad_scores = (probs * (grad_probs - along)).astype(bf16)
        side = jnp.concatenate([grad_scores[:chunk], grad_scores[chunk:]], axis=1)
        grad_q = mul(side, two_heads(keys)) * HEAD ** (-0.5)
        grad_k = mul_at(grad_scores, queries)
        grad_v = mul_at(probs.astype(bf16), grads)
        out_ref[:, pair_cols(0, pair)] = grad_q.astype(bf16)
        out_ref[:, pair_cols(1, pair)] = grad_k.astype(bf16)
        out_ref[:, pair_cols(2, pair)] = grad_v.astype(bf16)


def attention_back(grad_middle, weight_out, project, first, count, after=()):
    chunk = 128
    rows = count * chunk
    return pl.pallas_call(
        attention_back_kernel,
        grid=(count,),
        out_shape=[
            jax.ShapeDtypeStruct((rows, D), bf16),
            jax.ShapeDtypeStruct((rows, 3 * D), bf16),
        ],
        in_specs=[
            pl.BlockSpec((chunk, D), lambda i: (i + first, 0)),
            pl.BlockSpec((D, D), lambda i: (0, 0)),
            pl.BlockSpec((chunk, 3 * D), lambda i: (i + first, 0)),
        ]
        + anywhere(after),
        out_specs=[
            pl.BlockSpec((chunk, D), lambda i: (i, 0)),
            pl.BlockSpec((chunk, 3 * D), lambda i: (i, 0)),
        ],
        compiler_params=params(),
        cost_estimate=cost(10 * rows * D * D, 16 * rows * D + 2 * D * D, rows * 128 * HEADS),
        name="attention_back",
    )(grad_middle, weight_out, project, *after)


def mul_rows(lhs, parts):
    total, row = 0.0, 0
    for part in parts:
        total = total + mul(lhs[:, row : row + part.shape[0]], part[...])
        row += part.shape[0]
    return total


def weight_back_kernel(counts, lhs_ref, *refs):
    step, half = pl.program_id(0), D // 2
    keep, send = refs[-2:]
    row = 0
    for k, count in enumerate(counts):
        parts = refs[row : row + count]
        row += count

        @pl.when(step == k if len(counts) > 1 else step >= 0)
        def _(parts=parts):
            weight = mul_rows(lhs_ref[0], parts).astype(bf16)
            keep[...] = weight[:half]
            send[...] = weight[half:]


def weight_back(lhs, first, groups, blocks, after=()):
    rows = lhs.shape[2]
    steps = 2
    many = len(groups) > 1
    given = [part for group in groups for part in group]
    return pl.pallas_call(
        functools.partial(weight_back_kernel, [len(group) for group in groups]),
        grid=(steps,),
        out_shape=[jax.ShapeDtypeStruct((D // 2, steps * D), bf16)] * 2,
        in_specs=[pl.BlockSpec((1, D, rows), lambda i: (first + (i if many else 0), 0, 0))]
        + [
            pl.BlockSpec((part.shape[0], D), lambda i, col=col: (0, col + (0 if many else i)))
            for group, col in zip(groups, blocks)
            for part in group
        ]
        + anywhere(after),
        out_specs=[pl.BlockSpec((D // 2, D), lambda i: (0, i))] * 2,
        compiler_params=params(),
        cost_estimate=cost(4 * rows * D * D, 4 * rows * D + 7 * D * D),
        name="weight_back",
    )(lhs, *given, *after)


def input_back_kernel(count, *refs):
    projs = refs[:count]
    w_ref, x_ref, gain_ref, mid_ref = refs[count : count + 4]
    out_ref, gain_out, bias_out, acc = refs[-4:]
    step = pl.program_id(0)
    rows, chunk = x_ref.shape[0], 128
    row = 0
    for part in projs:
        at = slice(row, row + part.shape[0])
        row += part.shape[0]
        added = mul_bt(part[...], w_ref[...])

        @pl.when(step == 0)
        def _(at=at, added=added):
            acc[at, :] = added

        @pl.when(step > 0)
        def _(at=at, added=added):
            acc[at, :] += added

    @pl.when(step == pl.num_programs(0) - 1)
    def _():
        gain = gain_ref[...]
        gain_out[...] = jnp.zeros_like(gain_out)
        bias_out[...] = jnp.zeros_like(bias_out)

        @pl.loop(0, rows // chunk)
        def _(k):
            at = pl.ds(pl.multiple_of(k * chunk, chunk), chunk)
            unit, scale = norm_parts(x_ref[at, :].astype(f32))
            grad = acc[at, :]
            gain_out[...] += jnp.sum(grad * unit, axis=0, keepdims=True)
            bias_out[...] += jnp.sum(grad, axis=0, keepdims=True)
            out_ref[at, :] = mid_ref[at, :] + norm_back(unit, scale, gain, grad)


def input_back(grad_projs, weight, rows_in, gain, grad_middle, after=()):
    rows = rows_in.shape[0]
    fixed = lambda shape: pl.BlockSpec(shape, lambda i: (0, 0))
    line = jax.ShapeDtypeStruct((1, D), f32)
    return pl.pallas_call(
        functools.partial(input_back_kernel, len(grad_projs)),
        grid=(3,),
        out_shape=[jax.ShapeDtypeStruct((rows, D), f32), line, line],
        in_specs=[pl.BlockSpec((part.shape[0], D), lambda i: (0, i)) for part in grad_projs]
        + [
            pl.BlockSpec((D, D), lambda i: (0, i)),
            fixed((rows, D)), fixed((1, D)), fixed((rows, D)),
        ]
        + anywhere(after),
        out_specs=[fixed((rows, D)), fixed((1, D)), fixed((1, D))],
        scratch_shapes=[pltpu.VMEM((rows, D), f32)],
        compiler_params=params(),
        cost_estimate=cost(6 * rows * D * D, 14 * rows * D + 6 * D * D),
        name="input_back",
    )(*grad_projs, weight, rows_in, gain[None], grad_middle, *after)


def local(
    images,
    captions,
    img_gain1,
    img_bias1,
    img_qkv,
    img_out,
    img_gain2,
    img_bias2,
    img_up,
    img_down,
    txt_gain1,
    txt_bias1,
    txt_qkv,
    txt_out,
    txt_gain2,
    txt_bias2,
    txt_up,
    txt_down,
    counts,
    matches,
):
    peers = lax.axis_size(AXIS)
    own = lax.axis_index(AXIS)
    per = D // peers
    img_local = counts.shape[0]
    cap_local = matches.shape[0]
    total_images = matches.shape[1]

    whole = lax.all_gather(
        jnp.concatenate([img_up.reshape(per, FF), img_down.reshape(per, FF)], axis=1),
        AXIS,
        axis=0,
        tiled=True,
    )
    small = peers == 32
    shard = jnp.concatenate([img_qkv.reshape(per, 3 * D), img_out.reshape(per, D)], axis=1)
    if small:
        line, perm = gathered_line(shard), row_order((1, 4, 2, 16, 8))
    else:
        line, perm = lax.all_gather(shard, AXIS, axis=0, tiled=True), jnp.eye(D, dtype=bf16)

    normed1, project, attended, middle, normed2, middle_sum = text_front(
        captions, txt_gain1, txt_bias1, txt_qkv, txt_out, txt_gain2, txt_bias2
    )
    middle_sum, line = in_turn(middle_sum, line)
    beside, above = (swapped(line, 2), swapped(line, 4)) if small else (line, line)
    slope, hidden_sum, text_unit, inverse = text_up(
        normed2, txt_up, txt_down, middle_sum, (line,)
    )
    text_unit, (beside, above) = in_turn(text_unit, (beside, above))
    pieces = gathered_rows(line, beside, above) if small else [line]

    ends_at = jnp.cumsum(counts)
    slot_ids = lax.iota(jnp.int32, cap_local)
    owner = jnp.sum((ends_at[None, :] <= slot_ids[:, None]).astype(jnp.int32), axis=1)
    owner = owner + own * img_local
    live = slot_ids < ends_at[-1]
    columns = lax.iota(jnp.int32, total_images)
    positive = ((matches > 0) | (owner[:, None] == columns[None, :])) & live[:, None]

    own_pack = packed(text_unit, positive.astype(bf16), pieces[1:5] if small else ())
    pack = own_pack[None]
    if small:
        pack = gathered_with(pack, 16)

    normed_img, middle_img = image_front(
        images, pieces, perm, img_gain1, img_bias1, img_gain2, img_bias2
    )
    if small:
        normed_img, pack, scaled_sum = lax.optimization_barrier(
            (normed_img, pack, (hidden_sum * inverse[:, :1]).astype(bf16))
        )
        hidden_cols = lax.all_to_all(scaled_sum, AXIS, split_axis=1, concat_axis=0, tiled=True)
        pack = gathered_with(gathered_with(pack, 8), 4)
        normed_img, (pack, hidden_cols) = in_turn(normed_img, (pack, hidden_cols))
        pack = gathered_with(pack, 2)
    image_low = image_up(normed_img, whole, 0, FF, middle_img)
    if small:
        image_low, pack = in_turn(image_low, pack)
        text_pack = gathered_with(pack, 1).reshape(-1, D + total_images)
    image_all = spread(image_low).reshape(total_images, D)

    order_a, order_b, tail = stage_orders()
    matrix_a, matrix_b = row_order(order_a + tail[::-1]), row_order(order_b + tail[::-1])
    lhs_up = jnp.stack([placed(matrix_a, normed2), placed(matrix_b, normed2)])
    lhs_rest = jnp.stack(
        [placed(matrix_a, normed1), placed(matrix_b, normed1), placed(matrix_b, attended)]
    )

    if small:
        loss_value, grad_row, row_low, col_sum, col_count, live_total = loss_and_rows(
            text_pack, image_all, own_pack, text_unit, inverse
        )
        loss_value = loss_value[0, 0]
    else:
        text_low, pos = own_pack[:, :D], own_pack[:, D:].astype(f32)
        sums = lax.psum(sums_over_captions(text_low, pos, image_all), AXIS)
        loss_value = loss_from(sums)[0, 0]
        grad = grad_of_unit(text_low, pos, image_all, sums[0], sums[1], sums[4])
        grad_row = inverse[:, :1] * turned(grad, text_unit) * (1.0 / TXT_LEN)
        row_low = grad_row.astype(bf16)

    *up, grad_middle, gain_two, bias_two = mlp_back(
        grad_row, row_low, txt_down, slope, txt_up, lhs_up, middle, txt_gain2
    )
    stages = len(order_a)
    low_one, proj_one = attention_back(grad_middle, txt_out, project, 0, 2)
    for stage in range(stages - 2):
        up = fold(hand_on(up, stage), (proj_one,))
    low_two, proj_two = attention_back(grad_middle, txt_out, project, 2, 3, up)
    up = fold(hand_on(up, stages - 2), (proj_two,))
    projs, lows = (proj_one, proj_two), (low_one, low_two)
    rest_a = weight_back(lhs_rest, 0, [projs], [0], up)
    up = fold_last(hand_on(up, stages - 1), rest_a[1:])
    rest_b = weight_back(lhs_rest, 1, [projs, lows], [2, 0], up)
    rest = [*rest_a, *rest_b]
    for stage in range(stages - 2):
        rest = fold(hand_on(rest, stage))
    caption_grad, gain_one, bias_one = input_back(
        projs, txt_qkv, captions, txt_gain1, grad_middle, rest[:1]
    )
    caption_grad, up = in_turn(caption_grad, hand_on_last(up))
    rest = fold(hand_on(rest, stages - 2), (caption_grad,))
    if small:
        grad_down = grad_of_down(
            text_pack, image_all, col_sum, col_count, live_total, hidden_cols, rest
        )
        rest = fold_last(hand_on(rest, stages - 1), (grad_down,))
    else:
        grad_down = lax.psum_scatter(
            mul_at(hidden_sum.astype(bf16), row_low), AXIS, scatter_dimension=0, tiled=True
        )
        rest = fold_last(hand_on(rest, stages - 1))
    up_share = sum_last(*up)
    rest_share = sum_last(*hand_on_last(rest))
    norms = jnp.concatenate([gain_one, bias_one, gain_two, bias_two], axis=0)
    norms = jnp.sum(spread(norms[None]), axis=0).reshape(4, D)
    return (
        loss_value,
        caption_grad,
        norms[0],
        norms[1],
        rest_share[:, : 3 * D].reshape(-1),
        rest_share[:, 3 * D :].reshape(-1),
        norms[2],
        norms[3],
        up_share.reshape(-1),
        grad_down.reshape(-1),
    )


def solution(mesh):
    split, flat, whole = P("blk", None), P("blk"), P()
    image_block = (whole, whole, flat, flat, whole, whole, flat, flat)
    return jax.shard_map(
        local,
        mesh=mesh,
        in_specs=(split, split) + image_block + (whole,) * 8 + (flat, split),
        out_specs=(whole, split, whole, whole, flat, flat, whole, whole, flat, flat),
        check_vma=False,
    )
```

```python
import functools

import jax
import jax.numpy as jnp
from jax import lax
from jax.experimental import pallas as pl
from jax.experimental.pallas import tpu as pltpu
from jax.sharding import PartitionSpec as P

D = 768
FF = 3072
HEAD = 64
HEADS = D // HEAD
IMG_LEN = 50
TXT_LEN = 16
AXIS = "blk"

norm_eps = 1e-06
logit_scale = 50.0
f32 = jnp.float32
bf16 = jnp.bfloat16


def swapped(value, mask):
    peers = lax.axis_size(AXIS)
    return lax.ppermute(value, AXIS, [(i, i ^ mask) for i in range(peers)])


def bit_masks():
    peers = lax.axis_size(AXIS)
    return [1 << k for k in range(peers.bit_length() - 1)]


def joined(held, other, mask):
    upper = (lax.axis_index(AXIS) & mask) > 0
    first = jnp.where(upper, other, held)
    second = jnp.where(upper, held, other)
    return jnp.stack([first, second], axis=1).reshape((-1,) + held.shape[1:])


def spread(block):
    peers = lax.axis_size(AXIS)
    copies = jnp.broadcast_to(block[None], (peers,) + block.shape)
    return lax.all_to_all(copies, AXIS, split_axis=0, concat_axis=0, tiled=True)


def stage_orders():
    masks = bit_masks()
    head, tail = masks[:-2], masks[-2:]
    order_a = list(head)
    order_b = list(head)
    for k in range(1, len(head) - 1, 2):
        order_b[k], order_b[k + 1] = order_b[k + 1], order_b[k]
    return order_a, order_b, tail


def row_order(bits):
    peers = lax.axis_size(AXIS)
    own = lax.axis_index(AXIS)
    per = D // peers
    places = lax.iota(jnp.int32, D)
    block = places // per
    target = jnp.zeros_like(block) + own
    for k, mask in enumerate(bits):
        target = target ^ (((block >> (len(bits) - 1 - k)) & 1) * mask)
    source = target * per + places % per
    return (source[:, None] == lax.iota(jnp.int32, D)[None, :]).astype(bf16)


def gathered_line(shard):
    return jnp.concatenate([shard] + [swapped(shard, mask) for mask in (8, 16, 24)], axis=0)


def gathered_rows(line, beside, above):
    half = line.shape[0] // 2
    pieces = [line, beside, above, swapped(beside[:half], 4), swapped(above[half:], 2)]
    return pieces + [swapped(piece, 1) for piece in pieces]


def in_turn(first, then):
    return lax.optimization_barrier((first, then))


def placed(order, values):
    return mul_bt(order, values).astype(bf16)


def hand_on(parts, stage):
    order_a, order_b, _ = stage_orders()
    keep_a, send_a, keep_b, send_b = parts
    return keep_a, swapped(send_a, order_a[stage]), keep_b, swapped(send_b, order_b[stage])


def hand_on_last(blocks):
    low, high = stage_orders()[2]
    own, *others = blocks
    return own, [swapped(block, mask) for block, mask in zip(others, (low, high, low | high))]


def sum_last(own, others):
    total = own
    for other in others:
        total = total + other.astype(f32)
    return total


VMEM_BYTES = 56 << 20
TILE = 512


def norm_parts(values):
    average = jnp.mean(values, axis=-1, keepdims=True)
    centred = values - average
    variance = jnp.mean(centred * centred, axis=-1, keepdims=True)
    scale = lax.rsqrt(variance + norm_eps)
    return centred * scale, scale


def norm_back(unit, scale, gain, grad):
    inner = grad * gain
    shift = jnp.mean(inner, axis=-1, keepdims=True)
    along = jnp.mean(inner * unit, axis=-1, keepdims=True)
    return scale * (inner - shift - unit * along)


def mul(lhs, rhs):
    return jnp.dot(lhs, rhs, preferred_element_type=f32)


def mul_bt(lhs, rhs):
    return lax.dot_general(lhs, rhs, (((1,), (1,)), ((), ())), preferred_element_type=f32)


def mul_at(lhs, rhs):
    return lax.dot_general(lhs, rhs, (((0,), (0,)), ((), ())), preferred_element_type=f32)


def params(**more):
    return pltpu.CompilerParams(vmem_limit_bytes=VMEM_BYTES, **more)


def cost(flops, moved, transcendentals=0):
    return pl.CostEstimate(flops=flops, bytes_accessed=moved, transcendentals=transcendentals)


def lane_halves(dtype):
    lane = lax.broadcasted_iota(jnp.int32, (1, 2 * HEAD), 1)
    low = jnp.where(lane < HEAD, 1.0, 0.0)
    return low.astype(dtype), (1.0 - low).astype(dtype)


def two_heads(pair):
    low, high = lane_halves(bf16)
    return jnp.concatenate([pair * low, pair * high], axis=0)


def same_sequence(rows, row0, cols, col0, seq_len):
    row = (lax.broadcasted_iota(jnp.int32, (rows, cols), 0) + row0) // seq_len
    col = (lax.broadcasted_iota(jnp.int32, (rows, cols), 1) + col0) // seq_len
    return row == col


def masked_softmax(scores, mask):
    scores = jnp.where(mask, scores, -1e30)
    raised = jnp.exp(scores - jnp.max(scores, axis=-1, keepdims=True))
    return raised * (1.0 / jnp.sum(raised, axis=-1, keepdims=True))


def fold_kernel(keep_a, got_a, keep_b, got_b, *refs):
    outs = refs[-4:]
    half = outs[0].shape[0]
    for k, (kept, got) in enumerate(((keep_a, got_a), (keep_b, got_b))):
        for j in range(2):
            at = slice(j * half, (j + 1) * half)
            outs[2 * k + j][...] = (kept[at, :].astype(f32) + got[at, :].astype(f32)).astype(bf16)


def fold(parts, after=()):
    rows, cols = parts[0].shape
    if rows % 32:
        whole = [
            (kept.astype(f32) + got.astype(f32)).astype(bf16)
            for kept, got in (parts[:2], parts[2:])
        ]
        return [part for one in whole for part in (one[: rows // 2], one[rows // 2 :])]
    tile = 512
    return pl.pallas_call(
        fold_kernel,
        grid=(cols // tile,),
        out_shape=[jax.ShapeDtypeStruct((rows // 2, cols), bf16)] * 4,
        in_specs=[pl.BlockSpec((rows, tile), lambda i: (0, i))] * 4 + anywhere(after),
        out_specs=[pl.BlockSpec((rows // 2, tile), lambda i: (0, i))] * 4,
        compiler_params=params(),
        cost_estimate=cost(2 * rows * cols, 12 * rows * cols),
        name="fold",
    )(*parts, *after)


def fold_last_kernel(keep_a, got_a, keep_b, got_b, *refs):
    own_ref, *outs = refs[-4:]
    rows = own_ref.shape[0]
    cols = keep_a.shape[1]
    for k, (kept, got) in enumerate(((keep_a, got_a), (keep_b, got_b))):
        total = kept[...].astype(f32) + got[...].astype(f32)
        at = slice(k * cols, (k + 1) * cols)
        own_ref[:, at] = total[:rows]
        for j, out in enumerate(outs):
            out[:, at] = total[(j + 1) * rows : (j + 2) * rows].astype(bf16)


def fold_last(parts, after=()):
    rows, cols = parts[0].shape
    shape = (rows // 4, 2 * cols)
    if rows % 32:
        pairs = (parts[:2], parts[2:])
        both = [kept.astype(f32) + got.astype(f32) for kept, got in pairs]
        own, *others = jnp.split(jnp.concatenate(both, axis=1), 4)
        return [own] + [other.astype(bf16) for other in others]
    return pl.pallas_call(
        fold_last_kernel,
        out_shape=[jax.ShapeDtypeStruct(shape, f32)] + [jax.ShapeDtypeStruct(shape, bf16)] * 3,
        in_specs=[pl.BlockSpec(memory_space=pltpu.VMEM)] * 4 + anywhere(after),
        compiler_params=params(),
        cost_estimate=cost(2 * rows * cols, 12 * rows * cols),
        name="fold_last",
    )(*parts, *after)


def anywhere(after):
    return [pl.BlockSpec(memory_space=pl.ANY)] * len(after)


def pair_cols(part, pair):
    start = part * D + pair * 2 * HEAD
    return slice(start, start + 2 * HEAD)


def norm_rows(src, dst, gain, bias, step_rows):
    @pl.loop(0, src.shape[0] // step_rows)
    def _(step):
        at = pl.ds(pl.multiple_of(step * step_rows, step_rows), step_rows)
        unit, _ = norm_parts(src[at, :].astype(f32))
        dst[at, :] = (unit * gain + bias).astype(bf16)


def attend(qkv_ref, att_ref, q_rows, k_rows, mask):
    low, high = lane_halves(f32)
    for pair in range(HEADS // 2):
        queries = two_heads(qkv_ref[q_rows, pair_cols(0, pair)] * bf16(HEAD ** (-0.5)))
        scores = mul_bt(queries, qkv_ref[k_rows, pair_cols(1, pair)])
        probs = masked_softmax(scores, mask).astype(bf16)
        half = probs.shape[0] // 2
        mixed = mul(probs, qkv_ref[k_rows, pair_cols(2, pair)])
        att_ref[q_rows, pair_cols(0, pair)] = (mixed[:half] * low + mixed[half:] * high).astype(bf16)


def twice(mask):
    return jnp.concatenate([mask, mask], axis=0)


def text_front_kernel(
    x_ref, g1_ref, b1_ref, wqkv_ref, wo_ref, g2_ref, b2_ref, h1_ref, qkv_ref, att_ref, mid_ref,
    h2_ref, sum_ref
):
    rows, chunk = x_ref.shape[0], 128
    norm_rows(x_ref, h1_ref, g1_ref[...], b1_ref[...], chunk)

    @pl.loop(0, 3 * D // 256)
    def _(step):
        at = pl.ds(pl.multiple_of(step * 256, 256), 256)
        qkv_ref[:, at] = mul(h1_ref[...], wqkv_ref[:, at]).astype(bf16)

    mask = twice(same_sequence(chunk, 0, chunk, 0, TXT_LEN))

    @pl.loop(0, rows // chunk)
    def _(step):
        at = pl.ds(pl.multiple_of(step * chunk, chunk), chunk)
        attend(qkv_ref, att_ref, at, at, mask)

    @pl.loop(0, D // 256)
    def _(step):
        at = pl.ds(pl.multiple_of(step * 256, 256), 256)
        mid_ref[:, at] = x_ref[:, at].astype(f32) + mul(att_ref[...], wo_ref[:, at])

    norm_rows(mid_ref, h2_ref, g2_ref[...], b2_ref[...], chunk)
    per = chunk // TXT_LEN

    @pl.loop(0, rows // chunk)
    def _(step):
        values = mid_ref[pl.ds(pl.multiple_of(step * chunk, chunk), chunk), :]
        sum_ref[pl.ds(pl.multiple_of(step * per, per), per), :] = jnp.sum(
            values.reshape(per, TXT_LEN, D), axis=1
        )


def text_front(rows_in, gain1, bias1, wqkv, wo, gain2, bias2):
    rows = rows_in.shape[0]
    shapes = [
        ((rows, D), bf16),
        ((rows, 3 * D), bf16),
        ((rows, D), bf16),
        ((rows, D), f32),
        ((rows, D), bf16),
        ((rows // TXT_LEN, D), f32),
    ]
    return pl.pallas_call(
        text_front_kernel,
        out_shape=[jax.ShapeDtypeStruct(*item) for item in shapes],
        compiler_params=params(),
        cost_estimate=cost(rows * D * D * 8, 14 * D * rows + 8 * D * D, rows * 128 * HEADS),
        name="text_front",
    )(rows_in, gain1[None], bias1[None], wqkv, wo, gain2[None], bias2[None])


def image_front_kernel(
    windows, x_ref, perm_ref, g1_ref, b1_ref, g2_ref, b2_ref, *refs
):
    h2_ref, sum_ref, w_ref, h1_ref, placed_ref, qkv_ref, att_ref, mid_ref, sems = refs[-9:]
    rows, chunk = x_ref.shape[0], 80
    copies, row = [], 0
    for k, piece in enumerate(refs[:-9]):
        place = w_ref.at[pl.ds(row, piece.shape[0]), :]
        copies.append(pltpu.make_async_copy(piece, place, sems.at[k]))
        row += piece.shape[0]
    for copy in copies:
        copy.start()

    def place_columns(src):
        @pl.loop(0, D // 256)
        def _(step):
            at = pl.ds(pl.multiple_of(step * 256, 256), 256)
            placed_ref[:, at] = mul_bt(src[...], perm_ref[at, :]).astype(bf16)

    norm_rows(x_ref, h1_ref, g1_ref[...].astype(f32), b1_ref[...].astype(f32), chunk)
    place_columns(h1_ref)
    for copy in copies:
        copy.wait()

    @pl.loop(0, 3 * D // 256)
    def _(step):
        at = pl.ds(pl.multiple_of(step * 256, 256), 256)
        qkv_ref[:, at] = mul(placed_ref[...], w_ref[:, at]).astype(bf16)

    for row0, count, key0, keys in windows:
        mask = twice(same_sequence(count, row0, keys, key0, IMG_LEN))
        attend(qkv_ref, att_ref, pl.ds(row0, count), pl.ds(key0, keys), mask)
    place_columns(att_ref)

    @pl.loop(0, D // 256)
    def _(step):
        at = pl.ds(pl.multiple_of(step * 256, 256), 256)
        there = pl.ds(pl.multiple_of(step * 256 + 3 * D, 256), 256)
        mid_ref[:, at] = x_ref[:, at].astype(f32) + mul(placed_ref[...], w_ref[:, there])

    norm_rows(mid_ref, h2_ref, g2_ref[...].astype(f32), b2_ref[...].astype(f32), chunk)
    for k in range(rows // IMG_LEN):
        first, last = k * IMG_LEN, (k + 1) * IMG_LEN
        start, end = first // 8 * 8, -(-last // 8) * 8
        values = mid_ref[start:end, :]
        place = lax.broadcasted_iota(jnp.int32, values.shape, 0) + start
        inside = (place >= first) & (place < last)
        sum_ref[k : k + 1, :] = jnp.sum(jnp.where(inside, values, 0.0), axis=0, keepdims=True)


def image_front(rows_in, pieces, perm, gain1, bias1, gain2, bias2):
    rows = rows_in.shape[0]
    windows = ((0, 208, 0, 256), (208, 192, 192, 208))
    vmem = pl.BlockSpec(memory_space=pltpu.VMEM)
    return pl.pallas_call(
        functools.partial(image_front_kernel, windows),
        out_shape=[
            jax.ShapeDtypeStruct((rows, D), bf16),
            jax.ShapeDtypeStruct((rows // IMG_LEN, D), f32),
        ],
        in_specs=[vmem] * 6 + anywhere(pieces),
        out_specs=[vmem] * 2,
        scratch_shapes=[
            pltpu.VMEM((D, 4 * D), bf16),
            pltpu.VMEM((rows, D), bf16),
            pltpu.VMEM((rows, D), bf16),
            pltpu.VMEM((rows, 3 * D), bf16),
            pltpu.VMEM((rows, D), bf16),
            pltpu.VMEM((rows, D), f32),
            pltpu.SemaphoreType.DMA((len(pieces),)),
        ],
        compiler_params=params(),
        cost_estimate=cost(rows * D * D * 12, 8 * D * D, rows * 256 * HEADS),
        name="image_front",
    )(rows_in, perm, gain1[None], bias1[None], gain2[None], bias2[None], *pieces)


def gelu_parts(inner):
    half = 0.5 * (1.0 + lax.erf(inner * (0.5**0.5)))
    return inner * half, half


def pack_kernel(unit_ref, pos_ref, *refs):
    refs[-1][:, :D] = unit_ref[...].astype(bf16)
    refs[-1][:, D:] = pos_ref[...]


def packed(unit, positive, after):
    shape = (unit.shape[0], D + positive.shape[1])
    return pl.pallas_call(
        pack_kernel,
        out_shape=jax.ShapeDtypeStruct(shape, bf16),
        in_specs=[pl.BlockSpec(memory_space=pltpu.VMEM)] * 2 + anywhere(after),
        compiler_params=params(),
        cost_estimate=cost(shape[0] * shape[1], 4 * shape[0] * shape[1]),
        name="packed",
    )(unit, positive, *after)


def pool_matrix(count, rows, row0, seq_len):
    row = (lax.broadcasted_iota(jnp.int32, (count, rows), 1) + row0) // seq_len
    return jnp.where(row == lax.broadcasted_iota(jnp.int32, (count, rows), 0), 1.0, 0.0).astype(bf16)


def two_terms(mean):
    high = mean.astype(bf16)
    low = (mean - high.astype(f32)).astype(bf16)
    return jnp.concatenate([high, low], axis=0)


def unit_rows(pooled):
    inverse = lax.rsqrt(jnp.sum(pooled * pooled, axis=-1, keepdims=True) + norm_eps)
    return pooled * inverse, inverse


def text_up_kernel(h2_ref, wu_ref, wd_ref, sum_ref, *refs):
    slope_ref, hid_ref, unit_ref, inv_ref, acc = refs[-5:]
    step = pl.program_id(0)
    chunk = 128
    per = chunk // TXT_LEN
    pool = pool_matrix(per, chunk, 0, TXT_LEN)
    for k in range(h2_ref.shape[0] // chunk):
        inner = mul(h2_ref[k * chunk : (k + 1) * chunk, :], wu_ref[...])
        value, half = gelu_parts(inner)
        slope = half + inner * (jnp.exp(-0.5 * inner * inner) * 0.3989422804014327)
        slope_ref[k * chunk : (k + 1) * chunk, :] = slope.astype(bf16)
        hid_ref[k * per : (k + 1) * per, :] = mul(pool, value.astype(bf16))
    terms = mul(two_terms(hid_ref[...] * (1.0 / TXT_LEN)), wd_ref[...])
    count = hid_ref.shape[0]
    added = terms[:count] + terms[count:]

    @pl.when(step == 0)
    def _():
        acc[...] = sum_ref[...] * (1.0 / TXT_LEN) + added

    @pl.when(step > 0)
    def _():
        acc[...] += added

    @pl.when(step == pl.num_programs(0) - 1)
    def _():
        unit, inverse = unit_rows(acc[...])
        unit_ref[...] = unit
        inv_ref[...] = jnp.broadcast_to(inverse, inv_ref.shape)


def text_up(normed2, weight_up, weight_down, middle_sum, after=()):
    rows, count = normed2.shape[0], middle_sum.shape[0]
    fixed = lambda shape: pl.BlockSpec(shape, lambda i: (0, 0))
    return pl.pallas_call(
        text_up_kernel,
        grid=(FF // TILE,),
        out_shape=[
            jax.ShapeDtypeStruct((rows, FF), bf16),
            jax.ShapeDtypeStruct((count, FF), f32),
            jax.ShapeDtypeStruct((count, D), f32),
            jax.ShapeDtypeStruct((count, 128), f32),
        ],
        in_specs=[
            fixed((rows, D)),
            pl.BlockSpec((D, TILE), lambda i: (0, i)),
            pl.BlockSpec((TILE, D), lambda i: (i, 0)),
            fixed((count, D)),
        ]
        + anywhere(after),
        out_specs=[
            pl.BlockSpec((rows, TILE), lambda i: (0, i)),
            pl.BlockSpec((count, TILE), lambda i: (0, i)),
            fixed((count, D)),
            fixed((count, 128)),
        ],
        scratch_shapes=[pltpu.VMEM((count, D), f32)],
        compiler_params=params(),
        cost_estimate=cost(2 * rows * D * FF, 4 * D * FF + 2 * rows * FF, 20 * rows * FF),
        name="text_up",
    )(normed2, weight_up, weight_down, middle_sum, *after)


def image_up_kernel(fold, h2_ref, wu_ref, wd_ref, sum_ref, *refs):
    out_ref, acc = refs[-2:]
    step = pl.program_id(0)
    rows, count = h2_ref.shape[0], sum_ref.shape[0]
    chunk = 80
    summed = jnp.zeros((count, TILE), f32)
    for k in range(rows // chunk):
        inner = mul(h2_ref[k * chunk : (k + 1) * chunk, :], wu_ref[...])
        value, _ = gelu_parts(inner)
        pool = pool_matrix(count, chunk, k * chunk, IMG_LEN)
        summed = summed + mul(pool, value.astype(bf16))
    mean = two_terms(summed * (1.0 / IMG_LEN))
    place = lax.broadcasted_iota(jnp.int32, (TILE, TILE // fold), 0)
    picked = lax.broadcasted_iota(jnp.int32, (TILE, TILE // fold), 1) * fold
    terms = jnp.zeros((2 * count, D), f32)
    for k in range(fold):
        chosen = jnp.where(place == picked + k, 1.0, 0.0).astype(bf16)
        part = mul(mean, chosen).astype(bf16)
        terms = terms + mul(part, wd_ref[:, k * D : (k + 1) * D])
    added = terms[:count] + terms[count:]

    @pl.when(step == 0)
    def _():
        acc[...] = sum_ref[...] * (1.0 / IMG_LEN) + added

    @pl.when(step > 0)
    def _():
        acc[...] += added

    @pl.when(step == pl.num_programs(0) - 1)
    def _():
        out_ref[...] = unit_rows(acc[...])[0].astype(bf16)


def image_up(normed2, whole, up_col, down_col, middle_sum, after=()):
    rows, count = normed2.shape[0], middle_sum.shape[0]
    fold = FF // D
    fixed = lambda shape: pl.BlockSpec(shape, lambda i: (0, 0))
    return pl.pallas_call(
        functools.partial(image_up_kernel, fold),
        grid=(FF // TILE,),
        out_shape=jax.ShapeDtypeStruct((count, D), bf16),
        in_specs=[
            fixed((rows, D)),
            pl.BlockSpec((D, TILE), lambda i: (0, up_col // TILE + i)),
            pl.BlockSpec((TILE // fold, fold * D), lambda i: (i, down_col // (fold * D))),
            fixed((count, D)),
        ]
        + anywhere(after),
        out_specs=fixed((count, D)),
        scratch_shapes=[pltpu.VMEM((count, D), f32)],
        compiler_params=params(),
        cost_estimate=cost(2 * rows * D * FF, 4 * D * FF, 15 * rows * FF),
        name="image_up",
    )(normed2, whole, whole, middle_sum, *after)


def loss_parts(text_rows, pos, image_all):
    similar = mul_bt(text_rows, image_all) * logit_scale
    shifted = jnp.exp(similar - logit_scale)
    alive = jnp.max(pos, axis=1, keepdims=True)
    row_sum = jnp.sum(shifted, axis=1, keepdims=True)
    row_count = jnp.maximum(jnp.sum(pos, axis=1, keepdims=True), 1.0)
    return similar, shifted, alive, row_sum, row_count


def sums_over_captions(text_rows, pos, image_all):
    similar, shifted, alive, row_sum, row_count = loss_parts(text_rows, pos, image_all)
    pos_similar = pos * similar
    cap_term = alive * (
        logit_scale + jnp.log(row_sum) - jnp.sum(pos_similar, axis=1, keepdims=True) / row_count
    )
    return (
        jnp.sum(alive * shifted, axis=0, keepdims=True),
        jnp.sum(pos, axis=0, keepdims=True),
        jnp.sum(pos_similar, axis=0, keepdims=True),
        jnp.sum(cap_term, axis=0, keepdims=True),
        jnp.sum(alive, axis=0, keepdims=True),
    )


def loss_from(sums):
    col_sum, col_count, col_pos, cap_total, live_total = sums
    img_term = logit_scale + jnp.log(col_sum) - col_pos / col_count
    return 0.5 * cap_total / live_total + 0.5 * jnp.mean(img_term, axis=1, keepdims=True)


def grad_of_unit(text_rows, pos, image_all, col_sum, col_count, live_total):
    _, shifted, alive, row_sum, row_count = loss_parts(text_rows, pos, image_all)
    cap_share, img_share = 0.5 / live_total, 0.5 / image_all.shape[0]
    grad_sims = alive * shifted * (cap_share / row_sum + img_share / col_sum) - pos * (
        cap_share / row_count + img_share / col_count
    )
    return mul(grad_sims.astype(bf16), image_all) * logit_scale


def turned(grad, unit):
    return grad - unit * jnp.sum(grad * unit, axis=-1, keepdims=True)


def loss_kernel(
    pack_ref, image_ref, own_ref, unit_ref, inv_ref, loss_ref, row_ref, low_ref, col_sum_ref,
    col_count_ref, live_ref
):
    image_all = image_ref[...]
    chunk = 256
    total = None
    for k in range(pack_ref.shape[0] // chunk):
        at = slice(k * chunk, (k + 1) * chunk)
        part = sums_over_captions(pack_ref[at, :D], pack_ref[at, D:].astype(f32), image_all)
        total = part if total is None else [a + b for a, b in zip(total, part)]
    loss_ref[...] = jnp.broadcast_to(loss_from(total), loss_ref.shape)
    col_sum, col_count, _, _, live_total = total
    col_sum_ref[...] = col_sum
    col_count_ref[...] = col_count
    live_ref[...] = jnp.broadcast_to(live_total, live_ref.shape)
    grad = grad_of_unit(
        own_ref[:, :D], own_ref[:, D:].astype(f32), image_all, col_sum, col_count, live_total
    )
    row = inv_ref[:, :1] * turned(grad, unit_ref[...]) * (1.0 / TXT_LEN)
    row_ref[...] = row
    low_ref[...] = row.astype(bf16)


def loss_and_rows(pack, image_all, own_pack, unit, inverse):
    images, count = image_all.shape[0], own_pack.shape[0]
    shapes = [(1, 128), (count, D), (count, D), (1, images), (1, images), (1, 128)]
    kinds = [f32, f32, bf16, f32, f32, f32]
    return pl.pallas_call(
        loss_kernel,
        out_shape=[jax.ShapeDtypeStruct(*item) for item in zip(shapes, kinds)],
        compiler_params=params(),
        cost_estimate=cost(2 * pack.shape[0] * images * D, 2 * pack.size, pack.shape[0] * images),
        name="loss_and_rows",
    )(pack, image_all, own_pack, unit, inverse)


def down_kernel(pack_ref, image_ref, col_sum_ref, col_count_ref, live_ref, hid_ref, *refs):
    step, out_ref = pl.program_id(0), refs[-1]
    text_rows = pack_ref[:, :D]
    grad = grad_of_unit(
        text_rows, pack_ref[:, D:].astype(f32), image_ref[...], col_sum_ref[...],
        col_count_ref[...], live_ref[:, :1]
    )
    rows = (turned(grad, text_rows.astype(f32)) * (1.0 / TXT_LEN)).astype(bf16)
    part = mul_at(hid_ref[...], rows)

    @pl.when(step == 0)
    def _():
        out_ref[...] = part

    @pl.when(step > 0)
    def _():
        out_ref[...] += part


def grad_of_down(pack, image_all, col_sum, col_count, live_total, hidden_cols, after):
    images, chunk = image_all.shape[0], 256
    fixed = lambda shape: pl.BlockSpec(shape, lambda i: (0, 0))
    per = hidden_cols.shape[1]
    return pl.pallas_call(
        down_kernel,
        grid=(pack.shape[0] // chunk,),
        out_shape=jax.ShapeDtypeStruct((per, D), f32),
        in_specs=[
            pl.BlockSpec((chunk, pack.shape[1]), lambda i: (i, 0)),
            fixed((images, D)), fixed((1, images)), fixed((1, images)), fixed((1, 128)),
            pl.BlockSpec((chunk, per), lambda i: (i, 0)),
        ]
        + anywhere(after),
        out_specs=fixed((per, D)),
        compiler_params=params(),
        cost_estimate=cost(4 * pack.shape[0] * images * D, 2 * pack.size, pack.shape[0] * images),
        name="grad_of_down",
    )(pack, image_all, col_sum, col_count, live_total, hidden_cols, *after)


def mlp_back_kernel(
    low_ref, wd_ref, slope_ref, wu_ref, lhs_ref, mid_ref, gain_ref, row_ref, keep_a, send_a, keep_b,
    send_b, out_ref, gain_out, bias_out, acc
):
    step = pl.program_id(0)
    count, rows = low_ref.shape[0], slope_ref.shape[0]
    half = D // 2
    hidden = mul_bt(low_ref[...], wd_ref[...])
    wide = jnp.broadcast_to(hidden[:, None, :], (count, TXT_LEN, TILE)).reshape(rows, TILE)
    inner = (wide * slope_ref[...].astype(f32)).astype(bf16)
    weight = mul(lhs_ref[0], inner).astype(bf16)

    @pl.when(step < pl.num_programs(0) // 2)
    def _():
        keep_a[...] = weight[:half]
        send_a[...] = weight[half:]

    @pl.when(step >= pl.num_programs(0) // 2)
    def _():
        keep_b[...] = weight[:half]
        send_b[...] = weight[half:]

    added = mul_bt(inner, wu_ref[...])

    @pl.when(step == 0)
    def _():
        acc[...] = added

    @pl.when(step > 0)
    def _():
        acc[...] += added

    @pl.when(step == pl.num_programs(0) - 1)
    def _():
        chunk = 128
        per = chunk // TXT_LEN
        gain = gain_ref[...]
        gain_out[...] = jnp.zeros_like(gain_out)
        bias_out[...] = jnp.zeros_like(bias_out)

        @pl.loop(0, rows // chunk)
        def _(k):
            at = pl.ds(pl.multiple_of(k * chunk, chunk), chunk)
            unit, scale = norm_parts(mid_ref[at, :])
            grad = acc[at, :]
            gain_out[...] += jnp.sum(grad * unit, axis=0, keepdims=True)
            bias_out[...] += jnp.sum(grad, axis=0, keepdims=True)
            row = row_ref[pl.ds(pl.multiple_of(k * per, per), per), :]
            row = jnp.broadcast_to(row[:, None, :], (per, TXT_LEN, D)).reshape(chunk, D)
            out_ref[at, :] = row + norm_back(unit, scale, gain, grad)


def mlp_back(grad_row, grad_low, weight_down, slope, weight_up, lhs, middle, gain):
    rows, count = slope.shape[0], grad_row.shape[0]
    steps = FF // TILE
    fixed = lambda shape: pl.BlockSpec(shape, lambda i: (0, 0))
    first = pl.BlockSpec((D // 2, TILE), lambda i: (0, jnp.minimum(i, steps // 2 - 1)))
    second = pl.BlockSpec((D // 2, TILE), lambda i: (0, jnp.maximum(i - steps // 2, 0)))
    part = jax.ShapeDtypeStruct((D // 2, FF // 2), bf16)
    line = jax.ShapeDtypeStruct((1, D), f32)
    return pl.pallas_call(
        mlp_back_kernel,
        grid=(steps,),
        out_shape=[part] * 4 + [jax.ShapeDtypeStruct((rows, D), f32), line, line],
        in_specs=[
            fixed((count, D)),
            pl.BlockSpec((TILE, D), lambda i: (i, 0)),
            pl.BlockSpec((rows, TILE), lambda i: (0, i)),
            pl.BlockSpec((D, TILE), lambda i: (0, i)),
            pl.BlockSpec((1, D, rows), lambda i: (i // (steps // 2), 0, 0)),
            fixed((rows, D)),
            fixed((1, D)),
            fixed((count, D)),
        ],
        out_specs=[first, first, second, second, fixed((rows, D)), fixed((1, D)), fixed((1, D))],
        scratch_shapes=[pltpu.VMEM((rows, D), f32)],
        compiler_params=params(),
        cost_estimate=cost(4 * rows * D * FF, 4 * D * FF + 2 * rows * FF + 2 * D * FF, rows * FF),
        name="mlp_back",
    )(grad_low, weight_down, slope, weight_up, lhs, middle, gain[None], grad_row)


def attention_back_kernel(grad_ref, wo_ref, qkv_ref, *refs):
    low_ref, out_ref = refs[-2:]
    chunk = grad_ref.shape[0]
    one = same_sequence(chunk, 0, chunk, 0, TXT_LEN)
    mask = jnp.concatenate([one, one], axis=0)
    low = grad_ref[...].astype(bf16)
    low_ref[...] = low
    grad_att = mul_bt(low, wo_ref[...]).astype(bf16)
    for pair in range(HEADS // 2):
        queries = two_heads(qkv_ref[:, pair_cols(0, pair)] * bf16(HEAD ** (-0.5)))
        keys = qkv_ref[:, pair_cols(1, pair)]
        vals = qkv_ref[:, pair_cols(2, pair)]
        grads = two_heads(grad_att[:, pair_cols(0, pair)])
        probs = masked_softmax(mul_bt(queries, keys), mask)
        grad_probs = mul_bt(grads, vals)
        along = jnp.sum(grad_probs * probs, axis=-1, keepdims=True)
        grad_scores = (probs * (grad_probs - along)).astype(bf16)
        side = jnp.concatenate([grad_scores[:chunk], grad_scores[chunk:]], axis=1)
        grad_q = mul(side, two_heads(keys)) * HEAD ** (-0.5)
        grad_k = mul_at(grad_scores, queries)
        grad_v = mul_at(probs.astype(bf16), grads)
        out_ref[:, pair_cols(0, pair)] = grad_q.astype(bf16)
        out_ref[:, pair_cols(1, pair)] = grad_k.astype(bf16)
        out_ref[:, pair_cols(2, pair)] = grad_v.astype(bf16)


def attention_back(grad_middle, weight_out, project, first, count, after=()):
    chunk = 128
    rows = count * chunk
    return pl.pallas_call(
        attention_back_kernel,
        grid=(count,),
        out_shape=[
            jax.ShapeDtypeStruct((rows, D), bf16),
            jax.ShapeDtypeStruct((rows, 3 * D), bf16),
        ],
        in_specs=[
            pl.BlockSpec((chunk, D), lambda i: (i + first, 0)),
            pl.BlockSpec((D, D), lambda i: (0, 0)),
            pl.BlockSpec((chunk, 3 * D), lambda i: (i + first, 0)),
        ]
        + anywhere(after),
        out_specs=[
            pl.BlockSpec((chunk, D), lambda i: (i, 0)),
            pl.BlockSpec((chunk, 3 * D), lambda i: (i, 0)),
        ],
        compiler_params=params(),
        cost_estimate=cost(10 * rows * D * D, 16 * rows * D + 2 * D * D, rows * 128 * HEADS),
        name="attention_back",
    )(grad_middle, weight_out, project, *after)


def mul_rows(lhs, parts):
    total, row = 0.0, 0
    for part in parts:
        total = total + mul(lhs[:, row : row + part.shape[0]], part[...])
        row += part.shape[0]
    return total


def weight_back_kernel(counts, lhs_ref, *refs):
    step, half = pl.program_id(0), D // 2
    keep, send = refs[-2:]
    row = 0
    for k, count in enumerate(counts):
        parts = refs[row : row + count]
        row += count

        @pl.when(step == k if len(counts) > 1 else step >= 0)
        def _(parts=parts):
            weight = mul_rows(lhs_ref[0], parts).astype(bf16)
            keep[...] = weight[:half]
            send[...] = weight[half:]


def weight_back(lhs, first, groups, blocks, after=()):
    rows = lhs.shape[2]
    steps = 2
    many = len(groups) > 1
    given = [part for group in groups for part in group]
    return pl.pallas_call(
        functools.partial(weight_back_kernel, [len(group) for group in groups]),
        grid=(steps,),
        out_shape=[jax.ShapeDtypeStruct((D // 2, steps * D), bf16)] * 2,
        in_specs=[pl.BlockSpec((1, D, rows), lambda i: (first + (i if many else 0), 0, 0))]
        + [
            pl.BlockSpec((part.shape[0], D), lambda i, col=col: (0, col + (0 if many else i)))
            for group, col in zip(groups, blocks)
            for part in group
        ]
        + anywhere(after),
        out_specs=[pl.BlockSpec((D // 2, D), lambda i: (0, i))] * 2,
        compiler_params=params(),
        cost_estimate=cost(4 * rows * D * D, 4 * rows * D + 7 * D * D),
        name="weight_back",
    )(lhs, *given, *after)


def input_back_kernel(count, *refs):
    projs = refs[:count]
    w_ref, x_ref, gain_ref, mid_ref = refs[count : count + 4]
    out_ref, gain_out, bias_out, acc = refs[-4:]
    step = pl.program_id(0)
    rows, chunk = x_ref.shape[0], 128
    row = 0
    for part in projs:
        at = slice(row, row + part.shape[0])
        row += part.shape[0]
        added = mul_bt(part[...], w_ref[...])

        @pl.when(step == 0)
        def _(at=at, added=added):
            acc[at, :] = added

        @pl.when(step > 0)
        def _(at=at, added=added):
            acc[at, :] += added

    @pl.when(step == pl.num_programs(0) - 1)
    def _():
        gain = gain_ref[...]
        gain_out[...] = jnp.zeros_like(gain_out)
        bias_out[...] = jnp.zeros_like(bias_out)

        @pl.loop(0, rows // chunk)
        def _(k):
            at = pl.ds(pl.multiple_of(k * chunk, chunk), chunk)
            unit, scale = norm_parts(x_ref[at, :].astype(f32))
            grad = acc[at, :]
            gain_out[...] += jnp.sum(grad * unit, axis=0, keepdims=True)
            bias_out[...] += jnp.sum(grad, axis=0, keepdims=True)
            out_ref[at, :] = mid_ref[at, :] + norm_back(unit, scale, gain, grad)


def input_back(grad_projs, weight, rows_in, gain, grad_middle, after=()):
    rows = rows_in.shape[0]
    fixed = lambda shape: pl.BlockSpec(shape, lambda i: (0, 0))
    line = jax.ShapeDtypeStruct((1, D), f32)
    return pl.pallas_call(
        functools.partial(input_back_kernel, len(grad_projs)),
        grid=(3,),
        out_shape=[jax.ShapeDtypeStruct((rows, D), f32), line, line],
        in_specs=[pl.BlockSpec((part.shape[0], D), lambda i: (0, i)) for part in grad_projs]
        + [
            pl.BlockSpec((D, D), lambda i: (0, i)),
            fixed((rows, D)), fixed((1, D)), fixed((rows, D)),
        ]
        + anywhere(after),
        out_specs=[fixed((rows, D)), fixed((1, D)), fixed((1, D))],
        scratch_shapes=[pltpu.VMEM((rows, D), f32)],
        compiler_params=params(),
        cost_estimate=cost(6 * rows * D * D, 14 * rows * D + 6 * D * D),
        name="input_back",
    )(*grad_projs, weight, rows_in, gain[None], grad_middle, *after)


def local(
    images,
    captions,
    img_gain1,
    img_bias1,
    img_qkv,
    img_out,
    img_gain2,
    img_bias2,
    img_up,
    img_down,
    txt_gain1,
    txt_bias1,
    txt_qkv,
    txt_out,
    txt_gain2,
    txt_bias2,
    txt_up,
    txt_down,
    counts,
    matches,
):
    peers = lax.axis_size(AXIS)
    own = lax.axis_index(AXIS)
    per = D // peers
    img_local = counts.shape[0]
    cap_local = matches.shape[0]
    total_images = matches.shape[1]

    whole = lax.all_gather(
        jnp.concatenate([img_up.reshape(per, FF), img_down.reshape(per, FF)], axis=1),
        AXIS,
        axis=0,
        tiled=True,
    )
    small = peers == 32
    shard = jnp.concatenate([img_qkv.reshape(per, 3 * D), img_out.reshape(per, D)], axis=1)
    if small:
        line, perm = gathered_line(shard), row_order((1, 4, 2, 16, 8))
    else:
        line, perm = lax.all_gather(shard, AXIS, axis=0, tiled=True), jnp.eye(D, dtype=bf16)

    normed1, project, attended, middle, normed2, middle_sum = text_front(
        captions, txt_gain1, txt_bias1, txt_qkv, txt_out, txt_gain2, txt_bias2
    )
    middle_sum, line = in_turn(middle_sum, line)
    beside, above = (swapped(line, 2), swapped(line, 4)) if small else (line, line)
    slope, hidden_sum, text_unit, inverse = text_up(
        normed2, txt_up, txt_down, middle_sum, (line,)
    )
    text_unit, (beside, above) = in_turn(text_unit, (beside, above))
    pieces = gathered_rows(line, beside, above) if small else [line]

    ends_at = jnp.cumsum(counts)
    slot_ids = lax.iota(jnp.int32, cap_local)
    owner = jnp.sum((ends_at[None, :] <= slot_ids[:, None]).astype(jnp.int32), axis=1)
    owner = owner + own * img_local
    live = slot_ids < ends_at[-1]
    columns = lax.iota(jnp.int32, total_images)
    positive = ((matches > 0) | (owner[:, None] == columns[None, :])) & live[:, None]

    own_pack = packed(text_unit, positive.astype(bf16), pieces[1:5] if small else ())

    normed_img, middle_img = image_front(
        images, pieces, perm, img_gain1, img_bias1, img_gain2, img_bias2
    )
    if small:
        held = own_pack[None]
        scaled_sum = (hidden_sum * inverse[:, :1]).astype(bf16)
        normed_img, scaled_sum, other = lax.optimization_barrier(
            (normed_img, scaled_sum, swapped(held, 16))
        )
        held = joined(held, other, 16)
        hidden_cols = lax.all_to_all(scaled_sum, AXIS, split_axis=1, concat_axis=0, tiled=True)
        held = joined(held, swapped(held, 8), 8)
        whole, other = in_turn(whole, swapped(held, 4))
        held = joined(held, other, 4)
        other = swapped(held, 2)
    image_low = image_up(normed_img, whole, 0, FF, middle_img)
    if small:
        image_low, other, hidden_cols = lax.optimization_barrier((image_low, other, hidden_cols))
        held = joined(held, other, 2)
        text_pack = joined(held, swapped(held, 1), 1).reshape(-1, D + total_images)
    image_all = spread(image_low).reshape(total_images, D)

    order_a, order_b, tail = stage_orders()
    matrix_a, matrix_b = row_order(order_a + tail[::-1]), row_order(order_b + tail[::-1])
    lhs_up = jnp.stack([placed(matrix_a, normed2), placed(matrix_b, normed2)])
    lhs_rest = jnp.stack(
        [placed(matrix_a, normed1), placed(matrix_b, normed1), placed(matrix_b, attended)]
    )

    if small:
        loss_value, grad_row, row_low, col_sum, col_count, live_total = loss_and_rows(
            text_pack, image_all, own_pack, text_unit, inverse
        )
        loss_value = loss_value[0, 0]
    else:
        text_low, pos = own_pack[:, :D], own_pack[:, D:].astype(f32)
        sums = lax.psum(sums_over_captions(text_low, pos, image_all), AXIS)
        loss_value = loss_from(sums)[0, 0]
        grad = grad_of_unit(text_low, pos, image_all, sums[0], sums[1], sums[4])
        grad_row = inverse[:, :1] * turned(grad, text_unit) * (1.0 / TXT_LEN)
        row_low = grad_row.astype(bf16)

    *up, grad_middle, gain_two, bias_two = mlp_back(
        grad_row, row_low, txt_down, slope, txt_up, lhs_up, middle, txt_gain2
    )
    stages = len(order_a)
    low_one, proj_one = attention_back(grad_middle, txt_out, project, 0, 2)
    for stage in range(stages - 2):
        up = fold(hand_on(up, stage), (proj_one,))
    low_two, proj_two = attention_back(grad_middle, txt_out, project, 2, 3, up)
    up = fold(hand_on(up, stages - 2), (proj_two,))
    projs, lows = (proj_one, proj_two), (low_one, low_two)
    rest_a = weight_back(lhs_rest, 0, [projs], [0], up)
    up = hand_on_last(fold_last(hand_on(up, stages - 1), rest_a[1:]))
    rest_b = weight_back(lhs_rest, 1, [projs, lows], [2, 0], up[:1])
    rest = [*rest_a, *rest_b]
    for stage in range(stages - 2):
        rest = fold(hand_on(rest, stage), up[1])
    caption_grad, gain_one, bias_one = input_back(
        projs, txt_qkv, captions, txt_gain1, grad_middle, rest[:1]
    )
    rest = fold(hand_on(rest, stages - 2), (caption_grad,))
    if small:
        grad_down = grad_of_down(
            text_pack, image_all, col_sum, col_count, live_total, hidden_cols, rest
        )
        rest = fold_last(hand_on(rest, stages - 1), (grad_down,))
    else:
        grad_down = lax.psum_scatter(
            mul_at(hidden_sum.astype(bf16), row_low), AXIS, scatter_dimension=0, tiled=True
        )
        rest = fold_last(hand_on(rest, stages - 1))
    up_share = sum_last(*up)
    rest_share = sum_last(*hand_on_last(rest))
    norms = jnp.concatenate([gain_one, bias_one, gain_two, bias_two], axis=0)
    norms = jnp.sum(spread(norms[None]), axis=0).reshape(4, D)
    return (
        loss_value,
        caption_grad,
        norms[0],
        norms[1],
        rest_share[:, : 3 * D].reshape(-1),
        rest_share[:, 3 * D :].reshape(-1),
        norms[2],
        norms[3],
        up_share.reshape(-1),
        grad_down.reshape(-1),
    )


def solution(mesh):
    split, flat, whole = P("blk", None), P("blk"), P()
    image_block = (whole, whole, flat, flat, whole, whole, flat, flat)
    return jax.shard_map(
        local,
        mesh=mesh,
        in_specs=(split, split) + image_block + (whole,) * 8 + (flat, split),
        out_specs=(whole, split, whole, whole, flat, flat, whole, whole, flat, flat),
        check_vma=False,
    )
```

```python
import functools

import jax
import jax.numpy as jnp
from jax import lax
from jax.experimental import pallas as pl
from jax.experimental.pallas import tpu as pltpu
from jax.sharding import PartitionSpec as P

D = 768
FF = 3072
HEAD = 64
HEADS = D // HEAD
IMG_LEN = 50
TXT_LEN = 16
AXIS = "blk"

norm_eps = 1e-06
logit_scale = 50.0
f32 = jnp.float32
bf16 = jnp.bfloat16


def swapped(value, mask):
    peers = lax.axis_size(AXIS)
    return lax.ppermute(value, AXIS, [(i, i ^ mask) for i in range(peers)])


def bit_masks():
    peers = lax.axis_size(AXIS)
    return [1 << k for k in range(peers.bit_length() - 1)]


def joined(held, other, mask):
    upper = (lax.axis_index(AXIS) & mask) > 0
    first = jnp.where(upper, other, held)
    second = jnp.where(upper, held, other)
    return jnp.stack([first, second], axis=1).reshape((-1,) + held.shape[1:])


def spread(block):
    peers = lax.axis_size(AXIS)
    copies = jnp.broadcast_to(block[None], (peers,) + block.shape)
    return lax.all_to_all(copies, AXIS, split_axis=0, concat_axis=0, tiled=True)


def stage_orders():
    masks = bit_masks()
    head, tail = masks[:-2], masks[-2:]
    order_a = list(head)
    order_b = list(head)
    for k in range(1, len(head) - 1, 2):
        order_b[k], order_b[k + 1] = order_b[k + 1], order_b[k]
    return order_a, order_b, tail


def row_order(bits):
    peers = lax.axis_size(AXIS)
    own = lax.axis_index(AXIS)
    per = D // peers
    places = lax.iota(jnp.int32, D)
    block = places // per
    target = jnp.zeros_like(block) + own
    for k, mask in enumerate(bits):
        target = target ^ (((block >> (len(bits) - 1 - k)) & 1) * mask)
    source = target * per + places % per
    return (source[:, None] == lax.iota(jnp.int32, D)[None, :]).astype(bf16)


def gathered_line(shard):
    return jnp.concatenate([shard] + [swapped(shard, mask) for mask in (8, 16, 24)], axis=0)


def gathered_rows(line, beside, above):
    half = line.shape[0] // 2
    pieces = [line, beside, above, swapped(beside[:half], 4), swapped(above[half:], 2)]
    return pieces + [swapped(piece, 1) for piece in pieces]


def in_turn(first, then):
    return lax.optimization_barrier((first, then))


def placed(order, values):
    return mul_bt(order, values).astype(bf16)


def hand_on(parts, stage):
    order_a, order_b, _ = stage_orders()
    keep_a, send_a, keep_b, send_b = parts
    return keep_a, swapped(send_a, order_a[stage]), keep_b, swapped(send_b, order_b[stage])


def hand_on_last(blocks):
    low, high = stage_orders()[2]
    own, *others = blocks
    return own, [swapped(block, mask) for block, mask in zip(others, (low, high, low | high))]


def sum_last(own, others):
    total = own
    for other in others:
        total = total + other.astype(f32)
    return total


VMEM_BYTES = 56 << 20
TILE = 512


def norm_parts(values):
    average = jnp.mean(values, axis=-1, keepdims=True)
    centred = values - average
    variance = jnp.mean(centred * centred, axis=-1, keepdims=True)
    scale = lax.rsqrt(variance + norm_eps)
    return centred * scale, scale


def norm_back(unit, scale, gain, grad):
    inner = grad * gain
    shift = jnp.mean(inner, axis=-1, keepdims=True)
    along = jnp.mean(inner * unit, axis=-1, keepdims=True)
    return scale * (inner - shift - unit * along)


def mul(lhs, rhs):
    return jnp.dot(lhs, rhs, preferred_element_type=f32)


def mul_bt(lhs, rhs):
    return lax.dot_general(lhs, rhs, (((1,), (1,)), ((), ())), preferred_element_type=f32)


def mul_at(lhs, rhs):
    return lax.dot_general(lhs, rhs, (((0,), (0,)), ((), ())), preferred_element_type=f32)


def params(**more):
    return pltpu.CompilerParams(vmem_limit_bytes=VMEM_BYTES, **more)


def cost(flops, moved, transcendentals=0):
    return pl.CostEstimate(flops=flops, bytes_accessed=moved, transcendentals=transcendentals)


def lane_halves(dtype):
    lane = lax.broadcasted_iota(jnp.int32, (1, 2 * HEAD), 1)
    low = jnp.where(lane < HEAD, 1.0, 0.0)
    return low.astype(dtype), (1.0 - low).astype(dtype)


def two_heads(pair):
    low, high = lane_halves(bf16)
    return jnp.concatenate([pair * low, pair * high], axis=0)


def same_sequence(rows, row0, cols, col0, seq_len):
    row = (lax.broadcasted_iota(jnp.int32, (rows, cols), 0) + row0) // seq_len
    col = (lax.broadcasted_iota(jnp.int32, (rows, cols), 1) + col0) // seq_len
    return row == col


def softmax_down(scores, mask):
    keys = mask.shape[0]
    parts, sums = [], []
    for k in range(2):
        part = jnp.where(mask, scores[k * keys : (k + 1) * keys], -1e30)
        most = jnp.max(part, axis=0, keepdims=True)
        raised = jnp.exp(part - most)
        total = jnp.sum(raised, axis=0, keepdims=True)
        parts.append(raised * (1.0 / total))
        sums.append(most + jnp.log(total))
    return parts, sums


def fold_kernel(keep_a, got_a, keep_b, got_b, *refs):
    outs = refs[-4:]
    half = outs[0].shape[0]
    for k, (kept, got) in enumerate(((keep_a, got_a), (keep_b, got_b))):
        for j in range(2):
            at = slice(j * half, (j + 1) * half)
            outs[2 * k + j][...] = (kept[at, :].astype(f32) + got[at, :].astype(f32)).astype(bf16)


def fold(parts, after=()):
    rows, cols = parts[0].shape
    if rows % 32:
        whole = [
            (kept.astype(f32) + got.astype(f32)).astype(bf16)
            for kept, got in (parts[:2], parts[2:])
        ]
        return [part for one in whole for part in (one[: rows // 2], one[rows // 2 :])]
    tile = 512
    return pl.pallas_call(
        fold_kernel,
        grid=(cols // tile,),
        out_shape=[jax.ShapeDtypeStruct((rows // 2, cols), bf16)] * 4,
        in_specs=[pl.BlockSpec((rows, tile), lambda i: (0, i))] * 4 + anywhere(after),
        out_specs=[pl.BlockSpec((rows // 2, tile), lambda i: (0, i))] * 4,
        compiler_params=params(),
        cost_estimate=cost(2 * rows * cols, 12 * rows * cols),
        name="fold",
    )(*parts, *after)


def fold_last_kernel(keep_a, got_a, keep_b, got_b, *refs):
    own_ref, *outs = refs[-4:]
    rows = own_ref.shape[0]
    cols = keep_a.shape[1]
    for k, (kept, got) in enumerate(((keep_a, got_a), (keep_b, got_b))):
        total = kept[...].astype(f32) + got[...].astype(f32)
        at = slice(k * cols, (k + 1) * cols)
        own_ref[:, at] = total[:rows]
        for j, out in enumerate(outs):
            out[:, at] = total[(j + 1) * rows : (j + 2) * rows].astype(bf16)


def fold_last(parts, after=()):
    rows, cols = parts[0].shape
    shape = (rows // 4, 2 * cols)
    if rows % 32:
        pairs = (parts[:2], parts[2:])
        both = [kept.astype(f32) + got.astype(f32) for kept, got in pairs]
        own, *others = jnp.split(jnp.concatenate(both, axis=1), 4)
        return [own] + [other.astype(bf16) for other in others]
    return pl.pallas_call(
        fold_last_kernel,
        out_shape=[jax.ShapeDtypeStruct(shape, f32)] + [jax.ShapeDtypeStruct(shape, bf16)] * 3,
        in_specs=[pl.BlockSpec(memory_space=pltpu.VMEM)] * 4 + anywhere(after),
        compiler_params=params(),
        cost_estimate=cost(2 * rows * cols, 12 * rows * cols),
        name="fold_last",
    )(*parts, *after)


def anywhere(after):
    return [pl.BlockSpec(memory_space=pl.ANY)] * len(after)


def pair_cols(part, pair):
    start = part * D + pair * 2 * HEAD
    return slice(start, start + 2 * HEAD)


def norm_rows(src, dst, gain, bias, step_rows):
    @pl.loop(0, src.shape[0] // step_rows)
    def _(step):
        at = pl.ds(pl.multiple_of(step * step_rows, step_rows), step_rows)
        unit, _ = norm_parts(src[at, :].astype(f32))
        dst[at, :] = (unit * gain + bias).astype(bf16)


def attend_along(qkv_ref, att_ref, q_rows, k_rows, mask):
    low, high = lane_halves(f32)
    for pair in range(HEADS // 2):
        queries = two_heads(qkv_ref[q_rows, pair_cols(0, pair)] * bf16(HEAD ** (-0.5)))
        scores = mul_bt(queries, qkv_ref[k_rows, pair_cols(1, pair)])
        scores = jnp.where(mask, scores, -1e30)
        raised = jnp.exp(scores - jnp.max(scores, axis=-1, keepdims=True))
        probs = (raised * (1.0 / jnp.sum(raised, axis=-1, keepdims=True))).astype(bf16)
        half = probs.shape[0] // 2
        mixed = mul(probs, qkv_ref[k_rows, pair_cols(2, pair)])
        att_ref[q_rows, pair_cols(0, pair)] = (mixed[:half] * low + mixed[half:] * high).astype(bf16)


def attend(qkv_ref, att_ref, q_rows, k_rows, mask, keep_sums):
    for pair in range(HEADS // 2):
        queries = qkv_ref[q_rows, pair_cols(0, pair)] * bf16(HEAD ** (-0.5))
        scores = mul_bt(two_heads(qkv_ref[k_rows, pair_cols(1, pair)]), queries)
        probs, sums = softmax_down(scores, mask)
        vals = two_heads(qkv_ref[k_rows, pair_cols(2, pair)])
        mixed = mul_at(jnp.concatenate(probs, axis=0).astype(bf16), vals)
        att_ref[q_rows, pair_cols(0, pair)] = mixed.astype(bf16)
        for k in range(2):
            keep_sums(2 * pair + k, sums[k])


def text_front_kernel(
    x_ref, g1_ref, b1_ref, wqkv_ref, wo_ref, g2_ref, b2_ref, h1_ref, qkv_ref, att_ref, mid_ref,
    h2_ref, sum_ref, lse_ref
):
    rows, chunk = x_ref.shape[0], 128
    norm_rows(x_ref, h1_ref, g1_ref[...], b1_ref[...], chunk)

    @pl.loop(0, 3 * D // 256)
    def _(step):
        at = pl.ds(pl.multiple_of(step * 256, 256), 256)
        qkv_ref[:, at] = mul(h1_ref[...], wqkv_ref[:, at]).astype(bf16)

    mask = same_sequence(chunk, 0, chunk, 0, TXT_LEN)

    @pl.loop(0, rows // chunk)
    def _(step):
        at = pl.ds(pl.multiple_of(step * chunk, chunk), chunk)

        def keep_sums(head, value):
            lse_ref[pl.ds(step * 16 + head, 1), :] = value

        attend(qkv_ref, att_ref, at, at, mask, keep_sums)

    @pl.loop(0, D // 256)
    def _(step):
        at = pl.ds(pl.multiple_of(step * 256, 256), 256)
        mid_ref[:, at] = x_ref[:, at].astype(f32) + mul(att_ref[...], wo_ref[:, at])

    norm_rows(mid_ref, h2_ref, g2_ref[...], b2_ref[...], chunk)
    per = chunk // TXT_LEN

    @pl.loop(0, rows // chunk)
    def _(step):
        values = mid_ref[pl.ds(pl.multiple_of(step * chunk, chunk), chunk), :]
        sum_ref[pl.ds(pl.multiple_of(step * per, per), per), :] = jnp.sum(
            values.reshape(per, TXT_LEN, D), axis=1
        )


def text_front(rows_in, gain1, bias1, wqkv, wo, gain2, bias2):
    rows = rows_in.shape[0]
    shapes = [
        ((rows, D), bf16),
        ((rows, 3 * D), bf16),
        ((rows, D), bf16),
        ((rows, D), f32),
        ((rows, D), bf16),
        ((rows // TXT_LEN, D), f32),
        ((rows // 128 * 16, 128), f32),
    ]
    return pl.pallas_call(
        text_front_kernel,
        out_shape=[jax.ShapeDtypeStruct(*item) for item in shapes],
        compiler_params=params(),
        cost_estimate=cost(rows * D * D * 8, 14 * D * rows + 8 * D * D, rows * 128 * HEADS),
        name="text_front",
    )(rows_in, gain1[None], bias1[None], wqkv, wo, gain2[None], bias2[None])


def image_front_kernel(
    windows, x_ref, perm_ref, g1_ref, b1_ref, g2_ref, b2_ref, *refs
):
    h2_ref, sum_ref, w_ref, h1_ref, placed_ref, qkv_ref, att_ref, mid_ref, sems = refs[-9:]
    rows, chunk = x_ref.shape[0], 80
    copies, row = [], 0
    for k, piece in enumerate(refs[:-9]):
        place = w_ref.at[pl.ds(row, piece.shape[0]), :]
        copies.append(pltpu.make_async_copy(piece, place, sems.at[k]))
        row += piece.shape[0]
    for copy in copies:
        copy.start()

    def place_columns(src):
        @pl.loop(0, D // 256)
        def _(step):
            at = pl.ds(pl.multiple_of(step * 256, 256), 256)
            placed_ref[:, at] = mul_bt(src[...], perm_ref[at, :]).astype(bf16)

    norm_rows(x_ref, h1_ref, g1_ref[...].astype(f32), b1_ref[...].astype(f32), chunk)
    place_columns(h1_ref)
    for copy in copies:
        copy.wait()

    @pl.loop(0, 3 * D // 256)
    def _(step):
        at = pl.ds(pl.multiple_of(step * 256, 256), 256)
        qkv_ref[:, at] = mul(placed_ref[...], w_ref[:, at]).astype(bf16)

    for row0, count, key0, keys in windows:
        one = same_sequence(count, row0, keys, key0, IMG_LEN)
        mask = jnp.concatenate([one, one], axis=0)
        attend_along(qkv_ref, att_ref, pl.ds(row0, count), pl.ds(key0, keys), mask)
    place_columns(att_ref)

    @pl.loop(0, D // 256)
    def _(step):
        at = pl.ds(pl.multiple_of(step * 256, 256), 256)
        there = pl.ds(pl.multiple_of(step * 256 + 3 * D, 256), 256)
        mid_ref[:, at] = x_ref[:, at].astype(f32) + mul(placed_ref[...], w_ref[:, there])

    norm_rows(mid_ref, h2_ref, g2_ref[...].astype(f32), b2_ref[...].astype(f32), chunk)
    for k in range(rows // IMG_LEN):
        first, last = k * IMG_LEN, (k + 1) * IMG_LEN
        start, end = first // 8 * 8, -(-last // 8) * 8
        values = mid_ref[start:end, :]
        place = lax.broadcasted_iota(jnp.int32, values.shape, 0) + start
        inside = (place >= first) & (place < last)
        sum_ref[k : k + 1, :] = jnp.sum(jnp.where(inside, values, 0.0), axis=0, keepdims=True)


def image_front(rows_in, pieces, perm, gain1, bias1, gain2, bias2):
    rows = rows_in.shape[0]
    windows = ((0, 208, 0, 256), (208, 192, 192, 208))
    vmem = pl.BlockSpec(memory_space=pltpu.VMEM)
    return pl.pallas_call(
        functools.partial(image_front_kernel, windows),
        out_shape=[
            jax.ShapeDtypeStruct((rows, D), bf16),
            jax.ShapeDtypeStruct((rows // IMG_LEN, D), f32),
        ],
        in_specs=[vmem] * 6 + anywhere(pieces),
        out_specs=[vmem] * 2,
        scratch_shapes=[
            pltpu.VMEM((D, 4 * D), bf16),
            pltpu.VMEM((rows, D), bf16),
            pltpu.VMEM((rows, D), bf16),
            pltpu.VMEM((rows, 3 * D), bf16),
            pltpu.VMEM((rows, D), bf16),
            pltpu.VMEM((rows, D), f32),
            pltpu.SemaphoreType.DMA((len(pieces),)),
        ],
        compiler_params=params(),
        cost_estimate=cost(rows * D * D * 12, 8 * D * D, rows * 256 * HEADS),
        name="image_front",
    )(rows_in, perm, gain1[None], bias1[None], gain2[None], bias2[None], *pieces)


def gelu_parts(inner):
    half = 0.5 * (1.0 + lax.erf(inner * (0.5**0.5)))
    return inner * half, half


def pack_kernel(unit_ref, pos_ref, *refs):
    refs[-1][:, :D] = unit_ref[...].astype(bf16)
    refs[-1][:, D:] = pos_ref[...]


def packed(unit, positive, after):
    shape = (unit.shape[0], D + positive.shape[1])
    return pl.pallas_call(
        pack_kernel,
        out_shape=jax.ShapeDtypeStruct(shape, bf16),
        in_specs=[pl.BlockSpec(memory_space=pltpu.VMEM)] * 2 + anywhere(after),
        compiler_params=params(),
        cost_estimate=cost(shape[0] * shape[1], 4 * shape[0] * shape[1]),
        name="packed",
    )(unit, positive, *after)


def pool_matrix(count, rows, row0, seq_len):
    row = (lax.broadcasted_iota(jnp.int32, (count, rows), 1) + row0) // seq_len
    return jnp.where(row == lax.broadcasted_iota(jnp.int32, (count, rows), 0), 1.0, 0.0).astype(bf16)


def two_terms(mean):
    high = mean.astype(bf16)
    low = (mean - high.astype(f32)).astype(bf16)
    return jnp.concatenate([high, low], axis=0)


def unit_rows(pooled):
    inverse = lax.rsqrt(jnp.sum(pooled * pooled, axis=-1, keepdims=True) + norm_eps)
    return pooled * inverse, inverse


def text_up_kernel(h2_ref, wu_ref, wd_ref, sum_ref, *refs):
    slope_ref, hid_ref, unit_ref, inv_ref, acc = refs[-5:]
    step = pl.program_id(0)
    chunk = 128
    per = chunk // TXT_LEN
    pool = pool_matrix(per, chunk, 0, TXT_LEN)
    for k in range(h2_ref.shape[0] // chunk):
        inner = mul(h2_ref[k * chunk : (k + 1) * chunk, :], wu_ref[...])
        value, half = gelu_parts(inner)
        slope = half + inner * (jnp.exp(-0.5 * inner * inner) * 0.3989422804014327)
        slope_ref[k * chunk : (k + 1) * chunk, :] = slope.astype(bf16)
        hid_ref[k * per : (k + 1) * per, :] = mul(pool, value.astype(bf16))
    terms = mul(two_terms(hid_ref[...] * (1.0 / TXT_LEN)), wd_ref[...])
    count = hid_ref.shape[0]
    added = terms[:count] + terms[count:]

    @pl.when(step == 0)
    def _():
        acc[...] = sum_ref[...] * (1.0 / TXT_LEN) + added

    @pl.when(step > 0)
    def _():
        acc[...] += added

    @pl.when(step == pl.num_programs(0) - 1)
    def _():
        unit, inverse = unit_rows(acc[...])
        unit_ref[...] = unit
        inv_ref[...] = jnp.broadcast_to(inverse, inv_ref.shape)


def text_up(normed2, weight_up, weight_down, middle_sum, after=()):
    rows, count = normed2.shape[0], middle_sum.shape[0]
    fixed = lambda shape: pl.BlockSpec(shape, lambda i: (0, 0))
    return pl.pallas_call(
        text_up_kernel,
        grid=(FF // TILE,),
        out_shape=[
            jax.ShapeDtypeStruct((rows, FF), bf16),
            jax.ShapeDtypeStruct((count, FF), f32),
            jax.ShapeDtypeStruct((count, D), f32),
            jax.ShapeDtypeStruct((count, 128), f32),
        ],
        in_specs=[
            fixed((rows, D)),
            pl.BlockSpec((D, TILE), lambda i: (0, i)),
            pl.BlockSpec((TILE, D), lambda i: (i, 0)),
            fixed((count, D)),
        ]
        + anywhere(after),
        out_specs=[
            pl.BlockSpec((rows, TILE), lambda i: (0, i)),
            pl.BlockSpec((count, TILE), lambda i: (0, i)),
            fixed((count, D)),
            fixed((count, 128)),
        ],
        scratch_shapes=[pltpu.VMEM((count, D), f32)],
        compiler_params=params(),
        cost_estimate=cost(2 * rows * D * FF, 4 * D * FF + 2 * rows * FF, 20 * rows * FF),
        name="text_up",
    )(normed2, weight_up, weight_down, middle_sum, *after)


def image_up_kernel(fold, h2_ref, wu_ref, wd_ref, sum_ref, *refs):
    out_ref, acc = refs[-2:]
    step = pl.program_id(0)
    rows, count = h2_ref.shape[0], sum_ref.shape[0]
    chunk = 80
    summed = jnp.zeros((count, TILE), f32)
    for k in range(rows // chunk):
        inner = mul(h2_ref[k * chunk : (k + 1) * chunk, :], wu_ref[...])
        value, _ = gelu_parts(inner)
        pool = pool_matrix(count, chunk, k * chunk, IMG_LEN)
        summed = summed + mul(pool, value.astype(bf16))
    mean = two_terms(summed * (1.0 / IMG_LEN))
    place = lax.broadcasted_iota(jnp.int32, (TILE, TILE // fold), 0)
    picked = lax.broadcasted_iota(jnp.int32, (TILE, TILE // fold), 1) * fold
    terms = jnp.zeros((2 * count, D), f32)
    for k in range(fold):
        chosen = jnp.where(place == picked + k, 1.0, 0.0).astype(bf16)
        part = mul(mean, chosen).astype(bf16)
        terms = terms + mul(part, wd_ref[:, k * D : (k + 1) * D])
    added = terms[:count] + terms[count:]

    @pl.when(step == 0)
    def _():
        acc[...] = sum_ref[...] * (1.0 / IMG_LEN) + added

    @pl.when(step > 0)
    def _():
        acc[...] += added

    @pl.when(step == pl.num_programs(0) - 1)
    def _():
        out_ref[...] = unit_rows(acc[...])[0].astype(bf16)


def image_up(normed2, whole, up_col, down_col, middle_sum, after=()):
    rows, count = normed2.shape[0], middle_sum.shape[0]
    fold = FF // D
    fixed = lambda shape: pl.BlockSpec(shape, lambda i: (0, 0))
    return pl.pallas_call(
        functools.partial(image_up_kernel, fold),
        grid=(FF // TILE,),
        out_shape=jax.ShapeDtypeStruct((count, D), bf16),
        in_specs=[
            fixed((rows, D)),
            pl.BlockSpec((D, TILE), lambda i: (0, up_col // TILE + i)),
            pl.BlockSpec((TILE // fold, fold * D), lambda i: (i, down_col // (fold * D))),
            fixed((count, D)),
        ]
        + anywhere(after),
        out_specs=fixed((count, D)),
        scratch_shapes=[pltpu.VMEM((count, D), f32)],
        compiler_params=params(),
        cost_estimate=cost(2 * rows * D * FF, 4 * D * FF, 15 * rows * FF),
        name="image_up",
    )(normed2, whole, whole, middle_sum, *after)


def loss_parts(text_rows, pos, image_all):
    similar = mul_bt(text_rows, image_all) * logit_scale
    shifted = jnp.exp(similar - logit_scale)
    alive = jnp.max(pos, axis=1, keepdims=True)
    row_sum = jnp.sum(shifted, axis=1, keepdims=True)
    row_count = jnp.maximum(jnp.sum(pos, axis=1, keepdims=True), 1.0)
    return similar, shifted, alive, row_sum, row_count


def sums_over_captions(text_rows, pos, image_all):
    similar, shifted, alive, row_sum, row_count = loss_parts(text_rows, pos, image_all)
    pos_similar = pos * similar
    cap_term = alive * (
        logit_scale + jnp.log(row_sum) - jnp.sum(pos_similar, axis=1, keepdims=True) / row_count
    )
    return (
        jnp.sum(alive * shifted, axis=0, keepdims=True),
        jnp.sum(pos, axis=0, keepdims=True),
        jnp.sum(pos_similar, axis=0, keepdims=True),
        jnp.sum(cap_term, axis=0, keepdims=True),
        jnp.sum(alive, axis=0, keepdims=True),
    )


def loss_from(sums):
    col_sum, col_count, col_pos, cap_total, live_total = sums
    img_term = logit_scale + jnp.log(col_sum) - col_pos / col_count
    return 0.5 * cap_total / live_total + 0.5 * jnp.mean(img_term, axis=1, keepdims=True)


def grad_of_unit(text_rows, pos, image_all, col_sum, col_count, live_total):
    _, shifted, alive, row_sum, row_count = loss_parts(text_rows, pos, image_all)
    cap_share, img_share = 0.5 / live_total, 0.5 / image_all.shape[0]
    grad_sims = alive * shifted * (cap_share / row_sum + img_share / col_sum) - pos * (
        cap_share / row_count + img_share / col_count
    )
    return mul(grad_sims.astype(bf16), image_all) * logit_scale


def turned(grad, unit):
    return grad - unit * jnp.sum(grad * unit, axis=-1, keepdims=True)


def loss_kernel(
    pack_ref, image_ref, own_ref, unit_ref, inv_ref, loss_ref, row_ref, low_ref, col_sum_ref,
    col_count_ref, live_ref
):
    image_all = image_ref[...]
    chunk = 256
    total = None
    for k in range(pack_ref.shape[0] // chunk):
        at = slice(k * chunk, (k + 1) * chunk)
        part = sums_over_captions(pack_ref[at, :D], pack_ref[at, D:].astype(f32), image_all)
        total = part if total is None else [a + b for a, b in zip(total, part)]
    loss_ref[...] = jnp.broadcast_to(loss_from(total), loss_ref.shape)
    col_sum, col_count, _, _, live_total = total
    col_sum_ref[...] = col_sum
    col_count_ref[...] = col_count
    live_ref[...] = jnp.broadcast_to(live_total, live_ref.shape)
    grad = grad_of_unit(
        own_ref[:, :D], own_ref[:, D:].astype(f32), image_all, col_sum, col_count, live_total
    )
    row = inv_ref[:, :1] * turned(grad, unit_ref[...]) * (1.0 / TXT_LEN)
    row_ref[...] = row
    low_ref[...] = row.astype(bf16)


def loss_and_rows(pack, image_all, own_pack, unit, inverse):
    images, count = image_all.shape[0], own_pack.shape[0]
    shapes = [(1, 128), (count, D), (count, D), (1, images), (1, images), (1, 128)]
    kinds = [f32, f32, bf16, f32, f32, f32]
    return pl.pallas_call(
        loss_kernel,
        out_shape=[jax.ShapeDtypeStruct(*item) for item in zip(shapes, kinds)],
        compiler_params=params(),
        cost_estimate=cost(2 * pack.shape[0] * images * D, 2 * pack.size, pack.shape[0] * images),
        name="loss_and_rows",
    )(pack, image_all, own_pack, unit, inverse)


def down_kernel(pack_ref, image_ref, col_sum_ref, col_count_ref, live_ref, hid_ref, *refs):
    step, out_ref = pl.program_id(0), refs[-1]
    text_rows = pack_ref[:, :D]
    grad = grad_of_unit(
        text_rows, pack_ref[:, D:].astype(f32), image_ref[...], col_sum_ref[...],
        col_count_ref[...], live_ref[:, :1]
    )
    rows = (turned(grad, text_rows.astype(f32)) * (1.0 / TXT_LEN)).astype(bf16)
    part = mul_at(hid_ref[...], rows)

    @pl.when(step == 0)
    def _():
        out_ref[...] = part

    @pl.when(step > 0)
    def _():
        out_ref[...] += part


def grad_of_down(pack, image_all, col_sum, col_count, live_total, hidden_cols, after):
    images, chunk = image_all.shape[0], 256
    fixed = lambda shape: pl.BlockSpec(shape, lambda i: (0, 0))
    per = hidden_cols.shape[1]
    return pl.pallas_call(
        down_kernel,
        grid=(pack.shape[0] // chunk,),
        out_shape=jax.ShapeDtypeStruct((per, D), f32),
        in_specs=[
            pl.BlockSpec((chunk, pack.shape[1]), lambda i: (i, 0)),
            fixed((images, D)), fixed((1, images)), fixed((1, images)), fixed((1, 128)),
            pl.BlockSpec((chunk, per), lambda i: (i, 0)),
        ]
        + anywhere(after),
        out_specs=fixed((per, D)),
        compiler_params=params(),
        cost_estimate=cost(4 * pack.shape[0] * images * D, 2 * pack.size, pack.shape[0] * images),
        name="grad_of_down",
    )(pack, image_all, col_sum, col_count, live_total, hidden_cols, *after)


def mlp_back_kernel(
    low_ref, wd_ref, slope_ref, wu_ref, lhs_ref, mid_ref, gain_ref, row_ref, keep_a, send_a, keep_b,
    send_b, out_ref, gain_out, bias_out, acc
):
    step = pl.program_id(0)
    count, rows = low_ref.shape[0], slope_ref.shape[0]
    half = D // 2
    hidden = mul_bt(low_ref[...], wd_ref[...])
    wide = jnp.broadcast_to(hidden[:, None, :], (count, TXT_LEN, TILE)).reshape(rows, TILE)
    inner = (wide * slope_ref[...].astype(f32)).astype(bf16)
    weight = mul(lhs_ref[0], inner).astype(bf16)

    @pl.when(step < pl.num_programs(0) // 2)
    def _():
        keep_a[...] = weight[:half]
        send_a[...] = weight[half:]

    @pl.when(step >= pl.num_programs(0) // 2)
    def _():
        keep_b[...] = weight[:half]
        send_b[...] = weight[half:]

    added = mul_bt(inner, wu_ref[...])

    @pl.when(step == 0)
    def _():
        acc[...] = added

    @pl.when(step > 0)
    def _():
        acc[...] += added

    @pl.when(step == pl.num_programs(0) - 1)
    def _():
        chunk = 128
        per = chunk // TXT_LEN
        gain = gain_ref[...]
        gain_out[...] = jnp.zeros_like(gain_out)
        bias_out[...] = jnp.zeros_like(bias_out)

        @pl.loop(0, rows // chunk)
        def _(k):
            at = pl.ds(pl.multiple_of(k * chunk, chunk), chunk)
            unit, scale = norm_parts(mid_ref[at, :])
            grad = acc[at, :]
            gain_out[...] += jnp.sum(grad * unit, axis=0, keepdims=True)
            bias_out[...] += jnp.sum(grad, axis=0, keepdims=True)
            row = row_ref[pl.ds(pl.multiple_of(k * per, per), per), :]
            row = jnp.broadcast_to(row[:, None, :], (per, TXT_LEN, D)).reshape(chunk, D)
            out_ref[at, :] = row + norm_back(unit, scale, gain, grad)


def mlp_back(grad_row, grad_low, weight_down, slope, weight_up, lhs, middle, gain):
    rows, count = slope.shape[0], grad_row.shape[0]
    steps = FF // TILE
    fixed = lambda shape: pl.BlockSpec(shape, lambda i: (0, 0))
    first = pl.BlockSpec((D // 2, TILE), lambda i: (0, jnp.minimum(i, steps // 2 - 1)))
    second = pl.BlockSpec((D // 2, TILE), lambda i: (0, jnp.maximum(i - steps // 2, 0)))
    part = jax.ShapeDtypeStruct((D // 2, FF // 2), bf16)
    line = jax.ShapeDtypeStruct((1, D), f32)
    return pl.pallas_call(
        mlp_back_kernel,
        grid=(steps,),
        out_shape=[part] * 4 + [jax.ShapeDtypeStruct((rows, D), f32), line, line],
        in_specs=[
            fixed((count, D)),
            pl.BlockSpec((TILE, D), lambda i: (i, 0)),
            pl.BlockSpec((rows, TILE), lambda i: (0, i)),
            pl.BlockSpec((D, TILE), lambda i: (0, i)),
            pl.BlockSpec((1, D, rows), lambda i: (i // (steps // 2), 0, 0)),
            fixed((rows, D)),
            fixed((1, D)),
            fixed((count, D)),
        ],
        out_specs=[first, first, second, second, fixed((rows, D)), fixed((1, D)), fixed((1, D))],
        scratch_shapes=[pltpu.VMEM((rows, D), f32)],
        compiler_params=params(),
        cost_estimate=cost(4 * rows * D * FF, 4 * D * FF + 2 * rows * FF + 2 * D * FF, rows * FF),
        name="mlp_back",
    )(grad_low, weight_down, slope, weight_up, lhs, middle, gain[None], grad_row)


def attention_back_kernel(grad_ref, wo_ref, qkv_ref, lse_ref, *refs):
    low_ref, out_ref = refs[-2:]
    chunk = grad_ref.shape[0]
    mask = same_sequence(chunk, 0, chunk, 0, TXT_LEN)
    low = grad_ref[...].astype(bf16)
    low_ref[...] = low
    grad_att = mul_bt(low, wo_ref[...]).astype(bf16)
    for pair in range(HEADS // 2):
        queries = qkv_ref[:, pair_cols(0, pair)] * bf16(HEAD ** (-0.5))
        keys = two_heads(qkv_ref[:, pair_cols(1, pair)])
        vals = two_heads(qkv_ref[:, pair_cols(2, pair)])
        grads = grad_att[:, pair_cols(0, pair)]
        scores, grad_probs = mul_bt(keys, queries), mul_bt(vals, grads)
        probs, grad_scores = [], []
        for k in range(2):
            at = slice(k * chunk, (k + 1) * chunk)
            head = 2 * pair + k
            shifted = scores[at] - lse_ref[head : head + 1, :]
            prob = jnp.where(mask, jnp.exp(jnp.where(mask, shifted, 0.0)), 0.0)
            along = jnp.sum(grad_probs[at] * prob, axis=0, keepdims=True)
            grad_scores.append((prob * (grad_probs[at] - along)).astype(bf16))
            probs.append(prob.astype(bf16))
        grad_q = mul_at(jnp.concatenate(grad_scores, axis=0), keys) * HEAD ** (-0.5)
        grad_k = mul(jnp.concatenate(grad_scores, axis=1), two_heads(queries))
        grad_v = mul(jnp.concatenate(probs, axis=1), two_heads(grads))
        out_ref[:, pair_cols(0, pair)] = grad_q.astype(bf16)
        out_ref[:, pair_cols(1, pair)] = grad_k.astype(bf16)
        out_ref[:, pair_cols(2, pair)] = grad_v.astype(bf16)


def attention_back(grad_middle, weight_out, project, log_sums, first, count, after=()):
    chunk = 128
    rows = count * chunk
    return pl.pallas_call(
        attention_back_kernel,
        grid=(count,),
        out_shape=[
            jax.ShapeDtypeStruct((rows, D), bf16),
            jax.ShapeDtypeStruct((rows, 3 * D), bf16),
        ],
        in_specs=[
            pl.BlockSpec((chunk, D), lambda i: (i + first, 0)),
            pl.BlockSpec((D, D), lambda i: (0, 0)),
            pl.BlockSpec((chunk, 3 * D), lambda i: (i + first, 0)),
            pl.BlockSpec((16, chunk), lambda i: (i + first, 0)),
        ]
        + anywhere(after),
        out_specs=[
            pl.BlockSpec((chunk, D), lambda i: (i, 0)),
            pl.BlockSpec((chunk, 3 * D), lambda i: (i, 0)),
        ],
        compiler_params=params(),
        cost_estimate=cost(10 * rows * D * D, 16 * rows * D + 2 * D * D, rows * 128 * HEADS),
        name="attention_back",
    )(grad_middle, weight_out, project, log_sums, *after)


def mul_rows(lhs, parts):
    total, row = 0.0, 0
    for part in parts:
        total = total + mul(lhs[:, row : row + part.shape[0]], part[...])
        row += part.shape[0]
    return total


def weight_back_kernel(counts, lhs_ref, *refs):
    step, half = pl.program_id(0), D // 2
    keep, send = refs[-2:]
    row = 0
    for k, count in enumerate(counts):
        parts = refs[row : row + count]
        row += count

        @pl.when(step == k if len(counts) > 1 else step >= 0)
        def _(parts=parts):
            weight = mul_rows(lhs_ref[0], parts).astype(bf16)
            keep[...] = weight[:half]
            send[...] = weight[half:]


def weight_back(lhs, first, groups, blocks, after=()):
    rows = lhs.shape[2]
    steps = 2
    many = len(groups) > 1
    given = [part for group in groups for part in group]
    return pl.pallas_call(
        functools.partial(weight_back_kernel, [len(group) for group in groups]),
        grid=(steps,),
        out_shape=[jax.ShapeDtypeStruct((D // 2, steps * D), bf16)] * 2,
        in_specs=[pl.BlockSpec((1, D, rows), lambda i: (first + (i if many else 0), 0, 0))]
        + [
            pl.BlockSpec((part.shape[0], D), lambda i, col=col: (0, col + (0 if many else i)))
            for group, col in zip(groups, blocks)
            for part in group
        ]
        + anywhere(after),
        out_specs=[pl.BlockSpec((D // 2, D), lambda i: (0, i))] * 2,
        compiler_params=params(),
        cost_estimate=cost(4 * rows * D * D, 4 * rows * D + 7 * D * D),
        name="weight_back",
    )(lhs, *given, *after)


def input_back_kernel(count, *refs):
    projs = refs[:count]
    w_ref, x_ref, gain_ref, mid_ref = refs[count : count + 4]
    out_ref, gain_out, bias_out, acc = refs[-4:]
    step = pl.program_id(0)
    rows, chunk = x_ref.shape[0], 128
    row = 0
    for part in projs:
        at = slice(row, row + part.shape[0])
        row += part.shape[0]
        added = mul_bt(part[...], w_ref[...])

        @pl.when(step == 0)
        def _(at=at, added=added):
            acc[at, :] = added

        @pl.when(step > 0)
        def _(at=at, added=added):
            acc[at, :] += added

    @pl.when(step == pl.num_programs(0) - 1)
    def _():
        gain = gain_ref[...]
        gain_out[...] = jnp.zeros_like(gain_out)
        bias_out[...] = jnp.zeros_like(bias_out)

        @pl.loop(0, rows // chunk)
        def _(k):
            at = pl.ds(pl.multiple_of(k * chunk, chunk), chunk)
            unit, scale = norm_parts(x_ref[at, :].astype(f32))
            grad = acc[at, :]
            gain_out[...] += jnp.sum(grad * unit, axis=0, keepdims=True)
            bias_out[...] += jnp.sum(grad, axis=0, keepdims=True)
            out_ref[at, :] = mid_ref[at, :] + norm_back(unit, scale, gain, grad)


def input_back(grad_projs, weight, rows_in, gain, grad_middle, after=()):
    rows = rows_in.shape[0]
    fixed = lambda shape: pl.BlockSpec(shape, lambda i: (0, 0))
    line = jax.ShapeDtypeStruct((1, D), f32)
    return pl.pallas_call(
        functools.partial(input_back_kernel, len(grad_projs)),
        grid=(3,),
        out_shape=[jax.ShapeDtypeStruct((rows, D), f32), line, line],
        in_specs=[pl.BlockSpec((part.shape[0], D), lambda i: (0, i)) for part in grad_projs]
        + [
            pl.BlockSpec((D, D), lambda i: (0, i)),
            fixed((rows, D)), fixed((1, D)), fixed((rows, D)),
        ]
        + anywhere(after),
        out_specs=[fixed((rows, D)), fixed((1, D)), fixed((1, D))],
        scratch_shapes=[pltpu.VMEM((rows, D), f32)],
        compiler_params=params(),
        cost_estimate=cost(6 * rows * D * D, 14 * rows * D + 6 * D * D),
        name="input_back",
    )(*grad_projs, weight, rows_in, gain[None], grad_middle, *after)


def local(
    images,
    captions,
    img_gain1,
    img_bias1,
    img_qkv,
    img_out,
    img_gain2,
    img_bias2,
    img_up,
    img_down,
    txt_gain1,
    txt_bias1,
    txt_qkv,
    txt_out,
    txt_gain2,
    txt_bias2,
    txt_up,
    txt_down,
    counts,
    matches,
):
    peers = lax.axis_size(AXIS)
    own = lax.axis_index(AXIS)
    per = D // peers
    img_local = counts.shape[0]
    cap_local = matches.shape[0]
    total_images = matches.shape[1]

    whole = lax.all_gather(
        jnp.concatenate([img_up.reshape(per, FF), img_down.reshape(per, FF)], axis=1),
        AXIS,
        axis=0,
        tiled=True,
    )
    small = peers == 32
    shard = jnp.concatenate([img_qkv.reshape(per, 3 * D), img_out.reshape(per, D)], axis=1)
    if small:
        line, perm = gathered_line(shard), row_order((1, 4, 2, 16, 8))
    else:
        line, perm = lax.all_gather(shard, AXIS, axis=0, tiled=True), jnp.eye(D, dtype=bf16)

    normed1, project, attended, middle, normed2, middle_sum, log_sums = text_front(
        captions, txt_gain1, txt_bias1, txt_qkv, txt_out, txt_gain2, txt_bias2
    )
    middle_sum, line = in_turn(middle_sum, line)
    beside, above = (swapped(line, 2), swapped(line, 4)) if small else (line, line)
    slope, hidden_sum, text_unit, inverse = text_up(
        normed2, txt_up, txt_down, middle_sum, (line,)
    )
    text_unit, (beside, above) = in_turn(text_unit, (beside, above))
    pieces = gathered_rows(line, beside, above) if small else [line]

    ends_at = jnp.cumsum(counts)
    slot_ids = lax.iota(jnp.int32, cap_local)
    owner = jnp.sum((ends_at[None, :] <= slot_ids[:, None]).astype(jnp.int32), axis=1)
    owner = owner + own * img_local
    live = slot_ids < ends_at[-1]
    columns = lax.iota(jnp.int32, total_images)
    positive = ((matches > 0) | (owner[:, None] == columns[None, :])) & live[:, None]

    own_pack = packed(text_unit, positive.astype(bf16), pieces[1:5] if small else ())

    normed_img, middle_img = image_front(
        images, pieces, perm, img_gain1, img_bias1, img_gain2, img_bias2
    )
    if small:
        held = own_pack[None]
        scaled_sum = (hidden_sum * inverse[:, :1]).astype(bf16)
        normed_img, scaled_sum, other = lax.optimization_barrier(
            (normed_img, scaled_sum, swapped(held, 16))
        )
        held = joined(held, other, 16)
        hidden_cols = lax.all_to_all(scaled_sum, AXIS, split_axis=1, concat_axis=0, tiled=True)
        whole, other = in_turn(whole, swapped(held, 8))
        held = joined(held, other, 8)
        other = swapped(held, 4)
    image_low = image_up(normed_img, whole, 0, FF, middle_img)
    if small:
        image_low, other, hidden_cols = lax.optimization_barrier((image_low, other, hidden_cols))
        held = joined(held, other, 4)
        held = joined(held, swapped(held, 2), 2)
        text_pack = joined(held, swapped(held, 1), 1).reshape(-1, D + total_images)
    image_all = spread(image_low).reshape(total_images, D)

    order_a, order_b, tail = stage_orders()
    matrix_a, matrix_b = row_order(order_a + tail[::-1]), row_order(order_b + tail[::-1])
    lhs_up = jnp.stack([placed(matrix_a, normed2), placed(matrix_b, normed2)])
    lhs_rest = jnp.stack(
        [placed(matrix_a, normed1), placed(matrix_b, normed1), placed(matrix_b, attended)]
    )

    if small:
        loss_value, grad_row, row_low, col_sum, col_count, live_total = loss_and_rows(
            text_pack, image_all, own_pack, text_unit, inverse
        )
        loss_value = loss_value[0, 0]
    else:
        text_low, pos = own_pack[:, :D], own_pack[:, D:].astype(f32)
        sums = lax.psum(sums_over_captions(text_low, pos, image_all), AXIS)
        loss_value = loss_from(sums)[0, 0]
        grad = grad_of_unit(text_low, pos, image_all, sums[0], sums[1], sums[4])
        grad_row = inverse[:, :1] * turned(grad, text_unit) * (1.0 / TXT_LEN)
        row_low = grad_row.astype(bf16)

    *up, grad_middle, gain_two, bias_two = mlp_back(
        grad_row, row_low, txt_down, slope, txt_up, lhs_up, middle, txt_gain2
    )
    stages = len(order_a)
    low_one, proj_one = attention_back(grad_middle, txt_out, project, log_sums, 0, 2)
    for stage in range(stages - 2):
        up = fold(hand_on(up, stage), (proj_one,))
    low_two, proj_two = attention_back(grad_middle, txt_out, project, log_sums, 2, 3, up)
    up = fold(hand_on(up, stages - 2), (proj_two,))
    projs, lows = (proj_one, proj_two), (low_one, low_two)
    rest_a = weight_back(lhs_rest, 0, [projs], [0], up)
    up = hand_on_last(fold_last(hand_on(up, stages - 1), rest_a[1:]))
    rest_b = weight_back(lhs_rest, 1, [projs, lows], [2, 0], up[:1])
    rest = [*rest_a, *rest_b]
    for stage in range(stages - 2):
        rest = fold(hand_on(rest, stage))
    caption_grad, gain_one, bias_one = input_back(
        projs, txt_qkv, captions, txt_gain1, grad_middle, rest[:1]
    )
    caption_grad, up = in_turn(caption_grad, up)
    rest = fold(hand_on(rest, stages - 2), (caption_grad,))
    norms = jnp.concatenate([gain_one, bias_one, gain_two, bias_two], axis=0)
    norms, rest = in_turn(norms, rest)
    if small:
        grad_down = grad_of_down(
            text_pack, image_all, col_sum, col_count, live_total, hidden_cols, rest
        )
        rest = fold_last(hand_on(rest, stages - 1), (grad_down,))
    else:
        grad_down = lax.psum_scatter(
            mul_at(hidden_sum.astype(bf16), row_low), AXIS, scatter_dimension=0, tiled=True
        )
        rest = fold_last(hand_on(rest, stages - 1))
    up_share = sum_last(*up)
    rest_share = sum_last(*hand_on_last(rest))
    norms = jnp.sum(spread(norms[None]), axis=0).reshape(4, D)
    return (
        loss_value,
        caption_grad,
        norms[0],
        norms[1],
        rest_share[:, : 3 * D].reshape(-1),
        rest_share[:, 3 * D :].reshape(-1),
        norms[2],
        norms[3],
        up_share.reshape(-1),
        grad_down.reshape(-1),
    )


def solution(mesh):
    split, flat, whole = P("blk", None), P("blk"), P()
    image_block = (whole, whole, flat, flat, whole, whole, flat, flat)
    return jax.shard_map(
        local,
        mesh=mesh,
        in_specs=(split, split) + image_block + (whole,) * 8 + (flat, split),
        out_specs=(whole, split, whole, whole, flat, flat, whole, whole, flat, flat),
        check_vma=False,
    )
```

```python
import functools

import jax
import jax.numpy as jnp
from jax import lax
from jax.experimental import pallas as pl
from jax.experimental.pallas import tpu as pltpu
from jax.sharding import PartitionSpec as P

D = 768
FF = 3072
HEAD = 64
HEADS = D // HEAD
IMG_LEN = 50
TXT_LEN = 16
AXIS = "blk"

norm_eps = 1e-06
logit_scale = 50.0
f32 = jnp.float32
bf16 = jnp.bfloat16


def swapped(value, mask):
    peers = lax.axis_size(AXIS)
    return lax.ppermute(value, AXIS, [(i, i ^ mask) for i in range(peers)])


def bit_masks():
    peers = lax.axis_size(AXIS)
    return [1 << k for k in range(peers.bit_length() - 1)]


def joined(held, other, mask):
    upper = (lax.axis_index(AXIS) & mask) > 0
    first = jnp.where(upper, other, held)
    second = jnp.where(upper, held, other)
    return jnp.stack([first, second], axis=1).reshape((-1,) + held.shape[1:])


def spread(block):
    peers = lax.axis_size(AXIS)
    copies = jnp.broadcast_to(block[None], (peers,) + block.shape)
    return lax.all_to_all(copies, AXIS, split_axis=0, concat_axis=0, tiled=True)


def stage_orders():
    masks = bit_masks()
    head, tail = masks[:-2], masks[-2:]
    order_a = list(head)
    order_b = list(head)
    for k in range(1, len(head) - 1, 2):
        order_b[k], order_b[k + 1] = order_b[k + 1], order_b[k]
    return order_a, order_b, tail


def row_order(bits):
    peers = lax.axis_size(AXIS)
    own = lax.axis_index(AXIS)
    per = D // peers
    places = lax.iota(jnp.int32, D)
    block = places // per
    target = jnp.zeros_like(block) + own
    for k, mask in enumerate(bits):
        target = target ^ (((block >> (len(bits) - 1 - k)) & 1) * mask)
    source = target * per + places % per
    return (source[:, None] == lax.iota(jnp.int32, D)[None, :]).astype(bf16)


def gathered_line(shard):
    return jnp.concatenate([shard] + [swapped(shard, mask) for mask in (8, 16, 24)], axis=0)


def diagonal(beside, above):
    half = beside.shape[0] // 2
    return swapped(beside[:half], 4), swapped(above[half:], 2)


def in_turn(first, then):
    return lax.optimization_barrier((first, then))


def placed(order, values):
    return mul_bt(order, values).astype(bf16)


def hand_on(parts, stage):
    order_a, order_b, _ = stage_orders()
    keep_a, send_a, keep_b, send_b = parts
    return keep_a, swapped(send_a, order_a[stage]), keep_b, swapped(send_b, order_b[stage])


def hand_on_last(blocks):
    low, high = stage_orders()[2]
    own, *others = blocks
    return own, [swapped(block, mask) for block, mask in zip(others, (low, high, low | high))]


def sum_last(own, others):
    total = own
    for other in others:
        total = total + other.astype(f32)
    return total


VMEM_BYTES = 56 << 20
TILE = 512


def norm_parts(values):
    average = jnp.mean(values, axis=-1, keepdims=True)
    centred = values - average
    variance = jnp.mean(centred * centred, axis=-1, keepdims=True)
    scale = lax.rsqrt(variance + norm_eps)
    return centred * scale, scale


def norm_back(unit, scale, gain, grad):
    inner = grad * gain
    shift = jnp.mean(inner, axis=-1, keepdims=True)
    along = jnp.mean(inner * unit, axis=-1, keepdims=True)
    return scale * (inner - shift - unit * along)


def mul(lhs, rhs):
    return jnp.dot(lhs, rhs, preferred_element_type=f32)


def mul_bt(lhs, rhs):
    return lax.dot_general(lhs, rhs, (((1,), (1,)), ((), ())), preferred_element_type=f32)


def mul_at(lhs, rhs):
    return lax.dot_general(lhs, rhs, (((0,), (0,)), ((), ())), preferred_element_type=f32)


def params(**more):
    return pltpu.CompilerParams(vmem_limit_bytes=VMEM_BYTES, **more)


def cost(flops, moved, transcendentals=0):
    return pl.CostEstimate(flops=flops, bytes_accessed=moved, transcendentals=transcendentals)


def lane_halves(dtype):
    lane = lax.broadcasted_iota(jnp.int32, (1, 2 * HEAD), 1)
    low = jnp.where(lane < HEAD, 1.0, 0.0)
    return low.astype(dtype), (1.0 - low).astype(dtype)


def two_heads(pair):
    low, high = lane_halves(bf16)
    return jnp.concatenate([pair * low, pair * high], axis=0)


def same_sequence(rows, row0, cols, col0, seq_len):
    row = (lax.broadcasted_iota(jnp.int32, (rows, cols), 0) + row0) // seq_len
    col = (lax.broadcasted_iota(jnp.int32, (rows, cols), 1) + col0) // seq_len
    return row == col


def softmax_down(scores, mask):
    keys = mask.shape[0]
    parts, sums = [], []
    for k in range(2):
        part = jnp.where(mask, scores[k * keys : (k + 1) * keys], -1e30)
        most = jnp.max(part, axis=0, keepdims=True)
        raised = jnp.exp(part - most)
        total = jnp.sum(raised, axis=0, keepdims=True)
        parts.append(raised * (1.0 / total))
        sums.append(most + jnp.log(total))
    return parts, sums


def fold_kernel(keep_a, got_a, keep_b, got_b, *refs):
    outs = refs[-4:]
    half = outs[0].shape[0]
    for k, (kept, got) in enumerate(((keep_a, got_a), (keep_b, got_b))):
        for j in range(2):
            at = slice(j * half, (j + 1) * half)
            outs[2 * k + j][...] = (kept[at, :].astype(f32) + got[at, :].astype(f32)).astype(bf16)


def fold(parts, after=()):
    rows, cols = parts[0].shape
    if rows % 32:
        whole = [
            (kept.astype(f32) + got.astype(f32)).astype(bf16)
            for kept, got in (parts[:2], parts[2:])
        ]
        return [part for one in whole for part in (one[: rows // 2], one[rows // 2 :])]
    tile = 512
    return pl.pallas_call(
        fold_kernel,
        grid=(cols // tile,),
        out_shape=[jax.ShapeDtypeStruct((rows // 2, cols), bf16)] * 4,
        in_specs=[pl.BlockSpec((rows, tile), lambda i: (0, i))] * 4 + anywhere(after),
        out_specs=[pl.BlockSpec((rows // 2, tile), lambda i: (0, i))] * 4,
        compiler_params=params(),
        cost_estimate=cost(2 * rows * cols, 12 * rows * cols),
        name="fold",
    )(*parts, *after)


def fold_last_kernel(keep_a, got_a, keep_b, got_b, *refs):
    own_ref, *outs = refs[-4:]
    rows = own_ref.shape[0]
    cols = keep_a.shape[1]
    for k, (kept, got) in enumerate(((keep_a, got_a), (keep_b, got_b))):
        total = kept[...].astype(f32) + got[...].astype(f32)
        at = slice(k * cols, (k + 1) * cols)
        own_ref[:, at] = total[:rows]
        for j, out in enumerate(outs):
            out[:, at] = total[(j + 1) * rows : (j + 2) * rows].astype(bf16)


def fold_last(parts, after=()):
    rows, cols = parts[0].shape
    shape = (rows // 4, 2 * cols)
    if rows % 32:
        pairs = (parts[:2], parts[2:])
        both = [kept.astype(f32) + got.astype(f32) for kept, got in pairs]
        own, *others = jnp.split(jnp.concatenate(both, axis=1), 4)
        return [own] + [other.astype(bf16) for other in others]
    return pl.pallas_call(
        fold_last_kernel,
        out_shape=[jax.ShapeDtypeStruct(shape, f32)] + [jax.ShapeDtypeStruct(shape, bf16)] * 3,
        in_specs=[pl.BlockSpec(memory_space=pltpu.VMEM)] * 4 + anywhere(after),
        compiler_params=params(),
        cost_estimate=cost(2 * rows * cols, 12 * rows * cols),
        name="fold_last",
    )(*parts, *after)


def anywhere(after):
    return [pl.BlockSpec(memory_space=pl.ANY)] * len(after)


def pair_cols(part, pair):
    start = part * D + pair * 2 * HEAD
    return slice(start, start + 2 * HEAD)


def norm_rows(src, dst, gain, bias, step_rows):
    @pl.loop(0, src.shape[0] // step_rows)
    def _(step):
        at = pl.ds(pl.multiple_of(step * step_rows, step_rows), step_rows)
        unit, _ = norm_parts(src[at, :].astype(f32))
        dst[at, :] = (unit * gain + bias).astype(bf16)


def attend_along(qkv_ref, att_ref, q_rows, k_rows, mask):
    low, high = lane_halves(f32)
    for pair in range(HEADS // 2):
        queries = two_heads(qkv_ref[q_rows, pair_cols(0, pair)] * bf16(HEAD ** (-0.5)))
        scores = mul_bt(queries, qkv_ref[k_rows, pair_cols(1, pair)])
        scores = jnp.where(mask, scores, -1e30)
        raised = jnp.exp(scores - jnp.max(scores, axis=-1, keepdims=True))
        probs = (raised * (1.0 / jnp.sum(raised, axis=-1, keepdims=True))).astype(bf16)
        half = probs.shape[0] // 2
        mixed = mul(probs, qkv_ref[k_rows, pair_cols(2, pair)])
        att_ref[q_rows, pair_cols(0, pair)] = (mixed[:half] * low + mixed[half:] * high).astype(bf16)


def attend(qkv_ref, att_ref, q_rows, k_rows, mask, keep_sums):
    for pair in range(HEADS // 2):
        queries = qkv_ref[q_rows, pair_cols(0, pair)] * bf16(HEAD ** (-0.5))
        scores = mul_bt(two_heads(qkv_ref[k_rows, pair_cols(1, pair)]), queries)
        probs, sums = softmax_down(scores, mask)
        vals = two_heads(qkv_ref[k_rows, pair_cols(2, pair)])
        mixed = mul_at(jnp.concatenate(probs, axis=0).astype(bf16), vals)
        att_ref[q_rows, pair_cols(0, pair)] = mixed.astype(bf16)
        for k in range(2):
            keep_sums(2 * pair + k, sums[k])


def text_front_kernel(
    x_ref, g1_ref, b1_ref, wqkv_ref, wo_ref, g2_ref, b2_ref, h1_ref, qkv_ref, att_ref, mid_ref,
    h2_ref, sum_ref, lse_ref
):
    rows, chunk = x_ref.shape[0], 128
    norm_rows(x_ref, h1_ref, g1_ref[...], b1_ref[...], chunk)

    @pl.loop(0, 3 * D // 256)
    def _(step):
        at = pl.ds(pl.multiple_of(step * 256, 256), 256)
        qkv_ref[:, at] = mul(h1_ref[...], wqkv_ref[:, at]).astype(bf16)

    mask = same_sequence(chunk, 0, chunk, 0, TXT_LEN)

    @pl.loop(0, rows // chunk)
    def _(step):
        at = pl.ds(pl.multiple_of(step * chunk, chunk), chunk)

        def keep_sums(head, value):
            lse_ref[pl.ds(step * 16 + head, 1), :] = value

        attend(qkv_ref, att_ref, at, at, mask, keep_sums)

    @pl.loop(0, D // 256)
    def _(step):
        at = pl.ds(pl.multiple_of(step * 256, 256), 256)
        mid_ref[:, at] = x_ref[:, at].astype(f32) + mul(att_ref[...], wo_ref[:, at])

    norm_rows(mid_ref, h2_ref, g2_ref[...], b2_ref[...], chunk)
    per = chunk // TXT_LEN

    @pl.loop(0, rows // chunk)
    def _(step):
        values = mid_ref[pl.ds(pl.multiple_of(step * chunk, chunk), chunk), :]
        sum_ref[pl.ds(pl.multiple_of(step * per, per), per), :] = jnp.sum(
            values.reshape(per, TXT_LEN, D), axis=1
        )


def text_front(rows_in, gain1, bias1, wqkv, wo, gain2, bias2):
    rows = rows_in.shape[0]
    shapes = [
        ((rows, D), bf16),
        ((rows, 3 * D), bf16),
        ((rows, D), bf16),
        ((rows, D), f32),
        ((rows, D), bf16),
        ((rows // TXT_LEN, D), f32),
        ((rows // 128 * 16, 128), f32),
    ]
    return pl.pallas_call(
        text_front_kernel,
        out_shape=[jax.ShapeDtypeStruct(*item) for item in shapes],
        compiler_params=params(),
        cost_estimate=cost(rows * D * D * 8, 14 * D * rows + 8 * D * D, rows * 128 * HEADS),
        name="text_front",
    )(rows_in, gain1[None], bias1[None], wqkv, wo, gain2[None], bias2[None])


def image_front_kernel(
    windows, x_ref, perm_ref, g1_ref, b1_ref, g2_ref, b2_ref, *refs
):
    h2_ref, sum_ref, w_ref, h1_ref, placed_ref, qkv_ref, att_ref, mid_ref, sems = refs[-9:]
    rows, chunk = x_ref.shape[0], 80
    copies, row = [], 0
    for k, piece in enumerate(refs[:-9]):
        place = w_ref.at[pl.ds(row, piece.shape[0]), :]
        copies.append(pltpu.make_async_copy(piece.at[:, : 4 * D], place, sems.at[k]))
        row += piece.shape[0]
    for copy in copies:
        copy.start()

    def place_columns(src, dst):
        @pl.loop(0, D // 256)
        def _(step):
            at = pl.ds(pl.multiple_of(step * 256, 256), 256)
            dst[:, at] = mul_bt(src[...], perm_ref[at, :]).astype(bf16)

    norm_rows(x_ref, h1_ref, g1_ref[...].astype(f32), b1_ref[...].astype(f32), chunk)
    place_columns(h1_ref, placed_ref)
    for copy in copies:
        copy.wait()

    @pl.loop(0, 3 * D // 256)
    def _(step):
        at = pl.ds(pl.multiple_of(step * 256, 256), 256)
        qkv_ref[:, at] = mul(placed_ref[...], w_ref[:, at]).astype(bf16)

    for row0, count, key0, keys in windows:
        one = same_sequence(count, row0, keys, key0, IMG_LEN)
        mask = jnp.concatenate([one, one], axis=0)
        attend_along(qkv_ref, att_ref, pl.ds(row0, count), pl.ds(key0, keys), mask)
    place_columns(att_ref, placed_ref)

    @pl.loop(0, D // 256)
    def _(step):
        at = pl.ds(pl.multiple_of(step * 256, 256), 256)
        there = pl.ds(pl.multiple_of(step * 256 + 3 * D, 256), 256)
        mid_ref[:, at] = x_ref[:, at].astype(f32) + mul(placed_ref[...], w_ref[:, there])

    norm_rows(mid_ref, h1_ref, g2_ref[...].astype(f32), b2_ref[...].astype(f32), chunk)
    place_columns(h1_ref, h2_ref)
    for k in range(rows // IMG_LEN):
        first, last = k * IMG_LEN, (k + 1) * IMG_LEN
        start, end = first // 8 * 8, -(-last // 8) * 8
        values = mid_ref[start:end, :]
        place = lax.broadcasted_iota(jnp.int32, values.shape, 0) + start
        inside = (place >= first) & (place < last)
        sum_ref[k : k + 1, :] = jnp.sum(jnp.where(inside, values, 0.0), axis=0, keepdims=True)


def image_front(rows_in, pieces, perm, gain1, bias1, gain2, bias2):
    rows = rows_in.shape[0]
    windows = ((0, 208, 0, 256), (208, 192, 192, 208))
    vmem = pl.BlockSpec(memory_space=pltpu.VMEM)
    return pl.pallas_call(
        functools.partial(image_front_kernel, windows),
        out_shape=[
            jax.ShapeDtypeStruct((rows, D), bf16),
            jax.ShapeDtypeStruct((rows // IMG_LEN, D), f32),
        ],
        in_specs=[vmem] * 6 + anywhere(pieces),
        out_specs=[vmem] * 2,
        scratch_shapes=[
            pltpu.VMEM((D, 4 * D), bf16),
            pltpu.VMEM((rows, D), bf16),
            pltpu.VMEM((rows, D), bf16),
            pltpu.VMEM((rows, 3 * D), bf16),
            pltpu.VMEM((rows, D), bf16),
            pltpu.VMEM((rows, D), f32),
            pltpu.SemaphoreType.DMA((len(pieces),)),
        ],
        compiler_params=params(),
        cost_estimate=cost(rows * D * D * 12, 8 * D * D, rows * 256 * HEADS),
        name="image_front",
    )(rows_in, perm, gain1[None], bias1[None], gain2[None], bias2[None], *pieces)


def gelu_parts(inner):
    half = 0.5 * (1.0 + lax.erf(inner * (0.5**0.5)))
    return inner * half, half


def pack_kernel(unit_ref, pos_ref, *refs):
    refs[-1][:, :D] = unit_ref[...].astype(bf16)
    refs[-1][:, D:] = pos_ref[...]


def packed(unit, positive, after):
    shape = (unit.shape[0], D + positive.shape[1])
    return pl.pallas_call(
        pack_kernel,
        out_shape=jax.ShapeDtypeStruct(shape, bf16),
        in_specs=[pl.BlockSpec(memory_space=pltpu.VMEM)] * 2 + anywhere(after),
        compiler_params=params(),
        cost_estimate=cost(shape[0] * shape[1], 4 * shape[0] * shape[1]),
        name="packed",
    )(unit, positive, *after)


def pool_matrix(count, rows, row0, seq_len):
    row = (lax.broadcasted_iota(jnp.int32, (count, rows), 1) + row0) // seq_len
    return jnp.where(row == lax.broadcasted_iota(jnp.int32, (count, rows), 0), 1.0, 0.0).astype(bf16)


def two_terms(mean):
    high = mean.astype(bf16)
    low = (mean - high.astype(f32)).astype(bf16)
    return jnp.concatenate([high, low], axis=0)


def unit_rows(pooled):
    inverse = lax.rsqrt(jnp.sum(pooled * pooled, axis=-1, keepdims=True) + norm_eps)
    return pooled * inverse, inverse


def text_up_kernel(h2_ref, wu_ref, wd_ref, sum_ref, *refs):
    slope_ref, hid_ref, unit_ref, inv_ref, acc = refs[-5:]
    step = pl.program_id(0)
    chunk = 128
    per = chunk // TXT_LEN
    pool = pool_matrix(per, chunk, 0, TXT_LEN)
    for k in range(h2_ref.shape[0] // chunk):
        inner = mul(h2_ref[k * chunk : (k + 1) * chunk, :], wu_ref[...])
        value, half = gelu_parts(inner)
        slope = half + inner * (jnp.exp(-0.5 * inner * inner) * 0.3989422804014327)
        slope_ref[k * chunk : (k + 1) * chunk, :] = slope.astype(bf16)
        hid_ref[k * per : (k + 1) * per, :] = mul(pool, value.astype(bf16))
    terms = mul(two_terms(hid_ref[...] * (1.0 / TXT_LEN)), wd_ref[...])
    count = hid_ref.shape[0]
    added = terms[:count] + terms[count:]

    @pl.when(step == 0)
    def _():
        acc[...] = sum_ref[...] * (1.0 / TXT_LEN) + added

    @pl.when(step > 0)
    def _():
        acc[...] += added

    @pl.when(step == pl.num_programs(0) - 1)
    def _():
        unit, inverse = unit_rows(acc[...])
        unit_ref[...] = unit
        inv_ref[...] = jnp.broadcast_to(inverse, inv_ref.shape)


def text_up(normed2, weight_up, weight_down, middle_sum, after=()):
    rows, count = normed2.shape[0], middle_sum.shape[0]
    fixed = lambda shape: pl.BlockSpec(shape, lambda i: (0, 0))
    return pl.pallas_call(
        text_up_kernel,
        grid=(FF // TILE,),
        out_shape=[
            jax.ShapeDtypeStruct((rows, FF), bf16),
            jax.ShapeDtypeStruct((count, FF), f32),
            jax.ShapeDtypeStruct((count, D), f32),
            jax.ShapeDtypeStruct((count, 128), f32),
        ],
        in_specs=[
            fixed((rows, D)),
            pl.BlockSpec((D, TILE), lambda i: (0, i)),
            pl.BlockSpec((TILE, D), lambda i: (i, 0)),
            fixed((count, D)),
        ]
        + anywhere(after),
        out_specs=[
            pl.BlockSpec((rows, TILE), lambda i: (0, i)),
            pl.BlockSpec((count, TILE), lambda i: (0, i)),
            fixed((count, D)),
            fixed((count, 128)),
        ],
        scratch_shapes=[pltpu.VMEM((count, D), f32)],
        compiler_params=params(),
        cost_estimate=cost(2 * rows * D * FF, 4 * D * FF + 2 * rows * FF, 20 * rows * FF),
        name="text_up",
    )(normed2, weight_up, weight_down, middle_sum, *after)


def image_up_kernel(fold, count, h2_ref, wd_ref, sum_ref, *refs):
    pieces = refs[:count]
    out_ref, acc, wu_ref, sems = refs[-4:]
    step = pl.program_id(0)
    rows, images = h2_ref.shape[0], sum_ref.shape[0]
    chunk = 80

    def copies(tile):
        row = 0
        for k, piece in enumerate(pieces):
            cols = pl.ds(pl.multiple_of(4 * D + tile * TILE, TILE), TILE)
            there = wu_ref.at[tile, pl.ds(row, piece.shape[0]), :]
            yield pltpu.make_async_copy(piece.at[:, cols], there, sems.at[tile, k])
            row += piece.shape[0]

    @pl.when(step == 0)
    def _():
        for tile in range(FF // TILE):
            for copy in copies(tile):
                copy.start()

    for copy in copies(step):
        copy.wait()
    weight = wu_ref[step]
    summed = jnp.zeros((images, TILE), f32)
    for k in range(rows // chunk):
        inner = mul(h2_ref[k * chunk : (k + 1) * chunk, :], weight)
        value, _ = gelu_parts(inner)
        pool = pool_matrix(images, chunk, k * chunk, IMG_LEN)
        summed = summed + mul(pool, value.astype(bf16))
    mean = two_terms(summed * (1.0 / IMG_LEN))
    place = lax.broadcasted_iota(jnp.int32, (TILE, TILE // fold), 0)
    picked = lax.broadcasted_iota(jnp.int32, (TILE, TILE // fold), 1) * fold
    terms = jnp.zeros((2 * images, D), f32)
    for k in range(fold):
        chosen = jnp.where(place == picked + k, 1.0, 0.0).astype(bf16)
        part = mul(mean, chosen).astype(bf16)
        terms = terms + mul(part, wd_ref[:, k * D : (k + 1) * D])
    added = terms[:images] + terms[images:]

    @pl.when(step == 0)
    def _():
        acc[...] = sum_ref[...] * (1.0 / IMG_LEN) + added

    @pl.when(step > 0)
    def _():
        acc[...] += added

    @pl.when(step == pl.num_programs(0) - 1)
    def _():
        out_ref[...] = unit_rows(acc[...])[0].astype(bf16)


def image_up(normed2, pieces, whole, middle_sum, after=()):
    rows, images = normed2.shape[0], middle_sum.shape[0]
    fold = FF // D
    fixed = lambda shape: pl.BlockSpec(shape, lambda i: (0, 0))
    return pl.pallas_call(
        functools.partial(image_up_kernel, fold, len(pieces)),
        grid=(FF // TILE,),
        out_shape=jax.ShapeDtypeStruct((images, D), bf16),
        in_specs=[
            fixed((rows, D)),
            pl.BlockSpec((TILE // fold, fold * D), lambda i: (i, 0)),
            fixed((images, D)),
        ]
        + anywhere(pieces)
        + anywhere(after),
        out_specs=fixed((images, D)),
        scratch_shapes=[
            pltpu.VMEM((images, D), f32),
            pltpu.VMEM((FF // TILE, D, TILE), bf16),
            pltpu.SemaphoreType.DMA((FF // TILE, len(pieces))),
        ],
        compiler_params=params(),
        cost_estimate=cost(2 * rows * D * FF, 4 * D * FF, 15 * rows * FF),
        name="image_up",
    )(normed2, whole, middle_sum, *pieces, *after)


def loss_parts(text_rows, pos, image_all):
    similar = mul_bt(text_rows, image_all) * logit_scale
    shifted = jnp.exp(similar - logit_scale)
    alive = jnp.max(pos, axis=1, keepdims=True)
    row_sum = jnp.sum(shifted, axis=1, keepdims=True)
    row_count = jnp.maximum(jnp.sum(pos, axis=1, keepdims=True), 1.0)
    return similar, shifted, alive, row_sum, row_count


def sums_over_captions(text_rows, pos, image_all):
    similar, shifted, alive, row_sum, row_count = loss_parts(text_rows, pos, image_all)
    pos_similar = pos * similar
    cap_term = alive * (
        logit_scale + jnp.log(row_sum) - jnp.sum(pos_similar, axis=1, keepdims=True) / row_count
    )
    return (
        jnp.sum(alive * shifted, axis=0, keepdims=True),
        jnp.sum(pos, axis=0, keepdims=True),
        jnp.sum(pos_similar, axis=0, keepdims=True),
        jnp.sum(cap_term, axis=0, keepdims=True),
        jnp.sum(alive, axis=0, keepdims=True),
    )


def loss_from(sums):
    col_sum, col_count, col_pos, cap_total, live_total = sums
    img_term = logit_scale + jnp.log(col_sum) - col_pos / col_count
    return 0.5 * cap_total / live_total + 0.5 * jnp.mean(img_term, axis=1, keepdims=True)


def grad_of_unit(text_rows, pos, image_all, col_sum, col_count, live_total):
    _, shifted, alive, row_sum, row_count = loss_parts(text_rows, pos, image_all)
    cap_share, img_share = 0.5 / live_total, 0.5 / image_all.shape[0]
    grad_sims = alive * shifted * (cap_share / row_sum + img_share / col_sum) - pos * (
        cap_share / row_count + img_share / col_count
    )
    return mul(grad_sims.astype(bf16), image_all) * logit_scale


def turned(grad, unit):
    return grad - unit * jnp.sum(grad * unit, axis=-1, keepdims=True)


def loss_kernel(
    pack_ref, image_ref, own_ref, unit_ref, inv_ref, loss_ref, row_ref, low_ref, col_sum_ref,
    col_count_ref, live_ref
):
    image_all = image_ref[...]
    chunk = 256
    total = None
    for k in range(pack_ref.shape[0] // chunk):
        at = slice(k * chunk, (k + 1) * chunk)
        part = sums_over_captions(pack_ref[at, :D], pack_ref[at, D:].astype(f32), image_all)
        total = part if total is None else [a + b for a, b in zip(total, part)]
    loss_ref[...] = jnp.broadcast_to(loss_from(total), loss_ref.shape)
    col_sum, col_count, _, _, live_total = total
    col_sum_ref[...] = col_sum
    col_count_ref[...] = col_count
    live_ref[...] = jnp.broadcast_to(live_total, live_ref.shape)
    grad = grad_of_unit(
        own_ref[:, :D], own_ref[:, D:].astype(f32), image_all, col_sum, col_count, live_total
    )
    row = inv_ref[:, :1] * turned(grad, unit_ref[...]) * (1.0 / TXT_LEN)
    row_ref[...] = row
    low_ref[...] = row.astype(bf16)


def loss_and_rows(pack, image_all, own_pack, unit, inverse):
    images, count = image_all.shape[0], own_pack.shape[0]
    shapes = [(1, 128), (count, D), (count, D), (1, images), (1, images), (1, 128)]
    kinds = [f32, f32, bf16, f32, f32, f32]
    return pl.pallas_call(
        loss_kernel,
        out_shape=[jax.ShapeDtypeStruct(*item) for item in zip(shapes, kinds)],
        compiler_params=params(),
        cost_estimate=cost(2 * pack.shape[0] * images * D, 2 * pack.size, pack.shape[0] * images),
        name="loss_and_rows",
    )(pack, image_all, own_pack, unit, inverse)


def down_kernel(pack_ref, image_ref, col_sum_ref, col_count_ref, live_ref, hid_ref, *refs):
    step, out_ref = pl.program_id(0), refs[-1]
    text_rows = pack_ref[:, :D]
    grad = grad_of_unit(
        text_rows, pack_ref[:, D:].astype(f32), image_ref[...], col_sum_ref[...],
        col_count_ref[...], live_ref[:, :1]
    )
    rows = (turned(grad, text_rows.astype(f32)) * (1.0 / TXT_LEN)).astype(bf16)
    part = mul_at(hid_ref[...], rows)

    @pl.when(step == 0)
    def _():
        out_ref[...] = part

    @pl.when(step > 0)
    def _():
        out_ref[...] += part


def grad_of_down(pack, image_all, col_sum, col_count, live_total, hidden_cols, after):
    images, chunk = image_all.shape[0], 256
    fixed = lambda shape: pl.BlockSpec(shape, lambda i: (0, 0))
    per = hidden_cols.shape[1]
    return pl.pallas_call(
        down_kernel,
        grid=(pack.shape[0] // chunk,),
        out_shape=jax.ShapeDtypeStruct((per, D), f32),
        in_specs=[
            pl.BlockSpec((chunk, pack.shape[1]), lambda i: (i, 0)),
            fixed((images, D)), fixed((1, images)), fixed((1, images)), fixed((1, 128)),
            pl.BlockSpec((chunk, per), lambda i: (i, 0)),
        ]
        + anywhere(after),
        out_specs=fixed((per, D)),
        compiler_params=params(),
        cost_estimate=cost(4 * pack.shape[0] * images * D, 2 * pack.size, pack.shape[0] * images),
        name="grad_of_down",
    )(pack, image_all, col_sum, col_count, live_total, hidden_cols, *after)


def mlp_back_kernel(
    low_ref, wd_ref, slope_ref, wu_ref, lhs_ref, mid_ref, gain_ref, row_ref, keep_a, send_a, keep_b,
    send_b, out_ref, gain_out, bias_out, acc
):
    step = pl.program_id(0)
    count, rows = low_ref.shape[0], slope_ref.shape[0]
    half = D // 2
    hidden = mul_bt(low_ref[...], wd_ref[...])
    wide = jnp.broadcast_to(hidden[:, None, :], (count, TXT_LEN, TILE)).reshape(rows, TILE)
    inner = (wide * slope_ref[...].astype(f32)).astype(bf16)
    weight = mul(lhs_ref[0], inner).astype(bf16)

    @pl.when(step < pl.num_programs(0) // 2)
    def _():
        keep_a[...] = weight[:half]
        send_a[...] = weight[half:]

    @pl.when(step >= pl.num_programs(0) // 2)
    def _():
        keep_b[...] = weight[:half]
        send_b[...] = weight[half:]

    added = mul_bt(inner, wu_ref[...])

    @pl.when(step == 0)
    def _():
        acc[...] = added

    @pl.when(step > 0)
    def _():
        acc[...] += added

    @pl.when(step == pl.num_programs(0) - 1)
    def _():
        chunk = 128
        per = chunk // TXT_LEN
        gain = gain_ref[...]
        gain_out[...] = jnp.zeros_like(gain_out)
        bias_out[...] = jnp.zeros_like(bias_out)

        @pl.loop(0, rows // chunk)
        def _(k):
            at = pl.ds(pl.multiple_of(k * chunk, chunk), chunk)
            unit, scale = norm_parts(mid_ref[at, :])
            grad = acc[at, :]
            gain_out[...] += jnp.sum(grad * unit, axis=0, keepdims=True)
            bias_out[...] += jnp.sum(grad, axis=0, keepdims=True)
            row = row_ref[pl.ds(pl.multiple_of(k * per, per), per), :]
            row = jnp.broadcast_to(row[:, None, :], (per, TXT_LEN, D)).reshape(chunk, D)
            out_ref[at, :] = row + norm_back(unit, scale, gain, grad)


def mlp_back(grad_row, grad_low, weight_down, slope, weight_up, lhs, middle, gain):
    rows, count = slope.shape[0], grad_row.shape[0]
    steps = FF // TILE
    fixed = lambda shape: pl.BlockSpec(shape, lambda i: (0, 0))
    first = pl.BlockSpec((D // 2, TILE), lambda i: (0, jnp.minimum(i, steps // 2 - 1)))
    second = pl.BlockSpec((D // 2, TILE), lambda i: (0, jnp.maximum(i - steps // 2, 0)))
    part = jax.ShapeDtypeStruct((D // 2, FF // 2), bf16)
    line = jax.ShapeDtypeStruct((1, D), f32)
    return pl.pallas_call(
        mlp_back_kernel,
        grid=(steps,),
        out_shape=[part] * 4 + [jax.ShapeDtypeStruct((rows, D), f32), line, line],
        in_specs=[
            fixed((count, D)),
            pl.BlockSpec((TILE, D), lambda i: (i, 0)),
            pl.BlockSpec((rows, TILE), lambda i: (0, i)),
            pl.BlockSpec((D, TILE), lambda i: (0, i)),
            pl.BlockSpec((1, D, rows), lambda i: (i // (steps // 2), 0, 0)),
            fixed((rows, D)),
            fixed((1, D)),
            fixed((count, D)),
        ],
        out_specs=[first, first, second, second, fixed((rows, D)), fixed((1, D)), fixed((1, D))],
        scratch_shapes=[pltpu.VMEM((rows, D), f32)],
        compiler_params=params(),
        cost_estimate=cost(4 * rows * D * FF, 4 * D * FF + 2 * rows * FF + 2 * D * FF, rows * FF),
        name="mlp_back",
    )(grad_low, weight_down, slope, weight_up, lhs, middle, gain[None], grad_row)


def attention_back_kernel(grad_ref, wo_ref, qkv_ref, lse_ref, *refs):
    low_ref, out_ref = refs[-2:]
    chunk = grad_ref.shape[0]
    mask = same_sequence(chunk, 0, chunk, 0, TXT_LEN)
    low = grad_ref[...].astype(bf16)
    low_ref[...] = low
    grad_att = mul_bt(low, wo_ref[...]).astype(bf16)
    for pair in range(HEADS // 2):
        queries = qkv_ref[:, pair_cols(0, pair)] * bf16(HEAD ** (-0.5))
        keys = two_heads(qkv_ref[:, pair_cols(1, pair)])
        vals = two_heads(qkv_ref[:, pair_cols(2, pair)])
        grads = grad_att[:, pair_cols(0, pair)]
        scores, grad_probs = mul_bt(keys, queries), mul_bt(vals, grads)
        probs, grad_scores = [], []
        for k in range(2):
            at = slice(k * chunk, (k + 1) * chunk)
            head = 2 * pair + k
            shifted = scores[at] - lse_ref[head : head + 1, :]
            prob = jnp.where(mask, jnp.exp(jnp.where(mask, shifted, 0.0)), 0.0)
            along = jnp.sum(grad_probs[at] * prob, axis=0, keepdims=True)
            grad_scores.append((prob * (grad_probs[at] - along)).astype(bf16))
            probs.append(prob.astype(bf16))
        grad_q = mul_at(jnp.concatenate(grad_scores, axis=0), keys) * HEAD ** (-0.5)
        grad_k = mul(jnp.concatenate(grad_scores, axis=1), two_heads(queries))
        grad_v = mul(jnp.concatenate(probs, axis=1), two_heads(grads))
        out_ref[:, pair_cols(0, pair)] = grad_q.astype(bf16)
        out_ref[:, pair_cols(1, pair)] = grad_k.astype(bf16)
        out_ref[:, pair_cols(2, pair)] = grad_v.astype(bf16)


def attention_back(grad_middle, weight_out, project, log_sums, first, count, after=()):
    chunk = 128
    rows = count * chunk
    return pl.pallas_call(
        attention_back_kernel,
        grid=(count,),
        out_shape=[
            jax.ShapeDtypeStruct((rows, D), bf16),
            jax.ShapeDtypeStruct((rows, 3 * D), bf16),
        ],
        in_specs=[
            pl.BlockSpec((chunk, D), lambda i: (i + first, 0)),
            pl.BlockSpec((D, D), lambda i: (0, 0)),
            pl.BlockSpec((chunk, 3 * D), lambda i: (i + first, 0)),
            pl.BlockSpec((16, chunk), lambda i: (i + first, 0)),
        ]
        + anywhere(after),
        out_specs=[
            pl.BlockSpec((chunk, D), lambda i: (i, 0)),
            pl.BlockSpec((chunk, 3 * D), lambda i: (i, 0)),
        ],
        compiler_params=params(),
        cost_estimate=cost(10 * rows * D * D, 16 * rows * D + 2 * D * D, rows * 128 * HEADS),
        name="attention_back",
    )(grad_middle, weight_out, project, log_sums, *after)


def mul_rows(lhs, parts):
    total, row = 0.0, 0
    for part in parts:
        total = total + mul(lhs[:, row : row + part.shape[0]], part[...])
        row += part.shape[0]
    return total


def weight_back_kernel(counts, lhs_ref, *refs):
    step, half = pl.program_id(0), D // 2
    keep, send = refs[-2:]
    row = 0
    for k, count in enumerate(counts):
        parts = refs[row : row + count]
        row += count

        @pl.when(step == k if len(counts) > 1 else step >= 0)
        def _(parts=parts):
            weight = mul_rows(lhs_ref[0], parts).astype(bf16)
            keep[...] = weight[:half]
            send[...] = weight[half:]


def weight_back(lhs, first, groups, blocks, after=()):
    rows = lhs.shape[2]
    steps = 2
    many = len(groups) > 1
    given = [part for group in groups for part in group]
    return pl.pallas_call(
        functools.partial(weight_back_kernel, [len(group) for group in groups]),
        grid=(steps,),
        out_shape=[jax.ShapeDtypeStruct((D // 2, steps * D), bf16)] * 2,
        in_specs=[pl.BlockSpec((1, D, rows), lambda i: (first + (i if many else 0), 0, 0))]
        + [
            pl.BlockSpec((part.shape[0], D), lambda i, col=col: (0, col + (0 if many else i)))
            for group, col in zip(groups, blocks)
            for part in group
        ]
        + anywhere(after),
        out_specs=[pl.BlockSpec((D // 2, D), lambda i: (0, i))] * 2,
        compiler_params=params(),
        cost_estimate=cost(4 * rows * D * D, 4 * rows * D + 7 * D * D),
        name="weight_back",
    )(lhs, *given, *after)


def input_back_kernel(count, *refs):
    projs = refs[:count]
    w_ref, x_ref, gain_ref, mid_ref = refs[count : count + 4]
    out_ref, gain_out, bias_out, acc = refs[-4:]
    step = pl.program_id(0)
    rows, chunk = x_ref.shape[0], 128
    row = 0
    for part in projs:
        at = slice(row, row + part.shape[0])
        row += part.shape[0]
        added = mul_bt(part[...], w_ref[...])

        @pl.when(step == 0)
        def _(at=at, added=added):
            acc[at, :] = added

        @pl.when(step > 0)
        def _(at=at, added=added):
            acc[at, :] += added

    @pl.when(step == pl.num_programs(0) - 1)
    def _():
        gain = gain_ref[...]
        gain_out[...] = jnp.zeros_like(gain_out)
        bias_out[...] = jnp.zeros_like(bias_out)

        @pl.loop(0, rows // chunk)
        def _(k):
            at = pl.ds(pl.multiple_of(k * chunk, chunk), chunk)
            unit, scale = norm_parts(x_ref[at, :].astype(f32))
            grad = acc[at, :]
            gain_out[...] += jnp.sum(grad * unit, axis=0, keepdims=True)
            bias_out[...] += jnp.sum(grad, axis=0, keepdims=True)
            out_ref[at, :] = mid_ref[at, :] + norm_back(unit, scale, gain, grad)


def input_back(grad_projs, weight, rows_in, gain, grad_middle, after=()):
    rows = rows_in.shape[0]
    fixed = lambda shape: pl.BlockSpec(shape, lambda i: (0, 0))
    line = jax.ShapeDtypeStruct((1, D), f32)
    return pl.pallas_call(
        functools.partial(input_back_kernel, len(grad_projs)),
        grid=(3,),
        out_shape=[jax.ShapeDtypeStruct((rows, D), f32), line, line],
        in_specs=[pl.BlockSpec((part.shape[0], D), lambda i: (0, i)) for part in grad_projs]
        + [
            pl.BlockSpec((D, D), lambda i: (0, i)),
            fixed((rows, D)), fixed((1, D)), fixed((rows, D)),
        ]
        + anywhere(after),
        out_specs=[fixed((rows, D)), fixed((1, D)), fixed((1, D))],
        scratch_shapes=[pltpu.VMEM((rows, D), f32)],
        compiler_params=params(),
        cost_estimate=cost(6 * rows * D * D, 14 * rows * D + 6 * D * D),
        name="input_back",
    )(*grad_projs, weight, rows_in, gain[None], grad_middle, *after)


def local(
    images,
    captions,
    img_gain1,
    img_bias1,
    img_qkv,
    img_out,
    img_gain2,
    img_bias2,
    img_up,
    img_down,
    txt_gain1,
    txt_bias1,
    txt_qkv,
    txt_out,
    txt_gain2,
    txt_bias2,
    txt_up,
    txt_down,
    counts,
    matches,
):
    peers = lax.axis_size(AXIS)
    own = lax.axis_index(AXIS)
    per = D // peers
    img_local = counts.shape[0]
    cap_local = matches.shape[0]
    total_images = matches.shape[1]

    whole = lax.all_gather(img_down.reshape(per, FF), AXIS, axis=0, tiled=True)
    small = peers == 32
    shard = jnp.concatenate(
        [img_qkv.reshape(per, 3 * D), img_out.reshape(per, D), img_up.reshape(per, FF)], axis=1
    )
    if small:
        line, perm = gathered_line(shard), row_order((1, 4, 2, 16, 8))
    else:
        line, perm = lax.all_gather(shard, AXIS, axis=0, tiled=True), jnp.eye(D, dtype=bf16)

    normed1, project, attended, middle, normed2, middle_sum, log_sums = text_front(
        captions, txt_gain1, txt_bias1, txt_qkv, txt_out, txt_gain2, txt_bias2
    )
    middle_sum, line = in_turn(middle_sum, line)
    beside, above = (swapped(line, 2), swapped(line, 4)) if small else (line, line)
    slope, hidden_sum, text_unit, inverse = text_up(
        normed2, txt_up, txt_down, middle_sum, (line,)
    )
    text_unit, (beside, above) = in_turn(text_unit, (beside, above))

    ends_at = jnp.cumsum(counts)
    slot_ids = lax.iota(jnp.int32, cap_local)
    owner = jnp.sum((ends_at[None, :] <= slot_ids[:, None]).astype(jnp.int32), axis=1)
    owner = owner + own * img_local
    live = slot_ids < ends_at[-1]
    columns = lax.iota(jnp.int32, total_images)
    positive = ((matches > 0) | (owner[:, None] == columns[None, :])) & live[:, None]

    own_pack = packed(text_unit, positive.astype(bf16), ())
    pieces = [line]
    if small:
        held = own_pack[None]
        first, second = diagonal(beside, above)
        other, first, second = lax.optimization_barrier((swapped(held, 16), first, second))
        held = joined(held, other, 16)
        pieces = [line, beside, above, first, second]
        pieces = pieces + [swapped(piece, 1) for piece in pieces]

    normed_img, middle_img = image_front(
        images, pieces, perm, img_gain1, img_bias1, img_gain2, img_bias2
    )
    if small:
        scaled_sum = (hidden_sum * inverse[:, :1]).astype(bf16)
        normed_img, scaled_sum, other = lax.optimization_barrier(
            (normed_img, scaled_sum, swapped(held, 8))
        )
        held = joined(held, other, 8)
        hidden_cols = lax.all_to_all(scaled_sum, AXIS, split_axis=1, concat_axis=0, tiled=True)
        other = swapped(held, 4)
    image_low = image_up(normed_img, pieces, whole, middle_img)
    if small:
        image_low, other, hidden_cols = lax.optimization_barrier((image_low, other, hidden_cols))
        held = joined(held, other, 4)
        other = swapped(held, 2)
    image_all = spread(image_low).reshape(total_images, D)
    if small:
        image_all, other = in_turn(image_all, other)
        held = joined(held, other, 2)
        text_pack = joined(held, swapped(held, 1), 1).reshape(-1, D + total_images)

    order_a, order_b, tail = stage_orders()
    matrix_a, matrix_b = row_order(order_a + tail[::-1]), row_order(order_b + tail[::-1])
    lhs_up = jnp.stack([placed(matrix_a, normed2), placed(matrix_b, normed2)])
    lhs_rest = jnp.stack(
        [placed(matrix_a, normed1), placed(matrix_b, normed1), placed(matrix_b, attended)]
    )

    if small:
        loss_value, grad_row, row_low, col_sum, col_count, live_total = loss_and_rows(
            text_pack, image_all, own_pack, text_unit, inverse
        )
        loss_value = loss_value[0, 0]
    else:
        text_low, pos = own_pack[:, :D], own_pack[:, D:].astype(f32)
        sums = lax.psum(sums_over_captions(text_low, pos, image_all), AXIS)
        loss_value = loss_from(sums)[0, 0]
        grad = grad_of_unit(text_low, pos, image_all, sums[0], sums[1], sums[4])
        grad_row = inverse[:, :1] * turned(grad, text_unit) * (1.0 / TXT_LEN)
        row_low = grad_row.astype(bf16)

    *up, grad_middle, gain_two, bias_two = mlp_back(
        grad_row, row_low, txt_down, slope, txt_up, lhs_up, middle, txt_gain2
    )
    stages = len(order_a)
    low_one, proj_one = attention_back(grad_middle, txt_out, project, log_sums, 0, 2)
    for stage in range(stages - 2):
        up = fold(hand_on(up, stage), (proj_one,))
    low_two, proj_two = attention_back(grad_middle, txt_out, project, log_sums, 2, 3, up)
    up = fold(hand_on(up, stages - 2), (proj_two,))
    projs, lows = (proj_one, proj_two), (low_one, low_two)
    rest_a = weight_back(lhs_rest, 0, [projs], [0], up)
    up = hand_on_last(fold_last(hand_on(up, stages - 1), rest_a[1:]))
    rest_b = weight_back(lhs_rest, 1, [projs, lows], [2, 0], up[:1])
    rest = [*rest_a, *rest_b]
    for stage in range(stages - 2):
        rest = fold(hand_on(rest, stage))
    caption_grad, gain_one, bias_one = input_back(
        projs, txt_qkv, captions, txt_gain1, grad_middle, rest[:1]
    )
    caption_grad, up = in_turn(caption_grad, up)
    rest = fold(hand_on(rest, stages - 2), (caption_grad,))
    norms = jnp.concatenate([gain_one, bias_one, gain_two, bias_two], axis=0)
    norms, rest = in_turn(norms, rest)
    if small:
        grad_down = grad_of_down(
            text_pack, image_all, col_sum, col_count, live_total, hidden_cols, rest
        )
        rest = fold_last(hand_on(rest, stages - 1), (grad_down,))
    else:
        grad_down = lax.psum_scatter(
            mul_at(hidden_sum.astype(bf16), row_low), AXIS, scatter_dimension=0, tiled=True
        )
        rest = fold_last(hand_on(rest, stages - 1))
    up_share = sum_last(*up)
    rest_share = sum_last(*hand_on_last(rest))
    norms = jnp.sum(spread(norms[None]), axis=0).reshape(4, D)
    return (
        loss_value,
        caption_grad,
        norms[0],
        norms[1],
        rest_share[:, : 3 * D].reshape(-1),
        rest_share[:, 3 * D :].reshape(-1),
        norms[2],
        norms[3],
        up_share.reshape(-1),
        grad_down.reshape(-1),
    )


def solution(mesh):
    split, flat, whole = P("blk", None), P("blk"), P()
    image_block = (whole, whole, flat, flat, whole, whole, flat, flat)
    return jax.shard_map(
        local,
        mesh=mesh,
        in_specs=(split, split) + image_block + (whole,) * 8 + (flat, split),
        out_specs=(whole, split, whole, whole, flat, flat, whole, whole, flat, flat),
        check_vma=False,
    )
```

```python
import functools

import jax
import jax.numpy as jnp
from jax import lax
from jax.experimental import pallas as pl
from jax.experimental.pallas import tpu as pltpu
from jax.sharding import PartitionSpec as P

D = 768
FF = 3072
HEAD = 64
HEADS = D // HEAD
IMG_LEN = 50
TXT_LEN = 16
AXIS = "blk"

norm_eps = 1e-06
logit_scale = 50.0
f32 = jnp.float32
bf16 = jnp.bfloat16


def swapped(value, mask):
    peers = lax.axis_size(AXIS)
    return lax.ppermute(value, AXIS, [(i, i ^ mask) for i in range(peers)])


def bit_masks():
    peers = lax.axis_size(AXIS)
    return [1 << k for k in range(peers.bit_length() - 1)]


def joined(held, other, mask, outer=None):
    upper = (lax.axis_index(AXIS) & mask) > 0
    first = jnp.where(upper, other, held)
    second = jnp.where(upper, held, other)
    outer = held.shape[0] if outer is None else outer
    parts = [part.reshape((outer, -1) + held.shape[1:]) for part in (first, second)]
    return jnp.stack(parts, axis=1).reshape((-1,) + held.shape[1:])


def spread(block):
    peers = lax.axis_size(AXIS)
    copies = jnp.broadcast_to(block[None], (peers,) + block.shape)
    return lax.all_to_all(copies, AXIS, split_axis=0, concat_axis=0, tiled=True)


def stage_orders():
    masks = bit_masks()
    head, tail = masks[:-2], masks[-2:]
    order_a = list(head)
    order_b = list(head)
    for k in range(1, len(head) - 1, 2):
        order_b[k], order_b[k + 1] = order_b[k + 1], order_b[k]
    return order_a, order_b, tail


def row_order(bits):
    peers = lax.axis_size(AXIS)
    own = lax.axis_index(AXIS)
    per = D // peers
    places = lax.iota(jnp.int32, D)
    block = places // per
    target = jnp.zeros_like(block) + own
    for k, mask in enumerate(bits):
        target = target ^ (((block >> (len(bits) - 1 - k)) & 1) * mask)
    source = target * per + places % per
    return (source[:, None] == lax.iota(jnp.int32, D)[None, :]).astype(bf16)


def gathered_line(shard):
    return jnp.concatenate([shard] + [swapped(shard, mask) for mask in (8, 16, 24)], axis=0)


def diagonal(beside, above):
    half = beside.shape[0] // 2
    return swapped(beside[:half], 4), swapped(above[half:], 2)


def in_turn(first, then):
    return lax.optimization_barrier((first, then))


def placed(order, values):
    return mul_bt(order, values).astype(bf16)


def hand_on(parts, stage):
    order_a, order_b, _ = stage_orders()
    keep_a, send_a, keep_b, send_b = parts
    return keep_a, swapped(send_a, order_a[stage]), keep_b, swapped(send_b, order_b[stage])


def hand_on_last(blocks):
    low, high = stage_orders()[2]
    own, *others = blocks
    return own, [swapped(block, mask) for block, mask in zip(others, (low, high, low | high))]


def sum_last(own, others):
    total = own
    for other in others:
        total = total + other.astype(f32)
    return total


VMEM_BYTES = 56 << 20
TILE = 512


def norm_parts(values):
    average = jnp.mean(values, axis=-1, keepdims=True)
    centred = values - average
    variance = jnp.mean(centred * centred, axis=-1, keepdims=True)
    scale = lax.rsqrt(variance + norm_eps)
    return centred * scale, scale


def norm_back(unit, scale, gain, grad):
    inner = grad * gain
    shift = jnp.mean(inner, axis=-1, keepdims=True)
    along = jnp.mean(inner * unit, axis=-1, keepdims=True)
    return scale * (inner - shift - unit * along)


def mul(lhs, rhs):
    return jnp.dot(lhs, rhs, preferred_element_type=f32)


def mul_bt(lhs, rhs):
    return lax.dot_general(lhs, rhs, (((1,), (1,)), ((), ())), preferred_element_type=f32)


def mul_at(lhs, rhs):
    return lax.dot_general(lhs, rhs, (((0,), (0,)), ((), ())), preferred_element_type=f32)


def params(**more):
    return pltpu.CompilerParams(vmem_limit_bytes=VMEM_BYTES, **more)


def cost(flops, moved, transcendentals=0):
    return pl.CostEstimate(flops=flops, bytes_accessed=moved, transcendentals=transcendentals)


def lane_halves(dtype):
    lane = lax.broadcasted_iota(jnp.int32, (1, 2 * HEAD), 1)
    low = jnp.where(lane < HEAD, 1.0, 0.0)
    return low.astype(dtype), (1.0 - low).astype(dtype)


def two_heads(pair):
    low, high = lane_halves(bf16)
    return jnp.concatenate([pair * low, pair * high], axis=0)


def same_sequence(rows, row0, cols, col0, seq_len):
    row = (lax.broadcasted_iota(jnp.int32, (rows, cols), 0) + row0) // seq_len
    col = (lax.broadcasted_iota(jnp.int32, (rows, cols), 1) + col0) // seq_len
    return row == col


def softmax_down(scores, mask):
    keys = mask.shape[0]
    parts, sums = [], []
    for k in range(2):
        part = jnp.where(mask, scores[k * keys : (k + 1) * keys], -1e30)
        most = jnp.max(part, axis=0, keepdims=True)
        raised = jnp.exp(part - most)
        total = jnp.sum(raised, axis=0, keepdims=True)
        parts.append(raised * (1.0 / total))
        sums.append(most + jnp.log(total))
    return parts, sums


def fold_kernel(keep_a, got_a, keep_b, got_b, *refs):
    outs = refs[-4:]
    half = outs[0].shape[0]
    for k, (kept, got) in enumerate(((keep_a, got_a), (keep_b, got_b))):
        for j in range(2):
            at = slice(j * half, (j + 1) * half)
            outs[2 * k + j][...] = (kept[at, :].astype(f32) + got[at, :].astype(f32)).astype(bf16)


def fold(parts, after=()):
    rows, cols = parts[0].shape
    if rows % 32:
        whole = [
            (kept.astype(f32) + got.astype(f32)).astype(bf16)
            for kept, got in (parts[:2], parts[2:])
        ]
        return [part for one in whole for part in (one[: rows // 2], one[rows // 2 :])]
    tile = 512
    return pl.pallas_call(
        fold_kernel,
        grid=(cols // tile,),
        out_shape=[jax.ShapeDtypeStruct((rows // 2, cols), bf16)] * 4,
        in_specs=[pl.BlockSpec((rows, tile), lambda i: (0, i))] * 4 + anywhere(after),
        out_specs=[pl.BlockSpec((rows // 2, tile), lambda i: (0, i))] * 4,
        compiler_params=params(),
        cost_estimate=cost(2 * rows * cols, 12 * rows * cols),
        name="fold",
    )(*parts, *after)


def fold_last_kernel(keep_a, got_a, keep_b, got_b, *refs):
    own_ref, *outs = refs[-4:]
    rows = own_ref.shape[0]
    cols = keep_a.shape[1]
    for k, (kept, got) in enumerate(((keep_a, got_a), (keep_b, got_b))):
        total = kept[...].astype(f32) + got[...].astype(f32)
        at = slice(k * cols, (k + 1) * cols)
        own_ref[:, at] = total[:rows]
        for j, out in enumerate(outs):
            out[:, at] = total[(j + 1) * rows : (j + 2) * rows].astype(bf16)


def fold_last(parts, after=()):
    rows, cols = parts[0].shape
    shape = (rows // 4, 2 * cols)
    if rows % 32:
        pairs = (parts[:2], parts[2:])
        both = [kept.astype(f32) + got.astype(f32) for kept, got in pairs]
        own, *others = jnp.split(jnp.concatenate(both, axis=1), 4)
        return [own] + [other.astype(bf16) for other in others]
    return pl.pallas_call(
        fold_last_kernel,
        out_shape=[jax.ShapeDtypeStruct(shape, f32)] + [jax.ShapeDtypeStruct(shape, bf16)] * 3,
        in_specs=[pl.BlockSpec(memory_space=pltpu.VMEM)] * 4 + anywhere(after),
        compiler_params=params(),
        cost_estimate=cost(2 * rows * cols, 12 * rows * cols),
        name="fold_last",
    )(*parts, *after)


def anywhere(after):
    return [pl.BlockSpec(memory_space=pl.ANY)] * len(after)


def pair_cols(part, pair):
    start = part * D + pair * 2 * HEAD
    return slice(start, start + 2 * HEAD)


def norm_rows(src, dst, gain, bias, step_rows):
    @pl.loop(0, src.shape[0] // step_rows)
    def _(step):
        at = pl.ds(pl.multiple_of(step * step_rows, step_rows), step_rows)
        unit, _ = norm_parts(src[at, :].astype(f32))
        dst[at, :] = (unit * gain + bias).astype(bf16)


def attend_along(qkv_ref, att_ref, q_rows, k_rows, mask):
    low, high = lane_halves(f32)
    for pair in range(HEADS // 2):
        queries = two_heads(qkv_ref[q_rows, pair_cols(0, pair)] * bf16(HEAD ** (-0.5)))
        scores = mul_bt(queries, qkv_ref[k_rows, pair_cols(1, pair)])
        scores = jnp.where(mask, scores, -1e30)
        raised = jnp.exp(scores - jnp.max(scores, axis=-1, keepdims=True))
        probs = (raised * (1.0 / jnp.sum(raised, axis=-1, keepdims=True))).astype(bf16)
        half = probs.shape[0] // 2
        mixed = mul(probs, qkv_ref[k_rows, pair_cols(2, pair)])
        att_ref[q_rows, pair_cols(0, pair)] = (mixed[:half] * low + mixed[half:] * high).astype(bf16)


def attend(qkv_ref, att_ref, q_rows, k_rows, mask, keep_sums):
    for pair in range(HEADS // 2):
        queries = qkv_ref[q_rows, pair_cols(0, pair)] * bf16(HEAD ** (-0.5))
        scores = mul_bt(two_heads(qkv_ref[k_rows, pair_cols(1, pair)]), queries)
        probs, sums = softmax_down(scores, mask)
        vals = two_heads(qkv_ref[k_rows, pair_cols(2, pair)])
        mixed = mul_at(jnp.concatenate(probs, axis=0).astype(bf16), vals)
        att_ref[q_rows, pair_cols(0, pair)] = mixed.astype(bf16)
        for k in range(2):
            keep_sums(2 * pair + k, sums[k])


def text_front_kernel(
    x_ref, g1_ref, b1_ref, wqkv_ref, wo_ref, g2_ref, b2_ref, h1_ref, qkv_ref, att_ref, mid_ref,
    h2_ref, sum_ref, lse_ref
):
    rows, chunk = x_ref.shape[0], 128
    norm_rows(x_ref, h1_ref, g1_ref[...], b1_ref[...], chunk)

    @pl.loop(0, 3 * D // 256)
    def _(step):
        at = pl.ds(pl.multiple_of(step * 256, 256), 256)
        qkv_ref[:, at] = mul(h1_ref[...], wqkv_ref[:, at]).astype(bf16)

    mask = same_sequence(chunk, 0, chunk, 0, TXT_LEN)

    @pl.loop(0, rows // chunk)
    def _(step):
        at = pl.ds(pl.multiple_of(step * chunk, chunk), chunk)

        def keep_sums(head, value):
            lse_ref[pl.ds(step * 16 + head, 1), :] = value

        attend(qkv_ref, att_ref, at, at, mask, keep_sums)

    @pl.loop(0, D // 256)
    def _(step):
        at = pl.ds(pl.multiple_of(step * 256, 256), 256)
        mid_ref[:, at] = x_ref[:, at].astype(f32) + mul(att_ref[...], wo_ref[:, at])

    norm_rows(mid_ref, h2_ref, g2_ref[...], b2_ref[...], chunk)
    per = chunk // TXT_LEN

    @pl.loop(0, rows // chunk)
    def _(step):
        values = mid_ref[pl.ds(pl.multiple_of(step * chunk, chunk), chunk), :]
        sum_ref[pl.ds(pl.multiple_of(step * per, per), per), :] = jnp.sum(
            values.reshape(per, TXT_LEN, D), axis=1
        )


def text_front(rows_in, gain1, bias1, wqkv, wo, gain2, bias2):
    rows = rows_in.shape[0]
    shapes = [
        ((rows, D), bf16),
        ((rows, 3 * D), bf16),
        ((rows, D), bf16),
        ((rows, D), f32),
        ((rows, D), bf16),
        ((rows // TXT_LEN, D), f32),
        ((rows // 128 * 16, 128), f32),
    ]
    return pl.pallas_call(
        text_front_kernel,
        out_shape=[jax.ShapeDtypeStruct(*item) for item in shapes],
        compiler_params=params(),
        cost_estimate=cost(rows * D * D * 8, 14 * D * rows + 8 * D * D, rows * 128 * HEADS),
        name="text_front",
    )(rows_in, gain1[None], bias1[None], wqkv, wo, gain2[None], bias2[None])


def image_front_kernel(
    windows, x_ref, perm_ref, g1_ref, b1_ref, g2_ref, b2_ref, *refs
):
    h2_ref, sum_ref, w_ref, h1_ref, placed_ref, qkv_ref, att_ref, mid_ref, sems = refs[-9:]
    rows, chunk = x_ref.shape[0], 80
    copies, row = [], 0
    for k, piece in enumerate(refs[:-9]):
        place = w_ref.at[pl.ds(row, piece.shape[0]), :]
        copies.append(pltpu.make_async_copy(piece, place, sems.at[k]))
        row += piece.shape[0]
    for copy in copies:
        copy.start()

    def place_columns(src, dst):
        @pl.loop(0, D // 256)
        def _(step):
            at = pl.ds(pl.multiple_of(step * 256, 256), 256)
            dst[:, at] = mul_bt(src[...], perm_ref[at, :]).astype(bf16)

    norm_rows(x_ref, h1_ref, g1_ref[...].astype(f32), b1_ref[...].astype(f32), chunk)
    place_columns(h1_ref, placed_ref)
    for copy in copies:
        copy.wait()

    @pl.loop(0, 3 * D // 256)
    def _(step):
        at = pl.ds(pl.multiple_of(step * 256, 256), 256)
        qkv_ref[:, at] = mul(placed_ref[...], w_ref[:, at]).astype(bf16)

    for row0, count, key0, keys in windows:
        one = same_sequence(count, row0, keys, key0, IMG_LEN)
        mask = jnp.concatenate([one, one], axis=0)
        attend_along(qkv_ref, att_ref, pl.ds(row0, count), pl.ds(key0, keys), mask)
    place_columns(att_ref, placed_ref)

    @pl.loop(0, D // 256)
    def _(step):
        at = pl.ds(pl.multiple_of(step * 256, 256), 256)
        there = pl.ds(pl.multiple_of(step * 256 + 3 * D, 256), 256)
        mid_ref[:, at] = x_ref[:, at].astype(f32) + mul(placed_ref[...], w_ref[:, there])

    norm_rows(mid_ref, h2_ref, g2_ref[...].astype(f32), b2_ref[...].astype(f32), chunk)
    for k in range(rows // IMG_LEN):
        first, last = k * IMG_LEN, (k + 1) * IMG_LEN
        start, end = first // 8 * 8, -(-last // 8) * 8
        values = mid_ref[start:end, :]
        place = lax.broadcasted_iota(jnp.int32, values.shape, 0) + start
        inside = (place >= first) & (place < last)
        sum_ref[k : k + 1, :] = jnp.sum(jnp.where(inside, values, 0.0), axis=0, keepdims=True)


def image_front(rows_in, pieces, perm, gain1, bias1, gain2, bias2):
    rows = rows_in.shape[0]
    windows = ((0, 208, 0, 256), (208, 192, 192, 208))
    vmem = pl.BlockSpec(memory_space=pltpu.VMEM)
    return pl.pallas_call(
        functools.partial(image_front_kernel, windows),
        out_shape=[
            jax.ShapeDtypeStruct((rows, D), bf16),
            jax.ShapeDtypeStruct((rows // IMG_LEN, D), f32),
        ],
        in_specs=[vmem] * 6 + anywhere(pieces),
        out_specs=[vmem] * 2,
        scratch_shapes=[
            pltpu.VMEM((D, 4 * D), bf16),
            pltpu.VMEM((rows, D), bf16),
            pltpu.VMEM((rows, D), bf16),
            pltpu.VMEM((rows, 3 * D), bf16),
            pltpu.VMEM((rows, D), bf16),
            pltpu.VMEM((rows, D), f32),
            pltpu.SemaphoreType.DMA((len(pieces),)),
        ],
        compiler_params=params(),
        cost_estimate=cost(rows * D * D * 12, 8 * D * D, rows * 256 * HEADS),
        name="image_front",
    )(rows_in, perm, gain1[None], bias1[None], gain2[None], bias2[None], *pieces)


def gelu_parts(inner):
    half = 0.5 * (1.0 + lax.erf(inner * (0.5**0.5)))
    return inner * half, half


def pack_kernel(unit_ref, pos_ref, *refs):
    refs[-1][:, :D] = unit_ref[...].astype(bf16)
    refs[-1][:, D:] = pos_ref[...]


def packed(unit, positive, after):
    shape = (unit.shape[0], D + positive.shape[1])
    return pl.pallas_call(
        pack_kernel,
        out_shape=jax.ShapeDtypeStruct(shape, bf16),
        in_specs=[pl.BlockSpec(memory_space=pltpu.VMEM)] * 2 + anywhere(after),
        compiler_params=params(),
        cost_estimate=cost(shape[0] * shape[1], 4 * shape[0] * shape[1]),
        name="packed",
    )(unit, positive, *after)


def pool_matrix(count, rows, row0, seq_len):
    row = (lax.broadcasted_iota(jnp.int32, (count, rows), 1) + row0) // seq_len
    return jnp.where(row == lax.broadcasted_iota(jnp.int32, (count, rows), 0), 1.0, 0.0).astype(bf16)


def two_terms(mean):
    high = mean.astype(bf16)
    low = (mean - high.astype(f32)).astype(bf16)
    return jnp.concatenate([high, low], axis=0)


def unit_rows(pooled):
    inverse = lax.rsqrt(jnp.sum(pooled * pooled, axis=-1, keepdims=True) + norm_eps)
    return pooled * inverse, inverse


def text_up_kernel(h2_ref, wu_ref, wd_ref, sum_ref, *refs):
    slope_ref, hid_ref, unit_ref, inv_ref, acc = refs[-5:]
    step = pl.program_id(0)
    chunk = 128
    per = chunk // TXT_LEN
    pool = pool_matrix(per, chunk, 0, TXT_LEN)
    for k in range(h2_ref.shape[0] // chunk):
        inner = mul(h2_ref[k * chunk : (k + 1) * chunk, :], wu_ref[...])
        value, half = gelu_parts(inner)
        slope = half + inner * (jnp.exp(-0.5 * inner * inner) * 0.3989422804014327)
        slope_ref[k * chunk : (k + 1) * chunk, :] = slope.astype(bf16)
        hid_ref[k * per : (k + 1) * per, :] = mul(pool, value.astype(bf16))
    terms = mul(two_terms(hid_ref[...] * (1.0 / TXT_LEN)), wd_ref[...])
    count = hid_ref.shape[0]
    added = terms[:count] + terms[count:]

    @pl.when(step == 0)
    def _():
        acc[...] = sum_ref[...] * (1.0 / TXT_LEN) + added

    @pl.when(step > 0)
    def _():
        acc[...] += added

    @pl.when(step == pl.num_programs(0) - 1)
    def _():
        unit, inverse = unit_rows(acc[...])
        unit_ref[...] = unit
        inv_ref[...] = jnp.broadcast_to(inverse, inv_ref.shape)


def text_up(normed2, weight_up, weight_down, middle_sum, after=()):
    rows, count = normed2.shape[0], middle_sum.shape[0]
    fixed = lambda shape: pl.BlockSpec(shape, lambda i: (0, 0))
    return pl.pallas_call(
        text_up_kernel,
        grid=(FF // TILE,),
        out_shape=[
            jax.ShapeDtypeStruct((rows, FF), bf16),
            jax.ShapeDtypeStruct((count, FF), f32),
            jax.ShapeDtypeStruct((count, D), f32),
            jax.ShapeDtypeStruct((count, 128), f32),
        ],
        in_specs=[
            fixed((rows, D)),
            pl.BlockSpec((D, TILE), lambda i: (0, i)),
            pl.BlockSpec((TILE, D), lambda i: (i, 0)),
            fixed((count, D)),
        ]
        + anywhere(after),
        out_specs=[
            pl.BlockSpec((rows, TILE), lambda i: (0, i)),
            pl.BlockSpec((count, TILE), lambda i: (0, i)),
            fixed((count, D)),
            fixed((count, 128)),
        ],
        scratch_shapes=[pltpu.VMEM((count, D), f32)],
        compiler_params=params(),
        cost_estimate=cost(2 * rows * D * FF, 4 * D * FF + 2 * rows * FF, 20 * rows * FF),
        name="text_up",
    )(normed2, weight_up, weight_down, middle_sum, *after)


def image_up_kernel(fold, h2_ref, wu_ref, wd_ref, sum_ref, *refs):
    out_ref, acc = refs[-2:]
    step = pl.program_id(0)
    rows, count = h2_ref.shape[0], sum_ref.shape[0]
    chunk = 80
    summed = jnp.zeros((count, TILE), f32)
    for k in range(rows // chunk):
        inner = mul(h2_ref[k * chunk : (k + 1) * chunk, :], wu_ref[...])
        value, _ = gelu_parts(inner)
        pool = pool_matrix(count, chunk, k * chunk, IMG_LEN)
        summed = summed + mul(pool, value.astype(bf16))
    mean = two_terms(summed * (1.0 / IMG_LEN))
    place = lax.broadcasted_iota(jnp.int32, (TILE, TILE // fold), 0)
    picked = lax.broadcasted_iota(jnp.int32, (TILE, TILE // fold), 1) * fold
    terms = jnp.zeros((2 * count, D), f32)
    for k in range(fold):
        chosen = jnp.where(place == picked + k, 1.0, 0.0).astype(bf16)
        part = mul(mean, chosen).astype(bf16)
        terms = terms + mul(part, wd_ref[:, k * D : (k + 1) * D])
    added = terms[:count] + terms[count:]

    @pl.when(step == 0)
    def _():
        acc[...] = sum_ref[...] * (1.0 / IMG_LEN) + added

    @pl.when(step > 0)
    def _():
        acc[...] += added

    @pl.when(step == pl.num_programs(0) - 1)
    def _():
        out_ref[...] = unit_rows(acc[...])[0].astype(bf16)


def image_up(normed2, whole, up_col, down_col, middle_sum, after=()):
    rows, count = normed2.shape[0], middle_sum.shape[0]
    fold = FF // D
    fixed = lambda shape: pl.BlockSpec(shape, lambda i: (0, 0))
    return pl.pallas_call(
        functools.partial(image_up_kernel, fold),
        grid=(FF // TILE,),
        out_shape=jax.ShapeDtypeStruct((count, D), bf16),
        in_specs=[
            fixed((rows, D)),
            pl.BlockSpec((D, TILE), lambda i: (0, up_col // TILE + i)),
            pl.BlockSpec((TILE // fold, fold * D), lambda i: (i, down_col // (fold * D))),
            fixed((count, D)),
        ]
        + anywhere(after),
        out_specs=fixed((count, D)),
        scratch_shapes=[pltpu.VMEM((count, D), f32)],
        compiler_params=params(),
        cost_estimate=cost(2 * rows * D * FF, 4 * D * FF, 15 * rows * FF),
        name="image_up",
    )(normed2, whole, whole, middle_sum, *after)


def loss_parts(text_rows, pos, image_all):
    similar = mul_bt(text_rows, image_all) * logit_scale
    shifted = jnp.exp(similar - logit_scale)
    alive = jnp.max(pos, axis=1, keepdims=True)
    row_sum = jnp.sum(shifted, axis=1, keepdims=True)
    row_count = jnp.maximum(jnp.sum(pos, axis=1, keepdims=True), 1.0)
    return similar, shifted, alive, row_sum, row_count


def sums_over_captions(text_rows, pos, image_all):
    similar, shifted, alive, row_sum, row_count = loss_parts(text_rows, pos, image_all)
    pos_similar = pos * similar
    cap_term = alive * (
        logit_scale + jnp.log(row_sum) - jnp.sum(pos_similar, axis=1, keepdims=True) / row_count
    )
    return (
        jnp.sum(alive * shifted, axis=0, keepdims=True),
        jnp.sum(pos, axis=0, keepdims=True),
        jnp.sum(pos_similar, axis=0, keepdims=True),
        jnp.sum(cap_term, axis=0, keepdims=True),
        jnp.sum(alive, axis=0, keepdims=True),
    )


def loss_from(sums):
    col_sum, col_count, col_pos, cap_total, live_total = sums
    img_term = logit_scale + jnp.log(col_sum) - col_pos / col_count
    return 0.5 * cap_total / live_total + 0.5 * jnp.mean(img_term, axis=1, keepdims=True)


def grad_of_unit(text_rows, pos, image_all, col_sum, col_count, live_total):
    _, shifted, alive, row_sum, row_count = loss_parts(text_rows, pos, image_all)
    cap_share, img_share = 0.5 / live_total, 0.5 / image_all.shape[0]
    grad_sims = alive * shifted * (cap_share / row_sum + img_share / col_sum) - pos * (
        cap_share / row_count + img_share / col_count
    )
    return mul(grad_sims.astype(bf16), image_all) * logit_scale


def turned(grad, unit):
    return grad - unit * jnp.sum(grad * unit, axis=-1, keepdims=True)


def loss_kernel(
    pack_ref, image_ref, own_ref, unit_ref, inv_ref, loss_ref, row_ref, low_ref, col_sum_ref,
    col_count_ref, live_ref
):
    image_all = image_ref[...]
    chunk = 256
    total = None
    for k in range(pack_ref.shape[0] // chunk):
        at = slice(k * chunk, (k + 1) * chunk)
        part = sums_over_captions(pack_ref[at, :D], pack_ref[at, D:].astype(f32), image_all)
        total = part if total is None else [a + b for a, b in zip(total, part)]
    loss_ref[...] = jnp.broadcast_to(loss_from(total), loss_ref.shape)
    col_sum, col_count, _, _, live_total = total
    col_sum_ref[...] = col_sum
    col_count_ref[...] = col_count
    live_ref[...] = jnp.broadcast_to(live_total, live_ref.shape)
    grad = grad_of_unit(
        own_ref[:, :D], own_ref[:, D:].astype(f32), image_all, col_sum, col_count, live_total
    )
    row = inv_ref[:, :1] * turned(grad, unit_ref[...]) * (1.0 / TXT_LEN)
    row_ref[...] = row
    low_ref[...] = row.astype(bf16)


def loss_and_rows(pack, image_all, own_pack, unit, inverse):
    images, count = image_all.shape[0], own_pack.shape[0]
    shapes = [(1, 128), (count, D), (count, D), (1, images), (1, images), (1, 128)]
    kinds = [f32, f32, bf16, f32, f32, f32]
    return pl.pallas_call(
        loss_kernel,
        out_shape=[jax.ShapeDtypeStruct(*item) for item in zip(shapes, kinds)],
        compiler_params=params(),
        cost_estimate=cost(2 * pack.shape[0] * images * D, 2 * pack.size, pack.shape[0] * images),
        name="loss_and_rows",
    )(pack, image_all, own_pack, unit, inverse)


def down_kernel(pack_ref, image_ref, col_sum_ref, col_count_ref, live_ref, hid_ref, *refs):
    step, out_ref = pl.program_id(0), refs[-1]
    text_rows = pack_ref[:, :D]
    grad = grad_of_unit(
        text_rows, pack_ref[:, D:].astype(f32), image_ref[...], col_sum_ref[...],
        col_count_ref[...], live_ref[:, :1]
    )
    rows = (turned(grad, text_rows.astype(f32)) * (1.0 / TXT_LEN)).astype(bf16)
    part = mul_at(hid_ref[...], rows)

    @pl.when(step == 0)
    def _():
        out_ref[...] = part

    @pl.when(step > 0)
    def _():
        out_ref[...] += part


def grad_of_down(pack, image_all, col_sum, col_count, live_total, hidden_cols, after):
    images, chunk = image_all.shape[0], 256
    fixed = lambda shape: pl.BlockSpec(shape, lambda i: (0, 0))
    per = hidden_cols.shape[1]
    return pl.pallas_call(
        down_kernel,
        grid=(pack.shape[0] // chunk,),
        out_shape=jax.ShapeDtypeStruct((per, D), f32),
        in_specs=[
            pl.BlockSpec((chunk, pack.shape[1]), lambda i: (i, 0)),
            fixed((images, D)), fixed((1, images)), fixed((1, images)), fixed((1, 128)),
            pl.BlockSpec((chunk, per), lambda i: (i, 0)),
        ]
        + anywhere(after),
        out_specs=fixed((per, D)),
        compiler_params=params(),
        cost_estimate=cost(4 * pack.shape[0] * images * D, 2 * pack.size, pack.shape[0] * images),
        name="grad_of_down",
    )(pack, image_all, col_sum, col_count, live_total, hidden_cols, *after)


def mlp_back_kernel(
    low_ref, wd_ref, slope_ref, wu_ref, lhs_ref, mid_ref, gain_ref, row_ref, keep_a, send_a, keep_b,
    send_b, out_ref, gain_out, bias_out, acc
):
    step = pl.program_id(0)
    count, rows = low_ref.shape[0], slope_ref.shape[0]
    half = D // 2
    hidden = mul_bt(low_ref[...], wd_ref[...])
    wide = jnp.broadcast_to(hidden[:, None, :], (count, TXT_LEN, TILE)).reshape(rows, TILE)
    inner = (wide * slope_ref[...].astype(f32)).astype(bf16)
    weight = mul(lhs_ref[0], inner).astype(bf16)

    @pl.when(step < pl.num_programs(0) // 2)
    def _():
        keep_a[...] = weight[:half]
        send_a[...] = weight[half:]

    @pl.when(step >= pl.num_programs(0) // 2)
    def _():
        keep_b[...] = weight[:half]
        send_b[...] = weight[half:]

    added = mul_bt(inner, wu_ref[...])

    @pl.when(step == 0)
    def _():
        acc[...] = added

    @pl.when(step > 0)
    def _():
        acc[...] += added

    @pl.when(step == pl.num_programs(0) - 1)
    def _():
        chunk = 128
        per = chunk // TXT_LEN
        gain = gain_ref[...]
        gain_out[...] = jnp.zeros_like(gain_out)
        bias_out[...] = jnp.zeros_like(bias_out)

        @pl.loop(0, rows // chunk)
        def _(k):
            at = pl.ds(pl.multiple_of(k * chunk, chunk), chunk)
            unit, scale = norm_parts(mid_ref[at, :])
            grad = acc[at, :]
            gain_out[...] += jnp.sum(grad * unit, axis=0, keepdims=True)
            bias_out[...] += jnp.sum(grad, axis=0, keepdims=True)
            row = row_ref[pl.ds(pl.multiple_of(k * per, per), per), :]
            row = jnp.broadcast_to(row[:, None, :], (per, TXT_LEN, D)).reshape(chunk, D)
            out_ref[at, :] = row + norm_back(unit, scale, gain, grad)


def mlp_back(grad_row, grad_low, weight_down, slope, weight_up, lhs, middle, gain):
    rows, count = slope.shape[0], grad_row.shape[0]
    steps = FF // TILE
    fixed = lambda shape: pl.BlockSpec(shape, lambda i: (0, 0))
    first = pl.BlockSpec((D // 2, TILE), lambda i: (0, jnp.minimum(i, steps // 2 - 1)))
    second = pl.BlockSpec((D // 2, TILE), lambda i: (0, jnp.maximum(i - steps // 2, 0)))
    part = jax.ShapeDtypeStruct((D // 2, FF // 2), bf16)
    line = jax.ShapeDtypeStruct((1, D), f32)
    return pl.pallas_call(
        mlp_back_kernel,
        grid=(steps,),
        out_shape=[part] * 4 + [jax.ShapeDtypeStruct((rows, D), f32), line, line],
        in_specs=[
            fixed((count, D)),
            pl.BlockSpec((TILE, D), lambda i: (i, 0)),
            pl.BlockSpec((rows, TILE), lambda i: (0, i)),
            pl.BlockSpec((D, TILE), lambda i: (0, i)),
            pl.BlockSpec((1, D, rows), lambda i: (i // (steps // 2), 0, 0)),
            fixed((rows, D)),
            fixed((1, D)),
            fixed((count, D)),
        ],
        out_specs=[first, first, second, second, fixed((rows, D)), fixed((1, D)), fixed((1, D))],
        scratch_shapes=[pltpu.VMEM((rows, D), f32)],
        compiler_params=params(),
        cost_estimate=cost(4 * rows * D * FF, 4 * D * FF + 2 * rows * FF + 2 * D * FF, rows * FF),
        name="mlp_back",
    )(grad_low, weight_down, slope, weight_up, lhs, middle, gain[None], grad_row)


def attention_back_kernel(grad_ref, wo_ref, qkv_ref, lse_ref, *refs):
    low_ref, out_ref = refs[-2:]
    chunk = grad_ref.shape[0]
    mask = same_sequence(chunk, 0, chunk, 0, TXT_LEN)
    low = grad_ref[...].astype(bf16)
    low_ref[...] = low
    grad_att = mul_bt(low, wo_ref[...]).astype(bf16)
    for pair in range(HEADS // 2):
        queries = qkv_ref[:, pair_cols(0, pair)] * bf16(HEAD ** (-0.5))
        keys = two_heads(qkv_ref[:, pair_cols(1, pair)])
        vals = two_heads(qkv_ref[:, pair_cols(2, pair)])
        grads = grad_att[:, pair_cols(0, pair)]
        scores, grad_probs = mul_bt(keys, queries), mul_bt(vals, grads)
        probs, grad_scores = [], []
        for k in range(2):
            at = slice(k * chunk, (k + 1) * chunk)
            head = 2 * pair + k
            shifted = scores[at] - lse_ref[head : head + 1, :]
            prob = jnp.where(mask, jnp.exp(jnp.where(mask, shifted, 0.0)), 0.0)
            along = jnp.sum(grad_probs[at] * prob, axis=0, keepdims=True)
            grad_scores.append((prob * (grad_probs[at] - along)).astype(bf16))
            probs.append(prob.astype(bf16))
        grad_q = mul_at(jnp.concatenate(grad_scores, axis=0), keys) * HEAD ** (-0.5)
        grad_k = mul(jnp.concatenate(grad_scores, axis=1), two_heads(queries))
        grad_v = mul(jnp.concatenate(probs, axis=1), two_heads(grads))
        out_ref[:, pair_cols(0, pair)] = grad_q.astype(bf16)
        out_ref[:, pair_cols(1, pair)] = grad_k.astype(bf16)
        out_ref[:, pair_cols(2, pair)] = grad_v.astype(bf16)


def attention_back(grad_middle, weight_out, project, log_sums, first, count, after=()):
    chunk = 128
    rows = count * chunk
    return pl.pallas_call(
        attention_back_kernel,
        grid=(count,),
        out_shape=[
            jax.ShapeDtypeStruct((rows, D), bf16),
            jax.ShapeDtypeStruct((rows, 3 * D), bf16),
        ],
        in_specs=[
            pl.BlockSpec((chunk, D), lambda i: (i + first, 0)),
            pl.BlockSpec((D, D), lambda i: (0, 0)),
            pl.BlockSpec((chunk, 3 * D), lambda i: (i + first, 0)),
            pl.BlockSpec((16, chunk), lambda i: (i + first, 0)),
        ]
        + anywhere(after),
        out_specs=[
            pl.BlockSpec((chunk, D), lambda i: (i, 0)),
            pl.BlockSpec((chunk, 3 * D), lambda i: (i, 0)),
        ],
        compiler_params=params(),
        cost_estimate=cost(10 * rows * D * D, 16 * rows * D + 2 * D * D, rows * 128 * HEADS),
        name="attention_back",
    )(grad_middle, weight_out, project, log_sums, *after)


def mul_rows(lhs, parts):
    total, row = 0.0, 0
    for part in parts:
        total = total + mul(lhs[:, row : row + part.shape[0]], part[...])
        row += part.shape[0]
    return total


def weight_back_kernel(counts, lhs_ref, *refs):
    step, half = pl.program_id(0), D // 2
    keep, send = refs[-2:]
    row = 0
    for k, count in enumerate(counts):
        parts = refs[row : row + count]
        row += count

        @pl.when(step == k if len(counts) > 1 else step >= 0)
        def _(parts=parts):
            weight = mul_rows(lhs_ref[0], parts).astype(bf16)
            keep[...] = weight[:half]
            send[...] = weight[half:]


def weight_back(lhs, first, groups, blocks, after=()):
    rows = lhs.shape[2]
    steps = 2
    many = len(groups) > 1
    given = [part for group in groups for part in group]
    return pl.pallas_call(
        functools.partial(weight_back_kernel, [len(group) for group in groups]),
        grid=(steps,),
        out_shape=[jax.ShapeDtypeStruct((D // 2, steps * D), bf16)] * 2,
        in_specs=[pl.BlockSpec((1, D, rows), lambda i: (first + (i if many else 0), 0, 0))]
        + [
            pl.BlockSpec((part.shape[0], D), lambda i, col=col: (0, col + (0 if many else i)))
            for group, col in zip(groups, blocks)
            for part in group
        ]
        + anywhere(after),
        out_specs=[pl.BlockSpec((D // 2, D), lambda i: (0, i))] * 2,
        compiler_params=params(),
        cost_estimate=cost(4 * rows * D * D, 4 * rows * D + 7 * D * D),
        name="weight_back",
    )(lhs, *given, *after)


def input_back_kernel(count, *refs):
    projs = refs[:count]
    w_ref, x_ref, gain_ref, mid_ref = refs[count : count + 4]
    out_ref, gain_out, bias_out, acc = refs[-4:]
    step = pl.program_id(0)
    rows, chunk = x_ref.shape[0], 128
    row = 0
    for part in projs:
        at = slice(row, row + part.shape[0])
        row += part.shape[0]
        added = mul_bt(part[...], w_ref[...])

        @pl.when(step == 0)
        def _(at=at, added=added):
            acc[at, :] = added

        @pl.when(step > 0)
        def _(at=at, added=added):
            acc[at, :] += added

    @pl.when(step == pl.num_programs(0) - 1)
    def _():
        gain = gain_ref[...]
        gain_out[...] = jnp.zeros_like(gain_out)
        bias_out[...] = jnp.zeros_like(bias_out)

        @pl.loop(0, rows // chunk)
        def _(k):
            at = pl.ds(pl.multiple_of(k * chunk, chunk), chunk)
            unit, scale = norm_parts(x_ref[at, :].astype(f32))
            grad = acc[at, :]
            gain_out[...] += jnp.sum(grad * unit, axis=0, keepdims=True)
            bias_out[...] += jnp.sum(grad, axis=0, keepdims=True)
            out_ref[at, :] = mid_ref[at, :] + norm_back(unit, scale, gain, grad)


def input_back(grad_projs, weight, rows_in, gain, grad_middle, after=()):
    rows = rows_in.shape[0]
    fixed = lambda shape: pl.BlockSpec(shape, lambda i: (0, 0))
    line = jax.ShapeDtypeStruct((1, D), f32)
    return pl.pallas_call(
        functools.partial(input_back_kernel, len(grad_projs)),
        grid=(3,),
        out_shape=[jax.ShapeDtypeStruct((rows, D), f32), line, line],
        in_specs=[pl.BlockSpec((part.shape[0], D), lambda i: (0, i)) for part in grad_projs]
        + [
            pl.BlockSpec((D, D), lambda i: (0, i)),
            fixed((rows, D)), fixed((1, D)), fixed((rows, D)),
        ]
        + anywhere(after),
        out_specs=[fixed((rows, D)), fixed((1, D)), fixed((1, D))],
        scratch_shapes=[pltpu.VMEM((rows, D), f32)],
        compiler_params=params(),
        cost_estimate=cost(6 * rows * D * D, 14 * rows * D + 6 * D * D),
        name="input_back",
    )(*grad_projs, weight, rows_in, gain[None], grad_middle, *after)


def local(
    images,
    captions,
    img_gain1,
    img_bias1,
    img_qkv,
    img_out,
    img_gain2,
    img_bias2,
    img_up,
    img_down,
    txt_gain1,
    txt_bias1,
    txt_qkv,
    txt_out,
    txt_gain2,
    txt_bias2,
    txt_up,
    txt_down,
    counts,
    matches,
):
    peers = lax.axis_size(AXIS)
    own = lax.axis_index(AXIS)
    per = D // peers
    img_local = counts.shape[0]
    cap_local = matches.shape[0]
    total_images = matches.shape[1]

    whole = lax.all_gather(
        jnp.concatenate([img_up.reshape(per, FF), img_down.reshape(per, FF)], axis=1),
        AXIS,
        axis=0,
        tiled=True,
    )
    small = peers == 32
    shard = jnp.concatenate([img_qkv.reshape(per, 3 * D), img_out.reshape(per, D)], axis=1)
    if small:
        line, perm = gathered_line(shard), row_order((1, 4, 2, 16, 8))
    else:
        line, perm = lax.all_gather(shard, AXIS, axis=0, tiled=True), jnp.eye(D, dtype=bf16)

    normed1, project, attended, middle, normed2, middle_sum, log_sums = text_front(
        captions, txt_gain1, txt_bias1, txt_qkv, txt_out, txt_gain2, txt_bias2
    )
    middle_sum, line = in_turn(middle_sum, line)
    beside, above = (swapped(line, 2), swapped(line, 4)) if small else (line, line)
    slope, hidden_sum, text_unit, inverse = text_up(
        normed2, txt_up, txt_down, middle_sum, (line,)
    )
    text_unit, (beside, above) = in_turn(text_unit, (beside, above))

    ends_at = jnp.cumsum(counts)
    slot_ids = lax.iota(jnp.int32, cap_local)
    owner = jnp.sum((ends_at[None, :] <= slot_ids[:, None]).astype(jnp.int32), axis=1)
    owner = owner + own * img_local
    live = slot_ids < ends_at[-1]
    columns = lax.iota(jnp.int32, total_images)
    positive = ((matches > 0) | (owner[:, None] == columns[None, :])) & live[:, None]

    own_pack = packed(text_unit, positive.astype(bf16), ())
    pieces = [line]
    if small:
        held = own_pack[None]
        first, second = diagonal(beside, above)
        other, first, second = lax.optimization_barrier((swapped(held, 16), first, second))
        held = joined(held, other, 16)
        pieces = [line, beside, above, first, second]
        pieces = pieces + [swapped(piece, 1) for piece in pieces]

    normed_img, middle_img = image_front(
        images, pieces, perm, img_gain1, img_bias1, img_gain2, img_bias2
    )
    if small:
        scaled_sum = (hidden_sum * inverse[:, :1]).astype(bf16)
        normed_img, scaled_sum, other = lax.optimization_barrier(
            (normed_img, scaled_sum, swapped(held, 8))
        )
        held = joined(held, other, 8)
        hidden_cols = lax.all_to_all(scaled_sum, AXIS, split_axis=1, concat_axis=0, tiled=True)
        beside, above = swapped(held, 2), swapped(held, 4)
        whole, beside, above = lax.optimization_barrier((whole, beside, above))
        first, second = diagonal(beside, above)
    image_low = image_up(normed_img, whole, 0, FF, middle_img)
    if small:
        image_low, first, second, hidden_cols = lax.optimization_barrier(
            (image_low, first, second, hidden_cols)
        )
        across = jnp.concatenate([first, second], axis=0)
        held = joined(joined(held, beside, 2), joined(above, across, 2), 4, 4)
        other = swapped(held, 1)
    image_all = spread(image_low).reshape(total_images, D)
    if small:
        image_all, other = in_turn(image_all, other)
        text_pack = joined(held, other, 1).reshape(-1, D + total_images)

    order_a, order_b, tail = stage_orders()
    matrix_a, matrix_b = row_order(order_a + tail[::-1]), row_order(order_b + tail[::-1])
    lhs_up = jnp.stack([placed(matrix_a, normed2), placed(matrix_b, normed2)])
    lhs_rest = jnp.stack(
        [placed(matrix_a, normed1), placed(matrix_b, normed1), placed(matrix_b, attended)]
    )

    if small:
        loss_value, grad_row, row_low, col_sum, col_count, live_total = loss_and_rows(
            text_pack, image_all, own_pack, text_unit, inverse
        )
        loss_value = loss_value[0, 0]
    else:
        text_low, pos = own_pack[:, :D], own_pack[:, D:].astype(f32)
        sums = lax.psum(sums_over_captions(text_low, pos, image_all), AXIS)
        loss_value = loss_from(sums)[0, 0]
        grad = grad_of_unit(text_low, pos, image_all, sums[0], sums[1], sums[4])
        grad_row = inverse[:, :1] * turned(grad, text_unit) * (1.0 / TXT_LEN)
        row_low = grad_row.astype(bf16)

    *up, grad_middle, gain_two, bias_two = mlp_back(
        grad_row, row_low, txt_down, slope, txt_up, lhs_up, middle, txt_gain2
    )
    stages = len(order_a)
    low_one, proj_one = attention_back(grad_middle, txt_out, project, log_sums, 0, 2)
    for stage in range(stages - 2):
        up = fold(hand_on(up, stage), (proj_one,))
    low_two, proj_two = attention_back(grad_middle, txt_out, project, log_sums, 2, 3, up)
    up = fold(hand_on(up, stages - 2), (proj_two,))
    projs, lows = (proj_one, proj_two), (low_one, low_two)
    rest_a = weight_back(lhs_rest, 0, [projs], [0], up)
    up = hand_on_last(fold_last(hand_on(up, stages - 1), rest_a[1:]))
    rest_b = weight_back(lhs_rest, 1, [projs, lows], [2, 0], up[:1])
    rest = [*rest_a, *rest_b]
    for stage in range(stages - 2):
        rest = fold(hand_on(rest, stage))
    caption_grad, gain_one, bias_one = input_back(
        projs, txt_qkv, captions, txt_gain1, grad_middle, rest[:1]
    )
    caption_grad, up = in_turn(caption_grad, up)
    rest = fold(hand_on(rest, stages - 2), (caption_grad,))
    norms = jnp.concatenate([gain_one, bias_one, gain_two, bias_two], axis=0)
    norms, rest = in_turn(norms, rest)
    if small:
        grad_down = grad_of_down(
            text_pack, image_all, col_sum, col_count, live_total, hidden_cols, rest
        )
        rest = fold_last(hand_on(rest, stages - 1), (grad_down,))
    else:
        grad_down = lax.psum_scatter(
            mul_at(hidden_sum.astype(bf16), row_low), AXIS, scatter_dimension=0, tiled=True
        )
        rest = fold_last(hand_on(rest, stages - 1))
    up_share = sum_last(*up)
    rest_share = sum_last(*hand_on_last(rest))
    norms = jnp.sum(spread(norms[None]), axis=0).reshape(4, D)
    return (
        loss_value,
        caption_grad,
        norms[0],
        norms[1],
        rest_share[:, : 3 * D].reshape(-1),
        rest_share[:, 3 * D :].reshape(-1),
        norms[2],
        norms[3],
        up_share.reshape(-1),
        grad_down.reshape(-1),
    )


def solution(mesh):
    split, flat, whole = P("blk", None), P("blk"), P()
    image_block = (whole, whole, flat, flat, whole, whole, flat, flat)
    return jax.shard_map(
        local,
        mesh=mesh,
        in_specs=(split, split) + image_block + (whole,) * 8 + (flat, split),
        out_specs=(whole, split, whole, whole, flat, flat, whole, whole, flat, flat),
        check_vma=False,
    )
```

```python
import functools

import jax
import jax.numpy as jnp
from jax import lax
from jax.experimental import pallas as pl
from jax.experimental.pallas import tpu as pltpu
from jax.sharding import PartitionSpec as P

D = 768
FF = 3072
HEAD = 64
HEADS = D // HEAD
IMG_LEN = 50
TXT_LEN = 16
AXIS = "blk"

norm_eps = 1e-06
logit_scale = 50.0
f32 = jnp.float32
bf16 = jnp.bfloat16


def swapped(value, mask):
    peers = lax.axis_size(AXIS)
    return lax.ppermute(value, AXIS, [(i, i ^ mask) for i in range(peers)])


def bit_masks():
    peers = lax.axis_size(AXIS)
    return [1 << k for k in range(peers.bit_length() - 1)]


def joined(held, other, mask, outer=None):
    upper = (lax.axis_index(AXIS) & mask) > 0
    first = jnp.where(upper, other, held)
    second = jnp.where(upper, held, other)
    outer = held.shape[0] if outer is None else outer
    parts = [part.reshape((outer, -1) + held.shape[1:]) for part in (first, second)]
    return jnp.stack(parts, axis=1).reshape((-1,) + held.shape[1:])


def spread(block):
    peers = lax.axis_size(AXIS)
    copies = jnp.broadcast_to(block[None], (peers,) + block.shape)
    return lax.all_to_all(copies, AXIS, split_axis=0, concat_axis=0, tiled=True)


def stage_orders():
    masks = bit_masks()
    head, tail = masks[:-2], masks[-2:]
    order_a = list(head)
    order_b = list(head)
    for k in range(1, len(head) - 1, 2):
        order_b[k], order_b[k + 1] = order_b[k + 1], order_b[k]
    return order_a, order_b, tail


def row_order(bits):
    peers = lax.axis_size(AXIS)
    own = lax.axis_index(AXIS)
    per = D // peers
    places = lax.iota(jnp.int32, D)
    block = places // per
    target = jnp.zeros_like(block) + own
    for k, mask in enumerate(bits):
        target = target ^ (((block >> (len(bits) - 1 - k)) & 1) * mask)
    source = target * per + places % per
    return (source[:, None] == lax.iota(jnp.int32, D)[None, :]).astype(bf16)


def gathered_line(shard):
    return jnp.concatenate([shard] + [swapped(shard, mask) for mask in (8, 16, 24)], axis=0)


def diagonal(beside, above):
    half = beside.shape[0] // 2
    return swapped(beside[:half], 4), swapped(above[half:], 2)


def in_turn(first, then):
    return lax.optimization_barrier((first, then))


def placed(order, values):
    return mul_bt(order, values).astype(bf16)


def hand_on(parts, stage):
    order_a, order_b, _ = stage_orders()
    keep_a, send_a, keep_b, send_b = parts
    return keep_a, swapped(send_a, order_a[stage]), keep_b, swapped(send_b, order_b[stage])


def hand_on_last(blocks):
    low, high = stage_orders()[2]
    own, *others = blocks
    return own, [swapped(block, mask) for block, mask in zip(others, (low, high, low | high))]


def sum_last(own, others):
    total = own
    for other in others:
        total = total + other.astype(f32)
    return total


VMEM_BYTES = 56 << 20
TILE = 512


def norm_parts(values):
    average = jnp.mean(values, axis=-1, keepdims=True)
    centred = values - average
    variance = jnp.mean(centred * centred, axis=-1, keepdims=True)
    scale = lax.rsqrt(variance + norm_eps)
    return centred * scale, scale


def norm_back(unit, scale, gain, grad):
    inner = grad * gain
    shift = jnp.mean(inner, axis=-1, keepdims=True)
    along = jnp.mean(inner * unit, axis=-1, keepdims=True)
    return scale * (inner - shift - unit * along)


def mul(lhs, rhs):
    return jnp.dot(lhs, rhs, preferred_element_type=f32)


def mul_bt(lhs, rhs):
    return lax.dot_general(lhs, rhs, (((1,), (1,)), ((), ())), preferred_element_type=f32)


def mul_at(lhs, rhs):
    return lax.dot_general(lhs, rhs, (((0,), (0,)), ((), ())), preferred_element_type=f32)


def params(**more):
    return pltpu.CompilerParams(vmem_limit_bytes=VMEM_BYTES, **more)


def cost(flops, moved, transcendentals=0):
    return pl.CostEstimate(flops=flops, bytes_accessed=moved, transcendentals=transcendentals)


def lane_halves(dtype):
    lane = lax.broadcasted_iota(jnp.int32, (1, 2 * HEAD), 1)
    low = jnp.where(lane < HEAD, 1.0, 0.0)
    return low.astype(dtype), (1.0 - low).astype(dtype)


def two_heads(pair):
    low, high = lane_halves(bf16)
    return jnp.concatenate([pair * low, pair * high], axis=0)


def same_sequence(rows, row0, cols, col0, seq_len):
    row = (lax.broadcasted_iota(jnp.int32, (rows, cols), 0) + row0) // seq_len
    col = (lax.broadcasted_iota(jnp.int32, (rows, cols), 1) + col0) // seq_len
    return row == col


def softmax_down(scores, mask):
    keys = mask.shape[0]
    parts, sums = [], []
    for k in range(2):
        part = jnp.where(mask, scores[k * keys : (k + 1) * keys], -1e30)
        most = jnp.max(part, axis=0, keepdims=True)
        raised = jnp.exp(part - most)
        total = jnp.sum(raised, axis=0, keepdims=True)
        parts.append(raised * (1.0 / total))
        sums.append(most + jnp.log(total))
    return parts, sums


def fold_kernel(keep_a, got_a, keep_b, got_b, *refs):
    outs = refs[-4:]
    half = outs[0].shape[0]
    for k, (kept, got) in enumerate(((keep_a, got_a), (keep_b, got_b))):
        for j in range(2):
            at = slice(j * half, (j + 1) * half)
            outs[2 * k + j][...] = (kept[at, :].astype(f32) + got[at, :].astype(f32)).astype(bf16)


def fold(parts, after=()):
    rows, cols = parts[0].shape
    if rows % 32:
        whole = [
            (kept.astype(f32) + got.astype(f32)).astype(bf16)
            for kept, got in (parts[:2], parts[2:])
        ]
        return [part for one in whole for part in (one[: rows // 2], one[rows // 2 :])]
    tile = 512
    return pl.pallas_call(
        fold_kernel,
        grid=(cols // tile,),
        out_shape=[jax.ShapeDtypeStruct((rows // 2, cols), bf16)] * 4,
        in_specs=[pl.BlockSpec((rows, tile), lambda i: (0, i))] * 4 + anywhere(after),
        out_specs=[pl.BlockSpec((rows // 2, tile), lambda i: (0, i))] * 4,
        compiler_params=params(),
        cost_estimate=cost(2 * rows * cols, 12 * rows * cols),
        name="fold",
    )(*parts, *after)


def fold_last_kernel(keep_a, got_a, keep_b, got_b, *refs):
    own_ref, *outs = refs[-4:]
    rows = own_ref.shape[0]
    cols = keep_a.shape[1]
    for k, (kept, got) in enumerate(((keep_a, got_a), (keep_b, got_b))):
        total = kept[...].astype(f32) + got[...].astype(f32)
        at = slice(k * cols, (k + 1) * cols)
        own_ref[:, at] = total[:rows]
        for j, out in enumerate(outs):
            out[:, at] = total[(j + 1) * rows : (j + 2) * rows].astype(bf16)


def fold_last(parts, after=()):
    rows, cols = parts[0].shape
    shape = (rows // 4, 2 * cols)
    if rows % 32:
        pairs = (parts[:2], parts[2:])
        both = [kept.astype(f32) + got.astype(f32) for kept, got in pairs]
        own, *others = jnp.split(jnp.concatenate(both, axis=1), 4)
        return [own] + [other.astype(bf16) for other in others]
    return pl.pallas_call(
        fold_last_kernel,
        out_shape=[jax.ShapeDtypeStruct(shape, f32)] + [jax.ShapeDtypeStruct(shape, bf16)] * 3,
        in_specs=[pl.BlockSpec(memory_space=pltpu.VMEM)] * 4 + anywhere(after),
        compiler_params=params(),
        cost_estimate=cost(2 * rows * cols, 12 * rows * cols),
        name="fold_last",
    )(*parts, *after)


def anywhere(after):
    return [pl.BlockSpec(memory_space=pl.ANY)] * len(after)


def pair_cols(part, pair):
    start = part * D + pair * 2 * HEAD
    return slice(start, start + 2 * HEAD)


def norm_rows(src, dst, gain, bias, step_rows):
    @pl.loop(0, src.shape[0] // step_rows)
    def _(step):
        at = pl.ds(pl.multiple_of(step * step_rows, step_rows), step_rows)
        unit, _ = norm_parts(src[at, :].astype(f32))
        dst[at, :] = (unit * gain + bias).astype(bf16)


def attend_along(qkv_ref, att_ref, q_rows, k_rows, mask):
    low, high = lane_halves(f32)
    for pair in range(HEADS // 2):
        queries = two_heads(qkv_ref[q_rows, pair_cols(0, pair)] * bf16(HEAD ** (-0.5)))
        scores = mul_bt(queries, qkv_ref[k_rows, pair_cols(1, pair)])
        scores = jnp.where(mask, scores, -1e30)
        raised = jnp.exp(scores - jnp.max(scores, axis=-1, keepdims=True))
        probs = (raised * (1.0 / jnp.sum(raised, axis=-1, keepdims=True))).astype(bf16)
        half = probs.shape[0] // 2
        mixed = mul(probs, qkv_ref[k_rows, pair_cols(2, pair)])
        att_ref[q_rows, pair_cols(0, pair)] = (mixed[:half] * low + mixed[half:] * high).astype(bf16)


def attend(qkv_ref, att_ref, q_rows, k_rows, mask, keep_sums):
    for pair in range(HEADS // 2):
        queries = qkv_ref[q_rows, pair_cols(0, pair)] * bf16(HEAD ** (-0.5))
        scores = mul_bt(two_heads(qkv_ref[k_rows, pair_cols(1, pair)]), queries)
        probs, sums = softmax_down(scores, mask)
        vals = two_heads(qkv_ref[k_rows, pair_cols(2, pair)])
        mixed = mul_at(jnp.concatenate(probs, axis=0).astype(bf16), vals)
        att_ref[q_rows, pair_cols(0, pair)] = mixed.astype(bf16)
        for k in range(2):
            keep_sums(2 * pair + k, sums[k])


def text_front_kernel(
    x_ref, g1_ref, b1_ref, wqkv_ref, wo_ref, g2_ref, b2_ref, h1_ref, qkv_ref, att_ref, mid_ref,
    h2_ref, sum_ref, lse_ref
):
    rows, chunk = x_ref.shape[0], 128
    norm_rows(x_ref, h1_ref, g1_ref[...], b1_ref[...], chunk)

    @pl.loop(0, 3 * D // 256)
    def _(step):
        at = pl.ds(pl.multiple_of(step * 256, 256), 256)
        qkv_ref[:, at] = mul(h1_ref[...], wqkv_ref[:, at]).astype(bf16)

    mask = same_sequence(chunk, 0, chunk, 0, TXT_LEN)

    @pl.loop(0, rows // chunk)
    def _(step):
        at = pl.ds(pl.multiple_of(step * chunk, chunk), chunk)

        def keep_sums(head, value):
            lse_ref[pl.ds(step * 16 + head, 1), :] = value

        attend(qkv_ref, att_ref, at, at, mask, keep_sums)

    @pl.loop(0, D // 256)
    def _(step):
        at = pl.ds(pl.multiple_of(step * 256, 256), 256)
        mid_ref[:, at] = x_ref[:, at].astype(f32) + mul(att_ref[...], wo_ref[:, at])

    norm_rows(mid_ref, h2_ref, g2_ref[...], b2_ref[...], chunk)
    per = chunk // TXT_LEN

    @pl.loop(0, rows // chunk)
    def _(step):
        values = mid_ref[pl.ds(pl.multiple_of(step * chunk, chunk), chunk), :]
        sum_ref[pl.ds(pl.multiple_of(step * per, per), per), :] = jnp.sum(
            values.reshape(per, TXT_LEN, D), axis=1
        )


def text_front(rows_in, gain1, bias1, wqkv, wo, gain2, bias2):
    rows = rows_in.shape[0]
    shapes = [
        ((rows, D), bf16),
        ((rows, 3 * D), bf16),
        ((rows, D), bf16),
        ((rows, D), f32),
        ((rows, D), bf16),
        ((rows // TXT_LEN, D), f32),
        ((rows // 128 * 16, 128), f32),
    ]
    return pl.pallas_call(
        text_front_kernel,
        out_shape=[jax.ShapeDtypeStruct(*item) for item in shapes],
        compiler_params=params(),
        cost_estimate=cost(rows * D * D * 8, 14 * D * rows + 8 * D * D, rows * 128 * HEADS),
        name="text_front",
    )(rows_in, gain1[None], bias1[None], wqkv, wo, gain2[None], bias2[None])


def image_front_kernel(
    windows, x_ref, perm_ref, g1_ref, b1_ref, g2_ref, b2_ref, *refs
):
    h2_ref, sum_ref, w_ref, h1_ref, placed_ref, qkv_ref, att_ref, mid_ref, sems = refs[-9:]
    rows, chunk = x_ref.shape[0], 80
    copies, row = [], 0
    for k, piece in enumerate(refs[:-9]):
        place = w_ref.at[pl.ds(row, piece.shape[0]), :]
        copies.append(pltpu.make_async_copy(piece, place, sems.at[k]))
        row += piece.shape[0]
    for copy in copies:
        copy.start()

    def place_columns(src, dst):
        @pl.loop(0, D // 256)
        def _(step):
            at = pl.ds(pl.multiple_of(step * 256, 256), 256)
            dst[:, at] = mul_bt(src[...], perm_ref[at, :]).astype(bf16)

    norm_rows(x_ref, h1_ref, g1_ref[...].astype(f32), b1_ref[...].astype(f32), chunk)
    place_columns(h1_ref, placed_ref)
    for copy in copies:
        copy.wait()

    @pl.loop(0, 3 * D // 256)
    def _(step):
        at = pl.ds(pl.multiple_of(step * 256, 256), 256)
        qkv_ref[:, at] = mul(placed_ref[...], w_ref[:, at]).astype(bf16)

    for row0, count, key0, keys in windows:
        one = same_sequence(count, row0, keys, key0, IMG_LEN)
        mask = jnp.concatenate([one, one], axis=0)
        attend_along(qkv_ref, att_ref, pl.ds(row0, count), pl.ds(key0, keys), mask)
    place_columns(att_ref, placed_ref)

    @pl.loop(0, D // 256)
    def _(step):
        at = pl.ds(pl.multiple_of(step * 256, 256), 256)
        there = pl.ds(pl.multiple_of(step * 256 + 3 * D, 256), 256)
        mid_ref[:, at] = x_ref[:, at].astype(f32) + mul(placed_ref[...], w_ref[:, there])

    norm_rows(mid_ref, h2_ref, g2_ref[...].astype(f32), b2_ref[...].astype(f32), chunk)
    for k in range(rows // IMG_LEN):
        first, last = k * IMG_LEN, (k + 1) * IMG_LEN
        start, end = first // 8 * 8, -(-last // 8) * 8
        values = mid_ref[start:end, :]
        place = lax.broadcasted_iota(jnp.int32, values.shape, 0) + start
        inside = (place >= first) & (place < last)
        sum_ref[k : k + 1, :] = jnp.sum(jnp.where(inside, values, 0.0), axis=0, keepdims=True)


def image_front(rows_in, pieces, perm, gain1, bias1, gain2, bias2):
    rows = rows_in.shape[0]
    windows = ((0, 208, 0, 256), (208, 192, 192, 208))
    vmem = pl.BlockSpec(memory_space=pltpu.VMEM)
    return pl.pallas_call(
        functools.partial(image_front_kernel, windows),
        out_shape=[
            jax.ShapeDtypeStruct((rows, D), bf16),
            jax.ShapeDtypeStruct((rows // IMG_LEN, D), f32),
        ],
        in_specs=[vmem] * 6 + anywhere(pieces),
        out_specs=[vmem] * 2,
        scratch_shapes=[
            pltpu.VMEM((D, 4 * D), bf16),
            pltpu.VMEM((rows, D), bf16),
            pltpu.VMEM((rows, D), bf16),
            pltpu.VMEM((rows, 3 * D), bf16),
            pltpu.VMEM((rows, D), bf16),
            pltpu.VMEM((rows, D), f32),
            pltpu.SemaphoreType.DMA((len(pieces),)),
        ],
        compiler_params=params(),
        cost_estimate=cost(rows * D * D * 12, 8 * D * D, rows * 256 * HEADS),
        name="image_front",
    )(rows_in, perm, gain1[None], bias1[None], gain2[None], bias2[None], *pieces)


def gelu_parts(inner):
    half = 0.5 * (1.0 + lax.erf(inner * (0.5**0.5)))
    return inner * half, half


def pack_kernel(unit_ref, pos_ref, *refs):
    refs[-1][:, :D] = unit_ref[...].astype(bf16)
    refs[-1][:, D:] = pos_ref[...]


def packed(unit, positive, after):
    shape = (unit.shape[0], D + positive.shape[1])
    return pl.pallas_call(
        pack_kernel,
        out_shape=jax.ShapeDtypeStruct(shape, bf16),
        in_specs=[pl.BlockSpec(memory_space=pltpu.VMEM)] * 2 + anywhere(after),
        compiler_params=params(),
        cost_estimate=cost(shape[0] * shape[1], 4 * shape[0] * shape[1]),
        name="packed",
    )(unit, positive, *after)


def pool_matrix(count, rows, row0, seq_len):
    row = (lax.broadcasted_iota(jnp.int32, (count, rows), 1) + row0) // seq_len
    return jnp.where(row == lax.broadcasted_iota(jnp.int32, (count, rows), 0), 1.0, 0.0).astype(bf16)


def two_terms(mean):
    high = mean.astype(bf16)
    low = (mean - high.astype(f32)).astype(bf16)
    return jnp.concatenate([high, low], axis=0)


def unit_rows(pooled):
    inverse = lax.rsqrt(jnp.sum(pooled * pooled, axis=-1, keepdims=True) + norm_eps)
    return pooled * inverse, inverse


def text_up_kernel(h2_ref, wu_ref, wd_ref, sum_ref, *refs):
    slope_ref, hid_ref, unit_ref, inv_ref, acc = refs[-5:]
    step = pl.program_id(0)
    chunk = 128
    per = chunk // TXT_LEN
    pool = pool_matrix(per, chunk, 0, TXT_LEN)
    for k in range(h2_ref.shape[0] // chunk):
        inner = mul(h2_ref[k * chunk : (k + 1) * chunk, :], wu_ref[...])
        value, half = gelu_parts(inner)
        slope = half + inner * (jnp.exp(-0.5 * inner * inner) * 0.3989422804014327)
        slope_ref[k * chunk : (k + 1) * chunk, :] = slope.astype(bf16)
        hid_ref[k * per : (k + 1) * per, :] = mul(pool, value.astype(bf16))
    terms = mul(two_terms(hid_ref[...] * (1.0 / TXT_LEN)), wd_ref[...])
    count = hid_ref.shape[0]
    added = terms[:count] + terms[count:]

    @pl.when(step == 0)
    def _():
        acc[...] = sum_ref[...] * (1.0 / TXT_LEN) + added

    @pl.when(step > 0)
    def _():
        acc[...] += added

    @pl.when(step == pl.num_programs(0) - 1)
    def _():
        unit, inverse = unit_rows(acc[...])
        unit_ref[...] = unit
        inv_ref[...] = jnp.broadcast_to(inverse, inv_ref.shape)


def text_up(normed2, weight_up, weight_down, middle_sum, after=()):
    rows, count = normed2.shape[0], middle_sum.shape[0]
    fixed = lambda shape: pl.BlockSpec(shape, lambda i: (0, 0))
    return pl.pallas_call(
        text_up_kernel,
        grid=(FF // TILE,),
        out_shape=[
            jax.ShapeDtypeStruct((rows, FF), bf16),
            jax.ShapeDtypeStruct((count, FF), f32),
            jax.ShapeDtypeStruct((count, D), f32),
            jax.ShapeDtypeStruct((count, 128), f32),
        ],
        in_specs=[
            fixed((rows, D)),
            pl.BlockSpec((D, TILE), lambda i: (0, i)),
            pl.BlockSpec((TILE, D), lambda i: (i, 0)),
            fixed((count, D)),
        ]
        + anywhere(after),
        out_specs=[
            pl.BlockSpec((rows, TILE), lambda i: (0, i)),
            pl.BlockSpec((count, TILE), lambda i: (0, i)),
            fixed((count, D)),
            fixed((count, 128)),
        ],
        scratch_shapes=[pltpu.VMEM((count, D), f32)],
        compiler_params=params(),
        cost_estimate=cost(2 * rows * D * FF, 4 * D * FF + 2 * rows * FF, 20 * rows * FF),
        name="text_up",
    )(normed2, weight_up, weight_down, middle_sum, *after)


def image_up_kernel(fold, h2_ref, wu_ref, wd_ref, sum_ref, *refs):
    out_ref, acc = refs[-2:]
    step = pl.program_id(0)
    rows, count = h2_ref.shape[0], sum_ref.shape[0]
    chunk = 80
    summed = jnp.zeros((count, TILE), f32)
    for k in range(rows // chunk):
        inner = mul(h2_ref[k * chunk : (k + 1) * chunk, :], wu_ref[...])
        value, _ = gelu_parts(inner)
        pool = pool_matrix(count, chunk, k * chunk, IMG_LEN)
        summed = summed + mul(pool, value.astype(bf16))
    mean = two_terms(summed * (1.0 / IMG_LEN))
    place = lax.broadcasted_iota(jnp.int32, (TILE, TILE // fold), 0)
    picked = lax.broadcasted_iota(jnp.int32, (TILE, TILE // fold), 1) * fold
    terms = jnp.zeros((2 * count, D), f32)
    for k in range(fold):
        chosen = jnp.where(place == picked + k, 1.0, 0.0).astype(bf16)
        part = mul(mean, chosen).astype(bf16)
        terms = terms + mul(part, wd_ref[:, k * D : (k + 1) * D])
    added = terms[:count] + terms[count:]

    @pl.when(step == 0)
    def _():
        acc[...] = sum_ref[...] * (1.0 / IMG_LEN) + added

    @pl.when(step > 0)
    def _():
        acc[...] += added

    @pl.when(step == pl.num_programs(0) - 1)
    def _():
        out_ref[...] = unit_rows(acc[...])[0].astype(bf16)


def image_up(normed2, whole, up_col, down_col, middle_sum, after=()):
    rows, count = normed2.shape[0], middle_sum.shape[0]
    fold = FF // D
    fixed = lambda shape: pl.BlockSpec(shape, lambda i: (0, 0))
    return pl.pallas_call(
        functools.partial(image_up_kernel, fold),
        grid=(FF // TILE,),
        out_shape=jax.ShapeDtypeStruct((count, D), bf16),
        in_specs=[
            fixed((rows, D)),
            pl.BlockSpec((D, TILE), lambda i: (0, up_col // TILE + i)),
            pl.BlockSpec((TILE // fold, fold * D), lambda i: (i, down_col // (fold * D))),
            fixed((count, D)),
        ]
        + anywhere(after),
        out_specs=fixed((count, D)),
        scratch_shapes=[pltpu.VMEM((count, D), f32)],
        compiler_params=params(),
        cost_estimate=cost(2 * rows * D * FF, 4 * D * FF, 15 * rows * FF),
        name="image_up",
    )(normed2, whole, whole, middle_sum, *after)


def loss_parts(text_rows, pos, image_all):
    similar = mul_bt(text_rows, image_all) * logit_scale
    shifted = jnp.exp(similar - logit_scale)
    alive = jnp.max(pos, axis=1, keepdims=True)
    row_sum = jnp.sum(shifted, axis=1, keepdims=True)
    row_count = jnp.maximum(jnp.sum(pos, axis=1, keepdims=True), 1.0)
    return similar, shifted, alive, row_sum, row_count


def sums_over_captions(text_rows, pos, image_all):
    similar, shifted, alive, row_sum, row_count = loss_parts(text_rows, pos, image_all)
    pos_similar = pos * similar
    cap_term = alive * (
        logit_scale + jnp.log(row_sum) - jnp.sum(pos_similar, axis=1, keepdims=True) / row_count
    )
    return (
        jnp.sum(alive * shifted, axis=0, keepdims=True),
        jnp.sum(pos, axis=0, keepdims=True),
        jnp.sum(pos_similar, axis=0, keepdims=True),
        jnp.sum(cap_term, axis=0, keepdims=True),
        jnp.sum(alive, axis=0, keepdims=True),
    )


def loss_from(sums):
    col_sum, col_count, col_pos, cap_total, live_total = sums
    img_term = logit_scale + jnp.log(col_sum) - col_pos / col_count
    return 0.5 * cap_total / live_total + 0.5 * jnp.mean(img_term, axis=1, keepdims=True)


def grad_of_unit(text_rows, pos, image_all, col_sum, col_count, live_total):
    _, shifted, alive, row_sum, row_count = loss_parts(text_rows, pos, image_all)
    cap_share, img_share = 0.5 / live_total, 0.5 / image_all.shape[0]
    grad_sims = alive * shifted * (cap_share / row_sum + img_share / col_sum) - pos * (
        cap_share / row_count + img_share / col_count
    )
    return mul(grad_sims.astype(bf16), image_all) * logit_scale


def turned(grad, unit):
    return grad - unit * jnp.sum(grad * unit, axis=-1, keepdims=True)


def loss_kernel(
    pack_ref, image_ref, own_ref, unit_ref, inv_ref, loss_ref, row_ref, low_ref, col_sum_ref,
    col_count_ref, live_ref
):
    image_all = image_ref[...]
    chunk = 256
    total = None
    for k in range(pack_ref.shape[0] // chunk):
        at = slice(k * chunk, (k + 1) * chunk)
        part = sums_over_captions(pack_ref[at, :D], pack_ref[at, D:].astype(f32), image_all)
        total = part if total is None else [a + b for a, b in zip(total, part)]
    loss_ref[...] = jnp.broadcast_to(loss_from(total), loss_ref.shape)
    col_sum, col_count, _, _, live_total = total
    col_sum_ref[...] = col_sum
    col_count_ref[...] = col_count
    live_ref[...] = jnp.broadcast_to(live_total, live_ref.shape)
    grad = grad_of_unit(
        own_ref[:, :D], own_ref[:, D:].astype(f32), image_all, col_sum, col_count, live_total
    )
    row = inv_ref[:, :1] * turned(grad, unit_ref[...]) * (1.0 / TXT_LEN)
    row_ref[...] = row
    low_ref[...] = row.astype(bf16)


def loss_and_rows(pack, image_all, own_pack, unit, inverse):
    images, count = image_all.shape[0], own_pack.shape[0]
    shapes = [(1, 128), (count, D), (count, D), (1, images), (1, images), (1, 128)]
    kinds = [f32, f32, bf16, f32, f32, f32]
    return pl.pallas_call(
        loss_kernel,
        out_shape=[jax.ShapeDtypeStruct(*item) for item in zip(shapes, kinds)],
        compiler_params=params(),
        cost_estimate=cost(2 * pack.shape[0] * images * D, 2 * pack.size, pack.shape[0] * images),
        name="loss_and_rows",
    )(pack, image_all, own_pack, unit, inverse)


def down_kernel(pack_ref, image_ref, col_sum_ref, col_count_ref, live_ref, hid_ref, *refs):
    step, out_ref = pl.program_id(0), refs[-1]
    text_rows = pack_ref[:, :D]
    grad = grad_of_unit(
        text_rows, pack_ref[:, D:].astype(f32), image_ref[...], col_sum_ref[...],
        col_count_ref[...], live_ref[:, :1]
    )
    rows = (turned(grad, text_rows.astype(f32)) * (1.0 / TXT_LEN)).astype(bf16)
    part = mul_at(hid_ref[...], rows)

    @pl.when(step == 0)
    def _():
        out_ref[...] = part

    @pl.when(step > 0)
    def _():
        out_ref[...] += part


def grad_of_down(pack, image_all, col_sum, col_count, live_total, hidden_cols, after):
    images, chunk = image_all.shape[0], 256
    fixed = lambda shape: pl.BlockSpec(shape, lambda i: (0, 0))
    per = hidden_cols.shape[1]
    return pl.pallas_call(
        down_kernel,
        grid=(pack.shape[0] // chunk,),
        out_shape=jax.ShapeDtypeStruct((per, D), f32),
        in_specs=[
            pl.BlockSpec((chunk, pack.shape[1]), lambda i: (i, 0)),
            fixed((images, D)), fixed((1, images)), fixed((1, images)), fixed((1, 128)),
            pl.BlockSpec((chunk, per), lambda i: (i, 0)),
        ]
        + anywhere(after),
        out_specs=fixed((per, D)),
        compiler_params=params(),
        cost_estimate=cost(4 * pack.shape[0] * images * D, 2 * pack.size, pack.shape[0] * images),
        name="grad_of_down",
    )(pack, image_all, col_sum, col_count, live_total, hidden_cols, *after)


def mlp_back_kernel(
    low_ref, wd_ref, slope_ref, wu_ref, lhs_ref, mid_ref, gain_ref, row_ref, keep_a, send_a, keep_b,
    send_b, out_ref, gain_out, bias_out, acc
):
    step = pl.program_id(0)
    count, rows = low_ref.shape[0], slope_ref.shape[0]
    half = D // 2
    hidden = mul_bt(low_ref[...], wd_ref[...])
    wide = jnp.broadcast_to(hidden[:, None, :], (count, TXT_LEN, TILE)).reshape(rows, TILE)
    inner = (wide * slope_ref[...].astype(f32)).astype(bf16)
    weight = mul(lhs_ref[0], inner).astype(bf16)

    @pl.when(step < pl.num_programs(0) // 2)
    def _():
        keep_a[...] = weight[:half]
        send_a[...] = weight[half:]

    @pl.when(step >= pl.num_programs(0) // 2)
    def _():
        keep_b[...] = weight[:half]
        send_b[...] = weight[half:]

    added = mul_bt(inner, wu_ref[...])

    @pl.when(step == 0)
    def _():
        acc[...] = added

    @pl.when(step > 0)
    def _():
        acc[...] += added

    @pl.when(step == pl.num_programs(0) - 1)
    def _():
        chunk = 128
        per = chunk // TXT_LEN
        gain = gain_ref[...]
        gain_out[...] = jnp.zeros_like(gain_out)
        bias_out[...] = jnp.zeros_like(bias_out)

        @pl.loop(0, rows // chunk)
        def _(k):
            at = pl.ds(pl.multiple_of(k * chunk, chunk), chunk)
            unit, scale = norm_parts(mid_ref[at, :])
            grad = acc[at, :]
            gain_out[...] += jnp.sum(grad * unit, axis=0, keepdims=True)
            bias_out[...] += jnp.sum(grad, axis=0, keepdims=True)
            row = row_ref[pl.ds(pl.multiple_of(k * per, per), per), :]
            row = jnp.broadcast_to(row[:, None, :], (per, TXT_LEN, D)).reshape(chunk, D)
            out_ref[at, :] = row + norm_back(unit, scale, gain, grad)


def mlp_back(grad_row, grad_low, weight_down, slope, weight_up, lhs, middle, gain):
    rows, count = slope.shape[0], grad_row.shape[0]
    steps = FF // TILE
    fixed = lambda shape: pl.BlockSpec(shape, lambda i: (0, 0))
    first = pl.BlockSpec((D // 2, TILE), lambda i: (0, jnp.minimum(i, steps // 2 - 1)))
    second = pl.BlockSpec((D // 2, TILE), lambda i: (0, jnp.maximum(i - steps // 2, 0)))
    part = jax.ShapeDtypeStruct((D // 2, FF // 2), bf16)
    line = jax.ShapeDtypeStruct((1, D), f32)
    return pl.pallas_call(
        mlp_back_kernel,
        grid=(steps,),
        out_shape=[part] * 4 + [jax.ShapeDtypeStruct((rows, D), f32), line, line],
        in_specs=[
            fixed((count, D)),
            pl.BlockSpec((TILE, D), lambda i: (i, 0)),
            pl.BlockSpec((rows, TILE), lambda i: (0, i)),
            pl.BlockSpec((D, TILE), lambda i: (0, i)),
            pl.BlockSpec((1, D, rows), lambda i: (i // (steps // 2), 0, 0)),
            fixed((rows, D)),
            fixed((1, D)),
            fixed((count, D)),
        ],
        out_specs=[first, first, second, second, fixed((rows, D)), fixed((1, D)), fixed((1, D))],
        scratch_shapes=[pltpu.VMEM((rows, D), f32)],
        compiler_params=params(),
        cost_estimate=cost(4 * rows * D * FF, 4 * D * FF + 2 * rows * FF + 2 * D * FF, rows * FF),
        name="mlp_back",
    )(grad_low, weight_down, slope, weight_up, lhs, middle, gain[None], grad_row)


def attention_back_kernel(grad_ref, wo_ref, qkv_ref, lse_ref, *refs):
    low_ref, out_ref = refs[-2:]
    chunk = grad_ref.shape[0]
    mask = same_sequence(chunk, 0, chunk, 0, TXT_LEN)
    low = grad_ref[...].astype(bf16)
    low_ref[...] = low
    grad_att = mul_bt(low, wo_ref[...]).astype(bf16)
    for pair in range(HEADS // 2):
        queries = qkv_ref[:, pair_cols(0, pair)] * bf16(HEAD ** (-0.5))
        keys = two_heads(qkv_ref[:, pair_cols(1, pair)])
        vals = two_heads(qkv_ref[:, pair_cols(2, pair)])
        grads = grad_att[:, pair_cols(0, pair)]
        scores, grad_probs = mul_bt(keys, queries), mul_bt(vals, grads)
        probs, grad_scores = [], []
        for k in range(2):
            at = slice(k * chunk, (k + 1) * chunk)
            head = 2 * pair + k
            shifted = scores[at] - lse_ref[head : head + 1, :]
            prob = jnp.where(mask, jnp.exp(jnp.where(mask, shifted, 0.0)), 0.0)
            along = jnp.sum(grad_probs[at] * prob, axis=0, keepdims=True)
            grad_scores.append((prob * (grad_probs[at] - along)).astype(bf16))
            probs.append(prob.astype(bf16))
        grad_q = mul_at(jnp.concatenate(grad_scores, axis=0), keys) * HEAD ** (-0.5)
        grad_k = mul(jnp.concatenate(grad_scores, axis=1), two_heads(queries))
        grad_v = mul(jnp.concatenate(probs, axis=1), two_heads(grads))
        out_ref[:, pair_cols(0, pair)] = grad_q.astype(bf16)
        out_ref[:, pair_cols(1, pair)] = grad_k.astype(bf16)
        out_ref[:, pair_cols(2, pair)] = grad_v.astype(bf16)


def attention_back(grad_middle, weight_out, project, log_sums, first, count, after=()):
    chunk = 128
    rows = count * chunk
    return pl.pallas_call(
        attention_back_kernel,
        grid=(count,),
        out_shape=[
            jax.ShapeDtypeStruct((rows, D), bf16),
            jax.ShapeDtypeStruct((rows, 3 * D), bf16),
        ],
        in_specs=[
            pl.BlockSpec((chunk, D), lambda i: (i + first, 0)),
            pl.BlockSpec((D, D), lambda i: (0, 0)),
            pl.BlockSpec((chunk, 3 * D), lambda i: (i + first, 0)),
            pl.BlockSpec((16, chunk), lambda i: (i + first, 0)),
        ]
        + anywhere(after),
        out_specs=[
            pl.BlockSpec((chunk, D), lambda i: (i, 0)),
            pl.BlockSpec((chunk, 3 * D), lambda i: (i, 0)),
        ],
        compiler_params=params(),
        cost_estimate=cost(10 * rows * D * D, 16 * rows * D + 2 * D * D, rows * 128 * HEADS),
        name="attention_back",
    )(grad_middle, weight_out, project, log_sums, *after)


def mul_rows(lhs, parts):
    total, row = 0.0, 0
    for part in parts:
        total = total + mul(lhs[:, row : row + part.shape[0]], part[...])
        row += part.shape[0]
    return total


def weight_back_kernel(counts, lhs_ref, *refs):
    step, half = pl.program_id(0), D // 2
    keep, send = refs[-2:]
    row = 0
    for k, count in enumerate(counts):
        parts = refs[row : row + count]
        row += count

        @pl.when(step == k if len(counts) > 1 else step >= 0)
        def _(parts=parts):
            weight = mul_rows(lhs_ref[0], parts).astype(bf16)
            keep[...] = weight[:half]
            send[...] = weight[half:]


def weight_back(lhs, first, groups, blocks, after=()):
    rows = lhs.shape[2]
    steps = 2
    many = len(groups) > 1
    given = [part for group in groups for part in group]
    return pl.pallas_call(
        functools.partial(weight_back_kernel, [len(group) for group in groups]),
        grid=(steps,),
        out_shape=[jax.ShapeDtypeStruct((D // 2, steps * D), bf16)] * 2,
        in_specs=[pl.BlockSpec((1, D, rows), lambda i: (first + (i if many else 0), 0, 0))]
        + [
            pl.BlockSpec((part.shape[0], D), lambda i, col=col: (0, col + (0 if many else i)))
            for group, col in zip(groups, blocks)
            for part in group
        ]
        + anywhere(after),
        out_specs=[pl.BlockSpec((D // 2, D), lambda i: (0, i))] * 2,
        compiler_params=params(),
        cost_estimate=cost(4 * rows * D * D, 4 * rows * D + 7 * D * D),
        name="weight_back",
    )(lhs, *given, *after)


def input_back_kernel(count, *refs):
    projs = refs[:count]
    w_ref, x_ref, gain_ref, mid_ref = refs[count : count + 4]
    out_ref, gain_out, bias_out, acc = refs[-4:]
    step = pl.program_id(0)
    rows, chunk = x_ref.shape[0], 128
    row = 0
    for part in projs:
        at = slice(row, row + part.shape[0])
        row += part.shape[0]
        added = mul_bt(part[...], w_ref[...])

        @pl.when(step == 0)
        def _(at=at, added=added):
            acc[at, :] = added

        @pl.when(step > 0)
        def _(at=at, added=added):
            acc[at, :] += added

    @pl.when(step == pl.num_programs(0) - 1)
    def _():
        gain = gain_ref[...]
        gain_out[...] = jnp.zeros_like(gain_out)
        bias_out[...] = jnp.zeros_like(bias_out)

        @pl.loop(0, rows // chunk)
        def _(k):
            at = pl.ds(pl.multiple_of(k * chunk, chunk), chunk)
            unit, scale = norm_parts(x_ref[at, :].astype(f32))
            grad = acc[at, :]
            gain_out[...] += jnp.sum(grad * unit, axis=0, keepdims=True)
            bias_out[...] += jnp.sum(grad, axis=0, keepdims=True)
            out_ref[at, :] = mid_ref[at, :] + norm_back(unit, scale, gain, grad)


def input_back(grad_projs, weight, rows_in, gain, grad_middle, after=()):
    rows = rows_in.shape[0]
    fixed = lambda shape: pl.BlockSpec(shape, lambda i: (0, 0))
    line = jax.ShapeDtypeStruct((1, D), f32)
    return pl.pallas_call(
        functools.partial(input_back_kernel, len(grad_projs)),
        grid=(3,),
        out_shape=[jax.ShapeDtypeStruct((rows, D), f32), line, line],
        in_specs=[pl.BlockSpec((part.shape[0], D), lambda i: (0, i)) for part in grad_projs]
        + [
            pl.BlockSpec((D, D), lambda i: (0, i)),
            fixed((rows, D)), fixed((1, D)), fixed((rows, D)),
        ]
        + anywhere(after),
        out_specs=[fixed((rows, D)), fixed((1, D)), fixed((1, D))],
        scratch_shapes=[pltpu.VMEM((rows, D), f32)],
        compiler_params=params(),
        cost_estimate=cost(6 * rows * D * D, 14 * rows * D + 6 * D * D),
        name="input_back",
    )(*grad_projs, weight, rows_in, gain[None], grad_middle, *after)


def local(
    images,
    captions,
    img_gain1,
    img_bias1,
    img_qkv,
    img_out,
    img_gain2,
    img_bias2,
    img_up,
    img_down,
    txt_gain1,
    txt_bias1,
    txt_qkv,
    txt_out,
    txt_gain2,
    txt_bias2,
    txt_up,
    txt_down,
    counts,
    matches,
):
    peers = lax.axis_size(AXIS)
    own = lax.axis_index(AXIS)
    per = D // peers
    img_local = counts.shape[0]
    cap_local = matches.shape[0]
    total_images = matches.shape[1]

    whole = lax.all_gather(
        jnp.concatenate([img_up.reshape(per, FF), img_down.reshape(per, FF)], axis=1),
        AXIS,
        axis=0,
        tiled=True,
    )
    small = peers == 32
    shard = jnp.concatenate([img_qkv.reshape(per, 3 * D), img_out.reshape(per, D)], axis=1)
    if small:
        line, perm = gathered_line(shard), row_order((1, 4, 2, 16, 8))
    else:
        line, perm = lax.all_gather(shard, AXIS, axis=0, tiled=True), jnp.eye(D, dtype=bf16)

    normed1, project, attended, middle, normed2, middle_sum, log_sums = text_front(
        captions, txt_gain1, txt_bias1, txt_qkv, txt_out, txt_gain2, txt_bias2
    )
    middle_sum, line = in_turn(middle_sum, line)
    beside, above = (swapped(line, 2), swapped(line, 4)) if small else (line, line)
    slope, hidden_sum, text_unit, inverse = text_up(
        normed2, txt_up, txt_down, middle_sum, (line,)
    )
    text_unit, (beside, above) = in_turn(text_unit, (beside, above))

    ends_at = jnp.cumsum(counts)
    slot_ids = lax.iota(jnp.int32, cap_local)
    owner = jnp.sum((ends_at[None, :] <= slot_ids[:, None]).astype(jnp.int32), axis=1)
    owner = owner + own * img_local
    live = slot_ids < ends_at[-1]
    columns = lax.iota(jnp.int32, total_images)
    positive = ((matches > 0) | (owner[:, None] == columns[None, :])) & live[:, None]

    own_pack = packed(text_unit, positive.astype(bf16), ())
    pieces = [line]
    if small:
        held = own_pack[None]
        first, second = diagonal(beside, above)
        held = joined(held, swapped(held, 16), 16)
        other, first, second = lax.optimization_barrier((swapped(held, 8), first, second))
        held = joined(held, other, 8)
        text_beside, text_above = swapped(held, 2), swapped(held, 4)
        pieces = [line, beside, above, first, second]
        pieces = pieces + [swapped(piece, 1) for piece in pieces]

    normed_img, middle_img = image_front(
        images, pieces, perm, img_gain1, img_bias1, img_gain2, img_bias2
    )
    if small:
        scaled_sum = (hidden_sum * inverse[:, :1]).astype(bf16)
        hidden_cols = lax.all_to_all(scaled_sum, AXIS, split_axis=1, concat_axis=0, tiled=True)
        normed_img, hidden_cols, text_beside, text_above = lax.optimization_barrier(
            (normed_img, hidden_cols, text_beside, text_above)
        )
        across = jnp.concatenate(diagonal(text_beside, text_above), axis=0)
        held = joined(joined(held, text_beside, 2), joined(text_above, across, 2), 4, 4)

    order_a, order_b, tail = stage_orders()
    matrix_a, matrix_b = row_order(order_a + tail[::-1]), row_order(order_b + tail[::-1])
    lhs_up = jnp.stack([placed(matrix_a, normed2), placed(matrix_b, normed2)])
    lhs_rest = jnp.stack(
        [placed(matrix_a, normed1), placed(matrix_b, normed1), placed(matrix_b, attended)]
    )
    if small:
        whole, lhs_up, lhs_rest, held = lax.optimization_barrier((whole, lhs_up, lhs_rest, held))
        other = swapped(held, 1)
    image_low = image_up(normed_img, whole, 0, FF, middle_img)
    if small:
        text_pack = joined(held, other, 1).reshape(-1, D + total_images)
    image_all = spread(image_low).reshape(total_images, D)

    if small:
        loss_value, grad_row, row_low, col_sum, col_count, live_total = loss_and_rows(
            text_pack, image_all, own_pack, text_unit, inverse
        )
        loss_value = loss_value[0, 0]
    else:
        text_low, pos = own_pack[:, :D], own_pack[:, D:].astype(f32)
        sums = lax.psum(sums_over_captions(text_low, pos, image_all), AXIS)
        loss_value = loss_from(sums)[0, 0]
        grad = grad_of_unit(text_low, pos, image_all, sums[0], sums[1], sums[4])
        grad_row = inverse[:, :1] * turned(grad, text_unit) * (1.0 / TXT_LEN)
        row_low = grad_row.astype(bf16)

    *up, grad_middle, gain_two, bias_two = mlp_back(
        grad_row, row_low, txt_down, slope, txt_up, lhs_up, middle, txt_gain2
    )
    stages = len(order_a)
    low_one, proj_one = attention_back(grad_middle, txt_out, project, log_sums, 0, 2)
    for stage in range(stages - 2):
        up = fold(hand_on(up, stage), (proj_one,))
    low_two, proj_two = attention_back(grad_middle, txt_out, project, log_sums, 2, 3, up)
    up = fold(hand_on(up, stages - 2), (proj_two,))
    projs, lows = (proj_one, proj_two), (low_one, low_two)
    rest_a = weight_back(lhs_rest, 0, [projs], [0], up)
    up = hand_on_last(fold_last(hand_on(up, stages - 1), rest_a[1:]))
    rest_b = weight_back(lhs_rest, 1, [projs, lows], [2, 0], up[:1])
    rest = [*rest_a, *rest_b]
    for stage in range(stages - 2):
        rest = fold(hand_on(rest, stage))
    caption_grad, gain_one, bias_one = input_back(
        projs, txt_qkv, captions, txt_gain1, grad_middle, rest[:1]
    )
    caption_grad, up = in_turn(caption_grad, up)
    rest = fold(hand_on(rest, stages - 2), (caption_grad,))
    norms = jnp.concatenate([gain_one, bias_one, gain_two, bias_two], axis=0)
    norms, rest = in_turn(norms, rest)
    rest = fold_last(hand_on(rest, stages - 1))
    if small:
        grad_down = grad_of_down(
            text_pack, image_all, col_sum, col_count, live_total, hidden_cols, rest[:1]
        )
    else:
        grad_down = lax.psum_scatter(
            mul_at(hidden_sum.astype(bf16), row_low), AXIS, scatter_dimension=0, tiled=True
        )
    grad_down, rest = in_turn(grad_down, hand_on_last(rest))
    up_share = sum_last(*up)
    rest_share = sum_last(*rest)
    norms = jnp.sum(spread(norms[None]), axis=0).reshape(4, D)
    return (
        loss_value,
        caption_grad,
        norms[0],
        norms[1],
        rest_share[:, : 3 * D].reshape(-1),
        rest_share[:, 3 * D :].reshape(-1),
        norms[2],
        norms[3],
        up_share.reshape(-1),
        grad_down.reshape(-1),
    )


def solution(mesh):
    split, flat, whole = P("blk", None), P("blk"), P()
    image_block = (whole, whole, flat, flat, whole, whole, flat, flat)
    return jax.shard_map(
        local,
        mesh=mesh,
        in_specs=(split, split) + image_block + (whole,) * 8 + (flat, split),
        out_specs=(whole, split, whole, whole, flat, flat, whole, whole, flat, flat),
        check_vma=False,
    )
```

```python
import functools

import jax
import jax.numpy as jnp
from jax import lax
from jax.experimental import pallas as pl
from jax.experimental.pallas import tpu as pltpu
from jax.sharding import PartitionSpec as P

D = 768
FF = 3072
HEAD = 64
HEADS = D // HEAD
IMG_LEN = 50
TXT_LEN = 16
AXIS = "blk"

norm_eps = 1e-06
logit_scale = 50.0
f32 = jnp.float32
bf16 = jnp.bfloat16


def swapped(value, mask):
    peers = lax.axis_size(AXIS)
    return lax.ppermute(value, AXIS, [(i, i ^ mask) for i in range(peers)])


def bit_masks():
    peers = lax.axis_size(AXIS)
    return [1 << k for k in range(peers.bit_length() - 1)]


def joined(held, other, mask, outer=None):
    upper = (lax.axis_index(AXIS) & mask) > 0
    first = jnp.where(upper, other, held)
    second = jnp.where(upper, held, other)
    outer = held.shape[0] if outer is None else outer
    parts = [part.reshape((outer, -1) + held.shape[1:]) for part in (first, second)]
    return jnp.stack(parts, axis=1).reshape((-1,) + held.shape[1:])


def spread(block):
    peers = lax.axis_size(AXIS)
    copies = jnp.broadcast_to(block[None], (peers,) + block.shape)
    return lax.all_to_all(copies, AXIS, split_axis=0, concat_axis=0, tiled=True)


def stage_orders():
    masks = bit_masks()
    head, tail = masks[:-2], masks[-2:]
    order_a = list(head)
    order_b = list(head)
    for k in range(1, len(head) - 1, 2):
        order_b[k], order_b[k + 1] = order_b[k + 1], order_b[k]
    return order_a, order_b, tail


def row_order(bits):
    peers = lax.axis_size(AXIS)
    own = lax.axis_index(AXIS)
    per = D // peers
    places = lax.iota(jnp.int32, D)
    block = places // per
    target = jnp.zeros_like(block) + own
    for k, mask in enumerate(bits):
        target = target ^ (((block >> (len(bits) - 1 - k)) & 1) * mask)
    source = target * per + places % per
    return (source[:, None] == lax.iota(jnp.int32, D)[None, :]).astype(bf16)


def gathered_line(shard):
    return jnp.concatenate([shard] + [swapped(shard, mask) for mask in (8, 16, 24)], axis=0)


def diagonal(beside, above):
    half = beside.shape[0] // 2
    return swapped(beside[:half], 4), swapped(above[half:], 2)


def in_turn(first, then):
    return lax.optimization_barrier((first, then))


def placed(order, values):
    return mul_bt(order, values).astype(bf16)


def hand_on(parts, stage):
    order_a, order_b, _ = stage_orders()
    keep_a, send_a, keep_b, send_b = parts
    return keep_a, swapped(send_a, order_a[stage]), keep_b, swapped(send_b, order_b[stage])


def hand_on_last(blocks):
    low, high = stage_orders()[2]
    own, *others = blocks
    return own, [swapped(block, mask) for block, mask in zip(others, (low, high, low | high))]


def sum_last(own, others):
    total = own
    for other in others:
        total = total + other.astype(f32)
    return total


VMEM_BYTES = 56 << 20
TILE = 512


def norm_parts(values):
    average = jnp.mean(values, axis=-1, keepdims=True)
    centred = values - average
    variance = jnp.mean(centred * centred, axis=-1, keepdims=True)
    scale = lax.rsqrt(variance + norm_eps)
    return centred * scale, scale


def norm_back(unit, scale, gain, grad):
    inner = grad * gain
    shift = jnp.mean(inner, axis=-1, keepdims=True)
    along = jnp.mean(inner * unit, axis=-1, keepdims=True)
    return scale * (inner - shift - unit * along)


def mul(lhs, rhs):
    return jnp.dot(lhs, rhs, preferred_element_type=f32)


def mul_bt(lhs, rhs):
    return lax.dot_general(lhs, rhs, (((1,), (1,)), ((), ())), preferred_element_type=f32)


def mul_at(lhs, rhs):
    return lax.dot_general(lhs, rhs, (((0,), (0,)), ((), ())), preferred_element_type=f32)


def params(**more):
    return pltpu.CompilerParams(vmem_limit_bytes=VMEM_BYTES, **more)


def cost(flops, moved, transcendentals=0):
    return pl.CostEstimate(flops=flops, bytes_accessed=moved, transcendentals=transcendentals)


def lane_halves(dtype):
    lane = lax.broadcasted_iota(jnp.int32, (1, 2 * HEAD), 1)
    low = jnp.where(lane < HEAD, 1.0, 0.0)
    return low.astype(dtype), (1.0 - low).astype(dtype)


def two_heads(pair):
    low, high = lane_halves(bf16)
    return jnp.concatenate([pair * low, pair * high], axis=0)


def same_sequence(rows, row0, cols, col0, seq_len):
    row = (lax.broadcasted_iota(jnp.int32, (rows, cols), 0) + row0) // seq_len
    col = (lax.broadcasted_iota(jnp.int32, (rows, cols), 1) + col0) // seq_len
    return row == col


def softmax_down(scores, mask):
    keys = mask.shape[0]
    parts, sums = [], []
    for k in range(2):
        part = jnp.where(mask, scores[k * keys : (k + 1) * keys], -1e30)
        most = jnp.max(part, axis=0, keepdims=True)
        raised = jnp.exp(part - most)
        total = jnp.sum(raised, axis=0, keepdims=True)
        parts.append(raised * (1.0 / total))
        sums.append(most + jnp.log(total))
    return parts, sums


def fold_kernel(keep_a, got_a, keep_b, got_b, *refs):
    outs = refs[-4:]
    half = outs[0].shape[0]
    for k, (kept, got) in enumerate(((keep_a, got_a), (keep_b, got_b))):
        for j in range(2):
            at = slice(j * half, (j + 1) * half)
            outs[2 * k + j][...] = (kept[at, :].astype(f32) + got[at, :].astype(f32)).astype(bf16)


def fold(parts, after=()):
    rows, cols = parts[0].shape
    if rows % 32:
        whole = [
            (kept.astype(f32) + got.astype(f32)).astype(bf16)
            for kept, got in (parts[:2], parts[2:])
        ]
        return [part for one in whole for part in (one[: rows // 2], one[rows // 2 :])]
    tile = 512
    return pl.pallas_call(
        fold_kernel,
        grid=(cols // tile,),
        out_shape=[jax.ShapeDtypeStruct((rows // 2, cols), bf16)] * 4,
        in_specs=[pl.BlockSpec((rows, tile), lambda i: (0, i))] * 4 + anywhere(after),
        out_specs=[pl.BlockSpec((rows // 2, tile), lambda i: (0, i))] * 4,
        compiler_params=params(),
        cost_estimate=cost(2 * rows * cols, 12 * rows * cols),
        name="fold",
    )(*parts, *after)


def fold_last_kernel(keep_a, got_a, keep_b, got_b, *refs):
    own_ref, *outs = refs[-4:]
    rows = own_ref.shape[0]
    cols = keep_a.shape[1]
    for k, (kept, got) in enumerate(((keep_a, got_a), (keep_b, got_b))):
        total = kept[...].astype(f32) + got[...].astype(f32)
        at = slice(k * cols, (k + 1) * cols)
        own_ref[:, at] = total[:rows]
        for j, out in enumerate(outs):
            out[:, at] = total[(j + 1) * rows : (j + 2) * rows].astype(bf16)


def fold_last(parts, after=()):
    rows, cols = parts[0].shape
    shape = (rows // 4, 2 * cols)
    if rows % 32:
        pairs = (parts[:2], parts[2:])
        both = [kept.astype(f32) + got.astype(f32) for kept, got in pairs]
        own, *others = jnp.split(jnp.concatenate(both, axis=1), 4)
        return [own] + [other.astype(bf16) for other in others]
    return pl.pallas_call(
        fold_last_kernel,
        out_shape=[jax.ShapeDtypeStruct(shape, f32)] + [jax.ShapeDtypeStruct(shape, bf16)] * 3,
        in_specs=[pl.BlockSpec(memory_space=pltpu.VMEM)] * 4 + anywhere(after),
        compiler_params=params(),
        cost_estimate=cost(2 * rows * cols, 12 * rows * cols),
        name="fold_last",
    )(*parts, *after)


def anywhere(after):
    return [pl.BlockSpec(memory_space=pl.ANY)] * len(after)


def pair_cols(part, pair):
    start = part * D + pair * 2 * HEAD
    return slice(start, start + 2 * HEAD)


def norm_rows(src, dst, gain, bias, step_rows):
    @pl.loop(0, src.shape[0] // step_rows)
    def _(step):
        at = pl.ds(pl.multiple_of(step * step_rows, step_rows), step_rows)
        unit, _ = norm_parts(src[at, :].astype(f32))
        dst[at, :] = (unit * gain + bias).astype(bf16)


def attend_along(qkv_ref, att_ref, q_rows, k_rows, mask):
    low, high = lane_halves(f32)
    for pair in range(HEADS // 2):
        queries = two_heads(qkv_ref[q_rows, pair_cols(0, pair)] * bf16(HEAD ** (-0.5)))
        scores = mul_bt(queries, qkv_ref[k_rows, pair_cols(1, pair)])
        scores = jnp.where(mask, scores, -1e30)
        raised = jnp.exp(scores - jnp.max(scores, axis=-1, keepdims=True))
        probs = (raised * (1.0 / jnp.sum(raised, axis=-1, keepdims=True))).astype(bf16)
        half = probs.shape[0] // 2
        mixed = mul(probs, qkv_ref[k_rows, pair_cols(2, pair)])
        att_ref[q_rows, pair_cols(0, pair)] = (mixed[:half] * low + mixed[half:] * high).astype(bf16)


def attend(qkv_ref, att_ref, q_rows, k_rows, mask, keep_sums):
    for pair in range(HEADS // 2):
        queries = qkv_ref[q_rows, pair_cols(0, pair)] * bf16(HEAD ** (-0.5))
        scores = mul_bt(two_heads(qkv_ref[k_rows, pair_cols(1, pair)]), queries)
        probs, sums = softmax_down(scores, mask)
        vals = two_heads(qkv_ref[k_rows, pair_cols(2, pair)])
        mixed = mul_at(jnp.concatenate(probs, axis=0).astype(bf16), vals)
        att_ref[q_rows, pair_cols(0, pair)] = mixed.astype(bf16)
        for k in range(2):
            keep_sums(2 * pair + k, sums[k])


def text_front_kernel(
    x_ref, g1_ref, b1_ref, wqkv_ref, wo_ref, g2_ref, b2_ref, h1_ref, qkv_ref, att_ref, mid_ref,
    h2_ref, sum_ref, lse_ref
):
    rows, chunk = x_ref.shape[0], 128
    norm_rows(x_ref, h1_ref, g1_ref[...], b1_ref[...], chunk)

    @pl.loop(0, 3 * D // 256)
    def _(step):
        at = pl.ds(pl.multiple_of(step * 256, 256), 256)
        qkv_ref[:, at] = mul(h1_ref[...], wqkv_ref[:, at]).astype(bf16)

    mask = same_sequence(chunk, 0, chunk, 0, TXT_LEN)

    @pl.loop(0, rows // chunk)
    def _(step):
        at = pl.ds(pl.multiple_of(step * chunk, chunk), chunk)

        def keep_sums(head, value):
            lse_ref[pl.ds(step * 16 + head, 1), :] = value

        attend(qkv_ref, att_ref, at, at, mask, keep_sums)

    @pl.loop(0, D // 256)
    def _(step):
        at = pl.ds(pl.multiple_of(step * 256, 256), 256)
        mid_ref[:, at] = x_ref[:, at].astype(f32) + mul(att_ref[...], wo_ref[:, at])

    norm_rows(mid_ref, h2_ref, g2_ref[...], b2_ref[...], chunk)
    per = chunk // TXT_LEN

    @pl.loop(0, rows // chunk)
    def _(step):
        values = mid_ref[pl.ds(pl.multiple_of(step * chunk, chunk), chunk), :]
        sum_ref[pl.ds(pl.multiple_of(step * per, per), per), :] = jnp.sum(
            values.reshape(per, TXT_LEN, D), axis=1
        )


def text_front(rows_in, gain1, bias1, wqkv, wo, gain2, bias2):
    rows = rows_in.shape[0]
    shapes = [
        ((rows, D), bf16),
        ((rows, 3 * D), bf16),
        ((rows, D), bf16),
        ((rows, D), f32),
        ((rows, D), bf16),
        ((rows // TXT_LEN, D), f32),
        ((rows // 128 * 16, 128), f32),
    ]
    return pl.pallas_call(
        text_front_kernel,
        out_shape=[jax.ShapeDtypeStruct(*item) for item in shapes],
        compiler_params=params(),
        cost_estimate=cost(rows * D * D * 8, 14 * D * rows + 8 * D * D, rows * 128 * HEADS),
        name="text_front",
    )(rows_in, gain1[None], bias1[None], wqkv, wo, gain2[None], bias2[None])


def image_front_kernel(
    windows, x_ref, perm_ref, g1_ref, b1_ref, g2_ref, b2_ref, *refs
):
    h2_ref, sum_ref, w_ref, h1_ref, placed_ref, qkv_ref, att_ref, mid_ref, sems = refs[-9:]
    rows, chunk = x_ref.shape[0], 80
    copies, row = [], 0
    for k, piece in enumerate(refs[:-9]):
        place = w_ref.at[pl.ds(row, piece.shape[0]), :]
        copies.append(pltpu.make_async_copy(piece, place, sems.at[k]))
        row += piece.shape[0]
    for copy in copies:
        copy.start()

    def place_columns(src, dst):
        @pl.loop(0, D // 256)
        def _(step):
            at = pl.ds(pl.multiple_of(step * 256, 256), 256)
            dst[:, at] = mul_bt(src[...], perm_ref[at, :]).astype(bf16)

    norm_rows(x_ref, h1_ref, g1_ref[...].astype(f32), b1_ref[...].astype(f32), chunk)
    place_columns(h1_ref, placed_ref)
    for copy in copies:
        copy.wait()

    @pl.loop(0, 3 * D // 256)
    def _(step):
        at = pl.ds(pl.multiple_of(step * 256, 256), 256)
        qkv_ref[:, at] = mul(placed_ref[...], w_ref[:, at]).astype(bf16)

    for row0, count, key0, keys in windows:
        one = same_sequence(count, row0, keys, key0, IMG_LEN)
        mask = jnp.concatenate([one, one], axis=0)
        attend_along(qkv_ref, att_ref, pl.ds(row0, count), pl.ds(key0, keys), mask)
    place_columns(att_ref, placed_ref)

    @pl.loop(0, D // 256)
    def _(step):
        at = pl.ds(pl.multiple_of(step * 256, 256), 256)
        there = pl.ds(pl.multiple_of(step * 256 + 3 * D, 256), 256)
        mid_ref[:, at] = x_ref[:, at].astype(f32) + mul(placed_ref[...], w_ref[:, there])

    norm_rows(mid_ref, h2_ref, g2_ref[...].astype(f32), b2_ref[...].astype(f32), chunk)
    for k in range(rows // IMG_LEN):
        first, last = k * IMG_LEN, (k + 1) * IMG_LEN
        start, end = first // 8 * 8, -(-last // 8) * 8
        values = mid_ref[start:end, :]
        place = lax.broadcasted_iota(jnp.int32, values.shape, 0) + start
        inside = (place >= first) & (place < last)
        sum_ref[k : k + 1, :] = jnp.sum(jnp.where(inside, values, 0.0), axis=0, keepdims=True)


def image_front(rows_in, pieces, perm, gain1, bias1, gain2, bias2):
    rows = rows_in.shape[0]
    windows = ((0, 208, 0, 256), (208, 192, 192, 208))
    vmem = pl.BlockSpec(memory_space=pltpu.VMEM)
    return pl.pallas_call(
        functools.partial(image_front_kernel, windows),
        out_shape=[
            jax.ShapeDtypeStruct((rows, D), bf16),
            jax.ShapeDtypeStruct((rows // IMG_LEN, D), f32),
        ],
        in_specs=[vmem] * 6 + anywhere(pieces),
        out_specs=[vmem] * 2,
        scratch_shapes=[
            pltpu.VMEM((D, 4 * D), bf16),
            pltpu.VMEM((rows, D), bf16),
            pltpu.VMEM((rows, D), bf16),
            pltpu.VMEM((rows, 3 * D), bf16),
            pltpu.VMEM((rows, D), bf16),
            pltpu.VMEM((rows, D), f32),
            pltpu.SemaphoreType.DMA((len(pieces),)),
        ],
        compiler_params=params(),
        cost_estimate=cost(rows * D * D * 12, 8 * D * D, rows * 256 * HEADS),
        name="image_front",
    )(rows_in, perm, gain1[None], bias1[None], gain2[None], bias2[None], *pieces)


def gelu_parts(inner):
    half = 0.5 * (1.0 + lax.erf(inner * (0.5**0.5)))
    return inner * half, half


def pack_kernel(unit_ref, pos_ref, *refs):
    refs[-1][:, :D] = unit_ref[...].astype(bf16)
    refs[-1][:, D:] = pos_ref[...]


def packed(unit, positive, after):
    shape = (unit.shape[0], D + positive.shape[1])
    return pl.pallas_call(
        pack_kernel,
        out_shape=jax.ShapeDtypeStruct(shape, bf16),
        in_specs=[pl.BlockSpec(memory_space=pltpu.VMEM)] * 2 + anywhere(after),
        compiler_params=params(),
        cost_estimate=cost(shape[0] * shape[1], 4 * shape[0] * shape[1]),
        name="packed",
    )(unit, positive, *after)


def pool_matrix(count, rows, row0, seq_len):
    row = (lax.broadcasted_iota(jnp.int32, (count, rows), 1) + row0) // seq_len
    return jnp.where(row == lax.broadcasted_iota(jnp.int32, (count, rows), 0), 1.0, 0.0).astype(bf16)


def two_terms(mean):
    high = mean.astype(bf16)
    low = (mean - high.astype(f32)).astype(bf16)
    return jnp.concatenate([high, low], axis=0)


def unit_rows(pooled):
    inverse = lax.rsqrt(jnp.sum(pooled * pooled, axis=-1, keepdims=True) + norm_eps)
    return pooled * inverse, inverse


def text_up_kernel(h2_ref, wu_ref, wd_ref, sum_ref, *refs):
    slope_ref, hid_ref, unit_ref, inv_ref, acc = refs[-5:]
    step = pl.program_id(0)
    chunk = 128
    per = chunk // TXT_LEN
    pool = pool_matrix(per, chunk, 0, TXT_LEN)
    for k in range(h2_ref.shape[0] // chunk):
        inner = mul(h2_ref[k * chunk : (k + 1) * chunk, :], wu_ref[...])
        value, half = gelu_parts(inner)
        slope = half + inner * (jnp.exp(-0.5 * inner * inner) * 0.3989422804014327)
        slope_ref[k * chunk : (k + 1) * chunk, :] = slope.astype(bf16)
        hid_ref[k * per : (k + 1) * per, :] = mul(pool, value.astype(bf16))
    terms = mul(two_terms(hid_ref[...] * (1.0 / TXT_LEN)), wd_ref[...])
    count = hid_ref.shape[0]
    added = terms[:count] + terms[count:]

    @pl.when(step == 0)
    def _():
        acc[...] = sum_ref[...] * (1.0 / TXT_LEN) + added

    @pl.when(step > 0)
    def _():
        acc[...] += added

    @pl.when(step == pl.num_programs(0) - 1)
    def _():
        unit, inverse = unit_rows(acc[...])
        unit_ref[...] = unit
        inv_ref[...] = jnp.broadcast_to(inverse, inv_ref.shape)


def text_up(normed2, weight_up, weight_down, middle_sum, after=()):
    rows, count = normed2.shape[0], middle_sum.shape[0]
    fixed = lambda shape: pl.BlockSpec(shape, lambda i: (0, 0))
    return pl.pallas_call(
        text_up_kernel,
        grid=(FF // TILE,),
        out_shape=[
            jax.ShapeDtypeStruct((rows, FF), bf16),
            jax.ShapeDtypeStruct((count, FF), f32),
            jax.ShapeDtypeStruct((count, D), f32),
            jax.ShapeDtypeStruct((count, 128), f32),
        ],
        in_specs=[
            fixed((rows, D)),
            pl.BlockSpec((D, TILE), lambda i: (0, i)),
            pl.BlockSpec((TILE, D), lambda i: (i, 0)),
            fixed((count, D)),
        ]
        + anywhere(after),
        out_specs=[
            pl.BlockSpec((rows, TILE), lambda i: (0, i)),
            pl.BlockSpec((count, TILE), lambda i: (0, i)),
            fixed((count, D)),
            fixed((count, 128)),
        ],
        scratch_shapes=[pltpu.VMEM((count, D), f32)],
        compiler_params=params(),
        cost_estimate=cost(2 * rows * D * FF, 4 * D * FF + 2 * rows * FF, 20 * rows * FF),
        name="text_up",
    )(normed2, weight_up, weight_down, middle_sum, *after)


def image_up_kernel(fold, h2_ref, wu_ref, wd_ref, sum_ref, *refs):
    out_ref, acc = refs[-2:]
    step = pl.program_id(0)
    rows, count = h2_ref.shape[0], sum_ref.shape[0]
    chunk = 80
    summed = jnp.zeros((count, TILE), f32)
    for k in range(rows // chunk):
        inner = mul(h2_ref[k * chunk : (k + 1) * chunk, :], wu_ref[...])
        value, _ = gelu_parts(inner)
        pool = pool_matrix(count, chunk, k * chunk, IMG_LEN)
        summed = summed + mul(pool, value.astype(bf16))
    mean = two_terms(summed * (1.0 / IMG_LEN))
    place = lax.broadcasted_iota(jnp.int32, (TILE, TILE // fold), 0)
    picked = lax.broadcasted_iota(jnp.int32, (TILE, TILE // fold), 1) * fold
    terms = jnp.zeros((2 * count, D), f32)
    for k in range(fold):
        chosen = jnp.where(place == picked + k, 1.0, 0.0).astype(bf16)
        part = mul(mean, chosen).astype(bf16)
        terms = terms + mul(part, wd_ref[:, k * D : (k + 1) * D])
    added = terms[:count] + terms[count:]

    @pl.when(step == 0)
    def _():
        acc[...] = sum_ref[...] * (1.0 / IMG_LEN) + added

    @pl.when(step > 0)
    def _():
        acc[...] += added

    @pl.when(step == pl.num_programs(0) - 1)
    def _():
        out_ref[...] = unit_rows(acc[...])[0].astype(bf16)


def image_up(normed2, whole, up_col, down_col, middle_sum, after=()):
    rows, count = normed2.shape[0], middle_sum.shape[0]
    fold = FF // D
    fixed = lambda shape: pl.BlockSpec(shape, lambda i: (0, 0))
    return pl.pallas_call(
        functools.partial(image_up_kernel, fold),
        grid=(FF // TILE,),
        out_shape=jax.ShapeDtypeStruct((count, D), bf16),
        in_specs=[
            fixed((rows, D)),
            pl.BlockSpec((D, TILE), lambda i: (0, up_col // TILE + i)),
            pl.BlockSpec((TILE // fold, fold * D), lambda i: (i, down_col // (fold * D))),
            fixed((count, D)),
        ]
        + anywhere(after),
        out_specs=fixed((count, D)),
        scratch_shapes=[pltpu.VMEM((count, D), f32)],
        compiler_params=params(),
        cost_estimate=cost(2 * rows * D * FF, 4 * D * FF, 15 * rows * FF),
        name="image_up",
    )(normed2, whole, whole, middle_sum, *after)


def loss_parts(text_rows, pos, image_all):
    similar = mul_bt(text_rows, image_all) * logit_scale
    shifted = jnp.exp(similar - logit_scale)
    alive = jnp.max(pos, axis=1, keepdims=True)
    row_sum = jnp.sum(shifted, axis=1, keepdims=True)
    row_count = jnp.maximum(jnp.sum(pos, axis=1, keepdims=True), 1.0)
    return similar, shifted, alive, row_sum, row_count


def sums_over_captions(text_rows, pos, image_all):
    similar, shifted, alive, row_sum, row_count = loss_parts(text_rows, pos, image_all)
    pos_similar = pos * similar
    cap_term = alive * (
        logit_scale + jnp.log(row_sum) - jnp.sum(pos_similar, axis=1, keepdims=True) / row_count
    )
    return (
        jnp.sum(alive * shifted, axis=0, keepdims=True),
        jnp.sum(pos, axis=0, keepdims=True),
        jnp.sum(pos_similar, axis=0, keepdims=True),
        jnp.sum(cap_term, axis=0, keepdims=True),
        jnp.sum(alive, axis=0, keepdims=True),
    )


def loss_from(sums):
    col_sum, col_count, col_pos, cap_total, live_total = sums
    img_term = logit_scale + jnp.log(col_sum) - col_pos / col_count
    return 0.5 * cap_total / live_total + 0.5 * jnp.mean(img_term, axis=1, keepdims=True)


def grad_of_unit(text_rows, pos, image_all, col_sum, col_count, live_total):
    _, shifted, alive, row_sum, row_count = loss_parts(text_rows, pos, image_all)
    cap_share, img_share = 0.5 / live_total, 0.5 / image_all.shape[0]
    grad_sims = alive * shifted * (cap_share / row_sum + img_share / col_sum) - pos * (
        cap_share / row_count + img_share / col_count
    )
    return mul(grad_sims.astype(bf16), image_all) * logit_scale


def turned(grad, unit):
    return grad - unit * jnp.sum(grad * unit, axis=-1, keepdims=True)


def loss_kernel(
    pack_ref, image_ref, own_ref, unit_ref, inv_ref, loss_ref, row_ref, low_ref, col_sum_ref,
    col_count_ref, live_ref
):
    image_all = image_ref[...]
    chunk = 256
    total = None
    for k in range(pack_ref.shape[0] // chunk):
        at = slice(k * chunk, (k + 1) * chunk)
        part = sums_over_captions(pack_ref[at, :D], pack_ref[at, D:].astype(f32), image_all)
        total = part if total is None else [a + b for a, b in zip(total, part)]
    loss_ref[...] = jnp.broadcast_to(loss_from(total), loss_ref.shape)
    col_sum, col_count, _, _, live_total = total
    col_sum_ref[...] = col_sum
    col_count_ref[...] = col_count
    live_ref[...] = jnp.broadcast_to(live_total, live_ref.shape)
    grad = grad_of_unit(
        own_ref[:, :D], own_ref[:, D:].astype(f32), image_all, col_sum, col_count, live_total
    )
    row = inv_ref[:, :1] * turned(grad, unit_ref[...]) * (1.0 / TXT_LEN)
    row_ref[...] = row
    low_ref[...] = row.astype(bf16)


def loss_and_rows(pack, image_all, own_pack, unit, inverse):
    images, count = image_all.shape[0], own_pack.shape[0]
    shapes = [(1, 128), (count, D), (count, D), (1, images), (1, images), (1, 128)]
    kinds = [f32, f32, bf16, f32, f32, f32]
    return pl.pallas_call(
        loss_kernel,
        out_shape=[jax.ShapeDtypeStruct(*item) for item in zip(shapes, kinds)],
        compiler_params=params(),
        cost_estimate=cost(2 * pack.shape[0] * images * D, 2 * pack.size, pack.shape[0] * images),
        name="loss_and_rows",
    )(pack, image_all, own_pack, unit, inverse)


def down_kernel(pack_ref, image_ref, col_sum_ref, col_count_ref, live_ref, hid_ref, *refs):
    step, out_ref = pl.program_id(0), refs[-1]
    text_rows = pack_ref[:, :D]
    grad = grad_of_unit(
        text_rows, pack_ref[:, D:].astype(f32), image_ref[...], col_sum_ref[...],
        col_count_ref[...], live_ref[:, :1]
    )
    rows = (turned(grad, text_rows.astype(f32)) * (1.0 / TXT_LEN)).astype(bf16)
    part = mul_at(hid_ref[...], rows)

    @pl.when(step == 0)
    def _():
        out_ref[...] = part

    @pl.when(step > 0)
    def _():
        out_ref[...] += part


def grad_of_down(pack, image_all, col_sum, col_count, live_total, hidden_cols, after):
    images, chunk = image_all.shape[0], 256
    fixed = lambda shape: pl.BlockSpec(shape, lambda i: (0, 0))
    per = hidden_cols.shape[1]
    return pl.pallas_call(
        down_kernel,
        grid=(pack.shape[0] // chunk,),
        out_shape=jax.ShapeDtypeStruct((per, D), f32),
        in_specs=[
            pl.BlockSpec((chunk, pack.shape[1]), lambda i: (i, 0)),
            fixed((images, D)), fixed((1, images)), fixed((1, images)), fixed((1, 128)),
            pl.BlockSpec((chunk, per), lambda i: (i, 0)),
        ]
        + anywhere(after),
        out_specs=fixed((per, D)),
        compiler_params=params(),
        cost_estimate=cost(4 * pack.shape[0] * images * D, 2 * pack.size, pack.shape[0] * images),
        name="grad_of_down",
    )(pack, image_all, col_sum, col_count, live_total, hidden_cols, *after)


def mlp_back_kernel(
    low_ref, wd_ref, slope_ref, wu_ref, lhs_ref, mid_ref, gain_ref, row_ref, keep_a, send_a, keep_b,
    send_b, out_ref, gain_out, bias_out, acc
):
    step = pl.program_id(0)
    count, rows = low_ref.shape[0], slope_ref.shape[0]
    half = D // 2
    hidden = mul_bt(low_ref[...], wd_ref[...])
    wide = jnp.broadcast_to(hidden[:, None, :], (count, TXT_LEN, TILE)).reshape(rows, TILE)
    inner = (wide * slope_ref[...].astype(f32)).astype(bf16)
    weight = mul(lhs_ref[0], inner).astype(bf16)

    @pl.when(step < pl.num_programs(0) // 2)
    def _():
        keep_a[...] = weight[:half]
        send_a[...] = weight[half:]

    @pl.when(step >= pl.num_programs(0) // 2)
    def _():
        keep_b[...] = weight[:half]
        send_b[...] = weight[half:]

    added = mul_bt(inner, wu_ref[...])

    @pl.when(step == 0)
    def _():
        acc[...] = added

    @pl.when(step > 0)
    def _():
        acc[...] += added

    @pl.when(step == pl.num_programs(0) - 1)
    def _():
        chunk = 128
        per = chunk // TXT_LEN
        gain = gain_ref[...]
        gain_out[...] = jnp.zeros_like(gain_out)
        bias_out[...] = jnp.zeros_like(bias_out)

        @pl.loop(0, rows // chunk)
        def _(k):
            at = pl.ds(pl.multiple_of(k * chunk, chunk), chunk)
            unit, scale = norm_parts(mid_ref[at, :])
            grad = acc[at, :]
            gain_out[...] += jnp.sum(grad * unit, axis=0, keepdims=True)
            bias_out[...] += jnp.sum(grad, axis=0, keepdims=True)
            row = row_ref[pl.ds(pl.multiple_of(k * per, per), per), :]
            row = jnp.broadcast_to(row[:, None, :], (per, TXT_LEN, D)).reshape(chunk, D)
            out_ref[at, :] = row + norm_back(unit, scale, gain, grad)


def mlp_back(grad_row, grad_low, weight_down, slope, weight_up, lhs, middle, gain):
    rows, count = slope.shape[0], grad_row.shape[0]
    steps = FF // TILE
    fixed = lambda shape: pl.BlockSpec(shape, lambda i: (0, 0))
    first = pl.BlockSpec((D // 2, TILE), lambda i: (0, jnp.minimum(i, steps // 2 - 1)))
    second = pl.BlockSpec((D // 2, TILE), lambda i: (0, jnp.maximum(i - steps // 2, 0)))
    part = jax.ShapeDtypeStruct((D // 2, FF // 2), bf16)
    line = jax.ShapeDtypeStruct((1, D), f32)
    return pl.pallas_call(
        mlp_back_kernel,
        grid=(steps,),
        out_shape=[part] * 4 + [jax.ShapeDtypeStruct((rows, D), f32), line, line],
        in_specs=[
            fixed((count, D)),
            pl.BlockSpec((TILE, D), lambda i: (i, 0)),
            pl.BlockSpec((rows, TILE), lambda i: (0, i)),
            pl.BlockSpec((D, TILE), lambda i: (0, i)),
            pl.BlockSpec((1, D, rows), lambda i: (i // (steps // 2), 0, 0)),
            fixed((rows, D)),
            fixed((1, D)),
            fixed((count, D)),
        ],
        out_specs=[first, first, second, second, fixed((rows, D)), fixed((1, D)), fixed((1, D))],
        scratch_shapes=[pltpu.VMEM((rows, D), f32)],
        compiler_params=params(),
        cost_estimate=cost(4 * rows * D * FF, 4 * D * FF + 2 * rows * FF + 2 * D * FF, rows * FF),
        name="mlp_back",
    )(grad_low, weight_down, slope, weight_up, lhs, middle, gain[None], grad_row)


def attention_back_kernel(grad_ref, wo_ref, qkv_ref, lse_ref, *refs):
    low_ref, out_ref = refs[-2:]
    chunk = grad_ref.shape[0]
    mask = same_sequence(chunk, 0, chunk, 0, TXT_LEN)
    low = grad_ref[...].astype(bf16)
    low_ref[...] = low
    grad_att = mul_bt(low, wo_ref[...]).astype(bf16)
    for pair in range(HEADS // 2):
        queries = qkv_ref[:, pair_cols(0, pair)] * bf16(HEAD ** (-0.5))
        keys = two_heads(qkv_ref[:, pair_cols(1, pair)])
        vals = two_heads(qkv_ref[:, pair_cols(2, pair)])
        grads = grad_att[:, pair_cols(0, pair)]
        scores, grad_probs = mul_bt(keys, queries), mul_bt(vals, grads)
        probs, grad_scores = [], []
        for k in range(2):
            at = slice(k * chunk, (k + 1) * chunk)
            head = 2 * pair + k
            shifted = scores[at] - lse_ref[head : head + 1, :]
            prob = jnp.where(mask, jnp.exp(jnp.where(mask, shifted, 0.0)), 0.0)
            along = jnp.sum(grad_probs[at] * prob, axis=0, keepdims=True)
            grad_scores.append((prob * (grad_probs[at] - along)).astype(bf16))
            probs.append(prob.astype(bf16))
        grad_q = mul_at(jnp.concatenate(grad_scores, axis=0), keys) * HEAD ** (-0.5)
        grad_k = mul(jnp.concatenate(grad_scores, axis=1), two_heads(queries))
        grad_v = mul(jnp.concatenate(probs, axis=1), two_heads(grads))
        out_ref[:, pair_cols(0, pair)] = grad_q.astype(bf16)
        out_ref[:, pair_cols(1, pair)] = grad_k.astype(bf16)
        out_ref[:, pair_cols(2, pair)] = grad_v.astype(bf16)


def attention_back(grad_middle, weight_out, project, log_sums, first, count, after=()):
    chunk = 128
    rows = count * chunk
    return pl.pallas_call(
        attention_back_kernel,
        grid=(count,),
        out_shape=[
            jax.ShapeDtypeStruct((rows, D), bf16),
            jax.ShapeDtypeStruct((rows, 3 * D), bf16),
        ],
        in_specs=[
            pl.BlockSpec((chunk, D), lambda i: (i + first, 0)),
            pl.BlockSpec((D, D), lambda i: (0, 0)),
            pl.BlockSpec((chunk, 3 * D), lambda i: (i + first, 0)),
            pl.BlockSpec((16, chunk), lambda i: (i + first, 0)),
        ]
        + anywhere(after),
        out_specs=[
            pl.BlockSpec((chunk, D), lambda i: (i, 0)),
            pl.BlockSpec((chunk, 3 * D), lambda i: (i, 0)),
        ],
        compiler_params=params(),
        cost_estimate=cost(10 * rows * D * D, 16 * rows * D + 2 * D * D, rows * 128 * HEADS),
        name="attention_back",
    )(grad_middle, weight_out, project, log_sums, *after)


def mul_rows(lhs, parts):
    total, row = 0.0, 0
    for part in parts:
        total = total + mul(lhs[:, row : row + part.shape[0]], part[...])
        row += part.shape[0]
    return total


def weight_back_kernel(counts, lhs_ref, *refs):
    step, half = pl.program_id(0), D // 2
    keep, send = refs[-2:]
    row = 0
    for k, count in enumerate(counts):
        parts = refs[row : row + count]
        row += count

        @pl.when(step == k if len(counts) > 1 else step >= 0)
        def _(parts=parts):
            weight = mul_rows(lhs_ref[0], parts).astype(bf16)
            keep[...] = weight[:half]
            send[...] = weight[half:]


def weight_back(lhs, first, groups, blocks, after=()):
    rows = lhs.shape[2]
    steps = 2
    many = len(groups) > 1
    given = [part for group in groups for part in group]
    return pl.pallas_call(
        functools.partial(weight_back_kernel, [len(group) for group in groups]),
        grid=(steps,),
        out_shape=[jax.ShapeDtypeStruct((D // 2, steps * D), bf16)] * 2,
        in_specs=[pl.BlockSpec((1, D, rows), lambda i: (first + (i if many else 0), 0, 0))]
        + [
            pl.BlockSpec((part.shape[0], D), lambda i, col=col: (0, col + (0 if many else i)))
            for group, col in zip(groups, blocks)
            for part in group
        ]
        + anywhere(after),
        out_specs=[pl.BlockSpec((D // 2, D), lambda i: (0, i))] * 2,
        compiler_params=params(),
        cost_estimate=cost(4 * rows * D * D, 4 * rows * D + 7 * D * D),
        name="weight_back",
    )(lhs, *given, *after)


def input_back_kernel(count, *refs):
    projs = refs[:count]
    w_ref, x_ref, gain_ref, mid_ref = refs[count : count + 4]
    out_ref, gain_out, bias_out, acc = refs[-4:]
    step = pl.program_id(0)
    rows, chunk = x_ref.shape[0], 128
    row = 0
    for part in projs:
        at = slice(row, row + part.shape[0])
        row += part.shape[0]
        added = mul_bt(part[...], w_ref[...])

        @pl.when(step == 0)
        def _(at=at, added=added):
            acc[at, :] = added

        @pl.when(step > 0)
        def _(at=at, added=added):
            acc[at, :] += added

    @pl.when(step == pl.num_programs(0) - 1)
    def _():
        gain = gain_ref[...]
        gain_out[...] = jnp.zeros_like(gain_out)
        bias_out[...] = jnp.zeros_like(bias_out)

        @pl.loop(0, rows // chunk)
        def _(k):
            at = pl.ds(pl.multiple_of(k * chunk, chunk), chunk)
            unit, scale = norm_parts(x_ref[at, :].astype(f32))
            grad = acc[at, :]
            gain_out[...] += jnp.sum(grad * unit, axis=0, keepdims=True)
            bias_out[...] += jnp.sum(grad, axis=0, keepdims=True)
            out_ref[at, :] = mid_ref[at, :] + norm_back(unit, scale, gain, grad)


def input_back(grad_projs, weight, rows_in, gain, grad_middle, after=()):
    rows = rows_in.shape[0]
    fixed = lambda shape: pl.BlockSpec(shape, lambda i: (0, 0))
    line = jax.ShapeDtypeStruct((1, D), f32)
    return pl.pallas_call(
        functools.partial(input_back_kernel, len(grad_projs)),
        grid=(3,),
        out_shape=[jax.ShapeDtypeStruct((rows, D), f32), line, line],
        in_specs=[pl.BlockSpec((part.shape[0], D), lambda i: (0, i)) for part in grad_projs]
        + [
            pl.BlockSpec((D, D), lambda i: (0, i)),
            fixed((rows, D)), fixed((1, D)), fixed((rows, D)),
        ]
        + anywhere(after),
        out_specs=[fixed((rows, D)), fixed((1, D)), fixed((1, D))],
        scratch_shapes=[pltpu.VMEM((rows, D), f32)],
        compiler_params=params(),
        cost_estimate=cost(6 * rows * D * D, 14 * rows * D + 6 * D * D),
        name="input_back",
    )(*grad_projs, weight, rows_in, gain[None], grad_middle, *after)


def local(
    images,
    captions,
    img_gain1,
    img_bias1,
    img_qkv,
    img_out,
    img_gain2,
    img_bias2,
    img_up,
    img_down,
    txt_gain1,
    txt_bias1,
    txt_qkv,
    txt_out,
    txt_gain2,
    txt_bias2,
    txt_up,
    txt_down,
    counts,
    matches,
):
    peers = lax.axis_size(AXIS)
    own = lax.axis_index(AXIS)
    per = D // peers
    img_local = counts.shape[0]
    cap_local = matches.shape[0]
    total_images = matches.shape[1]

    whole = lax.all_gather(
        jnp.concatenate([img_up.reshape(per, FF), img_down.reshape(per, FF)], axis=1),
        AXIS,
        axis=0,
        tiled=True,
    )
    small = peers == 32
    shard = jnp.concatenate([img_qkv.reshape(per, 3 * D), img_out.reshape(per, D)], axis=1)
    if small:
        line, perm = gathered_line(shard), row_order((1, 4, 2, 16, 8))
    else:
        line, perm = lax.all_gather(shard, AXIS, axis=0, tiled=True), jnp.eye(D, dtype=bf16)

    normed1, project, attended, middle, normed2, middle_sum, log_sums = text_front(
        captions, txt_gain1, txt_bias1, txt_qkv, txt_out, txt_gain2, txt_bias2
    )
    middle_sum, line = in_turn(middle_sum, line)
    beside, above = (swapped(line, 2), swapped(line, 4)) if small else (line, line)
    slope, hidden_sum, text_unit, inverse = text_up(
        normed2, txt_up, txt_down, middle_sum, (line,)
    )
    text_unit, (beside, above) = in_turn(text_unit, (beside, above))

    ends_at = jnp.cumsum(counts)
    slot_ids = lax.iota(jnp.int32, cap_local)
    owner = jnp.sum((ends_at[None, :] <= slot_ids[:, None]).astype(jnp.int32), axis=1)
    owner = owner + own * img_local
    live = slot_ids < ends_at[-1]
    columns = lax.iota(jnp.int32, total_images)
    positive = ((matches > 0) | (owner[:, None] == columns[None, :])) & live[:, None]

    own_pack = packed(text_unit, positive.astype(bf16), ())
    pieces = [line]
    if small:
        held = own_pack[None]
        first, second = diagonal(beside, above)
        others = [swapped(held, mask) for mask in (8, 16, 24)]
        others, first, second = lax.optimization_barrier((others, first, second))
        held = joined(joined(held, others[0], 8), joined(others[1], others[2], 8), 16, 1)
        text_beside, text_above = swapped(held, 2), swapped(held, 4)
        pieces = [line, beside, above, first, second]
        pieces = pieces + [swapped(piece, 1) for piece in pieces]

    normed_img, middle_img = image_front(
        images, pieces, perm, img_gain1, img_bias1, img_gain2, img_bias2
    )
    if small:
        scaled_sum = (hidden_sum * inverse[:, :1]).astype(bf16)
        normed_img, scaled_sum, text_beside, text_above = lax.optimization_barrier(
            (normed_img, scaled_sum, text_beside, text_above)
        )
        hidden_cols = lax.all_to_all(scaled_sum, AXIS, split_axis=1, concat_axis=0, tiled=True)
        across = jnp.concatenate(diagonal(text_beside, text_above), axis=0)
        held = joined(joined(held, text_beside, 2), joined(text_above, across, 2), 4, 4)

    order_a, order_b, tail = stage_orders()
    matrix_a, matrix_b = row_order(order_a + tail[::-1]), row_order(order_b + tail[::-1])
    lhs_up = jnp.stack([placed(matrix_a, normed2), placed(matrix_b, normed2)])
    lhs_rest = jnp.stack(
        [placed(matrix_a, normed1), placed(matrix_b, normed1), placed(matrix_b, attended)]
    )
    if small:
        whole, lhs_up, lhs_rest, held = lax.optimization_barrier((whole, lhs_up, lhs_rest, held))
        other = swapped(held, 1)
    image_low = image_up(normed_img, whole, 0, FF, middle_img)
    if small:
        image_low, hidden_cols = in_turn(image_low, hidden_cols)
        text_pack = joined(held, other, 1).reshape(-1, D + total_images)
    image_all = spread(image_low).reshape(total_images, D)

    if small:
        loss_value, grad_row, row_low, col_sum, col_count, live_total = loss_and_rows(
            text_pack, image_all, own_pack, text_unit, inverse
        )
        loss_value = loss_value[0, 0]
    else:
        text_low, pos = own_pack[:, :D], own_pack[:, D:].astype(f32)
        sums = lax.psum(sums_over_captions(text_low, pos, image_all), AXIS)
        loss_value = loss_from(sums)[0, 0]
        grad = grad_of_unit(text_low, pos, image_all, sums[0], sums[1], sums[4])
        grad_row = inverse[:, :1] * turned(grad, text_unit) * (1.0 / TXT_LEN)
        row_low = grad_row.astype(bf16)

    *up, grad_middle, gain_two, bias_two = mlp_back(
        grad_row, row_low, txt_down, slope, txt_up, lhs_up, middle, txt_gain2
    )
    stages = len(order_a)
    low_one, proj_one = attention_back(grad_middle, txt_out, project, log_sums, 0, 2)
    for stage in range(stages - 2):
        up = fold(hand_on(up, stage), (proj_one,))
    low_two, proj_two = attention_back(grad_middle, txt_out, project, log_sums, 2, 3, up)
    up = fold(hand_on(up, stages - 2), (proj_two,))
    projs, lows = (proj_one, proj_two), (low_one, low_two)
    rest_a = weight_back(lhs_rest, 0, [projs], [0], up)
    up = hand_on_last(fold_last(hand_on(up, stages - 1), rest_a[1:]))
    rest_b = weight_back(lhs_rest, 1, [projs, lows], [2, 0], up[:1])
    rest = [*rest_a, *rest_b]
    for stage in range(stages - 2):
        rest = fold(hand_on(rest, stage))
    caption_grad, gain_one, bias_one = input_back(
        projs, txt_qkv, captions, txt_gain1, grad_middle, rest[:1]
    )
    caption_grad, up = in_turn(caption_grad, up)
    rest = fold(hand_on(rest, stages - 2), (caption_grad,))
    norms = jnp.concatenate([gain_one, bias_one, gain_two, bias_two], axis=0)
    norms, rest = in_turn(norms, rest)
    norms = jnp.sum(spread(norms[None]), axis=0).reshape(4, D)
    rest = fold_last(hand_on(rest, stages - 1))
    if small:
        grad_down = grad_of_down(
            text_pack, image_all, col_sum, col_count, live_total, hidden_cols, (rest[0], norms)
        )
    else:
        grad_down = lax.psum_scatter(
            mul_at(hidden_sum.astype(bf16), row_low), AXIS, scatter_dimension=0, tiled=True
        )
    grad_down, rest = in_turn(grad_down, hand_on_last(rest))
    up_share = sum_last(*up)
    rest_share = sum_last(*rest)
    return (
        loss_value,
        caption_grad,
        norms[0],
        norms[1],
        rest_share[:, : 3 * D].reshape(-1),
        rest_share[:, 3 * D :].reshape(-1),
        norms[2],
        norms[3],
        up_share.reshape(-1),
        grad_down.reshape(-1),
    )


def solution(mesh):
    split, flat, whole = P("blk", None), P("blk"), P()
    image_block = (whole, whole, flat, flat, whole, whole, flat, flat)
    return jax.shard_map(
        local,
        mesh=mesh,
        in_specs=(split, split) + image_block + (whole,) * 8 + (flat, split),
        out_specs=(whole, split, whole, whole, flat, flat, whole, whole, flat, flat),
        check_vma=False,
    )
```

```python
import functools

import jax
import jax.numpy as jnp
from jax import lax
from jax.experimental import pallas as pl
from jax.experimental.pallas import tpu as pltpu
from jax.sharding import PartitionSpec as P

D = 768
FF = 3072
HEAD = 64
HEADS = D // HEAD
IMG_LEN = 50
TXT_LEN = 16
AXIS = "blk"

norm_eps = 1e-06
logit_scale = 50.0
f32 = jnp.float32
bf16 = jnp.bfloat16


def swapped(value, mask):
    peers = lax.axis_size(AXIS)
    return lax.ppermute(value, AXIS, [(i, i ^ mask) for i in range(peers)])


def bit_masks():
    peers = lax.axis_size(AXIS)
    return [1 << k for k in range(peers.bit_length() - 1)]


def joined(held, other, mask, outer=None):
    upper = (lax.axis_index(AXIS) & mask) > 0
    first = jnp.where(upper, other, held)
    second = jnp.where(upper, held, other)
    outer = held.shape[0] if outer is None else outer
    parts = [part.reshape((outer, -1) + held.shape[1:]) for part in (first, second)]
    return jnp.stack(parts, axis=1).reshape((-1,) + held.shape[1:])


def spread(block):
    peers = lax.axis_size(AXIS)
    copies = jnp.broadcast_to(block[None], (peers,) + block.shape)
    return lax.all_to_all(copies, AXIS, split_axis=0, concat_axis=0, tiled=True)


def stage_orders():
    masks = bit_masks()
    head, tail = masks[:-2], masks[-2:]
    order_a = list(head)
    order_b = list(head)
    for k in range(1, len(head) - 1, 2):
        order_b[k], order_b[k + 1] = order_b[k + 1], order_b[k]
    return order_a, order_b, tail


def row_order(bits):
    peers = lax.axis_size(AXIS)
    own = lax.axis_index(AXIS)
    per = D // peers
    places = lax.iota(jnp.int32, D)
    block = places // per
    target = jnp.zeros_like(block) + own
    for k, mask in enumerate(bits):
        target = target ^ (((block >> (len(bits) - 1 - k)) & 1) * mask)
    source = target * per + places % per
    return (source[:, None] == lax.iota(jnp.int32, D)[None, :]).astype(bf16)


def gathered_line(shard):
    return jnp.concatenate([shard] + [swapped(shard, mask) for mask in (8, 16, 24)], axis=0)


def diagonal(beside, above):
    half = beside.shape[0] // 2
    return swapped(beside[:half], 4), swapped(above[half:], 2)


def in_turn(first, then):
    return lax.optimization_barrier((first, then))


def placed(order, values):
    return mul_bt(order, values).astype(bf16)


def hand_on(parts, stage):
    order_a, order_b, _ = stage_orders()
    keep_a, send_a, keep_b, send_b = parts
    return keep_a, swapped(send_a, order_a[stage]), keep_b, swapped(send_b, order_b[stage])


def hand_on_last(blocks):
    low, high = stage_orders()[2]
    own, *others = blocks
    return own, [swapped(block, mask) for block, mask in zip(others, (low, high, low | high))]


def sum_last(own, others):
    total = own
    for other in others:
        total = total + other.astype(f32)
    return total


VMEM_BYTES = 56 << 20
TILE = 512


def norm_parts(values):
    average = jnp.mean(values, axis=-1, keepdims=True)
    centred = values - average
    variance = jnp.mean(centred * centred, axis=-1, keepdims=True)
    scale = lax.rsqrt(variance + norm_eps)
    return centred * scale, scale


def norm_back(unit, scale, gain, grad):
    inner = grad * gain
    shift = jnp.mean(inner, axis=-1, keepdims=True)
    along = jnp.mean(inner * unit, axis=-1, keepdims=True)
    return scale * (inner - shift - unit * along)


def mul(lhs, rhs):
    return jnp.dot(lhs, rhs, preferred_element_type=f32)


def mul_bt(lhs, rhs):
    return lax.dot_general(lhs, rhs, (((1,), (1,)), ((), ())), preferred_element_type=f32)


def mul_at(lhs, rhs):
    return lax.dot_general(lhs, rhs, (((0,), (0,)), ((), ())), preferred_element_type=f32)


def params(**more):
    return pltpu.CompilerParams(vmem_limit_bytes=VMEM_BYTES, **more)


def cost(flops, moved, transcendentals=0):
    return pl.CostEstimate(flops=flops, bytes_accessed=moved, transcendentals=transcendentals)


def lane_halves(dtype):
    lane = lax.broadcasted_iota(jnp.int32, (1, 2 * HEAD), 1)
    low = jnp.where(lane < HEAD, 1.0, 0.0)
    return low.astype(dtype), (1.0 - low).astype(dtype)


def two_heads(pair):
    low, high = lane_halves(bf16)
    return jnp.concatenate([pair * low, pair * high], axis=0)


def same_sequence(rows, row0, cols, col0, seq_len):
    row = (lax.broadcasted_iota(jnp.int32, (rows, cols), 0) + row0) // seq_len
    col = (lax.broadcasted_iota(jnp.int32, (rows, cols), 1) + col0) // seq_len
    return row == col


def softmax_down(scores, mask):
    keys = mask.shape[0]
    parts, sums = [], []
    for k in range(2):
        part = jnp.where(mask, scores[k * keys : (k + 1) * keys], -1e30)
        most = jnp.max(part, axis=0, keepdims=True)
        raised = jnp.exp(part - most)
        total = jnp.sum(raised, axis=0, keepdims=True)
        parts.append(raised * (1.0 / total))
        sums.append(most + jnp.log(total))
    return parts, sums


def fold_kernel(keep_a, got_a, keep_b, got_b, *refs):
    outs = refs[-4:]
    half = outs[0].shape[0]
    for k, (kept, got) in enumerate(((keep_a, got_a), (keep_b, got_b))):
        for j in range(2):
            at = slice(j * half, (j + 1) * half)
            outs[2 * k + j][...] = (kept[at, :].astype(f32) + got[at, :].astype(f32)).astype(bf16)


def fold(parts, after=()):
    rows, cols = parts[0].shape
    if rows % 32:
        whole = [
            (kept.astype(f32) + got.astype(f32)).astype(bf16)
            for kept, got in (parts[:2], parts[2:])
        ]
        return [part for one in whole for part in (one[: rows // 2], one[rows // 2 :])]
    tile = 512
    return pl.pallas_call(
        fold_kernel,
        grid=(cols // tile,),
        out_shape=[jax.ShapeDtypeStruct((rows // 2, cols), bf16)] * 4,
        in_specs=[pl.BlockSpec((rows, tile), lambda i: (0, i))] * 4 + anywhere(after),
        out_specs=[pl.BlockSpec((rows // 2, tile), lambda i: (0, i))] * 4,
        compiler_params=params(),
        cost_estimate=cost(2 * rows * cols, 12 * rows * cols),
        name="fold",
    )(*parts, *after)


def fold_last_kernel(keep_a, got_a, keep_b, got_b, *refs):
    own_ref, *outs = refs[-4:]
    rows = own_ref.shape[0]
    cols = keep_a.shape[1]
    for k, (kept, got) in enumerate(((keep_a, got_a), (keep_b, got_b))):
        total = kept[...].astype(f32) + got[...].astype(f32)
        at = slice(k * cols, (k + 1) * cols)
        own_ref[:, at] = total[:rows]
        for j, out in enumerate(outs):
            out[:, at] = total[(j + 1) * rows : (j + 2) * rows].astype(bf16)


def fold_last(parts, after=()):
    rows, cols = parts[0].shape
    shape = (rows // 4, 2 * cols)
    if rows % 32:
        pairs = (parts[:2], parts[2:])
        both = [kept.astype(f32) + got.astype(f32) for kept, got in pairs]
        own, *others = jnp.split(jnp.concatenate(both, axis=1), 4)
        return [own] + [other.astype(bf16) for other in others]
    return pl.pallas_call(
        fold_last_kernel,
        out_shape=[jax.ShapeDtypeStruct(shape, f32)] + [jax.ShapeDtypeStruct(shape, bf16)] * 3,
        in_specs=[pl.BlockSpec(memory_space=pltpu.VMEM)] * 4 + anywhere(after),
        compiler_params=params(),
        cost_estimate=cost(2 * rows * cols, 12 * rows * cols),
        name="fold_last",
    )(*parts, *after)


def anywhere(after):
    return [pl.BlockSpec(memory_space=pl.ANY)] * len(after)


def pair_cols(part, pair):
    start = part * D + pair * 2 * HEAD
    return slice(start, start + 2 * HEAD)


def norm_rows(src, dst, gain, bias, step_rows):
    @pl.loop(0, src.shape[0] // step_rows)
    def _(step):
        at = pl.ds(pl.multiple_of(step * step_rows, step_rows), step_rows)
        unit, _ = norm_parts(src[at, :].astype(f32))
        dst[at, :] = (unit * gain + bias).astype(bf16)


def attend_along(qkv_ref, att_ref, q_rows, k_rows, mask):
    low, high = lane_halves(f32)
    for pair in range(HEADS // 2):
        queries = two_heads(qkv_ref[q_rows, pair_cols(0, pair)] * bf16(HEAD ** (-0.5)))
        scores = mul_bt(queries, qkv_ref[k_rows, pair_cols(1, pair)])
        scores = jnp.where(mask, scores, -1e30)
        raised = jnp.exp(scores - jnp.max(scores, axis=-1, keepdims=True))
        probs = (raised * (1.0 / jnp.sum(raised, axis=-1, keepdims=True))).astype(bf16)
        half = probs.shape[0] // 2
        mixed = mul(probs, qkv_ref[k_rows, pair_cols(2, pair)])
        att_ref[q_rows, pair_cols(0, pair)] = (mixed[:half] * low + mixed[half:] * high).astype(bf16)


def attend(qkv_ref, att_ref, q_rows, k_rows, mask, keep_sums):
    for pair in range(HEADS // 2):
        queries = qkv_ref[q_rows, pair_cols(0, pair)] * bf16(HEAD ** (-0.5))
        scores = mul_bt(two_heads(qkv_ref[k_rows, pair_cols(1, pair)]), queries)
        probs, sums = softmax_down(scores, mask)
        vals = two_heads(qkv_ref[k_rows, pair_cols(2, pair)])
        mixed = mul_at(jnp.concatenate(probs, axis=0).astype(bf16), vals)
        att_ref[q_rows, pair_cols(0, pair)] = mixed.astype(bf16)
        for k in range(2):
            keep_sums(2 * pair + k, sums[k])


def text_front_kernel(
    x_ref, g1_ref, b1_ref, wqkv_ref, wo_ref, g2_ref, b2_ref, h1_ref, qkv_ref, att_ref, mid_ref,
    h2_ref, sum_ref, lse_ref
):
    rows, chunk = x_ref.shape[0], 128
    norm_rows(x_ref, h1_ref, g1_ref[...], b1_ref[...], chunk)

    @pl.loop(0, 3 * D // 256)
    def _(step):
        at = pl.ds(pl.multiple_of(step * 256, 256), 256)
        qkv_ref[:, at] = mul(h1_ref[...], wqkv_ref[:, at]).astype(bf16)

    mask = same_sequence(chunk, 0, chunk, 0, TXT_LEN)

    @pl.loop(0, rows // chunk)
    def _(step):
        at = pl.ds(pl.multiple_of(step * chunk, chunk), chunk)

        def keep_sums(head, value):
            lse_ref[pl.ds(step * 16 + head, 1), :] = value

        attend(qkv_ref, att_ref, at, at, mask, keep_sums)

    @pl.loop(0, D // 256)
    def _(step):
        at = pl.ds(pl.multiple_of(step * 256, 256), 256)
        mid_ref[:, at] = x_ref[:, at].astype(f32) + mul(att_ref[...], wo_ref[:, at])

    norm_rows(mid_ref, h2_ref, g2_ref[...], b2_ref[...], chunk)
    per = chunk // TXT_LEN

    @pl.loop(0, rows // chunk)
    def _(step):
        values = mid_ref[pl.ds(pl.multiple_of(step * chunk, chunk), chunk), :]
        sum_ref[pl.ds(pl.multiple_of(step * per, per), per), :] = jnp.sum(
            values.reshape(per, TXT_LEN, D), axis=1
        )


def text_front(rows_in, gain1, bias1, wqkv, wo, gain2, bias2):
    rows = rows_in.shape[0]
    shapes = [
        ((rows, D), bf16),
        ((rows, 3 * D), bf16),
        ((rows, D), bf16),
        ((rows, D), f32),
        ((rows, D), bf16),
        ((rows // TXT_LEN, D), f32),
        ((rows // 128 * 16, 128), f32),
    ]
    return pl.pallas_call(
        text_front_kernel,
        out_shape=[jax.ShapeDtypeStruct(*item) for item in shapes],
        compiler_params=params(),
        cost_estimate=cost(rows * D * D * 8, 14 * D * rows + 8 * D * D, rows * 128 * HEADS),
        name="text_front",
    )(rows_in, gain1[None], bias1[None], wqkv, wo, gain2[None], bias2[None])


def image_front_kernel(
    windows, x_ref, perm_ref, g1_ref, b1_ref, g2_ref, b2_ref, *refs
):
    h2_ref, sum_ref, w_ref, h1_ref, placed_ref, qkv_ref, att_ref, mid_ref, sems = refs[-9:]
    rows, chunk = x_ref.shape[0], 80
    copies, row = [], 0
    for k, piece in enumerate(refs[:-9]):
        place = w_ref.at[pl.ds(row, piece.shape[0]), :]
        copies.append(pltpu.make_async_copy(piece, place, sems.at[k]))
        row += piece.shape[0]
    for copy in copies:
        copy.start()

    def place_columns(src, dst):
        @pl.loop(0, D // 256)
        def _(step):
            at = pl.ds(pl.multiple_of(step * 256, 256), 256)
            dst[:, at] = mul_bt(src[...], perm_ref[at, :]).astype(bf16)

    norm_rows(x_ref, h1_ref, g1_ref[...].astype(f32), b1_ref[...].astype(f32), chunk)
    place_columns(h1_ref, placed_ref)
    for copy in copies:
        copy.wait()

    @pl.loop(0, 3 * D // 256)
    def _(step):
        at = pl.ds(pl.multiple_of(step * 256, 256), 256)
        qkv_ref[:, at] = mul(placed_ref[...], w_ref[:, at]).astype(bf16)

    for row0, count, key0, keys in windows:
        one = same_sequence(count, row0, keys, key0, IMG_LEN)
        mask = jnp.concatenate([one, one], axis=0)
        attend_along(qkv_ref, att_ref, pl.ds(row0, count), pl.ds(key0, keys), mask)
    place_columns(att_ref, placed_ref)

    @pl.loop(0, D // 256)
    def _(step):
        at = pl.ds(pl.multiple_of(step * 256, 256), 256)
        there = pl.ds(pl.multiple_of(step * 256 + 3 * D, 256), 256)
        mid_ref[:, at] = x_ref[:, at].astype(f32) + mul(placed_ref[...], w_ref[:, there])

    norm_rows(mid_ref, h2_ref, g2_ref[...].astype(f32), b2_ref[...].astype(f32), chunk)
    for k in range(rows // IMG_LEN):
        first, last = k * IMG_LEN, (k + 1) * IMG_LEN
        start, end = first // 8 * 8, -(-last // 8) * 8
        values = mid_ref[start:end, :]
        place = lax.broadcasted_iota(jnp.int32, values.shape, 0) + start
        inside = (place >= first) & (place < last)
        sum_ref[k : k + 1, :] = jnp.sum(jnp.where(inside, values, 0.0), axis=0, keepdims=True)


def image_front(rows_in, pieces, perm, gain1, bias1, gain2, bias2):
    rows = rows_in.shape[0]
    windows = ((0, 208, 0, 256), (208, 192, 192, 208))
    vmem = pl.BlockSpec(memory_space=pltpu.VMEM)
    return pl.pallas_call(
        functools.partial(image_front_kernel, windows),
        out_shape=[
            jax.ShapeDtypeStruct((rows, D), bf16),
            jax.ShapeDtypeStruct((rows // IMG_LEN, D), f32),
        ],
        in_specs=[vmem] * 6 + anywhere(pieces),
        out_specs=[vmem] * 2,
        scratch_shapes=[
            pltpu.VMEM((D, 4 * D), bf16),
            pltpu.VMEM((rows, D), bf16),
            pltpu.VMEM((rows, D), bf16),
            pltpu.VMEM((rows, 3 * D), bf16),
            pltpu.VMEM((rows, D), bf16),
            pltpu.VMEM((rows, D), f32),
            pltpu.SemaphoreType.DMA((len(pieces),)),
        ],
        compiler_params=params(),
        cost_estimate=cost(rows * D * D * 12, 8 * D * D, rows * 256 * HEADS),
        name="image_front",
    )(rows_in, perm, gain1[None], bias1[None], gain2[None], bias2[None], *pieces)


def gelu_parts(inner):
    half = 0.5 * (1.0 + lax.erf(inner * (0.5**0.5)))
    return inner * half, half


def pack_kernel(unit_ref, pos_ref, *refs):
    refs[-1][:, :D] = unit_ref[...].astype(bf16)
    refs[-1][:, D:] = pos_ref[...]


def packed(unit, positive, after):
    shape = (unit.shape[0], D + positive.shape[1])
    return pl.pallas_call(
        pack_kernel,
        out_shape=jax.ShapeDtypeStruct(shape, bf16),
        in_specs=[pl.BlockSpec(memory_space=pltpu.VMEM)] * 2 + anywhere(after),
        compiler_params=params(),
        cost_estimate=cost(shape[0] * shape[1], 4 * shape[0] * shape[1]),
        name="packed",
    )(unit, positive, *after)


def pool_matrix(count, rows, row0, seq_len):
    row = (lax.broadcasted_iota(jnp.int32, (count, rows), 1) + row0) // seq_len
    return jnp.where(row == lax.broadcasted_iota(jnp.int32, (count, rows), 0), 1.0, 0.0).astype(bf16)


def two_terms(mean):
    high = mean.astype(bf16)
    low = (mean - high.astype(f32)).astype(bf16)
    return jnp.concatenate([high, low], axis=0)


def unit_rows(pooled):
    inverse = lax.rsqrt(jnp.sum(pooled * pooled, axis=-1, keepdims=True) + norm_eps)
    return pooled * inverse, inverse


def text_up_kernel(h2_ref, wu_ref, wd_ref, sum_ref, *refs):
    slope_ref, hid_ref, unit_ref, inv_ref, acc = refs[-5:]
    step = pl.program_id(0)
    chunk = 128
    per = chunk // TXT_LEN
    pool = pool_matrix(per, chunk, 0, TXT_LEN)
    for k in range(h2_ref.shape[0] // chunk):
        inner = mul(h2_ref[k * chunk : (k + 1) * chunk, :], wu_ref[...])
        value, half = gelu_parts(inner)
        slope = half + inner * (jnp.exp(-0.5 * inner * inner) * 0.3989422804014327)
        slope_ref[k * chunk : (k + 1) * chunk, :] = slope.astype(bf16)
        hid_ref[k * per : (k + 1) * per, :] = mul(pool, value.astype(bf16))
    terms = mul(two_terms(hid_ref[...] * (1.0 / TXT_LEN)), wd_ref[...])
    count = hid_ref.shape[0]
    added = terms[:count] + terms[count:]

    @pl.when(step == 0)
    def _():
        acc[...] = sum_ref[...] * (1.0 / TXT_LEN) + added

    @pl.when(step > 0)
    def _():
        acc[...] += added

    @pl.when(step == pl.num_programs(0) - 1)
    def _():
        unit, inverse = unit_rows(acc[...])
        unit_ref[...] = unit
        inv_ref[...] = jnp.broadcast_to(inverse, inv_ref.shape)


def text_up(normed2, weight_up, weight_down, middle_sum, after=()):
    rows, count = normed2.shape[0], middle_sum.shape[0]
    fixed = lambda shape: pl.BlockSpec(shape, lambda i: (0, 0))
    return pl.pallas_call(
        text_up_kernel,
        grid=(FF // TILE,),
        out_shape=[
            jax.ShapeDtypeStruct((rows, FF), bf16),
            jax.ShapeDtypeStruct((count, FF), f32),
            jax.ShapeDtypeStruct((count, D), f32),
            jax.ShapeDtypeStruct((count, 128), f32),
        ],
        in_specs=[
            fixed((rows, D)),
            pl.BlockSpec((D, TILE), lambda i: (0, i)),
            pl.BlockSpec((TILE, D), lambda i: (i, 0)),
            fixed((count, D)),
        ]
        + anywhere(after),
        out_specs=[
            pl.BlockSpec((rows, TILE), lambda i: (0, i)),
            pl.BlockSpec((count, TILE), lambda i: (0, i)),
            fixed((count, D)),
            fixed((count, 128)),
        ],
        scratch_shapes=[pltpu.VMEM((count, D), f32)],
        compiler_params=params(),
        cost_estimate=cost(2 * rows * D * FF, 4 * D * FF + 2 * rows * FF, 20 * rows * FF),
        name="text_up",
    )(normed2, weight_up, weight_down, middle_sum, *after)


def image_up_kernel(fold, h2_ref, wu_ref, wd_ref, sum_ref, *refs):
    out_ref, acc = refs[-2:]
    step = pl.program_id(0)
    rows, count = h2_ref.shape[0], sum_ref.shape[0]
    chunk = 80
    summed = jnp.zeros((count, TILE), f32)
    for k in range(rows // chunk):
        inner = mul(h2_ref[k * chunk : (k + 1) * chunk, :], wu_ref[...])
        value, _ = gelu_parts(inner)
        pool = pool_matrix(count, chunk, k * chunk, IMG_LEN)
        summed = summed + mul(pool, value.astype(bf16))
    mean = two_terms(summed * (1.0 / IMG_LEN))
    place = lax.broadcasted_iota(jnp.int32, (TILE, TILE // fold), 0)
    picked = lax.broadcasted_iota(jnp.int32, (TILE, TILE // fold), 1) * fold
    terms = jnp.zeros((2 * count, D), f32)
    for k in range(fold):
        chosen = jnp.where(place == picked + k, 1.0, 0.0).astype(bf16)
        part = mul(mean, chosen).astype(bf16)
        terms = terms + mul(part, wd_ref[:, k * D : (k + 1) * D])
    added = terms[:count] + terms[count:]

    @pl.when(step == 0)
    def _():
        acc[...] = sum_ref[...] * (1.0 / IMG_LEN) + added

    @pl.when(step > 0)
    def _():
        acc[...] += added

    @pl.when(step == pl.num_programs(0) - 1)
    def _():
        out_ref[...] = unit_rows(acc[...])[0].astype(bf16)


def image_up(normed2, whole, up_col, down_col, middle_sum, after=()):
    rows, count = normed2.shape[0], middle_sum.shape[0]
    fold = FF // D
    fixed = lambda shape: pl.BlockSpec(shape, lambda i: (0, 0))
    return pl.pallas_call(
        functools.partial(image_up_kernel, fold),
        grid=(FF // TILE,),
        out_shape=jax.ShapeDtypeStruct((count, D), bf16),
        in_specs=[
            fixed((rows, D)),
            pl.BlockSpec((D, TILE), lambda i: (0, up_col // TILE + i)),
            pl.BlockSpec((TILE // fold, fold * D), lambda i: (i, down_col // (fold * D))),
            fixed((count, D)),
        ]
        + anywhere(after),
        out_specs=fixed((count, D)),
        scratch_shapes=[pltpu.VMEM((count, D), f32)],
        compiler_params=params(),
        cost_estimate=cost(2 * rows * D * FF, 4 * D * FF, 15 * rows * FF),
        name="image_up",
    )(normed2, whole, whole, middle_sum, *after)


def left_kernel(order_ref, h2_ref, h1_ref, att_ref, up_ref, rest_ref):
    step = pl.program_id(0)

    @pl.when(step < 2)
    def _():
        up_ref[0] = placed(order_ref[0], h2_ref[...])

    @pl.when((step == 2) | (step == 3))
    def _():
        rest_ref[0] = placed(order_ref[0], h1_ref[...])

    @pl.when(step == 4)
    def _():
        rest_ref[0] = placed(order_ref[0], att_ref[...])


def left_factors(orders, normed2, normed1, attended):
    rows = normed1.shape[0]
    fixed = pl.BlockSpec((rows, D), lambda i: (0, 0))
    return pl.pallas_call(
        left_kernel,
        grid=(5,),
        out_shape=[
            jax.ShapeDtypeStruct((2, D, rows), bf16),
            jax.ShapeDtypeStruct((3, D, rows), bf16),
        ],
        in_specs=[
            pl.BlockSpec((1, D, D), lambda i: (jnp.minimum(i % 2 + i // 4, 1), 0, 0)),
            fixed,
            fixed,
            fixed,
        ],
        out_specs=[
            pl.BlockSpec((1, D, rows), lambda i: (jnp.minimum(i, 1), 0, 0)),
            pl.BlockSpec((1, D, rows), lambda i: (jnp.maximum(i - 2, 0), 0, 0)),
        ],
        compiler_params=params(),
        cost_estimate=cost(10 * rows * D * D, 16 * rows * D + 10 * D * D),
        name="left_factors",
    )(orders, normed2, normed1, attended)


def loss_parts(text_rows, pos, image_all):
    similar = mul_bt(text_rows, image_all) * logit_scale
    shifted = jnp.exp(similar - logit_scale)
    alive = jnp.max(pos, axis=1, keepdims=True)
    row_sum = jnp.sum(shifted, axis=1, keepdims=True)
    row_count = jnp.maximum(jnp.sum(pos, axis=1, keepdims=True), 1.0)
    return similar, shifted, alive, row_sum, row_count


def sums_over_captions(text_rows, pos, image_all):
    similar, shifted, alive, row_sum, row_count = loss_parts(text_rows, pos, image_all)
    pos_similar = pos * similar
    cap_term = alive * (
        logit_scale + jnp.log(row_sum) - jnp.sum(pos_similar, axis=1, keepdims=True) / row_count
    )
    return (
        jnp.sum(alive * shifted, axis=0, keepdims=True),
        jnp.sum(pos, axis=0, keepdims=True),
        jnp.sum(pos_similar, axis=0, keepdims=True),
        jnp.sum(cap_term, axis=0, keepdims=True),
        jnp.sum(alive, axis=0, keepdims=True),
    )


def loss_from(sums):
    col_sum, col_count, col_pos, cap_total, live_total = sums
    img_term = logit_scale + jnp.log(col_sum) - col_pos / col_count
    return 0.5 * cap_total / live_total + 0.5 * jnp.mean(img_term, axis=1, keepdims=True)


def grad_of_unit(text_rows, pos, image_all, col_sum, col_count, live_total):
    _, shifted, alive, row_sum, row_count = loss_parts(text_rows, pos, image_all)
    cap_share, img_share = 0.5 / live_total, 0.5 / image_all.shape[0]
    grad_sims = alive * shifted * (cap_share / row_sum + img_share / col_sum) - pos * (
        cap_share / row_count + img_share / col_count
    )
    return mul(grad_sims.astype(bf16), image_all) * logit_scale


def turned(grad, unit):
    return grad - unit * jnp.sum(grad * unit, axis=-1, keepdims=True)


def loss_kernel(
    pack_ref, image_ref, own_ref, unit_ref, inv_ref, loss_ref, row_ref, low_ref, col_sum_ref,
    col_count_ref, live_ref
):
    image_all = image_ref[...]
    chunk = 256
    total = None
    for k in range(pack_ref.shape[0] // chunk):
        at = slice(k * chunk, (k + 1) * chunk)
        part = sums_over_captions(pack_ref[at, :D], pack_ref[at, D:].astype(f32), image_all)
        total = part if total is None else [a + b for a, b in zip(total, part)]
    loss_ref[...] = jnp.broadcast_to(loss_from(total), loss_ref.shape)
    col_sum, col_count, _, _, live_total = total
    col_sum_ref[...] = col_sum
    col_count_ref[...] = col_count
    live_ref[...] = jnp.broadcast_to(live_total, live_ref.shape)
    grad = grad_of_unit(
        own_ref[:, :D], own_ref[:, D:].astype(f32), image_all, col_sum, col_count, live_total
    )
    row = inv_ref[:, :1] * turned(grad, unit_ref[...]) * (1.0 / TXT_LEN)
    row_ref[...] = row
    low_ref[...] = row.astype(bf16)


def loss_and_rows(pack, image_all, own_pack, unit, inverse):
    images, count = image_all.shape[0], own_pack.shape[0]
    shapes = [(1, 128), (count, D), (count, D), (1, images), (1, images), (1, 128)]
    kinds = [f32, f32, bf16, f32, f32, f32]
    return pl.pallas_call(
        loss_kernel,
        out_shape=[jax.ShapeDtypeStruct(*item) for item in zip(shapes, kinds)],
        compiler_params=params(),
        cost_estimate=cost(2 * pack.shape[0] * images * D, 2 * pack.size, pack.shape[0] * images),
        name="loss_and_rows",
    )(pack, image_all, own_pack, unit, inverse)


def down_kernel(pack_ref, image_ref, col_sum_ref, col_count_ref, live_ref, hid_ref, *refs):
    step, out_ref = pl.program_id(0), refs[-1]
    text_rows = pack_ref[:, :D]
    grad = grad_of_unit(
        text_rows, pack_ref[:, D:].astype(f32), image_ref[...], col_sum_ref[...],
        col_count_ref[...], live_ref[:, :1]
    )
    rows = (turned(grad, text_rows.astype(f32)) * (1.0 / TXT_LEN)).astype(bf16)
    part = mul_at(hid_ref[...], rows)

    @pl.when(step == 0)
    def _():
        out_ref[...] = part

    @pl.when(step > 0)
    def _():
        out_ref[...] += part


def grad_of_down(pack, image_all, col_sum, col_count, live_total, hidden_cols, after):
    images, chunk = image_all.shape[0], 256
    fixed = lambda shape: pl.BlockSpec(shape, lambda i: (0, 0))
    per = hidden_cols.shape[1]
    return pl.pallas_call(
        down_kernel,
        grid=(pack.shape[0] // chunk,),
        out_shape=jax.ShapeDtypeStruct((per, D), f32),
        in_specs=[
            pl.BlockSpec((chunk, pack.shape[1]), lambda i: (i, 0)),
            fixed((images, D)), fixed((1, images)), fixed((1, images)), fixed((1, 128)),
            pl.BlockSpec((chunk, per), lambda i: (i, 0)),
        ]
        + anywhere(after),
        out_specs=fixed((per, D)),
        compiler_params=params(),
        cost_estimate=cost(4 * pack.shape[0] * images * D, 2 * pack.size, pack.shape[0] * images),
        name="grad_of_down",
    )(pack, image_all, col_sum, col_count, live_total, hidden_cols, *after)


def mlp_back_kernel(
    low_ref, wd_ref, slope_ref, wu_ref, lhs_ref, mid_ref, gain_ref, row_ref, keep_a, send_a, keep_b,
    send_b, out_ref, gain_out, bias_out, acc
):
    step = pl.program_id(0)
    count, rows = low_ref.shape[0], slope_ref.shape[0]
    half = D // 2
    hidden = mul_bt(low_ref[...], wd_ref[...])
    wide = jnp.broadcast_to(hidden[:, None, :], (count, TXT_LEN, TILE)).reshape(rows, TILE)
    inner = (wide * slope_ref[...].astype(f32)).astype(bf16)
    weight = mul(lhs_ref[0], inner).astype(bf16)

    @pl.when(step < pl.num_programs(0) // 2)
    def _():
        keep_a[...] = weight[:half]
        send_a[...] = weight[half:]

    @pl.when(step >= pl.num_programs(0) // 2)
    def _():
        keep_b[...] = weight[:half]
        send_b[...] = weight[half:]

    added = mul_bt(inner, wu_ref[...])

    @pl.when(step == 0)
    def _():
        acc[...] = added

    @pl.when(step > 0)
    def _():
        acc[...] += added

    @pl.when(step == pl.num_programs(0) - 1)
    def _():
        chunk = 128
        per = chunk // TXT_LEN
        gain = gain_ref[...]
        gain_out[...] = jnp.zeros_like(gain_out)
        bias_out[...] = jnp.zeros_like(bias_out)

        @pl.loop(0, rows // chunk)
        def _(k):
            at = pl.ds(pl.multiple_of(k * chunk, chunk), chunk)
            unit, scale = norm_parts(mid_ref[at, :])
            grad = acc[at, :]
            gain_out[...] += jnp.sum(grad * unit, axis=0, keepdims=True)
            bias_out[...] += jnp.sum(grad, axis=0, keepdims=True)
            row = row_ref[pl.ds(pl.multiple_of(k * per, per), per), :]
            row = jnp.broadcast_to(row[:, None, :], (per, TXT_LEN, D)).reshape(chunk, D)
            out_ref[at, :] = row + norm_back(unit, scale, gain, grad)


def mlp_back(grad_row, grad_low, weight_down, slope, weight_up, lhs, middle, gain):
    rows, count = slope.shape[0], grad_row.shape[0]
    steps = FF // TILE
    fixed = lambda shape: pl.BlockSpec(shape, lambda i: (0, 0))
    first = pl.BlockSpec((D // 2, TILE), lambda i: (0, jnp.minimum(i, steps // 2 - 1)))
    second = pl.BlockSpec((D // 2, TILE), lambda i: (0, jnp.maximum(i - steps // 2, 0)))
    part = jax.ShapeDtypeStruct((D // 2, FF // 2), bf16)
    line = jax.ShapeDtypeStruct((1, D), f32)
    return pl.pallas_call(
        mlp_back_kernel,
        grid=(steps,),
        out_shape=[part] * 4 + [jax.ShapeDtypeStruct((rows, D), f32), line, line],
        in_specs=[
            fixed((count, D)),
            pl.BlockSpec((TILE, D), lambda i: (i, 0)),
            pl.BlockSpec((rows, TILE), lambda i: (0, i)),
            pl.BlockSpec((D, TILE), lambda i: (0, i)),
            pl.BlockSpec((1, D, rows), lambda i: (i // (steps // 2), 0, 0)),
            fixed((rows, D)),
            fixed((1, D)),
            fixed((count, D)),
        ],
        out_specs=[first, first, second, second, fixed((rows, D)), fixed((1, D)), fixed((1, D))],
        scratch_shapes=[pltpu.VMEM((rows, D), f32)],
        compiler_params=params(),
        cost_estimate=cost(4 * rows * D * FF, 4 * D * FF + 2 * rows * FF + 2 * D * FF, rows * FF),
        name="mlp_back",
    )(grad_low, weight_down, slope, weight_up, lhs, middle, gain[None], grad_row)


def attention_back_kernel(grad_ref, wo_ref, qkv_ref, lse_ref, *refs):
    low_ref, out_ref = refs[-2:]
    chunk = grad_ref.shape[0]
    mask = same_sequence(chunk, 0, chunk, 0, TXT_LEN)
    low = grad_ref[...].astype(bf16)
    low_ref[...] = low
    grad_att = mul_bt(low, wo_ref[...]).astype(bf16)
    for pair in range(HEADS // 2):
        queries = qkv_ref[:, pair_cols(0, pair)] * bf16(HEAD ** (-0.5))
        keys = two_heads(qkv_ref[:, pair_cols(1, pair)])
        vals = two_heads(qkv_ref[:, pair_cols(2, pair)])
        grads = grad_att[:, pair_cols(0, pair)]
        scores, grad_probs = mul_bt(keys, queries), mul_bt(vals, grads)
        probs, grad_scores = [], []
        for k in range(2):
            at = slice(k * chunk, (k + 1) * chunk)
            head = 2 * pair + k
            shifted = scores[at] - lse_ref[head : head + 1, :]
            prob = jnp.where(mask, jnp.exp(jnp.where(mask, shifted, 0.0)), 0.0)
            along = jnp.sum(grad_probs[at] * prob, axis=0, keepdims=True)
            grad_scores.append((prob * (grad_probs[at] - along)).astype(bf16))
            probs.append(prob.astype(bf16))
        grad_q = mul_at(jnp.concatenate(grad_scores, axis=0), keys) * HEAD ** (-0.5)
        grad_k = mul(jnp.concatenate(grad_scores, axis=1), two_heads(queries))
        grad_v = mul(jnp.concatenate(probs, axis=1), two_heads(grads))
        out_ref[:, pair_cols(0, pair)] = grad_q.astype(bf16)
        out_ref[:, pair_cols(1, pair)] = grad_k.astype(bf16)
        out_ref[:, pair_cols(2, pair)] = grad_v.astype(bf16)


def attention_back(grad_middle, weight_out, project, log_sums, first, count, after=()):
    chunk = 128
    rows = count * chunk
    return pl.pallas_call(
        attention_back_kernel,
        grid=(count,),
        out_shape=[
            jax.ShapeDtypeStruct((rows, D), bf16),
            jax.ShapeDtypeStruct((rows, 3 * D), bf16),
        ],
        in_specs=[
            pl.BlockSpec((chunk, D), lambda i: (i + first, 0)),
            pl.BlockSpec((D, D), lambda i: (0, 0)),
            pl.BlockSpec((chunk, 3 * D), lambda i: (i + first, 0)),
            pl.BlockSpec((16, chunk), lambda i: (i + first, 0)),
        ]
        + anywhere(after),
        out_specs=[
            pl.BlockSpec((chunk, D), lambda i: (i, 0)),
            pl.BlockSpec((chunk, 3 * D), lambda i: (i, 0)),
        ],
        compiler_params=params(),
        cost_estimate=cost(10 * rows * D * D, 16 * rows * D + 2 * D * D, rows * 128 * HEADS),
        name="attention_back",
    )(grad_middle, weight_out, project, log_sums, *after)


def mul_rows(lhs, parts):
    total, row = 0.0, 0
    for part in parts:
        total = total + mul(lhs[:, row : row + part.shape[0]], part[...])
        row += part.shape[0]
    return total


def weight_back_kernel(counts, lhs_ref, *refs):
    step, half = pl.program_id(0), D // 2
    keep, send = refs[-2:]
    row = 0
    for k, count in enumerate(counts):
        parts = refs[row : row + count]
        row += count

        @pl.when(step == k if len(counts) > 1 else step >= 0)
        def _(parts=parts):
            weight = mul_rows(lhs_ref[0], parts).astype(bf16)
            keep[...] = weight[:half]
            send[...] = weight[half:]


def weight_back(lhs, first, groups, blocks, after=()):
    rows = lhs.shape[2]
    steps = 2
    many = len(groups) > 1
    given = [part for group in groups for part in group]
    return pl.pallas_call(
        functools.partial(weight_back_kernel, [len(group) for group in groups]),
        grid=(steps,),
        out_shape=[jax.ShapeDtypeStruct((D // 2, steps * D), bf16)] * 2,
        in_specs=[pl.BlockSpec((1, D, rows), lambda i: (first + (i if many else 0), 0, 0))]
        + [
            pl.BlockSpec((part.shape[0], D), lambda i, col=col: (0, col + (0 if many else i)))
            for group, col in zip(groups, blocks)
            for part in group
        ]
        + anywhere(after),
        out_specs=[pl.BlockSpec((D // 2, D), lambda i: (0, i))] * 2,
        compiler_params=params(),
        cost_estimate=cost(4 * rows * D * D, 4 * rows * D + 7 * D * D),
        name="weight_back",
    )(lhs, *given, *after)


def input_back_kernel(count, *refs):
    projs = refs[:count]
    w_ref, x_ref, gain_ref, mid_ref = refs[count : count + 4]
    out_ref, gain_out, bias_out, acc = refs[-4:]
    step = pl.program_id(0)
    rows, chunk = x_ref.shape[0], 128
    row = 0
    for part in projs:
        at = slice(row, row + part.shape[0])
        row += part.shape[0]
        added = mul_bt(part[...], w_ref[...])

        @pl.when(step == 0)
        def _(at=at, added=added):
            acc[at, :] = added

        @pl.when(step > 0)
        def _(at=at, added=added):
            acc[at, :] += added

    @pl.when(step == pl.num_programs(0) - 1)
    def _():
        gain = gain_ref[...]
        gain_out[...] = jnp.zeros_like(gain_out)
        bias_out[...] = jnp.zeros_like(bias_out)

        @pl.loop(0, rows // chunk)
        def _(k):
            at = pl.ds(pl.multiple_of(k * chunk, chunk), chunk)
            unit, scale = norm_parts(x_ref[at, :].astype(f32))
            grad = acc[at, :]
            gain_out[...] += jnp.sum(grad * unit, axis=0, keepdims=True)
            bias_out[...] += jnp.sum(grad, axis=0, keepdims=True)
            out_ref[at, :] = mid_ref[at, :] + norm_back(unit, scale, gain, grad)


def input_back(grad_projs, weight, rows_in, gain, grad_middle, after=()):
    rows = rows_in.shape[0]
    fixed = lambda shape: pl.BlockSpec(shape, lambda i: (0, 0))
    line = jax.ShapeDtypeStruct((1, D), f32)
    return pl.pallas_call(
        functools.partial(input_back_kernel, len(grad_projs)),
        grid=(3,),
        out_shape=[jax.ShapeDtypeStruct((rows, D), f32), line, line],
        in_specs=[pl.BlockSpec((part.shape[0], D), lambda i: (0, i)) for part in grad_projs]
        + [
            pl.BlockSpec((D, D), lambda i: (0, i)),
            fixed((rows, D)), fixed((1, D)), fixed((rows, D)),
        ]
        + anywhere(after),
        out_specs=[fixed((rows, D)), fixed((1, D)), fixed((1, D))],
        scratch_shapes=[pltpu.VMEM((rows, D), f32)],
        compiler_params=params(),
        cost_estimate=cost(6 * rows * D * D, 14 * rows * D + 6 * D * D),
        name="input_back",
    )(*grad_projs, weight, rows_in, gain[None], grad_middle, *after)


def local(
    images,
    captions,
    img_gain1,
    img_bias1,
    img_qkv,
    img_out,
    img_gain2,
    img_bias2,
    img_up,
    img_down,
    txt_gain1,
    txt_bias1,
    txt_qkv,
    txt_out,
    txt_gain2,
    txt_bias2,
    txt_up,
    txt_down,
    counts,
    matches,
):
    peers = lax.axis_size(AXIS)
    own = lax.axis_index(AXIS)
    per = D // peers
    img_local = counts.shape[0]
    cap_local = matches.shape[0]
    total_images = matches.shape[1]

    whole = lax.all_gather(
        jnp.concatenate([img_up.reshape(per, FF), img_down.reshape(per, FF)], axis=1),
        AXIS,
        axis=0,
        tiled=True,
    )
    small = peers == 32
    shard = jnp.concatenate([img_qkv.reshape(per, 3 * D), img_out.reshape(per, D)], axis=1)
    if small:
        line, perm = gathered_line(shard), row_order((1, 4, 2, 16, 8))
    else:
        line, perm = lax.all_gather(shard, AXIS, axis=0, tiled=True), jnp.eye(D, dtype=bf16)

    normed1, project, attended, middle, normed2, middle_sum, log_sums = text_front(
        captions, txt_gain1, txt_bias1, txt_qkv, txt_out, txt_gain2, txt_bias2
    )
    middle_sum, line = in_turn(middle_sum, line)
    beside, above = (swapped(line, 2), swapped(line, 4)) if small else (line, line)
    slope, hidden_sum, text_unit, inverse = text_up(
        normed2, txt_up, txt_down, middle_sum, (line,)
    )
    text_unit, (beside, above) = in_turn(text_unit, (beside, above))

    ends_at = jnp.cumsum(counts)
    slot_ids = lax.iota(jnp.int32, cap_local)
    owner = jnp.sum((ends_at[None, :] <= slot_ids[:, None]).astype(jnp.int32), axis=1)
    owner = owner + own * img_local
    live = slot_ids < ends_at[-1]
    columns = lax.iota(jnp.int32, total_images)
    positive = ((matches > 0) | (owner[:, None] == columns[None, :])) & live[:, None]

    own_pack = packed(text_unit, positive.astype(bf16), ())
    pieces = [line]
    if small:
        held = own_pack[None]
        first, second = diagonal(beside, above)
        others = [swapped(held, mask) for mask in (8, 16, 24)]
        scaled_sum = (hidden_sum * inverse[:, :1]).astype(bf16)
        hidden_cols = lax.all_to_all(scaled_sum, AXIS, split_axis=1, concat_axis=0, tiled=True)
        others, first, second, hidden_cols = lax.optimization_barrier(
            (others, first, second, hidden_cols)
        )
        held = joined(joined(held, others[0], 8), joined(others[1], others[2], 8), 16, 1)
        text_beside, text_above = swapped(held, 2), swapped(held, 4)
        pieces = [line, beside, above, first, second]
        pieces = pieces + [swapped(piece, 1) for piece in pieces]

    normed_img, middle_img = image_front(
        images, pieces, perm, img_gain1, img_bias1, img_gain2, img_bias2
    )
    if small:
        normed_img, text_beside, text_above = lax.optimization_barrier(
            (normed_img, text_beside, text_above)
        )
        across = jnp.concatenate(diagonal(text_beside, text_above), axis=0)
        held = joined(joined(held, text_beside, 2), joined(text_above, across, 2), 4, 4)

    order_a, order_b, tail = stage_orders()
    orders = jnp.stack([row_order(order_a + tail[::-1]), row_order(order_b + tail[::-1])])
    if small:
        whole, held, orders = lax.optimization_barrier((whole, held, orders))
        other = swapped(held, 1)
    image_low = image_up(normed_img, whole, 0, FF, middle_img)
    if small:
        text_pack = joined(held, other, 1).reshape(-1, D + total_images)
    image_low, normed2 = in_turn(image_low, normed2)
    image_all = spread(image_low).reshape(total_images, D)
    lhs_up, lhs_rest = left_factors(orders, normed2, normed1, attended)
    image_all, lhs_up = in_turn(image_all, lhs_up)

    if small:
        loss_value, grad_row, row_low, col_sum, col_count, live_total = loss_and_rows(
            text_pack, image_all, own_pack, text_unit, inverse
        )
        loss_value = loss_value[0, 0]
    else:
        text_low, pos = own_pack[:, :D], own_pack[:, D:].astype(f32)
        sums = lax.psum(sums_over_captions(text_low, pos, image_all), AXIS)
        loss_value = loss_from(sums)[0, 0]
        grad = grad_of_unit(text_low, pos, image_all, sums[0], sums[1], sums[4])
        grad_row = inverse[:, :1] * turned(grad, text_unit) * (1.0 / TXT_LEN)
        row_low = grad_row.astype(bf16)

    *up, grad_middle, gain_two, bias_two = mlp_back(
        grad_row, row_low, txt_down, slope, txt_up, lhs_up, middle, txt_gain2
    )
    stages = len(order_a)
    low_one, proj_one = attention_back(grad_middle, txt_out, project, log_sums, 0, 1)
    for stage in range(stages - 2):
        up = fold(hand_on(up, stage), (proj_one,))
    low_two, proj_two = attention_back(grad_middle, txt_out, project, log_sums, 1, 4, up)
    up = fold(hand_on(up, stages - 2), (proj_two,))
    projs, lows = (proj_one, proj_two), (low_one, low_two)
    rest_a = weight_back(lhs_rest, 0, [projs], [0], up)
    up = hand_on_last(fold_last(hand_on(up, stages - 1), rest_a[1:]))
    rest_b = weight_back(lhs_rest, 1, [projs, lows], [2, 0], up[:1])
    rest = [*rest_a, *rest_b]
    for stage in range(stages - 2):
        rest = fold(hand_on(rest, stage))
    caption_grad, gain_one, bias_one = input_back(
        projs, txt_qkv, captions, txt_gain1, grad_middle, rest[:1]
    )
    caption_grad, up = in_turn(caption_grad, up)
    rest = fold(hand_on(rest, stages - 2), (caption_grad,))
    norms = jnp.concatenate([gain_one, bias_one, gain_two, bias_two], axis=0)
    norms, rest = in_turn(norms, rest)
    norms = jnp.sum(spread(norms[None].astype(bf16)).astype(f32), axis=0).reshape(4, D)
    rest = fold_last(hand_on(rest, stages - 1))
    if small:
        grad_down = grad_of_down(
            text_pack, image_all, col_sum, col_count, live_total, hidden_cols, (rest[0], norms)
        )
    else:
        grad_down = lax.psum_scatter(
            mul_at(hidden_sum.astype(bf16), row_low), AXIS, scatter_dimension=0, tiled=True
        )
    grad_down, rest = in_turn(grad_down, hand_on_last(rest))
    up_share = sum_last(*up)
    rest_share = sum_last(*rest)
    return (
        loss_value,
        caption_grad,
        norms[0],
        norms[1],
        rest_share[:, : 3 * D].reshape(-1),
        rest_share[:, 3 * D :].reshape(-1),
        norms[2],
        norms[3],
        up_share.reshape(-1),
        grad_down.reshape(-1),
    )


def solution(mesh):
    split, flat, whole = P("blk", None), P("blk"), P()
    image_block = (whole, whole, flat, flat, whole, whole, flat, flat)
    return jax.shard_map(
        local,
        mesh=mesh,
        in_specs=(split, split) + image_block + (whole,) * 8 + (flat, split),
        out_specs=(whole, split, whole, whole, flat, flat, whole, whole, flat, flat),
        check_vma=False,
    )
```

```python
import functools

import jax
import jax.numpy as jnp
from jax import lax
from jax.experimental import pallas as pl
from jax.experimental.pallas import tpu as pltpu
from jax.sharding import PartitionSpec as P

D = 768
FF = 3072
HEAD = 64
HEADS = D // HEAD
IMG_LEN = 50
TXT_LEN = 16
AXIS = "blk"

norm_eps = 1e-06
logit_scale = 50.0
f32 = jnp.float32
bf16 = jnp.bfloat16


def swapped(value, mask):
    peers = lax.axis_size(AXIS)
    return lax.ppermute(value, AXIS, [(i, i ^ mask) for i in range(peers)])


def bit_masks():
    peers = lax.axis_size(AXIS)
    return [1 << k for k in range(peers.bit_length() - 1)]


def joined(held, other, mask, outer=None):
    upper = (lax.axis_index(AXIS) & mask) > 0
    first = jnp.where(upper, other, held)
    second = jnp.where(upper, held, other)
    outer = held.shape[0] if outer is None else outer
    parts = [part.reshape((outer, -1) + held.shape[1:]) for part in (first, second)]
    return jnp.stack(parts, axis=1).reshape((-1,) + held.shape[1:])


def spread(block):
    peers = lax.axis_size(AXIS)
    copies = jnp.broadcast_to(block[None], (peers,) + block.shape)
    return lax.all_to_all(copies, AXIS, split_axis=0, concat_axis=0, tiled=True)


def stage_orders():
    masks = bit_masks()
    head, tail = masks[:-2], masks[-2:]
    order_a = list(head)
    order_b = list(head)
    for k in range(1, len(head) - 1, 2):
        order_b[k], order_b[k + 1] = order_b[k + 1], order_b[k]
    return order_a, order_b, tail


def row_order(bits):
    peers = lax.axis_size(AXIS)
    own = lax.axis_index(AXIS)
    per = D // peers
    places = lax.iota(jnp.int32, D)
    block = places // per
    target = jnp.zeros_like(block) + own
    for k, mask in enumerate(bits):
        target = target ^ (((block >> (len(bits) - 1 - k)) & 1) * mask)
    source = target * per + places % per
    return (source[:, None] == lax.iota(jnp.int32, D)[None, :]).astype(bf16)


def gathered_line(shard):
    return jnp.concatenate([shard] + [swapped(shard, mask) for mask in (8, 16, 24)], axis=0)


def diagonal(beside, above):
    half = beside.shape[0] // 2
    return swapped(beside[:half], 4), swapped(above[half:], 2)


def in_turn(first, then):
    return lax.optimization_barrier((first, then))


def placed(order, values):
    return mul_bt(order, values).astype(bf16)


def hand_on(parts, stage):
    order_a, order_b, _ = stage_orders()
    keep_a, send_a, keep_b, send_b = parts
    return keep_a, swapped(send_a, order_a[stage]), keep_b, swapped(send_b, order_b[stage])


def hand_on_last(blocks):
    low, high = stage_orders()[2]
    own, *others = blocks
    return own, [swapped(block, mask) for block, mask in zip(others, (low, high, low | high))]


def sum_last(own, others):
    total = own
    for other in others:
        total = total + other.astype(f32)
    return total


VMEM_BYTES = 40 << 20
TILE = 512


def norm_parts(values):
    average = jnp.mean(values, axis=-1, keepdims=True)
    centred = values - average
    variance = jnp.mean(centred * centred, axis=-1, keepdims=True)
    scale = lax.rsqrt(variance + norm_eps)
    return centred * scale, scale


def norm_back(unit, scale, gain, grad):
    inner = grad * gain
    shift = jnp.mean(inner, axis=-1, keepdims=True)
    along = jnp.mean(inner * unit, axis=-1, keepdims=True)
    return scale * (inner - shift - unit * along)


def mul(lhs, rhs):
    return jnp.dot(lhs, rhs, preferred_element_type=f32)


def mul_bt(lhs, rhs):
    return lax.dot_general(lhs, rhs, (((1,), (1,)), ((), ())), preferred_element_type=f32)


def mul_at(lhs, rhs):
    return lax.dot_general(lhs, rhs, (((0,), (0,)), ((), ())), preferred_element_type=f32)


def params(limit=VMEM_BYTES):
    return pltpu.CompilerParams(vmem_limit_bytes=limit)


def in_vmem(count):
    return [pl.BlockSpec(memory_space=pltpu.VMEM)] * count


def stays(shape, dtype):
    return pltpu.VMEM(shape, dtype)


def cost(flops, moved, transcendentals=0):
    return pl.CostEstimate(flops=flops, bytes_accessed=moved, transcendentals=transcendentals)


def lane_halves(dtype):
    lane = lax.broadcasted_iota(jnp.int32, (1, 2 * HEAD), 1)
    low = jnp.where(lane < HEAD, 1.0, 0.0)
    return low.astype(dtype), (1.0 - low).astype(dtype)


def two_heads(pair):
    low, high = lane_halves(bf16)
    return jnp.concatenate([pair * low, pair * high], axis=0)


def same_sequence(rows, row0, cols, col0, seq_len):
    row = (lax.broadcasted_iota(jnp.int32, (rows, cols), 0) + row0) // seq_len
    col = (lax.broadcasted_iota(jnp.int32, (rows, cols), 1) + col0) // seq_len
    return row == col


def softmax_down(scores, mask):
    keys = mask.shape[0]
    parts, sums = [], []
    for k in range(2):
        part = jnp.where(mask, scores[k * keys : (k + 1) * keys], -1e30)
        most = jnp.max(part, axis=0, keepdims=True)
        raised = jnp.exp(part - most)
        total = jnp.sum(raised, axis=0, keepdims=True)
        parts.append(raised * (1.0 / total))
        sums.append(most + jnp.log(total))
    return parts, sums


def fold_kernel(keep_a, got_a, keep_b, got_b, *refs):
    outs = refs[-4:]
    half, tile = outs[0].shape[0], 256

    @pl.loop(0, keep_a.shape[1] // tile)
    def _(step):
        cols = pl.ds(pl.multiple_of(step * tile, tile), tile)
        for k, (kept, got) in enumerate(((keep_a, got_a), (keep_b, got_b))):
            for j in range(2):
                at = slice(j * half, (j + 1) * half)
                total = kept[at, cols].astype(f32) + got[at, cols].astype(f32)
                outs[2 * k + j][:, cols] = total.astype(bf16)


def fold(parts, after=()):
    rows, cols = parts[0].shape
    if rows % 32:
        whole = [
            (kept.astype(f32) + got.astype(f32)).astype(bf16)
            for kept, got in (parts[:2], parts[2:])
        ]
        return [part for one in whole for part in (one[: rows // 2], one[rows // 2 :])]
    return pl.pallas_call(
        fold_kernel,
        out_shape=[stays((rows // 2, cols), bf16)] * 4,
        in_specs=in_vmem(4) + anywhere(after),
        out_specs=in_vmem(4),
        compiler_params=params(8 << 20),
        cost_estimate=cost(2 * rows * cols, 12 * rows * cols),
        name="fold",
    )(*parts, *after)


def fold_last_kernel(keep_a, got_a, keep_b, got_b, *refs):
    own_ref, *outs = refs[-4:]
    rows = own_ref.shape[0]
    cols = keep_a.shape[1]
    for k, (kept, got) in enumerate(((keep_a, got_a), (keep_b, got_b))):
        total = kept[...].astype(f32) + got[...].astype(f32)
        at = slice(k * cols, (k + 1) * cols)
        own_ref[:, at] = total[:rows]
        for j, out in enumerate(outs):
            out[:, at] = total[(j + 1) * rows : (j + 2) * rows].astype(bf16)


def fold_last(parts, after=()):
    rows, cols = parts[0].shape
    shape = (rows // 4, 2 * cols)
    if rows % 32:
        pairs = (parts[:2], parts[2:])
        both = [kept.astype(f32) + got.astype(f32) for kept, got in pairs]
        own, *others = jnp.split(jnp.concatenate(both, axis=1), 4)
        return [own] + [other.astype(bf16) for other in others]
    return pl.pallas_call(
        fold_last_kernel,
        out_shape=[stays(shape, f32)] + [stays(shape, bf16)] * 3,
        in_specs=in_vmem(4) + anywhere(after),
        out_specs=in_vmem(4),
        compiler_params=params(8 << 20),
        cost_estimate=cost(2 * rows * cols, 12 * rows * cols),
        name="fold_last",
    )(*parts, *after)


def anywhere(after):
    return [pl.BlockSpec(memory_space=pl.ANY)] * len(after)


def pair_cols(part, pair):
    start = part * D + pair * 2 * HEAD
    return slice(start, start + 2 * HEAD)


def norm_rows(src, dst, gain, bias, step_rows):
    @pl.loop(0, src.shape[0] // step_rows)
    def _(step):
        at = pl.ds(pl.multiple_of(step * step_rows, step_rows), step_rows)
        unit, _ = norm_parts(src[at, :].astype(f32))
        dst[at, :] = (unit * gain + bias).astype(bf16)


def attend_along(qkv_ref, att_ref, q_rows, k_rows, mask):
    low, high = lane_halves(f32)
    for pair in range(HEADS // 2):
        queries = two_heads(qkv_ref[q_rows, pair_cols(0, pair)] * bf16(HEAD ** (-0.5)))
        scores = mul_bt(queries, qkv_ref[k_rows, pair_cols(1, pair)])
        scores = jnp.where(mask, scores, -1e30)
        raised = jnp.exp(scores - jnp.max(scores, axis=-1, keepdims=True))
        probs = (raised * (1.0 / jnp.sum(raised, axis=-1, keepdims=True))).astype(bf16)
        half = probs.shape[0] // 2
        mixed = mul(probs, qkv_ref[k_rows, pair_cols(2, pair)])
        att_ref[q_rows, pair_cols(0, pair)] = (mixed[:half] * low + mixed[half:] * high).astype(bf16)


def attend(qkv_ref, att_ref, q_rows, k_rows, mask, keep_sums):
    for pair in range(HEADS // 2):
        queries = qkv_ref[q_rows, pair_cols(0, pair)] * bf16(HEAD ** (-0.5))
        scores = mul_bt(two_heads(qkv_ref[k_rows, pair_cols(1, pair)]), queries)
        probs, sums = softmax_down(scores, mask)
        vals = two_heads(qkv_ref[k_rows, pair_cols(2, pair)])
        mixed = mul_at(jnp.concatenate(probs, axis=0).astype(bf16), vals)
        att_ref[q_rows, pair_cols(0, pair)] = mixed.astype(bf16)
        for k in range(2):
            keep_sums(2 * pair + k, sums[k])


def text_front_kernel(
    x_ref, g1_ref, b1_ref, wqkv_ref, wo_ref, g2_ref, b2_ref, h1_ref, qkv_ref, att_ref, mid_ref,
    h2_ref, sum_ref, lse_ref
):
    rows, chunk = x_ref.shape[0], 128
    norm_rows(x_ref, h1_ref, g1_ref[...], b1_ref[...], chunk)

    @pl.loop(0, 3 * D // 256)
    def _(step):
        at = pl.ds(pl.multiple_of(step * 256, 256), 256)
        qkv_ref[:, at] = mul(h1_ref[...], wqkv_ref[:, at]).astype(bf16)

    mask = same_sequence(chunk, 0, chunk, 0, TXT_LEN)

    @pl.loop(0, rows // chunk)
    def _(step):
        at = pl.ds(pl.multiple_of(step * chunk, chunk), chunk)

        def keep_sums(head, value):
            lse_ref[pl.ds(step * 16 + head, 1), :] = value

        attend(qkv_ref, att_ref, at, at, mask, keep_sums)

    @pl.loop(0, D // 256)
    def _(step):
        at = pl.ds(pl.multiple_of(step * 256, 256), 256)
        mid_ref[:, at] = x_ref[:, at].astype(f32) + mul(att_ref[...], wo_ref[:, at])

    norm_rows(mid_ref, h2_ref, g2_ref[...], b2_ref[...], chunk)
    per = chunk // TXT_LEN

    @pl.loop(0, rows // chunk)
    def _(step):
        values = mid_ref[pl.ds(pl.multiple_of(step * chunk, chunk), chunk), :]
        sum_ref[pl.ds(pl.multiple_of(step * per, per), per), :] = jnp.sum(
            values.reshape(per, TXT_LEN, D), axis=1
        )


def text_front(rows_in, gain1, bias1, wqkv, wo, gain2, bias2):
    rows = rows_in.shape[0]
    shapes = [
        ((rows, D), bf16),
        ((rows, 3 * D), bf16),
        ((rows, D), bf16),
        ((rows, D), f32),
        ((rows, D), bf16),
        ((rows // TXT_LEN, D), f32),
        ((rows // 128 * 16, 128), f32),
    ]
    return pl.pallas_call(
        text_front_kernel,
        out_shape=[jax.ShapeDtypeStruct(*item) for item in shapes],
        compiler_params=params(),
        cost_estimate=cost(rows * D * D * 8, 14 * D * rows + 8 * D * D, rows * 128 * HEADS),
        name="text_front",
    )(rows_in, gain1[None], bias1[None], wqkv, wo, gain2[None], bias2[None])


def image_front_kernel(
    windows, x_ref, perm_ref, g1_ref, b1_ref, g2_ref, b2_ref, *refs
):
    h2_ref, sum_ref, w_ref, h1_ref, placed_ref, qkv_ref, att_ref, mid_ref, sems = refs[-9:]
    rows, chunk = x_ref.shape[0], 80
    copies, row = [], 0
    for k, piece in enumerate(refs[:-9]):
        place = w_ref.at[pl.ds(row, piece.shape[0]), :]
        copies.append(pltpu.make_async_copy(piece, place, sems.at[k]))
        row += piece.shape[0]
    for copy in copies:
        copy.start()

    def place_columns(src, dst):
        @pl.loop(0, D // 256)
        def _(step):
            at = pl.ds(pl.multiple_of(step * 256, 256), 256)
            dst[:, at] = mul_bt(src[...], perm_ref[at, :]).astype(bf16)

    norm_rows(x_ref, h1_ref, g1_ref[...].astype(f32), b1_ref[...].astype(f32), chunk)
    place_columns(h1_ref, placed_ref)
    for copy in copies:
        copy.wait()

    @pl.loop(0, 3 * D // 256)
    def _(step):
        at = pl.ds(pl.multiple_of(step * 256, 256), 256)
        qkv_ref[:, at] = mul(placed_ref[...], w_ref[:, at]).astype(bf16)

    for row0, count, key0, keys in windows:
        one = same_sequence(count, row0, keys, key0, IMG_LEN)
        mask = jnp.concatenate([one, one], axis=0)
        attend_along(qkv_ref, att_ref, pl.ds(row0, count), pl.ds(key0, keys), mask)
    place_columns(att_ref, placed_ref)

    @pl.loop(0, D // 256)
    def _(step):
        at = pl.ds(pl.multiple_of(step * 256, 256), 256)
        there = pl.ds(pl.multiple_of(step * 256 + 3 * D, 256), 256)
        mid_ref[:, at] = x_ref[:, at].astype(f32) + mul(placed_ref[...], w_ref[:, there])

    norm_rows(mid_ref, h2_ref, g2_ref[...].astype(f32), b2_ref[...].astype(f32), chunk)
    for k in range(rows // IMG_LEN):
        first, last = k * IMG_LEN, (k + 1) * IMG_LEN
        start, end = first // 8 * 8, -(-last // 8) * 8
        values = mid_ref[start:end, :]
        place = lax.broadcasted_iota(jnp.int32, values.shape, 0) + start
        inside = (place >= first) & (place < last)
        sum_ref[k : k + 1, :] = jnp.sum(jnp.where(inside, values, 0.0), axis=0, keepdims=True)


def image_front(rows_in, pieces, perm, gain1, bias1, gain2, bias2):
    rows = rows_in.shape[0]
    windows = ((0, 208, 0, 256), (208, 192, 192, 208))
    vmem = pl.BlockSpec(memory_space=pltpu.VMEM)
    return pl.pallas_call(
        functools.partial(image_front_kernel, windows),
        out_shape=[
            jax.ShapeDtypeStruct((rows, D), bf16),
            jax.ShapeDtypeStruct((rows // IMG_LEN, D), f32),
        ],
        in_specs=[vmem] * 6 + anywhere(pieces),
        out_specs=[vmem] * 2,
        scratch_shapes=[
            pltpu.VMEM((D, 4 * D), bf16),
            pltpu.VMEM((rows, D), bf16),
            pltpu.VMEM((rows, D), bf16),
            pltpu.VMEM((rows, 3 * D), bf16),
            pltpu.VMEM((rows, D), bf16),
            pltpu.VMEM((rows, D), f32),
            pltpu.SemaphoreType.DMA((len(pieces),)),
        ],
        compiler_params=params(),
        cost_estimate=cost(rows * D * D * 12, 8 * D * D, rows * 256 * HEADS),
        name="image_front",
    )(rows_in, perm, gain1[None], bias1[None], gain2[None], bias2[None], *pieces)


def gelu_parts(inner):
    half = 0.5 * (1.0 + lax.erf(inner * (0.5**0.5)))
    return inner * half, half


def pack_kernel(unit_ref, pos_ref, *refs):
    refs[-1][:, :D] = unit_ref[...].astype(bf16)
    refs[-1][:, D:] = pos_ref[...]


def packed(unit, positive, after):
    shape = (unit.shape[0], D + positive.shape[1])
    return pl.pallas_call(
        pack_kernel,
        out_shape=jax.ShapeDtypeStruct(shape, bf16),
        in_specs=[pl.BlockSpec(memory_space=pltpu.VMEM)] * 2 + anywhere(after),
        compiler_params=params(),
        cost_estimate=cost(shape[0] * shape[1], 4 * shape[0] * shape[1]),
        name="packed",
    )(unit, positive, *after)


def pool_matrix(count, rows, row0, seq_len):
    row = (lax.broadcasted_iota(jnp.int32, (count, rows), 1) + row0) // seq_len
    return jnp.where(row == lax.broadcasted_iota(jnp.int32, (count, rows), 0), 1.0, 0.0).astype(bf16)


def two_terms(mean):
    high = mean.astype(bf16)
    low = (mean - high.astype(f32)).astype(bf16)
    return jnp.concatenate([high, low], axis=0)


def unit_rows(pooled):
    inverse = lax.rsqrt(jnp.sum(pooled * pooled, axis=-1, keepdims=True) + norm_eps)
    return pooled * inverse, inverse


def text_up_kernel(h2_ref, wu_ref, wd_ref, sum_ref, *refs):
    slope_ref, hid_ref, unit_ref, inv_ref, acc = refs[-5:]
    step = pl.program_id(0)
    chunk = 128
    per = chunk // TXT_LEN
    pool = pool_matrix(per, chunk, 0, TXT_LEN)
    for k in range(h2_ref.shape[0] // chunk):
        inner = mul(h2_ref[k * chunk : (k + 1) * chunk, :], wu_ref[...])
        value, half = gelu_parts(inner)
        slope = half + inner * (jnp.exp(-0.5 * inner * inner) * 0.3989422804014327)
        slope_ref[k * chunk : (k + 1) * chunk, :] = slope.astype(bf16)
        hid_ref[k * per : (k + 1) * per, :] = mul(pool, value.astype(bf16))
    terms = mul(two_terms(hid_ref[...] * (1.0 / TXT_LEN)), wd_ref[...])
    count = hid_ref.shape[0]
    added = terms[:count] + terms[count:]

    @pl.when(step == 0)
    def _():
        acc[...] = sum_ref[...] * (1.0 / TXT_LEN) + added

    @pl.when(step > 0)
    def _():
        acc[...] += added

    @pl.when(step == pl.num_programs(0) - 1)
    def _():
        unit, inverse = unit_rows(acc[...])
        unit_ref[...] = unit
        inv_ref[...] = jnp.broadcast_to(inverse, inv_ref.shape)


def text_up(normed2, weight_up, weight_down, middle_sum, after=()):
    rows, count = normed2.shape[0], middle_sum.shape[0]
    fixed = lambda shape: pl.BlockSpec(shape, lambda i: (0, 0))
    return pl.pallas_call(
        text_up_kernel,
        grid=(FF // TILE,),
        out_shape=[
            jax.ShapeDtypeStruct((rows, FF), bf16),
            jax.ShapeDtypeStruct((count, FF), f32),
            jax.ShapeDtypeStruct((count, D), f32),
            jax.ShapeDtypeStruct((count, 128), f32),
        ],
        in_specs=[
            fixed((rows, D)),
            pl.BlockSpec((D, TILE), lambda i: (0, i)),
            pl.BlockSpec((TILE, D), lambda i: (i, 0)),
            fixed((count, D)),
        ]
        + anywhere(after),
        out_specs=[
            pl.BlockSpec((rows, TILE), lambda i: (0, i)),
            pl.BlockSpec((count, TILE), lambda i: (0, i)),
            fixed((count, D)),
            fixed((count, 128)),
        ],
        scratch_shapes=[pltpu.VMEM((count, D), f32)],
        compiler_params=params(),
        cost_estimate=cost(2 * rows * D * FF, 4 * D * FF + 2 * rows * FF, 20 * rows * FF),
        name="text_up",
    )(normed2, weight_up, weight_down, middle_sum, *after)


def image_up_kernel(fold, h2_ref, wu_ref, wd_ref, sum_ref, *refs):
    out_ref, acc = refs[-2:]
    step = pl.program_id(0)
    rows, count = h2_ref.shape[0], sum_ref.shape[0]
    chunk = 80
    summed = jnp.zeros((count, TILE), f32)
    for k in range(rows // chunk):
        inner = mul(h2_ref[k * chunk : (k + 1) * chunk, :], wu_ref[...])
        value, _ = gelu_parts(inner)
        pool = pool_matrix(count, chunk, k * chunk, IMG_LEN)
        summed = summed + mul(pool, value.astype(bf16))
    mean = two_terms(summed * (1.0 / IMG_LEN))
    place = lax.broadcasted_iota(jnp.int32, (TILE, TILE // fold), 0)
    picked = lax.broadcasted_iota(jnp.int32, (TILE, TILE // fold), 1) * fold
    terms = jnp.zeros((2 * count, D), f32)
    for k in range(fold):
        chosen = jnp.where(place == picked + k, 1.0, 0.0).astype(bf16)
        part = mul(mean, chosen).astype(bf16)
        terms = terms + mul(part, wd_ref[:, k * D : (k + 1) * D])
    added = terms[:count] + terms[count:]

    @pl.when(step == 0)
    def _():
        acc[...] = sum_ref[...] * (1.0 / IMG_LEN) + added

    @pl.when(step > 0)
    def _():
        acc[...] += added

    @pl.when(step == pl.num_programs(0) - 1)
    def _():
        out_ref[...] = unit_rows(acc[...])[0].astype(bf16)


def image_up(normed2, whole, up_col, down_col, middle_sum, after=()):
    rows, count = normed2.shape[0], middle_sum.shape[0]
    fold = FF // D
    fixed = lambda shape: pl.BlockSpec(shape, lambda i: (0, 0))
    return pl.pallas_call(
        functools.partial(image_up_kernel, fold),
        grid=(FF // TILE,),
        out_shape=jax.ShapeDtypeStruct((count, D), bf16),
        in_specs=[
            fixed((rows, D)),
            pl.BlockSpec((D, TILE), lambda i: (0, up_col // TILE + i)),
            pl.BlockSpec((TILE // fold, fold * D), lambda i: (i, down_col // (fold * D))),
            fixed((count, D)),
        ]
        + anywhere(after),
        out_specs=fixed((count, D)),
        scratch_shapes=[pltpu.VMEM((count, D), f32)],
        compiler_params=params(),
        cost_estimate=cost(2 * rows * D * FF, 4 * D * FF, 15 * rows * FF),
        name="image_up",
    )(normed2, whole, whole, middle_sum, *after)


def left_kernel(order_ref, h2_ref, h1_ref, att_ref, up_ref, rest_ref):
    step = pl.program_id(0)

    @pl.when(step < 2)
    def _():
        up_ref[0] = placed(order_ref[0], h2_ref[...])

    @pl.when((step == 2) | (step == 3))
    def _():
        rest_ref[0] = placed(order_ref[0], h1_ref[...])

    @pl.when(step == 4)
    def _():
        rest_ref[0] = placed(order_ref[0], att_ref[...])


def left_factors(orders, normed2, normed1, attended):
    rows = normed1.shape[0]
    fixed = pl.BlockSpec((rows, D), lambda i: (0, 0))
    return pl.pallas_call(
        left_kernel,
        grid=(5,),
        out_shape=[
            jax.ShapeDtypeStruct((2, D, rows), bf16),
            jax.ShapeDtypeStruct((3, D, rows), bf16),
        ],
        in_specs=[
            pl.BlockSpec((1, D, D), lambda i: (jnp.minimum(i % 2 + i // 4, 1), 0, 0)),
            fixed,
            fixed,
            fixed,
        ],
        out_specs=[
            pl.BlockSpec((1, D, rows), lambda i: (jnp.minimum(i, 1), 0, 0)),
            pl.BlockSpec((1, D, rows), lambda i: (jnp.maximum(i - 2, 0), 0, 0)),
        ],
        compiler_params=params(),
        cost_estimate=cost(10 * rows * D * D, 16 * rows * D + 10 * D * D),
        name="left_factors",
    )(orders, normed2, normed1, attended)


def loss_parts(text_rows, pos, image_all):
    similar = mul_bt(text_rows, image_all) * logit_scale
    shifted = jnp.exp(similar - logit_scale)
    alive = jnp.max(pos, axis=1, keepdims=True)
    row_sum = jnp.sum(shifted, axis=1, keepdims=True)
    row_count = jnp.maximum(jnp.sum(pos, axis=1, keepdims=True), 1.0)
    return similar, shifted, alive, row_sum, row_count


def sums_over_captions(text_rows, pos, image_all):
    similar, shifted, alive, row_sum, row_count = loss_parts(text_rows, pos, image_all)
    pos_similar = pos * similar
    cap_term = alive * (
        logit_scale + jnp.log(row_sum) - jnp.sum(pos_similar, axis=1, keepdims=True) / row_count
    )
    return (
        jnp.sum(alive * shifted, axis=0, keepdims=True),
        jnp.sum(pos, axis=0, keepdims=True),
        jnp.sum(pos_similar, axis=0, keepdims=True),
        jnp.sum(cap_term, axis=0, keepdims=True),
        jnp.sum(alive, axis=0, keepdims=True),
    )


def loss_from(sums):
    col_sum, col_count, col_pos, cap_total, live_total = sums
    img_term = logit_scale + jnp.log(col_sum) - col_pos / col_count
    return 0.5 * cap_total / live_total + 0.5 * jnp.mean(img_term, axis=1, keepdims=True)


def grad_of_unit(text_rows, pos, image_all, col_sum, col_count, live_total):
    _, shifted, alive, row_sum, row_count = loss_parts(text_rows, pos, image_all)
    cap_share, img_share = 0.5 / live_total, 0.5 / image_all.shape[0]
    grad_sims = alive * shifted * (cap_share / row_sum + img_share / col_sum) - pos * (
        cap_share / row_count + img_share / col_count
    )
    return mul(grad_sims.astype(bf16), image_all) * logit_scale


def turned(grad, unit):
    return grad - unit * jnp.sum(grad * unit, axis=-1, keepdims=True)


def loss_kernel(
    pack_ref, image_ref, own_ref, unit_ref, inv_ref, loss_ref, row_ref, low_ref, col_sum_ref,
    col_count_ref, live_ref
):
    image_all = image_ref[...]
    chunk = 256
    total = None
    for k in range(pack_ref.shape[0] // chunk):
        at = slice(k * chunk, (k + 1) * chunk)
        part = sums_over_captions(pack_ref[at, :D], pack_ref[at, D:].astype(f32), image_all)
        total = part if total is None else [a + b for a, b in zip(total, part)]
    loss_ref[...] = jnp.broadcast_to(loss_from(total), loss_ref.shape)
    col_sum, col_count, _, _, live_total = total
    col_sum_ref[...] = col_sum
    col_count_ref[...] = col_count
    live_ref[...] = jnp.broadcast_to(live_total, live_ref.shape)
    grad = grad_of_unit(
        own_ref[:, :D], own_ref[:, D:].astype(f32), image_all, col_sum, col_count, live_total
    )
    row = inv_ref[:, :1] * turned(grad, unit_ref[...]) * (1.0 / TXT_LEN)
    row_ref[...] = row
    low_ref[...] = row.astype(bf16)


def loss_and_rows(pack, image_all, own_pack, unit, inverse):
    images, count = image_all.shape[0], own_pack.shape[0]
    shapes = [(1, 128), (count, D), (count, D), (1, images), (1, images), (1, 128)]
    kinds = [f32, f32, bf16, f32, f32, f32]
    return pl.pallas_call(
        loss_kernel,
        out_shape=[jax.ShapeDtypeStruct(*item) for item in zip(shapes, kinds)],
        compiler_params=params(),
        cost_estimate=cost(2 * pack.shape[0] * images * D, 2 * pack.size, pack.shape[0] * images),
        name="loss_and_rows",
    )(pack, image_all, own_pack, unit, inverse)


def down_kernel(pack_ref, image_ref, col_sum_ref, col_count_ref, live_ref, hid_ref, *refs):
    step, out_ref = pl.program_id(0), refs[-1]
    text_rows = pack_ref[:, :D]
    grad = grad_of_unit(
        text_rows, pack_ref[:, D:].astype(f32), image_ref[...], col_sum_ref[...],
        col_count_ref[...], live_ref[:, :1]
    )
    rows = (turned(grad, text_rows.astype(f32)) * (1.0 / TXT_LEN)).astype(bf16)
    part = mul_at(hid_ref[...], rows)

    @pl.when(step == 0)
    def _():
        out_ref[...] = part

    @pl.when(step > 0)
    def _():
        out_ref[...] += part


def grad_of_down(pack, image_all, col_sum, col_count, live_total, hidden_cols, after):
    images, chunk = image_all.shape[0], 256
    fixed = lambda shape: pl.BlockSpec(shape, lambda i: (0, 0))
    per = hidden_cols.shape[1]
    return pl.pallas_call(
        down_kernel,
        grid=(pack.shape[0] // chunk,),
        out_shape=jax.ShapeDtypeStruct((per, D), f32),
        in_specs=[
            pl.BlockSpec((chunk, pack.shape[1]), lambda i: (i, 0)),
            fixed((images, D)), fixed((1, images)), fixed((1, images)), fixed((1, 128)),
            pl.BlockSpec((chunk, per), lambda i: (i, 0)),
        ]
        + anywhere(after),
        out_specs=fixed((per, D)),
        compiler_params=params(),
        cost_estimate=cost(4 * pack.shape[0] * images * D, 2 * pack.size, pack.shape[0] * images),
        name="grad_of_down",
    )(pack, image_all, col_sum, col_count, live_total, hidden_cols, *after)


def mlp_back_kernel(
    low_ref, wd_ref, slope_ref, wu_ref, lhs_ref, mid_ref, gain_ref, row_ref, keep_a, send_a, keep_b,
    send_b, out_ref, gain_out, bias_out
):
    count, rows = low_ref.shape[0], slope_ref.shape[0]
    half, steps = D // 2, FF // 2 // TILE
    for k, (keep, send) in enumerate(((keep_a, send_a), (keep_b, send_b))):

        @pl.loop(0, steps)
        def _(step, k=k, keep=keep, send=send):
            at = pl.ds(pl.multiple_of(k * (FF // 2) + step * TILE, TILE), TILE)
            there = pl.ds(pl.multiple_of(step * TILE, TILE), TILE)
            hidden = mul_bt(low_ref[...], wd_ref[at, :])
            wide = jnp.broadcast_to(hidden[:, None, :], (count, TXT_LEN, TILE))
            inner = (wide.reshape(rows, TILE) * slope_ref[:, at].astype(f32)).astype(bf16)
            weight = mul(lhs_ref[k], inner).astype(bf16)
            keep[:, there] = weight[:half]
            send[:, there] = weight[half:]
            added = mul_bt(inner, wu_ref[:, at])
            if k == 0:

                @pl.when(step == 0)
                def _():
                    out_ref[...] = added

                @pl.when(step > 0)
                def _():
                    out_ref[...] += added
            else:
                out_ref[...] += added

    chunk = 128
    per = chunk // TXT_LEN
    gain = gain_ref[...]
    gain_out[...] = jnp.zeros_like(gain_out)
    bias_out[...] = jnp.zeros_like(bias_out)

    @pl.loop(0, rows // chunk)
    def _(k):
        at = pl.ds(pl.multiple_of(k * chunk, chunk), chunk)
        unit, scale = norm_parts(mid_ref[at, :])
        grad = out_ref[at, :]
        gain_out[...] += jnp.sum(grad * unit, axis=0, keepdims=True)
        bias_out[...] += jnp.sum(grad, axis=0, keepdims=True)
        row = row_ref[pl.ds(pl.multiple_of(k * per, per), per), :]
        row = jnp.broadcast_to(row[:, None, :], (per, TXT_LEN, D)).reshape(chunk, D)
        out_ref[at, :] = row + norm_back(unit, scale, gain, grad)


def mlp_back(grad_row, grad_low, weight_down, slope, weight_up, lhs, middle, gain):
    rows = slope.shape[0]
    line = jax.ShapeDtypeStruct((1, D), f32)
    return pl.pallas_call(
        mlp_back_kernel,
        out_shape=[stays((D // 2, FF // 2), bf16)] * 4 + [stays((rows, D), f32), line, line],
        in_specs=in_vmem(8),
        out_specs=in_vmem(7),
        compiler_params=params(16 << 20),
        cost_estimate=cost(4 * rows * D * FF, 4 * D * FF + 2 * rows * FF + 2 * D * FF, rows * FF),
        name="mlp_back",
    )(grad_low, weight_down, slope, weight_up, lhs, middle, gain[None], grad_row)


def attention_back_kernel(first, grad_ref, wo_ref, qkv_ref, lse_ref, *refs):
    low_ref, out_ref = refs[-2:]
    chunk = 128
    mask = same_sequence(chunk, 0, chunk, 0, TXT_LEN)

    @pl.loop(0, low_ref.shape[0] // chunk)
    def _(step):
        here = pl.ds(pl.multiple_of((first + step) * chunk, chunk), chunk)
        there = pl.ds(pl.multiple_of(step * chunk, chunk), chunk)
        sums = lse_ref[pl.ds(pl.multiple_of((first + step) * 16, 16), 16), :]
        low = grad_ref[here, :].astype(bf16)
        low_ref[there, :] = low
        grad_att = mul_bt(low, wo_ref[...]).astype(bf16)
        for pair in range(HEADS // 2):
            queries = qkv_ref[here, pair_cols(0, pair)] * bf16(HEAD ** (-0.5))
            keys = two_heads(qkv_ref[here, pair_cols(1, pair)])
            vals = two_heads(qkv_ref[here, pair_cols(2, pair)])
            grads = grad_att[:, pair_cols(0, pair)]
            scores, grad_probs = mul_bt(keys, queries), mul_bt(vals, grads)
            probs, grad_scores = [], []
            for k in range(2):
                at = slice(k * chunk, (k + 1) * chunk)
                head = 2 * pair + k
                shifted = scores[at] - sums[head : head + 1, :]
                prob = jnp.where(mask, jnp.exp(jnp.where(mask, shifted, 0.0)), 0.0)
                along = jnp.sum(grad_probs[at] * prob, axis=0, keepdims=True)
                grad_scores.append((prob * (grad_probs[at] - along)).astype(bf16))
                probs.append(prob.astype(bf16))
            grad_q = mul_at(jnp.concatenate(grad_scores, axis=0), keys) * HEAD ** (-0.5)
            grad_k = mul(jnp.concatenate(grad_scores, axis=1), two_heads(queries))
            grad_v = mul(jnp.concatenate(probs, axis=1), two_heads(grads))
            out_ref[there, pair_cols(0, pair)] = grad_q.astype(bf16)
            out_ref[there, pair_cols(1, pair)] = grad_k.astype(bf16)
            out_ref[there, pair_cols(2, pair)] = grad_v.astype(bf16)


def attention_back(grad_middle, weight_out, project, log_sums, first, count, after=()):
    rows = count * 128
    return pl.pallas_call(
        functools.partial(attention_back_kernel, first),
        out_shape=[stays((rows, D), bf16), stays((rows, 3 * D), bf16)],
        in_specs=in_vmem(4) + anywhere(after),
        out_specs=in_vmem(2),
        compiler_params=params(16 << 20),
        cost_estimate=cost(10 * rows * D * D, 16 * rows * D + 2 * D * D, rows * 128 * HEADS),
        name="attention_back",
    )(grad_middle, weight_out, project, log_sums, *after)


def mul_rows(lhs, parts, cols):
    total, row = 0.0, 0
    for part in parts:
        total = total + mul(lhs[:, row : row + part.shape[0]], part[:, cols])
        row += part.shape[0]
    return total


def weight_back_kernel(factors, groups, lhs_ref, *refs):
    keep, send = refs[-2:]
    half = D // 2
    for k, (factor, group, col) in enumerate(factors):
        parts = refs[sum(groups[:group]) : sum(groups[: group + 1])]
        weight = mul_rows(lhs_ref.at[factor], parts, slice(col * D, (col + 1) * D)).astype(bf16)
        at = slice(k * D, (k + 1) * D)
        keep[:, at] = weight[:half]
        send[:, at] = weight[half:]


def weight_back(lhs, groups, factors, after=()):
    rows = lhs.shape[2]
    given = [part for group in groups for part in group]
    return pl.pallas_call(
        functools.partial(weight_back_kernel, factors, [len(group) for group in groups]),
        out_shape=[stays((D // 2, len(factors) * D), bf16)] * 2,
        in_specs=in_vmem(1 + len(given)) + anywhere(after),
        out_specs=in_vmem(2),
        compiler_params=params(16 << 20),
        cost_estimate=cost(4 * rows * D * D, 4 * rows * D + 7 * D * D),
        name="weight_back",
    )(lhs, *given, *after)


def input_back_kernel(count, *refs):
    projs = refs[:count]
    w_ref, x_ref, gain_ref, mid_ref = refs[count : count + 4]
    out_ref, gain_out, bias_out = refs[-3:]
    rows, chunk = x_ref.shape[0], 128

    @pl.loop(0, D // 256)
    def _(step):
        at = pl.ds(pl.multiple_of(step * 256, 256), 256)
        row = 0
        for part in projs:
            there = slice(row, row + part.shape[0])
            out_ref[there, at] = mul_bt(part[...], w_ref[at, :])
            row += part.shape[0]

    gain = gain_ref[...]
    gain_out[...] = jnp.zeros_like(gain_out)
    bias_out[...] = jnp.zeros_like(bias_out)

    @pl.loop(0, rows // chunk)
    def _(k):
        at = pl.ds(pl.multiple_of(k * chunk, chunk), chunk)
        unit, scale = norm_parts(x_ref[at, :].astype(f32))
        grad = out_ref[at, :]
        gain_out[...] += jnp.sum(grad * unit, axis=0, keepdims=True)
        bias_out[...] += jnp.sum(grad, axis=0, keepdims=True)
        out_ref[at, :] = mid_ref[at, :] + norm_back(unit, scale, gain, grad)


def input_back(grad_projs, weight, rows_in, gain, grad_middle, after=()):
    rows = rows_in.shape[0]
    line = jax.ShapeDtypeStruct((1, D), f32)
    return pl.pallas_call(
        functools.partial(input_back_kernel, len(grad_projs)),
        out_shape=[jax.ShapeDtypeStruct((rows, D), f32), line, line],
        in_specs=in_vmem(len(grad_projs) + 4) + anywhere(after),
        out_specs=in_vmem(3),
        compiler_params=params(16 << 20),
        cost_estimate=cost(6 * rows * D * D, 14 * rows * D + 6 * D * D),
        name="input_back",
    )(*grad_projs, weight, rows_in, gain[None], grad_middle, *after)


def local(
    images,
    captions,
    img_gain1,
    img_bias1,
    img_qkv,
    img_out,
    img_gain2,
    img_bias2,
    img_up,
    img_down,
    txt_gain1,
    txt_bias1,
    txt_qkv,
    txt_out,
    txt_gain2,
    txt_bias2,
    txt_up,
    txt_down,
    counts,
    matches,
):
    peers = lax.axis_size(AXIS)
    own = lax.axis_index(AXIS)
    per = D // peers
    img_local = counts.shape[0]
    cap_local = matches.shape[0]
    total_images = matches.shape[1]

    whole = lax.all_gather(
        jnp.concatenate([img_up.reshape(per, FF), img_down.reshape(per, FF)], axis=1),
        AXIS,
        axis=0,
        tiled=True,
    )
    small = peers == 32
    shard = jnp.concatenate([img_qkv.reshape(per, 3 * D), img_out.reshape(per, D)], axis=1)
    if small:
        line, perm = gathered_line(shard), row_order((1, 4, 2, 16, 8))
    else:
        line, perm = lax.all_gather(shard, AXIS, axis=0, tiled=True), jnp.eye(D, dtype=bf16)

    normed1, project, attended, middle, normed2, middle_sum, log_sums = text_front(
        captions, txt_gain1, txt_bias1, txt_qkv, txt_out, txt_gain2, txt_bias2
    )
    middle_sum, line = in_turn(middle_sum, line)
    beside, above = (swapped(line, 2), swapped(line, 4)) if small else (line, line)
    slope, hidden_sum, text_unit, inverse = text_up(
        normed2, txt_up, txt_down, middle_sum, (line,)
    )
    text_unit, (beside, above) = in_turn(text_unit, (beside, above))

    ends_at = jnp.cumsum(counts)
    slot_ids = lax.iota(jnp.int32, cap_local)
    owner = jnp.sum((ends_at[None, :] <= slot_ids[:, None]).astype(jnp.int32), axis=1)
    owner = owner + own * img_local
    live = slot_ids < ends_at[-1]
    columns = lax.iota(jnp.int32, total_images)
    positive = ((matches > 0) | (owner[:, None] == columns[None, :])) & live[:, None]

    own_pack = packed(text_unit, positive.astype(bf16), ())
    pieces = [line]
    if small:
        held = own_pack[None]
        first, second = diagonal(beside, above)
        others = [swapped(held, mask) for mask in (8, 16, 24)]
        scaled_sum = (hidden_sum * inverse[:, :1]).astype(bf16)
        hidden_cols = lax.all_to_all(scaled_sum, AXIS, split_axis=1, concat_axis=0, tiled=True)
        others, first, second, hidden_cols = lax.optimization_barrier(
            (others, first, second, hidden_cols)
        )
        held = joined(joined(held, others[0], 8), joined(others[1], others[2], 8), 16, 1)
        text_beside, text_above = swapped(held, 2), swapped(held, 4)
        pieces = [line, beside, above, first, second]
        pieces = pieces + [swapped(piece, 1) for piece in pieces]

    normed_img, middle_img = image_front(
        images, pieces, perm, img_gain1, img_bias1, img_gain2, img_bias2
    )
    if small:
        normed_img, text_beside, text_above = lax.optimization_barrier(
            (normed_img, text_beside, text_above)
        )
        across = jnp.concatenate(diagonal(text_beside, text_above), axis=0)
        held = joined(joined(held, text_beside, 2), joined(text_above, across, 2), 4, 4)

    order_a, order_b, tail = stage_orders()
    orders = jnp.stack([row_order(order_a + tail[::-1]), row_order(order_b + tail[::-1])])
    if small:
        whole, held, orders = lax.optimization_barrier((whole, held, orders))
        other = swapped(held, 1)
    image_low = image_up(normed_img, whole, 0, FF, middle_img)
    if small:
        text_pack = joined(held, other, 1).reshape(-1, D + total_images)
    image_low, normed2 = in_turn(image_low, normed2)
    image_all = spread(image_low).reshape(total_images, D)
    lhs_up, lhs_rest = left_factors(orders, normed2, normed1, attended)
    image_all, lhs_up = in_turn(image_all, lhs_up)

    if small:
        loss_value, grad_row, row_low, col_sum, col_count, live_total = loss_and_rows(
            text_pack, image_all, own_pack, text_unit, inverse
        )
        loss_value = loss_value[0, 0]
    else:
        text_low, pos = own_pack[:, :D], own_pack[:, D:].astype(f32)
        sums = lax.psum(sums_over_captions(text_low, pos, image_all), AXIS)
        loss_value = loss_from(sums)[0, 0]
        grad = grad_of_unit(text_low, pos, image_all, sums[0], sums[1], sums[4])
        grad_row = inverse[:, :1] * turned(grad, text_unit) * (1.0 / TXT_LEN)
        row_low = grad_row.astype(bf16)

    *up, grad_middle, gain_two, bias_two = mlp_back(
        grad_row, row_low, txt_down, slope, txt_up, lhs_up, middle, txt_gain2
    )
    stages = len(order_a)
    low_one, proj_one = attention_back(grad_middle, txt_out, project, log_sums, 0, 1)
    for stage in range(stages - 2):
        up = fold(hand_on(up, stage), (proj_one,))
    low_two, proj_two = attention_back(grad_middle, txt_out, project, log_sums, 1, 4, up)
    up = fold(hand_on(up, stages - 2), (proj_two,))
    projs, lows = (proj_one, proj_two), (low_one, low_two)
    rest_a = weight_back(lhs_rest, [projs], [(0, 0, 0), (0, 0, 1)], up)
    up = hand_on_last(fold_last(hand_on(up, stages - 1), rest_a[1:]))
    rest_b = weight_back(lhs_rest, [projs, lows], [(1, 0, 2), (2, 1, 0)], up[:1])
    rest = [*rest_a, *rest_b]
    for stage in range(stages - 2):
        rest = fold(hand_on(rest, stage))
    caption_grad, gain_one, bias_one = input_back(
        projs, txt_qkv, captions, txt_gain1, grad_middle, rest[:1]
    )
    caption_grad, up = in_turn(caption_grad, up)
    rest = fold(hand_on(rest, stages - 2), (caption_grad,))
    norms = jnp.concatenate([gain_one, bias_one, gain_two, bias_two], axis=0)
    norms, rest = in_turn(norms, rest)
    norms = jnp.sum(spread(norms[None].astype(bf16)).astype(f32), axis=0).reshape(4, D)
    rest = fold_last(hand_on(rest, stages - 1))
    if small:
        grad_down = grad_of_down(
            text_pack, image_all, col_sum, col_count, live_total, hidden_cols, (rest[0], norms)
        )
    else:
        grad_down = lax.psum_scatter(
            mul_at(hidden_sum.astype(bf16), row_low), AXIS, scatter_dimension=0, tiled=True
        )
    grad_down, rest = in_turn(grad_down, hand_on_last(rest))
    up_share = sum_last(*up)
    rest_share = sum_last(*rest)
    return (
        loss_value,
        caption_grad,
        norms[0],
        norms[1],
        rest_share[:, : 3 * D].reshape(-1),
        rest_share[:, 3 * D :].reshape(-1),
        norms[2],
        norms[3],
        up_share.reshape(-1),
        grad_down.reshape(-1),
    )


def solution(mesh):
    split, flat, whole = P("blk", None), P("blk"), P()
    image_block = (whole, whole, flat, flat, whole, whole, flat, flat)
    return jax.shard_map(
        local,
        mesh=mesh,
        in_specs=(split, split) + image_block + (whole,) * 8 + (flat, split),
        out_specs=(whole, split, whole, whole, flat, flat, whole, whole, flat, flat),
        check_vma=False,
    )
```

```python
import functools

import jax
import jax.numpy as jnp
from jax import lax
from jax.experimental import pallas as pl
from jax.experimental.pallas import tpu as pltpu
from jax.sharding import PartitionSpec as P

D = 768
FF = 3072
HEAD = 64
HEADS = D // HEAD
IMG_LEN = 50
TXT_LEN = 16
AXIS = "blk"

norm_eps = 1e-06
logit_scale = 50.0
f32 = jnp.float32
bf16 = jnp.bfloat16


def swapped(value, mask):
    peers = lax.axis_size(AXIS)
    return lax.ppermute(value, AXIS, [(i, i ^ mask) for i in range(peers)])


def bit_masks():
    peers = lax.axis_size(AXIS)
    return [1 << k for k in range(peers.bit_length() - 1)]


def joined(held, other, mask, outer=None):
    upper = (lax.axis_index(AXIS) & mask) > 0
    first = jnp.where(upper, other, held)
    second = jnp.where(upper, held, other)
    outer = held.shape[0] if outer is None else outer
    parts = [part.reshape((outer, -1) + held.shape[1:]) for part in (first, second)]
    return jnp.stack(parts, axis=1).reshape((-1,) + held.shape[1:])


def spread(block):
    peers = lax.axis_size(AXIS)
    copies = jnp.broadcast_to(block[None], (peers,) + block.shape)
    return lax.all_to_all(copies, AXIS, split_axis=0, concat_axis=0, tiled=True)


def stage_orders():
    masks = bit_masks()
    head, tail = masks[:-2], masks[-2:]
    order_a = list(head)
    order_b = list(head)
    for k in range(1, len(head) - 1, 2):
        order_b[k], order_b[k + 1] = order_b[k + 1], order_b[k]
    return order_a, order_b, tail


def row_order(bits):
    peers = lax.axis_size(AXIS)
    own = lax.axis_index(AXIS)
    per = D // peers
    places = lax.iota(jnp.int32, D)
    block = places // per
    target = jnp.zeros_like(block) + own
    for k, mask in enumerate(bits):
        target = target ^ (((block >> (len(bits) - 1 - k)) & 1) * mask)
    source = target * per + places % per
    return (source[:, None] == lax.iota(jnp.int32, D)[None, :]).astype(bf16)


def gathered_line(shard):
    return jnp.concatenate([shard] + [swapped(shard, mask) for mask in (8, 16, 24)], axis=0)


def diagonal(beside, above):
    half = beside.shape[0] // 2
    return swapped(beside[:half], 4), swapped(above[half:], 2)


def in_turn(first, then):
    return lax.optimization_barrier((first, then))


def placed(order, values):
    return mul_bt(order, values).astype(bf16)


def hand_on(parts, stage):
    order_a, order_b, _ = stage_orders()
    keep_a, send_a, keep_b, send_b = parts
    return keep_a, swapped(send_a, order_a[stage]), keep_b, swapped(send_b, order_b[stage])


def hand_on_last(blocks):
    low, high = stage_orders()[2]
    own, *others = blocks
    return own, [swapped(block, mask) for block, mask in zip(others, (low, high, low | high))]


def sum_last(own, others):
    total = own
    for other in others:
        total = total + other.astype(f32)
    return total


VMEM_BYTES = 56 << 20
TILE = 512


def norm_parts(values):
    average = jnp.mean(values, axis=-1, keepdims=True)
    centred = values - average
    variance = jnp.mean(centred * centred, axis=-1, keepdims=True)
    scale = lax.rsqrt(variance + norm_eps)
    return centred * scale, scale


def norm_back(unit, scale, gain, grad):
    inner = grad * gain
    shift = jnp.mean(inner, axis=-1, keepdims=True)
    along = jnp.mean(inner * unit, axis=-1, keepdims=True)
    return scale * (inner - shift - unit * along)


def mul(lhs, rhs):
    return jnp.dot(lhs, rhs, preferred_element_type=f32)


def mul_bt(lhs, rhs):
    return lax.dot_general(lhs, rhs, (((1,), (1,)), ((), ())), preferred_element_type=f32)


def mul_at(lhs, rhs):
    return lax.dot_general(lhs, rhs, (((0,), (0,)), ((), ())), preferred_element_type=f32)


def params(limit=VMEM_BYTES):
    return pltpu.CompilerParams(vmem_limit_bytes=limit)


def in_vmem(count):
    return [pl.BlockSpec(memory_space=pltpu.VMEM)] * count


def stays(shape, dtype):
    return pltpu.VMEM(shape, dtype)


def cost(flops, moved, transcendentals=0):
    return pl.CostEstimate(flops=flops, bytes_accessed=moved, transcendentals=transcendentals)


def lane_halves(dtype):
    lane = lax.broadcasted_iota(jnp.int32, (1, 2 * HEAD), 1)
    low = jnp.where(lane < HEAD, 1.0, 0.0)
    return low.astype(dtype), (1.0 - low).astype(dtype)


def two_heads(pair):
    low, high = lane_halves(bf16)
    return jnp.concatenate([pair * low, pair * high], axis=0)


def same_sequence(rows, row0, cols, col0, seq_len):
    row = (lax.broadcasted_iota(jnp.int32, (rows, cols), 0) + row0) // seq_len
    col = (lax.broadcasted_iota(jnp.int32, (rows, cols), 1) + col0) // seq_len
    return row == col


def softmax_down(scores, mask):
    keys = mask.shape[0]
    parts, sums = [], []
    for k in range(2):
        part = jnp.where(mask, scores[k * keys : (k + 1) * keys], -1e30)
        most = jnp.max(part, axis=0, keepdims=True)
        raised = jnp.exp(part - most)
        total = jnp.sum(raised, axis=0, keepdims=True)
        parts.append(raised * (1.0 / total))
        sums.append(most + jnp.log(total))
    return parts, sums


def fold_kernel(keep_a, got_a, keep_b, got_b, *refs):
    outs = refs[-4:]
    half, tile = outs[0].shape[0], 256

    @pl.loop(0, keep_a.shape[1] // tile)
    def _(step):
        cols = pl.ds(pl.multiple_of(step * tile, tile), tile)
        for k, (kept, got) in enumerate(((keep_a, got_a), (keep_b, got_b))):
            for j in range(2):
                at = slice(j * half, (j + 1) * half)
                total = kept[at, cols].astype(f32) + got[at, cols].astype(f32)
                outs[2 * k + j][:, cols] = total.astype(bf16)


def fold(parts, after=()):
    rows, cols = parts[0].shape
    if rows % 32:
        whole = [
            (kept.astype(f32) + got.astype(f32)).astype(bf16)
            for kept, got in (parts[:2], parts[2:])
        ]
        return [part for one in whole for part in (one[: rows // 2], one[rows // 2 :])]
    return pl.pallas_call(
        fold_kernel,
        out_shape=[stays((rows // 2, cols), bf16)] * 4,
        in_specs=in_vmem(4) + anywhere(after),
        out_specs=in_vmem(4),
        compiler_params=params(8 << 20),
        cost_estimate=cost(2 * rows * cols, 12 * rows * cols),
        name="fold",
    )(*parts, *after)


def fold_last_kernel(keep_a, got_a, keep_b, got_b, *refs):
    own_ref, *outs = refs[-4:]
    rows = own_ref.shape[0]
    cols = keep_a.shape[1]
    for k, (kept, got) in enumerate(((keep_a, got_a), (keep_b, got_b))):
        total = kept[...].astype(f32) + got[...].astype(f32)
        at = slice(k * cols, (k + 1) * cols)
        own_ref[:, at] = total[:rows]
        for j, out in enumerate(outs):
            out[:, at] = total[(j + 1) * rows : (j + 2) * rows].astype(bf16)


def fold_last(parts, after=()):
    rows, cols = parts[0].shape
    shape = (rows // 4, 2 * cols)
    if rows % 32:
        pairs = (parts[:2], parts[2:])
        both = [kept.astype(f32) + got.astype(f32) for kept, got in pairs]
        own, *others = jnp.split(jnp.concatenate(both, axis=1), 4)
        return [own] + [other.astype(bf16) for other in others]
    return pl.pallas_call(
        fold_last_kernel,
        out_shape=[stays(shape, f32)] + [stays(shape, bf16)] * 3,
        in_specs=in_vmem(4) + anywhere(after),
        out_specs=in_vmem(4),
        compiler_params=params(8 << 20),
        cost_estimate=cost(2 * rows * cols, 12 * rows * cols),
        name="fold_last",
    )(*parts, *after)


def anywhere(after):
    return [pl.BlockSpec(memory_space=pl.ANY)] * len(after)


def pair_cols(part, pair):
    start = part * D + pair * 2 * HEAD
    return slice(start, start + 2 * HEAD)


def norm_rows(src, dst, gain, bias, step_rows):
    @pl.loop(0, src.shape[0] // step_rows)
    def _(step):
        at = pl.ds(pl.multiple_of(step * step_rows, step_rows), step_rows)
        unit, _ = norm_parts(src[at, :].astype(f32))
        dst[at, :] = (unit * gain + bias).astype(bf16)


def attend_along(qkv_ref, att_ref, q_rows, k_rows, mask):
    low, high = lane_halves(f32)
    for pair in range(HEADS // 2):
        queries = two_heads(qkv_ref[q_rows, pair_cols(0, pair)] * bf16(HEAD ** (-0.5)))
        scores = mul_bt(queries, qkv_ref[k_rows, pair_cols(1, pair)])
        scores = jnp.where(mask, scores, -1e30)
        raised = jnp.exp(scores - jnp.max(scores, axis=-1, keepdims=True))
        probs = (raised * (1.0 / jnp.sum(raised, axis=-1, keepdims=True))).astype(bf16)
        half = probs.shape[0] // 2
        mixed = mul(probs, qkv_ref[k_rows, pair_cols(2, pair)])
        att_ref[q_rows, pair_cols(0, pair)] = (mixed[:half] * low + mixed[half:] * high).astype(bf16)


def attend(qkv_ref, att_ref, q_rows, k_rows, mask, keep_sums):
    for pair in range(HEADS // 2):
        queries = qkv_ref[q_rows, pair_cols(0, pair)] * bf16(HEAD ** (-0.5))
        scores = mul_bt(two_heads(qkv_ref[k_rows, pair_cols(1, pair)]), queries)
        probs, sums = softmax_down(scores, mask)
        vals = two_heads(qkv_ref[k_rows, pair_cols(2, pair)])
        mixed = mul_at(jnp.concatenate(probs, axis=0).astype(bf16), vals)
        att_ref[q_rows, pair_cols(0, pair)] = mixed.astype(bf16)
        for k in range(2):
            keep_sums(2 * pair + k, sums[k])


def text_front_kernel(
    x_ref, g1_ref, b1_ref, wqkv_ref, wo_ref, g2_ref, b2_ref, h1_ref, qkv_ref, att_ref, mid_ref,
    h2_ref, sum_ref, lse_ref
):
    rows, chunk = x_ref.shape[0], 128
    norm_rows(x_ref, h1_ref, g1_ref[...], b1_ref[...], chunk)

    @pl.loop(0, 3 * D // 256)
    def _(step):
        at = pl.ds(pl.multiple_of(step * 256, 256), 256)
        qkv_ref[:, at] = mul(h1_ref[...], wqkv_ref[:, at]).astype(bf16)

    mask = same_sequence(chunk, 0, chunk, 0, TXT_LEN)

    @pl.loop(0, rows // chunk)
    def _(step):
        at = pl.ds(pl.multiple_of(step * chunk, chunk), chunk)

        def keep_sums(head, value):
            lse_ref[pl.ds(step * 16 + head, 1), :] = value

        attend(qkv_ref, att_ref, at, at, mask, keep_sums)

    @pl.loop(0, D // 256)
    def _(step):
        at = pl.ds(pl.multiple_of(step * 256, 256), 256)
        mid_ref[:, at] = x_ref[:, at].astype(f32) + mul(att_ref[...], wo_ref[:, at])

    norm_rows(mid_ref, h2_ref, g2_ref[...], b2_ref[...], chunk)
    per = chunk // TXT_LEN

    @pl.loop(0, rows // chunk)
    def _(step):
        values = mid_ref[pl.ds(pl.multiple_of(step * chunk, chunk), chunk), :]
        sum_ref[pl.ds(pl.multiple_of(step * per, per), per), :] = jnp.sum(
            values.reshape(per, TXT_LEN, D), axis=1
        )


def text_front(rows_in, gain1, bias1, wqkv, wo, gain2, bias2):
    rows = rows_in.shape[0]
    shapes = [
        ((rows, D), bf16),
        ((rows, 3 * D), bf16),
        ((rows, D), bf16),
        ((rows, D), f32),
        ((rows, D), bf16),
        ((rows // TXT_LEN, D), f32),
        ((rows // 128 * 16, 128), f32),
    ]
    return pl.pallas_call(
        text_front_kernel,
        out_shape=[jax.ShapeDtypeStruct(*item) for item in shapes],
        compiler_params=params(),
        cost_estimate=cost(rows * D * D * 8, 14 * D * rows + 8 * D * D, rows * 128 * HEADS),
        name="text_front",
    )(rows_in, gain1[None], bias1[None], wqkv, wo, gain2[None], bias2[None])


def image_front_kernel(
    windows, x_ref, perm_ref, g1_ref, b1_ref, g2_ref, b2_ref, *refs
):
    h2_ref, sum_ref, w_ref, h1_ref, placed_ref, qkv_ref, att_ref, mid_ref, sems = refs[-9:]
    rows, chunk = x_ref.shape[0], 80
    copies, row = [], 0
    for k, piece in enumerate(refs[:-9]):
        place = w_ref.at[pl.ds(row, piece.shape[0]), :]
        copies.append(pltpu.make_async_copy(piece, place, sems.at[k]))
        row += piece.shape[0]
    for copy in copies:
        copy.start()

    def place_columns(src, dst):
        @pl.loop(0, D // 256)
        def _(step):
            at = pl.ds(pl.multiple_of(step * 256, 256), 256)
            dst[:, at] = mul_bt(src[...], perm_ref[at, :]).astype(bf16)

    norm_rows(x_ref, h1_ref, g1_ref[...].astype(f32), b1_ref[...].astype(f32), chunk)
    place_columns(h1_ref, placed_ref)
    for copy in copies:
        copy.wait()

    @pl.loop(0, 3 * D // 256)
    def _(step):
        at = pl.ds(pl.multiple_of(step * 256, 256), 256)
        qkv_ref[:, at] = mul(placed_ref[...], w_ref[:, at]).astype(bf16)

    for row0, count, key0, keys in windows:
        one = same_sequence(count, row0, keys, key0, IMG_LEN)
        mask = jnp.concatenate([one, one], axis=0)
        attend_along(qkv_ref, att_ref, pl.ds(row0, count), pl.ds(key0, keys), mask)
    place_columns(att_ref, placed_ref)

    @pl.loop(0, D // 256)
    def _(step):
        at = pl.ds(pl.multiple_of(step * 256, 256), 256)
        there = pl.ds(pl.multiple_of(step * 256 + 3 * D, 256), 256)
        mid_ref[:, at] = x_ref[:, at].astype(f32) + mul(placed_ref[...], w_ref[:, there])

    norm_rows(mid_ref, h2_ref, g2_ref[...].astype(f32), b2_ref[...].astype(f32), chunk)
    for k in range(rows // IMG_LEN):
        first, last = k * IMG_LEN, (k + 1) * IMG_LEN
        start, end = first // 8 * 8, -(-last // 8) * 8
        values = mid_ref[start:end, :]
        place = lax.broadcasted_iota(jnp.int32, values.shape, 0) + start
        inside = (place >= first) & (place < last)
        sum_ref[k : k + 1, :] = jnp.sum(jnp.where(inside, values, 0.0), axis=0, keepdims=True)


def image_front(rows_in, pieces, perm, gain1, bias1, gain2, bias2):
    rows = rows_in.shape[0]
    windows = ((0, 208, 0, 256), (208, 192, 192, 208))
    vmem = pl.BlockSpec(memory_space=pltpu.VMEM)
    return pl.pallas_call(
        functools.partial(image_front_kernel, windows),
        out_shape=[
            jax.ShapeDtypeStruct((rows, D), bf16),
            jax.ShapeDtypeStruct((rows // IMG_LEN, D), f32),
        ],
        in_specs=[vmem] * 6 + anywhere(pieces),
        out_specs=[vmem] * 2,
        scratch_shapes=[
            pltpu.VMEM((D, 4 * D), bf16),
            pltpu.VMEM((rows, D), bf16),
            pltpu.VMEM((rows, D), bf16),
            pltpu.VMEM((rows, 3 * D), bf16),
            pltpu.VMEM((rows, D), bf16),
            pltpu.VMEM((rows, D), f32),
            pltpu.SemaphoreType.DMA((len(pieces),)),
        ],
        compiler_params=params(),
        cost_estimate=cost(rows * D * D * 12, 8 * D * D, rows * 256 * HEADS),
        name="image_front",
    )(rows_in, perm, gain1[None], bias1[None], gain2[None], bias2[None], *pieces)


def gelu_parts(inner):
    half = 0.5 * (1.0 + lax.erf(inner * (0.5**0.5)))
    return inner * half, half


def pack_kernel(unit_ref, pos_ref, *refs):
    refs[-1][:, :D] = unit_ref[...].astype(bf16)
    refs[-1][:, D:] = pos_ref[...]


def packed(unit, positive, after):
    shape = (unit.shape[0], D + positive.shape[1])
    return pl.pallas_call(
        pack_kernel,
        out_shape=jax.ShapeDtypeStruct(shape, bf16),
        in_specs=[pl.BlockSpec(memory_space=pltpu.VMEM)] * 2 + anywhere(after),
        compiler_params=params(),
        cost_estimate=cost(shape[0] * shape[1], 4 * shape[0] * shape[1]),
        name="packed",
    )(unit, positive, *after)


def pool_matrix(count, rows, row0, seq_len):
    row = (lax.broadcasted_iota(jnp.int32, (count, rows), 1) + row0) // seq_len
    return jnp.where(row == lax.broadcasted_iota(jnp.int32, (count, rows), 0), 1.0, 0.0).astype(bf16)


def two_terms(mean):
    high = mean.astype(bf16)
    low = (mean - high.astype(f32)).astype(bf16)
    return jnp.concatenate([high, low], axis=0)


def unit_rows(pooled):
    inverse = lax.rsqrt(jnp.sum(pooled * pooled, axis=-1, keepdims=True) + norm_eps)
    return pooled * inverse, inverse


def text_up_kernel(h2_ref, wu_ref, wd_ref, sum_ref, *refs):
    slope_ref, hid_ref, unit_ref, inv_ref, acc = refs[-5:]
    step = pl.program_id(0)
    chunk = 320
    per = chunk // TXT_LEN
    pool = pool_matrix(per, chunk, 0, TXT_LEN)
    for k in range(h2_ref.shape[0] // chunk):
        inner = mul(h2_ref[k * chunk : (k + 1) * chunk, :], wu_ref[...])
        value, half = gelu_parts(inner)
        slope = half + inner * (jnp.exp(-0.5 * inner * inner) * 0.3989422804014327)
        slope_ref[k * chunk : (k + 1) * chunk, :] = slope.astype(bf16)
        hid_ref[k * per : (k + 1) * per, :] = mul(pool, value.astype(bf16))
    terms = mul(two_terms(hid_ref[...] * (1.0 / TXT_LEN)), wd_ref[...])
    count = hid_ref.shape[0]
    added = terms[:count] + terms[count:]

    @pl.when(step == 0)
    def _():
        acc[...] = sum_ref[...] * (1.0 / TXT_LEN) + added

    @pl.when(step > 0)
    def _():
        acc[...] += added

    @pl.when(step == pl.num_programs(0) - 1)
    def _():
        unit, inverse = unit_rows(acc[...])
        unit_ref[...] = unit
        inv_ref[...] = jnp.broadcast_to(inverse, inv_ref.shape)


def text_up(normed2, weight_up, weight_down, middle_sum, after=()):
    rows, count = normed2.shape[0], middle_sum.shape[0]
    fixed = lambda shape: pl.BlockSpec(shape, lambda i: (0, 0))
    return pl.pallas_call(
        text_up_kernel,
        grid=(FF // TILE,),
        out_shape=[
            jax.ShapeDtypeStruct((rows, FF), bf16),
            jax.ShapeDtypeStruct((count, FF), f32),
            jax.ShapeDtypeStruct((count, D), f32),
            jax.ShapeDtypeStruct((count, 128), f32),
        ],
        in_specs=[
            fixed((rows, D)),
            pl.BlockSpec((D, TILE), lambda i: (0, i)),
            pl.BlockSpec((TILE, D), lambda i: (i, 0)),
            fixed((count, D)),
        ]
        + anywhere(after),
        out_specs=[
            pl.BlockSpec((rows, TILE), lambda i: (0, i)),
            pl.BlockSpec((count, TILE), lambda i: (0, i)),
            fixed((count, D)),
            fixed((count, 128)),
        ],
        scratch_shapes=[pltpu.VMEM((count, D), f32)],
        compiler_params=params(),
        cost_estimate=cost(2 * rows * D * FF, 4 * D * FF + 2 * rows * FF, 20 * rows * FF),
        name="text_up",
    )(normed2, weight_up, weight_down, middle_sum, *after)


def image_up_kernel(fold, h2_ref, wu_ref, wd_ref, sum_ref, *refs):
    out_ref, acc, chosen_ref = refs[-3:]
    step = pl.program_id(0)
    rows, count = h2_ref.shape[0], sum_ref.shape[0]
    part = TILE // fold

    @pl.when(step == 0)
    def _():
        place = lax.broadcasted_iota(jnp.int32, (TILE, TILE), 0)
        col = lax.broadcasted_iota(jnp.int32, (TILE, TILE), 1)
        source = (col % part) * fold + col // part
        chosen_ref[...] = jnp.where(place == source, 1.0, 0.0).astype(bf16)

    inner = mul(h2_ref[...], wu_ref[...])
    value, _ = gelu_parts(inner)
    summed = mul(pool_matrix(count, rows, 0, IMG_LEN), value.astype(bf16))
    mean = two_terms(summed * (1.0 / IMG_LEN))
    moved = mul(mean, chosen_ref[...]).astype(bf16)
    weight = jnp.concatenate([wd_ref[:, k * D : (k + 1) * D] for k in range(fold)], axis=0)
    terms = mul(moved, weight)
    added = terms[:count] + terms[count:]

    @pl.when(step == 0)
    def _():
        acc[...] = sum_ref[...] * (1.0 / IMG_LEN) + added

    @pl.when(step > 0)
    def _():
        acc[...] += added

    @pl.when(step == pl.num_programs(0) - 1)
    def _():
        out_ref[...] = unit_rows(acc[...])[0].astype(bf16)


def image_up(normed2, whole, up_col, down_col, middle_sum, after=()):
    rows, count = normed2.shape[0], middle_sum.shape[0]
    fold = FF // D
    fixed = lambda shape: pl.BlockSpec(shape, lambda i: (0, 0))
    return pl.pallas_call(
        functools.partial(image_up_kernel, fold),
        grid=(FF // TILE,),
        out_shape=jax.ShapeDtypeStruct((count, D), bf16),
        in_specs=[
            fixed((rows, D)),
            pl.BlockSpec((D, TILE), lambda i: (0, up_col // TILE + i)),
            pl.BlockSpec((TILE // fold, fold * D), lambda i: (i, down_col // (fold * D))),
            fixed((count, D)),
        ]
        + anywhere(after),
        out_specs=fixed((count, D)),
        scratch_shapes=[pltpu.VMEM((count, D), f32), pltpu.VMEM((TILE, TILE), bf16)],
        compiler_params=params(),
        cost_estimate=cost(2 * rows * D * FF, 4 * D * FF, 15 * rows * FF),
        name="image_up",
    )(normed2, whole, whole, middle_sum, *after)


def left_kernel(order_ref, h2_ref, h1_ref, att_ref, up_ref, rest_ref):
    step = pl.program_id(0)

    @pl.when(step < 2)
    def _():
        up_ref[0] = placed(order_ref[0], h2_ref[...])

    @pl.when((step == 2) | (step == 3))
    def _():
        rest_ref[0] = placed(order_ref[0], h1_ref[...])

    @pl.when(step == 4)
    def _():
        rest_ref[0] = placed(order_ref[0], att_ref[...])


def left_factors(orders, normed2, normed1, attended):
    rows = normed1.shape[0]
    fixed = pl.BlockSpec((rows, D), lambda i: (0, 0))
    return pl.pallas_call(
        left_kernel,
        grid=(5,),
        out_shape=[
            jax.ShapeDtypeStruct((2, D, rows), bf16),
            jax.ShapeDtypeStruct((3, D, rows), bf16),
        ],
        in_specs=[
            pl.BlockSpec((1, D, D), lambda i: (jnp.minimum(i % 2 + i // 4, 1), 0, 0)),
            fixed,
            fixed,
            fixed,
        ],
        out_specs=[
            pl.BlockSpec((1, D, rows), lambda i: (jnp.minimum(i, 1), 0, 0)),
            pl.BlockSpec((1, D, rows), lambda i: (jnp.maximum(i - 2, 0), 0, 0)),
        ],
        compiler_params=params(24 << 20),
        cost_estimate=cost(10 * rows * D * D, 16 * rows * D + 10 * D * D),
        name="left_factors",
    )(orders, normed2, normed1, attended)


def loss_parts(text_rows, pos, image_all):
    similar = mul_bt(text_rows, image_all) * logit_scale
    shifted = jnp.exp(similar - logit_scale)
    alive = jnp.max(pos, axis=1, keepdims=True)
    row_sum = jnp.sum(shifted, axis=1, keepdims=True)
    row_count = jnp.maximum(jnp.sum(pos, axis=1, keepdims=True), 1.0)
    return similar, shifted, alive, row_sum, row_count


def sums_over_captions(text_rows, pos, image_all):
    similar, shifted, alive, row_sum, row_count = loss_parts(text_rows, pos, image_all)
    pos_similar = pos * similar
    cap_term = alive * (
        logit_scale + jnp.log(row_sum) - jnp.sum(pos_similar, axis=1, keepdims=True) / row_count
    )
    return (
        jnp.sum(alive * shifted, axis=0, keepdims=True),
        jnp.sum(pos, axis=0, keepdims=True),
        jnp.sum(pos_similar, axis=0, keepdims=True),
        jnp.sum(cap_term, axis=0, keepdims=True),
        jnp.sum(alive, axis=0, keepdims=True),
    )


def loss_from(sums):
    col_sum, col_count, col_pos, cap_total, live_total = sums
    img_term = logit_scale + jnp.log(col_sum) - col_pos / col_count
    return 0.5 * cap_total / live_total + 0.5 * jnp.mean(img_term, axis=1, keepdims=True)


def grad_of_unit(text_rows, pos, image_all, col_sum, col_count, live_total):
    _, shifted, alive, row_sum, row_count = loss_parts(text_rows, pos, image_all)
    cap_share, img_share = 0.5 / live_total, 0.5 / image_all.shape[0]
    grad_sims = alive * shifted * (cap_share / row_sum + img_share / col_sum) - pos * (
        cap_share / row_count + img_share / col_count
    )
    return mul(grad_sims.astype(bf16), image_all) * logit_scale


def turned(grad, unit):
    return grad - unit * jnp.sum(grad * unit, axis=-1, keepdims=True)


def loss_kernel(
    pack_ref, image_ref, own_ref, unit_ref, inv_ref, loss_ref, row_ref, low_ref, col_sum_ref,
    col_count_ref, live_ref
):
    image_all = image_ref[...]
    chunk = 256
    total = None
    for k in range(pack_ref.shape[0] // chunk):
        at = slice(k * chunk, (k + 1) * chunk)
        part = sums_over_captions(pack_ref[at, :D], pack_ref[at, D:].astype(f32), image_all)
        total = part if total is None else [a + b for a, b in zip(total, part)]
    loss_ref[...] = jnp.broadcast_to(loss_from(total), loss_ref.shape)
    col_sum, col_count, _, _, live_total = total
    col_sum_ref[...] = col_sum
    col_count_ref[...] = col_count
    live_ref[...] = jnp.broadcast_to(live_total, live_ref.shape)
    grad = grad_of_unit(
        own_ref[:, :D], own_ref[:, D:].astype(f32), image_all, col_sum, col_count, live_total
    )
    row = inv_ref[:, :1] * turned(grad, unit_ref[...]) * (1.0 / TXT_LEN)
    row_ref[...] = row
    low_ref[...] = row.astype(bf16)


def loss_and_rows(pack, image_all, own_pack, unit, inverse):
    images, count = image_all.shape[0], own_pack.shape[0]
    shapes = [(1, 128), (count, D), (count, D), (1, images), (1, images), (1, 128)]
    kinds = [f32, f32, bf16, f32, f32, f32]
    return pl.pallas_call(
        loss_kernel,
        out_shape=[jax.ShapeDtypeStruct(*item) for item in zip(shapes, kinds)],
        in_specs=in_vmem(5),
        out_specs=in_vmem(len(shapes)),
        compiler_params=params(16 << 20),
        cost_estimate=cost(2 * pack.shape[0] * images * D, 2 * pack.size, pack.shape[0] * images),
        name="loss_and_rows",
    )(pack, image_all, own_pack, unit, inverse)


def down_kernel(pack_ref, image_ref, col_sum_ref, col_count_ref, live_ref, hid_ref, *refs):
    step, out_ref = pl.program_id(0), refs[-1]
    text_rows = pack_ref[:, :D]
    grad = grad_of_unit(
        text_rows, pack_ref[:, D:].astype(f32), image_ref[...], col_sum_ref[...],
        col_count_ref[...], live_ref[:, :1]
    )
    rows = (turned(grad, text_rows.astype(f32)) * (1.0 / TXT_LEN)).astype(bf16)
    part = mul_at(hid_ref[...], rows)

    @pl.when(step == 0)
    def _():
        out_ref[...] = part

    @pl.when(step > 0)
    def _():
        out_ref[...] += part


def grad_of_down(pack, image_all, col_sum, col_count, live_total, hidden_cols, after):
    images, chunk = image_all.shape[0], 256
    fixed = lambda shape: pl.BlockSpec(shape, lambda i: (0, 0))
    per = hidden_cols.shape[1]
    return pl.pallas_call(
        down_kernel,
        grid=(pack.shape[0] // chunk,),
        out_shape=jax.ShapeDtypeStruct((per, D), f32),
        in_specs=[
            pl.BlockSpec((chunk, pack.shape[1]), lambda i: (i, 0)),
            fixed((images, D)), fixed((1, images)), fixed((1, images)), fixed((1, 128)),
            pl.BlockSpec((chunk, per), lambda i: (i, 0)),
        ]
        + anywhere(after),
        out_specs=fixed((per, D)),
        compiler_params=params(16 << 20),
        cost_estimate=cost(4 * pack.shape[0] * images * D, 2 * pack.size, pack.shape[0] * images),
        name="grad_of_down",
    )(pack, image_all, col_sum, col_count, live_total, hidden_cols, *after)


def mlp_back_kernel(
    low_ref, wd_ref, slope_ref, wu_ref, lhs_ref, mid_ref, gain_ref, row_ref, keep_a, send_a, keep_b,
    send_b, out_ref, gain_out, bias_out
):
    count, rows = low_ref.shape[0], slope_ref.shape[0]
    half, steps = D // 2, FF // 2 // TILE
    for k, (keep, send) in enumerate(((keep_a, send_a), (keep_b, send_b))):

        @pl.loop(0, steps)
        def _(step, k=k, keep=keep, send=send):
            at = pl.ds(pl.multiple_of(k * (FF // 2) + step * TILE, TILE), TILE)
            there = pl.ds(pl.multiple_of(step * TILE, TILE), TILE)
            hidden = mul_bt(low_ref[...], wd_ref[at, :])
            wide = jnp.broadcast_to(hidden[:, None, :], (count, TXT_LEN, TILE))
            inner = (wide.reshape(rows, TILE) * slope_ref[:, at].astype(f32)).astype(bf16)
            weight = mul(lhs_ref[k], inner).astype(bf16)
            keep[:, there] = weight[:half]
            send[:, there] = weight[half:]
            added = mul_bt(inner, wu_ref[:, at])
            if k == 0:

                @pl.when(step == 0)
                def _():
                    out_ref[...] = added

                @pl.when(step > 0)
                def _():
                    out_ref[...] += added
            else:
                out_ref[...] += added

    chunk = 128
    per = chunk // TXT_LEN
    gain = gain_ref[...]
    gain_out[...] = jnp.zeros_like(gain_out)
    bias_out[...] = jnp.zeros_like(bias_out)

    @pl.loop(0, rows // chunk)
    def _(k):
        at = pl.ds(pl.multiple_of(k * chunk, chunk), chunk)
        unit, scale = norm_parts(mid_ref[at, :])
        grad = out_ref[at, :]
        gain_out[...] += jnp.sum(grad * unit, axis=0, keepdims=True)
        bias_out[...] += jnp.sum(grad, axis=0, keepdims=True)
        row = row_ref[pl.ds(pl.multiple_of(k * per, per), per), :]
        row = jnp.broadcast_to(row[:, None, :], (per, TXT_LEN, D)).reshape(chunk, D)
        out_ref[at, :] = row + norm_back(unit, scale, gain, grad)


def mlp_back(grad_row, grad_low, weight_down, slope, weight_up, lhs, middle, gain):
    rows = slope.shape[0]
    line = jax.ShapeDtypeStruct((1, D), f32)
    return pl.pallas_call(
        mlp_back_kernel,
        out_shape=[stays((D // 2, FF // 2), bf16)] * 4 + [stays((rows, D), f32), line, line],
        in_specs=in_vmem(8),
        out_specs=in_vmem(7),
        compiler_params=params(16 << 20),
        cost_estimate=cost(4 * rows * D * FF, 4 * D * FF + 2 * rows * FF + 2 * D * FF, rows * FF),
        name="mlp_back",
    )(grad_low, weight_down, slope, weight_up, lhs, middle, gain[None], grad_row)


def attention_back_kernel(first, grad_ref, wo_ref, qkv_ref, lse_ref, *refs):
    low_ref, out_ref = refs[-2:]
    chunk = 128
    mask = same_sequence(chunk, 0, chunk, 0, TXT_LEN)

    @pl.loop(0, low_ref.shape[0] // chunk)
    def _(step):
        here = pl.ds(pl.multiple_of((first + step) * chunk, chunk), chunk)
        there = pl.ds(pl.multiple_of(step * chunk, chunk), chunk)
        sums = lse_ref[pl.ds(pl.multiple_of((first + step) * 16, 16), 16), :]
        low = grad_ref[here, :].astype(bf16)
        low_ref[there, :] = low
        grad_att = mul_bt(low, wo_ref[...]).astype(bf16)
        for pair in range(HEADS // 2):
            queries = qkv_ref[here, pair_cols(0, pair)] * bf16(HEAD ** (-0.5))
            keys = two_heads(qkv_ref[here, pair_cols(1, pair)])
            vals = two_heads(qkv_ref[here, pair_cols(2, pair)])
            grads = grad_att[:, pair_cols(0, pair)]
            scores, grad_probs = mul_bt(keys, queries), mul_bt(vals, grads)
            probs, grad_scores = [], []
            for k in range(2):
                at = slice(k * chunk, (k + 1) * chunk)
                head = 2 * pair + k
                shifted = scores[at] - sums[head : head + 1, :]
                prob = jnp.where(mask, jnp.exp(jnp.where(mask, shifted, 0.0)), 0.0)
                along = jnp.sum(grad_probs[at] * prob, axis=0, keepdims=True)
                grad_scores.append((prob * (grad_probs[at] - along)).astype(bf16))
                probs.append(prob.astype(bf16))
            grad_q = mul_at(jnp.concatenate(grad_scores, axis=0), keys) * HEAD ** (-0.5)
            grad_k = mul(jnp.concatenate(grad_scores, axis=1), two_heads(queries))
            grad_v = mul(jnp.concatenate(probs, axis=1), two_heads(grads))
            out_ref[there, pair_cols(0, pair)] = grad_q.astype(bf16)
            out_ref[there, pair_cols(1, pair)] = grad_k.astype(bf16)
            out_ref[there, pair_cols(2, pair)] = grad_v.astype(bf16)


def attention_back(grad_middle, weight_out, project, log_sums, first, count, after=()):
    rows = count * 128
    return pl.pallas_call(
        functools.partial(attention_back_kernel, first),
        out_shape=[stays((rows, D), bf16), stays((rows, 3 * D), bf16)],
        in_specs=in_vmem(4) + anywhere(after),
        out_specs=in_vmem(2),
        compiler_params=params(16 << 20),
        cost_estimate=cost(10 * rows * D * D, 16 * rows * D + 2 * D * D, rows * 128 * HEADS),
        name="attention_back",
    )(grad_middle, weight_out, project, log_sums, *after)


def mul_rows(lhs, parts, cols):
    total, row = 0.0, 0
    for part in parts:
        total = total + mul(lhs[:, row : row + part.shape[0]], part[:, cols])
        row += part.shape[0]
    return total


def weight_back_kernel(factors, groups, lhs_ref, *refs):
    keep_a, send_a, keep_b, send_b = refs[-4:]
    half = D // 2
    for k, (factor, group, col) in enumerate(factors):
        parts = refs[sum(groups[:group]) : sum(groups[: group + 1])]
        weight = mul_rows(lhs_ref.at[factor], parts, slice(col * D, (col + 1) * D)).astype(bf16)
        at = slice(k % 2 * D, (k % 2 + 1) * D)
        (keep_b if k > 1 else keep_a)[:, at] = weight[:half]
        (send_b if k > 1 else send_a)[:, at] = weight[half:]


def weight_back(lhs, groups, factors, after=()):
    rows = lhs.shape[2]
    given = [part for group in groups for part in group]
    return pl.pallas_call(
        functools.partial(weight_back_kernel, factors, [len(group) for group in groups]),
        out_shape=[stays((D // 2, 2 * D), bf16)] * 4,
        in_specs=in_vmem(1 + len(given)) + anywhere(after),
        out_specs=in_vmem(4),
        compiler_params=params(16 << 20),
        cost_estimate=cost(8 * rows * D * D, 8 * rows * D + 14 * D * D),
        name="weight_back",
    )(lhs, *given, *after)


def input_back_kernel(count, *refs):
    projs = refs[:count]
    w_ref, x_ref, gain_ref, mid_ref = refs[count : count + 4]
    out_ref, gain_out, bias_out = refs[-3:]
    rows, chunk = x_ref.shape[0], 128

    @pl.loop(0, D // 256)
    def _(step):
        at = pl.ds(pl.multiple_of(step * 256, 256), 256)
        row = 0
        for part in projs:
            there = slice(row, row + part.shape[0])
            out_ref[there, at] = mul_bt(part[...], w_ref[at, :])
            row += part.shape[0]

    gain = gain_ref[...]
    gain_out[...] = jnp.zeros_like(gain_out)
    bias_out[...] = jnp.zeros_like(bias_out)

    @pl.loop(0, rows // chunk)
    def _(k):
        at = pl.ds(pl.multiple_of(k * chunk, chunk), chunk)
        unit, scale = norm_parts(x_ref[at, :].astype(f32))
        grad = out_ref[at, :]
        gain_out[...] += jnp.sum(grad * unit, axis=0, keepdims=True)
        bias_out[...] += jnp.sum(grad, axis=0, keepdims=True)
        out_ref[at, :] = mid_ref[at, :] + norm_back(unit, scale, gain, grad)


def input_back(grad_projs, weight, rows_in, gain, grad_middle, after=()):
    rows = rows_in.shape[0]
    line = jax.ShapeDtypeStruct((1, D), f32)
    return pl.pallas_call(
        functools.partial(input_back_kernel, len(grad_projs)),
        out_shape=[jax.ShapeDtypeStruct((rows, D), f32), line, line],
        in_specs=in_vmem(len(grad_projs) + 4) + anywhere(after),
        out_specs=in_vmem(3),
        compiler_params=params(16 << 20),
        cost_estimate=cost(6 * rows * D * D, 14 * rows * D + 6 * D * D),
        name="input_back",
    )(*grad_projs, weight, rows_in, gain[None], grad_middle, *after)


def local(
    images,
    captions,
    img_gain1,
    img_bias1,
    img_qkv,
    img_out,
    img_gain2,
    img_bias2,
    img_up,
    img_down,
    txt_gain1,
    txt_bias1,
    txt_qkv,
    txt_out,
    txt_gain2,
    txt_bias2,
    txt_up,
    txt_down,
    counts,
    matches,
):
    peers = lax.axis_size(AXIS)
    own = lax.axis_index(AXIS)
    per = D // peers
    img_local = counts.shape[0]
    cap_local = matches.shape[0]
    total_images = matches.shape[1]

    whole = lax.all_gather(
        jnp.concatenate([img_up.reshape(per, FF), img_down.reshape(per, FF)], axis=1),
        AXIS,
        axis=0,
        tiled=True,
    )
    small = peers == 32
    shard = jnp.concatenate([img_qkv.reshape(per, 3 * D), img_out.reshape(per, D)], axis=1)
    if small:
        line, perm = gathered_line(shard), row_order((1, 4, 2, 16, 8))
    else:
        line, perm = lax.all_gather(shard, AXIS, axis=0, tiled=True), jnp.eye(D, dtype=bf16)

    normed1, project, attended, middle, normed2, middle_sum, log_sums = text_front(
        captions, txt_gain1, txt_bias1, txt_qkv, txt_out, txt_gain2, txt_bias2
    )
    middle_sum, line = in_turn(middle_sum, line)
    beside, above = (swapped(line, 2), swapped(line, 4)) if small else (line, line)
    slope, hidden_sum, text_unit, inverse = text_up(
        normed2, txt_up, txt_down, middle_sum, (line,)
    )
    text_unit, (beside, above) = in_turn(text_unit, (beside, above))

    ends_at = jnp.cumsum(counts)
    slot_ids = lax.iota(jnp.int32, cap_local)
    owner = jnp.sum((ends_at[None, :] <= slot_ids[:, None]).astype(jnp.int32), axis=1)
    owner = owner + own * img_local
    live = slot_ids < ends_at[-1]
    columns = lax.iota(jnp.int32, total_images)
    positive = ((matches > 0) | (owner[:, None] == columns[None, :])) & live[:, None]

    own_pack = packed(text_unit, positive.astype(bf16), ())
    pieces = [line]
    if small:
        held = own_pack[None]
        first, second = diagonal(beside, above)
        others = [swapped(held, mask) for mask in (8, 16, 24)]
        scaled_sum = (hidden_sum * inverse[:, :1]).astype(bf16)
        hidden_cols = lax.all_to_all(scaled_sum, AXIS, split_axis=1, concat_axis=0, tiled=True)
        others, first, second, hidden_cols = lax.optimization_barrier(
            (others, first, second, hidden_cols)
        )
        held = joined(joined(held, others[0], 8), joined(others[1], others[2], 8), 16, 1)
        text_beside, text_above = swapped(held, 2), swapped(held, 4)
        pieces = [line, beside, above, first, second]
        pieces = pieces + [swapped(piece, 1) for piece in pieces]

    normed_img, middle_img = image_front(
        images, pieces, perm, img_gain1, img_bias1, img_gain2, img_bias2
    )
    if small:
        normed_img, text_beside, text_above = lax.optimization_barrier(
            (normed_img, text_beside, text_above)
        )
        across = jnp.concatenate(diagonal(text_beside, text_above), axis=0)
        held = joined(joined(held, text_beside, 2), joined(text_above, across, 2), 4, 4)

    order_a, order_b, tail = stage_orders()
    orders = jnp.stack([row_order(order_a + tail[::-1]), row_order(order_b + tail[::-1])])
    if small:
        whole, held, orders = lax.optimization_barrier((whole, held, orders))
        other = swapped(held, 1)
    image_low = image_up(normed_img, whole, 0, FF, middle_img)
    if small:
        text_pack = joined(held, other, 1).reshape(-1, D + total_images)
    image_low, normed2 = in_turn(image_low, normed2)
    image_all = spread(image_low).reshape(total_images, D)
    lhs_up, lhs_rest = left_factors(orders, normed2, normed1, attended)
    image_all, lhs_up = in_turn(image_all, lhs_up)

    if small:
        loss_value, grad_row, row_low, col_sum, col_count, live_total = loss_and_rows(
            text_pack, image_all, own_pack, text_unit, inverse
        )
        loss_value = loss_value[0, 0]
    else:
        text_low, pos = own_pack[:, :D], own_pack[:, D:].astype(f32)
        sums = lax.psum(sums_over_captions(text_low, pos, image_all), AXIS)
        loss_value = loss_from(sums)[0, 0]
        grad = grad_of_unit(text_low, pos, image_all, sums[0], sums[1], sums[4])
        grad_row = inverse[:, :1] * turned(grad, text_unit) * (1.0 / TXT_LEN)
        row_low = grad_row.astype(bf16)

    *up, grad_middle, gain_two, bias_two = mlp_back(
        grad_row, row_low, txt_down, slope, txt_up, lhs_up, middle, txt_gain2
    )
    stages = len(order_a)
    low_one, proj_one = attention_back(grad_middle, txt_out, project, log_sums, 0, 1)
    for stage in range(stages - 2):
        up = fold(hand_on(up, stage), (proj_one,))
    low_two, proj_two = attention_back(grad_middle, txt_out, project, log_sums, 1, 4, up)
    up = fold(hand_on(up, stages - 2), (proj_two,))
    projs, lows = (proj_one, proj_two), (low_one, low_two)
    rest = weight_back(lhs_rest, [projs, lows], [(0, 0, 0), (0, 0, 1), (1, 0, 2), (2, 1, 0)], up)
    up = hand_on(up, stages - 1)
    caption_grad, gain_one, bias_one = input_back(
        projs, txt_qkv, captions, txt_gain1, grad_middle, rest[:1]
    )
    caption_grad, up = in_turn(caption_grad, up)
    up = fold_last(up)
    for stage in range(stages - 2):
        rest = fold(hand_on(rest, stage), up[:1])
    up = hand_on_last(up)
    norms = jnp.concatenate([gain_one, bias_one, gain_two, bias_two], axis=0)
    norms = jnp.sum(spread(norms[None].astype(bf16)).astype(f32), axis=0).reshape(4, D)
    rest = hand_on(rest, stages - 2)
    if small:
        grad_down = grad_of_down(
            text_pack, image_all, col_sum, col_count, live_total, hidden_cols, (caption_grad,)
        )
    else:
        grad_down = lax.psum_scatter(
            mul_at(hidden_sum.astype(bf16), row_low), AXIS, scatter_dimension=0, tiled=True
        )
    grad_down, rest, norms, up = lax.optimization_barrier((grad_down, rest, norms, up))
    rest = fold(rest)
    rest = hand_on_last(fold_last(hand_on(rest, stages - 1)))
    up_share = sum_last(*up)
    rest_share = sum_last(*rest)
    return (
        loss_value,
        caption_grad,
        norms[0],
        norms[1],
        rest_share[:, : 3 * D].reshape(-1),
        rest_share[:, 3 * D :].reshape(-1),
        norms[2],
        norms[3],
        up_share.reshape(-1),
        grad_down.reshape(-1),
    )


def solution(mesh):
    split, flat, whole = P("blk", None), P("blk"), P()
    image_block = (whole, whole, flat, flat, whole, whole, flat, flat)
    return jax.shard_map(
        local,
        mesh=mesh,
        in_specs=(split, split) + image_block + (whole,) * 8 + (flat, split),
        out_specs=(whole, split, whole, whole, flat, flat, whole, whole, flat, flat),
        check_vma=False,
    )
```

```python
import functools

import jax
import jax.numpy as jnp
from jax import lax
from jax.experimental import pallas as pl
from jax.experimental.pallas import tpu as pltpu
from jax.sharding import PartitionSpec as P

D = 768
FF = 3072
HEAD = 64
HEADS = D // HEAD
IMG_LEN = 50
TXT_LEN = 16
AXIS = "blk"

norm_eps = 1e-06
logit_scale = 50.0
f32 = jnp.float32
bf16 = jnp.bfloat16


def swapped(value, mask):
    peers = lax.axis_size(AXIS)
    return lax.ppermute(value, AXIS, [(i, i ^ mask) for i in range(peers)])


def bit_masks():
    peers = lax.axis_size(AXIS)
    return [1 << k for k in range(peers.bit_length() - 1)]


def joined(held, other, mask, outer=None):
    upper = (lax.axis_index(AXIS) & mask) > 0
    first = jnp.where(upper, other, held)
    second = jnp.where(upper, held, other)
    outer = held.shape[0] if outer is None else outer
    parts = [part.reshape((outer, -1) + held.shape[1:]) for part in (first, second)]
    return jnp.stack(parts, axis=1).reshape((-1,) + held.shape[1:])


def spread(block):
    peers = lax.axis_size(AXIS)
    copies = jnp.broadcast_to(block[None], (peers,) + block.shape)
    return lax.all_to_all(copies, AXIS, split_axis=0, concat_axis=0, tiled=True)


def stage_orders():
    masks = bit_masks()
    head, tail = masks[:-2], masks[-2:]
    order_a = list(head)
    order_b = list(head)
    for k in range(1, len(head) - 1, 2):
        order_b[k], order_b[k + 1] = order_b[k + 1], order_b[k]
    return order_a, order_b, tail


def row_order(bits):
    peers = lax.axis_size(AXIS)
    own = lax.axis_index(AXIS)
    per = D // peers
    places = lax.broadcasted_iota(jnp.int32, (D, 1), 0)
    block = places // per
    target = jnp.zeros_like(block) + own
    for k, mask in enumerate(bits):
        target = target ^ (((block >> (len(bits) - 1 - k)) & 1) * mask)
    return target * per + places % per


def chosen(source):
    column = lax.broadcasted_iota(jnp.int32, (source.shape[0], D), 1)
    return jnp.where(column == source, 1.0, 0.0).astype(bf16)


def gathered_line(shard):
    return jnp.concatenate([shard] + [swapped(shard, mask) for mask in (8, 16, 24)], axis=0)


def diagonal(beside, above):
    half = beside.shape[0] // 2
    return swapped(beside[:half], 4), swapped(above[half:], 2)


def in_turn(first, then):
    return lax.optimization_barrier((first, then))


def hand_on(parts, stage):
    order_a, order_b, _ = stage_orders()
    keep_a, send_a, keep_b, send_b = parts
    return keep_a, swapped(send_a, order_a[stage]), keep_b, swapped(send_b, order_b[stage])


def hand_on_last(blocks):
    low, high = stage_orders()[2]
    own, *others = blocks
    return own, [swapped(block, mask) for block, mask in zip(others, (low, high, low | high))]


def sum_last(own, others):
    total = own
    for other in others:
        total = total + other.astype(f32)
    return total


VMEM_BYTES = 56 << 20
TILE = 512


def norm_parts(values):
    average = jnp.mean(values, axis=-1, keepdims=True)
    centred = values - average
    variance = jnp.mean(centred * centred, axis=-1, keepdims=True)
    scale = lax.rsqrt(variance + norm_eps)
    return centred * scale, scale


def norm_back(unit, scale, gain, grad):
    inner = grad * gain
    shift = jnp.mean(inner, axis=-1, keepdims=True)
    along = jnp.mean(inner * unit, axis=-1, keepdims=True)
    return scale * (inner - shift - unit * along)


def mul(lhs, rhs):
    return jnp.dot(lhs, rhs, preferred_element_type=f32)


def mul_bt(lhs, rhs):
    return lax.dot_general(lhs, rhs, (((1,), (1,)), ((), ())), preferred_element_type=f32)


def mul_at(lhs, rhs):
    return lax.dot_general(lhs, rhs, (((0,), (0,)), ((), ())), preferred_element_type=f32)


def params(limit=VMEM_BYTES):
    return pltpu.CompilerParams(vmem_limit_bytes=limit)


def in_vmem(count):
    return [pl.BlockSpec(memory_space=pltpu.VMEM)] * count


def stays(shape, dtype):
    return pltpu.VMEM(shape, dtype)


def cost(flops, moved, transcendentals=0):
    return pl.CostEstimate(flops=flops, bytes_accessed=moved, transcendentals=transcendentals)


def lane_halves(dtype):
    lane = lax.broadcasted_iota(jnp.int32, (1, 2 * HEAD), 1)
    low = jnp.where(lane < HEAD, 1.0, 0.0)
    return low.astype(dtype), (1.0 - low).astype(dtype)


def two_heads(pair):
    low, high = lane_halves(bf16)
    return jnp.concatenate([pair * low, pair * high], axis=0)


def same_sequence(rows, row0, cols, col0, seq_len):
    row = (lax.broadcasted_iota(jnp.int32, (rows, cols), 0) + row0) // seq_len
    col = (lax.broadcasted_iota(jnp.int32, (rows, cols), 1) + col0) // seq_len
    return row == col


def softmax_down(scores, mask):
    keys = mask.shape[0]
    parts, sums = [], []
    for k in range(2):
        part = jnp.where(mask, scores[k * keys : (k + 1) * keys], -1e30)
        most = jnp.max(part, axis=0, keepdims=True)
        raised = jnp.exp(part - most)
        total = jnp.sum(raised, axis=0, keepdims=True)
        parts.append(raised * (1.0 / total))
        sums.append(most + jnp.log(total))
    return parts, sums


def fold_kernel(extra, keep_a, got_a, keep_b, got_b, *refs):
    outs = refs[-5:] if extra else refs[-4:]
    rows, half, tile = keep_a.shape[0], keep_a.shape[0] // 2, 256

    @pl.loop(0, keep_a.shape[1] // tile)
    def _(step):
        cols = pl.ds(pl.multiple_of(step * tile, tile), tile)
        for k, (kept, got) in enumerate(((keep_a, got_a), (keep_b, got_b))):
            for j in range(2):
                at = slice(j * half, (j + 1) * half)
                total = kept[at, cols].astype(f32) + got[at, cols].astype(f32)
                outs[2 * k + j][:half, cols] = total.astype(bf16)

    if extra:
        came = refs[1][...] if extra > 1 else got_a[rows : rows + 16, :].astype(f32)[:8]
        sums = refs[0][...] + came
        outs[4][...] = sums
        outs[1][half : half + 16, :] = jnp.concatenate([sums, sums], axis=0).astype(bf16)


def fold(parts, after=(), sums=()):
    rows, cols = parts[0].shape
    if rows % 32:
        whole = [
            (kept.astype(f32) + got.astype(f32)).astype(bf16)
            for kept, got in (parts[:2], parts[2:])
        ]
        return [part for one in whole for part in (one[: rows // 2], one[rows // 2 :])]
    half = (rows // 2, cols)
    shapes = [stays(half, bf16)] * 4
    if sums:
        shapes[1] = stays((rows // 2 + 16, cols), bf16)
        shapes.append(stays((8, cols), f32))
    return pl.pallas_call(
        functools.partial(fold_kernel, len(sums)),
        out_shape=shapes,
        in_specs=in_vmem(4 + len(sums)) + anywhere(after),
        out_specs=in_vmem(len(shapes)),
        compiler_params=params(8 << 20),
        cost_estimate=cost(2 * rows * cols, 12 * rows * cols),
        name="fold",
    )(*parts, *sums, *after)


def fold_last_kernel(extra, keep_a, got_a, keep_b, got_b, *refs):
    outs = refs[-4:]
    cols = keep_a.shape[1]
    rows = keep_a.shape[0] // 4
    if extra:
        sums = refs[0][...] + got_a[4 * rows : 4 * rows + 16, :].astype(f32)[:8]
    for k, (kept, got) in enumerate(((keep_a, got_a), (keep_b, got_b))):
        total = kept[...].astype(f32) + got[: 4 * rows, :].astype(f32)
        at = slice(k * cols, (k + 1) * cols)
        for j, out in enumerate(outs):
            part = total[j * rows : (j + 1) * rows]
            if extra:
                row = jnp.broadcast_to(sums[k : k + 1], (8, cols))
                part = jnp.concatenate([part, row], axis=0)
            out[:, at] = part.astype(out.dtype)


def fold_last(parts, after=(), sums=()):
    rows, cols = parts[0].shape
    shape = (rows // 4 + (8 if sums else 0), 2 * cols)
    if rows % 32:
        pairs = (parts[:2], parts[2:])
        both = [kept.astype(f32) + got.astype(f32) for kept, got in pairs]
        own, *others = jnp.split(jnp.concatenate(both, axis=1), 4)
        return [own] + [other.astype(bf16) for other in others]
    return pl.pallas_call(
        functools.partial(fold_last_kernel, len(sums)),
        out_shape=[stays(shape, f32)] + [stays(shape, bf16)] * 3,
        in_specs=in_vmem(4 + len(sums)) + anywhere(after),
        out_specs=in_vmem(4),
        compiler_params=params(8 << 20),
        cost_estimate=cost(2 * rows * cols, 12 * rows * cols),
        name="fold_last",
    )(*parts, *sums, *after)


def anywhere(after):
    return [pl.BlockSpec(memory_space=pl.ANY)] * len(after)


def pair_cols(part, pair):
    start = part * D + pair * 2 * HEAD
    return slice(start, start + 2 * HEAD)


def line(ref):
    return ref[...].astype(f32).reshape(1, -1)


def norm_rows(src, dst, gain, bias, step_rows):
    @pl.loop(0, src.shape[0] // step_rows)
    def _(step):
        at = pl.ds(pl.multiple_of(step * step_rows, step_rows), step_rows)
        unit, _ = norm_parts(src[at, :].astype(f32))
        dst[at, :] = (unit * gain + bias).astype(bf16)


def attend_along(qkv_ref, att_ref, q_rows, k_rows, mask):
    low, high = lane_halves(f32)
    for pair in range(HEADS // 2):
        queries = two_heads(qkv_ref[q_rows, pair_cols(0, pair)] * bf16(HEAD ** (-0.5)))
        scores = mul_bt(queries, qkv_ref[k_rows, pair_cols(1, pair)])
        scores = jnp.where(mask, scores, -1e30)
        raised = jnp.exp(scores - jnp.max(scores, axis=-1, keepdims=True))
        probs = (raised * (1.0 / jnp.sum(raised, axis=-1, keepdims=True))).astype(bf16)
        half = probs.shape[0] // 2
        mixed = mul(probs, qkv_ref[k_rows, pair_cols(2, pair)])
        att_ref[q_rows, pair_cols(0, pair)] = (mixed[:half] * low + mixed[half:] * high).astype(bf16)


def attend(qkv_ref, att_ref, q_rows, k_rows, mask, keep_sums):
    for pair in range(HEADS // 2):
        queries = qkv_ref[q_rows, pair_cols(0, pair)] * bf16(HEAD ** (-0.5))
        scores = mul_bt(two_heads(qkv_ref[k_rows, pair_cols(1, pair)]), queries)
        probs, sums = softmax_down(scores, mask)
        vals = two_heads(qkv_ref[k_rows, pair_cols(2, pair)])
        mixed = mul_at(jnp.concatenate(probs, axis=0).astype(bf16), vals)
        att_ref[q_rows, pair_cols(0, pair)] = mixed.astype(bf16)
        for k in range(2):
            keep_sums(2 * pair + k, sums[k])


def text_front_kernel(
    x_ref, g1_ref, b1_ref, wqkv_ref, wo_ref, g2_ref, b2_ref, h1_ref, qkv_ref, att_ref, mid_ref,
    h2_ref, sum_ref, lse_ref
):
    rows, chunk = x_ref.shape[0], 128
    norm_rows(x_ref, h1_ref, line(g1_ref), line(b1_ref), chunk)

    @pl.loop(0, 3 * D // 256)
    def _(step):
        at = pl.ds(pl.multiple_of(step * 256, 256), 256)
        qkv_ref[:, at] = mul(h1_ref[...], wqkv_ref[:, at]).astype(bf16)

    mask = same_sequence(chunk, 0, chunk, 0, TXT_LEN)

    @pl.loop(0, rows // chunk)
    def _(step):
        at = pl.ds(pl.multiple_of(step * chunk, chunk), chunk)

        def keep_sums(head, value):
            lse_ref[pl.ds(step * 16 + head, 1), :] = value

        attend(qkv_ref, att_ref, at, at, mask, keep_sums)

    @pl.loop(0, D // 256)
    def _(step):
        at = pl.ds(pl.multiple_of(step * 256, 256), 256)
        mid_ref[:, at] = x_ref[:, at].astype(f32) + mul(att_ref[...], wo_ref[:, at])

    norm_rows(mid_ref, h2_ref, line(g2_ref), line(b2_ref), chunk)
    per = chunk // TXT_LEN

    @pl.loop(0, rows // chunk)
    def _(step):
        values = mid_ref[pl.ds(pl.multiple_of(step * chunk, chunk), chunk), :]
        sum_ref[pl.ds(pl.multiple_of(step * per, per), per), :] = jnp.sum(
            values.reshape(per, TXT_LEN, D), axis=1
        )


def text_front(rows_in, gain1, bias1, wqkv, wo, gain2, bias2):
    rows = rows_in.shape[0]
    shapes = [
        ((rows, D), bf16),
        ((rows, 3 * D), bf16),
        ((rows, D), bf16),
        ((rows, D), f32),
        ((rows, D), bf16),
        ((rows // TXT_LEN, D), f32),
        ((rows // 128 * 16, 128), f32),
    ]
    return pl.pallas_call(
        text_front_kernel,
        out_shape=[jax.ShapeDtypeStruct(*item) for item in shapes],
        compiler_params=params(),
        cost_estimate=cost(rows * D * D * 8, 14 * D * rows + 8 * D * D, rows * 128 * HEADS),
        name="text_front",
    )(rows_in, gain1, bias1, wqkv, wo, gain2, bias2)


def image_front_kernel(
    windows, x_ref, order_ref, g1_ref, b1_ref, g2_ref, b2_ref, *refs
):
    h2_ref, sum_ref, w_ref, h1_ref, placed_ref, qkv_ref, att_ref, mid_ref, sems = refs[-9:]
    rows, chunk = x_ref.shape[0], 80
    copies, row = [], 0
    for k, piece in enumerate(refs[:-9]):
        place = w_ref.at[pl.ds(row, piece.shape[0]), :]
        copies.append(pltpu.make_async_copy(piece, place, sems.at[k]))
        row += piece.shape[0]
    for copy in copies:
        copy.start()

    def place_columns(src, dst):
        @pl.loop(0, D // 256)
        def _(step):
            at = pl.ds(pl.multiple_of(step * 256, 256), 256)
            dst[:, at] = mul_bt(src[...], chosen(order_ref[at, :])).astype(bf16)

    norm_rows(x_ref, h1_ref, line(g1_ref), line(b1_ref), chunk)
    place_columns(h1_ref, placed_ref)
    for copy in copies:
        copy.wait()

    @pl.loop(0, 3 * D // 256)
    def _(step):
        at = pl.ds(pl.multiple_of(step * 256, 256), 256)
        qkv_ref[:, at] = mul(placed_ref[...], w_ref[:, at]).astype(bf16)

    for row0, count, key0, keys in windows:
        one = same_sequence(count, row0, keys, key0, IMG_LEN)
        mask = jnp.concatenate([one, one], axis=0)
        attend_along(qkv_ref, att_ref, pl.ds(row0, count), pl.ds(key0, keys), mask)
    place_columns(att_ref, placed_ref)

    @pl.loop(0, D // 256)
    def _(step):
        at = pl.ds(pl.multiple_of(step * 256, 256), 256)
        there = pl.ds(pl.multiple_of(step * 256 + 3 * D, 256), 256)
        mid_ref[:, at] = x_ref[:, at].astype(f32) + mul(placed_ref[...], w_ref[:, there])

    norm_rows(mid_ref, h2_ref, line(g2_ref), line(b2_ref), chunk)
    for k in range(rows // IMG_LEN):
        first, last = k * IMG_LEN, (k + 1) * IMG_LEN
        start, end = first // 8 * 8, -(-last // 8) * 8
        values = mid_ref[start:end, :]
        place = lax.broadcasted_iota(jnp.int32, values.shape, 0) + start
        inside = (place >= first) & (place < last)
        sum_ref[k : k + 1, :] = jnp.sum(jnp.where(inside, values, 0.0), axis=0, keepdims=True)


def image_front(rows_in, pieces, source, gain1, bias1, gain2, bias2):
    rows = rows_in.shape[0]
    windows = ((0, 208, 0, 256), (208, 192, 192, 208))
    vmem = pl.BlockSpec(memory_space=pltpu.VMEM)
    return pl.pallas_call(
        functools.partial(image_front_kernel, windows),
        out_shape=[
            jax.ShapeDtypeStruct((rows, D), bf16),
            jax.ShapeDtypeStruct((rows // IMG_LEN, D), f32),
        ],
        in_specs=[vmem] * 6 + anywhere(pieces),
        out_specs=[vmem] * 2,
        scratch_shapes=[
            pltpu.VMEM((D, 4 * D), bf16),
            pltpu.VMEM((rows, D), bf16),
            pltpu.VMEM((rows, D), bf16),
            pltpu.VMEM((rows, 3 * D), bf16),
            pltpu.VMEM((rows, D), bf16),
            pltpu.VMEM((rows, D), f32),
            pltpu.SemaphoreType.DMA((len(pieces),)),
        ],
        compiler_params=params(),
        cost_estimate=cost(rows * D * D * 12, 8 * D * D, rows * 256 * HEADS),
        name="image_front",
    )(rows_in, source, gain1, bias1, gain2, bias2, *pieces)


def gelu_parts(inner):
    half = 0.5 * (1.0 + lax.erf(inner * (0.5**0.5)))
    return inner * half, half


def pack_kernel(unit_ref, pos_ref, *refs):
    refs[-1][:, :D] = unit_ref[...].astype(bf16)
    refs[-1][:, D:] = pos_ref[...]


def packed(unit, positive, after):
    shape = (unit.shape[0], D + positive.shape[1])
    return pl.pallas_call(
        pack_kernel,
        out_shape=jax.ShapeDtypeStruct(shape, bf16),
        in_specs=[pl.BlockSpec(memory_space=pltpu.VMEM)] * 2 + anywhere(after),
        compiler_params=params(),
        cost_estimate=cost(shape[0] * shape[1], 4 * shape[0] * shape[1]),
        name="packed",
    )(unit, positive, *after)


def pool_matrix(count, rows, row0, seq_len):
    row = (lax.broadcasted_iota(jnp.int32, (count, rows), 1) + row0) // seq_len
    return jnp.where(row == lax.broadcasted_iota(jnp.int32, (count, rows), 0), 1.0, 0.0).astype(bf16)


def two_terms(mean):
    high = mean.astype(bf16)
    low = (mean - high.astype(f32)).astype(bf16)
    return jnp.concatenate([high, low], axis=0)


def unit_rows(pooled):
    inverse = lax.rsqrt(jnp.sum(pooled * pooled, axis=-1, keepdims=True) + norm_eps)
    return pooled * inverse, inverse


def text_up_kernel(h2_ref, wu_ref, wd_ref, sum_ref, *refs):
    slope_ref, hid_ref, unit_ref, inv_ref, acc = refs[-5:]
    step = pl.program_id(0)
    chunk = 320
    per = chunk // TXT_LEN
    pool = pool_matrix(per, chunk, 0, TXT_LEN)
    for k in range(h2_ref.shape[0] // chunk):
        inner = mul(h2_ref[k * chunk : (k + 1) * chunk, :], wu_ref[...])
        value, half = gelu_parts(inner)
        slope = half + inner * (jnp.exp(-0.5 * inner * inner) * 0.3989422804014327)
        slope_ref[k * chunk : (k + 1) * chunk, :] = slope.astype(bf16)
        hid_ref[k * per : (k + 1) * per, :] = mul(pool, value.astype(bf16))
    terms = mul(two_terms(hid_ref[...] * (1.0 / TXT_LEN)), wd_ref[...])
    count = hid_ref.shape[0]
    added = terms[:count] + terms[count:]

    @pl.when(step == 0)
    def _():
        acc[...] = sum_ref[...] * (1.0 / TXT_LEN) + added

    @pl.when(step > 0)
    def _():
        acc[...] += added

    @pl.when(step == pl.num_programs(0) - 1)
    def _():
        unit, inverse = unit_rows(acc[...])
        unit_ref[...] = unit
        inv_ref[...] = jnp.broadcast_to(inverse, inv_ref.shape)


def text_up(normed2, weight_up, weight_down, middle_sum, after=()):
    rows, count = normed2.shape[0], middle_sum.shape[0]
    fixed = lambda shape: pl.BlockSpec(shape, lambda i: (0, 0))
    return pl.pallas_call(
        text_up_kernel,
        grid=(FF // TILE,),
        out_shape=[
            jax.ShapeDtypeStruct((rows, FF), bf16),
            jax.ShapeDtypeStruct((count, FF), f32),
            jax.ShapeDtypeStruct((count, D), f32),
            jax.ShapeDtypeStruct((count, 128), f32),
        ],
        in_specs=[
            fixed((rows, D)),
            pl.BlockSpec((D, TILE), lambda i: (0, i)),
            pl.BlockSpec((TILE, D), lambda i: (i, 0)),
            fixed((count, D)),
        ]
        + anywhere(after),
        out_specs=[
            pl.BlockSpec((rows, TILE), lambda i: (0, i)),
            pl.BlockSpec((count, TILE), lambda i: (0, i)),
            fixed((count, D)),
            fixed((count, 128)),
        ],
        scratch_shapes=[pltpu.VMEM((count, D), f32)],
        compiler_params=params(),
        cost_estimate=cost(2 * rows * D * FF, 4 * D * FF + 2 * rows * FF, 20 * rows * FF),
        name="text_up",
    )(normed2, weight_up, weight_down, middle_sum, *after)


def image_up_kernel(fold, h2_ref, wu_ref, wd_ref, sum_ref, *refs):
    out_ref, acc, chosen_ref = refs[-3:]
    step = pl.program_id(0)
    rows, count = h2_ref.shape[0], sum_ref.shape[0]
    part = TILE // fold

    @pl.when(step == 0)
    def _():
        place = lax.broadcasted_iota(jnp.int32, (TILE, TILE), 0)
        col = lax.broadcasted_iota(jnp.int32, (TILE, TILE), 1)
        source = (col % part) * fold + col // part
        chosen_ref[...] = jnp.where(place == source, 1.0, 0.0).astype(bf16)

    inner = mul(h2_ref[...], wu_ref[...])
    value, _ = gelu_parts(inner)
    summed = mul(pool_matrix(count, rows, 0, IMG_LEN), value.astype(bf16))
    mean = two_terms(summed * (1.0 / IMG_LEN))
    moved = mul(mean, chosen_ref[...]).astype(bf16)
    weight = jnp.concatenate([wd_ref[:, k * D : (k + 1) * D] for k in range(fold)], axis=0)
    terms = mul(moved, weight)
    added = terms[:count] + terms[count:]

    @pl.when(step == 0)
    def _():
        acc[...] = sum_ref[...] * (1.0 / IMG_LEN) + added

    @pl.when(step > 0)
    def _():
        acc[...] += added

    @pl.when(step == pl.num_programs(0) - 1)
    def _():
        out_ref[...] = unit_rows(acc[...])[0].astype(bf16)


def image_up(normed2, whole, up_col, down_col, middle_sum, after=()):
    rows, count = normed2.shape[0], middle_sum.shape[0]
    fold = FF // D
    fixed = lambda shape: pl.BlockSpec(shape, lambda i: (0, 0))
    return pl.pallas_call(
        functools.partial(image_up_kernel, fold),
        grid=(FF // TILE,),
        out_shape=jax.ShapeDtypeStruct((count, D), bf16),
        in_specs=[
            fixed((rows, D)),
            pl.BlockSpec((D, TILE), lambda i: (0, up_col // TILE + i)),
            pl.BlockSpec((TILE // fold, fold * D), lambda i: (i, down_col // (fold * D))),
            fixed((count, D)),
        ]
        + anywhere(after),
        out_specs=fixed((count, D)),
        scratch_shapes=[pltpu.VMEM((count, D), f32), pltpu.VMEM((TILE, TILE), bf16)],
        compiler_params=params(),
        cost_estimate=cost(2 * rows * D * FF, 4 * D * FF, 15 * rows * FF),
        name="image_up",
    )(normed2, whole, whole, middle_sum, *after)


def left_kernel(count, *refs):
    out_ref = refs[-1]
    for k in range(count):
        source_ref, values_ref = refs[2 * k : 2 * k + 2]

        @pl.loop(0, D // 256)
        def _(step, k=k, source_ref=source_ref, values_ref=values_ref):
            at = pl.ds(pl.multiple_of(step * 256, 256), 256)
            picked = mul_bt(chosen(source_ref[at, :]), values_ref[...])
            out_ref[k, at, :] = picked.astype(bf16)


def left_factors(*pairs):
    rows = pairs[0][1].shape[0]
    given = [item for pair in pairs for item in pair]
    return pl.pallas_call(
        functools.partial(left_kernel, len(pairs)),
        out_shape=jax.ShapeDtypeStruct((len(pairs), D, rows), bf16),
        in_specs=in_vmem(len(given)),
        out_specs=pl.BlockSpec(memory_space=pltpu.VMEM),
        compiler_params=params(24 << 20),
        cost_estimate=cost(2 * len(pairs) * rows * D * D, 4 * len(pairs) * rows * D),
        name="left_factors",
    )(*given)


def loss_parts(text_rows, pos, image_all):
    similar = mul_bt(text_rows, image_all) * logit_scale
    shifted = jnp.exp(similar - logit_scale)
    alive = jnp.max(pos, axis=1, keepdims=True)
    row_sum = jnp.sum(shifted, axis=1, keepdims=True)
    row_count = jnp.maximum(jnp.sum(pos, axis=1, keepdims=True), 1.0)
    return similar, shifted, alive, row_sum, row_count


def sums_over_captions(text_rows, pos, image_all):
    similar, shifted, alive, row_sum, row_count = loss_parts(text_rows, pos, image_all)
    pos_similar = pos * similar
    cap_term = alive * (
        logit_scale + jnp.log(row_sum) - jnp.sum(pos_similar, axis=1, keepdims=True) / row_count
    )
    return (
        jnp.sum(alive * shifted, axis=0, keepdims=True),
        jnp.sum(pos, axis=0, keepdims=True),
        jnp.sum(pos_similar, axis=0, keepdims=True),
        jnp.sum(cap_term, axis=0, keepdims=True),
        jnp.sum(alive, axis=0, keepdims=True),
    )


def loss_from(sums):
    col_sum, col_count, col_pos, cap_total, live_total = sums
    img_term = logit_scale + jnp.log(col_sum) - col_pos / col_count
    return 0.5 * cap_total / live_total + 0.5 * jnp.mean(img_term, axis=1, keepdims=True)


def grad_of_unit(text_rows, pos, image_all, col_sum, col_count, live_total):
    _, shifted, alive, row_sum, row_count = loss_parts(text_rows, pos, image_all)
    cap_share, img_share = 0.5 / live_total, 0.5 / image_all.shape[0]
    grad_sims = alive * shifted * (cap_share / row_sum + img_share / col_sum) - pos * (
        cap_share / row_count + img_share / col_count
    )
    return mul(grad_sims.astype(bf16), image_all) * logit_scale


def turned(grad, unit):
    return grad - unit * jnp.sum(grad * unit, axis=-1, keepdims=True)


def loss_kernel(
    pack_ref, image_ref, own_ref, unit_ref, inv_ref, loss_ref, row_ref, low_ref, col_sum_ref,
    col_count_ref, live_ref
):
    image_all = image_ref[...]
    chunk = 256
    total = None
    for k in range(pack_ref.shape[0] // chunk):
        at = slice(k * chunk, (k + 1) * chunk)
        part = sums_over_captions(pack_ref[at, :D], pack_ref[at, D:].astype(f32), image_all)
        total = part if total is None else [a + b for a, b in zip(total, part)]
    loss_ref[...] = jnp.broadcast_to(loss_from(total), loss_ref.shape)
    col_sum, col_count, _, _, live_total = total
    col_sum_ref[...] = col_sum
    col_count_ref[...] = col_count
    live_ref[...] = jnp.broadcast_to(live_total, live_ref.shape)
    grad = grad_of_unit(
        own_ref[:, :D], own_ref[:, D:].astype(f32), image_all, col_sum, col_count, live_total
    )
    row = inv_ref[:, :1] * turned(grad, unit_ref[...]) * (1.0 / TXT_LEN)
    row_ref[...] = row
    low_ref[...] = row.astype(bf16)


def loss_and_rows(pack, image_all, own_pack, unit, inverse):
    images, count = image_all.shape[0], own_pack.shape[0]
    shapes = [(1, 128), (count, D), (count, D), (1, images), (1, images), (1, 128)]
    kinds = [f32, f32, bf16, f32, f32, f32]
    return pl.pallas_call(
        loss_kernel,
        out_shape=[jax.ShapeDtypeStruct(*item) for item in zip(shapes, kinds)],
        in_specs=in_vmem(5),
        out_specs=in_vmem(len(shapes)),
        compiler_params=params(16 << 20),
        cost_estimate=cost(2 * pack.shape[0] * images * D, 2 * pack.size, pack.shape[0] * images),
        name="loss_and_rows",
    )(pack, image_all, own_pack, unit, inverse)


def down_kernel(pack_ref, image_ref, col_sum_ref, col_count_ref, live_ref, hid_ref, *refs):
    step, out_ref = pl.program_id(0), refs[-1]
    text_rows = pack_ref[:, :D]
    grad = grad_of_unit(
        text_rows, pack_ref[:, D:].astype(f32), image_ref[...], col_sum_ref[...],
        col_count_ref[...], live_ref[:, :1]
    )
    rows = (turned(grad, text_rows.astype(f32)) * (1.0 / TXT_LEN)).astype(bf16)
    part = mul_at(hid_ref[...], rows)

    @pl.when(step == 0)
    def _():
        out_ref[...] = part

    @pl.when(step > 0)
    def _():
        out_ref[...] += part


def grad_of_down(pack, image_all, col_sum, col_count, live_total, hidden_cols, after):
    images, chunk = image_all.shape[0], 256
    fixed = lambda shape: pl.BlockSpec(shape, lambda i: (0, 0))
    per = hidden_cols.shape[1]
    return pl.pallas_call(
        down_kernel,
        grid=(pack.shape[0] // chunk,),
        out_shape=jax.ShapeDtypeStruct((per, D), f32),
        in_specs=[
            pl.BlockSpec((chunk, pack.shape[1]), lambda i: (i, 0)),
            fixed((images, D)), fixed((1, images)), fixed((1, images)), fixed((1, 128)),
            pl.BlockSpec((chunk, per), lambda i: (i, 0)),
        ]
        + anywhere(after),
        out_specs=fixed((per, D)),
        compiler_params=params(16 << 20),
        cost_estimate=cost(4 * pack.shape[0] * images * D, 2 * pack.size, pack.shape[0] * images),
        name="grad_of_down",
    )(pack, image_all, col_sum, col_count, live_total, hidden_cols, *after)


def mlp_back_kernel(
    low_ref, wd_ref, slope_ref, wu_ref, lhs_ref, mid_ref, gain_ref, row_ref, keep_a, send_a, keep_b,
    send_b, out_ref, sums_out
):
    count, rows = low_ref.shape[0], slope_ref.shape[0]
    half, steps = D // 2, FF // 2 // TILE
    for k, (keep, send) in enumerate(((keep_a, send_a), (keep_b, send_b))):

        @pl.loop(0, steps)
        def _(step, k=k, keep=keep, send=send):
            at = pl.ds(pl.multiple_of(k * (FF // 2) + step * TILE, TILE), TILE)
            there = pl.ds(pl.multiple_of(step * TILE, TILE), TILE)
            hidden = mul_bt(low_ref[...], wd_ref[at, :])
            wide = jnp.broadcast_to(hidden[:, None, :], (count, TXT_LEN, TILE))
            inner = (wide.reshape(rows, TILE) * slope_ref[:, at].astype(f32)).astype(bf16)
            weight = mul(lhs_ref[k], inner).astype(bf16)
            keep[:, there] = weight[:half]
            send[:, there] = weight[half:]
            added = mul_bt(inner, wu_ref[:, at])
            if k == 0:

                @pl.when(step == 0)
                def _():
                    out_ref[...] = added

                @pl.when(step > 0)
                def _():
                    out_ref[...] += added
            else:
                out_ref[...] += added

    chunk = 128
    per = chunk // TXT_LEN
    gain = line(gain_ref)
    sums_out[...] = jnp.zeros_like(sums_out)

    @pl.loop(0, rows // chunk)
    def _(k):
        at = pl.ds(pl.multiple_of(k * chunk, chunk), chunk)
        unit, scale = norm_parts(mid_ref[at, :])
        grad = out_ref[at, :]
        sums_out[:, :D] += jnp.sum(grad * unit, axis=0, keepdims=True)
        sums_out[:, D:] += jnp.sum(grad, axis=0, keepdims=True)
        row = row_ref[pl.ds(pl.multiple_of(k * per, per), per), :]
        row = jnp.broadcast_to(row[:, None, :], (per, TXT_LEN, D)).reshape(chunk, D)
        out_ref[at, :] = row + norm_back(unit, scale, gain, grad)


def mlp_back(grad_row, grad_low, weight_down, slope, weight_up, lhs, middle, gain):
    rows = slope.shape[0]
    return pl.pallas_call(
        mlp_back_kernel,
        out_shape=[stays((D // 2, FF // 2), bf16)] * 4
        + [stays((rows, D), f32), stays((1, 2 * D), f32)],
        in_specs=in_vmem(8),
        out_specs=in_vmem(6),
        compiler_params=params(16 << 20),
        cost_estimate=cost(4 * rows * D * FF, 4 * D * FF + 2 * rows * FF + 2 * D * FF, rows * FF),
        name="mlp_back",
    )(grad_low, weight_down, slope, weight_up, lhs, middle, gain, grad_row)


def attention_back_kernel(first, grad_ref, wo_ref, qkv_ref, lse_ref, *refs):
    low_ref, out_ref = refs[-2:]
    chunk = 128
    mask = same_sequence(chunk, 0, chunk, 0, TXT_LEN)

    @pl.loop(0, low_ref.shape[0] // chunk)
    def _(step):
        here = pl.ds(pl.multiple_of((first + step) * chunk, chunk), chunk)
        there = pl.ds(pl.multiple_of(step * chunk, chunk), chunk)
        sums = lse_ref[pl.ds(pl.multiple_of((first + step) * 16, 16), 16), :]
        low = grad_ref[here, :].astype(bf16)
        low_ref[there, :] = low
        grad_att = mul_bt(low, wo_ref[...]).astype(bf16)
        for pair in range(HEADS // 2):
            queries = qkv_ref[here, pair_cols(0, pair)] * bf16(HEAD ** (-0.5))
            keys = two_heads(qkv_ref[here, pair_cols(1, pair)])
            vals = two_heads(qkv_ref[here, pair_cols(2, pair)])
            grads = grad_att[:, pair_cols(0, pair)]
            scores, grad_probs = mul_bt(keys, queries), mul_bt(vals, grads)
            probs, grad_scores = [], []
            for k in range(2):
                at = slice(k * chunk, (k + 1) * chunk)
                head = 2 * pair + k
                shifted = scores[at] - sums[head : head + 1, :]
                prob = jnp.where(mask, jnp.exp(jnp.where(mask, shifted, 0.0)), 0.0)
                along = jnp.sum(grad_probs[at] * prob, axis=0, keepdims=True)
                grad_scores.append((prob * (grad_probs[at] - along)).astype(bf16))
                probs.append(prob.astype(bf16))
            grad_q = mul_at(jnp.concatenate(grad_scores, axis=0), keys) * HEAD ** (-0.5)
            grad_k = mul(jnp.concatenate(grad_scores, axis=1), two_heads(queries))
            grad_v = mul(jnp.concatenate(probs, axis=1), two_heads(grads))
            out_ref[there, pair_cols(0, pair)] = grad_q.astype(bf16)
            out_ref[there, pair_cols(1, pair)] = grad_k.astype(bf16)
            out_ref[there, pair_cols(2, pair)] = grad_v.astype(bf16)


def attention_back(grad_middle, weight_out, project, log_sums, first, count, after=()):
    rows = count * 128
    return pl.pallas_call(
        functools.partial(attention_back_kernel, first),
        out_shape=[stays((rows, D), bf16), stays((rows, 3 * D), bf16)],
        in_specs=in_vmem(4) + anywhere(after),
        out_specs=in_vmem(2),
        compiler_params=params(16 << 20),
        cost_estimate=cost(10 * rows * D * D, 16 * rows * D + 2 * D * D, rows * 128 * HEADS),
        name="attention_back",
    )(grad_middle, weight_out, project, log_sums, *after)


def mul_rows(lhs, parts, cols):
    total, row = 0.0, 0
    for part in parts:
        total = total + mul(lhs[:, row : row + part.shape[0]], part[:, cols])
        row += part.shape[0]
    return total


def weight_back_kernel(factors, groups, lhs_ref, *refs):
    keep_a, send_a, keep_b, send_b = refs[-4:]
    half = D // 2
    for k, (factor, group, col) in enumerate(factors):
        parts = refs[sum(groups[:group]) : sum(groups[: group + 1])]
        weight = mul_rows(lhs_ref.at[factor], parts, slice(col * D, (col + 1) * D)).astype(bf16)
        at = slice(k % 2 * D, (k % 2 + 1) * D)
        (keep_b if k > 1 else keep_a)[:, at] = weight[:half]
        (send_b if k > 1 else send_a)[:, at] = weight[half:]


def weight_back(lhs, groups, factors, after=()):
    rows = lhs.shape[2]
    given = [part for group in groups for part in group]
    return pl.pallas_call(
        functools.partial(weight_back_kernel, factors, [len(group) for group in groups]),
        out_shape=[stays((D // 2, 2 * D), bf16)] * 4,
        in_specs=in_vmem(1 + len(given)) + anywhere(after),
        out_specs=in_vmem(4),
        compiler_params=params(16 << 20),
        cost_estimate=cost(8 * rows * D * D, 8 * rows * D + 14 * D * D),
        name="weight_back",
    )(lhs, *given, *after)


def input_back_kernel(count, *refs):
    projs = refs[:count]
    w_ref, x_ref, gain_ref, mid_ref, sums_ref = refs[count : count + 5]
    out_ref, sums_out = refs[-2:]
    rows, chunk = x_ref.shape[0], 128

    @pl.loop(0, D // 256)
    def _(step):
        at = pl.ds(pl.multiple_of(step * 256, 256), 256)
        row = 0
        for part in projs:
            there = slice(row, row + part.shape[0])
            out_ref[there, at] = mul_bt(part[...], w_ref[at, :])
            row += part.shape[0]

    gain = line(gain_ref)
    sums_out[...] = jnp.zeros_like(sums_out)
    sums_out[1:2, :] = sums_ref[...]

    @pl.loop(0, rows // chunk)
    def _(k):
        at = pl.ds(pl.multiple_of(k * chunk, chunk), chunk)
        unit, scale = norm_parts(x_ref[at, :].astype(f32))
        grad = out_ref[at, :]
        sums_out[0:1, :D] += jnp.sum(grad * unit, axis=0, keepdims=True)
        sums_out[0:1, D:] += jnp.sum(grad, axis=0, keepdims=True)
        out_ref[at, :] = mid_ref[at, :] + norm_back(unit, scale, gain, grad)


def input_back(grad_projs, weight, rows_in, gain, grad_middle, sums, after=()):
    rows = rows_in.shape[0]
    return pl.pallas_call(
        functools.partial(input_back_kernel, len(grad_projs)),
        out_shape=[jax.ShapeDtypeStruct((rows, D), f32), stays((8, 2 * D), f32)],
        in_specs=in_vmem(len(grad_projs) + 5) + anywhere(after),
        out_specs=in_vmem(2),
        compiler_params=params(16 << 20),
        cost_estimate=cost(6 * rows * D * D, 14 * rows * D + 6 * D * D),
        name="input_back",
    )(*grad_projs, weight, rows_in, gain, grad_middle, sums, *after)


def local(
    images,
    captions,
    img_gain1,
    img_bias1,
    img_qkv,
    img_out,
    img_gain2,
    img_bias2,
    img_up,
    img_down,
    txt_gain1,
    txt_bias1,
    txt_qkv,
    txt_out,
    txt_gain2,
    txt_bias2,
    txt_up,
    txt_down,
    counts,
    matches,
):
    peers = lax.axis_size(AXIS)
    own = lax.axis_index(AXIS)
    per = D // peers
    img_local = counts.shape[0]
    cap_local = matches.shape[0]
    total_images = matches.shape[1]

    whole = lax.all_gather(
        jnp.concatenate([img_up.reshape(per, FF), img_down.reshape(per, FF)], axis=1),
        AXIS,
        axis=0,
        tiled=True,
    )
    small = peers == 32
    shard = jnp.concatenate([img_qkv.reshape(per, 3 * D), img_out.reshape(per, D)], axis=1)
    if small:
        line, source = gathered_line(shard), row_order((1, 4, 2, 16, 8))
    else:
        line, source = lax.all_gather(shard, AXIS, axis=0, tiled=True), row_order(())

    normed1, project, attended, middle, normed2, middle_sum, log_sums = text_front(
        captions, txt_gain1, txt_bias1, txt_qkv, txt_out, txt_gain2, txt_bias2
    )
    middle_sum, line = in_turn(middle_sum, line)
    beside, above = (swapped(line, 2), swapped(line, 4)) if small else (line, line)
    slope, hidden_sum, text_unit, inverse = text_up(
        normed2, txt_up, txt_down, middle_sum, (line,)
    )
    text_unit, (beside, above) = in_turn(text_unit, (beside, above))

    ends_at = jnp.cumsum(counts)
    slot_ids = lax.iota(jnp.int32, cap_local)
    owner = jnp.sum((ends_at[None, :] <= slot_ids[:, None]).astype(jnp.int32), axis=1)
    owner = owner + own * img_local
    live = slot_ids < ends_at[-1]
    columns = lax.iota(jnp.int32, total_images)
    positive = ((matches > 0) | (owner[:, None] == columns[None, :])) & live[:, None]

    order_a, order_b, tail = stage_orders()
    source_a, source_b = row_order(order_a + tail[::-1]), row_order(order_b + tail[::-1])
    own_pack = packed(text_unit, positive.astype(bf16), ())
    own_pack, hidden_sum, normed2 = lax.optimization_barrier((own_pack, hidden_sum, normed2))
    lhs_up = left_factors((source_a, normed2), (source_b, normed2))
    pieces = [line]
    if small:
        held = own_pack[None]
        first, second = diagonal(beside, above)
        others = [swapped(held, mask) for mask in (8, 16, 24)]
        scaled_sum = (hidden_sum * inverse[:, :1]).astype(bf16)
        hidden_cols = lax.all_to_all(scaled_sum, AXIS, split_axis=1, concat_axis=0, tiled=True)
        others, first, second, hidden_cols, lhs_up = lax.optimization_barrier(
            (others, first, second, hidden_cols, lhs_up)
        )
        held = joined(joined(held, others[0], 8), joined(others[1], others[2], 8), 16, 1)
        text_beside, text_above = swapped(held, 2), swapped(held, 4)
        pieces = [line, beside, above, first, second]
        pieces = pieces + [swapped(piece, 1) for piece in pieces]

    normed_img, middle_img = image_front(
        images, pieces, source, img_gain1, img_bias1, img_gain2, img_bias2
    )
    if small:
        normed_img, text_beside, text_above = lax.optimization_barrier(
            (normed_img, text_beside, text_above)
        )
        across = jnp.concatenate(diagonal(text_beside, text_above), axis=0)
        held = joined(joined(held, text_beside, 2), joined(text_above, across, 2), 4, 4)

    if small:
        whole, held = in_turn(whole, held)
        other = swapped(held, 1)
    image_low = image_up(normed_img, whole, 0, FF, middle_img)
    if small:
        text_pack = joined(held, other, 1).reshape(-1, D + total_images)
    image_all = spread(image_low).reshape(total_images, D)
    if small:
        image_all, text_pack = in_turn(image_all, text_pack)

    if small:
        loss_value, grad_row, row_low, col_sum, col_count, live_total = loss_and_rows(
            text_pack, image_all, own_pack, text_unit, inverse
        )
        loss_value = loss_value[0, 0]
    else:
        text_low, pos = own_pack[:, :D], own_pack[:, D:].astype(f32)
        sums = lax.psum(sums_over_captions(text_low, pos, image_all), AXIS)
        loss_value = loss_from(sums)[0, 0]
        grad = grad_of_unit(text_low, pos, image_all, sums[0], sums[1], sums[4])
        grad_row = inverse[:, :1] * turned(grad, text_unit) * (1.0 / TXT_LEN)
        row_low = grad_row.astype(bf16)

    *up, grad_middle, sums = mlp_back(
        grad_row, row_low, txt_down, slope, txt_up, lhs_up, middle, txt_gain2
    )
    stages = len(order_a)
    low_one, proj_one = attention_back(grad_middle, txt_out, project, log_sums, 0, 1)
    for stage in range(stages - 2):
        up = fold(hand_on(up, stage), (proj_one,))
    low_two, proj_two = attention_back(grad_middle, txt_out, project, log_sums, 1, 4, up)
    proj_two, normed1 = in_turn(proj_two, normed1)
    lhs_rest = left_factors((source_a, normed1), (source_b, normed1), (source_b, attended))
    up = fold(hand_on(up, stages - 2), (proj_two, lhs_rest))
    projs, lows = (proj_one, proj_two), (low_one, low_two)
    rest = weight_back(lhs_rest, [projs, lows], [(0, 0, 0), (0, 0, 1), (1, 0, 2), (2, 1, 0)], up)
    up = hand_on(up, stages - 1)
    caption_grad, sums = input_back(
        projs, txt_qkv, captions, txt_gain1, grad_middle, sums, rest[:1]
    )
    caption_grad, up = in_turn(caption_grad, up)
    up = fold_last(up)
    if small:
        *rest, sums = fold(hand_on(rest, 0), up[:1], (sums, swapped(sums, 1)))
    else:
        norms = lax.psum(sums, AXIS)[:2].reshape(-1)
        for stage in range(stages - 2):
            rest = fold(hand_on(rest, stage), up[:1])
    up = hand_on_last(up)
    rest = hand_on(rest, stages - 2)
    if small:
        grad_down = grad_of_down(
            text_pack, image_all, col_sum, col_count, live_total, hidden_cols, (caption_grad,)
        )
    else:
        grad_down = lax.psum_scatter(
            mul_at(hidden_sum.astype(bf16), row_low), AXIS, scatter_dimension=0, tiled=True
        )
    grad_down, rest, up = lax.optimization_barrier((grad_down, rest, up))
    if small:
        *rest, sums = fold(rest, (), (sums,))
        rest = fold_last(hand_on(rest, stages - 1), (), (sums,))
    else:
        rest = fold_last(hand_on(fold(rest), stages - 1))
    up_share = sum_last(*up)
    rest_share = sum_last(*hand_on_last(rest))
    if small:
        norms = rest_share[per]
        rest_share = rest_share[:per]
    return (
        loss_value,
        caption_grad,
        norms[:D],
        norms[D : 2 * D],
        rest_share[:, : 3 * D].reshape(-1),
        rest_share[:, 3 * D :].reshape(-1),
        norms[2 * D : 3 * D],
        norms[3 * D :],
        up_share.reshape(-1),
        grad_down.reshape(-1),
    )


def solution(mesh):
    split, flat, whole = P("blk", None), P("blk"), P()
    image_block = (whole, whole, flat, flat, whole, whole, flat, flat)
    return jax.shard_map(
        local,
        mesh=mesh,
        in_specs=(split, split) + image_block + (whole,) * 8 + (flat, split),
        out_specs=(whole, split, whole, whole, flat, flat, whole, whole, flat, flat),
        check_vma=False,
    )
```

```python
import functools

import jax
import jax.numpy as jnp
from jax import lax
from jax.experimental import pallas as pl
from jax.experimental.pallas import tpu as pltpu
from jax.sharding import PartitionSpec as P

D = 768
FF = 3072
HEAD = 64
HEADS = D // HEAD
IMG_LEN = 50
TXT_LEN = 16
AXIS = "blk"

norm_eps = 1e-06
logit_scale = 50.0
f32 = jnp.float32
bf16 = jnp.bfloat16


def swapped(value, mask):
    peers = lax.axis_size(AXIS)
    return lax.ppermute(value, AXIS, [(i, i ^ mask) for i in range(peers)])


def bit_masks():
    peers = lax.axis_size(AXIS)
    return [1 << k for k in range(peers.bit_length() - 1)]


def joined(held, other, mask, outer=None):
    upper = (lax.axis_index(AXIS) & mask) > 0
    first = jnp.where(upper, other, held)
    second = jnp.where(upper, held, other)
    outer = held.shape[0] if outer is None else outer
    parts = [part.reshape((outer, -1) + held.shape[1:]) for part in (first, second)]
    return jnp.stack(parts, axis=1).reshape((-1,) + held.shape[1:])


def spread(block):
    peers = lax.axis_size(AXIS)
    copies = jnp.broadcast_to(block[None], (peers,) + block.shape)
    return lax.all_to_all(copies, AXIS, split_axis=0, concat_axis=0, tiled=True)


def stage_orders():
    masks = bit_masks()
    head, tail = masks[:-2], masks[-2:]
    order_a = list(head)
    order_b = list(head)
    for k in range(1, len(head) - 1, 2):
        order_b[k], order_b[k + 1] = order_b[k + 1], order_b[k]
    return order_a, order_b, tail


def row_order(bits):
    peers = lax.axis_size(AXIS)
    own = lax.axis_index(AXIS)
    per = D // peers
    places = lax.broadcasted_iota(jnp.int32, (D, 1), 0)
    block = places // per
    target = jnp.zeros_like(block) + own
    for k, mask in enumerate(bits):
        target = target ^ (((block >> (len(bits) - 1 - k)) & 1) * mask)
    return target * per + places % per


def chosen(source):
    column = lax.broadcasted_iota(jnp.int32, (source.shape[0], D), 1)
    return jnp.where(column == source, 1.0, 0.0).astype(bf16)


def gathered_line(shard):
    return jnp.concatenate([shard] + [swapped(shard, mask) for mask in (8, 16, 24)], axis=0)


def diagonal(beside, above):
    half = beside.shape[0] // 2
    return swapped(beside[:half], 4), swapped(above[half:], 2)


def in_turn(first, then):
    return lax.optimization_barrier((first, then))


def hand_on(parts, stage):
    order_a, order_b, _ = stage_orders()
    keep_a, send_a, keep_b, send_b = parts
    return keep_a, swapped(send_a, order_a[stage]), keep_b, swapped(send_b, order_b[stage])


def hand_on_last(blocks):
    low, high = stage_orders()[2]
    own, *others = blocks
    return own, [swapped(block, mask) for block, mask in zip(others, (low, high, low | high))]


def sum_last(own, others):
    total = own
    for other in others:
        total = total + other.astype(f32)
    return total


VMEM_BYTES = 56 << 20
TILE = 512


def norm_parts(values):
    average = jnp.mean(values, axis=-1, keepdims=True)
    centred = values - average
    variance = jnp.mean(centred * centred, axis=-1, keepdims=True)
    scale = lax.rsqrt(variance + norm_eps)
    return centred * scale, scale


def norm_back(unit, scale, gain, grad):
    inner = grad * gain
    shift = jnp.mean(inner, axis=-1, keepdims=True)
    along = jnp.mean(inner * unit, axis=-1, keepdims=True)
    return scale * (inner - shift - unit * along)


def mul(lhs, rhs):
    return jnp.dot(lhs, rhs, preferred_element_type=f32)


def mul_bt(lhs, rhs):
    return lax.dot_general(lhs, rhs, (((1,), (1,)), ((), ())), preferred_element_type=f32)


def mul_at(lhs, rhs):
    return lax.dot_general(lhs, rhs, (((0,), (0,)), ((), ())), preferred_element_type=f32)


def params(limit=VMEM_BYTES):
    return pltpu.CompilerParams(vmem_limit_bytes=limit)


def in_vmem(count):
    return [pl.BlockSpec(memory_space=pltpu.VMEM)] * count


def in_hbm(*arrays):
    return [pltpu.with_memory_space_constraint(array, pltpu.HBM) for array in arrays]


def stays(shape, dtype):
    return pltpu.VMEM(shape, dtype)


def cost(flops, moved, transcendentals=0):
    return pl.CostEstimate(flops=flops, bytes_accessed=moved, transcendentals=transcendentals)


def lane_halves(dtype):
    lane = lax.broadcasted_iota(jnp.int32, (1, 2 * HEAD), 1)
    low = jnp.where(lane < HEAD, 1.0, 0.0)
    return low.astype(dtype), (1.0 - low).astype(dtype)


def two_heads(pair):
    low, high = lane_halves(bf16)
    return jnp.concatenate([pair * low, pair * high], axis=0)


def same_sequence(rows, row0, cols, col0, seq_len):
    row = (lax.broadcasted_iota(jnp.int32, (rows, cols), 0) + row0) // seq_len
    col = (lax.broadcasted_iota(jnp.int32, (rows, cols), 1) + col0) // seq_len
    return row == col


def softmax_down(scores, mask):
    keys = mask.shape[0]
    parts, sums = [], []
    for k in range(2):
        part = jnp.where(mask, scores[k * keys : (k + 1) * keys], -1e30)
        most = jnp.max(part, axis=0, keepdims=True)
        raised = jnp.exp(part - most)
        total = jnp.sum(raised, axis=0, keepdims=True)
        parts.append(raised * (1.0 / total))
        sums.append(most + jnp.log(total))
    return parts, sums


def fold_kernel(extra, keep_a, got_a, keep_b, got_b, *refs):
    outs = refs[-5:] if extra else refs[-4:]
    rows, half, tile = keep_a.shape[0], keep_a.shape[0] // 2, 256

    @pl.loop(0, keep_a.shape[1] // tile)
    def _(step):
        cols = pl.ds(pl.multiple_of(step * tile, tile), tile)
        for k, (kept, got) in enumerate(((keep_a, got_a), (keep_b, got_b))):
            for j in range(2):
                at = slice(j * half, (j + 1) * half)
                total = kept[at, cols].astype(f32) + got[at, cols].astype(f32)
                outs[2 * k + j][:half, cols] = total.astype(bf16)

    if extra:
        came = refs[1][...] if extra > 1 else got_a[rows : rows + 16, :].astype(f32)[:8]
        sums = refs[0][...] + came
        outs[4][...] = sums
        outs[1][half : half + 16, :] = jnp.concatenate([sums, sums], axis=0).astype(bf16)


def fold(parts, after=(), sums=()):
    rows, cols = parts[0].shape
    if rows % 32:
        whole = [
            (kept.astype(f32) + got.astype(f32)).astype(bf16)
            for kept, got in (parts[:2], parts[2:])
        ]
        return [part for one in whole for part in (one[: rows // 2], one[rows // 2 :])]
    half = (rows // 2, cols)
    shapes = [stays(half, bf16)] * 4
    if sums:
        shapes[1] = stays((rows // 2 + 16, cols), bf16)
        shapes.append(stays((8, cols), f32))
    return pl.pallas_call(
        functools.partial(fold_kernel, len(sums)),
        out_shape=shapes,
        in_specs=in_vmem(4 + len(sums)) + anywhere(after),
        out_specs=in_vmem(len(shapes)),
        compiler_params=params(8 << 20),
        cost_estimate=cost(2 * rows * cols, 12 * rows * cols),
        name="fold",
    )(*parts, *sums, *after)


def fold_last_kernel(extra, keep_a, got_a, keep_b, got_b, *refs):
    outs = refs[-4:]
    cols = keep_a.shape[1]
    rows = keep_a.shape[0] // 4
    if extra:
        sums = refs[0][...] + got_a[4 * rows : 4 * rows + 16, :].astype(f32)[:8]
    for k, (kept, got) in enumerate(((keep_a, got_a), (keep_b, got_b))):
        total = kept[...].astype(f32) + got[: 4 * rows, :].astype(f32)
        at = slice(k * cols, (k + 1) * cols)
        for j, out in enumerate(outs):
            part = total[j * rows : (j + 1) * rows]
            if extra:
                row = jnp.broadcast_to(sums[k : k + 1], (8, cols))
                part = jnp.concatenate([part, row], axis=0)
            out[:, at] = part.astype(out.dtype)


def fold_last(parts, after=(), sums=()):
    rows, cols = parts[0].shape
    shape = (rows // 4 + (8 if sums else 0), 2 * cols)
    if rows % 32:
        pairs = (parts[:2], parts[2:])
        both = [kept.astype(f32) + got.astype(f32) for kept, got in pairs]
        own, *others = jnp.split(jnp.concatenate(both, axis=1), 4)
        return [own] + [other.astype(bf16) for other in others]
    return pl.pallas_call(
        functools.partial(fold_last_kernel, len(sums)),
        out_shape=[stays(shape, f32)] + [stays(shape, bf16)] * 3,
        in_specs=in_vmem(4 + len(sums)) + anywhere(after),
        out_specs=in_vmem(4),
        compiler_params=params(8 << 20),
        cost_estimate=cost(2 * rows * cols, 12 * rows * cols),
        name="fold_last",
    )(*parts, *sums, *after)


def anywhere(after):
    return [pl.BlockSpec(memory_space=pl.ANY)] * len(after)


def pair_cols(part, pair):
    start = part * D + pair * 2 * HEAD
    return slice(start, start + 2 * HEAD)


def line(ref):
    return ref[...].astype(f32).reshape(1, -1)


def norm_rows(src, dst, gain, bias, step_rows):
    @pl.loop(0, src.shape[0] // step_rows)
    def _(step):
        at = pl.ds(pl.multiple_of(step * step_rows, step_rows), step_rows)
        unit, _ = norm_parts(src[at, :].astype(f32))
        dst[at, :] = (unit * gain + bias).astype(bf16)


def attend_along(qkv_ref, att_ref, q_rows, k_rows, mask):
    low, high = lane_halves(f32)
    for pair in range(HEADS // 2):
        queries = two_heads(qkv_ref[q_rows, pair_cols(0, pair)] * bf16(HEAD ** (-0.5)))
        scores = mul_bt(queries, qkv_ref[k_rows, pair_cols(1, pair)])
        scores = jnp.where(mask, scores, -1e30)
        raised = jnp.exp(scores - jnp.max(scores, axis=-1, keepdims=True))
        probs = (raised * (1.0 / jnp.sum(raised, axis=-1, keepdims=True))).astype(bf16)
        half = probs.shape[0] // 2
        mixed = mul(probs, qkv_ref[k_rows, pair_cols(2, pair)])
        att_ref[q_rows, pair_cols(0, pair)] = (mixed[:half] * low + mixed[half:] * high).astype(bf16)


def attend(qkv_ref, att_ref, q_rows, k_rows, mask, keep_sums):
    for pair in range(HEADS // 2):
        queries = qkv_ref[q_rows, pair_cols(0, pair)] * bf16(HEAD ** (-0.5))
        scores = mul_bt(two_heads(qkv_ref[k_rows, pair_cols(1, pair)]), queries)
        probs, sums = softmax_down(scores, mask)
        vals = two_heads(qkv_ref[k_rows, pair_cols(2, pair)])
        mixed = mul_at(jnp.concatenate(probs, axis=0).astype(bf16), vals)
        att_ref[q_rows, pair_cols(0, pair)] = mixed.astype(bf16)
        for k in range(2):
            keep_sums(2 * pair + k, sums[k])


def text_front_kernel(
    x_ref, g1_ref, b1_ref, wqkv_ref, wo_ref, g2_ref, b2_ref, h1_ref, qkv_ref, att_ref, mid_ref,
    h2_ref, sum_ref, lse_ref
):
    rows, chunk = x_ref.shape[0], 128
    norm_rows(x_ref, h1_ref, line(g1_ref), line(b1_ref), chunk)

    @pl.loop(0, 3 * D // 256)
    def _(step):
        at = pl.ds(pl.multiple_of(step * 256, 256), 256)
        qkv_ref[:, at] = mul(h1_ref[...], wqkv_ref[:, at]).astype(bf16)

    mask = same_sequence(chunk, 0, chunk, 0, TXT_LEN)

    @pl.loop(0, rows // chunk)
    def _(step):
        at = pl.ds(pl.multiple_of(step * chunk, chunk), chunk)

        def keep_sums(head, value):
            lse_ref[pl.ds(step * 16 + head, 1), :] = value

        attend(qkv_ref, att_ref, at, at, mask, keep_sums)

    @pl.loop(0, D // 256)
    def _(step):
        at = pl.ds(pl.multiple_of(step * 256, 256), 256)
        mid_ref[:, at] = x_ref[:, at].astype(f32) + mul(att_ref[...], wo_ref[:, at])

    norm_rows(mid_ref, h2_ref, line(g2_ref), line(b2_ref), chunk)
    per = chunk // TXT_LEN

    @pl.loop(0, rows // chunk)
    def _(step):
        values = mid_ref[pl.ds(pl.multiple_of(step * chunk, chunk), chunk), :]
        sum_ref[pl.ds(pl.multiple_of(step * per, per), per), :] = jnp.sum(
            values.reshape(per, TXT_LEN, D), axis=1
        )


def text_front(rows_in, gain1, bias1, wqkv, wo, gain2, bias2):
    rows = rows_in.shape[0]
    shapes = [
        ((rows, D), bf16),
        ((rows, 3 * D), bf16),
        ((rows, D), bf16),
        ((rows, D), f32),
        ((rows, D), bf16),
        ((rows // TXT_LEN, D), f32),
        ((rows // 128 * 16, 128), f32),
    ]
    return pl.pallas_call(
        text_front_kernel,
        out_shape=[jax.ShapeDtypeStruct(*item) for item in shapes],
        compiler_params=params(),
        cost_estimate=cost(rows * D * D * 8, 14 * D * rows + 8 * D * D, rows * 128 * HEADS),
        name="text_front",
    )(rows_in, gain1, bias1, wqkv, wo, gain2, bias2)


def image_front_kernel(
    windows, x_ref, order_ref, g1_ref, b1_ref, g2_ref, b2_ref, *refs
):
    h2_ref, sum_ref, w_ref, h1_ref, placed_ref, qkv_ref, att_ref, mid_ref, sems = refs[-9:]
    rows, chunk = x_ref.shape[0], 80
    copies, row = [], 0
    for k, piece in enumerate(refs[:-9]):
        place = w_ref.at[pl.ds(row, piece.shape[0]), :]
        copies.append(pltpu.make_async_copy(piece, place, sems.at[k]))
        row += piece.shape[0]
    for copy in copies:
        copy.start()

    def place_columns(src, dst):
        @pl.loop(0, D // 256)
        def _(step):
            at = pl.ds(pl.multiple_of(step * 256, 256), 256)
            dst[:, at] = mul_bt(src[...], chosen(order_ref[at, :])).astype(bf16)

    norm_rows(x_ref, h1_ref, line(g1_ref), line(b1_ref), chunk)
    place_columns(h1_ref, placed_ref)
    for copy in copies:
        copy.wait()

    @pl.loop(0, 3 * D // 256)
    def _(step):
        at = pl.ds(pl.multiple_of(step * 256, 256), 256)
        qkv_ref[:, at] = mul(placed_ref[...], w_ref[:, at]).astype(bf16)

    for row0, count, key0, keys in windows:
        one = same_sequence(count, row0, keys, key0, IMG_LEN)
        mask = jnp.concatenate([one, one], axis=0)
        attend_along(qkv_ref, att_ref, pl.ds(row0, count), pl.ds(key0, keys), mask)
    place_columns(att_ref, placed_ref)

    @pl.loop(0, D // 256)
    def _(step):
        at = pl.ds(pl.multiple_of(step * 256, 256), 256)
        there = pl.ds(pl.multiple_of(step * 256 + 3 * D, 256), 256)
        mid_ref[:, at] = x_ref[:, at].astype(f32) + mul(placed_ref[...], w_ref[:, there])

    norm_rows(mid_ref, h2_ref, line(g2_ref), line(b2_ref), chunk)
    for k in range(rows // IMG_LEN):
        first, last = k * IMG_LEN, (k + 1) * IMG_LEN
        start, end = first // 8 * 8, -(-last // 8) * 8
        values = mid_ref[start:end, :]
        place = lax.broadcasted_iota(jnp.int32, values.shape, 0) + start
        inside = (place >= first) & (place < last)
        sum_ref[k : k + 1, :] = jnp.sum(jnp.where(inside, values, 0.0), axis=0, keepdims=True)


def image_front(rows_in, pieces, source, gain1, bias1, gain2, bias2):
    rows = rows_in.shape[0]
    windows = ((0, 208, 0, 256), (208, 192, 192, 208))
    vmem = pl.BlockSpec(memory_space=pltpu.VMEM)
    return pl.pallas_call(
        functools.partial(image_front_kernel, windows),
        out_shape=[
            jax.ShapeDtypeStruct((rows, D), bf16),
            jax.ShapeDtypeStruct((rows // IMG_LEN, D), f32),
        ],
        in_specs=[vmem] * 6 + anywhere(pieces),
        out_specs=[vmem] * 2,
        scratch_shapes=[
            pltpu.VMEM((D, 4 * D), bf16),
            pltpu.VMEM((rows, D), bf16),
            pltpu.VMEM((rows, D), bf16),
            pltpu.VMEM((rows, 3 * D), bf16),
            pltpu.VMEM((rows, D), bf16),
            pltpu.VMEM((rows, D), f32),
            pltpu.SemaphoreType.DMA((len(pieces),)),
        ],
        compiler_params=params(),
        cost_estimate=cost(rows * D * D * 12, 8 * D * D, rows * 256 * HEADS),
        name="image_front",
    )(rows_in, source, gain1, bias1, gain2, bias2, *pieces)


def gelu_parts(inner):
    half = 0.5 * (1.0 + lax.erf(inner * (0.5**0.5)))
    return inner * half, half


def pack_kernel(unit_ref, pos_ref, *refs):
    refs[-1][:, :D] = unit_ref[...].astype(bf16)
    refs[-1][:, D:] = pos_ref[...]


def packed(unit, positive, after):
    shape = (unit.shape[0], D + positive.shape[1])
    return pl.pallas_call(
        pack_kernel,
        out_shape=jax.ShapeDtypeStruct(shape, bf16),
        in_specs=[pl.BlockSpec(memory_space=pltpu.VMEM)] * 2 + anywhere(after),
        compiler_params=params(),
        cost_estimate=cost(shape[0] * shape[1], 4 * shape[0] * shape[1]),
        name="packed",
    )(unit, positive, *after)


def pool_matrix(count, rows, row0, seq_len):
    row = (lax.broadcasted_iota(jnp.int32, (count, rows), 1) + row0) // seq_len
    return jnp.where(row == lax.broadcasted_iota(jnp.int32, (count, rows), 0), 1.0, 0.0).astype(bf16)


def two_terms(mean):
    high = mean.astype(bf16)
    low = (mean - high.astype(f32)).astype(bf16)
    return jnp.concatenate([high, low], axis=0)


def unit_rows(pooled):
    inverse = lax.rsqrt(jnp.sum(pooled * pooled, axis=-1, keepdims=True) + norm_eps)
    return pooled * inverse, inverse


def text_up_kernel(h2_ref, wu_ref, wd_ref, sum_ref, *refs):
    slope_ref, hid_ref, unit_ref, inv_ref, acc = refs[-5:]
    step = pl.program_id(0)
    chunk = 320
    per = chunk // TXT_LEN
    pool = pool_matrix(per, chunk, 0, TXT_LEN)
    for k in range(h2_ref.shape[0] // chunk):
        inner = mul(h2_ref[k * chunk : (k + 1) * chunk, :], wu_ref[...])
        value, half = gelu_parts(inner)
        slope = half + inner * (jnp.exp(-0.5 * inner * inner) * 0.3989422804014327)
        slope_ref[k * chunk : (k + 1) * chunk, :] = slope.astype(bf16)
        hid_ref[k * per : (k + 1) * per, :] = mul(pool, value.astype(bf16))
    terms = mul(two_terms(hid_ref[...] * (1.0 / TXT_LEN)), wd_ref[...])
    count = hid_ref.shape[0]
    added = terms[:count] + terms[count:]

    @pl.when(step == 0)
    def _():
        acc[...] = sum_ref[...] * (1.0 / TXT_LEN) + added

    @pl.when(step > 0)
    def _():
        acc[...] += added

    @pl.when(step == pl.num_programs(0) - 1)
    def _():
        unit, inverse = unit_rows(acc[...])
        unit_ref[...] = unit
        inv_ref[...] = jnp.broadcast_to(inverse, inv_ref.shape)


def text_up(normed2, weight_up, weight_down, middle_sum, after=()):
    rows, count = normed2.shape[0], middle_sum.shape[0]
    fixed = lambda shape: pl.BlockSpec(shape, lambda i: (0, 0))
    return pl.pallas_call(
        text_up_kernel,
        grid=(FF // TILE,),
        out_shape=[
            jax.ShapeDtypeStruct((rows, FF), bf16),
            jax.ShapeDtypeStruct((count, FF), f32),
            jax.ShapeDtypeStruct((count, D), f32),
            jax.ShapeDtypeStruct((count, 128), f32),
        ],
        in_specs=[
            fixed((rows, D)),
            pl.BlockSpec((D, TILE), lambda i: (0, i)),
            pl.BlockSpec((TILE, D), lambda i: (i, 0)),
            fixed((count, D)),
        ]
        + anywhere(after),
        out_specs=[
            pl.BlockSpec((rows, TILE), lambda i: (0, i)),
            pl.BlockSpec((count, TILE), lambda i: (0, i)),
            fixed((count, D)),
            fixed((count, 128)),
        ],
        scratch_shapes=[pltpu.VMEM((count, D), f32)],
        compiler_params=params(),
        cost_estimate=cost(2 * rows * D * FF, 4 * D * FF + 2 * rows * FF, 20 * rows * FF),
        name="text_up",
    )(normed2, weight_up, weight_down, middle_sum, *after)


def image_up_kernel(fold, h2_ref, wu_ref, wd_ref, sum_ref, *refs):
    out_ref, acc, chosen_ref = refs[-3:]
    step = pl.program_id(0)
    rows, count = h2_ref.shape[0], sum_ref.shape[0]
    part = TILE // fold

    @pl.when(step == 0)
    def _():
        place = lax.broadcasted_iota(jnp.int32, (TILE, TILE), 0)
        col = lax.broadcasted_iota(jnp.int32, (TILE, TILE), 1)
        source = (col % part) * fold + col // part
        chosen_ref[...] = jnp.where(place == source, 1.0, 0.0).astype(bf16)

    inner = mul(h2_ref[...], wu_ref[...])
    value, _ = gelu_parts(inner)
    summed = mul(pool_matrix(count, rows, 0, IMG_LEN), value.astype(bf16))
    mean = two_terms(summed * (1.0 / IMG_LEN))
    moved = mul(mean, chosen_ref[...]).astype(bf16)
    weight = jnp.concatenate([wd_ref[:, k * D : (k + 1) * D] for k in range(fold)], axis=0)
    terms = mul(moved, weight)
    added = terms[:count] + terms[count:]

    @pl.when(step == 0)
    def _():
        acc[...] = sum_ref[...] * (1.0 / IMG_LEN) + added

    @pl.when(step > 0)
    def _():
        acc[...] += added

    @pl.when(step == pl.num_programs(0) - 1)
    def _():
        out_ref[...] = unit_rows(acc[...])[0].astype(bf16)


def image_up(normed2, whole, up_col, down_col, middle_sum, after=()):
    rows, count = normed2.shape[0], middle_sum.shape[0]
    fold = FF // D
    fixed = lambda shape: pl.BlockSpec(shape, lambda i: (0, 0))
    return pl.pallas_call(
        functools.partial(image_up_kernel, fold),
        grid=(FF // TILE,),
        out_shape=jax.ShapeDtypeStruct((count, D), bf16),
        in_specs=[
            fixed((rows, D)),
            pl.BlockSpec((D, TILE), lambda i: (0, up_col // TILE + i)),
            pl.BlockSpec((TILE // fold, fold * D), lambda i: (i, down_col // (fold * D))),
            fixed((count, D)),
        ]
        + anywhere(after),
        out_specs=fixed((count, D)),
        scratch_shapes=[pltpu.VMEM((count, D), f32), pltpu.VMEM((TILE, TILE), bf16)],
        compiler_params=params(),
        cost_estimate=cost(2 * rows * D * FF, 4 * D * FF, 15 * rows * FF),
        name="image_up",
    )(normed2, whole, whole, middle_sum, *after)


def left_kernel(count, *refs):
    out_ref = refs[-1]
    for k in range(count):
        source_ref, values_ref = refs[2 * k : 2 * k + 2]

        @pl.loop(0, D // 256)
        def _(step, k=k, source_ref=source_ref, values_ref=values_ref):
            at = pl.ds(pl.multiple_of(step * 256, 256), 256)
            picked = mul_bt(chosen(source_ref[at, :]), values_ref[...])
            out_ref[k, at, :] = picked.astype(bf16)


def left_factors(*pairs):
    rows = pairs[0][1].shape[0]
    given = [item for pair in pairs for item in pair]
    return pl.pallas_call(
        functools.partial(left_kernel, len(pairs)),
        out_shape=jax.ShapeDtypeStruct((len(pairs), D, rows), bf16),
        in_specs=in_vmem(len(given)),
        out_specs=pl.BlockSpec(memory_space=pltpu.VMEM),
        compiler_params=params(24 << 20),
        cost_estimate=cost(2 * len(pairs) * rows * D * D, 4 * len(pairs) * rows * D),
        name="left_factors",
    )(*given)


def loss_parts(text_rows, pos, image_all):
    similar = mul_bt(text_rows, image_all) * logit_scale
    shifted = jnp.exp(similar - logit_scale)
    alive = jnp.max(pos, axis=1, keepdims=True)
    row_sum = jnp.sum(shifted, axis=1, keepdims=True)
    row_count = jnp.maximum(jnp.sum(pos, axis=1, keepdims=True), 1.0)
    return similar, shifted, alive, row_sum, row_count


def sums_over_captions(text_rows, pos, image_all):
    similar, shifted, alive, row_sum, row_count = loss_parts(text_rows, pos, image_all)
    pos_similar = pos * similar
    cap_term = alive * (
        logit_scale + jnp.log(row_sum) - jnp.sum(pos_similar, axis=1, keepdims=True) / row_count
    )
    return (
        jnp.sum(alive * shifted, axis=0, keepdims=True),
        jnp.sum(pos, axis=0, keepdims=True),
        jnp.sum(pos_similar, axis=0, keepdims=True),
        jnp.sum(cap_term, axis=0, keepdims=True),
        jnp.sum(alive, axis=0, keepdims=True),
    )


def loss_from(sums):
    col_sum, col_count, col_pos, cap_total, live_total = sums
    img_term = logit_scale + jnp.log(col_sum) - col_pos / col_count
    return 0.5 * cap_total / live_total + 0.5 * jnp.mean(img_term, axis=1, keepdims=True)


def grad_of_unit(text_rows, pos, image_all, col_sum, col_count, live_total):
    _, shifted, alive, row_sum, row_count = loss_parts(text_rows, pos, image_all)
    cap_share, img_share = 0.5 / live_total, 0.5 / image_all.shape[0]
    grad_sims = alive * shifted * (cap_share / row_sum + img_share / col_sum) - pos * (
        cap_share / row_count + img_share / col_count
    )
    return mul(grad_sims.astype(bf16), image_all) * logit_scale


def turned(grad, unit):
    return grad - unit * jnp.sum(grad * unit, axis=-1, keepdims=True)


def loss_kernel(
    pack_ref, image_ref, own_ref, unit_ref, inv_ref, loss_ref, row_ref, low_ref, col_sum_ref,
    col_count_ref, live_ref
):
    image_all = image_ref[...]
    chunk = 256
    total = None
    for k in range(pack_ref.shape[0] // chunk):
        at = slice(k * chunk, (k + 1) * chunk)
        part = sums_over_captions(pack_ref[at, :D], pack_ref[at, D:].astype(f32), image_all)
        total = part if total is None else [a + b for a, b in zip(total, part)]
    loss_ref[...] = jnp.broadcast_to(loss_from(total), loss_ref.shape)
    col_sum, col_count, _, _, live_total = total
    col_sum_ref[...] = col_sum
    col_count_ref[...] = col_count
    live_ref[...] = jnp.broadcast_to(live_total, live_ref.shape)
    grad = grad_of_unit(
        own_ref[:, :D], own_ref[:, D:].astype(f32), image_all, col_sum, col_count, live_total
    )
    row = inv_ref[:, :1] * turned(grad, unit_ref[...]) * (1.0 / TXT_LEN)
    row_ref[...] = row
    low_ref[...] = row.astype(bf16)


def loss_and_rows(pack, image_all, own_pack, unit, inverse):
    images, count = image_all.shape[0], own_pack.shape[0]
    shapes = [(1, 128), (count, D), (count, D), (1, images), (1, images), (1, 128)]
    kinds = [f32, f32, bf16, f32, f32, f32]
    return pl.pallas_call(
        loss_kernel,
        out_shape=[jax.ShapeDtypeStruct(*item) for item in zip(shapes, kinds)],
        in_specs=in_vmem(5),
        out_specs=in_vmem(len(shapes)),
        compiler_params=params(16 << 20),
        cost_estimate=cost(2 * pack.shape[0] * images * D, 2 * pack.size, pack.shape[0] * images),
        name="loss_and_rows",
    )(pack, image_all, own_pack, unit, inverse)


def down_kernel(pack_ref, image_ref, col_sum_ref, col_count_ref, live_ref, hid_ref, *refs):
    step, out_ref = pl.program_id(0), refs[-1]
    text_rows = pack_ref[:, :D]
    grad = grad_of_unit(
        text_rows, pack_ref[:, D:].astype(f32), image_ref[...], col_sum_ref[...],
        col_count_ref[...], live_ref[:, :1]
    )
    rows = (turned(grad, text_rows.astype(f32)) * (1.0 / TXT_LEN)).astype(bf16)
    part = mul_at(hid_ref[...], rows)

    @pl.when(step == 0)
    def _():
        out_ref[...] = part

    @pl.when(step > 0)
    def _():
        out_ref[...] += part


def grad_of_down(pack, image_all, col_sum, col_count, live_total, hidden_cols, after):
    images, chunk = image_all.shape[0], 256
    fixed = lambda shape: pl.BlockSpec(shape, lambda i: (0, 0))
    per = hidden_cols.shape[1]
    return pl.pallas_call(
        down_kernel,
        grid=(pack.shape[0] // chunk,),
        out_shape=jax.ShapeDtypeStruct((per, D), f32),
        in_specs=[
            pl.BlockSpec((chunk, pack.shape[1]), lambda i: (i, 0)),
            fixed((images, D)), fixed((1, images)), fixed((1, images)), fixed((1, 128)),
            pl.BlockSpec((chunk, per), lambda i: (i, 0)),
        ]
        + anywhere(after),
        out_specs=fixed((per, D)),
        compiler_params=params(16 << 20),
        cost_estimate=cost(4 * pack.shape[0] * images * D, 2 * pack.size, pack.shape[0] * images),
        name="grad_of_down",
    )(pack, image_all, col_sum, col_count, live_total, hidden_cols, *after)


def mlp_back_kernel(
    low_ref, gain_ref, row_ref, wd_hbm, slope_hbm, wu_hbm, lhs_hbm, mid_hbm, keep_a, send_a, keep_b,
    send_b, out_ref, sums_out, wd_ref, slope_ref, wu_ref, lhs_ref, mid_ref, sems, whole_sems
):
    count, rows = low_ref.shape[0], out_ref.shape[0]
    half, steps = D // 2, FF // 2 // TILE

    def copies(tile, slot):
        at = pl.ds(pl.multiple_of(tile * TILE, TILE), TILE)
        return (
            pltpu.make_async_copy(wd_hbm.at[at, :], wd_ref.at[slot], sems.at[0, slot]),
            pltpu.make_async_copy(slope_hbm.at[:, at], slope_ref.at[slot], sems.at[1, slot]),
            pltpu.make_async_copy(wu_hbm.at[:, at], wu_ref.at[slot], sems.at[2, slot]),
        )

    lhs_copy = pltpu.make_async_copy(lhs_hbm, lhs_ref, whole_sems.at[0])
    mid_copy = pltpu.make_async_copy(mid_hbm, mid_ref, whole_sems.at[1])
    for copy in copies(0, 0):
        copy.start()
    lhs_copy.start()
    for k, (keep, send) in enumerate(((keep_a, send_a), (keep_b, send_b))):

        @pl.loop(0, steps)
        def _(step, k=k, keep=keep, send=send):
            tile = k * steps + step
            slot = lax.rem(tile, 2)

            @pl.when(tile + 1 < 2 * steps)
            def _():
                for copy in copies(tile + 1, 1 - slot):
                    copy.start()

            for copy in copies(tile, slot):
                copy.wait()
            if k == 0:

                @pl.when(step == 0)
                def _():
                    lhs_copy.wait()
                    mid_copy.start()

            there = pl.ds(pl.multiple_of(step * TILE, TILE), TILE)
            hidden = mul_bt(low_ref[...], wd_ref[slot])
            wide = jnp.broadcast_to(hidden[:, None, :], (count, TXT_LEN, TILE))
            inner = (wide.reshape(rows, TILE) * slope_ref[slot].astype(f32)).astype(bf16)
            weight = mul(lhs_ref[k], inner).astype(bf16)
            keep[:, there] = weight[:half]
            send[:, there] = weight[half:]
            added = mul_bt(inner, wu_ref[slot])
            if k == 0:

                @pl.when(step == 0)
                def _():
                    out_ref[...] = added

                @pl.when(step > 0)
                def _():
                    out_ref[...] += added
            else:
                out_ref[...] += added

    chunk = 128
    per = chunk // TXT_LEN
    gain = line(gain_ref)
    sums_out[...] = jnp.zeros_like(sums_out)
    mid_copy.wait()

    @pl.loop(0, rows // chunk)
    def _(k):
        at = pl.ds(pl.multiple_of(k * chunk, chunk), chunk)
        unit, scale = norm_parts(mid_ref[at, :])
        grad = out_ref[at, :]
        sums_out[:, :D] += jnp.sum(grad * unit, axis=0, keepdims=True)
        sums_out[:, D:] += jnp.sum(grad, axis=0, keepdims=True)
        row = row_ref[pl.ds(pl.multiple_of(k * per, per), per), :]
        row = jnp.broadcast_to(row[:, None, :], (per, TXT_LEN, D)).reshape(chunk, D)
        out_ref[at, :] = row + norm_back(unit, scale, gain, grad)


def mlp_back(grad_row, grad_low, weight_down, slope, weight_up, lhs, middle, gain):
    rows = slope.shape[0]
    return pl.pallas_call(
        mlp_back_kernel,
        out_shape=[stays((D // 2, FF // 2), bf16)] * 4
        + [stays((rows, D), f32), stays((1, 2 * D), f32)],
        in_specs=in_vmem(3) + [pl.BlockSpec(memory_space=pltpu.HBM)] * 5,
        out_specs=in_vmem(6),
        scratch_shapes=[
            pltpu.VMEM((2, TILE, D), bf16),
            pltpu.VMEM((2, rows, TILE), bf16),
            pltpu.VMEM((2, D, TILE), bf16),
            pltpu.VMEM((2, D, rows), bf16),
            pltpu.VMEM((rows, D), f32),
            pltpu.SemaphoreType.DMA((3, 2)),
            pltpu.SemaphoreType.DMA((2,)),
        ],
        compiler_params=params(28 << 20),
        cost_estimate=cost(4 * rows * D * FF, 4 * D * FF + 2 * rows * FF + 2 * D * FF, rows * FF),
        name="mlp_back",
    )(grad_low, gain, grad_row, *in_hbm(weight_down, slope, weight_up, lhs, middle))


def attention_back_kernel(first, grad_ref, wo_ref, qkv_ref, lse_ref, *refs):
    low_ref, out_ref = refs[-2:]
    chunk = 128
    mask = same_sequence(chunk, 0, chunk, 0, TXT_LEN)

    @pl.loop(0, low_ref.shape[0] // chunk)
    def _(step):
        here = pl.ds(pl.multiple_of((first + step) * chunk, chunk), chunk)
        there = pl.ds(pl.multiple_of(step * chunk, chunk), chunk)
        sums = lse_ref[pl.ds(pl.multiple_of((first + step) * 16, 16), 16), :]
        low = grad_ref[here, :].astype(bf16)
        low_ref[there, :] = low
        grad_att = mul_bt(low, wo_ref[...]).astype(bf16)
        for pair in range(HEADS // 2):
            queries = qkv_ref[here, pair_cols(0, pair)] * bf16(HEAD ** (-0.5))
            keys = two_heads(qkv_ref[here, pair_cols(1, pair)])
            vals = two_heads(qkv_ref[here, pair_cols(2, pair)])
            grads = grad_att[:, pair_cols(0, pair)]
            scores, grad_probs = mul_bt(keys, queries), mul_bt(vals, grads)
            probs, grad_scores = [], []
            for k in range(2):
                at = slice(k * chunk, (k + 1) * chunk)
                head = 2 * pair + k
                shifted = scores[at] - sums[head : head + 1, :]
                prob = jnp.where(mask, jnp.exp(jnp.where(mask, shifted, 0.0)), 0.0)
                along = jnp.sum(grad_probs[at] * prob, axis=0, keepdims=True)
                grad_scores.append((prob * (grad_probs[at] - along)).astype(bf16))
                probs.append(prob.astype(bf16))
            grad_q = mul_at(jnp.concatenate(grad_scores, axis=0), keys) * HEAD ** (-0.5)
            grad_k = mul(jnp.concatenate(grad_scores, axis=1), two_heads(queries))
            grad_v = mul(jnp.concatenate(probs, axis=1), two_heads(grads))
            out_ref[there, pair_cols(0, pair)] = grad_q.astype(bf16)
            out_ref[there, pair_cols(1, pair)] = grad_k.astype(bf16)
            out_ref[there, pair_cols(2, pair)] = grad_v.astype(bf16)


def attention_back(grad_middle, weight_out, project, log_sums, first, count, after=()):
    rows = count * 128
    return pl.pallas_call(
        functools.partial(attention_back_kernel, first),
        out_shape=[stays((rows, D), bf16), stays((rows, 3 * D), bf16)],
        in_specs=in_vmem(4) + anywhere(after),
        out_specs=in_vmem(2),
        compiler_params=params(16 << 20),
        cost_estimate=cost(10 * rows * D * D, 16 * rows * D + 2 * D * D, rows * 128 * HEADS),
        name="attention_back",
    )(grad_middle, weight_out, project, log_sums, *after)


def mul_rows(lhs, parts, cols):
    total, row = 0.0, 0
    for part in parts:
        total = total + mul(lhs[:, row : row + part.shape[0]], part[:, cols])
        row += part.shape[0]
    return total


def weight_back_kernel(factors, groups, lhs_ref, *refs):
    keep_a, send_a, keep_b, send_b = refs[-4:]
    half = D // 2
    for k, (factor, group, col) in enumerate(factors):
        parts = refs[sum(groups[:group]) : sum(groups[: group + 1])]
        weight = mul_rows(lhs_ref.at[factor], parts, slice(col * D, (col + 1) * D)).astype(bf16)
        at = slice(k % 2 * D, (k % 2 + 1) * D)
        (keep_b if k > 1 else keep_a)[:, at] = weight[:half]
        (send_b if k > 1 else send_a)[:, at] = weight[half:]


def weight_back(lhs, groups, factors, after=()):
    rows = lhs.shape[2]
    given = [part for group in groups for part in group]
    return pl.pallas_call(
        functools.partial(weight_back_kernel, factors, [len(group) for group in groups]),
        out_shape=[stays((D // 2, 2 * D), bf16)] * 4,
        in_specs=in_vmem(1 + len(given)) + anywhere(after),
        out_specs=in_vmem(4),
        compiler_params=params(16 << 20),
        cost_estimate=cost(8 * rows * D * D, 8 * rows * D + 14 * D * D),
        name="weight_back",
    )(lhs, *given, *after)


def input_back_kernel(count, *refs):
    projs = refs[:count]
    w_ref, x_ref, gain_ref, mid_ref, sums_ref = refs[count : count + 5]
    out_ref, sums_out = refs[-2:]
    rows, chunk = x_ref.shape[0], 128

    @pl.loop(0, D // 256)
    def _(step):
        at = pl.ds(pl.multiple_of(step * 256, 256), 256)
        row = 0
        for part in projs:
            there = slice(row, row + part.shape[0])
            out_ref[there, at] = mul_bt(part[...], w_ref[at, :])
            row += part.shape[0]

    gain = line(gain_ref)
    sums_out[...] = jnp.zeros_like(sums_out)
    sums_out[1:2, :] = sums_ref[...]

    @pl.loop(0, rows // chunk)
    def _(k):
        at = pl.ds(pl.multiple_of(k * chunk, chunk), chunk)
        unit, scale = norm_parts(x_ref[at, :].astype(f32))
        grad = out_ref[at, :]
        sums_out[0:1, :D] += jnp.sum(grad * unit, axis=0, keepdims=True)
        sums_out[0:1, D:] += jnp.sum(grad, axis=0, keepdims=True)
        out_ref[at, :] = mid_ref[at, :] + norm_back(unit, scale, gain, grad)


def input_back(grad_projs, weight, rows_in, gain, grad_middle, sums, after=()):
    rows = rows_in.shape[0]
    return pl.pallas_call(
        functools.partial(input_back_kernel, len(grad_projs)),
        out_shape=[jax.ShapeDtypeStruct((rows, D), f32), stays((8, 2 * D), f32)],
        in_specs=in_vmem(len(grad_projs) + 5) + anywhere(after),
        out_specs=in_vmem(2),
        compiler_params=params(16 << 20),
        cost_estimate=cost(6 * rows * D * D, 14 * rows * D + 6 * D * D),
        name="input_back",
    )(*grad_projs, weight, rows_in, gain, grad_middle, sums, *after)


def local(
    images,
    captions,
    img_gain1,
    img_bias1,
    img_qkv,
    img_out,
    img_gain2,
    img_bias2,
    img_up,
    img_down,
    txt_gain1,
    txt_bias1,
    txt_qkv,
    txt_out,
    txt_gain2,
    txt_bias2,
    txt_up,
    txt_down,
    counts,
    matches,
):
    peers = lax.axis_size(AXIS)
    own = lax.axis_index(AXIS)
    per = D // peers
    img_local = counts.shape[0]
    cap_local = matches.shape[0]
    total_images = matches.shape[1]

    whole = lax.all_gather(
        jnp.concatenate([img_up.reshape(per, FF), img_down.reshape(per, FF)], axis=1),
        AXIS,
        axis=0,
        tiled=True,
    )
    small = peers == 32
    shard = jnp.concatenate([img_qkv.reshape(per, 3 * D), img_out.reshape(per, D)], axis=1)
    if small:
        line, source = gathered_line(shard), row_order((1, 4, 2, 16, 8))
    else:
        line, source = lax.all_gather(shard, AXIS, axis=0, tiled=True), row_order(())

    normed1, project, attended, middle, normed2, middle_sum, log_sums = text_front(
        captions, txt_gain1, txt_bias1, txt_qkv, txt_out, txt_gain2, txt_bias2
    )
    middle_sum, line = in_turn(middle_sum, line)
    beside, above = (swapped(line, 2), swapped(line, 4)) if small else (line, line)
    slope, hidden_sum, text_unit, inverse = text_up(
        normed2, txt_up, txt_down, middle_sum, (line,)
    )
    text_unit, normed2, beside, above = lax.optimization_barrier(
        (text_unit, normed2, beside, above)
    )

    ends_at = jnp.cumsum(counts)
    slot_ids = lax.iota(jnp.int32, cap_local)
    owner = jnp.sum((ends_at[None, :] <= slot_ids[:, None]).astype(jnp.int32), axis=1)
    owner = owner + own * img_local
    live = slot_ids < ends_at[-1]
    columns = lax.iota(jnp.int32, total_images)
    positive = ((matches > 0) | (owner[:, None] == columns[None, :])) & live[:, None]

    order_a, order_b, tail = stage_orders()
    source_a, source_b = row_order(order_a + tail[::-1]), row_order(order_b + tail[::-1])
    own_pack = packed(text_unit, positive.astype(bf16), ())
    lhs_up = left_factors((source_a, normed2), (source_b, normed2))
    pieces = [line]
    if small:
        first, second = diagonal(beside, above)
        own_pack, first, second, lhs_up = lax.optimization_barrier(
            (own_pack, first, second, lhs_up)
        )
        held = own_pack[None]
        others = [swapped(held, mask) for mask in (8, 16, 24)]
        pieces = [line, beside, above, first, second]
        pieces = pieces + [swapped(piece, 1) for piece in pieces]

    normed_img, middle_img = image_front(
        images, pieces, source, img_gain1, img_bias1, img_gain2, img_bias2
    )
    if small:
        scaled_sum = (hidden_sum * inverse[:, :1]).astype(bf16)
        normed_img, scaled_sum, others = lax.optimization_barrier((normed_img, scaled_sum, others))
        held = joined(joined(held, others[0], 8), joined(others[1], others[2], 8), 16, 1)
        text_beside, text_above = swapped(held, 2), swapped(held, 4)
        hidden_cols = lax.all_to_all(scaled_sum, AXIS, split_axis=1, concat_axis=0, tiled=True)
        whole, text_beside, text_above = lax.optimization_barrier((whole, text_beside, text_above))
        halves = diagonal(text_beside, text_above)
    image_low = image_up(normed_img, whole, 0, FF, middle_img)
    if small:
        image_low, halves, hidden_cols = lax.optimization_barrier((image_low, halves, hidden_cols))
        across = jnp.concatenate(halves, axis=0)
        held = joined(joined(held, text_beside, 2), joined(text_above, across, 2), 4, 4)
        text_pack = joined(held, swapped(held, 1), 1).reshape(-1, D + total_images)
    image_all = spread(image_low).reshape(total_images, D)
    if small:
        image_all, text_pack = in_turn(image_all, text_pack)

    if small:
        loss_value, grad_row, row_low, col_sum, col_count, live_total = loss_and_rows(
            text_pack, image_all, own_pack, text_unit, inverse
        )
        loss_value = loss_value[0, 0]
    else:
        text_low, pos = own_pack[:, :D], own_pack[:, D:].astype(f32)
        sums = lax.psum(sums_over_captions(text_low, pos, image_all), AXIS)
        loss_value = loss_from(sums)[0, 0]
        grad = grad_of_unit(text_low, pos, image_all, sums[0], sums[1], sums[4])
        grad_row = inverse[:, :1] * turned(grad, text_unit) * (1.0 / TXT_LEN)
        row_low = grad_row.astype(bf16)

    *up, grad_middle, sums = mlp_back(
        grad_row, row_low, txt_down, slope, txt_up, lhs_up, middle, txt_gain2
    )
    stages = len(order_a)
    low_one, proj_one = attention_back(grad_middle, txt_out, project, log_sums, 0, 1)
    for stage in range(stages - 2):
        up = fold(hand_on(up, stage), (proj_one,))
    low_two, proj_two = attention_back(grad_middle, txt_out, project, log_sums, 1, 4, up)
    proj_two, normed1 = in_turn(proj_two, normed1)
    lhs_rest = left_factors((source_a, normed1), (source_b, normed1), (source_b, attended))
    up = fold(hand_on(up, stages - 2), (proj_two, lhs_rest))
    projs, lows = (proj_one, proj_two), (low_one, low_two)
    rest = weight_back(lhs_rest, [projs, lows], [(0, 0, 0), (0, 0, 1), (1, 0, 2), (2, 1, 0)], up)
    up = hand_on(up, stages - 1)
    caption_grad, sums = input_back(
        projs, txt_qkv, captions, txt_gain1, grad_middle, sums, rest[:1]
    )
    caption_grad, up = in_turn(caption_grad, up)
    up = fold_last(up)
    if small:
        *rest, sums = fold(hand_on(rest, 0), up[:1], (sums, swapped(sums, 1)))
    else:
        norms = lax.psum(sums, AXIS)[:2].reshape(-1)
        for stage in range(stages - 2):
            rest = fold(hand_on(rest, stage), up[:1])
    up = hand_on_last(up)
    rest = hand_on(rest, stages - 2)
    if small:
        grad_down = grad_of_down(
            text_pack, image_all, col_sum, col_count, live_total, hidden_cols, (caption_grad,)
        )
    else:
        grad_down = lax.psum_scatter(
            mul_at(hidden_sum.astype(bf16), row_low), AXIS, scatter_dimension=0, tiled=True
        )
    grad_down, rest, up = lax.optimization_barrier((grad_down, rest, up))
    if small:
        *rest, sums = fold(rest, (), (sums,))
        rest = fold_last(hand_on(rest, stages - 1), (), (sums,))
    else:
        rest = fold_last(hand_on(fold(rest), stages - 1))
    up_share = sum_last(*up)
    rest_share = sum_last(*hand_on_last(rest))
    if small:
        norms = rest_share[per]
        rest_share = rest_share[:per]
    return (
        loss_value,
        caption_grad,
        norms[:D],
        norms[D : 2 * D],
        rest_share[:, : 3 * D].reshape(-1),
        rest_share[:, 3 * D :].reshape(-1),
        norms[2 * D : 3 * D],
        norms[3 * D :],
        up_share.reshape(-1),
        grad_down.reshape(-1),
    )


def solution(mesh):
    split, flat, whole = P("blk", None), P("blk"), P()
    image_block = (whole, whole, flat, flat, whole, whole, flat, flat)
    return jax.shard_map(
        local,
        mesh=mesh,
        in_specs=(split, split) + image_block + (whole,) * 8 + (flat, split),
        out_specs=(whole, split, whole, whole, flat, flat, whole, whole, flat, flat),
        check_vma=False,
    )
```

```python
import functools

import jax
import jax.numpy as jnp
from jax import lax
from jax.experimental import pallas as pl
from jax.experimental.pallas import tpu as pltpu
from jax.sharding import PartitionSpec as P

D = 768
FF = 3072
HEAD = 64
HEADS = D // HEAD
IMG_LEN = 50
TXT_LEN = 16
AXIS = "blk"

norm_eps = 1e-06
logit_scale = 50.0
f32 = jnp.float32
bf16 = jnp.bfloat16


def swapped(value, mask):
    peers = lax.axis_size(AXIS)
    return lax.ppermute(value, AXIS, [(i, i ^ mask) for i in range(peers)])


def bit_masks():
    peers = lax.axis_size(AXIS)
    return [1 << k for k in range(peers.bit_length() - 1)]


def joined(held, other, mask, outer=None):
    upper = (lax.axis_index(AXIS) & mask) > 0
    first = jnp.where(upper, other, held)
    second = jnp.where(upper, held, other)
    outer = held.shape[0] if outer is None else outer
    parts = [part.reshape((outer, -1) + held.shape[1:]) for part in (first, second)]
    return jnp.stack(parts, axis=1).reshape((-1,) + held.shape[1:])


def spread(block):
    peers = lax.axis_size(AXIS)
    copies = jnp.broadcast_to(block[None], (peers,) + block.shape)
    return lax.all_to_all(copies, AXIS, split_axis=0, concat_axis=0, tiled=True)


def stage_orders():
    masks = bit_masks()
    head, tail = masks[:-2], masks[-2:]
    order_a = list(head)
    order_b = list(head)
    for k in range(1, len(head) - 1, 2):
        order_b[k], order_b[k + 1] = order_b[k + 1], order_b[k]
    return order_a, order_b, tail


def row_order(bits):
    peers = lax.axis_size(AXIS)
    own = lax.axis_index(AXIS)
    per = D // peers
    places = lax.broadcasted_iota(jnp.int32, (D, 1), 0)
    block = places // per
    target = jnp.zeros_like(block) + own
    for k, mask in enumerate(bits):
        target = target ^ (((block >> (len(bits) - 1 - k)) & 1) * mask)
    return target * per + places % per


def chosen(source):
    column = lax.broadcasted_iota(jnp.int32, (source.shape[0], D), 1)
    return jnp.where(column == source, 1.0, 0.0).astype(bf16)


def gathered_line(shard):
    return jnp.concatenate([shard] + [swapped(shard, mask) for mask in (8, 16, 24)], axis=0)


def diagonal(beside, above):
    half = beside.shape[0] // 2
    return swapped(beside[:half], 4), swapped(above[half:], 2)


def in_turn(first, then):
    return lax.optimization_barrier((first, then))


def hand_on(parts, stage):
    order_a, order_b, _ = stage_orders()
    keep_a, send_a, keep_b, send_b = parts
    return keep_a, swapped(send_a, order_a[stage]), keep_b, swapped(send_b, order_b[stage])


def hand_on_last(blocks):
    low, high = stage_orders()[2]
    own, *others = blocks
    return own, [swapped(block, mask) for block, mask in zip(others, (low, high, low | high))]


def sum_last(own, others):
    total = own
    for other in others:
        total = total + other.astype(f32)
    return total


VMEM_BYTES = 56 << 20
TILE = 512
EARLY = 2 * TILE


def norm_parts(values):
    average = jnp.mean(values, axis=-1, keepdims=True)
    centred = values - average
    variance = jnp.mean(centred * centred, axis=-1, keepdims=True)
    scale = lax.rsqrt(variance + norm_eps)
    return centred * scale, scale


def norm_back(unit, scale, gain, grad):
    inner = grad * gain
    shift = jnp.mean(inner, axis=-1, keepdims=True)
    along = jnp.mean(inner * unit, axis=-1, keepdims=True)
    return scale * (inner - shift - unit * along)


def mul(lhs, rhs):
    return jnp.dot(lhs, rhs, preferred_element_type=f32)


def mul_bt(lhs, rhs):
    return lax.dot_general(lhs, rhs, (((1,), (1,)), ((), ())), preferred_element_type=f32)


def mul_at(lhs, rhs):
    return lax.dot_general(lhs, rhs, (((0,), (0,)), ((), ())), preferred_element_type=f32)


def params(limit=VMEM_BYTES):
    return pltpu.CompilerParams(vmem_limit_bytes=limit)


def in_vmem(count):
    return [pl.BlockSpec(memory_space=pltpu.VMEM)] * count


def in_hbm(*arrays):
    return [pltpu.with_memory_space_constraint(array, pltpu.HBM) for array in arrays]


def stays(shape, dtype):
    return pltpu.VMEM(shape, dtype)


def cost(flops, moved, transcendentals=0):
    return pl.CostEstimate(flops=flops, bytes_accessed=moved, transcendentals=transcendentals)


def lane_halves(dtype):
    lane = lax.broadcasted_iota(jnp.int32, (1, 2 * HEAD), 1)
    low = jnp.where(lane < HEAD, 1.0, 0.0)
    return low.astype(dtype), (1.0 - low).astype(dtype)


def two_heads(pair):
    low, high = lane_halves(bf16)
    return jnp.concatenate([pair * low, pair * high], axis=0)


def same_sequence(rows, row0, cols, col0, seq_len):
    row = (lax.broadcasted_iota(jnp.int32, (rows, cols), 0) + row0) // seq_len
    col = (lax.broadcasted_iota(jnp.int32, (rows, cols), 1) + col0) // seq_len
    return row == col


def softmax_down(scores, mask):
    keys = mask.shape[0]
    parts, sums = [], []
    for k in range(2):
        part = jnp.where(mask, scores[k * keys : (k + 1) * keys], -1e30)
        most = jnp.max(part, axis=0, keepdims=True)
        raised = jnp.exp(part - most)
        total = jnp.sum(raised, axis=0, keepdims=True)
        parts.append(raised * (1.0 / total))
        sums.append(most + jnp.log(total))
    return parts, sums


def fold_kernel(extra, keep_a, got_a, keep_b, got_b, *refs):
    outs = refs[-5:] if extra else refs[-4:]
    rows, half, tile = keep_a.shape[0], keep_a.shape[0] // 2, 256

    @pl.loop(0, keep_a.shape[1] // tile)
    def _(step):
        cols = pl.ds(pl.multiple_of(step * tile, tile), tile)
        for k, (kept, got) in enumerate(((keep_a, got_a), (keep_b, got_b))):
            for j in range(2):
                at = slice(j * half, (j + 1) * half)
                total = kept[at, cols].astype(f32) + got[at, cols].astype(f32)
                outs[2 * k + j][:half, cols] = total.astype(bf16)

    if extra:
        came = refs[1][...] if extra > 1 else got_a[rows : rows + 16, :].astype(f32)[:8]
        sums = refs[0][...] + came
        outs[4][...] = sums
        outs[1][half : half + 16, :] = jnp.concatenate([sums, sums], axis=0).astype(bf16)


def fold(parts, after=(), sums=()):
    rows, cols = parts[0].shape
    if rows % 32:
        whole = [
            (kept.astype(f32) + got.astype(f32)).astype(bf16)
            for kept, got in (parts[:2], parts[2:])
        ]
        return [part for one in whole for part in (one[: rows // 2], one[rows // 2 :])]
    half = (rows // 2, cols)
    shapes = [stays(half, bf16)] * 4
    if sums:
        shapes[1] = stays((rows // 2 + 16, cols), bf16)
        shapes.append(stays((8, cols), f32))
    return pl.pallas_call(
        functools.partial(fold_kernel, len(sums)),
        out_shape=shapes,
        in_specs=in_vmem(4 + len(sums)) + anywhere(after),
        out_specs=in_vmem(len(shapes)),
        compiler_params=params(8 << 20),
        cost_estimate=cost(2 * rows * cols, 12 * rows * cols),
        name="fold",
    )(*parts, *sums, *after)


def fold_last_kernel(extra, keep_a, got_a, keep_b, got_b, *refs):
    outs = refs[-4:]
    cols = keep_a.shape[1]
    rows = keep_a.shape[0] // 4
    if extra:
        sums = refs[0][...] + got_a[4 * rows : 4 * rows + 16, :].astype(f32)[:8]
    for k, (kept, got) in enumerate(((keep_a, got_a), (keep_b, got_b))):
        total = kept[...].astype(f32) + got[: 4 * rows, :].astype(f32)
        at = slice(k * cols, (k + 1) * cols)
        for j, out in enumerate(outs):
            part = total[j * rows : (j + 1) * rows]
            if extra:
                row = jnp.broadcast_to(sums[k : k + 1], (8, cols))
                part = jnp.concatenate([part, row], axis=0)
            out[:, at] = part.astype(out.dtype)


def fold_last(parts, after=(), sums=()):
    rows, cols = parts[0].shape
    shape = (rows // 4 + (8 if sums else 0), 2 * cols)
    if rows % 32:
        pairs = (parts[:2], parts[2:])
        both = [kept.astype(f32) + got.astype(f32) for kept, got in pairs]
        own, *others = jnp.split(jnp.concatenate(both, axis=1), 4)
        return [own] + [other.astype(bf16) for other in others]
    return pl.pallas_call(
        functools.partial(fold_last_kernel, len(sums)),
        out_shape=[stays(shape, f32)] + [stays(shape, bf16)] * 3,
        in_specs=in_vmem(4 + len(sums)) + anywhere(after),
        out_specs=in_vmem(4),
        compiler_params=params(8 << 20),
        cost_estimate=cost(2 * rows * cols, 12 * rows * cols),
        name="fold_last",
    )(*parts, *sums, *after)


def anywhere(after):
    return [pl.BlockSpec(memory_space=pl.ANY)] * len(after)


def pair_cols(part, pair):
    start = part * D + pair * 2 * HEAD
    return slice(start, start + 2 * HEAD)


def line(ref):
    return ref[...].astype(f32).reshape(1, -1)


def norm_rows(src, dst, gain, bias, step_rows):
    @pl.loop(0, src.shape[0] // step_rows)
    def _(step):
        at = pl.ds(pl.multiple_of(step * step_rows, step_rows), step_rows)
        unit, _ = norm_parts(src[at, :].astype(f32))
        dst[at, :] = (unit * gain + bias).astype(bf16)


def attend_along(qkv_ref, att_ref, q_rows, k_rows, mask):
    low, high = lane_halves(f32)
    for pair in range(HEADS // 2):
        queries = two_heads(qkv_ref[q_rows, pair_cols(0, pair)] * bf16(HEAD ** (-0.5)))
        scores = mul_bt(queries, qkv_ref[k_rows, pair_cols(1, pair)])
        scores = jnp.where(mask, scores, -1e30)
        raised = jnp.exp(scores - jnp.max(scores, axis=-1, keepdims=True))
        probs = (raised * (1.0 / jnp.sum(raised, axis=-1, keepdims=True))).astype(bf16)
        half = probs.shape[0] // 2
        mixed = mul(probs, qkv_ref[k_rows, pair_cols(2, pair)])
        att_ref[q_rows, pair_cols(0, pair)] = (mixed[:half] * low + mixed[half:] * high).astype(bf16)


def attend(qkv_ref, att_ref, q_rows, k_rows, mask, keep_sums):
    for pair in range(HEADS // 2):
        queries = qkv_ref[q_rows, pair_cols(0, pair)] * bf16(HEAD ** (-0.5))
        scores = mul_bt(two_heads(qkv_ref[k_rows, pair_cols(1, pair)]), queries)
        probs, sums = softmax_down(scores, mask)
        vals = two_heads(qkv_ref[k_rows, pair_cols(2, pair)])
        mixed = mul_at(jnp.concatenate(probs, axis=0).astype(bf16), vals)
        att_ref[q_rows, pair_cols(0, pair)] = mixed.astype(bf16)
        for k in range(2):
            keep_sums(2 * pair + k, sums[k])


def text_front_kernel(
    x_ref, g1_ref, b1_ref, wqkv_ref, wo_ref, g2_ref, b2_ref, h1_ref, qkv_ref, att_ref, mid_ref,
    h2_ref, sum_ref, lse_ref
):
    rows, chunk = x_ref.shape[0], 128
    norm_rows(x_ref, h1_ref, line(g1_ref), line(b1_ref), chunk)

    @pl.loop(0, 3 * D // 256)
    def _(step):
        at = pl.ds(pl.multiple_of(step * 256, 256), 256)
        qkv_ref[:, at] = mul(h1_ref[...], wqkv_ref[:, at]).astype(bf16)

    mask = same_sequence(chunk, 0, chunk, 0, TXT_LEN)

    @pl.loop(0, rows // chunk)
    def _(step):
        at = pl.ds(pl.multiple_of(step * chunk, chunk), chunk)

        def keep_sums(head, value):
            lse_ref[pl.ds(step * 16 + head, 1), :] = value

        attend(qkv_ref, att_ref, at, at, mask, keep_sums)

    @pl.loop(0, D // 256)
    def _(step):
        at = pl.ds(pl.multiple_of(step * 256, 256), 256)
        mid_ref[:, at] = x_ref[:, at].astype(f32) + mul(att_ref[...], wo_ref[:, at])

    norm_rows(mid_ref, h2_ref, line(g2_ref), line(b2_ref), chunk)
    per = chunk // TXT_LEN

    @pl.loop(0, rows // chunk)
    def _(step):
        values = mid_ref[pl.ds(pl.multiple_of(step * chunk, chunk), chunk), :]
        sum_ref[pl.ds(pl.multiple_of(step * per, per), per), :] = jnp.sum(
            values.reshape(per, TXT_LEN, D), axis=1
        )


def text_front(rows_in, gain1, bias1, wqkv, wo, gain2, bias2):
    rows = rows_in.shape[0]
    shapes = [
        ((rows, D), bf16),
        ((rows, 3 * D), bf16),
        ((rows, D), bf16),
        ((rows, D), f32),
        ((rows, D), bf16),
        ((rows // TXT_LEN, D), f32),
        ((rows // 128 * 16, 128), f32),
    ]
    return pl.pallas_call(
        text_front_kernel,
        out_shape=[jax.ShapeDtypeStruct(*item) for item in shapes],
        compiler_params=params(),
        cost_estimate=cost(rows * D * D * 8, 14 * D * rows + 8 * D * D, rows * 128 * HEADS),
        name="text_front",
    )(rows_in, gain1, bias1, wqkv, wo, gain2, bias2)


def image_front_kernel(
    windows, x_ref, order_ref, g1_ref, b1_ref, g2_ref, b2_ref, *refs
):
    h2_ref, sum_ref, early_ref = refs[-10:-7]
    w_ref, h1_ref, placed_ref, qkv_ref, att_ref, mid_ref, sems = refs[-7:]
    rows, chunk = x_ref.shape[0], 80
    copies, row = [], 0
    for k, piece in enumerate(refs[:-10]):
        place = w_ref.at[pl.ds(row, piece.shape[0]), :]
        copies.append(pltpu.make_async_copy(piece, place, sems.at[k]))
        row += piece.shape[0]
    for copy in copies:
        copy.start()

    def place_columns(src, dst):
        @pl.loop(0, D // 256)
        def _(step):
            at = pl.ds(pl.multiple_of(step * 256, 256), 256)
            dst[:, at] = mul_bt(src[...], chosen(order_ref[at, :])).astype(bf16)

    norm_rows(x_ref, h1_ref, line(g1_ref), line(b1_ref), chunk)
    place_columns(h1_ref, placed_ref)
    for copy in copies:
        copy.wait()

    @pl.loop(0, 3 * D // 256)
    def _(step):
        at = pl.ds(pl.multiple_of(step * 256, 256), 256)
        qkv_ref[:, at] = mul(placed_ref[...], w_ref[:, at]).astype(bf16)

    for row0, count, key0, keys in windows:
        one = same_sequence(count, row0, keys, key0, IMG_LEN)
        mask = jnp.concatenate([one, one], axis=0)
        attend_along(qkv_ref, att_ref, pl.ds(row0, count), pl.ds(key0, keys), mask)
    place_columns(att_ref, placed_ref)

    @pl.loop(0, D // 256)
    def _(step):
        at = pl.ds(pl.multiple_of(step * 256, 256), 256)
        there = pl.ds(pl.multiple_of(step * 256 + 3 * D, 256), 256)
        mid_ref[:, at] = x_ref[:, at].astype(f32) + mul(placed_ref[...], w_ref[:, there])

    norm_rows(mid_ref, h2_ref, line(g2_ref), line(b2_ref), chunk)
    place_columns(h2_ref, placed_ref)
    pool = pool_matrix(rows // IMG_LEN, rows, 0, IMG_LEN)

    @pl.loop(0, EARLY // TILE)
    def _(step):
        at = pl.ds(pl.multiple_of(step * TILE, TILE), TILE)
        there = pl.ds(pl.multiple_of(step * TILE + 4 * D, TILE), TILE)
        value, _ = gelu_parts(mul(placed_ref[...], w_ref[:, there]))
        early_ref[:, at] = mul(pool, value.astype(bf16))

    for k in range(rows // IMG_LEN):
        first, last = k * IMG_LEN, (k + 1) * IMG_LEN
        start, end = first // 8 * 8, -(-last // 8) * 8
        values = mid_ref[start:end, :]
        place = lax.broadcasted_iota(jnp.int32, values.shape, 0) + start
        inside = (place >= first) & (place < last)
        sum_ref[k : k + 1, :] = jnp.sum(jnp.where(inside, values, 0.0), axis=0, keepdims=True)


def image_front(rows_in, pieces, source, gain1, bias1, gain2, bias2):
    rows = rows_in.shape[0]
    windows = ((0, 208, 0, 256), (208, 192, 192, 208))
    vmem = pl.BlockSpec(memory_space=pltpu.VMEM)
    return pl.pallas_call(
        functools.partial(image_front_kernel, windows),
        out_shape=[
            jax.ShapeDtypeStruct((rows, D), bf16),
            jax.ShapeDtypeStruct((rows // IMG_LEN, D), f32),
            jax.ShapeDtypeStruct((rows // IMG_LEN, EARLY), f32),
        ],
        in_specs=[vmem] * 6 + anywhere(pieces),
        out_specs=[vmem] * 3,
        scratch_shapes=[
            pltpu.VMEM((D, 4 * D + EARLY), bf16),
            pltpu.VMEM((rows, D), bf16),
            pltpu.VMEM((rows, D), bf16),
            pltpu.VMEM((rows, 3 * D), bf16),
            pltpu.VMEM((rows, D), bf16),
            pltpu.VMEM((rows, D), f32),
            pltpu.SemaphoreType.DMA((len(pieces),)),
        ],
        compiler_params=params(),
        cost_estimate=cost(rows * D * D * 12, 8 * D * D, rows * 256 * HEADS),
        name="image_front",
    )(rows_in, source, gain1, bias1, gain2, bias2, *pieces)


def gelu_parts(inner):
    half = 0.5 * (1.0 + lax.erf(inner * (0.5**0.5)))
    return inner * half, half


def pack_kernel(unit_ref, pos_ref, *refs):
    refs[-1][:, :D] = unit_ref[...].astype(bf16)
    refs[-1][:, D:] = pos_ref[...]


def packed(unit, positive, after):
    shape = (unit.shape[0], D + positive.shape[1])
    return pl.pallas_call(
        pack_kernel,
        out_shape=jax.ShapeDtypeStruct(shape, bf16),
        in_specs=[pl.BlockSpec(memory_space=pltpu.VMEM)] * 2 + anywhere(after),
        compiler_params=params(),
        cost_estimate=cost(shape[0] * shape[1], 4 * shape[0] * shape[1]),
        name="packed",
    )(unit, positive, *after)


def pool_matrix(count, rows, row0, seq_len):
    row = (lax.broadcasted_iota(jnp.int32, (count, rows), 1) + row0) // seq_len
    return jnp.where(row == lax.broadcasted_iota(jnp.int32, (count, rows), 0), 1.0, 0.0).astype(bf16)


def two_terms(mean):
    high = mean.astype(bf16)
    low = (mean - high.astype(f32)).astype(bf16)
    return jnp.concatenate([high, low], axis=0)


def unit_rows(pooled):
    inverse = lax.rsqrt(jnp.sum(pooled * pooled, axis=-1, keepdims=True) + norm_eps)
    return pooled * inverse, inverse


def text_up_kernel(h2_ref, wu_ref, wd_ref, sum_ref, *refs):
    slope_ref, hid_ref, unit_ref, inv_ref, acc = refs[-5:]
    step = pl.program_id(0)
    chunk = 320
    per = chunk // TXT_LEN
    pool = pool_matrix(per, chunk, 0, TXT_LEN)
    for k in range(h2_ref.shape[0] // chunk):
        inner = mul(h2_ref[k * chunk : (k + 1) * chunk, :], wu_ref[...])
        value, half = gelu_parts(inner)
        slope = half + inner * (jnp.exp(-0.5 * inner * inner) * 0.3989422804014327)
        slope_ref[k * chunk : (k + 1) * chunk, :] = slope.astype(bf16)
        hid_ref[k * per : (k + 1) * per, :] = mul(pool, value.astype(bf16))
    terms = mul(two_terms(hid_ref[...] * (1.0 / TXT_LEN)), wd_ref[...])
    count = hid_ref.shape[0]
    added = terms[:count] + terms[count:]

    @pl.when(step == 0)
    def _():
        acc[...] = sum_ref[...] * (1.0 / TXT_LEN) + added

    @pl.when(step > 0)
    def _():
        acc[...] += added

    @pl.when(step == pl.num_programs(0) - 1)
    def _():
        unit, inverse = unit_rows(acc[...])
        unit_ref[...] = unit
        inv_ref[...] = jnp.broadcast_to(inverse, inv_ref.shape)


def text_up(normed2, weight_up, weight_down, middle_sum, after=()):
    rows, count = normed2.shape[0], middle_sum.shape[0]
    fixed = lambda shape: pl.BlockSpec(shape, lambda i: (0, 0))
    return pl.pallas_call(
        text_up_kernel,
        grid=(FF // TILE,),
        out_shape=[
            jax.ShapeDtypeStruct((rows, FF), bf16),
            jax.ShapeDtypeStruct((count, FF), f32),
            jax.ShapeDtypeStruct((count, D), f32),
            jax.ShapeDtypeStruct((count, 128), f32),
        ],
        in_specs=[
            fixed((rows, D)),
            pl.BlockSpec((D, TILE), lambda i: (0, i)),
            pl.BlockSpec((TILE, D), lambda i: (i, 0)),
            fixed((count, D)),
        ]
        + anywhere(after),
        out_specs=[
            pl.BlockSpec((rows, TILE), lambda i: (0, i)),
            pl.BlockSpec((count, TILE), lambda i: (0, i)),
            fixed((count, D)),
            fixed((count, 128)),
        ],
        scratch_shapes=[pltpu.VMEM((count, D), f32)],
        compiler_params=params(),
        cost_estimate=cost(2 * rows * D * FF, 4 * D * FF + 2 * rows * FF, 20 * rows * FF),
        name="text_up",
    )(normed2, weight_up, weight_down, middle_sum, *after)


def image_up_kernel(fold, h2_ref, wu_ref, wd_ref, first_ref, sum_ref, early_ref, out_ref, acc, picked):
    step = pl.program_id(0)
    rows, count = h2_ref.shape[0], sum_ref.shape[0]
    part = TILE // fold

    def through_down(summed, groups):
        moved = mul(two_terms(summed * (1.0 / IMG_LEN)), picked[...]).astype(bf16)
        weight = jnp.concatenate([groups[:, k * D : (k + 1) * D] for k in range(fold)], axis=0)
        terms = mul(moved, weight)
        return terms[:count] + terms[count:]

    @pl.when(step == 0)
    def _():
        place = lax.broadcasted_iota(jnp.int32, (TILE, TILE), 0)
        col = lax.broadcasted_iota(jnp.int32, (TILE, TILE), 1)
        source = (col % part) * fold + col // part
        picked[...] = jnp.where(place == source, 1.0, 0.0).astype(bf16)
        total = sum_ref[...] * (1.0 / IMG_LEN)
        for k in range(EARLY // TILE):
            total = total + through_down(
                early_ref[:, k * TILE : (k + 1) * TILE], first_ref[k * part : (k + 1) * part, :]
            )
        acc[...] = total

    value, _ = gelu_parts(mul(h2_ref[...], wu_ref[...]))
    summed = mul(pool_matrix(count, rows, 0, IMG_LEN), value.astype(bf16))
    acc[...] += through_down(summed, wd_ref[...])

    @pl.when(step == pl.num_programs(0) - 1)
    def _():
        out_ref[...] = unit_rows(acc[...])[0].astype(bf16)


def image_up(normed2, whole, middle_sum, early):
    rows, count = normed2.shape[0], middle_sum.shape[0]
    fold = FF // D
    before, part = EARLY // TILE, TILE // fold
    fixed = lambda shape: pl.BlockSpec(shape, lambda i: (0, 0))
    return pl.pallas_call(
        functools.partial(image_up_kernel, fold),
        grid=(FF // TILE - before,),
        out_shape=jax.ShapeDtypeStruct((count, D), bf16),
        in_specs=[
            fixed((rows, D)),
            pl.BlockSpec((D, TILE), lambda i: (0, FF // TILE + i)),
            pl.BlockSpec((part, FF), lambda i: (i + before, 0)),
            fixed((before * part, FF)),
            fixed((count, D)),
            fixed((count, EARLY)),
        ],
        out_specs=fixed((count, D)),
        scratch_shapes=[pltpu.VMEM((count, D), f32), pltpu.VMEM((TILE, TILE), bf16)],
        compiler_params=params(),
        cost_estimate=cost(2 * rows * D * FF, 4 * D * FF, 15 * rows * FF),
        name="image_up",
    )(normed2, whole, whole, whole, middle_sum, early)


def left_kernel(count, *refs):
    out_ref = refs[-1]
    for k in range(count):
        source_ref, values_ref = refs[2 * k : 2 * k + 2]

        @pl.loop(0, D // 256)
        def _(step, k=k, source_ref=source_ref, values_ref=values_ref):
            at = pl.ds(pl.multiple_of(step * 256, 256), 256)
            picked = mul_bt(chosen(source_ref[at, :]), values_ref[...])
            out_ref[k, at, :] = picked.astype(bf16)


def left_factors(*pairs):
    rows = pairs[0][1].shape[0]
    given = [item for pair in pairs for item in pair]
    return pl.pallas_call(
        functools.partial(left_kernel, len(pairs)),
        out_shape=jax.ShapeDtypeStruct((len(pairs), D, rows), bf16),
        in_specs=in_vmem(len(given)),
        out_specs=pl.BlockSpec(memory_space=pltpu.VMEM),
        compiler_params=params(24 << 20),
        cost_estimate=cost(2 * len(pairs) * rows * D * D, 4 * len(pairs) * rows * D),
        name="left_factors",
    )(*given)


def loss_parts(text_rows, pos, image_all):
    similar = mul_bt(text_rows, image_all) * logit_scale
    shifted = jnp.exp(similar - logit_scale)
    alive = jnp.max(pos, axis=1, keepdims=True)
    row_sum = jnp.sum(shifted, axis=1, keepdims=True)
    row_count = jnp.maximum(jnp.sum(pos, axis=1, keepdims=True), 1.0)
    return similar, shifted, alive, row_sum, row_count


def sums_over_captions(text_rows, pos, image_all):
    similar, shifted, alive, row_sum, row_count = loss_parts(text_rows, pos, image_all)
    pos_similar = pos * similar
    cap_term = alive * (
        logit_scale + jnp.log(row_sum) - jnp.sum(pos_similar, axis=1, keepdims=True) / row_count
    )
    return (
        jnp.sum(alive * shifted, axis=0, keepdims=True),
        jnp.sum(pos, axis=0, keepdims=True),
        jnp.sum(pos_similar, axis=0, keepdims=True),
        jnp.sum(cap_term, axis=0, keepdims=True),
        jnp.sum(alive, axis=0, keepdims=True),
    )


def loss_from(sums):
    col_sum, col_count, col_pos, cap_total, live_total = sums
    img_term = logit_scale + jnp.log(col_sum) - col_pos / col_count
    return 0.5 * cap_total / live_total + 0.5 * jnp.mean(img_term, axis=1, keepdims=True)


def grad_of_unit(text_rows, pos, image_all, col_sum, col_count, live_total):
    _, shifted, alive, row_sum, row_count = loss_parts(text_rows, pos, image_all)
    cap_share, img_share = 0.5 / live_total, 0.5 / image_all.shape[0]
    grad_sims = alive * shifted * (cap_share / row_sum + img_share / col_sum) - pos * (
        cap_share / row_count + img_share / col_count
    )
    return mul(grad_sims.astype(bf16), image_all) * logit_scale


def turned(grad, unit):
    return grad - unit * jnp.sum(grad * unit, axis=-1, keepdims=True)


def loss_kernel(
    pack_ref, image_ref, own_ref, unit_ref, inv_ref, loss_ref, row_ref, low_ref, col_sum_ref,
    col_count_ref, live_ref
):
    image_all = image_ref[...]
    chunk = 256
    total = None
    for k in range(pack_ref.shape[0] // chunk):
        at = slice(k * chunk, (k + 1) * chunk)
        part = sums_over_captions(pack_ref[at, :D], pack_ref[at, D:].astype(f32), image_all)
        total = part if total is None else [a + b for a, b in zip(total, part)]
    loss_ref[...] = jnp.broadcast_to(loss_from(total), loss_ref.shape)
    col_sum, col_count, _, _, live_total = total
    col_sum_ref[...] = col_sum
    col_count_ref[...] = col_count
    live_ref[...] = jnp.broadcast_to(live_total, live_ref.shape)
    grad = grad_of_unit(
        own_ref[:, :D], own_ref[:, D:].astype(f32), image_all, col_sum, col_count, live_total
    )
    row = inv_ref[:, :1] * turned(grad, unit_ref[...]) * (1.0 / TXT_LEN)
    row_ref[...] = row
    low_ref[...] = row.astype(bf16)


def loss_and_rows(pack, image_all, own_pack, unit, inverse):
    images, count = image_all.shape[0], own_pack.shape[0]
    shapes = [(1, 128), (count, D), (count, D), (1, images), (1, images), (1, 128)]
    kinds = [f32, f32, bf16, f32, f32, f32]
    return pl.pallas_call(
        loss_kernel,
        out_shape=[jax.ShapeDtypeStruct(*item) for item in zip(shapes, kinds)],
        in_specs=in_vmem(5),
        out_specs=in_vmem(len(shapes)),
        compiler_params=params(16 << 20),
        cost_estimate=cost(2 * pack.shape[0] * images * D, 2 * pack.size, pack.shape[0] * images),
        name="loss_and_rows",
    )(pack, image_all, own_pack, unit, inverse)


def down_kernel(pack_ref, image_ref, col_sum_ref, col_count_ref, live_ref, hid_ref, *refs):
    step, out_ref = pl.program_id(0), refs[-1]
    text_rows = pack_ref[:, :D]
    grad = grad_of_unit(
        text_rows, pack_ref[:, D:].astype(f32), image_ref[...], col_sum_ref[...],
        col_count_ref[...], live_ref[:, :1]
    )
    rows = (turned(grad, text_rows.astype(f32)) * (1.0 / TXT_LEN)).astype(bf16)
    part = mul_at(hid_ref[...], rows)

    @pl.when(step == 0)
    def _():
        out_ref[...] = part

    @pl.when(step > 0)
    def _():
        out_ref[...] += part


def grad_of_down(pack, image_all, col_sum, col_count, live_total, hidden_cols, after):
    images, chunk = image_all.shape[0], 256
    fixed = lambda shape: pl.BlockSpec(shape, lambda i: (0, 0))
    per = hidden_cols.shape[1]
    return pl.pallas_call(
        down_kernel,
        grid=(pack.shape[0] // chunk,),
        out_shape=jax.ShapeDtypeStruct((per, D), f32),
        in_specs=[
            pl.BlockSpec((chunk, pack.shape[1]), lambda i: (i, 0)),
            fixed((images, D)), fixed((1, images)), fixed((1, images)), fixed((1, 128)),
            pl.BlockSpec((chunk, per), lambda i: (i, 0)),
        ]
        + anywhere(after),
        out_specs=fixed((per, D)),
        compiler_params=params(16 << 20),
        cost_estimate=cost(4 * pack.shape[0] * images * D, 2 * pack.size, pack.shape[0] * images),
        name="grad_of_down",
    )(pack, image_all, col_sum, col_count, live_total, hidden_cols, *after)


def mlp_back_kernel(
    low_ref, gain_ref, row_ref, wd_hbm, slope_hbm, wu_hbm, lhs_hbm, mid_hbm, keep_a, send_a, keep_b,
    send_b, out_ref, sums_out, wd_ref, slope_ref, wu_ref, lhs_ref, mid_ref, sems, whole_sems
):
    count, rows = low_ref.shape[0], out_ref.shape[0]
    half, steps = D // 2, FF // 2 // TILE

    def copies(tile, slot):
        at = pl.ds(pl.multiple_of(tile * TILE, TILE), TILE)
        return (
            pltpu.make_async_copy(wd_hbm.at[at, :], wd_ref.at[slot], sems.at[0, slot]),
            pltpu.make_async_copy(slope_hbm.at[:, at], slope_ref.at[slot], sems.at[1, slot]),
            pltpu.make_async_copy(wu_hbm.at[:, at], wu_ref.at[slot], sems.at[2, slot]),
        )

    lhs_copy = pltpu.make_async_copy(lhs_hbm, lhs_ref, whole_sems.at[0])
    mid_copy = pltpu.make_async_copy(mid_hbm, mid_ref, whole_sems.at[1])
    for copy in copies(0, 0):
        copy.start()
    lhs_copy.start()
    for k, (keep, send) in enumerate(((keep_a, send_a), (keep_b, send_b))):

        @pl.loop(0, steps)
        def _(step, k=k, keep=keep, send=send):
            tile = k * steps + step
            slot = lax.rem(tile, 2)

            @pl.when(tile + 1 < 2 * steps)
            def _():
                for copy in copies(tile + 1, 1 - slot):
                    copy.start()

            for copy in copies(tile, slot):
                copy.wait()
            if k == 0:

                @pl.when(step == 0)
                def _():
                    lhs_copy.wait()
                    mid_copy.start()

            there = pl.ds(pl.multiple_of(step * TILE, TILE), TILE)
            hidden = mul_bt(low_ref[...], wd_ref[slot])
            wide = jnp.broadcast_to(hidden[:, None, :], (count, TXT_LEN, TILE))
            inner = (wide.reshape(rows, TILE) * slope_ref[slot].astype(f32)).astype(bf16)
            weight = mul(lhs_ref[k], inner).astype(bf16)
            keep[:, there] = weight[:half]
            send[:, there] = weight[half:]
            added = mul_bt(inner, wu_ref[slot])
            if k == 0:

                @pl.when(step == 0)
                def _():
                    out_ref[...] = added

                @pl.when(step > 0)
                def _():
                    out_ref[...] += added
            else:
                out_ref[...] += added

    chunk = 128
    per = chunk // TXT_LEN
    gain = line(gain_ref)
    sums_out[...] = jnp.zeros_like(sums_out)
    mid_copy.wait()

    @pl.loop(0, rows // chunk)
    def _(k):
        at = pl.ds(pl.multiple_of(k * chunk, chunk), chunk)
        unit, scale = norm_parts(mid_ref[at, :])
        grad = out_ref[at, :]
        sums_out[:, :D] += jnp.sum(grad * unit, axis=0, keepdims=True)
        sums_out[:, D:] += jnp.sum(grad, axis=0, keepdims=True)
        row = row_ref[pl.ds(pl.multiple_of(k * per, per), per), :]
        row = jnp.broadcast_to(row[:, None, :], (per, TXT_LEN, D)).reshape(chunk, D)
        out_ref[at, :] = row + norm_back(unit, scale, gain, grad)


def mlp_back(grad_row, grad_low, weight_down, slope, weight_up, lhs, middle, gain):
    rows = slope.shape[0]
    return pl.pallas_call(
        mlp_back_kernel,
        out_shape=[stays((D // 2, FF // 2), bf16)] * 4
        + [stays((rows, D), f32), stays((1, 2 * D), f32)],
        in_specs=in_vmem(3) + [pl.BlockSpec(memory_space=pltpu.HBM)] * 5,
        out_specs=in_vmem(6),
        scratch_shapes=[
            pltpu.VMEM((2, TILE, D), bf16),
            pltpu.VMEM((2, rows, TILE), bf16),
            pltpu.VMEM((2, D, TILE), bf16),
            pltpu.VMEM((2, D, rows), bf16),
            pltpu.VMEM((rows, D), f32),
            pltpu.SemaphoreType.DMA((3, 2)),
            pltpu.SemaphoreType.DMA((2,)),
        ],
        compiler_params=params(28 << 20),
        cost_estimate=cost(4 * rows * D * FF, 4 * D * FF + 2 * rows * FF + 2 * D * FF, rows * FF),
        name="mlp_back",
    )(grad_low, gain, grad_row, *in_hbm(weight_down, slope, weight_up, lhs, middle))


def attention_back_kernel(first, grad_ref, wo_ref, qkv_ref, lse_ref, *refs):
    low_ref, out_ref = refs[-2:]
    chunk = 128
    mask = same_sequence(chunk, 0, chunk, 0, TXT_LEN)

    @pl.loop(0, low_ref.shape[0] // chunk)
    def _(step):
        here = pl.ds(pl.multiple_of((first + step) * chunk, chunk), chunk)
        there = pl.ds(pl.multiple_of(step * chunk, chunk), chunk)
        sums = lse_ref[pl.ds(pl.multiple_of((first + step) * 16, 16), 16), :]
        low = grad_ref[here, :].astype(bf16)
        low_ref[there, :] = low
        grad_att = mul_bt(low, wo_ref[...]).astype(bf16)
        for pair in range(HEADS // 2):
            queries = qkv_ref[here, pair_cols(0, pair)] * bf16(HEAD ** (-0.5))
            keys = two_heads(qkv_ref[here, pair_cols(1, pair)])
            vals = two_heads(qkv_ref[here, pair_cols(2, pair)])
            grads = grad_att[:, pair_cols(0, pair)]
            scores, grad_probs = mul_bt(keys, queries), mul_bt(vals, grads)
            probs, grad_scores = [], []
            for k in range(2):
                at = slice(k * chunk, (k + 1) * chunk)
                head = 2 * pair + k
                shifted = scores[at] - sums[head : head + 1, :]
                prob = jnp.where(mask, jnp.exp(jnp.where(mask, shifted, 0.0)), 0.0)
                along = jnp.sum(grad_probs[at] * prob, axis=0, keepdims=True)
                grad_scores.append((prob * (grad_probs[at] - along)).astype(bf16))
                probs.append(prob.astype(bf16))
            grad_q = mul_at(jnp.concatenate(grad_scores, axis=0), keys) * HEAD ** (-0.5)
            grad_k = mul(jnp.concatenate(grad_scores, axis=1), two_heads(queries))
            grad_v = mul(jnp.concatenate(probs, axis=1), two_heads(grads))
            out_ref[there, pair_cols(0, pair)] = grad_q.astype(bf16)
            out_ref[there, pair_cols(1, pair)] = grad_k.astype(bf16)
            out_ref[there, pair_cols(2, pair)] = grad_v.astype(bf16)


def attention_back(grad_middle, weight_out, project, log_sums, first, count, after=()):
    rows = count * 128
    return pl.pallas_call(
        functools.partial(attention_back_kernel, first),
        out_shape=[stays((rows, D), bf16), stays((rows, 3 * D), bf16)],
        in_specs=in_vmem(4) + anywhere(after),
        out_specs=in_vmem(2),
        compiler_params=params(16 << 20),
        cost_estimate=cost(10 * rows * D * D, 16 * rows * D + 2 * D * D, rows * 128 * HEADS),
        name="attention_back",
    )(grad_middle, weight_out, project, log_sums, *after)


def mul_rows(lhs, parts, cols):
    total, row = 0.0, 0
    for part in parts:
        total = total + mul(lhs[:, row : row + part.shape[0]], part[:, cols])
        row += part.shape[0]
    return total


def weight_back_kernel(factors, groups, lhs_ref, *refs):
    keep_a, send_a, keep_b, send_b = refs[-4:]
    half = D // 2
    for k, (factor, group, col) in enumerate(factors):
        parts = refs[sum(groups[:group]) : sum(groups[: group + 1])]
        weight = mul_rows(lhs_ref.at[factor], parts, slice(col * D, (col + 1) * D)).astype(bf16)
        at = slice(k % 2 * D, (k % 2 + 1) * D)
        (keep_b if k > 1 else keep_a)[:, at] = weight[:half]
        (send_b if k > 1 else send_a)[:, at] = weight[half:]


def weight_back(lhs, groups, factors, after=()):
    rows = lhs.shape[2]
    given = [part for group in groups for part in group]
    return pl.pallas_call(
        functools.partial(weight_back_kernel, factors, [len(group) for group in groups]),
        out_shape=[stays((D // 2, 2 * D), bf16)] * 4,
        in_specs=in_vmem(1 + len(given)) + anywhere(after),
        out_specs=in_vmem(4),
        compiler_params=params(16 << 20),
        cost_estimate=cost(8 * rows * D * D, 8 * rows * D + 14 * D * D),
        name="weight_back",
    )(lhs, *given, *after)


def input_back_kernel(count, *refs):
    projs = refs[:count]
    w_ref, x_ref, gain_ref, mid_ref, sums_ref = refs[count : count + 5]
    out_ref, sums_out = refs[-2:]
    rows, chunk = x_ref.shape[0], 128

    @pl.loop(0, D // 256)
    def _(step):
        at = pl.ds(pl.multiple_of(step * 256, 256), 256)
        row = 0
        for part in projs:
            there = slice(row, row + part.shape[0])
            out_ref[there, at] = mul_bt(part[...], w_ref[at, :])
            row += part.shape[0]

    gain = line(gain_ref)
    sums_out[...] = jnp.zeros_like(sums_out)
    sums_out[1:2, :] = sums_ref[...]

    @pl.loop(0, rows // chunk)
    def _(k):
        at = pl.ds(pl.multiple_of(k * chunk, chunk), chunk)
        unit, scale = norm_parts(x_ref[at, :].astype(f32))
        grad = out_ref[at, :]
        sums_out[0:1, :D] += jnp.sum(grad * unit, axis=0, keepdims=True)
        sums_out[0:1, D:] += jnp.sum(grad, axis=0, keepdims=True)
        out_ref[at, :] = mid_ref[at, :] + norm_back(unit, scale, gain, grad)


def input_back(grad_projs, weight, rows_in, gain, grad_middle, sums, after=()):
    rows = rows_in.shape[0]
    return pl.pallas_call(
        functools.partial(input_back_kernel, len(grad_projs)),
        out_shape=[jax.ShapeDtypeStruct((rows, D), f32), stays((8, 2 * D), f32)],
        in_specs=in_vmem(len(grad_projs) + 5) + anywhere(after),
        out_specs=in_vmem(2),
        compiler_params=params(16 << 20),
        cost_estimate=cost(6 * rows * D * D, 14 * rows * D + 6 * D * D),
        name="input_back",
    )(*grad_projs, weight, rows_in, gain, grad_middle, sums, *after)


def local(
    images,
    captions,
    img_gain1,
    img_bias1,
    img_qkv,
    img_out,
    img_gain2,
    img_bias2,
    img_up,
    img_down,
    txt_gain1,
    txt_bias1,
    txt_qkv,
    txt_out,
    txt_gain2,
    txt_bias2,
    txt_up,
    txt_down,
    counts,
    matches,
):
    peers = lax.axis_size(AXIS)
    own = lax.axis_index(AXIS)
    per = D // peers
    img_local = counts.shape[0]
    cap_local = matches.shape[0]
    total_images = matches.shape[1]

    up_rows = img_up.reshape(per, FF)
    whole = lax.all_gather(
        jnp.concatenate([img_down.reshape(per, FF), up_rows[:, EARLY:]], axis=1),
        AXIS,
        axis=0,
        tiled=True,
    )
    small = peers == 32
    shard = jnp.concatenate(
        [img_qkv.reshape(per, 3 * D), img_out.reshape(per, D), up_rows[:, :EARLY]], axis=1
    )
    if small:
        line, source = gathered_line(shard), row_order((1, 4, 2, 16, 8))
    else:
        line, source = lax.all_gather(shard, AXIS, axis=0, tiled=True), row_order(())

    normed1, project, attended, middle, normed2, middle_sum, log_sums = text_front(
        captions, txt_gain1, txt_bias1, txt_qkv, txt_out, txt_gain2, txt_bias2
    )
    middle_sum, line = in_turn(middle_sum, line)
    beside, above = (swapped(line, 2), swapped(line, 4)) if small else (line, line)
    slope, hidden_sum, text_unit, inverse = text_up(
        normed2, txt_up, txt_down, middle_sum, (line,)
    )
    text_unit, normed2, beside, above = lax.optimization_barrier(
        (text_unit, normed2, beside, above)
    )

    ends_at = jnp.cumsum(counts)
    slot_ids = lax.iota(jnp.int32, cap_local)
    owner = jnp.sum((ends_at[None, :] <= slot_ids[:, None]).astype(jnp.int32), axis=1)
    owner = owner + own * img_local
    live = slot_ids < ends_at[-1]
    columns = lax.iota(jnp.int32, total_images)
    positive = ((matches > 0) | (owner[:, None] == columns[None, :])) & live[:, None]

    order_a, order_b, tail = stage_orders()
    source_a, source_b = row_order(order_a + tail[::-1]), row_order(order_b + tail[::-1])
    own_pack = packed(text_unit, positive.astype(bf16), ())
    lhs_up = left_factors((source_a, normed2), (source_b, normed2))
    pieces = [line]
    if small:
        first, second = diagonal(beside, above)
        own_pack, first, second, lhs_up = lax.optimization_barrier(
            (own_pack, first, second, lhs_up)
        )
        held = own_pack[None]
        others = [swapped(held, mask) for mask in (8, 16, 24)]
        pieces = [line, beside, above, first, second]
        pieces = pieces + [swapped(piece, 1) for piece in pieces]

    normed_img, middle_img, early = image_front(
        images, pieces, source, img_gain1, img_bias1, img_gain2, img_bias2
    )
    if small:
        scaled_sum = (hidden_sum * inverse[:, :1]).astype(bf16)
        normed_img, scaled_sum, others = lax.optimization_barrier((normed_img, scaled_sum, others))
        held = joined(joined(held, others[0], 8), joined(others[1], others[2], 8), 16, 1)
        text_beside, text_above = swapped(held, 2), swapped(held, 4)
        hidden_cols = lax.all_to_all(scaled_sum, AXIS, split_axis=1, concat_axis=0, tiled=True)
        whole, text_beside, text_above = lax.optimization_barrier((whole, text_beside, text_above))
        halves = diagonal(text_beside, text_above)
    image_low = image_up(normed_img, whole, middle_img, early)
    if small:
        image_low, halves, hidden_cols = lax.optimization_barrier((image_low, halves, hidden_cols))
        across = jnp.concatenate(halves, axis=0)
        held = joined(joined(held, text_beside, 2), joined(text_above, across, 2), 4, 4)
        text_pack = joined(held, swapped(held, 1), 1).reshape(-1, D + total_images)
    image_all = spread(image_low).reshape(total_images, D)
    if small:
        image_all, text_pack = in_turn(image_all, text_pack)

    if small:
        loss_value, grad_row, row_low, col_sum, col_count, live_total = loss_and_rows(
            text_pack, image_all, own_pack, text_unit, inverse
        )
        loss_value = loss_value[0, 0]
    else:
        text_low, pos = own_pack[:, :D], own_pack[:, D:].astype(f32)
        sums = lax.psum(sums_over_captions(text_low, pos, image_all), AXIS)
        loss_value = loss_from(sums)[0, 0]
        grad = grad_of_unit(text_low, pos, image_all, sums[0], sums[1], sums[4])
        grad_row = inverse[:, :1] * turned(grad, text_unit) * (1.0 / TXT_LEN)
        row_low = grad_row.astype(bf16)

    *up, grad_middle, sums = mlp_back(
        grad_row, row_low, txt_down, slope, txt_up, lhs_up, middle, txt_gain2
    )
    stages = len(order_a)
    low_one, proj_one = attention_back(grad_middle, txt_out, project, log_sums, 0, 1)
    for stage in range(stages - 2):
        up = fold(hand_on(up, stage), (proj_one,))
    low_two, proj_two = attention_back(grad_middle, txt_out, project, log_sums, 1, 4, up)
    proj_two, normed1 = in_turn(proj_two, normed1)
    lhs_rest = left_factors((source_a, normed1), (source_b, normed1), (source_b, attended))
    up = fold(hand_on(up, stages - 2), (proj_two, lhs_rest))
    projs, lows = (proj_one, proj_two), (low_one, low_two)
    rest = weight_back(lhs_rest, [projs, lows], [(0, 0, 0), (0, 0, 1), (1, 0, 2), (2, 1, 0)], up)
    up = hand_on(up, stages - 1)
    caption_grad, sums = input_back(
        projs, txt_qkv, captions, txt_gain1, grad_middle, sums, rest[:1]
    )
    caption_grad, up = in_turn(caption_grad, up)
    up = fold_last(up)
    if small:
        *rest, sums = fold(hand_on(rest, 0), up[:1], (sums, swapped(sums, 1)))
    else:
        norms = lax.psum(sums, AXIS)[:2].reshape(-1)
        for stage in range(stages - 2):
            rest = fold(hand_on(rest, stage), up[:1])
    up = hand_on_last(up)
    rest = hand_on(rest, stages - 2)
    if small:
        grad_down = grad_of_down(
            text_pack, image_all, col_sum, col_count, live_total, hidden_cols, (caption_grad,)
        )
    else:
        grad_down = lax.psum_scatter(
            mul_at(hidden_sum.astype(bf16), row_low), AXIS, scatter_dimension=0, tiled=True
        )
    grad_down, rest, up = lax.optimization_barrier((grad_down, rest, up))
    if small:
        *rest, sums = fold(rest, (), (sums,))
        rest = fold_last(hand_on(rest, stages - 1), (), (sums,))
    else:
        rest = fold_last(hand_on(fold(rest), stages - 1))
    up_share = sum_last(*up)
    rest_share = sum_last(*hand_on_last(rest))
    if small:
        norms = rest_share[per]
        rest_share = rest_share[:per]
    return (
        loss_value,
        caption_grad,
        norms[:D],
        norms[D : 2 * D],
        rest_share[:, : 3 * D].reshape(-1),
        rest_share[:, 3 * D :].reshape(-1),
        norms[2 * D : 3 * D],
        norms[3 * D :],
        up_share.reshape(-1),
        grad_down.reshape(-1),
    )


def solution(mesh):
    split, flat, whole = P("blk", None), P("blk"), P()
    image_block = (whole, whole, flat, flat, whole, whole, flat, flat)
    return jax.shard_map(
        local,
        mesh=mesh,
        in_specs=(split, split) + image_block + (whole,) * 8 + (flat, split),
        out_specs=(whole, split, whole, whole, flat, flat, whole, whole, flat, flat),
        check_vma=False,
    )
```

```python
import functools

import jax
import jax.numpy as jnp
from jax import lax
from jax.experimental import pallas as pl
from jax.experimental.pallas import tpu as pltpu
from jax.sharding import PartitionSpec as P

D = 768
FF = 3072
HEAD = 64
HEADS = D // HEAD
IMG_LEN = 50
TXT_LEN = 16
AXIS = "blk"

norm_eps = 1e-06
logit_scale = 50.0
f32 = jnp.float32
bf16 = jnp.bfloat16


def swapped(value, mask):
    peers = lax.axis_size(AXIS)
    return lax.ppermute(value, AXIS, [(i, i ^ mask) for i in range(peers)])


def bit_masks():
    peers = lax.axis_size(AXIS)
    return [1 << k for k in range(peers.bit_length() - 1)]


def joined(held, other, mask, outer=None):
    upper = (lax.axis_index(AXIS) & mask) > 0
    first = jnp.where(upper, other, held)
    second = jnp.where(upper, held, other)
    outer = held.shape[0] if outer is None else outer
    parts = [part.reshape((outer, -1) + held.shape[1:]) for part in (first, second)]
    return jnp.stack(parts, axis=1).reshape((-1,) + held.shape[1:])


def spread(block):
    peers = lax.axis_size(AXIS)
    copies = jnp.broadcast_to(block[None], (peers,) + block.shape)
    return lax.all_to_all(copies, AXIS, split_axis=0, concat_axis=0, tiled=True)


def stage_orders():
    masks = bit_masks()
    head, tail = masks[:-2], masks[-2:]
    order_a = list(head)
    order_b = list(head)
    for k in range(1, len(head) - 1, 2):
        order_b[k], order_b[k + 1] = order_b[k + 1], order_b[k]
    return order_a, order_b, tail


def row_order(bits):
    peers = lax.axis_size(AXIS)
    own = lax.axis_index(AXIS)
    per = D // peers
    places = lax.broadcasted_iota(jnp.int32, (D, 1), 0)
    block = places // per
    target = jnp.zeros_like(block) + own
    for k, mask in enumerate(bits):
        target = target ^ (((block >> (len(bits) - 1 - k)) & 1) * mask)
    return target * per + places % per


def chosen(source):
    column = lax.broadcasted_iota(jnp.int32, (source.shape[0], D), 1)
    return jnp.where(column == source, 1.0, 0.0).astype(bf16)


def gathered_line(shard):
    return jnp.concatenate([shard] + [swapped(shard, mask) for mask in (8, 16, 24)], axis=0)


def diagonal(beside, above):
    half = beside.shape[0] // 2
    return swapped(beside[:half], 4), swapped(above[half:], 2)


def in_turn(first, then):
    return lax.optimization_barrier((first, then))


def hand_on(parts, stage):
    order_a, order_b, _ = stage_orders()
    keep_a, send_a, keep_b, send_b = parts
    return keep_a, swapped(send_a, order_a[stage]), keep_b, swapped(send_b, order_b[stage])


def hand_on_last(blocks):
    low, high = stage_orders()[2]
    own, *others = blocks
    return own, [swapped(block, mask) for block, mask in zip(others, (low, high, low | high))]


def sum_last(own, others):
    total = own
    for other in others:
        total = total + other.astype(f32)
    return total


VMEM_BYTES = 56 << 20
TILE = 512
EARLY = 2 * TILE


def norm_parts(values):
    average = jnp.mean(values, axis=-1, keepdims=True)
    centred = values - average
    variance = jnp.mean(centred * centred, axis=-1, keepdims=True)
    scale = lax.rsqrt(variance + norm_eps)
    return centred * scale, scale


def norm_back(unit, scale, gain, grad):
    inner = grad * gain
    shift = jnp.mean(inner, axis=-1, keepdims=True)
    along = jnp.mean(inner * unit, axis=-1, keepdims=True)
    return scale * (inner - shift - unit * along)


def mul(lhs, rhs):
    return jnp.dot(lhs, rhs, preferred_element_type=f32)


def mul_bt(lhs, rhs):
    return lax.dot_general(lhs, rhs, (((1,), (1,)), ((), ())), preferred_element_type=f32)


def mul_at(lhs, rhs):
    return lax.dot_general(lhs, rhs, (((0,), (0,)), ((), ())), preferred_element_type=f32)


def params(limit=VMEM_BYTES):
    return pltpu.CompilerParams(vmem_limit_bytes=limit)


def in_vmem(count):
    return [pl.BlockSpec(memory_space=pltpu.VMEM)] * count


def in_hbm(*arrays):
    return [pltpu.with_memory_space_constraint(array, pltpu.HBM) for array in arrays]


def stays(shape, dtype):
    return pltpu.VMEM(shape, dtype)


def cost(flops, moved, transcendentals=0):
    return pl.CostEstimate(flops=flops, bytes_accessed=moved, transcendentals=transcendentals)


def lane_halves(dtype):
    lane = lax.broadcasted_iota(jnp.int32, (1, 2 * HEAD), 1)
    low = jnp.where(lane < HEAD, 1.0, 0.0)
    return low.astype(dtype), (1.0 - low).astype(dtype)


def two_heads(pair):
    low, high = lane_halves(bf16)
    return jnp.concatenate([pair * low, pair * high], axis=0)


def same_sequence(rows, row0, cols, col0, seq_len):
    row = (lax.broadcasted_iota(jnp.int32, (rows, cols), 0) + row0) // seq_len
    col = (lax.broadcasted_iota(jnp.int32, (rows, cols), 1) + col0) // seq_len
    return row == col


def softmax_down(scores, mask):
    keys = mask.shape[0]
    parts, sums = [], []
    for k in range(2):
        part = jnp.where(mask, scores[k * keys : (k + 1) * keys], -1e30)
        most = jnp.max(part, axis=0, keepdims=True)
        raised = jnp.exp(part - most)
        total = jnp.sum(raised, axis=0, keepdims=True)
        parts.append(raised * (1.0 / total))
        sums.append(most + jnp.log(total))
    return parts, sums


def fold_kernel(extra, keep_a, got_a, keep_b, got_b, *refs):
    outs = refs[-5:] if extra else refs[-4:]
    rows, half, tile = keep_a.shape[0], keep_a.shape[0] // 2, 256

    @pl.loop(0, keep_a.shape[1] // tile)
    def _(step):
        cols = pl.ds(pl.multiple_of(step * tile, tile), tile)
        for k, (kept, got) in enumerate(((keep_a, got_a), (keep_b, got_b))):
            for j in range(2):
                at = slice(j * half, (j + 1) * half)
                total = kept[at, cols].astype(f32) + got[at, cols].astype(f32)
                outs[2 * k + j][:half, cols] = total.astype(bf16)

    if extra:
        came = refs[1][...] if extra > 1 else got_a[rows : rows + 16, :].astype(f32)[:8]
        sums = refs[0][...] + came
        outs[4][...] = sums
        outs[1][half : half + 16, :] = jnp.concatenate([sums, sums], axis=0).astype(bf16)


def fold(parts, after=(), sums=()):
    rows, cols = parts[0].shape
    if rows % 32:
        whole = [
            (kept.astype(f32) + got.astype(f32)).astype(bf16)
            for kept, got in (parts[:2], parts[2:])
        ]
        return [part for one in whole for part in (one[: rows // 2], one[rows // 2 :])]
    half = (rows // 2, cols)
    shapes = [stays(half, bf16)] * 4
    if sums:
        shapes[1] = stays((rows // 2 + 16, cols), bf16)
        shapes.append(stays((8, cols), f32))
    return pl.pallas_call(
        functools.partial(fold_kernel, len(sums)),
        out_shape=shapes,
        in_specs=in_vmem(4 + len(sums)) + anywhere(after),
        out_specs=in_vmem(len(shapes)),
        compiler_params=params(8 << 20),
        cost_estimate=cost(2 * rows * cols, 12 * rows * cols),
        name="fold",
    )(*parts, *sums, *after)


def fold_last_kernel(extra, keep_a, got_a, keep_b, got_b, *refs):
    outs = refs[-4:]
    cols = keep_a.shape[1]
    rows = keep_a.shape[0] // 4
    if extra:
        sums = refs[0][...] + got_a[4 * rows : 4 * rows + 16, :].astype(f32)[:8]
    for k, (kept, got) in enumerate(((keep_a, got_a), (keep_b, got_b))):
        total = kept[...].astype(f32) + got[: 4 * rows, :].astype(f32)
        at = slice(k * cols, (k + 1) * cols)
        for j, out in enumerate(outs):
            part = total[j * rows : (j + 1) * rows]
            if extra:
                row = jnp.broadcast_to(sums[k : k + 1], (8, cols))
                part = jnp.concatenate([part, row], axis=0)
            out[:, at] = part.astype(out.dtype)


def fold_last(parts, after=(), sums=()):
    rows, cols = parts[0].shape
    shape = (rows // 4 + (8 if sums else 0), 2 * cols)
    if rows % 32:
        pairs = (parts[:2], parts[2:])
        both = [kept.astype(f32) + got.astype(f32) for kept, got in pairs]
        own, *others = jnp.split(jnp.concatenate(both, axis=1), 4)
        return [own] + [other.astype(bf16) for other in others]
    return pl.pallas_call(
        functools.partial(fold_last_kernel, len(sums)),
        out_shape=[stays(shape, f32)] + [stays(shape, bf16)] * 3,
        in_specs=in_vmem(4 + len(sums)) + anywhere(after),
        out_specs=in_vmem(4),
        compiler_params=params(8 << 20),
        cost_estimate=cost(2 * rows * cols, 12 * rows * cols),
        name="fold_last",
    )(*parts, *sums, *after)


def anywhere(after):
    return [pl.BlockSpec(memory_space=pl.ANY)] * len(after)


def pair_cols(part, pair):
    start = part * D + pair * 2 * HEAD
    return slice(start, start + 2 * HEAD)


def line(ref):
    return ref[...].astype(f32).reshape(1, -1)


def norm_rows(src, dst, gain, bias, step_rows):
    @pl.loop(0, src.shape[0] // step_rows)
    def _(step):
        at = pl.ds(pl.multiple_of(step * step_rows, step_rows), step_rows)
        unit, _ = norm_parts(src[at, :].astype(f32))
        dst[at, :] = (unit * gain + bias).astype(bf16)


def attend_along(qkv_ref, att_ref, q_rows, k_rows, mask):
    low, high = lane_halves(f32)
    for pair in range(HEADS // 2):
        queries = two_heads(qkv_ref[q_rows, pair_cols(0, pair)] * bf16(HEAD ** (-0.5)))
        scores = mul_bt(queries, qkv_ref[k_rows, pair_cols(1, pair)])
        scores = jnp.where(mask, scores, -1e30)
        raised = jnp.exp(scores - jnp.max(scores, axis=-1, keepdims=True))
        probs = (raised * (1.0 / jnp.sum(raised, axis=-1, keepdims=True))).astype(bf16)
        half = probs.shape[0] // 2
        mixed = mul(probs, qkv_ref[k_rows, pair_cols(2, pair)])
        att_ref[q_rows, pair_cols(0, pair)] = (mixed[:half] * low + mixed[half:] * high).astype(bf16)


def attend(qkv_ref, att_ref, q_rows, k_rows, mask, keep_sums):
    for pair in range(HEADS // 2):
        queries = qkv_ref[q_rows, pair_cols(0, pair)] * bf16(HEAD ** (-0.5))
        scores = mul_bt(two_heads(qkv_ref[k_rows, pair_cols(1, pair)]), queries)
        probs, sums = softmax_down(scores, mask)
        vals = two_heads(qkv_ref[k_rows, pair_cols(2, pair)])
        mixed = mul_at(jnp.concatenate(probs, axis=0).astype(bf16), vals)
        att_ref[q_rows, pair_cols(0, pair)] = mixed.astype(bf16)
        for k in range(2):
            keep_sums(2 * pair + k, sums[k])


def text_front_kernel(
    x_ref, g1_ref, b1_ref, wqkv_ref, wo_ref, g2_ref, b2_ref, h1_ref, qkv_ref, att_ref, mid_ref,
    h2_ref, sum_ref, lse_ref
):
    rows, chunk = x_ref.shape[0], 128
    norm_rows(x_ref, h1_ref, line(g1_ref), line(b1_ref), chunk)

    @pl.loop(0, 3 * D // 256)
    def _(step):
        at = pl.ds(pl.multiple_of(step * 256, 256), 256)
        qkv_ref[:, at] = mul(h1_ref[...], wqkv_ref[:, at]).astype(bf16)

    mask = same_sequence(chunk, 0, chunk, 0, TXT_LEN)

    @pl.loop(0, rows // chunk)
    def _(step):
        at = pl.ds(pl.multiple_of(step * chunk, chunk), chunk)

        def keep_sums(head, value):
            lse_ref[pl.ds(step * 16 + head, 1), :] = value

        attend(qkv_ref, att_ref, at, at, mask, keep_sums)

    @pl.loop(0, D // 256)
    def _(step):
        at = pl.ds(pl.multiple_of(step * 256, 256), 256)
        mid_ref[:, at] = x_ref[:, at].astype(f32) + mul(att_ref[...], wo_ref[:, at])

    norm_rows(mid_ref, h2_ref, line(g2_ref), line(b2_ref), chunk)
    per = chunk // TXT_LEN

    @pl.loop(0, rows // chunk)
    def _(step):
        values = mid_ref[pl.ds(pl.multiple_of(step * chunk, chunk), chunk), :]
        sum_ref[pl.ds(pl.multiple_of(step * per, per), per), :] = jnp.sum(
            values.reshape(per, TXT_LEN, D), axis=1
        )


def text_front(rows_in, gain1, bias1, wqkv, wo, gain2, bias2):
    rows = rows_in.shape[0]
    shapes = [
        ((rows, D), bf16),
        ((rows, 3 * D), bf16),
        ((rows, D), bf16),
        ((rows, D), f32),
        ((rows, D), bf16),
        ((rows // TXT_LEN, D), f32),
        ((rows // 128 * 16, 128), f32),
    ]
    return pl.pallas_call(
        text_front_kernel,
        out_shape=[jax.ShapeDtypeStruct(*item) for item in shapes],
        compiler_params=params(),
        cost_estimate=cost(rows * D * D * 8, 14 * D * rows + 8 * D * D, rows * 128 * HEADS),
        name="text_front",
    )(rows_in, gain1, bias1, wqkv, wo, gain2, bias2)


def image_front_kernel(
    windows, x_ref, order_ref, g1_ref, b1_ref, g2_ref, b2_ref, *refs
):
    h2_ref, sum_ref, early_ref = refs[-10:-7]
    w_ref, h1_ref, placed_ref, qkv_ref, att_ref, mid_ref, sems = refs[-7:]
    rows, chunk = x_ref.shape[0], 80
    copies, row = [], 0
    for k, piece in enumerate(refs[:-10]):
        place = w_ref.at[pl.ds(row, piece.shape[0]), :]
        copies.append(pltpu.make_async_copy(piece, place, sems.at[k]))
        row += piece.shape[0]
    for copy in copies:
        copy.start()

    def place_columns(src, dst):
        @pl.loop(0, D // 256)
        def _(step):
            at = pl.ds(pl.multiple_of(step * 256, 256), 256)
            dst[:, at] = mul_bt(src[...], chosen(order_ref[at, :])).astype(bf16)

    norm_rows(x_ref, h1_ref, line(g1_ref), line(b1_ref), chunk)
    place_columns(h1_ref, placed_ref)
    for copy in copies:
        copy.wait()

    @pl.loop(0, 3 * D // 256)
    def _(step):
        at = pl.ds(pl.multiple_of(step * 256, 256), 256)
        qkv_ref[:, at] = mul(placed_ref[...], w_ref[:, at]).astype(bf16)

    for row0, count, key0, keys in windows:
        one = same_sequence(count, row0, keys, key0, IMG_LEN)
        mask = jnp.concatenate([one, one], axis=0)
        attend_along(qkv_ref, att_ref, pl.ds(row0, count), pl.ds(key0, keys), mask)
    place_columns(att_ref, placed_ref)

    @pl.loop(0, D // 256)
    def _(step):
        at = pl.ds(pl.multiple_of(step * 256, 256), 256)
        there = pl.ds(pl.multiple_of(step * 256 + 3 * D, 256), 256)
        mid_ref[:, at] = x_ref[:, at].astype(f32) + mul(placed_ref[...], w_ref[:, there])

    norm_rows(mid_ref, h2_ref, line(g2_ref), line(b2_ref), chunk)
    place_columns(h2_ref, placed_ref)
    pool = pool_matrix(rows // IMG_LEN, rows, 0, IMG_LEN)

    @pl.loop(0, EARLY // TILE)
    def _(step):
        at = pl.ds(pl.multiple_of(step * TILE, TILE), TILE)
        there = pl.ds(pl.multiple_of(step * TILE + 4 * D, TILE), TILE)
        value, _ = gelu_parts(mul(placed_ref[...], w_ref[:, there]))
        early_ref[:, at] = mul(pool, value.astype(bf16))

    for k in range(rows // IMG_LEN):
        first, last = k * IMG_LEN, (k + 1) * IMG_LEN
        start, end = first // 8 * 8, -(-last // 8) * 8
        values = mid_ref[start:end, :]
        place = lax.broadcasted_iota(jnp.int32, values.shape, 0) + start
        inside = (place >= first) & (place < last)
        sum_ref[k : k + 1, :] = jnp.sum(jnp.where(inside, values, 0.0), axis=0, keepdims=True)


def image_front(rows_in, pieces, source, gain1, bias1, gain2, bias2):
    rows = rows_in.shape[0]
    windows = ((0, 208, 0, 256), (208, 192, 192, 208))
    vmem = pl.BlockSpec(memory_space=pltpu.VMEM)
    return pl.pallas_call(
        functools.partial(image_front_kernel, windows),
        out_shape=[
            jax.ShapeDtypeStruct((rows, D), bf16),
            jax.ShapeDtypeStruct((rows // IMG_LEN, D), f32),
            jax.ShapeDtypeStruct((rows // IMG_LEN, EARLY), f32),
        ],
        in_specs=[vmem] * 6 + anywhere(pieces),
        out_specs=[vmem] * 3,
        scratch_shapes=[
            pltpu.VMEM((D, 4 * D + EARLY), bf16),
            pltpu.VMEM((rows, D), bf16),
            pltpu.VMEM((rows, D), bf16),
            pltpu.VMEM((rows, 3 * D), bf16),
            pltpu.VMEM((rows, D), bf16),
            pltpu.VMEM((rows, D), f32),
            pltpu.SemaphoreType.DMA((len(pieces),)),
        ],
        compiler_params=params(),
        cost_estimate=cost(rows * D * D * 12, 8 * D * D, rows * 256 * HEADS),
        name="image_front",
    )(rows_in, source, gain1, bias1, gain2, bias2, *pieces)


def gelu_parts(inner):
    half = 0.5 * (1.0 + lax.erf(inner * (0.5**0.5)))
    return inner * half, half


def pack_kernel(unit_ref, pos_ref, *refs):
    refs[-1][:, :D] = unit_ref[...].astype(bf16)
    refs[-1][:, D:] = pos_ref[...]


def packed(unit, positive, after):
    shape = (unit.shape[0], D + positive.shape[1])
    return pl.pallas_call(
        pack_kernel,
        out_shape=jax.ShapeDtypeStruct(shape, bf16),
        in_specs=[pl.BlockSpec(memory_space=pltpu.VMEM)] * 2 + anywhere(after),
        compiler_params=params(),
        cost_estimate=cost(shape[0] * shape[1], 4 * shape[0] * shape[1]),
        name="packed",
    )(unit, positive, *after)


def pool_matrix(count, rows, row0, seq_len):
    row = (lax.broadcasted_iota(jnp.int32, (count, rows), 1) + row0) // seq_len
    return jnp.where(row == lax.broadcasted_iota(jnp.int32, (count, rows), 0), 1.0, 0.0).astype(bf16)


def two_terms(mean):
    high = mean.astype(bf16)
    low = (mean - high.astype(f32)).astype(bf16)
    return jnp.concatenate([high, low], axis=0)


def unit_rows(pooled):
    inverse = lax.rsqrt(jnp.sum(pooled * pooled, axis=-1, keepdims=True) + norm_eps)
    return pooled * inverse, inverse


def text_up_kernel(h2_ref, wu_ref, wd_ref, sum_ref, *refs):
    slope_ref, hid_ref, unit_ref, inv_ref, acc = refs[-5:]
    step = pl.program_id(0)
    chunk = 320
    per = chunk // TXT_LEN
    pool = pool_matrix(per, chunk, 0, TXT_LEN)
    for k in range(h2_ref.shape[0] // chunk):
        inner = mul(h2_ref[k * chunk : (k + 1) * chunk, :], wu_ref[...])
        value, half = gelu_parts(inner)
        slope = half + inner * (jnp.exp(-0.5 * inner * inner) * 0.3989422804014327)
        slope_ref[k * chunk : (k + 1) * chunk, :] = slope.astype(bf16)
        hid_ref[k * per : (k + 1) * per, :] = mul(pool, value.astype(bf16))
    terms = mul(two_terms(hid_ref[...] * (1.0 / TXT_LEN)), wd_ref[...])
    count = hid_ref.shape[0]
    added = terms[:count] + terms[count:]

    @pl.when(step == 0)
    def _():
        acc[...] = sum_ref[...] * (1.0 / TXT_LEN) + added

    @pl.when(step > 0)
    def _():
        acc[...] += added

    @pl.when(step == pl.num_programs(0) - 1)
    def _():
        unit, inverse = unit_rows(acc[...])
        unit_ref[...] = unit
        inv_ref[...] = jnp.broadcast_to(inverse, inv_ref.shape)


def text_up(normed2, weight_up, weight_down, middle_sum, after=()):
    rows, count = normed2.shape[0], middle_sum.shape[0]
    fixed = lambda shape: pl.BlockSpec(shape, lambda i: (0, 0))
    return pl.pallas_call(
        text_up_kernel,
        grid=(FF // TILE,),
        out_shape=[
            jax.ShapeDtypeStruct((rows, FF), bf16),
            jax.ShapeDtypeStruct((count, FF), f32),
            jax.ShapeDtypeStruct((count, D), f32),
            jax.ShapeDtypeStruct((count, 128), f32),
        ],
        in_specs=[
            fixed((rows, D)),
            pl.BlockSpec((D, TILE), lambda i: (0, i)),
            pl.BlockSpec((TILE, D), lambda i: (i, 0)),
            fixed((count, D)),
        ]
        + anywhere(after),
        out_specs=[
            pl.BlockSpec((rows, TILE), lambda i: (0, i)),
            pl.BlockSpec((count, TILE), lambda i: (0, i)),
            fixed((count, D)),
            fixed((count, 128)),
        ],
        scratch_shapes=[pltpu.VMEM((count, D), f32)],
        compiler_params=params(),
        cost_estimate=cost(2 * rows * D * FF, 4 * D * FF + 2 * rows * FF, 20 * rows * FF),
        name="text_up",
    )(normed2, weight_up, weight_down, middle_sum, *after)


def image_up_kernel(fold, h2_ref, wu_ref, wd_ref, first_ref, sum_ref, early_ref, out_ref, acc, picked):
    step = pl.program_id(0)
    rows, count = h2_ref.shape[0], sum_ref.shape[0]
    part = TILE // fold

    def through_down(summed, groups):
        moved = mul(two_terms(summed * (1.0 / IMG_LEN)), picked[...]).astype(bf16)
        weight = jnp.concatenate([groups[:, k * D : (k + 1) * D] for k in range(fold)], axis=0)
        terms = mul(moved, weight)
        return terms[:count] + terms[count:]

    @pl.when(step == 0)
    def _():
        place = lax.broadcasted_iota(jnp.int32, (TILE, TILE), 0)
        col = lax.broadcasted_iota(jnp.int32, (TILE, TILE), 1)
        source = (col % part) * fold + col // part
        picked[...] = jnp.where(place == source, 1.0, 0.0).astype(bf16)
        total = sum_ref[...] * (1.0 / IMG_LEN)
        for k in range(EARLY // TILE):
            total = total + through_down(
                early_ref[:, k * TILE : (k + 1) * TILE], first_ref[k * part : (k + 1) * part, :]
            )
        acc[...] = total

    value, _ = gelu_parts(mul(h2_ref[...], wu_ref[...]))
    summed = mul(pool_matrix(count, rows, 0, IMG_LEN), value.astype(bf16))
    acc[...] += through_down(summed, wd_ref[...])

    @pl.when(step == pl.num_programs(0) - 1)
    def _():
        out_ref[...] = unit_rows(acc[...])[0].astype(bf16)


def image_up(normed2, whole, middle_sum, early):
    rows, count = normed2.shape[0], middle_sum.shape[0]
    fold = FF // D
    before, part = EARLY // TILE, TILE // fold
    fixed = lambda shape: pl.BlockSpec(shape, lambda i: (0, 0))
    return pl.pallas_call(
        functools.partial(image_up_kernel, fold),
        grid=(FF // TILE - before,),
        out_shape=jax.ShapeDtypeStruct((count, D), bf16),
        in_specs=[
            fixed((rows, D)),
            pl.BlockSpec((D, TILE), lambda i: (0, FF // TILE + i)),
            pl.BlockSpec((part, FF), lambda i: (i + before, 0)),
            fixed((before * part, FF)),
            fixed((count, D)),
            fixed((count, EARLY)),
        ],
        out_specs=fixed((count, D)),
        scratch_shapes=[pltpu.VMEM((count, D), f32), pltpu.VMEM((TILE, TILE), bf16)],
        compiler_params=params(),
        cost_estimate=cost(2 * rows * D * FF, 4 * D * FF, 15 * rows * FF),
        name="image_up",
    )(normed2, whole, whole, whole, middle_sum, early)


def left_kernel(count, *refs):
    out_ref = refs[-1]
    for k in range(count):
        source_ref, values_ref = refs[2 * k : 2 * k + 2]

        @pl.loop(0, D // 256)
        def _(step, k=k, source_ref=source_ref, values_ref=values_ref):
            at = pl.ds(pl.multiple_of(step * 256, 256), 256)
            picked = mul_bt(chosen(source_ref[at, :]), values_ref[...])
            out_ref[k, at, :] = picked.astype(bf16)


def left_factors(*pairs):
    rows = pairs[0][1].shape[0]
    given = [item for pair in pairs for item in pair]
    return pl.pallas_call(
        functools.partial(left_kernel, len(pairs)),
        out_shape=jax.ShapeDtypeStruct((len(pairs), D, rows), bf16),
        in_specs=in_vmem(len(given)),
        out_specs=pl.BlockSpec(memory_space=pltpu.VMEM),
        compiler_params=params(24 << 20),
        cost_estimate=cost(2 * len(pairs) * rows * D * D, 4 * len(pairs) * rows * D),
        name="left_factors",
    )(*given)


def loss_parts(text_rows, pos, image_all):
    similar = mul_bt(text_rows, image_all) * logit_scale
    shifted = jnp.exp(similar - logit_scale)
    alive = jnp.max(pos, axis=1, keepdims=True)
    row_sum = jnp.sum(shifted, axis=1, keepdims=True)
    row_count = jnp.maximum(jnp.sum(pos, axis=1, keepdims=True), 1.0)
    return similar, shifted, alive, row_sum, row_count


def sums_over_captions(text_rows, pos, image_all):
    similar, shifted, alive, row_sum, row_count = loss_parts(text_rows, pos, image_all)
    pos_similar = pos * similar
    cap_term = alive * (
        logit_scale + jnp.log(row_sum) - jnp.sum(pos_similar, axis=1, keepdims=True) / row_count
    )
    return (
        jnp.sum(alive * shifted, axis=0, keepdims=True),
        jnp.sum(pos, axis=0, keepdims=True),
        jnp.sum(pos_similar, axis=0, keepdims=True),
        jnp.sum(cap_term, axis=0, keepdims=True),
        jnp.sum(alive, axis=0, keepdims=True),
    )


def loss_from(sums):
    col_sum, col_count, col_pos, cap_total, live_total = sums
    img_term = logit_scale + jnp.log(col_sum) - col_pos / col_count
    return 0.5 * cap_total / live_total + 0.5 * jnp.mean(img_term, axis=1, keepdims=True)


def grad_of_unit(text_rows, pos, image_all, col_sum, col_count, live_total):
    _, shifted, alive, row_sum, row_count = loss_parts(text_rows, pos, image_all)
    cap_share, img_share = 0.5 / live_total, 0.5 / image_all.shape[0]
    grad_sims = alive * shifted * (cap_share / row_sum + img_share / col_sum) - pos * (
        cap_share / row_count + img_share / col_count
    )
    return mul(grad_sims.astype(bf16), image_all) * logit_scale


def turned(grad, unit):
    return grad - unit * jnp.sum(grad * unit, axis=-1, keepdims=True)


def loss_kernel(
    pack_ref, image_ref, own_ref, unit_ref, inv_ref, loss_ref, row_ref, low_ref, col_sum_ref,
    col_count_ref, live_ref
):
    image_all = image_ref[...]
    chunk = 256
    total = None
    for k in range(pack_ref.shape[0] // chunk):
        at = slice(k * chunk, (k + 1) * chunk)
        part = sums_over_captions(pack_ref[at, :D], pack_ref[at, D:].astype(f32), image_all)
        total = part if total is None else [a + b for a, b in zip(total, part)]
    loss_ref[...] = jnp.broadcast_to(loss_from(total), loss_ref.shape)
    col_sum, col_count, _, _, live_total = total
    col_sum_ref[...] = col_sum
    col_count_ref[...] = col_count
    live_ref[...] = jnp.broadcast_to(live_total, live_ref.shape)
    grad = grad_of_unit(
        own_ref[:, :D], own_ref[:, D:].astype(f32), image_all, col_sum, col_count, live_total
    )
    row = inv_ref[:, :1] * turned(grad, unit_ref[...]) * (1.0 / TXT_LEN)
    row_ref[...] = row
    low_ref[...] = row.astype(bf16)


def loss_and_rows(pack, image_all, own_pack, unit, inverse):
    images, count = image_all.shape[0], own_pack.shape[0]
    shapes = [(1, 128), (count, D), (count, D), (1, images), (1, images), (1, 128)]
    kinds = [f32, f32, bf16, f32, f32, f32]
    return pl.pallas_call(
        loss_kernel,
        out_shape=[jax.ShapeDtypeStruct(*item) for item in zip(shapes, kinds)],
        in_specs=in_vmem(5),
        out_specs=in_vmem(len(shapes)),
        compiler_params=params(16 << 20),
        cost_estimate=cost(2 * pack.shape[0] * images * D, 2 * pack.size, pack.shape[0] * images),
        name="loss_and_rows",
    )(pack, image_all, own_pack, unit, inverse)


def down_kernel(pack_ref, image_ref, col_sum_ref, col_count_ref, live_ref, hid_ref, *refs):
    step, out_ref = pl.program_id(0), refs[-1]
    text_rows = pack_ref[:, :D]
    grad = grad_of_unit(
        text_rows, pack_ref[:, D:].astype(f32), image_ref[...], col_sum_ref[...],
        col_count_ref[...], live_ref[:, :1]
    )
    rows = (turned(grad, text_rows.astype(f32)) * (1.0 / TXT_LEN)).astype(bf16)
    part = mul_at(hid_ref[...], rows)

    @pl.when(step == 0)
    def _():
        out_ref[...] = part

    @pl.when(step > 0)
    def _():
        out_ref[...] += part


def grad_of_down(pack, image_all, col_sum, col_count, live_total, hidden_cols, after):
    images, chunk = image_all.shape[0], 256
    fixed = lambda shape: pl.BlockSpec(shape, lambda i: (0, 0))
    per = hidden_cols.shape[1]
    return pl.pallas_call(
        down_kernel,
        grid=(pack.shape[0] // chunk,),
        out_shape=jax.ShapeDtypeStruct((per, D), f32),
        in_specs=[
            pl.BlockSpec((chunk, pack.shape[1]), lambda i: (i, 0)),
            fixed((images, D)), fixed((1, images)), fixed((1, images)), fixed((1, 128)),
            pl.BlockSpec((chunk, per), lambda i: (i, 0)),
        ]
        + anywhere(after),
        out_specs=fixed((per, D)),
        compiler_params=params(16 << 20),
        cost_estimate=cost(4 * pack.shape[0] * images * D, 2 * pack.size, pack.shape[0] * images),
        name="grad_of_down",
    )(pack, image_all, col_sum, col_count, live_total, hidden_cols, *after)


def mlp_back_kernel(
    low_ref, gain_ref, row_ref, wd_hbm, slope_hbm, wu_hbm, lhs_hbm, mid_hbm, keep_a, send_a, keep_b,
    send_b, out_ref, sums_out, wd_ref, slope_ref, wu_ref, lhs_ref, mid_ref, sems, whole_sems
):
    count, rows = low_ref.shape[0], out_ref.shape[0]
    half, steps = D // 2, FF // 2 // TILE

    def copies(tile, slot):
        at = pl.ds(pl.multiple_of(tile * TILE, TILE), TILE)
        return (
            pltpu.make_async_copy(wd_hbm.at[at, :], wd_ref.at[slot], sems.at[0, slot]),
            pltpu.make_async_copy(slope_hbm.at[:, at], slope_ref.at[slot], sems.at[1, slot]),
            pltpu.make_async_copy(wu_hbm.at[:, at], wu_ref.at[slot], sems.at[2, slot]),
        )

    lhs_copy = pltpu.make_async_copy(lhs_hbm, lhs_ref, whole_sems.at[0])
    mid_copy = pltpu.make_async_copy(mid_hbm, mid_ref, whole_sems.at[1])
    for copy in copies(0, 0):
        copy.start()
    lhs_copy.start()
    for k, (keep, send) in enumerate(((keep_a, send_a), (keep_b, send_b))):

        @pl.loop(0, steps)
        def _(step, k=k, keep=keep, send=send):
            tile = k * steps + step
            slot = lax.rem(tile, 2)

            @pl.when(tile + 1 < 2 * steps)
            def _():
                for copy in copies(tile + 1, 1 - slot):
                    copy.start()

            for copy in copies(tile, slot):
                copy.wait()
            if k == 0:

                @pl.when(step == 0)
                def _():
                    lhs_copy.wait()
                    mid_copy.start()

            there = pl.ds(pl.multiple_of(step * TILE, TILE), TILE)
            hidden = mul_bt(low_ref[...], wd_ref[slot])
            wide = jnp.broadcast_to(hidden[:, None, :], (count, TXT_LEN, TILE))
            inner = (wide.reshape(rows, TILE) * slope_ref[slot].astype(f32)).astype(bf16)
            weight = mul(lhs_ref[k], inner).astype(bf16)
            keep[:, there] = weight[:half]
            send[:, there] = weight[half:]
            added = mul_bt(inner, wu_ref[slot])
            if k == 0:

                @pl.when(step == 0)
                def _():
                    out_ref[...] = added

                @pl.when(step > 0)
                def _():
                    out_ref[...] += added
            else:
                out_ref[...] += added

    chunk = 128
    per = chunk // TXT_LEN
    gain = line(gain_ref)
    sums_out[...] = jnp.zeros_like(sums_out)
    mid_copy.wait()

    @pl.loop(0, rows // chunk)
    def _(k):
        at = pl.ds(pl.multiple_of(k * chunk, chunk), chunk)
        unit, scale = norm_parts(mid_ref[at, :])
        grad = out_ref[at, :]
        sums_out[:, :D] += jnp.sum(grad * unit, axis=0, keepdims=True)
        sums_out[:, D:] += jnp.sum(grad, axis=0, keepdims=True)
        row = row_ref[pl.ds(pl.multiple_of(k * per, per), per), :]
        row = jnp.broadcast_to(row[:, None, :], (per, TXT_LEN, D)).reshape(chunk, D)
        out_ref[at, :] = row + norm_back(unit, scale, gain, grad)


def mlp_back(grad_row, grad_low, weight_down, slope, weight_up, lhs, middle, gain):
    rows = slope.shape[0]
    return pl.pallas_call(
        mlp_back_kernel,
        out_shape=[stays((D // 2, FF // 2), bf16)] * 4
        + [stays((rows, D), f32), stays((1, 2 * D), f32)],
        in_specs=in_vmem(3) + [pl.BlockSpec(memory_space=pltpu.HBM)] * 5,
        out_specs=in_vmem(6),
        scratch_shapes=[
            pltpu.VMEM((2, TILE, D), bf16),
            pltpu.VMEM((2, rows, TILE), bf16),
            pltpu.VMEM((2, D, TILE), bf16),
            pltpu.VMEM((2, D, rows), bf16),
            pltpu.VMEM((rows, D), f32),
            pltpu.SemaphoreType.DMA((3, 2)),
            pltpu.SemaphoreType.DMA((2,)),
        ],
        compiler_params=params(28 << 20),
        cost_estimate=cost(4 * rows * D * FF, 4 * D * FF + 2 * rows * FF + 2 * D * FF, rows * FF),
        name="mlp_back",
    )(grad_low, gain, grad_row, *in_hbm(weight_down, slope, weight_up, lhs, middle))


def attention_back_kernel(first, grad_ref, wo_ref, qkv_ref, lse_ref, *refs):
    low_ref, out_ref = refs[-2:]
    chunk = 128
    mask = same_sequence(chunk, 0, chunk, 0, TXT_LEN)

    @pl.loop(0, low_ref.shape[0] // chunk)
    def _(step):
        here = pl.ds(pl.multiple_of((first + step) * chunk, chunk), chunk)
        there = pl.ds(pl.multiple_of(step * chunk, chunk), chunk)
        sums = lse_ref[pl.ds(pl.multiple_of((first + step) * 16, 16), 16), :]
        low = grad_ref[here, :].astype(bf16)
        low_ref[there, :] = low
        grad_att = mul_bt(low, wo_ref[...]).astype(bf16)
        for pair in range(HEADS // 2):
            queries = qkv_ref[here, pair_cols(0, pair)] * bf16(HEAD ** (-0.5))
            keys = two_heads(qkv_ref[here, pair_cols(1, pair)])
            vals = two_heads(qkv_ref[here, pair_cols(2, pair)])
            grads = grad_att[:, pair_cols(0, pair)]
            scores, grad_probs = mul_bt(keys, queries), mul_bt(vals, grads)
            probs, grad_scores = [], []
            for k in range(2):
                at = slice(k * chunk, (k + 1) * chunk)
                head = 2 * pair + k
                shifted = scores[at] - sums[head : head + 1, :]
                prob = jnp.where(mask, jnp.exp(jnp.where(mask, shifted, 0.0)), 0.0)
                along = jnp.sum(grad_probs[at] * prob, axis=0, keepdims=True)
                grad_scores.append((prob * (grad_probs[at] - along)).astype(bf16))
                probs.append(prob.astype(bf16))
            grad_q = mul_at(jnp.concatenate(grad_scores, axis=0), keys) * HEAD ** (-0.5)
            grad_k = mul(jnp.concatenate(grad_scores, axis=1), two_heads(queries))
            grad_v = mul(jnp.concatenate(probs, axis=1), two_heads(grads))
            out_ref[there, pair_cols(0, pair)] = grad_q.astype(bf16)
            out_ref[there, pair_cols(1, pair)] = grad_k.astype(bf16)
            out_ref[there, pair_cols(2, pair)] = grad_v.astype(bf16)


def attention_back(grad_middle, weight_out, project, log_sums, first, count, after=()):
    rows = count * 128
    return pl.pallas_call(
        functools.partial(attention_back_kernel, first),
        out_shape=[stays((rows, D), bf16), stays((rows, 3 * D), bf16)],
        in_specs=in_vmem(4) + anywhere(after),
        out_specs=in_vmem(2),
        compiler_params=params(16 << 20),
        cost_estimate=cost(10 * rows * D * D, 16 * rows * D + 2 * D * D, rows * 128 * HEADS),
        name="attention_back",
    )(grad_middle, weight_out, project, log_sums, *after)


def mul_rows(lhs, parts, cols):
    total, row = 0.0, 0
    for part in parts:
        total = total + mul(lhs[:, row : row + part.shape[0]], part[:, cols])
        row += part.shape[0]
    return total


def weight_back_kernel(factors, groups, lhs_ref, *refs):
    keep_a, send_a, keep_b, send_b = refs[-4:]
    half = D // 2
    for k, (factor, group, col) in enumerate(factors):
        parts = refs[sum(groups[:group]) : sum(groups[: group + 1])]
        weight = mul_rows(lhs_ref.at[factor], parts, slice(col * D, (col + 1) * D)).astype(bf16)
        at = slice(k % 2 * D, (k % 2 + 1) * D)
        (keep_b if k > 1 else keep_a)[:, at] = weight[:half]
        (send_b if k > 1 else send_a)[:, at] = weight[half:]


def weight_back(lhs, groups, factors, after=()):
    rows = lhs.shape[2]
    given = [part for group in groups for part in group]
    return pl.pallas_call(
        functools.partial(weight_back_kernel, factors, [len(group) for group in groups]),
        out_shape=[stays((D // 2, 2 * D), bf16)] * 4,
        in_specs=in_vmem(1 + len(given)) + anywhere(after),
        out_specs=in_vmem(4),
        compiler_params=params(16 << 20),
        cost_estimate=cost(8 * rows * D * D, 8 * rows * D + 14 * D * D),
        name="weight_back",
    )(lhs, *given, *after)


def input_back_kernel(count, *refs):
    projs = refs[:count]
    w_ref, x_ref, gain_ref, mid_ref, sums_ref = refs[count : count + 5]
    out_ref, sums_out = refs[-2:]
    rows, chunk = x_ref.shape[0], 128

    @pl.loop(0, D // 256)
    def _(step):
        at = pl.ds(pl.multiple_of(step * 256, 256), 256)
        row = 0
        for part in projs:
            there = slice(row, row + part.shape[0])
            out_ref[there, at] = mul_bt(part[...], w_ref[at, :])
            row += part.shape[0]

    gain = line(gain_ref)
    sums_out[...] = jnp.zeros_like(sums_out)
    sums_out[1:2, :] = sums_ref[...]

    @pl.loop(0, rows // chunk)
    def _(k):
        at = pl.ds(pl.multiple_of(k * chunk, chunk), chunk)
        unit, scale = norm_parts(x_ref[at, :].astype(f32))
        grad = out_ref[at, :]
        sums_out[0:1, :D] += jnp.sum(grad * unit, axis=0, keepdims=True)
        sums_out[0:1, D:] += jnp.sum(grad, axis=0, keepdims=True)
        out_ref[at, :] = mid_ref[at, :] + norm_back(unit, scale, gain, grad)


def input_back(grad_projs, weight, rows_in, gain, grad_middle, sums, after=()):
    rows = rows_in.shape[0]
    return pl.pallas_call(
        functools.partial(input_back_kernel, len(grad_projs)),
        out_shape=[jax.ShapeDtypeStruct((rows, D), f32), stays((8, 2 * D), f32)],
        in_specs=in_vmem(len(grad_projs) + 5) + anywhere(after),
        out_specs=in_vmem(2),
        compiler_params=params(16 << 20),
        cost_estimate=cost(6 * rows * D * D, 14 * rows * D + 6 * D * D),
        name="input_back",
    )(*grad_projs, weight, rows_in, gain, grad_middle, sums, *after)


def local(
    images,
    captions,
    img_gain1,
    img_bias1,
    img_qkv,
    img_out,
    img_gain2,
    img_bias2,
    img_up,
    img_down,
    txt_gain1,
    txt_bias1,
    txt_qkv,
    txt_out,
    txt_gain2,
    txt_bias2,
    txt_up,
    txt_down,
    counts,
    matches,
):
    peers = lax.axis_size(AXIS)
    own = lax.axis_index(AXIS)
    per = D // peers
    img_local = counts.shape[0]
    cap_local = matches.shape[0]
    total_images = matches.shape[1]

    up_rows = img_up.reshape(per, FF)
    whole = lax.all_gather(
        jnp.concatenate([img_down.reshape(per, FF), up_rows[:, EARLY:]], axis=1),
        AXIS,
        axis=0,
        tiled=True,
    )
    small = peers == 32
    shard = jnp.concatenate(
        [img_qkv.reshape(per, 3 * D), img_out.reshape(per, D), up_rows[:, :EARLY]], axis=1
    )
    if small:
        line, source = gathered_line(shard), row_order((1, 4, 2, 16, 8))
    else:
        line, source = lax.all_gather(shard, AXIS, axis=0, tiled=True), row_order(())

    normed1, project, attended, middle, normed2, middle_sum, log_sums = text_front(
        captions, txt_gain1, txt_bias1, txt_qkv, txt_out, txt_gain2, txt_bias2
    )
    middle_sum, line = in_turn(middle_sum, line)
    beside, above = (swapped(line, 2), swapped(line, 4)) if small else (line, line)
    slope, hidden_sum, text_unit, inverse = text_up(
        normed2, txt_up, txt_down, middle_sum, (line,)
    )
    text_unit, normed2, beside, above = lax.optimization_barrier(
        (text_unit, normed2, beside, above)
    )

    ends_at = jnp.cumsum(counts)
    slot_ids = lax.iota(jnp.int32, cap_local)
    owner = jnp.sum((ends_at[None, :] <= slot_ids[:, None]).astype(jnp.int32), axis=1)
    owner = owner + own * img_local
    live = slot_ids < ends_at[-1]
    columns = lax.iota(jnp.int32, total_images)
    positive = ((matches > 0) | (owner[:, None] == columns[None, :])) & live[:, None]

    order_a, order_b, tail = stage_orders()
    source_a, source_b = row_order(order_a + tail[::-1]), row_order(order_b + tail[::-1])
    own_pack = packed(text_unit, positive.astype(bf16), ())
    lhs_up = left_factors((source_a, normed2), (source_b, normed2))
    pieces = [line]
    if small:
        first, second = diagonal(beside, above)
        own_pack, first, second, lhs_up = lax.optimization_barrier(
            (own_pack, first, second, lhs_up)
        )
        held = own_pack[None]
        others = [swapped(held, mask) for mask in (8, 16, 24)]
        pieces = [line, beside, above, first, second]
        pieces = pieces + [swapped(piece, 1) for piece in pieces]

    normed_img, middle_img, early = image_front(
        images, pieces, source, img_gain1, img_bias1, img_gain2, img_bias2
    )
    if small:
        scaled_sum = (hidden_sum * inverse[:, :1]).astype(bf16)
        normed_img, scaled_sum, others = lax.optimization_barrier((normed_img, scaled_sum, others))
        held = joined(joined(held, others[0], 8), joined(others[1], others[2], 8), 16, 1)
        text_beside, text_above = swapped(held, 2), swapped(held, 4)
        hidden_cols = lax.all_to_all(scaled_sum, AXIS, split_axis=1, concat_axis=0, tiled=True)
    image_low = image_up(normed_img, whole, middle_img, early)
    if small:
        image_low, text_beside, text_above, hidden_cols = lax.optimization_barrier(
            (image_low, text_beside, text_above, hidden_cols)
        )
        across = jnp.concatenate(diagonal(text_beside, text_above), axis=0)
        held = joined(joined(held, text_beside, 2), joined(text_above, across, 2), 4, 4)
        text_pack = joined(held, swapped(held, 1), 1).reshape(-1, D + total_images)
    image_all = spread(image_low).reshape(total_images, D)
    if small:
        image_all, text_pack = in_turn(image_all, text_pack)

    if small:
        loss_value, grad_row, row_low, col_sum, col_count, live_total = loss_and_rows(
            text_pack, image_all, own_pack, text_unit, inverse
        )
        loss_value = loss_value[0, 0]
    else:
        text_low, pos = own_pack[:, :D], own_pack[:, D:].astype(f32)
        sums = lax.psum(sums_over_captions(text_low, pos, image_all), AXIS)
        loss_value = loss_from(sums)[0, 0]
        grad = grad_of_unit(text_low, pos, image_all, sums[0], sums[1], sums[4])
        grad_row = inverse[:, :1] * turned(grad, text_unit) * (1.0 / TXT_LEN)
        row_low = grad_row.astype(bf16)

    *up, grad_middle, sums = mlp_back(
        grad_row, row_low, txt_down, slope, txt_up, lhs_up, middle, txt_gain2
    )
    stages = len(order_a)
    low_one, proj_one = attention_back(grad_middle, txt_out, project, log_sums, 0, 1)
    for stage in range(stages - 2):
        up = fold(hand_on(up, stage), (proj_one,))
    low_two, proj_two = attention_back(grad_middle, txt_out, project, log_sums, 1, 4, up)
    proj_two, normed1 = in_turn(proj_two, normed1)
    lhs_rest = left_factors((source_a, normed1), (source_b, normed1), (source_b, attended))
    up = fold(hand_on(up, stages - 2), (proj_two, lhs_rest))
    projs, lows = (proj_one, proj_two), (low_one, low_two)
    rest = weight_back(lhs_rest, [projs, lows], [(0, 0, 0), (0, 0, 1), (1, 0, 2), (2, 1, 0)], up)
    up = hand_on(up, stages - 1)
    caption_grad, sums = input_back(
        projs, txt_qkv, captions, txt_gain1, grad_middle, sums, rest[:1]
    )
    caption_grad, up = in_turn(caption_grad, up)
    up = fold_last(up)
    if small:
        *rest, sums = fold(hand_on(rest, 0), up[:1], (sums, swapped(sums, 1)))
    else:
        norms = lax.psum(sums, AXIS)[:2].reshape(-1)
        for stage in range(stages - 2):
            rest = fold(hand_on(rest, stage), up[:1])
    up = hand_on_last(up)
    rest = hand_on(rest, stages - 2)
    if small:
        grad_down = grad_of_down(
            text_pack, image_all, col_sum, col_count, live_total, hidden_cols, (caption_grad,)
        )
    else:
        grad_down = lax.psum_scatter(
            mul_at(hidden_sum.astype(bf16), row_low), AXIS, scatter_dimension=0, tiled=True
        )
    grad_down, rest, up = lax.optimization_barrier((grad_down, rest, up))
    if small:
        *rest, sums = fold(rest, (), (sums,))
        rest = fold_last(hand_on(rest, stages - 1), (), (sums,))
    else:
        rest = fold_last(hand_on(fold(rest), stages - 1))
    up_share = sum_last(*up)
    rest_share = sum_last(*hand_on_last(rest))
    if small:
        norms = rest_share[per]
        rest_share = rest_share[:per]
    return (
        loss_value,
        caption_grad,
        norms[:D],
        norms[D : 2 * D],
        rest_share[:, : 3 * D].reshape(-1),
        rest_share[:, 3 * D :].reshape(-1),
        norms[2 * D : 3 * D],
        norms[3 * D :],
        up_share.reshape(-1),
        grad_down.reshape(-1),
    )


def solution(mesh):
    split, flat, whole = P("blk", None), P("blk"), P()
    image_block = (whole, whole, flat, flat, whole, whole, flat, flat)
    return jax.shard_map(
        local,
        mesh=mesh,
        in_specs=(split, split) + image_block + (whole,) * 8 + (flat, split),
        out_specs=(whole, split, whole, whole, flat, flat, whole, whole, flat, flat),
        check_vma=False,
    )
```

```python
import functools

import jax
import jax.numpy as jnp
from jax import lax
from jax.experimental import pallas as pl
from jax.experimental.pallas import tpu as pltpu
from jax.sharding import PartitionSpec as P

D = 768
FF = 3072
HEAD = 64
HEADS = D // HEAD
IMG_LEN = 50
TXT_LEN = 16
AXIS = "blk"

norm_eps = 1e-06
logit_scale = 50.0
f32 = jnp.float32
bf16 = jnp.bfloat16


def swapped(value, mask):
    peers = lax.axis_size(AXIS)
    return lax.ppermute(value, AXIS, [(i, i ^ mask) for i in range(peers)])


def bit_masks():
    peers = lax.axis_size(AXIS)
    return [1 << k for k in range(peers.bit_length() - 1)]


def joined(held, other, mask, outer=None):
    upper = (lax.axis_index(AXIS) & mask) > 0
    first = jnp.where(upper, other, held)
    second = jnp.where(upper, held, other)
    outer = held.shape[0] if outer is None else outer
    parts = [part.reshape((outer, -1) + held.shape[1:]) for part in (first, second)]
    return jnp.stack(parts, axis=1).reshape((-1,) + held.shape[1:])


def spread(block):
    peers = lax.axis_size(AXIS)
    copies = jnp.broadcast_to(block[None], (peers,) + block.shape)
    return lax.all_to_all(copies, AXIS, split_axis=0, concat_axis=0, tiled=True)


def stage_orders():
    masks = bit_masks()
    head, tail = masks[:-2], masks[-2:]
    order_a = list(head)
    order_b = list(head)
    for k in range(1, len(head) - 1, 2):
        order_b[k], order_b[k + 1] = order_b[k + 1], order_b[k]
    return order_a, order_b, tail


def row_order(bits):
    peers = lax.axis_size(AXIS)
    own = lax.axis_index(AXIS)
    per = D // peers
    places = lax.broadcasted_iota(jnp.int32, (D, 1), 0)
    block = places // per
    target = jnp.zeros_like(block) + own
    for k, mask in enumerate(bits):
        target = target ^ (((block >> (len(bits) - 1 - k)) & 1) * mask)
    return target * per + places % per


def chosen(source):
    column = lax.broadcasted_iota(jnp.int32, (source.shape[0], D), 1)
    return jnp.where(column == source, 1.0, 0.0).astype(bf16)


def gathered_line(shard):
    return jnp.concatenate([shard] + [swapped(shard, mask) for mask in (8, 16, 24)], axis=0)


def diagonal(beside, above):
    half = beside.shape[0] // 2
    return swapped(beside[:half], 4), swapped(above[half:], 2)


def in_turn(first, then):
    return lax.optimization_barrier((first, then))


def hand_on(parts, stage):
    order_a, order_b, _ = stage_orders()
    keep_a, send_a, keep_b, send_b = parts
    return keep_a, swapped(send_a, order_a[stage]), keep_b, swapped(send_b, order_b[stage])


def hand_on_last(blocks):
    low, high = stage_orders()[2]
    own, *others = blocks
    return own, [swapped(block, mask) for block, mask in zip(others, (low, high, low | high))]


def sum_last(own, others):
    total = own
    for other in others:
        total = total + other.astype(f32)
    return total


VMEM_BYTES = 56 << 20
TILE = 512
EARLY = TILE


def norm_parts(values):
    average = jnp.mean(values, axis=-1, keepdims=True)
    centred = values - average
    variance = jnp.mean(centred * centred, axis=-1, keepdims=True)
    scale = lax.rsqrt(variance + norm_eps)
    return centred * scale, scale


def norm_back(unit, scale, gain, grad):
    inner = grad * gain
    shift = jnp.mean(inner, axis=-1, keepdims=True)
    along = jnp.mean(inner * unit, axis=-1, keepdims=True)
    return scale * (inner - shift - unit * along)


def mul(lhs, rhs):
    return jnp.dot(lhs, rhs, preferred_element_type=f32)


def mul_bt(lhs, rhs):
    return lax.dot_general(lhs, rhs, (((1,), (1,)), ((), ())), preferred_element_type=f32)


def mul_at(lhs, rhs):
    return lax.dot_general(lhs, rhs, (((0,), (0,)), ((), ())), preferred_element_type=f32)


def params(limit=VMEM_BYTES):
    return pltpu.CompilerParams(vmem_limit_bytes=limit)


def in_vmem(count):
    return [pl.BlockSpec(memory_space=pltpu.VMEM)] * count


def in_hbm(*arrays):
    return [pltpu.with_memory_space_constraint(array, pltpu.HBM) for array in arrays]


def stays(shape, dtype):
    return pltpu.VMEM(shape, dtype)


def cost(flops, moved, transcendentals=0):
    return pl.CostEstimate(flops=flops, bytes_accessed=moved, transcendentals=transcendentals)


def lane_halves(dtype):
    lane = lax.broadcasted_iota(jnp.int32, (1, 2 * HEAD), 1)
    low = jnp.where(lane < HEAD, 1.0, 0.0)
    return low.astype(dtype), (1.0 - low).astype(dtype)


def two_heads(pair):
    low, high = lane_halves(bf16)
    return jnp.concatenate([pair * low, pair * high], axis=0)


def same_sequence(rows, row0, cols, col0, seq_len):
    row = (lax.broadcasted_iota(jnp.int32, (rows, cols), 0) + row0) // seq_len
    col = (lax.broadcasted_iota(jnp.int32, (rows, cols), 1) + col0) // seq_len
    return row == col


def softmax_down(scores, mask):
    keys = mask.shape[0]
    parts, sums = [], []
    for k in range(2):
        part = jnp.where(mask, scores[k * keys : (k + 1) * keys], -1e30)
        most = jnp.max(part, axis=0, keepdims=True)
        raised = jnp.exp(part - most)
        total = jnp.sum(raised, axis=0, keepdims=True)
        parts.append(raised * (1.0 / total))
        sums.append(most + jnp.log(total))
    return parts, sums


def fold_kernel(extra, keep_a, got_a, keep_b, got_b, *refs):
    outs = refs[-5:] if extra else refs[-4:]
    rows, half, tile = keep_a.shape[0], keep_a.shape[0] // 2, 256

    @pl.loop(0, keep_a.shape[1] // tile)
    def _(step):
        cols = pl.ds(pl.multiple_of(step * tile, tile), tile)
        for k, (kept, got) in enumerate(((keep_a, got_a), (keep_b, got_b))):
            for j in range(2):
                at = slice(j * half, (j + 1) * half)
                total = kept[at, cols].astype(f32) + got[at, cols].astype(f32)
                outs[2 * k + j][:half, cols] = total.astype(bf16)

    if extra:
        came = refs[1][...] if extra > 1 else got_a[rows : rows + 16, :].astype(f32)[:8]
        sums = refs[0][...] + came
        outs[4][...] = sums
        outs[1][half : half + 16, :] = jnp.concatenate([sums, sums], axis=0).astype(bf16)


def fold(parts, after=(), sums=()):
    rows, cols = parts[0].shape
    if rows % 32:
        whole = [
            (kept.astype(f32) + got.astype(f32)).astype(bf16)
            for kept, got in (parts[:2], parts[2:])
        ]
        return [part for one in whole for part in (one[: rows // 2], one[rows // 2 :])]
    half = (rows // 2, cols)
    shapes = [stays(half, bf16)] * 4
    if sums:
        shapes[1] = stays((rows // 2 + 16, cols), bf16)
        shapes.append(stays((8, cols), f32))
    return pl.pallas_call(
        functools.partial(fold_kernel, len(sums)),
        out_shape=shapes,
        in_specs=in_vmem(4 + len(sums)) + anywhere(after),
        out_specs=in_vmem(len(shapes)),
        compiler_params=params(8 << 20),
        cost_estimate=cost(2 * rows * cols, 12 * rows * cols),
        name="fold",
    )(*parts, *sums, *after)


def fold_last_kernel(extra, keep_a, got_a, keep_b, got_b, *refs):
    outs = refs[-4:]
    cols = keep_a.shape[1]
    rows = keep_a.shape[0] // 4
    if extra:
        sums = refs[0][...] + got_a[4 * rows : 4 * rows + 16, :].astype(f32)[:8]
    for k, (kept, got) in enumerate(((keep_a, got_a), (keep_b, got_b))):
        total = kept[...].astype(f32) + got[: 4 * rows, :].astype(f32)
        at = slice(k * cols, (k + 1) * cols)
        for j, out in enumerate(outs):
            part = total[j * rows : (j + 1) * rows]
            if extra:
                row = jnp.broadcast_to(sums[k : k + 1], (8, cols))
                part = jnp.concatenate([part, row], axis=0)
            out[:, at] = part.astype(out.dtype)


def fold_last(parts, after=(), sums=()):
    rows, cols = parts[0].shape
    shape = (rows // 4 + (8 if sums else 0), 2 * cols)
    if rows % 32:
        pairs = (parts[:2], parts[2:])
        both = [kept.astype(f32) + got.astype(f32) for kept, got in pairs]
        own, *others = jnp.split(jnp.concatenate(both, axis=1), 4)
        return [own] + [other.astype(bf16) for other in others]
    return pl.pallas_call(
        functools.partial(fold_last_kernel, len(sums)),
        out_shape=[stays(shape, f32)] + [stays(shape, bf16)] * 3,
        in_specs=in_vmem(4 + len(sums)) + anywhere(after),
        out_specs=in_vmem(4),
        compiler_params=params(8 << 20),
        cost_estimate=cost(2 * rows * cols, 12 * rows * cols),
        name="fold_last",
    )(*parts, *sums, *after)


def anywhere(after):
    return [pl.BlockSpec(memory_space=pl.ANY)] * len(after)


def pair_cols(part, pair):
    start = part * D + pair * 2 * HEAD
    return slice(start, start + 2 * HEAD)


def line(ref):
    return ref[...].astype(f32).reshape(1, -1)


def norm_rows(src, dst, gain, bias, step_rows):
    @pl.loop(0, src.shape[0] // step_rows)
    def _(step):
        at = pl.ds(pl.multiple_of(step * step_rows, step_rows), step_rows)
        unit, _ = norm_parts(src[at, :].astype(f32))
        dst[at, :] = (unit * gain + bias).astype(bf16)


def attend_along(qkv_ref, att_ref, q_rows, k_rows, mask):
    low, high = lane_halves(f32)
    for pair in range(HEADS // 2):
        queries = two_heads(qkv_ref[q_rows, pair_cols(0, pair)] * bf16(HEAD ** (-0.5)))
        scores = mul_bt(queries, qkv_ref[k_rows, pair_cols(1, pair)])
        scores = jnp.where(mask, scores, -1e30)
        raised = jnp.exp(scores - jnp.max(scores, axis=-1, keepdims=True))
        probs = (raised * (1.0 / jnp.sum(raised, axis=-1, keepdims=True))).astype(bf16)
        half = probs.shape[0] // 2
        mixed = mul(probs, qkv_ref[k_rows, pair_cols(2, pair)])
        att_ref[q_rows, pair_cols(0, pair)] = (mixed[:half] * low + mixed[half:] * high).astype(bf16)


def attend(qkv_ref, att_ref, q_rows, k_rows, mask, keep_sums):
    for pair in range(HEADS // 2):
        queries = qkv_ref[q_rows, pair_cols(0, pair)] * bf16(HEAD ** (-0.5))
        scores = mul_bt(two_heads(qkv_ref[k_rows, pair_cols(1, pair)]), queries)
        probs, sums = softmax_down(scores, mask)
        vals = two_heads(qkv_ref[k_rows, pair_cols(2, pair)])
        mixed = mul_at(jnp.concatenate(probs, axis=0).astype(bf16), vals)
        att_ref[q_rows, pair_cols(0, pair)] = mixed.astype(bf16)
        for k in range(2):
            keep_sums(2 * pair + k, sums[k])


def text_front_kernel(
    x_ref, g1_ref, b1_ref, wqkv_ref, wo_ref, g2_ref, b2_ref, h1_ref, qkv_ref, att_ref, mid_ref,
    h2_ref, sum_ref, lse_ref
):
    rows, chunk = x_ref.shape[0], 128
    norm_rows(x_ref, h1_ref, line(g1_ref), line(b1_ref), chunk)

    @pl.loop(0, 3 * D // 256)
    def _(step):
        at = pl.ds(pl.multiple_of(step * 256, 256), 256)
        qkv_ref[:, at] = mul(h1_ref[...], wqkv_ref[:, at]).astype(bf16)

    mask = same_sequence(chunk, 0, chunk, 0, TXT_LEN)

    @pl.loop(0, rows // chunk)
    def _(step):
        at = pl.ds(pl.multiple_of(step * chunk, chunk), chunk)

        def keep_sums(head, value):
            lse_ref[pl.ds(step * 16 + head, 1), :] = value

        attend(qkv_ref, att_ref, at, at, mask, keep_sums)

    @pl.loop(0, D // 256)
    def _(step):
        at = pl.ds(pl.multiple_of(step * 256, 256), 256)
        mid_ref[:, at] = x_ref[:, at].astype(f32) + mul(att_ref[...], wo_ref[:, at])

    norm_rows(mid_ref, h2_ref, line(g2_ref), line(b2_ref), chunk)
    per = chunk // TXT_LEN

    @pl.loop(0, rows // chunk)
    def _(step):
        values = mid_ref[pl.ds(pl.multiple_of(step * chunk, chunk), chunk), :]
        sum_ref[pl.ds(pl.multiple_of(step * per, per), per), :] = jnp.sum(
            values.reshape(per, TXT_LEN, D), axis=1
        )


def text_front(rows_in, gain1, bias1, wqkv, wo, gain2, bias2):
    rows = rows_in.shape[0]
    shapes = [
        ((rows, D), bf16),
        ((rows, 3 * D), bf16),
        ((rows, D), bf16),
        ((rows, D), f32),
        ((rows, D), bf16),
        ((rows // TXT_LEN, D), f32),
        ((rows // 128 * 16, 128), f32),
    ]
    return pl.pallas_call(
        text_front_kernel,
        out_shape=[jax.ShapeDtypeStruct(*item) for item in shapes],
        compiler_params=params(),
        cost_estimate=cost(rows * D * D * 8, 14 * D * rows + 8 * D * D, rows * 128 * HEADS),
        name="text_front",
    )(rows_in, gain1, bias1, wqkv, wo, gain2, bias2)


def image_front_kernel(
    windows, x_ref, order_ref, g1_ref, b1_ref, g2_ref, b2_ref, *refs
):
    h2_ref, sum_ref, early_ref = refs[-10:-7]
    w_ref, h1_ref, placed_ref, qkv_ref, att_ref, mid_ref, sems = refs[-7:]
    rows, chunk = x_ref.shape[0], 80
    copies, row = [], 0
    for k, piece in enumerate(refs[:-10]):
        place = w_ref.at[pl.ds(row, piece.shape[0]), :]
        copies.append(pltpu.make_async_copy(piece, place, sems.at[k]))
        row += piece.shape[0]
    for copy in copies:
        copy.start()

    def place_columns(src, dst):
        @pl.loop(0, D // 256)
        def _(step):
            at = pl.ds(pl.multiple_of(step * 256, 256), 256)
            dst[:, at] = mul_bt(src[...], chosen(order_ref[at, :])).astype(bf16)

    norm_rows(x_ref, h1_ref, line(g1_ref), line(b1_ref), chunk)
    place_columns(h1_ref, placed_ref)
    for copy in copies:
        copy.wait()

    @pl.loop(0, 3 * D // 256)
    def _(step):
        at = pl.ds(pl.multiple_of(step * 256, 256), 256)
        qkv_ref[:, at] = mul(placed_ref[...], w_ref[:, at]).astype(bf16)

    for row0, count, key0, keys in windows:
        one = same_sequence(count, row0, keys, key0, IMG_LEN)
        mask = jnp.concatenate([one, one], axis=0)
        attend_along(qkv_ref, att_ref, pl.ds(row0, count), pl.ds(key0, keys), mask)
    place_columns(att_ref, placed_ref)

    @pl.loop(0, D // 256)
    def _(step):
        at = pl.ds(pl.multiple_of(step * 256, 256), 256)
        there = pl.ds(pl.multiple_of(step * 256 + 3 * D, 256), 256)
        mid_ref[:, at] = x_ref[:, at].astype(f32) + mul(placed_ref[...], w_ref[:, there])

    norm_rows(mid_ref, h2_ref, line(g2_ref), line(b2_ref), chunk)
    place_columns(h2_ref, placed_ref)
    pool = pool_matrix(rows // IMG_LEN, rows, 0, IMG_LEN)

    @pl.loop(0, EARLY // TILE)
    def _(step):
        at = pl.ds(pl.multiple_of(step * TILE, TILE), TILE)
        there = pl.ds(pl.multiple_of(step * TILE + 4 * D, TILE), TILE)
        value, _ = gelu_parts(mul(placed_ref[...], w_ref[:, there]))
        early_ref[:, at] = mul(pool, value.astype(bf16))

    for k in range(rows // IMG_LEN):
        first, last = k * IMG_LEN, (k + 1) * IMG_LEN
        start, end = first // 8 * 8, -(-last // 8) * 8
        values = mid_ref[start:end, :]
        place = lax.broadcasted_iota(jnp.int32, values.shape, 0) + start
        inside = (place >= first) & (place < last)
        sum_ref[k : k + 1, :] = jnp.sum(jnp.where(inside, values, 0.0), axis=0, keepdims=True)


def image_front(rows_in, pieces, source, gain1, bias1, gain2, bias2):
    rows = rows_in.shape[0]
    windows = ((0, 208, 0, 256), (208, 192, 192, 208))
    vmem = pl.BlockSpec(memory_space=pltpu.VMEM)
    return pl.pallas_call(
        functools.partial(image_front_kernel, windows),
        out_shape=[
            jax.ShapeDtypeStruct((rows, D), bf16),
            jax.ShapeDtypeStruct((rows // IMG_LEN, D), f32),
            jax.ShapeDtypeStruct((rows // IMG_LEN, EARLY), f32),
        ],
        in_specs=[vmem] * 6 + anywhere(pieces),
        out_specs=[vmem] * 3,
        scratch_shapes=[
            pltpu.VMEM((D, 4 * D + EARLY), bf16),
            pltpu.VMEM((rows, D), bf16),
            pltpu.VMEM((rows, D), bf16),
            pltpu.VMEM((rows, 3 * D), bf16),
            pltpu.VMEM((rows, D), bf16),
            pltpu.VMEM((rows, D), f32),
            pltpu.SemaphoreType.DMA((len(pieces),)),
        ],
        compiler_params=params(),
        cost_estimate=cost(rows * D * D * 12, 8 * D * D, rows * 256 * HEADS),
        name="image_front",
    )(rows_in, source, gain1, bias1, gain2, bias2, *pieces)


def gelu_parts(inner):
    half = 0.5 * (1.0 + lax.erf(inner * (0.5**0.5)))
    return inner * half, half


def pack_kernel(unit_ref, pos_ref, *refs):
    refs[-1][:, :D] = unit_ref[...].astype(bf16)
    refs[-1][:, D:] = pos_ref[...]


def packed(unit, positive, after):
    shape = (unit.shape[0], D + positive.shape[1])
    return pl.pallas_call(
        pack_kernel,
        out_shape=jax.ShapeDtypeStruct(shape, bf16),
        in_specs=[pl.BlockSpec(memory_space=pltpu.VMEM)] * 2 + anywhere(after),
        compiler_params=params(),
        cost_estimate=cost(shape[0] * shape[1], 4 * shape[0] * shape[1]),
        name="packed",
    )(unit, positive, *after)


def pool_matrix(count, rows, row0, seq_len):
    row = (lax.broadcasted_iota(jnp.int32, (count, rows), 1) + row0) // seq_len
    return jnp.where(row == lax.broadcasted_iota(jnp.int32, (count, rows), 0), 1.0, 0.0).astype(bf16)


def two_terms(mean):
    high = mean.astype(bf16)
    low = (mean - high.astype(f32)).astype(bf16)
    return jnp.concatenate([high, low], axis=0)


def unit_rows(pooled):
    inverse = lax.rsqrt(jnp.sum(pooled * pooled, axis=-1, keepdims=True) + norm_eps)
    return pooled * inverse, inverse


def text_up_kernel(h2_ref, wu_ref, wd_ref, sum_ref, *refs):
    slope_ref, hid_ref, unit_ref, inv_ref, acc = refs[-5:]
    step = pl.program_id(0)
    chunk = 320
    per = chunk // TXT_LEN
    pool = pool_matrix(per, chunk, 0, TXT_LEN)
    for k in range(h2_ref.shape[0] // chunk):
        inner = mul(h2_ref[k * chunk : (k + 1) * chunk, :], wu_ref[...])
        value, half = gelu_parts(inner)
        slope = half + inner * (jnp.exp(-0.5 * inner * inner) * 0.3989422804014327)
        slope_ref[k * chunk : (k + 1) * chunk, :] = slope.astype(bf16)
        hid_ref[k * per : (k + 1) * per, :] = mul(pool, value.astype(bf16))
    terms = mul(two_terms(hid_ref[...] * (1.0 / TXT_LEN)), wd_ref[...])
    count = hid_ref.shape[0]
    added = terms[:count] + terms[count:]

    @pl.when(step == 0)
    def _():
        acc[...] = sum_ref[...] * (1.0 / TXT_LEN) + added

    @pl.when(step > 0)
    def _():
        acc[...] += added

    @pl.when(step == pl.num_programs(0) - 1)
    def _():
        unit, inverse = unit_rows(acc[...])
        unit_ref[...] = unit
        inv_ref[...] = jnp.broadcast_to(inverse, inv_ref.shape)


def text_up(normed2, weight_up, weight_down, middle_sum, after=()):
    rows, count = normed2.shape[0], middle_sum.shape[0]
    fixed = lambda shape: pl.BlockSpec(shape, lambda i: (0, 0))
    return pl.pallas_call(
        text_up_kernel,
        grid=(FF // TILE,),
        out_shape=[
            jax.ShapeDtypeStruct((rows, FF), bf16),
            jax.ShapeDtypeStruct((count, FF), f32),
            jax.ShapeDtypeStruct((count, D), f32),
            jax.ShapeDtypeStruct((count, 128), f32),
        ],
        in_specs=[
            fixed((rows, D)),
            pl.BlockSpec((D, TILE), lambda i: (0, i)),
            pl.BlockSpec((TILE, D), lambda i: (i, 0)),
            fixed((count, D)),
        ]
        + anywhere(after),
        out_specs=[
            pl.BlockSpec((rows, TILE), lambda i: (0, i)),
            pl.BlockSpec((count, TILE), lambda i: (0, i)),
            fixed((count, D)),
            fixed((count, 128)),
        ],
        scratch_shapes=[pltpu.VMEM((count, D), f32)],
        compiler_params=params(),
        cost_estimate=cost(2 * rows * D * FF, 4 * D * FF + 2 * rows * FF, 20 * rows * FF),
        name="text_up",
    )(normed2, weight_up, weight_down, middle_sum, *after)


def image_up_kernel(fold, h2_ref, wu_ref, wd_ref, first_ref, sum_ref, early_ref, out_ref, acc, picked):
    step = pl.program_id(0)
    rows, count = h2_ref.shape[0], sum_ref.shape[0]
    part = TILE // fold

    def through_down(summed, groups):
        moved = mul(two_terms(summed * (1.0 / IMG_LEN)), picked[...]).astype(bf16)
        weight = jnp.concatenate([groups[:, k * D : (k + 1) * D] for k in range(fold)], axis=0)
        terms = mul(moved, weight)
        return terms[:count] + terms[count:]

    @pl.when(step == 0)
    def _():
        place = lax.broadcasted_iota(jnp.int32, (TILE, TILE), 0)
        col = lax.broadcasted_iota(jnp.int32, (TILE, TILE), 1)
        source = (col % part) * fold + col // part
        picked[...] = jnp.where(place == source, 1.0, 0.0).astype(bf16)
        total = sum_ref[...] * (1.0 / IMG_LEN)
        for k in range(EARLY // TILE):
            total = total + through_down(
                early_ref[:, k * TILE : (k + 1) * TILE], first_ref[k * part : (k + 1) * part, :]
            )
        acc[...] = total

    value, _ = gelu_parts(mul(h2_ref[...], wu_ref[...]))
    summed = mul(pool_matrix(count, rows, 0, IMG_LEN), value.astype(bf16))
    acc[...] += through_down(summed, wd_ref[...])

    @pl.when(step == pl.num_programs(0) - 1)
    def _():
        out_ref[...] = unit_rows(acc[...])[0].astype(bf16)


def image_up(normed2, whole, middle_sum, early):
    rows, count = normed2.shape[0], middle_sum.shape[0]
    fold = FF // D
    before, part = EARLY // TILE, TILE // fold
    fixed = lambda shape: pl.BlockSpec(shape, lambda i: (0, 0))
    return pl.pallas_call(
        functools.partial(image_up_kernel, fold),
        grid=(FF // TILE - before,),
        out_shape=jax.ShapeDtypeStruct((count, D), bf16),
        in_specs=[
            fixed((rows, D)),
            pl.BlockSpec((D, TILE), lambda i: (0, FF // TILE + i)),
            pl.BlockSpec((part, FF), lambda i: (i + before, 0)),
            fixed((before * part, FF)),
            fixed((count, D)),
            fixed((count, EARLY)),
        ],
        out_specs=fixed((count, D)),
        scratch_shapes=[pltpu.VMEM((count, D), f32), pltpu.VMEM((TILE, TILE), bf16)],
        compiler_params=params(),
        cost_estimate=cost(2 * rows * D * FF, 4 * D * FF, 15 * rows * FF),
        name="image_up",
    )(normed2, whole, whole, whole, middle_sum, early)


def left_kernel(count, *refs):
    out_ref = refs[-1]
    for k in range(count):
        source_ref, values_ref = refs[2 * k : 2 * k + 2]

        @pl.loop(0, D // 256)
        def _(step, k=k, source_ref=source_ref, values_ref=values_ref):
            at = pl.ds(pl.multiple_of(step * 256, 256), 256)
            picked = mul_bt(chosen(source_ref[at, :]), values_ref[...])
            out_ref[k, at, :] = picked.astype(bf16)


def left_factors(*pairs):
    rows = pairs[0][1].shape[0]
    given = [item for pair in pairs for item in pair]
    return pl.pallas_call(
        functools.partial(left_kernel, len(pairs)),
        out_shape=jax.ShapeDtypeStruct((len(pairs), D, rows), bf16),
        in_specs=in_vmem(len(given)),
        out_specs=pl.BlockSpec(memory_space=pltpu.VMEM),
        compiler_params=params(24 << 20),
        cost_estimate=cost(2 * len(pairs) * rows * D * D, 4 * len(pairs) * rows * D),
        name="left_factors",
    )(*given)


def loss_parts(text_rows, pos, image_all):
    similar = mul_bt(text_rows, image_all) * logit_scale
    shifted = jnp.exp(similar - logit_scale)
    alive = jnp.max(pos, axis=1, keepdims=True)
    row_sum = jnp.sum(shifted, axis=1, keepdims=True)
    row_count = jnp.maximum(jnp.sum(pos, axis=1, keepdims=True), 1.0)
    return similar, shifted, alive, row_sum, row_count


def sums_over_captions(text_rows, pos, image_all):
    similar, shifted, alive, row_sum, row_count = loss_parts(text_rows, pos, image_all)
    pos_similar = pos * similar
    cap_term = alive * (
        logit_scale + jnp.log(row_sum) - jnp.sum(pos_similar, axis=1, keepdims=True) / row_count
    )
    return (
        jnp.sum(alive * shifted, axis=0, keepdims=True),
        jnp.sum(pos, axis=0, keepdims=True),
        jnp.sum(pos_similar, axis=0, keepdims=True),
        jnp.sum(cap_term, axis=0, keepdims=True),
        jnp.sum(alive, axis=0, keepdims=True),
    )


def loss_from(sums):
    col_sum, col_count, col_pos, cap_total, live_total = sums
    img_term = logit_scale + jnp.log(col_sum) - col_pos / col_count
    return 0.5 * cap_total / live_total + 0.5 * jnp.mean(img_term, axis=1, keepdims=True)


def grad_of_unit(text_rows, pos, image_all, col_sum, col_count, live_total):
    _, shifted, alive, row_sum, row_count = loss_parts(text_rows, pos, image_all)
    cap_share, img_share = 0.5 / live_total, 0.5 / image_all.shape[0]
    grad_sims = alive * shifted * (cap_share / row_sum + img_share / col_sum) - pos * (
        cap_share / row_count + img_share / col_count
    )
    return mul(grad_sims.astype(bf16), image_all) * logit_scale


def turned(grad, unit):
    return grad - unit * jnp.sum(grad * unit, axis=-1, keepdims=True)


def loss_kernel(
    pack_ref, image_ref, own_ref, unit_ref, inv_ref, loss_ref, row_ref, low_ref, col_sum_ref,
    col_count_ref, live_ref
):
    image_all = image_ref[...]
    chunk = 256
    total = None
    for k in range(pack_ref.shape[0] // chunk):
        at = slice(k * chunk, (k + 1) * chunk)
        part = sums_over_captions(pack_ref[at, :D], pack_ref[at, D:].astype(f32), image_all)
        total = part if total is None else [a + b for a, b in zip(total, part)]
    loss_ref[...] = jnp.broadcast_to(loss_from(total), loss_ref.shape)
    col_sum, col_count, _, _, live_total = total
    col_sum_ref[...] = col_sum
    col_count_ref[...] = col_count
    live_ref[...] = jnp.broadcast_to(live_total, live_ref.shape)
    grad = grad_of_unit(
        own_ref[:, :D], own_ref[:, D:].astype(f32), image_all, col_sum, col_count, live_total
    )
    row = inv_ref[:, :1] * turned(grad, unit_ref[...]) * (1.0 / TXT_LEN)
    row_ref[...] = row
    low_ref[...] = row.astype(bf16)


def loss_and_rows(pack, image_all, own_pack, unit, inverse):
    images, count = image_all.shape[0], own_pack.shape[0]
    shapes = [(1, 128), (count, D), (count, D), (1, images), (1, images), (1, 128)]
    kinds = [f32, f32, bf16, f32, f32, f32]
    return pl.pallas_call(
        loss_kernel,
        out_shape=[jax.ShapeDtypeStruct(*item) for item in zip(shapes, kinds)],
        in_specs=in_vmem(5),
        out_specs=in_vmem(len(shapes)),
        compiler_params=params(16 << 20),
        cost_estimate=cost(2 * pack.shape[0] * images * D, 2 * pack.size, pack.shape[0] * images),
        name="loss_and_rows",
    )(pack, image_all, own_pack, unit, inverse)


def down_kernel(pack_ref, image_ref, col_sum_ref, col_count_ref, live_ref, hid_ref, *refs):
    step, out_ref = pl.program_id(0), refs[-1]
    text_rows = pack_ref[:, :D]
    grad = grad_of_unit(
        text_rows, pack_ref[:, D:].astype(f32), image_ref[...], col_sum_ref[...],
        col_count_ref[...], live_ref[:, :1]
    )
    rows = (turned(grad, text_rows.astype(f32)) * (1.0 / TXT_LEN)).astype(bf16)
    part = mul_at(hid_ref[...], rows)

    @pl.when(step == 0)
    def _():
        out_ref[...] = part

    @pl.when(step > 0)
    def _():
        out_ref[...] += part


def grad_of_down(pack, image_all, col_sum, col_count, live_total, hidden_cols, after):
    images, chunk = image_all.shape[0], 256
    fixed = lambda shape: pl.BlockSpec(shape, lambda i: (0, 0))
    per = hidden_cols.shape[1]
    return pl.pallas_call(
        down_kernel,
        grid=(pack.shape[0] // chunk,),
        out_shape=jax.ShapeDtypeStruct((per, D), f32),
        in_specs=[
            pl.BlockSpec((chunk, pack.shape[1]), lambda i: (i, 0)),
            fixed((images, D)), fixed((1, images)), fixed((1, images)), fixed((1, 128)),
            pl.BlockSpec((chunk, per), lambda i: (i, 0)),
        ]
        + anywhere(after),
        out_specs=fixed((per, D)),
        compiler_params=params(16 << 20),
        cost_estimate=cost(4 * pack.shape[0] * images * D, 2 * pack.size, pack.shape[0] * images),
        name="grad_of_down",
    )(pack, image_all, col_sum, col_count, live_total, hidden_cols, *after)


def mlp_back_kernel(
    low_ref, gain_ref, row_ref, wd_hbm, slope_hbm, wu_hbm, lhs_hbm, mid_hbm, keep_a, send_a, keep_b,
    send_b, out_ref, sums_out, wd_ref, slope_ref, wu_ref, lhs_ref, mid_ref, sems, whole_sems
):
    count, rows = low_ref.shape[0], out_ref.shape[0]
    half, steps = D // 2, FF // 2 // TILE

    def copies(tile, slot):
        at = pl.ds(pl.multiple_of(tile * TILE, TILE), TILE)
        return (
            pltpu.make_async_copy(wd_hbm.at[at, :], wd_ref.at[slot], sems.at[0, slot]),
            pltpu.make_async_copy(slope_hbm.at[:, at], slope_ref.at[slot], sems.at[1, slot]),
            pltpu.make_async_copy(wu_hbm.at[:, at], wu_ref.at[slot], sems.at[2, slot]),
        )

    lhs_copy = pltpu.make_async_copy(lhs_hbm, lhs_ref, whole_sems.at[0])
    mid_copy = pltpu.make_async_copy(mid_hbm, mid_ref, whole_sems.at[1])
    for copy in copies(0, 0):
        copy.start()
    lhs_copy.start()
    for k, (keep, send) in enumerate(((keep_a, send_a), (keep_b, send_b))):

        @pl.loop(0, steps)
        def _(step, k=k, keep=keep, send=send):
            tile = k * steps + step
            slot = lax.rem(tile, 2)

            @pl.when(tile + 1 < 2 * steps)
            def _():
                for copy in copies(tile + 1, 1 - slot):
                    copy.start()

            for copy in copies(tile, slot):
                copy.wait()
            if k == 0:

                @pl.when(step == 0)
                def _():
                    lhs_copy.wait()
                    mid_copy.start()

            there = pl.ds(pl.multiple_of(step * TILE, TILE), TILE)
            hidden = mul_bt(low_ref[...], wd_ref[slot])
            wide = jnp.broadcast_to(hidden[:, None, :], (count, TXT_LEN, TILE))
            inner = (wide.reshape(rows, TILE) * slope_ref[slot].astype(f32)).astype(bf16)
            weight = mul(lhs_ref[k], inner).astype(bf16)
            keep[:, there] = weight[:half]
            send[:, there] = weight[half:]
            added = mul_bt(inner, wu_ref[slot])
            if k == 0:

                @pl.when(step == 0)
                def _():
                    out_ref[...] = added

                @pl.when(step > 0)
                def _():
                    out_ref[...] += added
            else:
                out_ref[...] += added

    chunk = 128
    per = chunk // TXT_LEN
    gain = line(gain_ref)
    sums_out[...] = jnp.zeros_like(sums_out)
    mid_copy.wait()

    @pl.loop(0, rows // chunk)
    def _(k):
        at = pl.ds(pl.multiple_of(k * chunk, chunk), chunk)
        unit, scale = norm_parts(mid_ref[at, :])
        grad = out_ref[at, :]
        sums_out[:, :D] += jnp.sum(grad * unit, axis=0, keepdims=True)
        sums_out[:, D:] += jnp.sum(grad, axis=0, keepdims=True)
        row = row_ref[pl.ds(pl.multiple_of(k * per, per), per), :]
        row = jnp.broadcast_to(row[:, None, :], (per, TXT_LEN, D)).reshape(chunk, D)
        out_ref[at, :] = row + norm_back(unit, scale, gain, grad)


def mlp_back(grad_row, grad_low, weight_down, slope, weight_up, lhs, middle, gain):
    rows = slope.shape[0]
    return pl.pallas_call(
        mlp_back_kernel,
        out_shape=[stays((D // 2, FF // 2), bf16)] * 4
        + [stays((rows, D), f32), stays((1, 2 * D), f32)],
        in_specs=in_vmem(3) + [pl.BlockSpec(memory_space=pltpu.HBM)] * 5,
        out_specs=in_vmem(6),
        scratch_shapes=[
            pltpu.VMEM((2, TILE, D), bf16),
            pltpu.VMEM((2, rows, TILE), bf16),
            pltpu.VMEM((2, D, TILE), bf16),
            pltpu.VMEM((2, D, rows), bf16),
            pltpu.VMEM((rows, D), f32),
            pltpu.SemaphoreType.DMA((3, 2)),
            pltpu.SemaphoreType.DMA((2,)),
        ],
        compiler_params=params(28 << 20),
        cost_estimate=cost(4 * rows * D * FF, 4 * D * FF + 2 * rows * FF + 2 * D * FF, rows * FF),
        name="mlp_back",
    )(grad_low, gain, grad_row, *in_hbm(weight_down, slope, weight_up, lhs, middle))


def attention_back_kernel(first, grad_ref, wo_ref, qkv_ref, lse_ref, *refs):
    low_ref, out_ref = refs[-2:]
    chunk = 128
    mask = same_sequence(chunk, 0, chunk, 0, TXT_LEN)

    @pl.loop(0, low_ref.shape[0] // chunk)
    def _(step):
        here = pl.ds(pl.multiple_of((first + step) * chunk, chunk), chunk)
        there = pl.ds(pl.multiple_of(step * chunk, chunk), chunk)
        sums = lse_ref[pl.ds(pl.multiple_of((first + step) * 16, 16), 16), :]
        low = grad_ref[here, :].astype(bf16)
        low_ref[there, :] = low
        grad_att = mul_bt(low, wo_ref[...]).astype(bf16)
        for pair in range(HEADS // 2):
            queries = qkv_ref[here, pair_cols(0, pair)] * bf16(HEAD ** (-0.5))
            keys = two_heads(qkv_ref[here, pair_cols(1, pair)])
            vals = two_heads(qkv_ref[here, pair_cols(2, pair)])
            grads = grad_att[:, pair_cols(0, pair)]
            scores, grad_probs = mul_bt(keys, queries), mul_bt(vals, grads)
            probs, grad_scores = [], []
            for k in range(2):
                at = slice(k * chunk, (k + 1) * chunk)
                head = 2 * pair + k
                shifted = scores[at] - sums[head : head + 1, :]
                prob = jnp.where(mask, jnp.exp(jnp.where(mask, shifted, 0.0)), 0.0)
                along = jnp.sum(grad_probs[at] * prob, axis=0, keepdims=True)
                grad_scores.append((prob * (grad_probs[at] - along)).astype(bf16))
                probs.append(prob.astype(bf16))
            grad_q = mul_at(jnp.concatenate(grad_scores, axis=0), keys) * HEAD ** (-0.5)
            grad_k = mul(jnp.concatenate(grad_scores, axis=1), two_heads(queries))
            grad_v = mul(jnp.concatenate(probs, axis=1), two_heads(grads))
            out_ref[there, pair_cols(0, pair)] = grad_q.astype(bf16)
            out_ref[there, pair_cols(1, pair)] = grad_k.astype(bf16)
            out_ref[there, pair_cols(2, pair)] = grad_v.astype(bf16)


def attention_back(grad_middle, weight_out, project, log_sums, first, count, after=()):
    rows = count * 128
    return pl.pallas_call(
        functools.partial(attention_back_kernel, first),
        out_shape=[stays((rows, D), bf16), stays((rows, 3 * D), bf16)],
        in_specs=in_vmem(4) + anywhere(after),
        out_specs=in_vmem(2),
        compiler_params=params(16 << 20),
        cost_estimate=cost(10 * rows * D * D, 16 * rows * D + 2 * D * D, rows * 128 * HEADS),
        name="attention_back",
    )(grad_middle, weight_out, project, log_sums, *after)


def mul_rows(lhs, parts, cols):
    total, row = 0.0, 0
    for part in parts:
        total = total + mul(lhs[:, row : row + part.shape[0]], part[:, cols])
        row += part.shape[0]
    return total


def weight_back_kernel(factors, groups, lhs_ref, *refs):
    keep_a, send_a, keep_b, send_b = refs[-4:]
    half = D // 2
    for k, (factor, group, col) in enumerate(factors):
        parts = refs[sum(groups[:group]) : sum(groups[: group + 1])]
        weight = mul_rows(lhs_ref.at[factor], parts, slice(col * D, (col + 1) * D)).astype(bf16)
        at = slice(k % 2 * D, (k % 2 + 1) * D)
        (keep_b if k > 1 else keep_a)[:, at] = weight[:half]
        (send_b if k > 1 else send_a)[:, at] = weight[half:]


def weight_back(lhs, groups, factors, after=()):
    rows = lhs.shape[2]
    given = [part for group in groups for part in group]
    return pl.pallas_call(
        functools.partial(weight_back_kernel, factors, [len(group) for group in groups]),
        out_shape=[stays((D // 2, 2 * D), bf16)] * 4,
        in_specs=in_vmem(1 + len(given)) + anywhere(after),
        out_specs=in_vmem(4),
        compiler_params=params(16 << 20),
        cost_estimate=cost(8 * rows * D * D, 8 * rows * D + 14 * D * D),
        name="weight_back",
    )(lhs, *given, *after)


def input_back_kernel(count, *refs):
    projs = refs[:count]
    w_ref, x_ref, gain_ref, mid_ref, sums_ref = refs[count : count + 5]
    out_ref, sums_out = refs[-2:]
    rows, chunk = x_ref.shape[0], 128

    @pl.loop(0, D // 256)
    def _(step):
        at = pl.ds(pl.multiple_of(step * 256, 256), 256)
        row = 0
        for part in projs:
            there = slice(row, row + part.shape[0])
            out_ref[there, at] = mul_bt(part[...], w_ref[at, :])
            row += part.shape[0]

    gain = line(gain_ref)
    sums_out[...] = jnp.zeros_like(sums_out)
    sums_out[1:2, :] = sums_ref[...]

    @pl.loop(0, rows // chunk)
    def _(k):
        at = pl.ds(pl.multiple_of(k * chunk, chunk), chunk)
        unit, scale = norm_parts(x_ref[at, :].astype(f32))
        grad = out_ref[at, :]
        sums_out[0:1, :D] += jnp.sum(grad * unit, axis=0, keepdims=True)
        sums_out[0:1, D:] += jnp.sum(grad, axis=0, keepdims=True)
        out_ref[at, :] = mid_ref[at, :] + norm_back(unit, scale, gain, grad)


def input_back(grad_projs, weight, rows_in, gain, grad_middle, sums, after=()):
    rows = rows_in.shape[0]
    return pl.pallas_call(
        functools.partial(input_back_kernel, len(grad_projs)),
        out_shape=[jax.ShapeDtypeStruct((rows, D), f32), stays((8, 2 * D), f32)],
        in_specs=in_vmem(len(grad_projs) + 5) + anywhere(after),
        out_specs=in_vmem(2),
        compiler_params=params(16 << 20),
        cost_estimate=cost(6 * rows * D * D, 14 * rows * D + 6 * D * D),
        name="input_back",
    )(*grad_projs, weight, rows_in, gain, grad_middle, sums, *after)


def local(
    images,
    captions,
    img_gain1,
    img_bias1,
    img_qkv,
    img_out,
    img_gain2,
    img_bias2,
    img_up,
    img_down,
    txt_gain1,
    txt_bias1,
    txt_qkv,
    txt_out,
    txt_gain2,
    txt_bias2,
    txt_up,
    txt_down,
    counts,
    matches,
):
    peers = lax.axis_size(AXIS)
    own = lax.axis_index(AXIS)
    per = D // peers
    img_local = counts.shape[0]
    cap_local = matches.shape[0]
    total_images = matches.shape[1]

    up_rows = img_up.reshape(per, FF)
    whole = lax.all_gather(
        jnp.concatenate([img_down.reshape(per, FF), up_rows[:, EARLY:]], axis=1),
        AXIS,
        axis=0,
        tiled=True,
    )
    small = peers == 32
    shard = jnp.concatenate(
        [img_qkv.reshape(per, 3 * D), img_out.reshape(per, D), up_rows[:, :EARLY]], axis=1
    )
    if small:
        line, source = gathered_line(shard), row_order((1, 4, 2, 16, 8))
    else:
        line, source = lax.all_gather(shard, AXIS, axis=0, tiled=True), row_order(())

    normed1, project, attended, middle, normed2, middle_sum, log_sums = text_front(
        captions, txt_gain1, txt_bias1, txt_qkv, txt_out, txt_gain2, txt_bias2
    )
    middle_sum, line = in_turn(middle_sum, line)
    beside, above = (swapped(line, 2), swapped(line, 4)) if small else (line, line)
    slope, hidden_sum, text_unit, inverse = text_up(
        normed2, txt_up, txt_down, middle_sum, (line,)
    )
    text_unit, normed2, beside, above = lax.optimization_barrier(
        (text_unit, normed2, beside, above)
    )

    ends_at = jnp.cumsum(counts)
    slot_ids = lax.iota(jnp.int32, cap_local)
    owner = jnp.sum((ends_at[None, :] <= slot_ids[:, None]).astype(jnp.int32), axis=1)
    owner = owner + own * img_local
    live = slot_ids < ends_at[-1]
    columns = lax.iota(jnp.int32, total_images)
    positive = ((matches > 0) | (owner[:, None] == columns[None, :])) & live[:, None]

    order_a, order_b, tail = stage_orders()
    source_a, source_b = row_order(order_a + tail[::-1]), row_order(order_b + tail[::-1])
    own_pack = packed(text_unit, positive.astype(bf16), ())
    lhs_up = left_factors((source_a, normed2), (source_b, normed2))
    pieces = [line]
    if small:
        first, second = diagonal(beside, above)
        own_pack, first, second, lhs_up = lax.optimization_barrier(
            (own_pack, first, second, lhs_up)
        )
        held = own_pack[None]
        others = [swapped(held, mask) for mask in (8, 16, 24)]
        pieces = [line, beside, above, first, second]
        pieces = pieces + [swapped(piece, 1) for piece in pieces]

    normed_img, middle_img, early = image_front(
        images, pieces, source, img_gain1, img_bias1, img_gain2, img_bias2
    )
    if small:
        scaled_sum = (hidden_sum * inverse[:, :1]).astype(bf16)
        normed_img, scaled_sum, others = lax.optimization_barrier((normed_img, scaled_sum, others))
        held = joined(joined(held, others[0], 8), joined(others[1], others[2], 8), 16, 1)
        text_beside, text_above = swapped(held, 2), swapped(held, 4)
        hidden_cols = lax.all_to_all(scaled_sum, AXIS, split_axis=1, concat_axis=0, tiled=True)
        whole, text_beside, text_above = lax.optimization_barrier((whole, text_beside, text_above))
        halves = diagonal(text_beside, text_above)
    image_low = image_up(normed_img, whole, middle_img, early)
    if small:
        image_low, halves, hidden_cols = lax.optimization_barrier((image_low, halves, hidden_cols))
        across = jnp.concatenate(halves, axis=0)
        held = joined(joined(held, text_beside, 2), joined(text_above, across, 2), 4, 4)
        text_pack = joined(held, swapped(held, 1), 1).reshape(-1, D + total_images)
    image_all = spread(image_low).reshape(total_images, D)
    if small:
        image_all, text_pack = in_turn(image_all, text_pack)

    if small:
        loss_value, grad_row, row_low, col_sum, col_count, live_total = loss_and_rows(
            text_pack, image_all, own_pack, text_unit, inverse
        )
        loss_value = loss_value[0, 0]
    else:
        text_low, pos = own_pack[:, :D], own_pack[:, D:].astype(f32)
        sums = lax.psum(sums_over_captions(text_low, pos, image_all), AXIS)
        loss_value = loss_from(sums)[0, 0]
        grad = grad_of_unit(text_low, pos, image_all, sums[0], sums[1], sums[4])
        grad_row = inverse[:, :1] * turned(grad, text_unit) * (1.0 / TXT_LEN)
        row_low = grad_row.astype(bf16)

    *up, grad_middle, sums = mlp_back(
        grad_row, row_low, txt_down, slope, txt_up, lhs_up, middle, txt_gain2
    )
    stages = len(order_a)
    low_one, proj_one = attention_back(grad_middle, txt_out, project, log_sums, 0, 1)
    for stage in range(stages - 2):
        up = fold(hand_on(up, stage), (proj_one,))
    low_two, proj_two = attention_back(grad_middle, txt_out, project, log_sums, 1, 4, up)
    proj_two, normed1 = in_turn(proj_two, normed1)
    lhs_rest = left_factors((source_a, normed1), (source_b, normed1), (source_b, attended))
    up = fold(hand_on(up, stages - 2), (proj_two, lhs_rest))
    projs, lows = (proj_one, proj_two), (low_one, low_two)
    rest = weight_back(lhs_rest, [projs, lows], [(0, 0, 0), (0, 0, 1), (1, 0, 2), (2, 1, 0)], up)
    up = hand_on(up, stages - 1)
    caption_grad, sums = input_back(
        projs, txt_qkv, captions, txt_gain1, grad_middle, sums, rest[:1]
    )
    caption_grad, up = in_turn(caption_grad, up)
    up = fold_last(up)
    if small:
        *rest, sums = fold(hand_on(rest, 0), up[:1], (sums, swapped(sums, 1)))
    else:
        norms = lax.psum(sums, AXIS)[:2].reshape(-1)
        for stage in range(stages - 2):
            rest = fold(hand_on(rest, stage), up[:1])
    up = hand_on_last(up)
    rest = hand_on(rest, stages - 2)
    if small:
        grad_down = grad_of_down(
            text_pack, image_all, col_sum, col_count, live_total, hidden_cols, (caption_grad,)
        )
    else:
        grad_down = lax.psum_scatter(
            mul_at(hidden_sum.astype(bf16), row_low), AXIS, scatter_dimension=0, tiled=True
        )
    grad_down, rest, up = lax.optimization_barrier((grad_down, rest, up))
    if small:
        *rest, sums = fold(rest, (), (sums,))
        rest = fold_last(hand_on(rest, stages - 1), (), (sums,))
    else:
        rest = fold_last(hand_on(fold(rest), stages - 1))
    up_share = sum_last(*up)
    rest_share = sum_last(*hand_on_last(rest))
    if small:
        norms = rest_share[per]
        rest_share = rest_share[:per]
    return (
        loss_value,
        caption_grad,
        norms[:D],
        norms[D : 2 * D],
        rest_share[:, : 3 * D].reshape(-1),
        rest_share[:, 3 * D :].reshape(-1),
        norms[2 * D : 3 * D],
        norms[3 * D :],
        up_share.reshape(-1),
        grad_down.reshape(-1),
    )


def solution(mesh):
    split, flat, whole = P("blk", None), P("blk"), P()
    image_block = (whole, whole, flat, flat, whole, whole, flat, flat)
    return jax.shard_map(
        local,
        mesh=mesh,
        in_specs=(split, split) + image_block + (whole,) * 8 + (flat, split),
        out_specs=(whole, split, whole, whole, flat, flat, whole, whole, flat, flat),
        check_vma=False,
    )
```

```python
import functools

import jax
import jax.numpy as jnp
from jax import lax
from jax.experimental import pallas as pl
from jax.experimental.pallas import tpu as pltpu
from jax.sharding import PartitionSpec as P

D = 768
FF = 3072
HEAD = 64
HEADS = D // HEAD
IMG_LEN = 50
TXT_LEN = 16
AXIS = "blk"

norm_eps = 1e-06
logit_scale = 50.0
f32 = jnp.float32
bf16 = jnp.bfloat16


def swapped(value, mask):
    peers = lax.axis_size(AXIS)
    return lax.ppermute(value, AXIS, [(i, i ^ mask) for i in range(peers)])


def bit_masks():
    peers = lax.axis_size(AXIS)
    return [1 << k for k in range(peers.bit_length() - 1)]


def joined(held, other, mask, outer=None):
    upper = (lax.axis_index(AXIS) & mask) > 0
    first = jnp.where(upper, other, held)
    second = jnp.where(upper, held, other)
    outer = held.shape[0] if outer is None else outer
    parts = [part.reshape((outer, -1) + held.shape[1:]) for part in (first, second)]
    return jnp.stack(parts, axis=1).reshape((-1,) + held.shape[1:])


def exchanged(copies):
    return lax.all_to_all(copies, AXIS, split_axis=0, concat_axis=0, tiled=True)


def stage_orders():
    masks = bit_masks()
    head, tail = masks[:-2], masks[-2:]
    order_a = list(head)
    order_b = list(head)
    for k in range(1, len(head) - 1, 2):
        order_b[k], order_b[k + 1] = order_b[k + 1], order_b[k]
    return order_a, order_b, tail


def row_order(bits):
    peers = lax.axis_size(AXIS)
    own = lax.axis_index(AXIS)
    per = D // peers
    places = lax.broadcasted_iota(jnp.int32, (D, 1), 0)
    block = places // per
    target = jnp.zeros_like(block) + own
    for k, mask in enumerate(bits):
        target = target ^ (((block >> (len(bits) - 1 - k)) & 1) * mask)
    return target * per + places % per


def chosen(source):
    column = lax.broadcasted_iota(jnp.int32, (source.shape[0], D), 1)
    return jnp.where(column == source, 1.0, 0.0).astype(bf16)


def gathered_line(shard):
    return jnp.concatenate([shard] + [swapped(shard, mask) for mask in (8, 16, 24)], axis=0)


def diagonal(beside, above):
    half = beside.shape[0] // 2
    return swapped(beside[:half], 4), swapped(above[half:], 2)


def in_turn(first, then):
    return lax.optimization_barrier((first, then))


def hand_on(parts, stage):
    order_a, order_b, _ = stage_orders()
    keep_a, send_a, keep_b, send_b = parts
    return keep_a, swapped(send_a, order_a[stage]), keep_b, swapped(send_b, order_b[stage])


def hand_on_last(blocks):
    low, high = stage_orders()[2]
    own, *others = blocks
    return own, [swapped(block, mask) for block, mask in zip(others, (low, high, low | high))]


def sum_last(own, others):
    total = own
    for other in others:
        total = total + other.astype(f32)
    return total


VMEM_BYTES = 56 << 20
TILE = 512
EARLY = TILE


def norm_parts(values):
    average = jnp.mean(values, axis=-1, keepdims=True)
    centred = values - average
    variance = jnp.mean(centred * centred, axis=-1, keepdims=True)
    scale = lax.rsqrt(variance + norm_eps)
    return centred * scale, scale


def norm_back(unit, scale, gain, grad):
    inner = grad * gain
    shift = jnp.mean(inner, axis=-1, keepdims=True)
    along = jnp.mean(inner * unit, axis=-1, keepdims=True)
    return scale * (inner - shift - unit * along)


def mul(lhs, rhs):
    return jnp.dot(lhs, rhs, preferred_element_type=f32)


def mul_bt(lhs, rhs):
    return lax.dot_general(lhs, rhs, (((1,), (1,)), ((), ())), preferred_element_type=f32)


def mul_at(lhs, rhs):
    return lax.dot_general(lhs, rhs, (((0,), (0,)), ((), ())), preferred_element_type=f32)


def params(limit=VMEM_BYTES):
    return pltpu.CompilerParams(vmem_limit_bytes=limit)


def in_vmem(count):
    return [pl.BlockSpec(memory_space=pltpu.VMEM)] * count


def in_hbm(*arrays):
    return [pltpu.with_memory_space_constraint(array, pltpu.HBM) for array in arrays]


def stays(shape, dtype):
    return pltpu.VMEM(shape, dtype)


def cost(flops, moved, transcendentals=0):
    return pl.CostEstimate(flops=flops, bytes_accessed=moved, transcendentals=transcendentals)


def lane_halves(dtype):
    lane = lax.broadcasted_iota(jnp.int32, (1, 2 * HEAD), 1)
    low = jnp.where(lane < HEAD, 1.0, 0.0)
    return low.astype(dtype), (1.0 - low).astype(dtype)


def two_heads(pair):
    low, high = lane_halves(bf16)
    return jnp.concatenate([pair * low, pair * high], axis=0)


def same_sequence(rows, row0, cols, col0, seq_len):
    row = (lax.broadcasted_iota(jnp.int32, (rows, cols), 0) + row0) // seq_len
    col = (lax.broadcasted_iota(jnp.int32, (rows, cols), 1) + col0) // seq_len
    return row == col


def softmax_down(scores, mask):
    keys = mask.shape[0]
    parts, sums = [], []
    for k in range(2):
        part = jnp.where(mask, scores[k * keys : (k + 1) * keys], -1e30)
        most = jnp.max(part, axis=0, keepdims=True)
        raised = jnp.exp(part - most)
        total = jnp.sum(raised, axis=0, keepdims=True)
        parts.append(raised * (1.0 / total))
        sums.append(most + jnp.log(total))
    return parts, sums


def fold_kernel(extra, keep_a, got_a, keep_b, got_b, *refs):
    outs = refs[-5:] if extra else refs[-4:]
    rows, half, tile = keep_a.shape[0], keep_a.shape[0] // 2, 256

    @pl.loop(0, keep_a.shape[1] // tile)
    def _(step):
        cols = pl.ds(pl.multiple_of(step * tile, tile), tile)
        for k, (kept, got) in enumerate(((keep_a, got_a), (keep_b, got_b))):
            for j in range(2):
                at = slice(j * half, (j + 1) * half)
                total = kept[at, cols].astype(f32) + got[at, cols].astype(f32)
                outs[2 * k + j][:half, cols] = total.astype(bf16)

    if extra:
        came = refs[1][...] if extra > 1 else got_a[rows : rows + 16, :].astype(f32)[:8]
        sums = refs[0][...] + came
        outs[4][...] = sums
        outs[1][half : half + 16, :] = jnp.concatenate([sums, sums], axis=0).astype(bf16)


def fold(parts, after=(), sums=()):
    rows, cols = parts[0].shape
    if rows % 32:
        whole = [
            (kept.astype(f32) + got.astype(f32)).astype(bf16)
            for kept, got in (parts[:2], parts[2:])
        ]
        return [part for one in whole for part in (one[: rows // 2], one[rows // 2 :])]
    half = (rows // 2, cols)
    shapes = [stays(half, bf16)] * 4
    if sums:
        shapes[1] = stays((rows // 2 + 16, cols), bf16)
        shapes.append(stays((8, cols), f32))
    return pl.pallas_call(
        functools.partial(fold_kernel, len(sums)),
        out_shape=shapes,
        in_specs=in_vmem(4 + len(sums)) + anywhere(after),
        out_specs=in_vmem(len(shapes)),
        compiler_params=params(8 << 20),
        cost_estimate=cost(2 * rows * cols, 12 * rows * cols),
        name="fold",
    )(*parts, *sums, *after)


def fold_last_kernel(extra, keep_a, got_a, keep_b, got_b, *refs):
    outs = refs[-4:]
    cols = keep_a.shape[1]
    rows = keep_a.shape[0] // 4
    if extra:
        sums = refs[0][...] + got_a[4 * rows : 4 * rows + 16, :].astype(f32)[:8]
    for k, (kept, got) in enumerate(((keep_a, got_a), (keep_b, got_b))):
        total = kept[...].astype(f32) + got[: 4 * rows, :].astype(f32)
        at = slice(k * cols, (k + 1) * cols)
        for j, out in enumerate(outs):
            part = total[j * rows : (j + 1) * rows]
            if extra:
                row = jnp.broadcast_to(sums[k : k + 1], (8, cols))
                part = jnp.concatenate([part, row], axis=0)
            out[:, at] = part.astype(out.dtype)


def fold_last(parts, after=(), sums=()):
    rows, cols = parts[0].shape
    shape = (rows // 4 + (8 if sums else 0), 2 * cols)
    if rows % 32:
        pairs = (parts[:2], parts[2:])
        both = [kept.astype(f32) + got.astype(f32) for kept, got in pairs]
        own, *others = jnp.split(jnp.concatenate(both, axis=1), 4)
        return [own] + [other.astype(bf16) for other in others]
    return pl.pallas_call(
        functools.partial(fold_last_kernel, len(sums)),
        out_shape=[stays(shape, f32)] + [stays(shape, bf16)] * 3,
        in_specs=in_vmem(4 + len(sums)) + anywhere(after),
        out_specs=in_vmem(4),
        compiler_params=params(8 << 20),
        cost_estimate=cost(2 * rows * cols, 12 * rows * cols),
        name="fold_last",
    )(*parts, *sums, *after)


def anywhere(after):
    return [pl.BlockSpec(memory_space=pl.ANY)] * len(after)


def pair_cols(part, pair):
    start = part * D + pair * 2 * HEAD
    return slice(start, start + 2 * HEAD)


def line(ref):
    return ref[...].astype(f32).reshape(1, -1)


def norm_rows(src, dst, gain, bias, step_rows):
    @pl.loop(0, src.shape[0] // step_rows)
    def _(step):
        at = pl.ds(pl.multiple_of(step * step_rows, step_rows), step_rows)
        unit, _ = norm_parts(src[at, :].astype(f32))
        dst[at, :] = (unit * gain + bias).astype(bf16)


def attend_along(qkv_ref, att_ref, q_rows, k_rows, mask):
    low, high = lane_halves(f32)
    for pair in range(HEADS // 2):
        queries = two_heads(qkv_ref[q_rows, pair_cols(0, pair)] * bf16(HEAD ** (-0.5)))
        scores = mul_bt(queries, qkv_ref[k_rows, pair_cols(1, pair)])
        scores = jnp.where(mask, scores, -1e30)
        raised = jnp.exp(scores - jnp.max(scores, axis=-1, keepdims=True))
        probs = (raised * (1.0 / jnp.sum(raised, axis=-1, keepdims=True))).astype(bf16)
        half = probs.shape[0] // 2
        mixed = mul(probs, qkv_ref[k_rows, pair_cols(2, pair)])
        att_ref[q_rows, pair_cols(0, pair)] = (mixed[:half] * low + mixed[half:] * high).astype(bf16)


def attend(qkv_ref, att_ref, q_rows, k_rows, mask, keep_sums):
    for pair in range(HEADS // 2):
        queries = qkv_ref[q_rows, pair_cols(0, pair)] * bf16(HEAD ** (-0.5))
        scores = mul_bt(two_heads(qkv_ref[k_rows, pair_cols(1, pair)]), queries)
        probs, sums = softmax_down(scores, mask)
        vals = two_heads(qkv_ref[k_rows, pair_cols(2, pair)])
        mixed = mul_at(jnp.concatenate(probs, axis=0).astype(bf16), vals)
        att_ref[q_rows, pair_cols(0, pair)] = mixed.astype(bf16)
        for k in range(2):
            keep_sums(2 * pair + k, sums[k])


def text_front_kernel(
    x_ref, g1_ref, b1_ref, wqkv_ref, wo_ref, g2_ref, b2_ref, h1_ref, qkv_ref, att_ref, mid_ref,
    h2_ref, sum_ref, lse_ref
):
    rows, chunk = x_ref.shape[0], 128
    norm_rows(x_ref, h1_ref, line(g1_ref), line(b1_ref), chunk)

    @pl.loop(0, 3 * D // 256)
    def _(step):
        at = pl.ds(pl.multiple_of(step * 256, 256), 256)
        qkv_ref[:, at] = mul(h1_ref[...], wqkv_ref[:, at]).astype(bf16)

    mask = same_sequence(chunk, 0, chunk, 0, TXT_LEN)

    @pl.loop(0, rows // chunk)
    def _(step):
        at = pl.ds(pl.multiple_of(step * chunk, chunk), chunk)

        def keep_sums(head, value):
            lse_ref[pl.ds(step * 16 + head, 1), :] = value

        attend(qkv_ref, att_ref, at, at, mask, keep_sums)

    @pl.loop(0, D // 256)
    def _(step):
        at = pl.ds(pl.multiple_of(step * 256, 256), 256)
        mid_ref[:, at] = x_ref[:, at].astype(f32) + mul(att_ref[...], wo_ref[:, at])

    norm_rows(mid_ref, h2_ref, line(g2_ref), line(b2_ref), chunk)
    per = chunk // TXT_LEN

    @pl.loop(0, rows // chunk)
    def _(step):
        values = mid_ref[pl.ds(pl.multiple_of(step * chunk, chunk), chunk), :]
        sum_ref[pl.ds(pl.multiple_of(step * per, per), per), :] = jnp.sum(
            values.reshape(per, TXT_LEN, D), axis=1
        )


def text_front(rows_in, gain1, bias1, wqkv, wo, gain2, bias2):
    rows = rows_in.shape[0]
    shapes = [
        ((rows, D), bf16),
        ((rows, 3 * D), bf16),
        ((rows, D), bf16),
        ((rows, D), f32),
        ((rows, D), bf16),
        ((rows // TXT_LEN, D), f32),
        ((rows // 128 * 16, 128), f32),
    ]
    return pl.pallas_call(
        text_front_kernel,
        out_shape=[jax.ShapeDtypeStruct(*item) for item in shapes],
        compiler_params=params(),
        cost_estimate=cost(rows * D * D * 8, 14 * D * rows + 8 * D * D, rows * 128 * HEADS),
        name="text_front",
    )(rows_in, gain1, bias1, wqkv, wo, gain2, bias2)


def image_front_kernel(
    windows, x_ref, order_ref, g1_ref, b1_ref, g2_ref, b2_ref, *refs
):
    h2_ref, sum_ref, early_ref = refs[-10:-7]
    w_ref, h1_ref, placed_ref, qkv_ref, att_ref, mid_ref, sems = refs[-7:]
    rows, chunk = x_ref.shape[0], 80
    copies, row = [], 0
    for k, piece in enumerate(refs[:-10]):
        place = w_ref.at[pl.ds(row, piece.shape[0]), :]
        copies.append(pltpu.make_async_copy(piece, place, sems.at[k]))
        row += piece.shape[0]
    for copy in copies:
        copy.start()

    def place_columns(src, dst):
        @pl.loop(0, D // 256)
        def _(step):
            at = pl.ds(pl.multiple_of(step * 256, 256), 256)
            dst[:, at] = mul_bt(src[...], chosen(order_ref[at, :])).astype(bf16)

    norm_rows(x_ref, h1_ref, line(g1_ref), line(b1_ref), chunk)
    place_columns(h1_ref, placed_ref)
    for copy in copies:
        copy.wait()

    @pl.loop(0, 3 * D // 256)
    def _(step):
        at = pl.ds(pl.multiple_of(step * 256, 256), 256)
        qkv_ref[:, at] = mul(placed_ref[...], w_ref[:, at]).astype(bf16)

    for row0, count, key0, keys in windows:
        one = same_sequence(count, row0, keys, key0, IMG_LEN)
        mask = jnp.concatenate([one, one], axis=0)
        attend_along(qkv_ref, att_ref, pl.ds(row0, count), pl.ds(key0, keys), mask)
    place_columns(att_ref, placed_ref)

    @pl.loop(0, D // 256)
    def _(step):
        at = pl.ds(pl.multiple_of(step * 256, 256), 256)
        there = pl.ds(pl.multiple_of(step * 256 + 3 * D, 256), 256)
        mid_ref[:, at] = x_ref[:, at].astype(f32) + mul(placed_ref[...], w_ref[:, there])

    norm_rows(mid_ref, h2_ref, line(g2_ref), line(b2_ref), chunk)
    place_columns(h2_ref, placed_ref)
    pool = pool_matrix(rows // IMG_LEN, rows, 0, IMG_LEN)

    @pl.loop(0, EARLY // TILE)
    def _(step):
        at = pl.ds(pl.multiple_of(step * TILE, TILE), TILE)
        there = pl.ds(pl.multiple_of(step * TILE + 4 * D, TILE), TILE)
        value, _ = gelu_parts(mul(placed_ref[...], w_ref[:, there]))
        early_ref[:, at] = mul(pool, value.astype(bf16))

    for k in range(rows // IMG_LEN):
        first, last = k * IMG_LEN, (k + 1) * IMG_LEN
        start, end = first // 8 * 8, -(-last // 8) * 8
        values = mid_ref[start:end, :]
        place = lax.broadcasted_iota(jnp.int32, values.shape, 0) + start
        inside = (place >= first) & (place < last)
        sum_ref[k : k + 1, :] = jnp.sum(jnp.where(inside, values, 0.0), axis=0, keepdims=True)


def image_front(rows_in, pieces, source, gain1, bias1, gain2, bias2):
    rows = rows_in.shape[0]
    windows = ((0, 208, 0, 256), (208, 192, 192, 208))
    vmem = pl.BlockSpec(memory_space=pltpu.VMEM)
    return pl.pallas_call(
        functools.partial(image_front_kernel, windows),
        out_shape=[
            jax.ShapeDtypeStruct((rows, D), bf16),
            jax.ShapeDtypeStruct((rows // IMG_LEN, D), f32),
            jax.ShapeDtypeStruct((rows // IMG_LEN, EARLY), f32),
        ],
        in_specs=[vmem] * 6 + anywhere(pieces),
        out_specs=[vmem] * 3,
        scratch_shapes=[
            pltpu.VMEM((D, 4 * D + EARLY), bf16),
            pltpu.VMEM((rows, D), bf16),
            pltpu.VMEM((rows, D), bf16),
            pltpu.VMEM((rows, 3 * D), bf16),
            pltpu.VMEM((rows, D), bf16),
            pltpu.VMEM((rows, D), f32),
            pltpu.SemaphoreType.DMA((len(pieces),)),
        ],
        compiler_params=params(),
        cost_estimate=cost(rows * D * D * 12, 8 * D * D, rows * 256 * HEADS),
        name="image_front",
    )(rows_in, source, gain1, bias1, gain2, bias2, *pieces)


def gelu_parts(inner):
    half = 0.5 * (1.0 + lax.erf(inner * (0.5**0.5)))
    return inner * half, half


def pack_kernel(unit_ref, pos_ref, *refs):
    refs[-1][:, :D] = unit_ref[...].astype(bf16)
    refs[-1][:, D:] = pos_ref[...]


def packed(unit, positive, after):
    shape = (unit.shape[0], D + positive.shape[1])
    return pl.pallas_call(
        pack_kernel,
        out_shape=jax.ShapeDtypeStruct(shape, bf16),
        in_specs=[pl.BlockSpec(memory_space=pltpu.VMEM)] * 2 + anywhere(after),
        compiler_params=params(),
        cost_estimate=cost(shape[0] * shape[1], 4 * shape[0] * shape[1]),
        name="packed",
    )(unit, positive, *after)


def pool_matrix(count, rows, row0, seq_len):
    row = (lax.broadcasted_iota(jnp.int32, (count, rows), 1) + row0) // seq_len
    return jnp.where(row == lax.broadcasted_iota(jnp.int32, (count, rows), 0), 1.0, 0.0).astype(bf16)


def two_terms(mean):
    high = mean.astype(bf16)
    low = (mean - high.astype(f32)).astype(bf16)
    return jnp.concatenate([high, low], axis=0)


def unit_rows(pooled):
    inverse = lax.rsqrt(jnp.sum(pooled * pooled, axis=-1, keepdims=True) + norm_eps)
    return pooled * inverse, inverse


def text_up_kernel(h2_ref, wu_ref, wd_ref, sum_ref, *refs):
    slope_ref, hid_ref, unit_ref, inv_ref, acc = refs[-5:]
    step = pl.program_id(0)
    chunk = 320
    per = chunk // TXT_LEN
    pool = pool_matrix(per, chunk, 0, TXT_LEN)
    for k in range(h2_ref.shape[0] // chunk):
        inner = mul(h2_ref[k * chunk : (k + 1) * chunk, :], wu_ref[...])
        value, half = gelu_parts(inner)
        slope = half + inner * (jnp.exp(-0.5 * inner * inner) * 0.3989422804014327)
        slope_ref[k * chunk : (k + 1) * chunk, :] = slope.astype(bf16)
        hid_ref[k * per : (k + 1) * per, :] = mul(pool, value.astype(bf16))
    terms = mul(two_terms(hid_ref[...] * (1.0 / TXT_LEN)), wd_ref[...])
    count = hid_ref.shape[0]
    added = terms[:count] + terms[count:]

    @pl.when(step == 0)
    def _():
        acc[...] = sum_ref[...] * (1.0 / TXT_LEN) + added

    @pl.when(step > 0)
    def _():
        acc[...] += added

    @pl.when(step == pl.num_programs(0) - 1)
    def _():
        unit, inverse = unit_rows(acc[...])
        unit_ref[...] = unit
        inv_ref[...] = jnp.broadcast_to(inverse, inv_ref.shape)


def text_up(normed2, weight_up, weight_down, middle_sum, after=()):
    rows, count = normed2.shape[0], middle_sum.shape[0]
    fixed = lambda shape: pl.BlockSpec(shape, lambda i: (0, 0))
    return pl.pallas_call(
        text_up_kernel,
        grid=(FF // TILE,),
        out_shape=[
            jax.ShapeDtypeStruct((rows, FF), bf16),
            jax.ShapeDtypeStruct((count, FF), f32),
            jax.ShapeDtypeStruct((count, D), f32),
            jax.ShapeDtypeStruct((count, 128), f32),
        ],
        in_specs=[
            fixed((rows, D)),
            pl.BlockSpec((D, TILE), lambda i: (0, i)),
            pl.BlockSpec((TILE, D), lambda i: (i, 0)),
            fixed((count, D)),
        ]
        + anywhere(after),
        out_specs=[
            pl.BlockSpec((rows, TILE), lambda i: (0, i)),
            pl.BlockSpec((count, TILE), lambda i: (0, i)),
            fixed((count, D)),
            fixed((count, 128)),
        ],
        scratch_shapes=[pltpu.VMEM((count, D), f32)],
        compiler_params=params(),
        cost_estimate=cost(2 * rows * D * FF, 4 * D * FF + 2 * rows * FF, 20 * rows * FF),
        name="text_up",
    )(normed2, weight_up, weight_down, middle_sum, *after)


def image_up_kernel(fold, h2_ref, wu_ref, wd_ref, first_ref, sum_ref, early_ref, out_ref, acc, picked):
    step = pl.program_id(0)
    rows, count = h2_ref.shape[0], sum_ref.shape[0]
    part = TILE // fold

    def through_down(summed, groups):
        moved = mul(two_terms(summed * (1.0 / IMG_LEN)), picked[...]).astype(bf16)
        weight = jnp.concatenate([groups[:, k * D : (k + 1) * D] for k in range(fold)], axis=0)
        terms = mul(moved, weight)
        return terms[:count] + terms[count:]

    @pl.when(step == 0)
    def _():
        place = lax.broadcasted_iota(jnp.int32, (TILE, TILE), 0)
        col = lax.broadcasted_iota(jnp.int32, (TILE, TILE), 1)
        source = (col % part) * fold + col // part
        picked[...] = jnp.where(place == source, 1.0, 0.0).astype(bf16)
        total = sum_ref[...] * (1.0 / IMG_LEN)
        for k in range(EARLY // TILE):
            total = total + through_down(
                early_ref[:, k * TILE : (k + 1) * TILE], first_ref[k * part : (k + 1) * part, :]
            )
        acc[...] = total

    value, _ = gelu_parts(mul(h2_ref[...], wu_ref[...]))
    summed = mul(pool_matrix(count, rows, 0, IMG_LEN), value.astype(bf16))
    acc[...] += through_down(summed, wd_ref[...])

    @pl.when(step == pl.num_programs(0) - 1)
    def _():
        unit = unit_rows(acc[...])[0].astype(bf16)
        out_ref[...] = jnp.broadcast_to(unit[None], out_ref.shape)


def image_up(normed2, whole, middle_sum, early, peers):
    rows, count = normed2.shape[0], middle_sum.shape[0]
    fold = FF // D
    before, part = EARLY // TILE, TILE // fold
    fixed = lambda shape: pl.BlockSpec(shape, lambda i: (0, 0))
    return pl.pallas_call(
        functools.partial(image_up_kernel, fold),
        grid=(FF // TILE - before,),
        out_shape=jax.ShapeDtypeStruct((peers, count, D), bf16),
        in_specs=[
            fixed((rows, D)),
            pl.BlockSpec((D, TILE), lambda i: (0, FF // TILE + i)),
            pl.BlockSpec((part, FF), lambda i: (i + before, 0)),
            fixed((before * part, FF)),
            fixed((count, D)),
            fixed((count, EARLY)),
        ],
        out_specs=pl.BlockSpec((peers, count, D), lambda i: (0, 0, 0)),
        scratch_shapes=[pltpu.VMEM((count, D), f32), pltpu.VMEM((TILE, TILE), bf16)],
        compiler_params=params(),
        cost_estimate=cost(2 * rows * D * FF, 4 * D * FF, 15 * rows * FF),
        name="image_up",
    )(normed2, whole, whole, whole, middle_sum, early)


def left_kernel(count, *refs):
    out_ref = refs[-1]
    for k in range(count):
        source_ref, values_ref = refs[2 * k : 2 * k + 2]

        @pl.loop(0, D // 256)
        def _(step, k=k, source_ref=source_ref, values_ref=values_ref):
            at = pl.ds(pl.multiple_of(step * 256, 256), 256)
            picked = mul_bt(chosen(source_ref[at, :]), values_ref[...])
            out_ref[k, at, :] = picked.astype(bf16)


def left_factors(*pairs):
    rows = pairs[0][1].shape[0]
    given = [item for pair in pairs for item in pair]
    return pl.pallas_call(
        functools.partial(left_kernel, len(pairs)),
        out_shape=jax.ShapeDtypeStruct((len(pairs), D, rows), bf16),
        in_specs=in_vmem(len(given)),
        out_specs=pl.BlockSpec(memory_space=pltpu.VMEM),
        compiler_params=params(24 << 20),
        cost_estimate=cost(2 * len(pairs) * rows * D * D, 4 * len(pairs) * rows * D),
        name="left_factors",
    )(*given)


def loss_parts(text_rows, pos, image_all):
    similar = mul_bt(text_rows, image_all) * logit_scale
    shifted = jnp.exp(similar - logit_scale)
    alive = jnp.max(pos, axis=1, keepdims=True)
    row_sum = jnp.sum(shifted, axis=1, keepdims=True)
    row_count = jnp.maximum(jnp.sum(pos, axis=1, keepdims=True), 1.0)
    return similar, shifted, alive, row_sum, row_count


def sums_over_captions(text_rows, pos, image_all):
    similar, shifted, alive, row_sum, row_count = loss_parts(text_rows, pos, image_all)
    pos_similar = pos * similar
    cap_term = alive * (
        logit_scale + jnp.log(row_sum) - jnp.sum(pos_similar, axis=1, keepdims=True) / row_count
    )
    return (
        jnp.sum(alive * shifted, axis=0, keepdims=True),
        jnp.sum(pos, axis=0, keepdims=True),
        jnp.sum(pos_similar, axis=0, keepdims=True),
        jnp.sum(cap_term, axis=0, keepdims=True),
        jnp.sum(alive, axis=0, keepdims=True),
    )


def loss_from(sums):
    col_sum, col_count, col_pos, cap_total, live_total = sums
    img_term = logit_scale + jnp.log(col_sum) - col_pos / col_count
    return 0.5 * cap_total / live_total + 0.5 * jnp.mean(img_term, axis=1, keepdims=True)


def grad_of_unit(text_rows, pos, image_all, col_sum, col_count, live_total):
    _, shifted, alive, row_sum, row_count = loss_parts(text_rows, pos, image_all)
    cap_share, img_share = 0.5 / live_total, 0.5 / image_all.shape[0]
    grad_sims = alive * shifted * (cap_share / row_sum + img_share / col_sum) - pos * (
        cap_share / row_count + img_share / col_count
    )
    return mul(grad_sims.astype(bf16), image_all) * logit_scale


def turned(grad, unit):
    return grad - unit * jnp.sum(grad * unit, axis=-1, keepdims=True)


def loss_into(
    pack_ref, image_ref, own_ref, unit_ref, inv_ref, loss_ref, row_ref, low_ref, col_sum_ref,
    col_count_ref, live_ref
):
    image_all = image_ref[...]
    chunk = 256
    total = None
    for k in range(pack_ref.shape[0] // chunk):
        at = slice(k * chunk, (k + 1) * chunk)
        part = sums_over_captions(pack_ref[at, :D], pack_ref[at, D:].astype(f32), image_all)
        total = part if total is None else [a + b for a, b in zip(total, part)]
    loss_ref[...] = jnp.broadcast_to(loss_from(total), loss_ref.shape)
    col_sum, col_count, _, _, live_total = total
    col_sum_ref[...] = col_sum
    col_count_ref[...] = col_count
    live_ref[...] = jnp.broadcast_to(live_total, live_ref.shape)
    grad = grad_of_unit(
        own_ref[:, :D], own_ref[:, D:].astype(f32), image_all, col_sum, col_count, live_total
    )
    row = inv_ref[:, :1] * turned(grad, unit_ref[...]) * (1.0 / TXT_LEN)
    row_ref[...] = row
    low_ref[...] = row.astype(bf16)


def down_kernel(pack_ref, image_ref, col_sum_ref, col_count_ref, live_ref, hid_ref, *refs):
    step, out_ref = pl.program_id(0), refs[-1]
    text_rows = pack_ref[:, :D]
    grad = grad_of_unit(
        text_rows, pack_ref[:, D:].astype(f32), image_ref[...], col_sum_ref[...],
        col_count_ref[...], live_ref[:, :1]
    )
    rows = (turned(grad, text_rows.astype(f32)) * (1.0 / TXT_LEN)).astype(bf16)
    part = mul_at(hid_ref[...], rows)

    @pl.when(step == 0)
    def _():
        out_ref[...] = part

    @pl.when(step > 0)
    def _():
        out_ref[...] += part


def grad_of_down(pack, image_all, col_sum, col_count, live_total, hidden_cols, after):
    images, chunk = image_all.shape[0], 256
    fixed = lambda shape: pl.BlockSpec(shape, lambda i: (0, 0))
    per = hidden_cols.shape[1]
    return pl.pallas_call(
        down_kernel,
        grid=(pack.shape[0] // chunk,),
        out_shape=jax.ShapeDtypeStruct((per, D), f32),
        in_specs=[
            pl.BlockSpec((chunk, pack.shape[1]), lambda i: (i, 0)),
            fixed((images, D)), fixed((1, images)), fixed((1, images)), fixed((1, 128)),
            pl.BlockSpec((chunk, per), lambda i: (i, 0)),
        ]
        + anywhere(after),
        out_specs=fixed((per, D)),
        compiler_params=params(16 << 20),
        cost_estimate=cost(4 * pack.shape[0] * images * D, 2 * pack.size, pack.shape[0] * images),
        name="grad_of_down",
    )(pack, image_all, col_sum, col_count, live_total, hidden_cols, *after)


def mlp_back_kernel(with_loss, gain_ref, *refs):
    given, refs = (refs[:5], refs[5:]) if with_loss else (refs[:2], refs[2:])
    wd_hbm, slope_hbm, wu_hbm, lhs_hbm, mid_hbm = refs[:5]
    keep_a, send_a, keep_b, send_b, out_ref, sums_out = refs[5:11]
    wd_ref, slope_ref, wu_ref, lhs_ref, mid_ref, sems, whole_sems = refs[-7:]
    low_ref, row_ref = refs[-9:-7] if with_loss else given
    count, rows = low_ref.shape[0], out_ref.shape[0]
    half, steps = D // 2, FF // 2 // TILE

    def copies(tile, slot):
        at = pl.ds(pl.multiple_of(tile * TILE, TILE), TILE)
        return (
            pltpu.make_async_copy(wd_hbm.at[at, :], wd_ref.at[slot], sems.at[0, slot]),
            pltpu.make_async_copy(slope_hbm.at[:, at], slope_ref.at[slot], sems.at[1, slot]),
            pltpu.make_async_copy(wu_hbm.at[:, at], wu_ref.at[slot], sems.at[2, slot]),
        )

    lhs_copy = pltpu.make_async_copy(lhs_hbm, lhs_ref, whole_sems.at[0])
    mid_copy = pltpu.make_async_copy(mid_hbm, mid_ref, whole_sems.at[1])
    for copy in copies(0, 0):
        copy.start()
    lhs_copy.start()
    if with_loss:
        loss_ref, *stats = refs[11:15]
        loss_into(*given, loss_ref, row_ref, low_ref, *stats)
    for k, (keep, send) in enumerate(((keep_a, send_a), (keep_b, send_b))):

        @pl.loop(0, steps)
        def _(step, k=k, keep=keep, send=send):
            tile = k * steps + step
            slot = lax.rem(tile, 2)

            @pl.when(tile + 1 < 2 * steps)
            def _():
                for copy in copies(tile + 1, 1 - slot):
                    copy.start()

            for copy in copies(tile, slot):
                copy.wait()
            if k == 0:

                @pl.when(step == 0)
                def _():
                    lhs_copy.wait()
                    mid_copy.start()

            there = pl.ds(pl.multiple_of(step * TILE, TILE), TILE)
            hidden = mul_bt(low_ref[...], wd_ref[slot])
            wide = jnp.broadcast_to(hidden[:, None, :], (count, TXT_LEN, TILE))
            inner = (wide.reshape(rows, TILE) * slope_ref[slot].astype(f32)).astype(bf16)
            weight = mul(lhs_ref[k], inner).astype(bf16)
            keep[:, there] = weight[:half]
            send[:, there] = weight[half:]
            added = mul_bt(inner, wu_ref[slot])
            if k == 0:

                @pl.when(step == 0)
                def _():
                    out_ref[...] = added

                @pl.when(step > 0)
                def _():
                    out_ref[...] += added
            else:
                out_ref[...] += added

    chunk = 128
    per = chunk // TXT_LEN
    gain = line(gain_ref)
    sums_out[...] = jnp.zeros_like(sums_out)
    mid_copy.wait()

    @pl.loop(0, rows // chunk)
    def _(k):
        at = pl.ds(pl.multiple_of(k * chunk, chunk), chunk)
        unit, scale = norm_parts(mid_ref[at, :])
        grad = out_ref[at, :]
        sums_out[:, :D] += jnp.sum(grad * unit, axis=0, keepdims=True)
        sums_out[:, D:] += jnp.sum(grad, axis=0, keepdims=True)
        row = row_ref[pl.ds(pl.multiple_of(k * per, per), per), :]
        row = jnp.broadcast_to(row[:, None, :], (per, TXT_LEN, D)).reshape(chunk, D)
        out_ref[at, :] = row + norm_back(unit, scale, gain, grad)


def mlp_back(given, weight_down, slope, weight_up, lhs, middle, gain):
    rows, count = slope.shape[0], given[-2].shape[0]
    with_loss = len(given) == 5
    shapes = [stays((D // 2, FF // 2), bf16)] * 4 + [stays((rows, D), f32), stays((1, 2 * D), f32)]
    scratch = [
        pltpu.VMEM((2, TILE, D), bf16),
        pltpu.VMEM((2, rows, TILE), bf16),
        pltpu.VMEM((2, D, TILE), bf16),
        pltpu.VMEM((2, D, rows), bf16),
        pltpu.VMEM((rows, D), f32),
        pltpu.SemaphoreType.DMA((3, 2)),
        pltpu.SemaphoreType.DMA((2,)),
    ]
    if with_loss:
        images = given[1].shape[0]
        wide = [(1, 128), (1, images), (1, images), (1, 128)]
        shapes += [jax.ShapeDtypeStruct(shape, f32) for shape in wide]
        scratch = [pltpu.VMEM((count, D), bf16), pltpu.VMEM((count, D), f32)] + scratch
    return pl.pallas_call(
        functools.partial(mlp_back_kernel, with_loss),
        out_shape=shapes,
        in_specs=in_vmem(1 + len(given)) + [pl.BlockSpec(memory_space=pltpu.HBM)] * 5,
        out_specs=in_vmem(len(shapes)),
        scratch_shapes=scratch,
        compiler_params=params(32 << 20),
        cost_estimate=cost(4 * rows * D * FF, 4 * D * FF + 2 * rows * FF + 2 * D * FF, rows * FF),
        name="mlp_back",
    )(gain, *given, *in_hbm(weight_down, slope, weight_up, lhs, middle))


def attention_back_kernel(first, grad_ref, wo_ref, qkv_ref, lse_ref, *refs):
    low_ref, out_ref = refs[-2:]
    chunk = 128
    mask = same_sequence(chunk, 0, chunk, 0, TXT_LEN)

    @pl.loop(0, low_ref.shape[0] // chunk)
    def _(step):
        here = pl.ds(pl.multiple_of((first + step) * chunk, chunk), chunk)
        there = pl.ds(pl.multiple_of(step * chunk, chunk), chunk)
        sums = lse_ref[pl.ds(pl.multiple_of((first + step) * 16, 16), 16), :]
        low = grad_ref[here, :].astype(bf16)
        low_ref[there, :] = low
        grad_att = mul_bt(low, wo_ref[...]).astype(bf16)
        for pair in range(HEADS // 2):
            queries = qkv_ref[here, pair_cols(0, pair)] * bf16(HEAD ** (-0.5))
            keys = two_heads(qkv_ref[here, pair_cols(1, pair)])
            vals = two_heads(qkv_ref[here, pair_cols(2, pair)])
            grads = grad_att[:, pair_cols(0, pair)]
            scores, grad_probs = mul_bt(keys, queries), mul_bt(vals, grads)
            probs, grad_scores = [], []
            for k in range(2):
                at = slice(k * chunk, (k + 1) * chunk)
                head = 2 * pair + k
                shifted = scores[at] - sums[head : head + 1, :]
                prob = jnp.where(mask, jnp.exp(jnp.where(mask, shifted, 0.0)), 0.0)
                along = jnp.sum(grad_probs[at] * prob, axis=0, keepdims=True)
                grad_scores.append((prob * (grad_probs[at] - along)).astype(bf16))
                probs.append(prob.astype(bf16))
            grad_q = mul_at(jnp.concatenate(grad_scores, axis=0), keys) * HEAD ** (-0.5)
            grad_k = mul(jnp.concatenate(grad_scores, axis=1), two_heads(queries))
            grad_v = mul(jnp.concatenate(probs, axis=1), two_heads(grads))
            out_ref[there, pair_cols(0, pair)] = grad_q.astype(bf16)
            out_ref[there, pair_cols(1, pair)] = grad_k.astype(bf16)
            out_ref[there, pair_cols(2, pair)] = grad_v.astype(bf16)


def attention_back(grad_middle, weight_out, project, log_sums, first, count, after=()):
    rows = count * 128
    return pl.pallas_call(
        functools.partial(attention_back_kernel, first),
        out_shape=[stays((rows, D), bf16), stays((rows, 3 * D), bf16)],
        in_specs=in_vmem(4) + anywhere(after),
        out_specs=in_vmem(2),
        compiler_params=params(16 << 20),
        cost_estimate=cost(10 * rows * D * D, 16 * rows * D + 2 * D * D, rows * 128 * HEADS),
        name="attention_back",
    )(grad_middle, weight_out, project, log_sums, *after)


def mul_rows(lhs, parts, cols):
    total, row = 0.0, 0
    for part in parts:
        total = total + mul(lhs[:, row : row + part.shape[0]], part[:, cols])
        row += part.shape[0]
    return total


def weight_back_kernel(factors, groups, lhs_ref, *refs):
    keep_a, send_a, keep_b, send_b = refs[-4:]
    half = D // 2
    for k, (factor, group, col) in enumerate(factors):
        parts = refs[sum(groups[:group]) : sum(groups[: group + 1])]
        weight = mul_rows(lhs_ref.at[factor], parts, slice(col * D, (col + 1) * D)).astype(bf16)
        at = slice(k % 2 * D, (k % 2 + 1) * D)
        (keep_b if k > 1 else keep_a)[:, at] = weight[:half]
        (send_b if k > 1 else send_a)[:, at] = weight[half:]


def weight_back(lhs, groups, factors, after=()):
    rows = lhs.shape[2]
    given = [part for group in groups for part in group]
    return pl.pallas_call(
        functools.partial(weight_back_kernel, factors, [len(group) for group in groups]),
        out_shape=[stays((D // 2, 2 * D), bf16)] * 4,
        in_specs=in_vmem(1 + len(given)) + anywhere(after),
        out_specs=in_vmem(4),
        compiler_params=params(16 << 20),
        cost_estimate=cost(8 * rows * D * D, 8 * rows * D + 14 * D * D),
        name="weight_back",
    )(lhs, *given, *after)


def input_back_kernel(count, *refs):
    projs = refs[:count]
    w_ref, x_ref, gain_ref, mid_ref, sums_ref = refs[count : count + 5]
    out_ref, sums_out = refs[-2:]
    rows, chunk = x_ref.shape[0], 128

    @pl.loop(0, D // 256)
    def _(step):
        at = pl.ds(pl.multiple_of(step * 256, 256), 256)
        row = 0
        for part in projs:
            there = slice(row, row + part.shape[0])
            out_ref[there, at] = mul_bt(part[...], w_ref[at, :])
            row += part.shape[0]

    gain = line(gain_ref)
    sums_out[...] = jnp.zeros_like(sums_out)
    sums_out[1:2, :] = sums_ref[...]

    @pl.loop(0, rows // chunk)
    def _(k):
        at = pl.ds(pl.multiple_of(k * chunk, chunk), chunk)
        unit, scale = norm_parts(x_ref[at, :].astype(f32))
        grad = out_ref[at, :]
        sums_out[0:1, :D] += jnp.sum(grad * unit, axis=0, keepdims=True)
        sums_out[0:1, D:] += jnp.sum(grad, axis=0, keepdims=True)
        out_ref[at, :] = mid_ref[at, :] + norm_back(unit, scale, gain, grad)


def input_back(grad_projs, weight, rows_in, gain, grad_middle, sums, after=()):
    rows = rows_in.shape[0]
    return pl.pallas_call(
        functools.partial(input_back_kernel, len(grad_projs)),
        out_shape=[jax.ShapeDtypeStruct((rows, D), f32), stays((8, 2 * D), f32)],
        in_specs=in_vmem(len(grad_projs) + 5) + anywhere(after),
        out_specs=in_vmem(2),
        compiler_params=params(16 << 20),
        cost_estimate=cost(6 * rows * D * D, 14 * rows * D + 6 * D * D),
        name="input_back",
    )(*grad_projs, weight, rows_in, gain, grad_middle, sums, *after)


def local(
    images,
    captions,
    img_gain1,
    img_bias1,
    img_qkv,
    img_out,
    img_gain2,
    img_bias2,
    img_up,
    img_down,
    txt_gain1,
    txt_bias1,
    txt_qkv,
    txt_out,
    txt_gain2,
    txt_bias2,
    txt_up,
    txt_down,
    counts,
    matches,
):
    peers = lax.axis_size(AXIS)
    own = lax.axis_index(AXIS)
    per = D // peers
    img_local = counts.shape[0]
    cap_local = matches.shape[0]
    total_images = matches.shape[1]

    up_rows = img_up.reshape(per, FF)
    whole = lax.all_gather(
        jnp.concatenate([img_down.reshape(per, FF), up_rows[:, EARLY:]], axis=1),
        AXIS,
        axis=0,
        tiled=True,
    )
    small = peers == 32
    shard = jnp.concatenate(
        [img_qkv.reshape(per, 3 * D), img_out.reshape(per, D), up_rows[:, :EARLY]], axis=1
    )
    if small:
        line, source = gathered_line(shard), row_order((1, 4, 2, 16, 8))
    else:
        line, source = lax.all_gather(shard, AXIS, axis=0, tiled=True), row_order(())

    normed1, project, attended, middle, normed2, middle_sum, log_sums = text_front(
        captions, txt_gain1, txt_bias1, txt_qkv, txt_out, txt_gain2, txt_bias2
    )
    middle_sum, line = in_turn(middle_sum, line)
    beside, above = (swapped(line, 2), swapped(line, 4)) if small else (line, line)
    slope, hidden_sum, text_unit, inverse = text_up(
        normed2, txt_up, txt_down, middle_sum, (line,)
    )
    text_unit, normed2, beside, above = lax.optimization_barrier(
        (text_unit, normed2, beside, above)
    )

    ends_at = jnp.cumsum(counts)
    slot_ids = lax.iota(jnp.int32, cap_local)
    owner = jnp.sum((ends_at[None, :] <= slot_ids[:, None]).astype(jnp.int32), axis=1)
    owner = owner + own * img_local
    live = slot_ids < ends_at[-1]
    columns = lax.iota(jnp.int32, total_images)
    positive = ((matches > 0) | (owner[:, None] == columns[None, :])) & live[:, None]

    order_a, order_b, tail = stage_orders()
    source_a, source_b = row_order(order_a + tail[::-1]), row_order(order_b + tail[::-1])
    own_pack = packed(text_unit, positive.astype(bf16), ())
    lhs_up = left_factors((source_a, normed2), (source_b, normed2))
    pieces = [line]
    if small:
        first, second = diagonal(beside, above)
        own_pack, first, second, lhs_up = lax.optimization_barrier(
            (own_pack, first, second, lhs_up)
        )
        held = own_pack[None]
        others = [swapped(held, mask) for mask in (8, 16, 24)]
        pieces = [line, beside, above, first, second]
        pieces = pieces + [swapped(piece, 1) for piece in pieces]

    normed_img, middle_img, early = image_front(
        images, pieces, source, img_gain1, img_bias1, img_gain2, img_bias2
    )
    if small:
        scaled_sum = (hidden_sum * inverse[:, :1]).astype(bf16)
        normed_img, scaled_sum, others = lax.optimization_barrier((normed_img, scaled_sum, others))
        held = joined(joined(held, others[0], 8), joined(others[1], others[2], 8), 16, 1)
        text_beside, text_above = swapped(held, 2), swapped(held, 4)
        hidden_cols = lax.all_to_all(scaled_sum, AXIS, split_axis=1, concat_axis=0, tiled=True)
        whole, text_beside, text_above = lax.optimization_barrier((whole, text_beside, text_above))
        halves = diagonal(text_beside, text_above)
    image_low = image_up(normed_img, whole, middle_img, early, peers)
    if small:
        image_low, halves, hidden_cols = lax.optimization_barrier((image_low, halves, hidden_cols))
        across = jnp.concatenate(halves, axis=0)
        held = joined(joined(held, text_beside, 2), joined(text_above, across, 2), 4, 4)
        text_pack = joined(held, swapped(held, 1), 1).reshape(-1, D + total_images)
    image_all = exchanged(image_low).reshape(total_images, D)
    if small:
        image_all, text_pack = in_turn(image_all, text_pack)

    if small:
        given = (text_pack, image_all, own_pack, text_unit, inverse)
    else:
        text_low, pos = own_pack[:, :D], own_pack[:, D:].astype(f32)
        totals = lax.psum(sums_over_captions(text_low, pos, image_all), AXIS)
        loss_value = loss_from(totals)
        grad = grad_of_unit(text_low, pos, image_all, totals[0], totals[1], totals[4])
        grad_row = inverse[:, :1] * turned(grad, text_unit) * (1.0 / TXT_LEN)
        row_low = grad_row.astype(bf16)
        given = (row_low, grad_row)

    *up, grad_middle, sums = mlp_back(given, txt_down, slope, txt_up, lhs_up, middle, txt_gain2)
    if small:
        *up, grad_middle, sums, loss_value, col_sum, col_count, live_total = (
            *up, grad_middle, sums
        )
    stages = len(order_a)
    low_one, proj_one = attention_back(grad_middle, txt_out, project, log_sums, 0, 2)
    for stage in range(stages - 2):
        up = fold(hand_on(up, stage), (proj_one,))
    low_two, proj_two = attention_back(grad_middle, txt_out, project, log_sums, 2, 3, up)
    proj_two, normed1 = in_turn(proj_two, normed1)
    lhs_rest = left_factors((source_a, normed1), (source_b, normed1), (source_b, attended))
    up = fold(hand_on(up, stages - 2), (proj_two, lhs_rest))
    projs, lows = (proj_one, proj_two), (low_one, low_two)
    rest = weight_back(lhs_rest, [projs, lows], [(0, 0, 0), (0, 0, 1), (1, 0, 2), (2, 1, 0)], up)
    up = hand_on(up, stages - 1)
    caption_grad, sums = input_back(
        projs, txt_qkv, captions, txt_gain1, grad_middle, sums, rest[:1]
    )
    caption_grad, up = in_turn(caption_grad, up)
    up = fold_last(up)
    if small:
        *rest, sums = fold(hand_on(rest, 0), up[:1], (sums, swapped(sums, 1)))
    else:
        norms = lax.psum(sums, AXIS)[:2].reshape(-1)
        for stage in range(stages - 2):
            rest = fold(hand_on(rest, stage), up[:1])
    up = hand_on_last(up)
    rest = hand_on(rest, stages - 2)
    if small:
        grad_down = grad_of_down(
            text_pack, image_all, col_sum, col_count, live_total, hidden_cols, (caption_grad,)
        )
    else:
        grad_down = lax.psum_scatter(
            mul_at(hidden_sum.astype(bf16), row_low), AXIS, scatter_dimension=0, tiled=True
        )
    grad_down, rest, up = lax.optimization_barrier((grad_down, rest, up))
    if small:
        *rest, sums = fold(rest, (), (sums,))
        rest = fold_last(hand_on(rest, stages - 1), (), (sums,))
    else:
        rest = fold_last(hand_on(fold(rest), stages - 1))
    up_share = sum_last(*up)
    rest_share = sum_last(*hand_on_last(rest))
    if small:
        norms = rest_share[per]
        rest_share = rest_share[:per]
    return (
        loss_value[0, 0],
        caption_grad,
        norms[:D],
        norms[D : 2 * D],
        rest_share[:, : 3 * D].reshape(-1),
        rest_share[:, 3 * D :].reshape(-1),
        norms[2 * D : 3 * D],
        norms[3 * D :],
        up_share.reshape(-1),
        grad_down.reshape(-1),
    )


def solution(mesh):
    split, flat, whole = P("blk", None), P("blk"), P()
    image_block = (whole, whole, flat, flat, whole, whole, flat, flat)
    return jax.shard_map(
        local,
        mesh=mesh,
        in_specs=(split, split) + image_block + (whole,) * 8 + (flat, split),
        out_specs=(whole, split, whole, whole, flat, flat, whole, whole, flat, flat),
        check_vma=False,
    )
```

```python
import functools

import jax
import jax.numpy as jnp
from jax import lax
from jax.experimental import pallas as pl
from jax.experimental.pallas import tpu as pltpu
from jax.sharding import PartitionSpec as P

D = 768
FF = 3072
HEAD = 64
HEADS = D // HEAD
IMG_LEN = 50
TXT_LEN = 16
AXIS = "blk"

norm_eps = 1e-06
logit_scale = 50.0
f32 = jnp.float32
bf16 = jnp.bfloat16


def swapped(value, mask):
    peers = lax.axis_size(AXIS)
    return lax.ppermute(value, AXIS, [(i, i ^ mask) for i in range(peers)])


def bit_masks():
    peers = lax.axis_size(AXIS)
    return [1 << k for k in range(peers.bit_length() - 1)]


def joined(held, other, mask, outer=None):
    upper = (lax.axis_index(AXIS) & mask) > 0
    first = jnp.where(upper, other, held)
    second = jnp.where(upper, held, other)
    outer = held.shape[0] if outer is None else outer
    parts = [part.reshape((outer, -1) + held.shape[1:]) for part in (first, second)]
    return jnp.stack(parts, axis=1).reshape((-1,) + held.shape[1:])


def exchanged(copies):
    return lax.all_to_all(copies, AXIS, split_axis=0, concat_axis=0, tiled=True)


def stage_orders():
    masks = bit_masks()
    head, tail = masks[:-2], masks[-2:]
    order_a = list(head)
    order_b = list(head)
    for k in range(1, len(head) - 1, 2):
        order_b[k], order_b[k + 1] = order_b[k + 1], order_b[k]
    return order_a, order_b, tail


def row_order(bits):
    peers = lax.axis_size(AXIS)
    own = lax.axis_index(AXIS)
    per = D // peers
    places = lax.broadcasted_iota(jnp.int32, (D, 1), 0)
    block = places // per
    target = jnp.zeros_like(block) + own
    for k, mask in enumerate(bits):
        target = target ^ (((block >> (len(bits) - 1 - k)) & 1) * mask)
    return target * per + places % per


def chosen(source):
    column = lax.broadcasted_iota(jnp.int32, (source.shape[0], D), 1)
    return jnp.where(column == source, 1.0, 0.0).astype(bf16)


def gathered_line(shard):
    return jnp.concatenate([shard] + [swapped(shard, mask) for mask in (8, 16, 24)], axis=0)


def diagonal(beside, above):
    half = beside.shape[0] // 2
    return swapped(beside[:half], 4), swapped(above[half:], 2)


def in_turn(first, then):
    return lax.optimization_barrier((first, then))


def hand_on(parts, stage):
    order_a, order_b, _ = stage_orders()
    keep_a, send_a, keep_b, send_b = parts
    return keep_a, swapped(send_a, order_a[stage]), keep_b, swapped(send_b, order_b[stage])


def hand_on_last(blocks):
    low, high = stage_orders()[2]
    own, *others = blocks
    return own, [swapped(block, mask) for block, mask in zip(others, (low, high, low | high))]


def sum_last(own, others):
    total = own
    for other in others:
        total = total + other.astype(f32)
    return total


VMEM_BYTES = 56 << 20
TILE = 512
EARLY = TILE


def norm_parts(values):
    average = jnp.mean(values, axis=-1, keepdims=True)
    centred = values - average
    variance = jnp.mean(centred * centred, axis=-1, keepdims=True)
    scale = lax.rsqrt(variance + norm_eps)
    return centred * scale, scale


def norm_back(unit, scale, gain, grad):
    inner = grad * gain
    shift = jnp.mean(inner, axis=-1, keepdims=True)
    along = jnp.mean(inner * unit, axis=-1, keepdims=True)
    return scale * (inner - shift - unit * along)


def mul(lhs, rhs):
    return jnp.dot(lhs, rhs, preferred_element_type=f32)


def mul_bt(lhs, rhs):
    return lax.dot_general(lhs, rhs, (((1,), (1,)), ((), ())), preferred_element_type=f32)


def mul_at(lhs, rhs):
    return lax.dot_general(lhs, rhs, (((0,), (0,)), ((), ())), preferred_element_type=f32)


def params(limit=VMEM_BYTES):
    return pltpu.CompilerParams(vmem_limit_bytes=limit)


def in_vmem(count):
    return [pl.BlockSpec(memory_space=pltpu.VMEM)] * count


def in_hbm(*arrays):
    return [pltpu.with_memory_space_constraint(array, pltpu.HBM) for array in arrays]


def stays(shape, dtype):
    return pltpu.VMEM(shape, dtype)


def cost(flops, moved, transcendentals=0):
    return pl.CostEstimate(flops=flops, bytes_accessed=moved, transcendentals=transcendentals)


def lane_halves(dtype):
    lane = lax.broadcasted_iota(jnp.int32, (1, 2 * HEAD), 1)
    low = jnp.where(lane < HEAD, 1.0, 0.0)
    return low.astype(dtype), (1.0 - low).astype(dtype)


def two_heads(pair):
    low, high = lane_halves(bf16)
    return jnp.concatenate([pair * low, pair * high], axis=0)


def same_sequence(rows, row0, cols, col0, seq_len):
    row = (lax.broadcasted_iota(jnp.int32, (rows, cols), 0) + row0) // seq_len
    col = (lax.broadcasted_iota(jnp.int32, (rows, cols), 1) + col0) // seq_len
    return row == col


def softmax_down(scores, mask):
    keys = mask.shape[0]
    parts, sums = [], []
    for k in range(2):
        part = jnp.where(mask, scores[k * keys : (k + 1) * keys], -1e30)
        most = jnp.max(part, axis=0, keepdims=True)
        raised = jnp.exp(part - most)
        total = jnp.sum(raised, axis=0, keepdims=True)
        parts.append(raised * (1.0 / total))
        sums.append(most + jnp.log(total))
    return parts, sums


def fold_kernel(extra, keep_a, got_a, keep_b, got_b, *refs):
    outs = refs[-5:] if extra else refs[-4:]
    rows, half, tile = keep_a.shape[0], keep_a.shape[0] // 2, 256

    @pl.loop(0, keep_a.shape[1] // tile)
    def _(step):
        cols = pl.ds(pl.multiple_of(step * tile, tile), tile)
        for k, (kept, got) in enumerate(((keep_a, got_a), (keep_b, got_b))):
            for j in range(2):
                at = slice(j * half, (j + 1) * half)
                total = kept[at, cols].astype(f32) + got[at, cols].astype(f32)
                outs[2 * k + j][:half, cols] = total.astype(bf16)

    if extra:
        came = refs[1][...] if extra > 1 else got_a[rows : rows + 16, :].astype(f32)[:8]
        sums = refs[0][...] + came
        outs[4][...] = sums
        outs[1][half : half + 16, :] = jnp.concatenate([sums, sums], axis=0).astype(bf16)


def fold(parts, after=(), sums=()):
    rows, cols = parts[0].shape
    if rows % 32:
        whole = [
            (kept.astype(f32) + got.astype(f32)).astype(bf16)
            for kept, got in (parts[:2], parts[2:])
        ]
        return [part for one in whole for part in (one[: rows // 2], one[rows // 2 :])]
    half = (rows // 2, cols)
    shapes = [stays(half, bf16)] * 4
    if sums:
        shapes[1] = stays((rows // 2 + 16, cols), bf16)
        shapes.append(stays((8, cols), f32))
    return pl.pallas_call(
        functools.partial(fold_kernel, len(sums)),
        out_shape=shapes,
        in_specs=in_vmem(4 + len(sums)) + anywhere(after),
        out_specs=in_vmem(len(shapes)),
        compiler_params=params(8 << 20),
        cost_estimate=cost(2 * rows * cols, 12 * rows * cols),
        name="fold",
    )(*parts, *sums, *after)


def fold_last_kernel(extra, keep_a, got_a, keep_b, got_b, *refs):
    outs = refs[-4:]
    cols = keep_a.shape[1]
    rows = keep_a.shape[0] // 4
    if extra:
        sums = refs[0][...] + got_a[4 * rows : 4 * rows + 16, :].astype(f32)[:8]
    for k, (kept, got) in enumerate(((keep_a, got_a), (keep_b, got_b))):
        total = kept[...].astype(f32) + got[: 4 * rows, :].astype(f32)
        at = slice(k * cols, (k + 1) * cols)
        for j, out in enumerate(outs):
            part = total[j * rows : (j + 1) * rows]
            if extra:
                row = jnp.broadcast_to(sums[k : k + 1], (8, cols))
                part = jnp.concatenate([part, row], axis=0)
            out[:, at] = part.astype(out.dtype)


def fold_last(parts, after=(), sums=()):
    rows, cols = parts[0].shape
    shape = (rows // 4 + (8 if sums else 0), 2 * cols)
    if rows % 32:
        pairs = (parts[:2], parts[2:])
        both = [kept.astype(f32) + got.astype(f32) for kept, got in pairs]
        own, *others = jnp.split(jnp.concatenate(both, axis=1), 4)
        return [own] + [other.astype(bf16) for other in others]
    return pl.pallas_call(
        functools.partial(fold_last_kernel, len(sums)),
        out_shape=[stays(shape, f32)] + [stays(shape, bf16)] * 3,
        in_specs=in_vmem(4 + len(sums)) + anywhere(after),
        out_specs=in_vmem(4),
        compiler_params=params(8 << 20),
        cost_estimate=cost(2 * rows * cols, 12 * rows * cols),
        name="fold_last",
    )(*parts, *sums, *after)


def anywhere(after):
    return [pl.BlockSpec(memory_space=pl.ANY)] * len(after)


def pair_cols(part, pair):
    start = part * D + pair * 2 * HEAD
    return slice(start, start + 2 * HEAD)


def line(ref):
    return ref[...].astype(f32).reshape(1, -1)


def norm_rows(src, dst, gain, bias, step_rows):
    @pl.loop(0, src.shape[0] // step_rows)
    def _(step):
        at = pl.ds(pl.multiple_of(step * step_rows, step_rows), step_rows)
        unit, _ = norm_parts(src[at, :].astype(f32))
        dst[at, :] = (unit * gain + bias).astype(bf16)


def attend_along(qkv_ref, att_ref, q_rows, k_rows, mask):
    low, high = lane_halves(f32)
    for pair in range(HEADS // 2):
        queries = two_heads(qkv_ref[q_rows, pair_cols(0, pair)] * bf16(HEAD ** (-0.5)))
        scores = mul_bt(queries, qkv_ref[k_rows, pair_cols(1, pair)])
        scores = jnp.where(mask, scores, -1e30)
        raised = jnp.exp(scores - jnp.max(scores, axis=-1, keepdims=True))
        probs = (raised * (1.0 / jnp.sum(raised, axis=-1, keepdims=True))).astype(bf16)
        half = probs.shape[0] // 2
        mixed = mul(probs, qkv_ref[k_rows, pair_cols(2, pair)])
        att_ref[q_rows, pair_cols(0, pair)] = (mixed[:half] * low + mixed[half:] * high).astype(bf16)


def attend(qkv_ref, att_ref, q_rows, k_rows, mask, keep_sums):
    for pair in range(HEADS // 2):
        queries = qkv_ref[q_rows, pair_cols(0, pair)] * bf16(HEAD ** (-0.5))
        scores = mul_bt(two_heads(qkv_ref[k_rows, pair_cols(1, pair)]), queries)
        probs, sums = softmax_down(scores, mask)
        vals = two_heads(qkv_ref[k_rows, pair_cols(2, pair)])
        mixed = mul_at(jnp.concatenate(probs, axis=0).astype(bf16), vals)
        att_ref[q_rows, pair_cols(0, pair)] = mixed.astype(bf16)
        for k in range(2):
            keep_sums(2 * pair + k, sums[k])


def text_front_kernel(
    x_ref, g1_ref, b1_ref, wqkv_ref, wo_ref, g2_ref, b2_ref, h1_ref, qkv_ref, att_ref, mid_ref,
    h2_ref, sum_ref, lse_ref
):
    rows, chunk = x_ref.shape[0], 128
    norm_rows(x_ref, h1_ref, line(g1_ref), line(b1_ref), chunk)

    @pl.loop(0, 3 * D // 256)
    def _(step):
        at = pl.ds(pl.multiple_of(step * 256, 256), 256)
        qkv_ref[:, at] = mul(h1_ref[...], wqkv_ref[:, at]).astype(bf16)

    mask = same_sequence(chunk, 0, chunk, 0, TXT_LEN)

    @pl.loop(0, rows // chunk)
    def _(step):
        at = pl.ds(pl.multiple_of(step * chunk, chunk), chunk)

        def keep_sums(head, value):
            lse_ref[pl.ds(step * 16 + head, 1), :] = value

        attend(qkv_ref, att_ref, at, at, mask, keep_sums)

    @pl.loop(0, D // 256)
    def _(step):
        at = pl.ds(pl.multiple_of(step * 256, 256), 256)
        mid_ref[:, at] = x_ref[:, at].astype(f32) + mul(att_ref[...], wo_ref[:, at])

    norm_rows(mid_ref, h2_ref, line(g2_ref), line(b2_ref), chunk)
    per = chunk // TXT_LEN

    @pl.loop(0, rows // chunk)
    def _(step):
        values = mid_ref[pl.ds(pl.multiple_of(step * chunk, chunk), chunk), :]
        sum_ref[pl.ds(pl.multiple_of(step * per, per), per), :] = jnp.sum(
            values.reshape(per, TXT_LEN, D), axis=1
        )


def text_front(rows_in, gain1, bias1, wqkv, wo, gain2, bias2):
    rows = rows_in.shape[0]
    shapes = [
        ((rows, D), bf16),
        ((rows, 3 * D), bf16),
        ((rows, D), bf16),
        ((rows, D), f32),
        ((rows, D), bf16),
        ((rows // TXT_LEN, D), f32),
        ((rows // 128 * 16, 128), f32),
    ]
    return pl.pallas_call(
        text_front_kernel,
        out_shape=[jax.ShapeDtypeStruct(*item) for item in shapes],
        compiler_params=params(),
        cost_estimate=cost(rows * D * D * 8, 14 * D * rows + 8 * D * D, rows * 128 * HEADS),
        name="text_front",
    )(rows_in, gain1, bias1, wqkv, wo, gain2, bias2)


def image_front_kernel(
    windows, x_ref, order_ref, g1_ref, b1_ref, g2_ref, b2_ref, *refs
):
    h2_ref, sum_ref, early_ref = refs[-10:-7]
    w_ref, h1_ref, placed_ref, qkv_ref, att_ref, mid_ref, sems = refs[-7:]
    rows, chunk = x_ref.shape[0], 80
    copies, row = [], 0
    for k, piece in enumerate(refs[:-10]):
        place = w_ref.at[pl.ds(row, piece.shape[0]), :]
        copies.append(pltpu.make_async_copy(piece, place, sems.at[k]))
        row += piece.shape[0]
    for copy in copies:
        copy.start()

    def place_columns(src, dst):
        @pl.loop(0, D // 256)
        def _(step):
            at = pl.ds(pl.multiple_of(step * 256, 256), 256)
            dst[:, at] = mul_bt(src[...], chosen(order_ref[at, :])).astype(bf16)

    norm_rows(x_ref, h1_ref, line(g1_ref), line(b1_ref), chunk)
    place_columns(h1_ref, placed_ref)
    for copy in copies:
        copy.wait()

    @pl.loop(0, 3 * D // 256)
    def _(step):
        at = pl.ds(pl.multiple_of(step * 256, 256), 256)
        qkv_ref[:, at] = mul(placed_ref[...], w_ref[:, at]).astype(bf16)

    for row0, count, key0, keys in windows:
        one = same_sequence(count, row0, keys, key0, IMG_LEN)
        mask = jnp.concatenate([one, one], axis=0)
        attend_along(qkv_ref, att_ref, pl.ds(row0, count), pl.ds(key0, keys), mask)
    place_columns(att_ref, placed_ref)

    @pl.loop(0, D // 256)
    def _(step):
        at = pl.ds(pl.multiple_of(step * 256, 256), 256)
        there = pl.ds(pl.multiple_of(step * 256 + 3 * D, 256), 256)
        mid_ref[:, at] = x_ref[:, at].astype(f32) + mul(placed_ref[...], w_ref[:, there])

    norm_rows(mid_ref, h2_ref, line(g2_ref), line(b2_ref), chunk)
    place_columns(h2_ref, placed_ref)
    pool = pool_matrix(rows // IMG_LEN, rows, 0, IMG_LEN)

    @pl.loop(0, EARLY // TILE)
    def _(step):
        at = pl.ds(pl.multiple_of(step * TILE, TILE), TILE)
        there = pl.ds(pl.multiple_of(step * TILE + 4 * D, TILE), TILE)
        value, _ = gelu_parts(mul(placed_ref[...], w_ref[:, there]))
        early_ref[:, at] = mul(pool, value.astype(bf16))

    for k in range(rows // IMG_LEN):
        first, last = k * IMG_LEN, (k + 1) * IMG_LEN
        start, end = first // 8 * 8, -(-last // 8) * 8
        values = mid_ref[start:end, :]
        place = lax.broadcasted_iota(jnp.int32, values.shape, 0) + start
        inside = (place >= first) & (place < last)
        sum_ref[k : k + 1, :] = jnp.sum(jnp.where(inside, values, 0.0), axis=0, keepdims=True)


def image_front(rows_in, pieces, source, gain1, bias1, gain2, bias2):
    rows = rows_in.shape[0]
    windows = ((0, 208, 0, 256), (208, 192, 192, 208))
    vmem = pl.BlockSpec(memory_space=pltpu.VMEM)
    return pl.pallas_call(
        functools.partial(image_front_kernel, windows),
        out_shape=[
            jax.ShapeDtypeStruct((rows, D), bf16),
            jax.ShapeDtypeStruct((rows // IMG_LEN, D), f32),
            jax.ShapeDtypeStruct((rows // IMG_LEN, EARLY), f32),
        ],
        in_specs=[vmem] * 6 + anywhere(pieces),
        out_specs=[vmem] * 3,
        scratch_shapes=[
            pltpu.VMEM((D, 4 * D + EARLY), bf16),
            pltpu.VMEM((rows, D), bf16),
            pltpu.VMEM((rows, D), bf16),
            pltpu.VMEM((rows, 3 * D), bf16),
            pltpu.VMEM((rows, D), bf16),
            pltpu.VMEM((rows, D), f32),
            pltpu.SemaphoreType.DMA((len(pieces),)),
        ],
        compiler_params=params(),
        cost_estimate=cost(rows * D * D * 12, 8 * D * D, rows * 256 * HEADS),
        name="image_front",
    )(rows_in, source, gain1, bias1, gain2, bias2, *pieces)


def gelu_parts(inner):
    half = 0.5 * (1.0 + lax.erf(inner * (0.5**0.5)))
    return inner * half, half


def pack_kernel(unit_ref, pos_ref, *refs):
    refs[-1][:, :D] = unit_ref[...].astype(bf16)
    refs[-1][:, D:] = pos_ref[...]


def packed(unit, positive, after):
    shape = (unit.shape[0], D + positive.shape[1])
    return pl.pallas_call(
        pack_kernel,
        out_shape=jax.ShapeDtypeStruct(shape, bf16),
        in_specs=[pl.BlockSpec(memory_space=pltpu.VMEM)] * 2 + anywhere(after),
        compiler_params=params(),
        cost_estimate=cost(shape[0] * shape[1], 4 * shape[0] * shape[1]),
        name="packed",
    )(unit, positive, *after)


def pool_matrix(count, rows, row0, seq_len):
    row = (lax.broadcasted_iota(jnp.int32, (count, rows), 1) + row0) // seq_len
    return jnp.where(row == lax.broadcasted_iota(jnp.int32, (count, rows), 0), 1.0, 0.0).astype(bf16)


def two_terms(mean):
    high = mean.astype(bf16)
    low = (mean - high.astype(f32)).astype(bf16)
    return jnp.concatenate([high, low], axis=0)


def unit_rows(pooled):
    inverse = lax.rsqrt(jnp.sum(pooled * pooled, axis=-1, keepdims=True) + norm_eps)
    return pooled * inverse, inverse


def text_up_kernel(h2_ref, wu_ref, wd_ref, sum_ref, *refs):
    slope_ref, hid_ref, unit_ref, inv_ref, acc = refs[-5:]
    step = pl.program_id(0)
    chunk = 320
    per = chunk // TXT_LEN
    pool = pool_matrix(per, chunk, 0, TXT_LEN)
    for k in range(h2_ref.shape[0] // chunk):
        inner = mul(h2_ref[k * chunk : (k + 1) * chunk, :], wu_ref[...])
        value, half = gelu_parts(inner)
        slope = half + inner * (jnp.exp(-0.5 * inner * inner) * 0.3989422804014327)
        slope_ref[k * chunk : (k + 1) * chunk, :] = slope.astype(bf16)
        hid_ref[k * per : (k + 1) * per, :] = mul(pool, value.astype(bf16))
    terms = mul(two_terms(hid_ref[...] * (1.0 / TXT_LEN)), wd_ref[...])
    count = hid_ref.shape[0]
    added = terms[:count] + terms[count:]

    @pl.when(step == 0)
    def _():
        acc[...] = sum_ref[...] * (1.0 / TXT_LEN) + added

    @pl.when(step > 0)
    def _():
        acc[...] += added

    @pl.when(step == pl.num_programs(0) - 1)
    def _():
        unit, inverse = unit_rows(acc[...])
        unit_ref[...] = unit
        inv_ref[...] = jnp.broadcast_to(inverse, inv_ref.shape)


def text_up(normed2, weight_up, weight_down, middle_sum, after=()):
    rows, count = normed2.shape[0], middle_sum.shape[0]
    fixed = lambda shape: pl.BlockSpec(shape, lambda i: (0, 0))
    return pl.pallas_call(
        text_up_kernel,
        grid=(FF // TILE,),
        out_shape=[
            jax.ShapeDtypeStruct((rows, FF), bf16),
            jax.ShapeDtypeStruct((count, FF), f32),
            jax.ShapeDtypeStruct((count, D), f32),
            jax.ShapeDtypeStruct((count, 128), f32),
        ],
        in_specs=[
            fixed((rows, D)),
            pl.BlockSpec((D, TILE), lambda i: (0, i)),
            pl.BlockSpec((TILE, D), lambda i: (i, 0)),
            fixed((count, D)),
        ]
        + anywhere(after),
        out_specs=[
            pl.BlockSpec((rows, TILE), lambda i: (0, i)),
            pl.BlockSpec((count, TILE), lambda i: (0, i)),
            fixed((count, D)),
            fixed((count, 128)),
        ],
        scratch_shapes=[pltpu.VMEM((count, D), f32)],
        compiler_params=params(),
        cost_estimate=cost(2 * rows * D * FF, 4 * D * FF + 2 * rows * FF, 20 * rows * FF),
        name="text_up",
    )(normed2, weight_up, weight_down, middle_sum, *after)


def image_up_kernel(fold, h2_ref, wu_ref, wd_ref, first_ref, sum_ref, early_ref, out_ref, acc, picked):
    step = pl.program_id(0)
    rows, count = h2_ref.shape[0], sum_ref.shape[0]
    part = TILE // fold

    def through_down(summed, groups):
        moved = mul(two_terms(summed * (1.0 / IMG_LEN)), picked[...]).astype(bf16)
        weight = jnp.concatenate([groups[:, k * D : (k + 1) * D] for k in range(fold)], axis=0)
        terms = mul(moved, weight)
        return terms[:count] + terms[count:]

    @pl.when(step == 0)
    def _():
        place = lax.broadcasted_iota(jnp.int32, (TILE, TILE), 0)
        col = lax.broadcasted_iota(jnp.int32, (TILE, TILE), 1)
        source = (col % part) * fold + col // part
        picked[...] = jnp.where(place == source, 1.0, 0.0).astype(bf16)
        total = sum_ref[...] * (1.0 / IMG_LEN)
        for k in range(EARLY // TILE):
            total = total + through_down(
                early_ref[:, k * TILE : (k + 1) * TILE], first_ref[k * part : (k + 1) * part, :]
            )
        acc[...] = total

    value, _ = gelu_parts(mul(h2_ref[...], wu_ref[...]))
    summed = mul(pool_matrix(count, rows, 0, IMG_LEN), value.astype(bf16))
    acc[...] += through_down(summed, wd_ref[...])

    @pl.when(step == pl.num_programs(0) - 1)
    def _():
        unit = unit_rows(acc[...])[0].astype(bf16)
        out_ref[...] = jnp.broadcast_to(unit[None], out_ref.shape)


def image_up(normed2, whole, middle_sum, early, peers):
    rows, count = normed2.shape[0], middle_sum.shape[0]
    fold = FF // D
    before, part = EARLY // TILE, TILE // fold
    fixed = lambda shape: pl.BlockSpec(shape, lambda i: (0, 0))
    return pl.pallas_call(
        functools.partial(image_up_kernel, fold),
        grid=(FF // TILE - before,),
        out_shape=jax.ShapeDtypeStruct((peers, count, D), bf16),
        in_specs=[
            fixed((rows, D)),
            pl.BlockSpec((D, TILE), lambda i: (0, FF // TILE + i)),
            pl.BlockSpec((part, FF), lambda i: (i + before, 0)),
            fixed((before * part, FF)),
            fixed((count, D)),
            fixed((count, EARLY)),
        ],
        out_specs=pl.BlockSpec((peers, count, D), lambda i: (0, 0, 0)),
        scratch_shapes=[pltpu.VMEM((count, D), f32), pltpu.VMEM((TILE, TILE), bf16)],
        compiler_params=params(),
        cost_estimate=cost(2 * rows * D * FF, 4 * D * FF, 15 * rows * FF),
        name="image_up",
    )(normed2, whole, whole, whole, middle_sum, early)


def left_kernel(count, *refs):
    out_ref = refs[-1]
    for k in range(count):
        source_ref, values_ref = refs[2 * k : 2 * k + 2]

        @pl.loop(0, D // 256)
        def _(step, k=k, source_ref=source_ref, values_ref=values_ref):
            at = pl.ds(pl.multiple_of(step * 256, 256), 256)
            picked = mul_bt(chosen(source_ref[at, :]), values_ref[...])
            out_ref[k, at, :] = picked.astype(bf16)


def left_factors(*pairs):
    rows = pairs[0][1].shape[0]
    given = [item for pair in pairs for item in pair]
    return pl.pallas_call(
        functools.partial(left_kernel, len(pairs)),
        out_shape=jax.ShapeDtypeStruct((len(pairs), D, rows), bf16),
        in_specs=in_vmem(len(given)),
        out_specs=pl.BlockSpec(memory_space=pltpu.VMEM),
        compiler_params=params(24 << 20),
        cost_estimate=cost(2 * len(pairs) * rows * D * D, 4 * len(pairs) * rows * D),
        name="left_factors",
    )(*given)


def loss_parts(text_rows, pos, image_all):
    similar = mul_bt(text_rows, image_all) * logit_scale
    shifted = jnp.exp(similar - logit_scale)
    alive = jnp.max(pos, axis=1, keepdims=True)
    row_sum = jnp.sum(shifted, axis=1, keepdims=True)
    row_count = jnp.maximum(jnp.sum(pos, axis=1, keepdims=True), 1.0)
    return similar, shifted, alive, row_sum, row_count


def sums_over_captions(text_rows, pos, image_all):
    similar, shifted, alive, row_sum, row_count = loss_parts(text_rows, pos, image_all)
    pos_similar = pos * similar
    cap_term = alive * (
        logit_scale + jnp.log(row_sum) - jnp.sum(pos_similar, axis=1, keepdims=True) / row_count
    )
    return (
        jnp.sum(alive * shifted, axis=0, keepdims=True),
        jnp.sum(pos, axis=0, keepdims=True),
        jnp.sum(pos_similar, axis=0, keepdims=True),
        jnp.sum(cap_term, axis=0, keepdims=True),
        jnp.sum(alive, axis=0, keepdims=True),
    )


def loss_from(sums):
    col_sum, col_count, col_pos, cap_total, live_total = sums
    img_term = logit_scale + jnp.log(col_sum) - col_pos / col_count
    return 0.5 * cap_total / live_total + 0.5 * jnp.mean(img_term, axis=1, keepdims=True)


def grad_of_unit(text_rows, pos, image_all, col_sum, col_count, live_total):
    _, shifted, alive, row_sum, row_count = loss_parts(text_rows, pos, image_all)
    cap_share, img_share = 0.5 / live_total, 0.5 / image_all.shape[0]
    grad_sims = alive * shifted * (cap_share / row_sum + img_share / col_sum) - pos * (
        cap_share / row_count + img_share / col_count
    )
    return mul(grad_sims.astype(bf16), image_all) * logit_scale


def turned(grad, unit):
    return grad - unit * jnp.sum(grad * unit, axis=-1, keepdims=True)


def loss_into(
    pack_ref, image_ref, own_ref, unit_ref, inv_ref, loss_ref, row_ref, low_ref, col_sum_ref,
    col_count_ref, live_ref
):
    image_all = image_ref[...]
    chunk = 256
    total = None
    for k in range(pack_ref.shape[0] // chunk):
        at = slice(k * chunk, (k + 1) * chunk)
        part = sums_over_captions(pack_ref[at, :D], pack_ref[at, D:].astype(f32), image_all)
        total = part if total is None else [a + b for a, b in zip(total, part)]
    loss_ref[...] = jnp.broadcast_to(loss_from(total), loss_ref.shape)
    col_sum, col_count, _, _, live_total = total
    col_sum_ref[...] = col_sum
    col_count_ref[...] = col_count
    live_ref[...] = jnp.broadcast_to(live_total, live_ref.shape)
    grad = grad_of_unit(
        own_ref[:, :D], own_ref[:, D:].astype(f32), image_all, col_sum, col_count, live_total
    )
    row = inv_ref[:, :1] * turned(grad, unit_ref[...]) * (1.0 / TXT_LEN)
    row_ref[...] = row
    low_ref[...] = row.astype(bf16)


def down_kernel(pack_ref, image_ref, col_sum_ref, col_count_ref, live_ref, hid_ref, *refs):
    step, out_ref = pl.program_id(0), refs[-1]
    text_rows = pack_ref[:, :D]
    grad = grad_of_unit(
        text_rows, pack_ref[:, D:].astype(f32), image_ref[...], col_sum_ref[...],
        col_count_ref[...], live_ref[:, :1]
    )
    rows = (turned(grad, text_rows.astype(f32)) * (1.0 / TXT_LEN)).astype(bf16)
    part = mul_at(hid_ref[...], rows)

    @pl.when(step == 0)
    def _():
        out_ref[...] = part

    @pl.when(step > 0)
    def _():
        out_ref[...] += part


def grad_of_down(pack, image_all, col_sum, col_count, live_total, hidden_cols, after):
    images, chunk = image_all.shape[0], 256
    fixed = lambda shape: pl.BlockSpec(shape, lambda i: (0, 0))
    per = hidden_cols.shape[1]
    return pl.pallas_call(
        down_kernel,
        grid=(pack.shape[0] // chunk,),
        out_shape=jax.ShapeDtypeStruct((per, D), f32),
        in_specs=[
            pl.BlockSpec((chunk, pack.shape[1]), lambda i: (i, 0)),
            fixed((images, D)), fixed((1, images)), fixed((1, images)), fixed((1, 128)),
            pl.BlockSpec((chunk, per), lambda i: (i, 0)),
        ]
        + anywhere(after),
        out_specs=fixed((per, D)),
        compiler_params=params(16 << 20),
        cost_estimate=cost(4 * pack.shape[0] * images * D, 2 * pack.size, pack.shape[0] * images),
        name="grad_of_down",
    )(pack, image_all, col_sum, col_count, live_total, hidden_cols, *after)


def mlp_back_kernel(with_loss, gain_ref, *refs):
    given, refs = (refs[:5], refs[5:]) if with_loss else (refs[:2], refs[2:])
    wd_hbm, slope_hbm, wu_hbm, lhs_hbm, mid_hbm = refs[:5]
    keep_a, send_a, keep_b, send_b, out_ref, sums_out = refs[5:11]
    wd_ref, slope_ref, wu_ref, lhs_ref, mid_ref, sems, whole_sems = refs[-7:]
    low_ref, row_ref = refs[-9:-7] if with_loss else given
    count, rows = low_ref.shape[0], out_ref.shape[0]
    half, steps = D // 2, FF // 2 // TILE

    def copies(tile, slot):
        at = pl.ds(pl.multiple_of(tile * TILE, TILE), TILE)
        return (
            pltpu.make_async_copy(wd_hbm.at[at, :], wd_ref.at[slot], sems.at[0, slot]),
            pltpu.make_async_copy(slope_hbm.at[:, at], slope_ref.at[slot], sems.at[1, slot]),
            pltpu.make_async_copy(wu_hbm.at[:, at], wu_ref.at[slot], sems.at[2, slot]),
        )

    lhs_copy = pltpu.make_async_copy(lhs_hbm, lhs_ref, whole_sems.at[0])
    mid_copy = pltpu.make_async_copy(mid_hbm, mid_ref, whole_sems.at[1])
    for copy in copies(0, 0):
        copy.start()
    lhs_copy.start()
    if with_loss:
        loss_ref, *stats = refs[11:15]
        loss_into(*given, loss_ref, row_ref, low_ref, *stats)
    for k, (keep, send) in enumerate(((keep_a, send_a), (keep_b, send_b))):

        @pl.loop(0, steps)
        def _(step, k=k, keep=keep, send=send):
            tile = k * steps + step
            slot = lax.rem(tile, 2)

            @pl.when(tile + 1 < 2 * steps)
            def _():
                for copy in copies(tile + 1, 1 - slot):
                    copy.start()

            for copy in copies(tile, slot):
                copy.wait()
            if k == 0:

                @pl.when(step == 0)
                def _():
                    lhs_copy.wait()
                    mid_copy.start()

            there = pl.ds(pl.multiple_of(step * TILE, TILE), TILE)
            hidden = mul_bt(low_ref[...], wd_ref[slot])
            wide = jnp.broadcast_to(hidden[:, None, :], (count, TXT_LEN, TILE))
            inner = (wide.reshape(rows, TILE) * slope_ref[slot].astype(f32)).astype(bf16)
            weight = mul(lhs_ref[k], inner).astype(bf16)
            keep[:, there] = weight[:half]
            send[:, there] = weight[half:]
            added = mul_bt(inner, wu_ref[slot])
            if k == 0:

                @pl.when(step == 0)
                def _():
                    out_ref[...] = added

                @pl.when(step > 0)
                def _():
                    out_ref[...] += added
            else:
                out_ref[...] += added

    chunk = 128
    per = chunk // TXT_LEN
    gain = line(gain_ref)
    sums_out[...] = jnp.zeros_like(sums_out)
    mid_copy.wait()

    @pl.loop(0, rows // chunk)
    def _(k):
        at = pl.ds(pl.multiple_of(k * chunk, chunk), chunk)
        unit, scale = norm_parts(mid_ref[at, :])
        grad = out_ref[at, :]
        sums_out[:, :D] += jnp.sum(grad * unit, axis=0, keepdims=True)
        sums_out[:, D:] += jnp.sum(grad, axis=0, keepdims=True)
        row = row_ref[pl.ds(pl.multiple_of(k * per, per), per), :]
        row = jnp.broadcast_to(row[:, None, :], (per, TXT_LEN, D)).reshape(chunk, D)
        out_ref[at, :] = row + norm_back(unit, scale, gain, grad)


def mlp_back(given, weight_down, slope, weight_up, lhs, middle, gain):
    rows, count = slope.shape[0], given[-2].shape[0]
    with_loss = len(given) == 5
    shapes = [stays((D // 2, FF // 2), bf16)] * 4 + [stays((rows, D), f32), stays((1, 2 * D), f32)]
    scratch = [
        pltpu.VMEM((2, TILE, D), bf16),
        pltpu.VMEM((2, rows, TILE), bf16),
        pltpu.VMEM((2, D, TILE), bf16),
        pltpu.VMEM((2, D, rows), bf16),
        pltpu.VMEM((rows, D), f32),
        pltpu.SemaphoreType.DMA((3, 2)),
        pltpu.SemaphoreType.DMA((2,)),
    ]
    if with_loss:
        images = given[1].shape[0]
        wide = [(1, 128), (1, images), (1, images), (1, 128)]
        shapes += [jax.ShapeDtypeStruct(shape, f32) for shape in wide]
        scratch = [pltpu.VMEM((count, D), bf16), pltpu.VMEM((count, D), f32)] + scratch
    return pl.pallas_call(
        functools.partial(mlp_back_kernel, with_loss),
        out_shape=shapes,
        in_specs=in_vmem(1 + len(given)) + [pl.BlockSpec(memory_space=pltpu.HBM)] * 5,
        out_specs=in_vmem(len(shapes)),
        scratch_shapes=scratch,
        compiler_params=params(32 << 20),
        cost_estimate=cost(4 * rows * D * FF, 4 * D * FF + 2 * rows * FF + 2 * D * FF, rows * FF),
        name="mlp_back",
    )(gain, *given, *in_hbm(weight_down, slope, weight_up, lhs, middle))


def attention_back_kernel(first, grad_ref, wo_ref, qkv_ref, lse_ref, *refs):
    low_ref, out_ref = refs[-2:]
    chunk = 128
    mask = same_sequence(chunk, 0, chunk, 0, TXT_LEN)

    @pl.loop(0, low_ref.shape[0] // chunk)
    def _(step):
        here = pl.ds(pl.multiple_of((first + step) * chunk, chunk), chunk)
        there = pl.ds(pl.multiple_of(step * chunk, chunk), chunk)
        sums = lse_ref[pl.ds(pl.multiple_of((first + step) * 16, 16), 16), :]
        low = grad_ref[here, :].astype(bf16)
        low_ref[there, :] = low
        grad_att = mul_bt(low, wo_ref[...]).astype(bf16)
        for pair in range(HEADS // 2):
            queries = qkv_ref[here, pair_cols(0, pair)] * bf16(HEAD ** (-0.5))
            keys = two_heads(qkv_ref[here, pair_cols(1, pair)])
            vals = two_heads(qkv_ref[here, pair_cols(2, pair)])
            grads = grad_att[:, pair_cols(0, pair)]
            scores, grad_probs = mul_bt(keys, queries), mul_bt(vals, grads)
            probs, grad_scores = [], []
            for k in range(2):
                at = slice(k * chunk, (k + 1) * chunk)
                head = 2 * pair + k
                shifted = scores[at] - sums[head : head + 1, :]
                prob = jnp.where(mask, jnp.exp(jnp.where(mask, shifted, 0.0)), 0.0)
                along = jnp.sum(grad_probs[at] * prob, axis=0, keepdims=True)
                grad_scores.append((prob * (grad_probs[at] - along)).astype(bf16))
                probs.append(prob.astype(bf16))
            grad_q = mul_at(jnp.concatenate(grad_scores, axis=0), keys) * HEAD ** (-0.5)
            grad_k = mul(jnp.concatenate(grad_scores, axis=1), two_heads(queries))
            grad_v = mul(jnp.concatenate(probs, axis=1), two_heads(grads))
            out_ref[there, pair_cols(0, pair)] = grad_q.astype(bf16)
            out_ref[there, pair_cols(1, pair)] = grad_k.astype(bf16)
            out_ref[there, pair_cols(2, pair)] = grad_v.astype(bf16)


def attention_back(grad_middle, weight_out, project, log_sums, first, count, after=()):
    rows = count * 128
    return pl.pallas_call(
        functools.partial(attention_back_kernel, first),
        out_shape=[stays((rows, D), bf16), stays((rows, 3 * D), bf16)],
        in_specs=in_vmem(4) + anywhere(after),
        out_specs=in_vmem(2),
        compiler_params=params(16 << 20),
        cost_estimate=cost(10 * rows * D * D, 16 * rows * D + 2 * D * D, rows * 128 * HEADS),
        name="attention_back",
    )(grad_middle, weight_out, project, log_sums, *after)


def mul_rows(lhs, parts, cols):
    total, row = 0.0, 0
    for part in parts:
        total = total + mul(lhs[:, row : row + part.shape[0]], part[:, cols])
        row += part.shape[0]
    return total


def weight_back_kernel(factors, groups, lhs_ref, *refs):
    keep_a, send_a, keep_b, send_b = refs[-4:]
    half = D // 2
    for k, (factor, group, col) in enumerate(factors):
        parts = refs[sum(groups[:group]) : sum(groups[: group + 1])]
        weight = mul_rows(lhs_ref.at[factor], parts, slice(col * D, (col + 1) * D)).astype(bf16)
        at = slice(k % 2 * D, (k % 2 + 1) * D)
        (keep_b if k > 1 else keep_a)[:, at] = weight[:half]
        (send_b if k > 1 else send_a)[:, at] = weight[half:]


def weight_back(lhs, groups, factors, after=()):
    rows = lhs.shape[2]
    given = [part for group in groups for part in group]
    return pl.pallas_call(
        functools.partial(weight_back_kernel, factors, [len(group) for group in groups]),
        out_shape=[stays((D // 2, 2 * D), bf16)] * 4,
        in_specs=in_vmem(1 + len(given)) + anywhere(after),
        out_specs=in_vmem(4),
        compiler_params=params(16 << 20),
        cost_estimate=cost(8 * rows * D * D, 8 * rows * D + 14 * D * D),
        name="weight_back",
    )(lhs, *given, *after)


def input_back_kernel(count, *refs):
    projs = refs[:count]
    w_ref, x_ref, gain_ref, mid_ref, sums_ref = refs[count : count + 5]
    out_ref, sums_out = refs[-2:]
    rows, chunk = x_ref.shape[0], 128

    @pl.loop(0, D // 256)
    def _(step):
        at = pl.ds(pl.multiple_of(step * 256, 256), 256)
        row = 0
        for part in projs:
            there = slice(row, row + part.shape[0])
            out_ref[there, at] = mul_bt(part[...], w_ref[at, :])
            row += part.shape[0]

    gain = line(gain_ref)
    sums_out[...] = jnp.zeros_like(sums_out)
    sums_out[1:2, :] = sums_ref[...]

    @pl.loop(0, rows // chunk)
    def _(k):
        at = pl.ds(pl.multiple_of(k * chunk, chunk), chunk)
        unit, scale = norm_parts(x_ref[at, :].astype(f32))
        grad = out_ref[at, :]
        sums_out[0:1, :D] += jnp.sum(grad * unit, axis=0, keepdims=True)
        sums_out[0:1, D:] += jnp.sum(grad, axis=0, keepdims=True)
        out_ref[at, :] = mid_ref[at, :] + norm_back(unit, scale, gain, grad)


def input_back(grad_projs, weight, rows_in, gain, grad_middle, sums, after=()):
    rows = rows_in.shape[0]
    return pl.pallas_call(
        functools.partial(input_back_kernel, len(grad_projs)),
        out_shape=[jax.ShapeDtypeStruct((rows, D), f32), stays((8, 2 * D), f32)],
        in_specs=in_vmem(len(grad_projs) + 5) + anywhere(after),
        out_specs=in_vmem(2),
        compiler_params=params(16 << 20),
        cost_estimate=cost(6 * rows * D * D, 14 * rows * D + 6 * D * D),
        name="input_back",
    )(*grad_projs, weight, rows_in, gain, grad_middle, sums, *after)


def local(
    images,
    captions,
    img_gain1,
    img_bias1,
    img_qkv,
    img_out,
    img_gain2,
    img_bias2,
    img_up,
    img_down,
    txt_gain1,
    txt_bias1,
    txt_qkv,
    txt_out,
    txt_gain2,
    txt_bias2,
    txt_up,
    txt_down,
    counts,
    matches,
):
    peers = lax.axis_size(AXIS)
    own = lax.axis_index(AXIS)
    per = D // peers
    img_local = counts.shape[0]
    cap_local = matches.shape[0]
    total_images = matches.shape[1]

    up_rows = img_up.reshape(per, FF)
    whole = lax.all_gather(
        jnp.concatenate([img_down.reshape(per, FF), up_rows[:, EARLY:]], axis=1),
        AXIS,
        axis=0,
        tiled=True,
    )
    small = peers == 32
    shard = jnp.concatenate(
        [img_qkv.reshape(per, 3 * D), img_out.reshape(per, D), up_rows[:, :EARLY]], axis=1
    )
    if small:
        line, source = gathered_line(shard), row_order((1, 4, 2, 16, 8))
    else:
        line, source = lax.all_gather(shard, AXIS, axis=0, tiled=True), row_order(())

    normed1, project, attended, middle, normed2, middle_sum, log_sums = text_front(
        captions, txt_gain1, txt_bias1, txt_qkv, txt_out, txt_gain2, txt_bias2
    )
    middle_sum, line = in_turn(middle_sum, line)
    beside, above = (swapped(line, 2), swapped(line, 4)) if small else (line, line)
    slope, hidden_sum, text_unit, inverse = text_up(
        normed2, txt_up, txt_down, middle_sum, (line,)
    )
    text_unit, normed2, beside, above = lax.optimization_barrier(
        (text_unit, normed2, beside, above)
    )

    ends_at = jnp.cumsum(counts)
    slot_ids = lax.iota(jnp.int32, cap_local)
    owner = jnp.sum((ends_at[None, :] <= slot_ids[:, None]).astype(jnp.int32), axis=1)
    owner = owner + own * img_local
    live = slot_ids < ends_at[-1]
    columns = lax.iota(jnp.int32, total_images)
    positive = ((matches > 0) | (owner[:, None] == columns[None, :])) & live[:, None]

    order_a, order_b, tail = stage_orders()
    source_a, source_b = row_order(order_a + tail[::-1]), row_order(order_b + tail[::-1])
    own_pack = packed(text_unit, positive.astype(bf16), ())
    lhs_up = left_factors((source_a, normed2), (source_b, normed2))
    pieces = [line]
    if small:
        first, second = diagonal(beside, above)
        own_pack, first, second, lhs_up = lax.optimization_barrier(
            (own_pack, first, second, lhs_up)
        )
        held = own_pack[None]
        others = [swapped(held, mask) for mask in (8, 16, 24)]
        pieces = [line, beside, above, first, second]
        pieces = pieces + [swapped(piece, 1) for piece in pieces]

    normed_img, middle_img, early = image_front(
        images, pieces, source, img_gain1, img_bias1, img_gain2, img_bias2
    )
    if small:
        scaled_sum = (hidden_sum * inverse[:, :1]).astype(bf16)
        normed_img, scaled_sum, others = lax.optimization_barrier((normed_img, scaled_sum, others))
        held = joined(joined(held, others[0], 8), joined(others[1], others[2], 8), 16, 1)
        text_beside, text_above = swapped(held, 2), swapped(held, 4)
        hidden_cols = lax.all_to_all(scaled_sum, AXIS, split_axis=1, concat_axis=0, tiled=True)
        normed_img, text_beside, text_above = lax.optimization_barrier(
            (normed_img, text_beside, text_above)
        )
        halves = diagonal(text_beside, text_above)
    image_low = image_up(normed_img, whole, middle_img, early, peers)
    if small:
        image_low, halves, hidden_cols = lax.optimization_barrier((image_low, halves, hidden_cols))
        across = jnp.concatenate(halves, axis=0)
        held = joined(joined(held, text_beside, 2), joined(text_above, across, 2), 4, 4)
        text_pack = joined(held, swapped(held, 1), 1).reshape(-1, D + total_images)
    image_all = exchanged(image_low).reshape(total_images, D)
    if small:
        image_all, text_pack = in_turn(image_all, text_pack)

    if small:
        given = (text_pack, image_all, own_pack, text_unit, inverse)
    else:
        text_low, pos = own_pack[:, :D], own_pack[:, D:].astype(f32)
        totals = lax.psum(sums_over_captions(text_low, pos, image_all), AXIS)
        loss_value = loss_from(totals)
        grad = grad_of_unit(text_low, pos, image_all, totals[0], totals[1], totals[4])
        grad_row = inverse[:, :1] * turned(grad, text_unit) * (1.0 / TXT_LEN)
        row_low = grad_row.astype(bf16)
        given = (row_low, grad_row)

    *up, grad_middle, sums = mlp_back(given, txt_down, slope, txt_up, lhs_up, middle, txt_gain2)
    if small:
        *up, grad_middle, sums, loss_value, col_sum, col_count, live_total = (
            *up, grad_middle, sums
        )
    stages = len(order_a)
    low_one, proj_one = attention_back(grad_middle, txt_out, project, log_sums, 0, 2)
    for stage in range(stages - 2):
        up = fold(hand_on(up, stage), (proj_one,))
    low_two, proj_two = attention_back(grad_middle, txt_out, project, log_sums, 2, 3, up)
    proj_two, normed1 = in_turn(proj_two, normed1)
    lhs_rest = left_factors((source_a, normed1), (source_b, normed1), (source_b, attended))
    up = fold(hand_on(up, stages - 2), (proj_two, lhs_rest))
    projs, lows = (proj_one, proj_two), (low_one, low_two)
    rest = weight_back(lhs_rest, [projs, lows], [(0, 0, 0), (0, 0, 1), (1, 0, 2), (2, 1, 0)], up)
    up = hand_on(up, stages - 1)
    caption_grad, sums = input_back(
        projs, txt_qkv, captions, txt_gain1, grad_middle, sums, rest[:1]
    )
    caption_grad, up = in_turn(caption_grad, up)
    up = fold_last(up)
    if small:
        *rest, sums = fold(hand_on(rest, 0), up[:1], (sums, swapped(sums, 1)))
    else:
        norms = lax.psum(sums, AXIS)[:2].reshape(-1)
        for stage in range(stages - 2):
            rest = fold(hand_on(rest, stage), up[:1])
    up = hand_on_last(up)
    rest = hand_on(rest, stages - 2)
    if small:
        grad_down = grad_of_down(
            text_pack, image_all, col_sum, col_count, live_total, hidden_cols, (caption_grad,)
        )
    else:
        grad_down = lax.psum_scatter(
            mul_at(hidden_sum.astype(bf16), row_low), AXIS, scatter_dimension=0, tiled=True
        )
    grad_down, rest, up = lax.optimization_barrier((grad_down, rest, up))
    if small:
        *rest, sums = fold(rest, (), (sums,))
        rest = fold_last(hand_on(rest, stages - 1), (), (sums,))
    else:
        rest = fold_last(hand_on(fold(rest), stages - 1))
    up_share = sum_last(*up)
    rest_share = sum_last(*hand_on_last(rest))
    if small:
        norms = rest_share[per]
        rest_share = rest_share[:per]
    return (
        loss_value[0, 0],
        caption_grad,
        norms[:D],
        norms[D : 2 * D],
        rest_share[:, : 3 * D].reshape(-1),
        rest_share[:, 3 * D :].reshape(-1),
        norms[2 * D : 3 * D],
        norms[3 * D :],
        up_share.reshape(-1),
        grad_down.reshape(-1),
    )


def solution(mesh):
    split, flat, whole = P("blk", None), P("blk"), P()
    image_block = (whole, whole, flat, flat, whole, whole, flat, flat)
    return jax.shard_map(
        local,
        mesh=mesh,
        in_specs=(split, split) + image_block + (whole,) * 8 + (flat, split),
        out_specs=(whole, split, whole, whole, flat, flat, whole, whole, flat, flat),
        check_vma=False,
    )
```

```python
import functools

import jax
import jax.numpy as jnp
from jax import lax
from jax.experimental import pallas as pl
from jax.experimental.pallas import tpu as pltpu
from jax.sharding import PartitionSpec as P

D = 768
FF = 3072
HEAD = 64
HEADS = D // HEAD
IMG_LEN = 50
TXT_LEN = 16
AXIS = "blk"

norm_eps = 1e-06
logit_scale = 50.0
f32 = jnp.float32
bf16 = jnp.bfloat16


def swapped(value, mask):
    peers = lax.axis_size(AXIS)
    return lax.ppermute(value, AXIS, [(i, i ^ mask) for i in range(peers)])


def bit_masks():
    peers = lax.axis_size(AXIS)
    return [1 << k for k in range(peers.bit_length() - 1)]


def joined(held, other, mask, outer=None):
    upper = (lax.axis_index(AXIS) & mask) > 0
    first = jnp.where(upper, other, held)
    second = jnp.where(upper, held, other)
    outer = held.shape[0] if outer is None else outer
    parts = [part.reshape((outer, -1) + held.shape[1:]) for part in (first, second)]
    return jnp.stack(parts, axis=1).reshape((-1,) + held.shape[1:])


def exchanged(copies):
    return lax.all_to_all(copies, AXIS, split_axis=0, concat_axis=0, tiled=True)


def stage_orders():
    masks = bit_masks()
    head, tail = masks[:-2], masks[-2:]
    order_a = list(head)
    order_b = list(head)
    for k in range(1, len(head) - 1, 2):
        order_b[k], order_b[k + 1] = order_b[k + 1], order_b[k]
    return order_a, order_b, tail


def row_order(bits):
    peers = lax.axis_size(AXIS)
    own = lax.axis_index(AXIS)
    per = D // peers
    places = lax.broadcasted_iota(jnp.int32, (D, 1), 0)
    block = places // per
    target = jnp.zeros_like(block) + own
    for k, mask in enumerate(bits):
        target = target ^ (((block >> (len(bits) - 1 - k)) & 1) * mask)
    return target * per + places % per


def chosen(source):
    column = lax.broadcasted_iota(jnp.int32, (source.shape[0], D), 1)
    return jnp.where(column == source, 1.0, 0.0).astype(bf16)


def gathered_line(shard):
    return jnp.concatenate([shard] + [swapped(shard, mask) for mask in (8, 16, 24)], axis=0)


def diagonal(beside, above):
    half = beside.shape[0] // 2
    return swapped(beside[:half], 4), swapped(above[half:], 2)


def in_turn(first, then):
    return lax.optimization_barrier((first, then))


def hand_on(parts, stage):
    order_a, order_b, _ = stage_orders()
    keep_a, send_a, keep_b, send_b = parts
    return keep_a, swapped(send_a, order_a[stage]), keep_b, swapped(send_b, order_b[stage])


def hand_on_last(blocks):
    low, high = stage_orders()[2]
    own, *others = blocks
    return own, [swapped(block, mask) for block, mask in zip(others, (low, high, low | high))]


def sum_last(own, others):
    total = own
    for other in others:
        total = total + other.astype(f32)
    return total


VMEM_BYTES = 56 << 20
TILE = 512
EARLY = TILE


def norm_parts(values):
    average = jnp.mean(values, axis=-1, keepdims=True)
    centred = values - average
    variance = jnp.mean(centred * centred, axis=-1, keepdims=True)
    scale = lax.rsqrt(variance + norm_eps)
    return centred * scale, scale


def norm_back(unit, scale, gain, grad):
    inner = grad * gain
    shift = jnp.mean(inner, axis=-1, keepdims=True)
    along = jnp.mean(inner * unit, axis=-1, keepdims=True)
    return scale * (inner - shift - unit * along)


def mul(lhs, rhs):
    return jnp.dot(lhs, rhs, preferred_element_type=f32)


def mul_bt(lhs, rhs):
    return lax.dot_general(lhs, rhs, (((1,), (1,)), ((), ())), preferred_element_type=f32)


def mul_at(lhs, rhs):
    return lax.dot_general(lhs, rhs, (((0,), (0,)), ((), ())), preferred_element_type=f32)


def params(limit=VMEM_BYTES):
    return pltpu.CompilerParams(vmem_limit_bytes=limit)


def in_vmem(count):
    return [pl.BlockSpec(memory_space=pltpu.VMEM)] * count


def in_hbm(*arrays):
    return [pltpu.with_memory_space_constraint(array, pltpu.HBM) for array in arrays]


def stays(shape, dtype):
    return pltpu.VMEM(shape, dtype)


def cost(flops, moved, transcendentals=0):
    return pl.CostEstimate(flops=flops, bytes_accessed=moved, transcendentals=transcendentals)


def lane_halves(dtype):
    lane = lax.broadcasted_iota(jnp.int32, (1, 2 * HEAD), 1)
    low = jnp.where(lane < HEAD, 1.0, 0.0)
    return low.astype(dtype), (1.0 - low).astype(dtype)


def two_heads(pair):
    low, high = lane_halves(bf16)
    return jnp.concatenate([pair * low, pair * high], axis=0)


def same_sequence(rows, row0, cols, col0, seq_len):
    row = (lax.broadcasted_iota(jnp.int32, (rows, cols), 0) + row0) // seq_len
    col = (lax.broadcasted_iota(jnp.int32, (rows, cols), 1) + col0) // seq_len
    return row == col


def softmax_down(scores, mask):
    keys = mask.shape[0]
    parts, sums = [], []
    for k in range(2):
        part = jnp.where(mask, scores[k * keys : (k + 1) * keys], -1e30)
        most = jnp.max(part, axis=0, keepdims=True)
        raised = jnp.exp(part - most)
        total = jnp.sum(raised, axis=0, keepdims=True)
        parts.append(raised * (1.0 / total))
        sums.append(most + jnp.log(total))
    return parts, sums


def fold_kernel(extra, keep_a, got_a, keep_b, got_b, *refs):
    outs = refs[-5:] if extra else refs[-4:]
    rows, half, tile = keep_a.shape[0], keep_a.shape[0] // 2, 256

    @pl.loop(0, keep_a.shape[1] // tile)
    def _(step):
        cols = pl.ds(pl.multiple_of(step * tile, tile), tile)
        for k, (kept, got) in enumerate(((keep_a, got_a), (keep_b, got_b))):
            for j in range(2):
                at = slice(j * half, (j + 1) * half)
                total = kept[at, cols].astype(f32) + got[at, cols].astype(f32)
                outs[2 * k + j][:half, cols] = total.astype(bf16)

    if extra:
        came = refs[1][...] if extra > 1 else got_a[rows : rows + 16, :].astype(f32)[:8]
        sums = refs[0][...] + came
        outs[4][...] = sums
        outs[1][half : half + 16, :] = jnp.concatenate([sums, sums], axis=0).astype(bf16)


def fold(parts, after=(), sums=()):
    rows, cols = parts[0].shape
    if rows % 32:
        whole = [
            (kept.astype(f32) + got.astype(f32)).astype(bf16)
            for kept, got in (parts[:2], parts[2:])
        ]
        return [part for one in whole for part in (one[: rows // 2], one[rows // 2 :])]
    half = (rows // 2, cols)
    shapes = [stays(half, bf16)] * 4
    if sums:
        shapes[1] = stays((rows // 2 + 16, cols), bf16)
        shapes.append(stays((8, cols), f32))
    return pl.pallas_call(
        functools.partial(fold_kernel, len(sums)),
        out_shape=shapes,
        in_specs=in_vmem(4 + len(sums)) + anywhere(after),
        out_specs=in_vmem(len(shapes)),
        compiler_params=params(8 << 20),
        cost_estimate=cost(2 * rows * cols, 12 * rows * cols),
        name="fold",
    )(*parts, *sums, *after)


def fold_last_kernel(extra, keep_a, got_a, keep_b, got_b, *refs):
    outs = refs[-4:]
    cols = keep_a.shape[1]
    rows = keep_a.shape[0] // 4
    if extra:
        sums = refs[0][...] + got_a[4 * rows : 4 * rows + 16, :].astype(f32)[:8]
    for k, (kept, got) in enumerate(((keep_a, got_a), (keep_b, got_b))):
        total = kept[...].astype(f32) + got[: 4 * rows, :].astype(f32)
        at = slice(k * cols, (k + 1) * cols)
        for j, out in enumerate(outs):
            part = total[j * rows : (j + 1) * rows]
            if extra:
                row = jnp.broadcast_to(sums[k : k + 1], (8, cols))
                part = jnp.concatenate([part, row], axis=0)
            out[:, at] = part.astype(out.dtype)


def fold_last(parts, after=(), sums=()):
    rows, cols = parts[0].shape
    shape = (rows // 4 + (8 if sums else 0), 2 * cols)
    if rows % 32:
        pairs = (parts[:2], parts[2:])
        both = [kept.astype(f32) + got.astype(f32) for kept, got in pairs]
        own, *others = jnp.split(jnp.concatenate(both, axis=1), 4)
        return [own] + [other.astype(bf16) for other in others]
    return pl.pallas_call(
        functools.partial(fold_last_kernel, len(sums)),
        out_shape=[stays(shape, f32)] + [stays(shape, bf16)] * 3,
        in_specs=in_vmem(4 + len(sums)) + anywhere(after),
        out_specs=in_vmem(4),
        compiler_params=params(8 << 20),
        cost_estimate=cost(2 * rows * cols, 12 * rows * cols),
        name="fold_last",
    )(*parts, *sums, *after)


def anywhere(after):
    return [pl.BlockSpec(memory_space=pl.ANY)] * len(after)


def pair_cols(part, pair):
    start = part * D + pair * 2 * HEAD
    return slice(start, start + 2 * HEAD)


def line(ref):
    return ref[...].astype(f32).reshape(1, -1)


def norm_rows(src, dst, gain, bias, step_rows):
    @pl.loop(0, src.shape[0] // step_rows)
    def _(step):
        at = pl.ds(pl.multiple_of(step * step_rows, step_rows), step_rows)
        unit, _ = norm_parts(src[at, :].astype(f32))
        dst[at, :] = (unit * gain + bias).astype(bf16)


def attend_along(qkv_ref, att_ref, q_rows, k_rows, mask):
    low, high = lane_halves(f32)
    for pair in range(HEADS // 2):
        queries = two_heads(qkv_ref[q_rows, pair_cols(0, pair)] * bf16(HEAD ** (-0.5)))
        scores = mul_bt(queries, qkv_ref[k_rows, pair_cols(1, pair)])
        scores = jnp.where(mask, scores, -1e30)
        raised = jnp.exp(scores - jnp.max(scores, axis=-1, keepdims=True))
        probs = (raised * (1.0 / jnp.sum(raised, axis=-1, keepdims=True))).astype(bf16)
        half = probs.shape[0] // 2
        mixed = mul(probs, qkv_ref[k_rows, pair_cols(2, pair)])
        att_ref[q_rows, pair_cols(0, pair)] = (mixed[:half] * low + mixed[half:] * high).astype(bf16)


def attend(qkv_ref, att_ref, q_rows, k_rows, mask, keep_sums):
    for pair in range(HEADS // 2):
        queries = qkv_ref[q_rows, pair_cols(0, pair)] * bf16(HEAD ** (-0.5))
        scores = mul_bt(two_heads(qkv_ref[k_rows, pair_cols(1, pair)]), queries)
        probs, sums = softmax_down(scores, mask)
        vals = two_heads(qkv_ref[k_rows, pair_cols(2, pair)])
        mixed = mul_at(jnp.concatenate(probs, axis=0).astype(bf16), vals)
        att_ref[q_rows, pair_cols(0, pair)] = mixed.astype(bf16)
        for k in range(2):
            keep_sums(2 * pair + k, sums[k])


def text_front_kernel(
    x_ref, g1_ref, b1_ref, wqkv_ref, wo_ref, g2_ref, b2_ref, h1_ref, qkv_ref, att_ref, mid_ref,
    h2_ref, sum_ref, lse_ref
):
    rows, chunk = x_ref.shape[0], 128
    norm_rows(x_ref, h1_ref, line(g1_ref), line(b1_ref), chunk)

    @pl.loop(0, 3 * D // 256)
    def _(step):
        at = pl.ds(pl.multiple_of(step * 256, 256), 256)
        qkv_ref[:, at] = mul(h1_ref[...], wqkv_ref[:, at]).astype(bf16)

    mask = same_sequence(chunk, 0, chunk, 0, TXT_LEN)

    @pl.loop(0, rows // chunk)
    def _(step):
        at = pl.ds(pl.multiple_of(step * chunk, chunk), chunk)

        def keep_sums(head, value):
            lse_ref[pl.ds(step * 16 + head, 1), :] = value

        attend(qkv_ref, att_ref, at, at, mask, keep_sums)

    @pl.loop(0, D // 256)
    def _(step):
        at = pl.ds(pl.multiple_of(step * 256, 256), 256)
        mid_ref[:, at] = x_ref[:, at].astype(f32) + mul(att_ref[...], wo_ref[:, at])

    norm_rows(mid_ref, h2_ref, line(g2_ref), line(b2_ref), chunk)
    per = chunk // TXT_LEN

    @pl.loop(0, rows // chunk)
    def _(step):
        values = mid_ref[pl.ds(pl.multiple_of(step * chunk, chunk), chunk), :]
        sum_ref[pl.ds(pl.multiple_of(step * per, per), per), :] = jnp.sum(
            values.reshape(per, TXT_LEN, D), axis=1
        )


def text_front(rows_in, gain1, bias1, wqkv, wo, gain2, bias2):
    rows = rows_in.shape[0]
    shapes = [
        ((rows, D), bf16),
        ((rows, 3 * D), bf16),
        ((rows, D), bf16),
        ((rows, D), f32),
        ((rows, D), bf16),
        ((rows // TXT_LEN, D), f32),
        ((rows // 128 * 16, 128), f32),
    ]
    return pl.pallas_call(
        text_front_kernel,
        out_shape=[jax.ShapeDtypeStruct(*item) for item in shapes],
        compiler_params=params(),
        cost_estimate=cost(rows * D * D * 8, 14 * D * rows + 8 * D * D, rows * 128 * HEADS),
        name="text_front",
    )(rows_in, gain1, bias1, wqkv, wo, gain2, bias2)


def image_front_kernel(
    windows, x_ref, order_ref, g1_ref, b1_ref, g2_ref, b2_ref, *refs
):
    h2_ref, sum_ref, early_ref = refs[-10:-7]
    w_ref, h1_ref, placed_ref, qkv_ref, att_ref, mid_ref, sems = refs[-7:]
    rows, chunk = x_ref.shape[0], 80
    copies, row = [], 0
    for k, piece in enumerate(refs[:-10]):
        place = w_ref.at[pl.ds(row, piece.shape[0]), :]
        copies.append(pltpu.make_async_copy(piece, place, sems.at[k]))
        row += piece.shape[0]
    for copy in copies:
        copy.start()

    def place_columns(src, dst):
        @pl.loop(0, D // 256)
        def _(step):
            at = pl.ds(pl.multiple_of(step * 256, 256), 256)
            dst[:, at] = mul_bt(src[...], chosen(order_ref[at, :])).astype(bf16)

    norm_rows(x_ref, h1_ref, line(g1_ref), line(b1_ref), chunk)
    place_columns(h1_ref, placed_ref)
    for copy in copies:
        copy.wait()

    @pl.loop(0, 3 * D // 256)
    def _(step):
        at = pl.ds(pl.multiple_of(step * 256, 256), 256)
        qkv_ref[:, at] = mul(placed_ref[...], w_ref[:, at]).astype(bf16)

    for row0, count, key0, keys in windows:
        one = same_sequence(count, row0, keys, key0, IMG_LEN)
        mask = jnp.concatenate([one, one], axis=0)
        attend_along(qkv_ref, att_ref, pl.ds(row0, count), pl.ds(key0, keys), mask)
    place_columns(att_ref, placed_ref)

    @pl.loop(0, D // 256)
    def _(step):
        at = pl.ds(pl.multiple_of(step * 256, 256), 256)
        there = pl.ds(pl.multiple_of(step * 256 + 3 * D, 256), 256)
        mid_ref[:, at] = x_ref[:, at].astype(f32) + mul(placed_ref[...], w_ref[:, there])

    norm_rows(mid_ref, h2_ref, line(g2_ref), line(b2_ref), chunk)
    place_columns(h2_ref, placed_ref)
    pool = pool_matrix(rows // IMG_LEN, rows, 0, IMG_LEN)

    @pl.loop(0, EARLY // TILE)
    def _(step):
        at = pl.ds(pl.multiple_of(step * TILE, TILE), TILE)
        there = pl.ds(pl.multiple_of(step * TILE + 4 * D, TILE), TILE)
        value, _ = gelu_parts(mul(placed_ref[...], w_ref[:, there]))
        early_ref[:, at] = mul(pool, value.astype(bf16))

    for k in range(rows // IMG_LEN):
        first, last = k * IMG_LEN, (k + 1) * IMG_LEN
        start, end = first // 8 * 8, -(-last // 8) * 8
        values = mid_ref[start:end, :]
        place = lax.broadcasted_iota(jnp.int32, values.shape, 0) + start
        inside = (place >= first) & (place < last)
        sum_ref[k : k + 1, :] = jnp.sum(jnp.where(inside, values, 0.0), axis=0, keepdims=True)


def image_front(rows_in, pieces, source, gain1, bias1, gain2, bias2):
    rows = rows_in.shape[0]
    windows = ((0, 208, 0, 256), (208, 192, 192, 208))
    vmem = pl.BlockSpec(memory_space=pltpu.VMEM)
    return pl.pallas_call(
        functools.partial(image_front_kernel, windows),
        out_shape=[
            jax.ShapeDtypeStruct((rows, D), bf16),
            jax.ShapeDtypeStruct((rows // IMG_LEN, D), f32),
            jax.ShapeDtypeStruct((rows // IMG_LEN, EARLY), f32),
        ],
        in_specs=[vmem] * 6 + anywhere(pieces),
        out_specs=[vmem] * 3,
        scratch_shapes=[
            pltpu.VMEM((D, 4 * D + EARLY), bf16),
            pltpu.VMEM((rows, D), bf16),
            pltpu.VMEM((rows, D), bf16),
            pltpu.VMEM((rows, 3 * D), bf16),
            pltpu.VMEM((rows, D), bf16),
            pltpu.VMEM((rows, D), f32),
            pltpu.SemaphoreType.DMA((len(pieces),)),
        ],
        compiler_params=params(),
        cost_estimate=cost(rows * D * D * 12, 8 * D * D, rows * 256 * HEADS),
        name="image_front",
    )(rows_in, source, gain1, bias1, gain2, bias2, *pieces)


def gelu_parts(inner):
    half = 0.5 * (1.0 + lax.erf(inner * (0.5**0.5)))
    return inner * half, half


def pack_kernel(unit_ref, pos_ref, *refs):
    refs[-1][:, :D] = unit_ref[...].astype(bf16)
    refs[-1][:, D:] = pos_ref[...]


def packed(unit, positive, after):
    shape = (unit.shape[0], D + positive.shape[1])
    return pl.pallas_call(
        pack_kernel,
        out_shape=jax.ShapeDtypeStruct(shape, bf16),
        in_specs=[pl.BlockSpec(memory_space=pltpu.VMEM)] * 2 + anywhere(after),
        compiler_params=params(),
        cost_estimate=cost(shape[0] * shape[1], 4 * shape[0] * shape[1]),
        name="packed",
    )(unit, positive, *after)


def pool_matrix(count, rows, row0, seq_len):
    row = (lax.broadcasted_iota(jnp.int32, (count, rows), 1) + row0) // seq_len
    return jnp.where(row == lax.broadcasted_iota(jnp.int32, (count, rows), 0), 1.0, 0.0).astype(bf16)


def two_terms(mean):
    high = mean.astype(bf16)
    low = (mean - high.astype(f32)).astype(bf16)
    return jnp.concatenate([high, low], axis=0)


def unit_rows(pooled):
    inverse = lax.rsqrt(jnp.sum(pooled * pooled, axis=-1, keepdims=True) + norm_eps)
    return pooled * inverse, inverse


def text_up_kernel(h2_ref, wu_ref, wd_ref, sum_ref, *refs):
    slope_ref, hid_ref, unit_ref, inv_ref, acc = refs[-5:]
    step = pl.program_id(0)
    chunk = 320
    per = chunk // TXT_LEN
    pool = pool_matrix(per, chunk, 0, TXT_LEN)
    for k in range(h2_ref.shape[0] // chunk):
        inner = mul(h2_ref[k * chunk : (k + 1) * chunk, :], wu_ref[...])
        value, half = gelu_parts(inner)
        slope = half + inner * (jnp.exp(-0.5 * inner * inner) * 0.3989422804014327)
        slope_ref[k * chunk : (k + 1) * chunk, :] = slope.astype(bf16)
        hid_ref[k * per : (k + 1) * per, :] = mul(pool, value.astype(bf16))
    terms = mul(two_terms(hid_ref[...] * (1.0 / TXT_LEN)), wd_ref[...])
    count = hid_ref.shape[0]
    added = terms[:count] + terms[count:]

    @pl.when(step == 0)
    def _():
        acc[...] = sum_ref[...] * (1.0 / TXT_LEN) + added

    @pl.when(step > 0)
    def _():
        acc[...] += added

    @pl.when(step == pl.num_programs(0) - 1)
    def _():
        unit, inverse = unit_rows(acc[...])
        unit_ref[...] = unit
        inv_ref[...] = jnp.broadcast_to(inverse, inv_ref.shape)


def text_up(normed2, weight_up, weight_down, middle_sum, after=()):
    rows, count = normed2.shape[0], middle_sum.shape[0]
    fixed = lambda shape: pl.BlockSpec(shape, lambda i: (0, 0))
    return pl.pallas_call(
        text_up_kernel,
        grid=(FF // TILE,),
        out_shape=[
            jax.ShapeDtypeStruct((rows, FF), bf16),
            jax.ShapeDtypeStruct((count, FF), f32),
            jax.ShapeDtypeStruct((count, D), f32),
            jax.ShapeDtypeStruct((count, 128), f32),
        ],
        in_specs=[
            fixed((rows, D)),
            pl.BlockSpec((D, TILE), lambda i: (0, i)),
            pl.BlockSpec((TILE, D), lambda i: (i, 0)),
            fixed((count, D)),
        ]
        + anywhere(after),
        out_specs=[
            pl.BlockSpec((rows, TILE), lambda i: (0, i)),
            pl.BlockSpec((count, TILE), lambda i: (0, i)),
            fixed((count, D)),
            fixed((count, 128)),
        ],
        scratch_shapes=[pltpu.VMEM((count, D), f32)],
        compiler_params=params(),
        cost_estimate=cost(2 * rows * D * FF, 4 * D * FF + 2 * rows * FF, 20 * rows * FF),
        name="text_up",
    )(normed2, weight_up, weight_down, middle_sum, *after)


def image_up_kernel(fold, h2_ref, wu_ref, wd_ref, first_ref, sum_ref, early_ref, out_ref, acc, picked):
    step = pl.program_id(0)
    rows, count = h2_ref.shape[0], sum_ref.shape[0]
    part = TILE // fold

    def through_down(summed, groups):
        moved = mul(two_terms(summed * (1.0 / IMG_LEN)), picked[...]).astype(bf16)
        weight = jnp.concatenate([groups[:, k * D : (k + 1) * D] for k in range(fold)], axis=0)
        terms = mul(moved, weight)
        return terms[:count] + terms[count:]

    @pl.when(step == 0)
    def _():
        place = lax.broadcasted_iota(jnp.int32, (TILE, TILE), 0)
        col = lax.broadcasted_iota(jnp.int32, (TILE, TILE), 1)
        source = (col % part) * fold + col // part
        picked[...] = jnp.where(place == source, 1.0, 0.0).astype(bf16)
        total = sum_ref[...] * (1.0 / IMG_LEN)
        for k in range(EARLY // TILE):
            total = total + through_down(
                early_ref[:, k * TILE : (k + 1) * TILE], first_ref[k * part : (k + 1) * part, :]
            )
        acc[...] = total

    value, _ = gelu_parts(mul(h2_ref[...], wu_ref[...]))
    summed = mul(pool_matrix(count, rows, 0, IMG_LEN), value.astype(bf16))
    acc[...] += through_down(summed, wd_ref[...])

    @pl.when(step == pl.num_programs(0) - 1)
    def _():
        unit = unit_rows(acc[...])[0].astype(bf16)
        out_ref[...] = jnp.broadcast_to(unit[None], out_ref.shape)


def image_up(normed2, whole, middle_sum, early, peers):
    rows, count = normed2.shape[0], middle_sum.shape[0]
    fold = FF // D
    before, part = EARLY // TILE, TILE // fold
    fixed = lambda shape: pl.BlockSpec(shape, lambda i: (0, 0))
    return pl.pallas_call(
        functools.partial(image_up_kernel, fold),
        grid=(FF // TILE - before,),
        out_shape=jax.ShapeDtypeStruct((peers, count, D), bf16),
        in_specs=[
            fixed((rows, D)),
            pl.BlockSpec((D, TILE), lambda i: (0, FF // TILE + i)),
            pl.BlockSpec((part, FF), lambda i: (i + before, 0)),
            fixed((before * part, FF)),
            fixed((count, D)),
            fixed((count, EARLY)),
        ],
        out_specs=pl.BlockSpec((peers, count, D), lambda i: (0, 0, 0)),
        scratch_shapes=[pltpu.VMEM((count, D), f32), pltpu.VMEM((TILE, TILE), bf16)],
        compiler_params=params(),
        cost_estimate=cost(2 * rows * D * FF, 4 * D * FF, 15 * rows * FF),
        name="image_up",
    )(normed2, whole, whole, whole, middle_sum, early)


def left_kernel(count, *refs):
    out_ref = refs[-1]
    for k in range(count):
        source_ref, values_ref = refs[2 * k : 2 * k + 2]

        @pl.loop(0, D // 256)
        def _(step, k=k, source_ref=source_ref, values_ref=values_ref):
            at = pl.ds(pl.multiple_of(step * 256, 256), 256)
            picked = mul_bt(chosen(source_ref[at, :]), values_ref[...])
            out_ref[k, at, :] = picked.astype(bf16)


def left_factors(*pairs):
    rows = pairs[0][1].shape[0]
    given = [item for pair in pairs for item in pair]
    return pl.pallas_call(
        functools.partial(left_kernel, len(pairs)),
        out_shape=jax.ShapeDtypeStruct((len(pairs), D, rows), bf16),
        in_specs=in_vmem(len(given)),
        out_specs=pl.BlockSpec(memory_space=pltpu.VMEM),
        compiler_params=params(24 << 20),
        cost_estimate=cost(2 * len(pairs) * rows * D * D, 4 * len(pairs) * rows * D),
        name="left_factors",
    )(*given)


def loss_parts(text_rows, pos, image_all):
    similar = mul_bt(text_rows, image_all) * logit_scale
    shifted = jnp.exp(similar - logit_scale)
    alive = jnp.max(pos, axis=1, keepdims=True)
    row_sum = jnp.sum(shifted, axis=1, keepdims=True)
    row_count = jnp.maximum(jnp.sum(pos, axis=1, keepdims=True), 1.0)
    return similar, shifted, alive, row_sum, row_count


def sums_over_captions(text_rows, pos, image_all):
    similar, shifted, alive, row_sum, row_count = loss_parts(text_rows, pos, image_all)
    pos_similar = pos * similar
    cap_term = alive * (
        logit_scale + jnp.log(row_sum) - jnp.sum(pos_similar, axis=1, keepdims=True) / row_count
    )
    return (
        jnp.sum(alive * shifted, axis=0, keepdims=True),
        jnp.sum(pos, axis=0, keepdims=True),
        jnp.sum(pos_similar, axis=0, keepdims=True),
        jnp.sum(cap_term, axis=0, keepdims=True),
        jnp.sum(alive, axis=0, keepdims=True),
    )


def loss_from(sums):
    col_sum, col_count, col_pos, cap_total, live_total = sums
    img_term = logit_scale + jnp.log(col_sum) - col_pos / col_count
    return 0.5 * cap_total / live_total + 0.5 * jnp.mean(img_term, axis=1, keepdims=True)


def grad_of_unit(text_rows, pos, image_all, col_sum, col_count, live_total):
    _, shifted, alive, row_sum, row_count = loss_parts(text_rows, pos, image_all)
    cap_share, img_share = 0.5 / live_total, 0.5 / image_all.shape[0]
    grad_sims = alive * shifted * (cap_share / row_sum + img_share / col_sum) - pos * (
        cap_share / row_count + img_share / col_count
    )
    return mul(grad_sims.astype(bf16), image_all) * logit_scale


def turned(grad, unit):
    return grad - unit * jnp.sum(grad * unit, axis=-1, keepdims=True)


def loss_into(
    pack_ref, image_ref, own_ref, unit_ref, inv_ref, loss_ref, row_ref, low_ref, col_sum_ref,
    col_count_ref, live_ref
):
    image_all = image_ref[...]
    chunk = 256
    total = None
    for k in range(pack_ref.shape[0] // chunk):
        at = slice(k * chunk, (k + 1) * chunk)
        part = sums_over_captions(pack_ref[at, :D], pack_ref[at, D:].astype(f32), image_all)
        total = part if total is None else [a + b for a, b in zip(total, part)]
    loss_ref[...] = jnp.broadcast_to(loss_from(total), loss_ref.shape)
    col_sum, col_count, _, _, live_total = total
    col_sum_ref[...] = col_sum
    col_count_ref[...] = col_count
    live_ref[...] = jnp.broadcast_to(live_total, live_ref.shape)
    grad = grad_of_unit(
        own_ref[:, :D], own_ref[:, D:].astype(f32), image_all, col_sum, col_count, live_total
    )
    row = inv_ref[:, :1] * turned(grad, unit_ref[...]) * (1.0 / TXT_LEN)
    row_ref[...] = row
    low_ref[...] = row.astype(bf16)


def down_kernel(pack_ref, image_ref, col_sum_ref, col_count_ref, live_ref, hid_ref, *refs):
    step, out_ref = pl.program_id(0), refs[-1]
    text_rows = pack_ref[:, :D]
    grad = grad_of_unit(
        text_rows, pack_ref[:, D:].astype(f32), image_ref[...], col_sum_ref[...],
        col_count_ref[...], live_ref[:, :1]
    )
    rows = (turned(grad, text_rows.astype(f32)) * (1.0 / TXT_LEN)).astype(bf16)
    part = mul_at(hid_ref[...], rows)

    @pl.when(step == 0)
    def _():
        out_ref[...] = part

    @pl.when(step > 0)
    def _():
        out_ref[...] += part


def grad_of_down(pack, image_all, col_sum, col_count, live_total, hidden_cols, after):
    images, chunk = image_all.shape[0], 256
    fixed = lambda shape: pl.BlockSpec(shape, lambda i: (0, 0))
    per = hidden_cols.shape[1]
    return pl.pallas_call(
        down_kernel,
        grid=(pack.shape[0] // chunk,),
        out_shape=jax.ShapeDtypeStruct((per, D), f32),
        in_specs=[
            pl.BlockSpec((chunk, pack.shape[1]), lambda i: (i, 0)),
            fixed((images, D)), fixed((1, images)), fixed((1, images)), fixed((1, 128)),
            pl.BlockSpec((chunk, per), lambda i: (i, 0)),
        ]
        + anywhere(after),
        out_specs=fixed((per, D)),
        compiler_params=params(16 << 20),
        cost_estimate=cost(4 * pack.shape[0] * images * D, 2 * pack.size, pack.shape[0] * images),
        name="grad_of_down",
    )(pack, image_all, col_sum, col_count, live_total, hidden_cols, *after)


def load_kernel(*refs):
    count = (len(refs) - 1) // 2
    sems = refs[-1]
    copies = [
        pltpu.make_async_copy(refs[k], refs[count + k], sems.at[k]) for k in range(count)
    ]
    for copy in copies:
        copy.start()
    for copy in copies:
        copy.wait()


def loaded(*arrays):
    return pl.pallas_call(
        load_kernel,
        out_shape=[stays(array.shape, array.dtype) for array in arrays],
        in_specs=[pl.BlockSpec(memory_space=pltpu.HBM)] * len(arrays),
        out_specs=in_vmem(len(arrays)),
        scratch_shapes=[pltpu.SemaphoreType.DMA((len(arrays),))],
        compiler_params=params(4 << 20),
        cost_estimate=cost(0, sum(2 * array.size * array.dtype.itemsize for array in arrays)),
        name="loaded",
    )(*in_hbm(*arrays))


def mlp_back_kernel(with_loss, gain_ref, *refs):
    given, refs = (refs[:5], refs[5:]) if with_loss else (refs[:2], refs[2:])
    wd_ref, slope_ref, wu_ref, lhs_ref, mid_ref = refs[:5]
    keep_a, send_a, keep_b, send_b, out_ref, sums_out = refs[5:11]
    low_ref, row_ref = refs[-2:] if with_loss else given
    count, rows = low_ref.shape[0], out_ref.shape[0]
    half, steps = D // 2, FF // 2 // TILE
    if with_loss:
        loss_ref, *stats = refs[11:15]
        loss_into(*given, loss_ref, row_ref, low_ref, *stats)
    for k, (keep, send) in enumerate(((keep_a, send_a), (keep_b, send_b))):

        @pl.loop(0, steps)
        def _(step, k=k, keep=keep, send=send):
            at = pl.ds(pl.multiple_of(k * (FF // 2) + step * TILE, TILE), TILE)
            there = pl.ds(pl.multiple_of(step * TILE, TILE), TILE)
            hidden = mul_bt(low_ref[...], wd_ref[at, :])
            wide = jnp.broadcast_to(hidden[:, None, :], (count, TXT_LEN, TILE))
            inner = (wide.reshape(rows, TILE) * slope_ref[:, at].astype(f32)).astype(bf16)
            weight = mul(lhs_ref[k], inner).astype(bf16)
            keep[:, there] = weight[:half]
            send[:, there] = weight[half:]
            added = mul_bt(inner, wu_ref[:, at])
            if k == 0:

                @pl.when(step == 0)
                def _():
                    out_ref[...] = added

                @pl.when(step > 0)
                def _():
                    out_ref[...] += added
            else:
                out_ref[...] += added

    chunk = 128
    per = chunk // TXT_LEN
    gain = line(gain_ref)
    sums_out[...] = jnp.zeros_like(sums_out)

    @pl.loop(0, rows // chunk)
    def _(k):
        at = pl.ds(pl.multiple_of(k * chunk, chunk), chunk)
        unit, scale = norm_parts(mid_ref[at, :])
        grad = out_ref[at, :]
        sums_out[:, :D] += jnp.sum(grad * unit, axis=0, keepdims=True)
        sums_out[:, D:] += jnp.sum(grad, axis=0, keepdims=True)
        row = row_ref[pl.ds(pl.multiple_of(k * per, per), per), :]
        row = jnp.broadcast_to(row[:, None, :], (per, TXT_LEN, D)).reshape(chunk, D)
        out_ref[at, :] = row + norm_back(unit, scale, gain, grad)


def mlp_back(given, weight_down, slope, weight_up, lhs, middle, gain):
    rows, count = slope.shape[0], given[-2].shape[0]
    with_loss = len(given) == 5
    shapes = [stays((D // 2, FF // 2), bf16)] * 4 + [stays((rows, D), f32), stays((1, 2 * D), f32)]
    scratch = []
    if with_loss:
        images = given[1].shape[0]
        wide = [(1, 128), (1, images), (1, images), (1, 128)]
        shapes += [jax.ShapeDtypeStruct(shape, f32) for shape in wide]
        scratch = [pltpu.VMEM((count, D), bf16), pltpu.VMEM((count, D), f32)]
    return pl.pallas_call(
        functools.partial(mlp_back_kernel, with_loss),
        out_shape=shapes,
        in_specs=in_vmem(6 + len(given)),
        out_specs=in_vmem(len(shapes)),
        scratch_shapes=scratch,
        compiler_params=params(16 << 20),
        cost_estimate=cost(4 * rows * D * FF, 4 * D * FF + 2 * rows * FF + 2 * D * FF, rows * FF),
        name="mlp_back",
    )(gain, *given, weight_down, slope, weight_up, lhs, middle)


def attention_back_kernel(first, grad_ref, wo_ref, qkv_ref, lse_ref, *refs):
    low_ref, out_ref = refs[-2:]
    chunk = 128
    mask = same_sequence(chunk, 0, chunk, 0, TXT_LEN)

    @pl.loop(0, low_ref.shape[0] // chunk)
    def _(step):
        here = pl.ds(pl.multiple_of((first + step) * chunk, chunk), chunk)
        there = pl.ds(pl.multiple_of(step * chunk, chunk), chunk)
        sums = lse_ref[pl.ds(pl.multiple_of((first + step) * 16, 16), 16), :]
        low = grad_ref[here, :].astype(bf16)
        low_ref[there, :] = low
        grad_att = mul_bt(low, wo_ref[...]).astype(bf16)
        for pair in range(HEADS // 2):
            queries = qkv_ref[here, pair_cols(0, pair)] * bf16(HEAD ** (-0.5))
            keys = two_heads(qkv_ref[here, pair_cols(1, pair)])
            vals = two_heads(qkv_ref[here, pair_cols(2, pair)])
            grads = grad_att[:, pair_cols(0, pair)]
            scores, grad_probs = mul_bt(keys, queries), mul_bt(vals, grads)
            probs, grad_scores = [], []
            for k in range(2):
                at = slice(k * chunk, (k + 1) * chunk)
                head = 2 * pair + k
                shifted = scores[at] - sums[head : head + 1, :]
                prob = jnp.where(mask, jnp.exp(jnp.where(mask, shifted, 0.0)), 0.0)
                along = jnp.sum(grad_probs[at] * prob, axis=0, keepdims=True)
                grad_scores.append((prob * (grad_probs[at] - along)).astype(bf16))
                probs.append(prob.astype(bf16))
            grad_q = mul_at(jnp.concatenate(grad_scores, axis=0), keys) * HEAD ** (-0.5)
            grad_k = mul(jnp.concatenate(grad_scores, axis=1), two_heads(queries))
            grad_v = mul(jnp.concatenate(probs, axis=1), two_heads(grads))
            out_ref[there, pair_cols(0, pair)] = grad_q.astype(bf16)
            out_ref[there, pair_cols(1, pair)] = grad_k.astype(bf16)
            out_ref[there, pair_cols(2, pair)] = grad_v.astype(bf16)


def attention_back(grad_middle, weight_out, project, log_sums, first, count, after=()):
    rows = count * 128
    return pl.pallas_call(
        functools.partial(attention_back_kernel, first),
        out_shape=[stays((rows, D), bf16), stays((rows, 3 * D), bf16)],
        in_specs=in_vmem(4) + anywhere(after),
        out_specs=in_vmem(2),
        compiler_params=params(16 << 20),
        cost_estimate=cost(10 * rows * D * D, 16 * rows * D + 2 * D * D, rows * 128 * HEADS),
        name="attention_back",
    )(grad_middle, weight_out, project, log_sums, *after)


def mul_rows(lhs, parts, cols):
    total, row = 0.0, 0
    for part in parts:
        total = total + mul(lhs[:, row : row + part.shape[0]], part[:, cols])
        row += part.shape[0]
    return total


def weight_back_kernel(factors, groups, lhs_ref, *refs):
    keep_a, send_a, keep_b, send_b = refs[-4:]
    half = D // 2
    for k, (factor, group, col) in enumerate(factors):
        parts = refs[sum(groups[:group]) : sum(groups[: group + 1])]
        weight = mul_rows(lhs_ref.at[factor], parts, slice(col * D, (col + 1) * D)).astype(bf16)
        at = slice(k % 2 * D, (k % 2 + 1) * D)
        (keep_b if k > 1 else keep_a)[:, at] = weight[:half]
        (send_b if k > 1 else send_a)[:, at] = weight[half:]


def weight_back(lhs, groups, factors, after=()):
    rows = lhs.shape[2]
    given = [part for group in groups for part in group]
    return pl.pallas_call(
        functools.partial(weight_back_kernel, factors, [len(group) for group in groups]),
        out_shape=[stays((D // 2, 2 * D), bf16)] * 4,
        in_specs=in_vmem(1 + len(given)) + anywhere(after),
        out_specs=in_vmem(4),
        compiler_params=params(16 << 20),
        cost_estimate=cost(8 * rows * D * D, 8 * rows * D + 14 * D * D),
        name="weight_back",
    )(lhs, *given, *after)


def input_back_kernel(count, *refs):
    projs = refs[:count]
    w_ref, x_ref, gain_ref, mid_ref, sums_ref = refs[count : count + 5]
    out_ref, sums_out = refs[-2:]
    rows, chunk = x_ref.shape[0], 128

    @pl.loop(0, D // 256)
    def _(step):
        at = pl.ds(pl.multiple_of(step * 256, 256), 256)
        row = 0
        for part in projs:
            there = slice(row, row + part.shape[0])
            out_ref[there, at] = mul_bt(part[...], w_ref[at, :])
            row += part.shape[0]

    gain = line(gain_ref)
    sums_out[...] = jnp.zeros_like(sums_out)
    sums_out[1:2, :] = sums_ref[...]

    @pl.loop(0, rows // chunk)
    def _(k):
        at = pl.ds(pl.multiple_of(k * chunk, chunk), chunk)
        unit, scale = norm_parts(x_ref[at, :].astype(f32))
        grad = out_ref[at, :]
        sums_out[0:1, :D] += jnp.sum(grad * unit, axis=0, keepdims=True)
        sums_out[0:1, D:] += jnp.sum(grad, axis=0, keepdims=True)
        out_ref[at, :] = mid_ref[at, :] + norm_back(unit, scale, gain, grad)


def input_back(grad_projs, weight, rows_in, gain, grad_middle, sums, after=()):
    rows = rows_in.shape[0]
    return pl.pallas_call(
        functools.partial(input_back_kernel, len(grad_projs)),
        out_shape=[jax.ShapeDtypeStruct((rows, D), f32), stays((8, 2 * D), f32)],
        in_specs=in_vmem(len(grad_projs) + 5) + anywhere(after),
        out_specs=in_vmem(2),
        compiler_params=params(16 << 20),
        cost_estimate=cost(6 * rows * D * D, 14 * rows * D + 6 * D * D),
        name="input_back",
    )(*grad_projs, weight, rows_in, gain, grad_middle, sums, *after)


def local(
    images,
    captions,
    img_gain1,
    img_bias1,
    img_qkv,
    img_out,
    img_gain2,
    img_bias2,
    img_up,
    img_down,
    txt_gain1,
    txt_bias1,
    txt_qkv,
    txt_out,
    txt_gain2,
    txt_bias2,
    txt_up,
    txt_down,
    counts,
    matches,
):
    peers = lax.axis_size(AXIS)
    own = lax.axis_index(AXIS)
    per = D // peers
    img_local = counts.shape[0]
    cap_local = matches.shape[0]
    total_images = matches.shape[1]

    up_rows = img_up.reshape(per, FF)
    whole = lax.all_gather(
        jnp.concatenate([img_down.reshape(per, FF), up_rows[:, EARLY:]], axis=1),
        AXIS,
        axis=0,
        tiled=True,
    )
    small = peers == 32
    shard = jnp.concatenate(
        [img_qkv.reshape(per, 3 * D), img_out.reshape(per, D), up_rows[:, :EARLY]], axis=1
    )
    if small:
        line, source = gathered_line(shard), row_order((1, 4, 2, 16, 8))
    else:
        line, source = lax.all_gather(shard, AXIS, axis=0, tiled=True), row_order(())

    normed1, project, attended, middle, normed2, middle_sum, log_sums = text_front(
        captions, txt_gain1, txt_bias1, txt_qkv, txt_out, txt_gain2, txt_bias2
    )
    middle_sum, line = in_turn(middle_sum, line)
    beside, above = (swapped(line, 2), swapped(line, 4)) if small else (line, line)
    slope, hidden_sum, text_unit, inverse = text_up(
        normed2, txt_up, txt_down, middle_sum, (line,)
    )
    text_unit, normed2, beside, above = lax.optimization_barrier(
        (text_unit, normed2, beside, above)
    )

    ends_at = jnp.cumsum(counts)
    slot_ids = lax.iota(jnp.int32, cap_local)
    owner = jnp.sum((ends_at[None, :] <= slot_ids[:, None]).astype(jnp.int32), axis=1)
    owner = owner + own * img_local
    live = slot_ids < ends_at[-1]
    columns = lax.iota(jnp.int32, total_images)
    positive = ((matches > 0) | (owner[:, None] == columns[None, :])) & live[:, None]

    order_a, order_b, tail = stage_orders()
    source_a, source_b = row_order(order_a + tail[::-1]), row_order(order_b + tail[::-1])
    own_pack = packed(text_unit, positive.astype(bf16), ())
    lhs_up = left_factors((source_a, normed2), (source_b, normed2))
    pieces = [line]
    if small:
        first, second = diagonal(beside, above)
        own_pack, first, second, lhs_up = lax.optimization_barrier(
            (own_pack, first, second, lhs_up)
        )
        held = own_pack[None]
        others = [swapped(held, mask) for mask in (8, 16, 24)]
        pieces = [line, beside, above, first, second]
        pieces = pieces + [swapped(piece, 1) for piece in pieces]

    normed_img, middle_img, early = image_front(
        images, pieces, source, img_gain1, img_bias1, img_gain2, img_bias2
    )
    if small:
        scaled_sum = (hidden_sum * inverse[:, :1]).astype(bf16)
        normed_img, scaled_sum, others = lax.optimization_barrier((normed_img, scaled_sum, others))
        held = joined(joined(held, others[0], 8), joined(others[1], others[2], 8), 16, 1)
        text_beside, text_above = swapped(held, 2), swapped(held, 4)
        hidden_cols = lax.all_to_all(scaled_sum, AXIS, split_axis=1, concat_axis=0, tiled=True)
        normed_img, text_beside, text_above = lax.optimization_barrier(
            (normed_img, text_beside, text_above)
        )
        halves = diagonal(text_beside, text_above)
    image_low = image_up(normed_img, whole, middle_img, early, peers)
    if small:
        image_low, halves, hidden_cols = lax.optimization_barrier((image_low, halves, hidden_cols))
        across = jnp.concatenate(halves, axis=0)
        held = joined(joined(held, text_beside, 2), joined(text_above, across, 2), 4, 4)
        other, slope = in_turn(swapped(held, 1), slope)
        text_pack = joined(held, other, 1).reshape(-1, D + total_images)
    image_all = exchanged(image_low).reshape(total_images, D)
    if small:
        image_all, text_pack = in_turn(image_all, text_pack)

    heavy = loaded(txt_down, slope, txt_up, lhs_up, middle)
    image_all, heavy = in_turn(image_all, heavy)

    if small:
        given = (text_pack, image_all, own_pack, text_unit, inverse)
    else:
        text_low, pos = own_pack[:, :D], own_pack[:, D:].astype(f32)
        totals = lax.psum(sums_over_captions(text_low, pos, image_all), AXIS)
        loss_value = loss_from(totals)
        grad = grad_of_unit(text_low, pos, image_all, totals[0], totals[1], totals[4])
        grad_row = inverse[:, :1] * turned(grad, text_unit) * (1.0 / TXT_LEN)
        row_low = grad_row.astype(bf16)
        given = (row_low, grad_row)

    *up, grad_middle, sums = mlp_back(given, *heavy, txt_gain2)
    if small:
        *up, grad_middle, sums, loss_value, col_sum, col_count, live_total = (
            *up, grad_middle, sums
        )
    stages = len(order_a)
    low_one, proj_one = attention_back(grad_middle, txt_out, project, log_sums, 0, 2)
    for stage in range(stages - 2):
        up = fold(hand_on(up, stage), (proj_one,))
    low_two, proj_two = attention_back(grad_middle, txt_out, project, log_sums, 2, 3, up)
    proj_two, normed1 = in_turn(proj_two, normed1)
    lhs_rest = left_factors((source_a, normed1), (source_b, normed1), (source_b, attended))
    up = fold(hand_on(up, stages - 2), (proj_two, lhs_rest))
    projs, lows = (proj_one, proj_two), (low_one, low_two)
    rest = weight_back(lhs_rest, [projs, lows], [(0, 0, 0), (0, 0, 1), (1, 0, 2), (2, 1, 0)], up)
    up = hand_on(up, stages - 1)
    caption_grad, sums = input_back(
        projs, txt_qkv, captions, txt_gain1, grad_middle, sums, rest[:1]
    )
    caption_grad, up = in_turn(caption_grad, up)
    up = fold_last(up)
    if small:
        *rest, sums = fold(hand_on(rest, 0), up[:1], (sums, swapped(sums, 1)))
    else:
        norms = lax.psum(sums, AXIS)[:2].reshape(-1)
        for stage in range(stages - 2):
            rest = fold(hand_on(rest, stage), up[:1])
    up = hand_on_last(up)
    rest = hand_on(rest, stages - 2)
    if small:
        grad_down = grad_of_down(
            text_pack, image_all, col_sum, col_count, live_total, hidden_cols, (caption_grad,)
        )
    else:
        grad_down = lax.psum_scatter(
            mul_at(hidden_sum.astype(bf16), row_low), AXIS, scatter_dimension=0, tiled=True
        )
    grad_down, rest, up = lax.optimization_barrier((grad_down, rest, up))
    if small:
        *rest, sums = fold(rest, (), (sums,))
        rest = fold_last(hand_on(rest, stages - 1), (), (sums,))
    else:
        rest = fold_last(hand_on(fold(rest), stages - 1))
    up_share = sum_last(*up)
    rest_share = sum_last(*hand_on_last(rest))
    if small:
        norms = rest_share[per]
        rest_share = rest_share[:per]
    return (
        loss_value[0, 0],
        caption_grad,
        norms[:D],
        norms[D : 2 * D],
        rest_share[:, : 3 * D].reshape(-1),
        rest_share[:, 3 * D :].reshape(-1),
        norms[2 * D : 3 * D],
        norms[3 * D :],
        up_share.reshape(-1),
        grad_down.reshape(-1),
    )


def solution(mesh):
    split, flat, whole = P("blk", None), P("blk"), P()
    image_block = (whole, whole, flat, flat, whole, whole, flat, flat)
    return jax.shard_map(
        local,
        mesh=mesh,
        in_specs=(split, split) + image_block + (whole,) * 8 + (flat, split),
        out_specs=(whole, split, whole, whole, flat, flat, whole, whole, flat, flat),
        check_vma=False,
    )
```

```python
import functools

import jax
import jax.numpy as jnp
from jax import lax
from jax.experimental import pallas as pl
from jax.experimental.pallas import tpu as pltpu
from jax.sharding import PartitionSpec as P

D = 768
FF = 3072
HEAD = 64
HEADS = D // HEAD
IMG_LEN = 50
TXT_LEN = 16
AXIS = "blk"

norm_eps = 1e-06
logit_scale = 50.0
f32 = jnp.float32
bf16 = jnp.bfloat16


def swapped(value, mask):
    peers = lax.axis_size(AXIS)
    return lax.ppermute(value, AXIS, [(i, i ^ mask) for i in range(peers)])


def bit_masks():
    peers = lax.axis_size(AXIS)
    return [1 << k for k in range(peers.bit_length() - 1)]


def joined(held, other, mask, outer=None):
    upper = (lax.axis_index(AXIS) & mask) > 0
    first = jnp.where(upper, other, held)
    second = jnp.where(upper, held, other)
    outer = held.shape[0] if outer is None else outer
    parts = [part.reshape((outer, -1) + held.shape[1:]) for part in (first, second)]
    return jnp.stack(parts, axis=1).reshape((-1,) + held.shape[1:])


def exchanged(copies):
    return lax.all_to_all(copies, AXIS, split_axis=0, concat_axis=0, tiled=True)


def stage_orders():
    masks = bit_masks()
    head, tail = masks[:-2], masks[-2:]
    order_a = list(head)
    order_b = list(head)
    for k in range(1, len(head) - 1, 2):
        order_b[k], order_b[k + 1] = order_b[k + 1], order_b[k]
    return order_a, order_b, tail


def row_order(bits):
    peers = lax.axis_size(AXIS)
    own = lax.axis_index(AXIS)
    per = D // peers
    places = lax.broadcasted_iota(jnp.int32, (D, 1), 0)
    block = places // per
    target = jnp.zeros_like(block) + own
    for k, mask in enumerate(bits):
        target = target ^ (((block >> (len(bits) - 1 - k)) & 1) * mask)
    return target * per + places % per


def chosen(source):
    column = lax.broadcasted_iota(jnp.int32, (source.shape[0], D), 1)
    return jnp.where(column == source, 1.0, 0.0).astype(bf16)


def gathered_line(shard):
    return jnp.concatenate([shard] + [swapped(shard, mask) for mask in (8, 16, 24)], axis=0)


def diagonal(beside, above):
    half = beside.shape[0] // 2
    return swapped(beside[:half], 4), swapped(above[half:], 2)


def in_turn(first, then):
    return lax.optimization_barrier((first, then))


def hand_on(parts, stage):
    order_a, order_b, _ = stage_orders()
    keep_a, send_a, keep_b, send_b = parts
    return keep_a, swapped(send_a, order_a[stage]), keep_b, swapped(send_b, order_b[stage])


def hand_on_last(blocks):
    low, high = stage_orders()[2]
    own, *others = blocks
    return own, [swapped(block, mask) for block, mask in zip(others, (low, high, low | high))]


def sum_last(own, others):
    total = own
    for other in others:
        total = total + other.astype(f32)
    return total


VMEM_BYTES = 56 << 20
TILE = 512
EARLY = TILE


def norm_parts(values):
    average = jnp.mean(values, axis=-1, keepdims=True)
    centred = values - average
    variance = jnp.mean(centred * centred, axis=-1, keepdims=True)
    scale = lax.rsqrt(variance + norm_eps)
    return centred * scale, scale


def norm_back(unit, scale, gain, grad):
    inner = grad * gain
    shift = jnp.mean(inner, axis=-1, keepdims=True)
    along = jnp.mean(inner * unit, axis=-1, keepdims=True)
    return scale * (inner - shift - unit * along)


def mul(lhs, rhs):
    return jnp.dot(lhs, rhs, preferred_element_type=f32)


def mul_bt(lhs, rhs):
    return lax.dot_general(lhs, rhs, (((1,), (1,)), ((), ())), preferred_element_type=f32)


def mul_at(lhs, rhs):
    return lax.dot_general(lhs, rhs, (((0,), (0,)), ((), ())), preferred_element_type=f32)


def params(limit=VMEM_BYTES):
    return pltpu.CompilerParams(vmem_limit_bytes=limit)


def in_vmem(count):
    return [pl.BlockSpec(memory_space=pltpu.VMEM)] * count


def in_hbm(*arrays):
    return [pltpu.with_memory_space_constraint(array, pltpu.HBM) for array in arrays]


def stays(shape, dtype):
    return pltpu.VMEM(shape, dtype)


def cost(flops, moved, transcendentals=0):
    return pl.CostEstimate(flops=flops, bytes_accessed=moved, transcendentals=transcendentals)


def lane_halves(dtype):
    lane = lax.broadcasted_iota(jnp.int32, (1, 2 * HEAD), 1)
    low = jnp.where(lane < HEAD, 1.0, 0.0)
    return low.astype(dtype), (1.0 - low).astype(dtype)


def two_heads(pair):
    low, high = lane_halves(bf16)
    return jnp.concatenate([pair * low, pair * high], axis=0)


def same_sequence(rows, row0, cols, col0, seq_len):
    row = (lax.broadcasted_iota(jnp.int32, (rows, cols), 0) + row0) // seq_len
    col = (lax.broadcasted_iota(jnp.int32, (rows, cols), 1) + col0) // seq_len
    return row == col


def softmax_down(scores, mask):
    keys = mask.shape[0]
    parts, sums = [], []
    for k in range(2):
        part = jnp.where(mask, scores[k * keys : (k + 1) * keys], -1e30)
        most = jnp.max(part, axis=0, keepdims=True)
        raised = jnp.exp(part - most)
        total = jnp.sum(raised, axis=0, keepdims=True)
        parts.append(raised * (1.0 / total))
        sums.append(most + jnp.log(total))
    return parts, sums


def fold_kernel(extra, keep_a, got_a, keep_b, got_b, *refs):
    outs = refs[-5:] if extra else refs[-4:]
    rows, half, tile = keep_a.shape[0], keep_a.shape[0] // 2, 256

    @pl.loop(0, keep_a.shape[1] // tile)
    def _(step):
        cols = pl.ds(pl.multiple_of(step * tile, tile), tile)
        for k, (kept, got) in enumerate(((keep_a, got_a), (keep_b, got_b))):
            for j in range(2):
                at = slice(j * half, (j + 1) * half)
                total = kept[at, cols].astype(f32) + got[at, cols].astype(f32)
                outs[2 * k + j][:half, cols] = total.astype(bf16)

    if extra:
        came = refs[1][...] if extra > 1 else got_a[rows : rows + 16, :].astype(f32)[:8]
        sums = refs[0][...] + came
        outs[4][...] = sums
        outs[1][half : half + 16, :] = jnp.concatenate([sums, sums], axis=0).astype(bf16)


def fold(parts, after=(), sums=()):
    rows, cols = parts[0].shape
    if rows % 32:
        whole = [
            (kept.astype(f32) + got.astype(f32)).astype(bf16)
            for kept, got in (parts[:2], parts[2:])
        ]
        return [part for one in whole for part in (one[: rows // 2], one[rows // 2 :])]
    half = (rows // 2, cols)
    shapes = [stays(half, bf16)] * 4
    if sums:
        shapes[1] = stays((rows // 2 + 16, cols), bf16)
        shapes.append(stays((8, cols), f32))
    return pl.pallas_call(
        functools.partial(fold_kernel, len(sums)),
        out_shape=shapes,
        in_specs=in_vmem(4 + len(sums)) + anywhere(after),
        out_specs=in_vmem(len(shapes)),
        compiler_params=params(8 << 20),
        cost_estimate=cost(2 * rows * cols, 12 * rows * cols),
        name="fold",
    )(*parts, *sums, *after)


def fold_last_kernel(extra, keep_a, got_a, keep_b, got_b, *refs):
    outs = refs[-4:]
    cols = keep_a.shape[1]
    rows = keep_a.shape[0] // 4
    if extra:
        sums = refs[0][...] + got_a[4 * rows : 4 * rows + 16, :].astype(f32)[:8]
    for k, (kept, got) in enumerate(((keep_a, got_a), (keep_b, got_b))):
        total = kept[...].astype(f32) + got[: 4 * rows, :].astype(f32)
        at = slice(k * cols, (k + 1) * cols)
        for j, out in enumerate(outs):
            part = total[j * rows : (j + 1) * rows]
            if extra:
                row = jnp.broadcast_to(sums[k : k + 1], (8, cols))
                part = jnp.concatenate([part, row], axis=0)
            out[:, at] = part.astype(out.dtype)


def fold_last(parts, after=(), sums=()):
    rows, cols = parts[0].shape
    shape = (rows // 4 + (8 if sums else 0), 2 * cols)
    if rows % 32:
        pairs = (parts[:2], parts[2:])
        both = [kept.astype(f32) + got.astype(f32) for kept, got in pairs]
        own, *others = jnp.split(jnp.concatenate(both, axis=1), 4)
        return [own] + [other.astype(bf16) for other in others]
    return pl.pallas_call(
        functools.partial(fold_last_kernel, len(sums)),
        out_shape=[stays(shape, f32)] + [stays(shape, bf16)] * 3,
        in_specs=in_vmem(4 + len(sums)) + anywhere(after),
        out_specs=in_vmem(4),
        compiler_params=params(8 << 20),
        cost_estimate=cost(2 * rows * cols, 12 * rows * cols),
        name="fold_last",
    )(*parts, *sums, *after)


def anywhere(after):
    return [pl.BlockSpec(memory_space=pl.ANY)] * len(after)


def pair_cols(part, pair):
    start = part * D + pair * 2 * HEAD
    return slice(start, start + 2 * HEAD)


def line(ref):
    return ref[...].astype(f32).reshape(1, -1)


def norm_rows(src, dst, gain, bias, step_rows):
    @pl.loop(0, src.shape[0] // step_rows)
    def _(step):
        at = pl.ds(pl.multiple_of(step * step_rows, step_rows), step_rows)
        unit, _ = norm_parts(src[at, :].astype(f32))
        dst[at, :] = (unit * gain + bias).astype(bf16)


def attend_along(qkv_ref, att_ref, q_rows, k_rows, mask):
    low, high = lane_halves(f32)
    for pair in range(HEADS // 2):
        queries = two_heads(qkv_ref[q_rows, pair_cols(0, pair)] * bf16(HEAD ** (-0.5)))
        scores = mul_bt(queries, qkv_ref[k_rows, pair_cols(1, pair)])
        scores = jnp.where(mask, scores, -1e30)
        raised = jnp.exp(scores - jnp.max(scores, axis=-1, keepdims=True))
        probs = (raised * (1.0 / jnp.sum(raised, axis=-1, keepdims=True))).astype(bf16)
        half = probs.shape[0] // 2
        mixed = mul(probs, qkv_ref[k_rows, pair_cols(2, pair)])
        att_ref[q_rows, pair_cols(0, pair)] = (mixed[:half] * low + mixed[half:] * high).astype(bf16)


def attend(qkv_ref, att_ref, q_rows, k_rows, mask, keep_sums):
    for pair in range(HEADS // 2):
        queries = qkv_ref[q_rows, pair_cols(0, pair)] * bf16(HEAD ** (-0.5))
        scores = mul_bt(two_heads(qkv_ref[k_rows, pair_cols(1, pair)]), queries)
        probs, sums = softmax_down(scores, mask)
        vals = two_heads(qkv_ref[k_rows, pair_cols(2, pair)])
        mixed = mul_at(jnp.concatenate(probs, axis=0).astype(bf16), vals)
        att_ref[q_rows, pair_cols(0, pair)] = mixed.astype(bf16)
        for k in range(2):
            keep_sums(2 * pair + k, sums[k])


def text_front_kernel(
    x_ref, g1_ref, b1_ref, wqkv_ref, wo_ref, g2_ref, b2_ref, h1_ref, qkv_ref, att_ref, mid_ref,
    h2_ref, sum_ref, lse_ref
):
    rows, chunk = x_ref.shape[0], 128
    norm_rows(x_ref, h1_ref, line(g1_ref), line(b1_ref), chunk)

    @pl.loop(0, 3 * D // 256)
    def _(step):
        at = pl.ds(pl.multiple_of(step * 256, 256), 256)
        qkv_ref[:, at] = mul(h1_ref[...], wqkv_ref[:, at]).astype(bf16)

    mask = same_sequence(chunk, 0, chunk, 0, TXT_LEN)

    @pl.loop(0, rows // chunk)
    def _(step):
        at = pl.ds(pl.multiple_of(step * chunk, chunk), chunk)

        def keep_sums(head, value):
            lse_ref[pl.ds(step * 16 + head, 1), :] = value

        attend(qkv_ref, att_ref, at, at, mask, keep_sums)

    @pl.loop(0, D // 256)
    def _(step):
        at = pl.ds(pl.multiple_of(step * 256, 256), 256)
        mid_ref[:, at] = x_ref[:, at].astype(f32) + mul(att_ref[...], wo_ref[:, at])

    norm_rows(mid_ref, h2_ref, line(g2_ref), line(b2_ref), chunk)
    per = chunk // TXT_LEN

    @pl.loop(0, rows // chunk)
    def _(step):
        values = mid_ref[pl.ds(pl.multiple_of(step * chunk, chunk), chunk), :]
        sum_ref[pl.ds(pl.multiple_of(step * per, per), per), :] = jnp.sum(
            values.reshape(per, TXT_LEN, D), axis=1
        )


def text_front(rows_in, gain1, bias1, wqkv, wo, gain2, bias2):
    rows = rows_in.shape[0]
    shapes = [
        ((rows, D), bf16),
        ((rows, 3 * D), bf16),
        ((rows, D), bf16),
        ((rows, D), f32),
        ((rows, D), bf16),
        ((rows // TXT_LEN, D), f32),
        ((rows // 128 * 16, 128), f32),
    ]
    return pl.pallas_call(
        text_front_kernel,
        out_shape=[jax.ShapeDtypeStruct(*item) for item in shapes],
        compiler_params=params(),
        cost_estimate=cost(rows * D * D * 8, 14 * D * rows + 8 * D * D, rows * 128 * HEADS),
        name="text_front",
    )(rows_in, gain1, bias1, wqkv, wo, gain2, bias2)


def image_front_kernel(
    windows, x_ref, order_ref, g1_ref, b1_ref, g2_ref, b2_ref, *refs
):
    h2_ref, sum_ref, early_ref = refs[-10:-7]
    w_ref, h1_ref, placed_ref, qkv_ref, att_ref, mid_ref, sems = refs[-7:]
    rows, chunk = x_ref.shape[0], 80
    copies, row = [], 0
    for k, piece in enumerate(refs[:-10]):
        place = w_ref.at[pl.ds(row, piece.shape[0]), :]
        copies.append(pltpu.make_async_copy(piece, place, sems.at[k]))
        row += piece.shape[0]
    for copy in copies:
        copy.start()

    def place_columns(src, dst):
        @pl.loop(0, D // 256)
        def _(step):
            at = pl.ds(pl.multiple_of(step * 256, 256), 256)
            dst[:, at] = mul_bt(src[...], chosen(order_ref[at, :])).astype(bf16)

    norm_rows(x_ref, h1_ref, line(g1_ref), line(b1_ref), chunk)
    place_columns(h1_ref, placed_ref)
    for copy in copies:
        copy.wait()

    @pl.loop(0, 3 * D // 256)
    def _(step):
        at = pl.ds(pl.multiple_of(step * 256, 256), 256)
        qkv_ref[:, at] = mul(placed_ref[...], w_ref[:, at]).astype(bf16)

    for row0, count, key0, keys in windows:
        one = same_sequence(count, row0, keys, key0, IMG_LEN)
        mask = jnp.concatenate([one, one], axis=0)
        attend_along(qkv_ref, att_ref, pl.ds(row0, count), pl.ds(key0, keys), mask)
    place_columns(att_ref, placed_ref)

    @pl.loop(0, D // 256)
    def _(step):
        at = pl.ds(pl.multiple_of(step * 256, 256), 256)
        there = pl.ds(pl.multiple_of(step * 256 + 3 * D, 256), 256)
        mid_ref[:, at] = x_ref[:, at].astype(f32) + mul(placed_ref[...], w_ref[:, there])

    norm_rows(mid_ref, h2_ref, line(g2_ref), line(b2_ref), chunk)
    place_columns(h2_ref, placed_ref)
    pool = pool_matrix(rows // IMG_LEN, rows, 0, IMG_LEN)

    @pl.loop(0, EARLY // TILE)
    def _(step):
        at = pl.ds(pl.multiple_of(step * TILE, TILE), TILE)
        there = pl.ds(pl.multiple_of(step * TILE + 4 * D, TILE), TILE)
        value, _ = gelu_parts(mul(placed_ref[...], w_ref[:, there]))
        early_ref[:, at] = mul(pool, value.astype(bf16))

    for k in range(rows // IMG_LEN):
        first, last = k * IMG_LEN, (k + 1) * IMG_LEN
        start, end = first // 8 * 8, -(-last // 8) * 8
        values = mid_ref[start:end, :]
        place = lax.broadcasted_iota(jnp.int32, values.shape, 0) + start
        inside = (place >= first) & (place < last)
        sum_ref[k : k + 1, :] = jnp.sum(jnp.where(inside, values, 0.0), axis=0, keepdims=True)


def image_front(rows_in, pieces, source, gain1, bias1, gain2, bias2):
    rows = rows_in.shape[0]
    windows = ((0, 208, 0, 256), (208, 192, 192, 208))
    vmem = pl.BlockSpec(memory_space=pltpu.VMEM)
    return pl.pallas_call(
        functools.partial(image_front_kernel, windows),
        out_shape=[
            jax.ShapeDtypeStruct((rows, D), bf16),
            jax.ShapeDtypeStruct((rows // IMG_LEN, D), f32),
            jax.ShapeDtypeStruct((rows // IMG_LEN, EARLY), f32),
        ],
        in_specs=[vmem] * 6 + anywhere(pieces),
        out_specs=[vmem] * 3,
        scratch_shapes=[
            pltpu.VMEM((D, 4 * D + EARLY), bf16),
            pltpu.VMEM((rows, D), bf16),
            pltpu.VMEM((rows, D), bf16),
            pltpu.VMEM((rows, 3 * D), bf16),
            pltpu.VMEM((rows, D), bf16),
            pltpu.VMEM((rows, D), f32),
            pltpu.SemaphoreType.DMA((len(pieces),)),
        ],
        compiler_params=params(),
        cost_estimate=cost(rows * D * D * 12, 8 * D * D, rows * 256 * HEADS),
        name="image_front",
    )(rows_in, source, gain1, bias1, gain2, bias2, *pieces)


def gelu_parts(inner):
    half = 0.5 * (1.0 + lax.erf(inner * (0.5**0.5)))
    return inner * half, half


def pack_kernel(unit_ref, pos_ref, *refs):
    refs[-1][:, :D] = unit_ref[...].astype(bf16)
    refs[-1][:, D:] = pos_ref[...]


def packed(unit, positive, after):
    shape = (unit.shape[0], D + positive.shape[1])
    return pl.pallas_call(
        pack_kernel,
        out_shape=jax.ShapeDtypeStruct(shape, bf16),
        in_specs=[pl.BlockSpec(memory_space=pltpu.VMEM)] * 2 + anywhere(after),
        compiler_params=params(),
        cost_estimate=cost(shape[0] * shape[1], 4 * shape[0] * shape[1]),
        name="packed",
    )(unit, positive, *after)


def pool_matrix(count, rows, row0, seq_len):
    row = (lax.broadcasted_iota(jnp.int32, (count, rows), 1) + row0) // seq_len
    return jnp.where(row == lax.broadcasted_iota(jnp.int32, (count, rows), 0), 1.0, 0.0).astype(bf16)


def two_terms(mean):
    high = mean.astype(bf16)
    low = (mean - high.astype(f32)).astype(bf16)
    return jnp.concatenate([high, low], axis=0)


def unit_rows(pooled):
    inverse = lax.rsqrt(jnp.sum(pooled * pooled, axis=-1, keepdims=True) + norm_eps)
    return pooled * inverse, inverse


def text_up_kernel(h2_ref, wu_ref, wd_ref, sum_ref, *refs):
    slope_ref, hid_ref, unit_ref, inv_ref, acc = refs[-5:]
    step = pl.program_id(0)
    chunk = 320
    per = chunk // TXT_LEN
    pool = pool_matrix(per, chunk, 0, TXT_LEN)
    for k in range(h2_ref.shape[0] // chunk):
        inner = mul(h2_ref[k * chunk : (k + 1) * chunk, :], wu_ref[...])
        value, half = gelu_parts(inner)
        slope = half + inner * (jnp.exp(-0.5 * inner * inner) * 0.3989422804014327)
        slope_ref[k * chunk : (k + 1) * chunk, :] = slope.astype(bf16)
        hid_ref[k * per : (k + 1) * per, :] = mul(pool, value.astype(bf16))
    terms = mul(two_terms(hid_ref[...] * (1.0 / TXT_LEN)), wd_ref[...])
    count = hid_ref.shape[0]
    added = terms[:count] + terms[count:]

    @pl.when(step == 0)
    def _():
        acc[...] = sum_ref[...] * (1.0 / TXT_LEN) + added

    @pl.when(step > 0)
    def _():
        acc[...] += added

    @pl.when(step == pl.num_programs(0) - 1)
    def _():
        unit, inverse = unit_rows(acc[...])
        unit_ref[...] = unit
        inv_ref[...] = jnp.broadcast_to(inverse, inv_ref.shape)


def text_up(normed2, weight_up, weight_down, middle_sum, after=()):
    rows, count = normed2.shape[0], middle_sum.shape[0]
    fixed = lambda shape: pl.BlockSpec(shape, lambda i: (0, 0))
    return pl.pallas_call(
        text_up_kernel,
        grid=(FF // TILE,),
        out_shape=[
            jax.ShapeDtypeStruct((rows, FF), bf16),
            jax.ShapeDtypeStruct((count, FF), f32),
            jax.ShapeDtypeStruct((count, D), f32),
            jax.ShapeDtypeStruct((count, 128), f32),
        ],
        in_specs=[
            fixed((rows, D)),
            pl.BlockSpec((D, TILE), lambda i: (0, i)),
            pl.BlockSpec((TILE, D), lambda i: (i, 0)),
            fixed((count, D)),
        ]
        + anywhere(after),
        out_specs=[
            pl.BlockSpec((rows, TILE), lambda i: (0, i)),
            pl.BlockSpec((count, TILE), lambda i: (0, i)),
            fixed((count, D)),
            fixed((count, 128)),
        ],
        scratch_shapes=[pltpu.VMEM((count, D), f32)],
        compiler_params=params(),
        cost_estimate=cost(2 * rows * D * FF, 4 * D * FF + 2 * rows * FF, 20 * rows * FF),
        name="text_up",
    )(normed2, weight_up, weight_down, middle_sum, *after)


def image_up_kernel(fold, h2_ref, wu_ref, wd_ref, first_ref, sum_ref, early_ref, out_ref, acc, picked):
    step = pl.program_id(0)
    rows, count = h2_ref.shape[0], sum_ref.shape[0]
    part = TILE // fold

    def through_down(summed, groups):
        moved = mul(two_terms(summed * (1.0 / IMG_LEN)), picked[...]).astype(bf16)
        weight = jnp.concatenate([groups[:, k * D : (k + 1) * D] for k in range(fold)], axis=0)
        terms = mul(moved, weight)
        return terms[:count] + terms[count:]

    @pl.when(step == 0)
    def _():
        place = lax.broadcasted_iota(jnp.int32, (TILE, TILE), 0)
        col = lax.broadcasted_iota(jnp.int32, (TILE, TILE), 1)
        source = (col % part) * fold + col // part
        picked[...] = jnp.where(place == source, 1.0, 0.0).astype(bf16)
        total = sum_ref[...] * (1.0 / IMG_LEN)
        for k in range(EARLY // TILE):
            total = total + through_down(
                early_ref[:, k * TILE : (k + 1) * TILE], first_ref[k * part : (k + 1) * part, :]
            )
        acc[...] = total

    value, _ = gelu_parts(mul(h2_ref[...], wu_ref[...]))
    summed = mul(pool_matrix(count, rows, 0, IMG_LEN), value.astype(bf16))
    acc[...] += through_down(summed, wd_ref[...])

    @pl.when(step == pl.num_programs(0) - 1)
    def _():
        unit = unit_rows(acc[...])[0].astype(bf16)
        out_ref[...] = jnp.broadcast_to(unit[None], out_ref.shape)


def image_up(normed2, whole, middle_sum, early, peers):
    rows, count = normed2.shape[0], middle_sum.shape[0]
    fold = FF // D
    before, part = EARLY // TILE, TILE // fold
    fixed = lambda shape: pl.BlockSpec(shape, lambda i: (0, 0))
    return pl.pallas_call(
        functools.partial(image_up_kernel, fold),
        grid=(FF // TILE - before,),
        out_shape=jax.ShapeDtypeStruct((peers, count, D), bf16),
        in_specs=[
            fixed((rows, D)),
            pl.BlockSpec((D, TILE), lambda i: (0, FF // TILE + i)),
            pl.BlockSpec((part, FF), lambda i: (i + before, 0)),
            fixed((before * part, FF)),
            fixed((count, D)),
            fixed((count, EARLY)),
        ],
        out_specs=pl.BlockSpec((peers, count, D), lambda i: (0, 0, 0)),
        scratch_shapes=[pltpu.VMEM((count, D), f32), pltpu.VMEM((TILE, TILE), bf16)],
        compiler_params=params(),
        cost_estimate=cost(2 * rows * D * FF, 4 * D * FF, 15 * rows * FF),
        name="image_up",
    )(normed2, whole, whole, whole, middle_sum, early)


def left_kernel(count, *refs):
    out_ref = refs[-1]
    for k in range(count):
        source_ref, values_ref = refs[2 * k : 2 * k + 2]

        @pl.loop(0, D // 256)
        def _(step, k=k, source_ref=source_ref, values_ref=values_ref):
            at = pl.ds(pl.multiple_of(step * 256, 256), 256)
            picked = mul_bt(chosen(source_ref[at, :]), values_ref[...])
            out_ref[k, at, :] = picked.astype(bf16)


def left_factors(*pairs):
    rows = pairs[0][1].shape[0]
    given = [item for pair in pairs for item in pair]
    return pl.pallas_call(
        functools.partial(left_kernel, len(pairs)),
        out_shape=jax.ShapeDtypeStruct((len(pairs), D, rows), bf16),
        in_specs=in_vmem(len(given)),
        out_specs=pl.BlockSpec(memory_space=pltpu.VMEM),
        compiler_params=params(24 << 20),
        cost_estimate=cost(2 * len(pairs) * rows * D * D, 4 * len(pairs) * rows * D),
        name="left_factors",
    )(*given)


def loss_parts(text_rows, pos, image_all):
    similar = mul_bt(text_rows, image_all) * logit_scale
    shifted = jnp.exp(similar - logit_scale)
    alive = jnp.max(pos, axis=1, keepdims=True)
    row_sum = jnp.sum(shifted, axis=1, keepdims=True)
    row_count = jnp.maximum(jnp.sum(pos, axis=1, keepdims=True), 1.0)
    return similar, shifted, alive, row_sum, row_count


def sums_over_captions(text_rows, pos, image_all):
    similar, shifted, alive, row_sum, row_count = loss_parts(text_rows, pos, image_all)
    pos_similar = pos * similar
    cap_term = alive * (
        logit_scale + jnp.log(row_sum) - jnp.sum(pos_similar, axis=1, keepdims=True) / row_count
    )
    return (
        jnp.sum(alive * shifted, axis=0, keepdims=True),
        jnp.sum(pos, axis=0, keepdims=True),
        jnp.sum(pos_similar, axis=0, keepdims=True),
        jnp.sum(cap_term, axis=0, keepdims=True),
        jnp.sum(alive, axis=0, keepdims=True),
    )


def loss_from(sums):
    col_sum, col_count, col_pos, cap_total, live_total = sums
    img_term = logit_scale + jnp.log(col_sum) - col_pos / col_count
    return 0.5 * cap_total / live_total + 0.5 * jnp.mean(img_term, axis=1, keepdims=True)


def grad_of_unit(text_rows, pos, image_all, col_sum, col_count, live_total):
    _, shifted, alive, row_sum, row_count = loss_parts(text_rows, pos, image_all)
    cap_share, img_share = 0.5 / live_total, 0.5 / image_all.shape[0]
    grad_sims = alive * shifted * (cap_share / row_sum + img_share / col_sum) - pos * (
        cap_share / row_count + img_share / col_count
    )
    return mul(grad_sims.astype(bf16), image_all) * logit_scale


def turned(grad, unit):
    return grad - unit * jnp.sum(grad * unit, axis=-1, keepdims=True)


def loss_into(
    pack_ref, image_ref, own_ref, unit_ref, inv_ref, loss_ref, row_ref, low_ref, col_sum_ref,
    col_count_ref, live_ref
):
    image_all = image_ref[...]
    chunk = 256
    total = None
    for k in range(pack_ref.shape[0] // chunk):
        at = slice(k * chunk, (k + 1) * chunk)
        part = sums_over_captions(pack_ref[at, :D], pack_ref[at, D:].astype(f32), image_all)
        total = part if total is None else [a + b for a, b in zip(total, part)]
    loss_ref[...] = jnp.broadcast_to(loss_from(total), loss_ref.shape)
    col_sum, col_count, _, _, live_total = total
    col_sum_ref[...] = col_sum
    col_count_ref[...] = col_count
    live_ref[...] = jnp.broadcast_to(live_total, live_ref.shape)
    grad = grad_of_unit(
        own_ref[:, :D], own_ref[:, D:].astype(f32), image_all, col_sum, col_count, live_total
    )
    row = inv_ref[:, :1] * turned(grad, unit_ref[...]) * (1.0 / TXT_LEN)
    row_ref[...] = row
    low_ref[...] = row.astype(bf16)


def down_kernel(pack_ref, image_ref, col_sum_ref, col_count_ref, live_ref, hid_ref, *refs):
    step, out_ref = pl.program_id(0), refs[-1]
    text_rows = pack_ref[:, :D]
    grad = grad_of_unit(
        text_rows, pack_ref[:, D:].astype(f32), image_ref[...], col_sum_ref[...],
        col_count_ref[...], live_ref[:, :1]
    )
    rows = (turned(grad, text_rows.astype(f32)) * (1.0 / TXT_LEN)).astype(bf16)
    part = mul_at(hid_ref[...], rows)

    @pl.when(step == 0)
    def _():
        out_ref[...] = part

    @pl.when(step > 0)
    def _():
        out_ref[...] += part


def grad_of_down(pack, image_all, col_sum, col_count, live_total, hidden_cols, after):
    images, chunk = image_all.shape[0], 256
    fixed = lambda shape: pl.BlockSpec(shape, lambda i: (0, 0))
    per = hidden_cols.shape[1]
    return pl.pallas_call(
        down_kernel,
        grid=(pack.shape[0] // chunk,),
        out_shape=jax.ShapeDtypeStruct((per, D), f32),
        in_specs=[
            pl.BlockSpec((chunk, pack.shape[1]), lambda i: (i, 0)),
            fixed((images, D)), fixed((1, images)), fixed((1, images)), fixed((1, 128)),
            pl.BlockSpec((chunk, per), lambda i: (i, 0)),
        ]
        + anywhere(after),
        out_specs=fixed((per, D)),
        compiler_params=params(16 << 20),
        cost_estimate=cost(4 * pack.shape[0] * images * D, 2 * pack.size, pack.shape[0] * images),
        name="grad_of_down",
    )(pack, image_all, col_sum, col_count, live_total, hidden_cols, *after)


def load_kernel(*refs):
    count = (len(refs) - 1) // 2
    sems = refs[-1]
    copies = [
        pltpu.make_async_copy(refs[k], refs[count + k], sems.at[k]) for k in range(count)
    ]
    for copy in copies:
        copy.start()
    for copy in copies:
        copy.wait()


def loaded(*arrays):
    return pl.pallas_call(
        load_kernel,
        out_shape=[stays(array.shape, array.dtype) for array in arrays],
        in_specs=[pl.BlockSpec(memory_space=pltpu.HBM)] * len(arrays),
        out_specs=in_vmem(len(arrays)),
        scratch_shapes=[pltpu.SemaphoreType.DMA((len(arrays),))],
        compiler_params=params(4 << 20),
        cost_estimate=cost(0, sum(2 * array.size * array.dtype.itemsize for array in arrays)),
        name="loaded",
    )(*in_hbm(*arrays))


def mlp_back_kernel(with_loss, gain_ref, *refs):
    given, refs = (refs[:5], refs[5:]) if with_loss else (refs[:2], refs[2:])
    wd_ref, slope_ref, wu_ref, lhs_ref, mid_ref = refs[:5]
    keep_a, send_a, keep_b, send_b, out_ref, sums_out = refs[5:11]
    low_ref, row_ref = refs[-2:] if with_loss else given
    count, rows = low_ref.shape[0], out_ref.shape[0]
    half, steps = D // 2, FF // 2 // TILE
    if with_loss:
        loss_ref, *stats = refs[11:15]
        loss_into(*given, loss_ref, row_ref, low_ref, *stats)
    for k, (keep, send) in enumerate(((keep_a, send_a), (keep_b, send_b))):

        @pl.loop(0, steps)
        def _(step, k=k, keep=keep, send=send):
            at = pl.ds(pl.multiple_of(k * (FF // 2) + step * TILE, TILE), TILE)
            there = pl.ds(pl.multiple_of(step * TILE, TILE), TILE)
            hidden = mul_bt(low_ref[...], wd_ref[at, :])
            wide = jnp.broadcast_to(hidden[:, None, :], (count, TXT_LEN, TILE))
            inner = (wide.reshape(rows, TILE) * slope_ref[:, at].astype(f32)).astype(bf16)
            weight = mul(lhs_ref[k], inner).astype(bf16)
            keep[:, there] = weight[:half]
            send[:, there] = weight[half:]
            added = mul_bt(inner, wu_ref[:, at])
            if k == 0:

                @pl.when(step == 0)
                def _():
                    out_ref[...] = added

                @pl.when(step > 0)
                def _():
                    out_ref[...] += added
            else:
                out_ref[...] += added

    chunk = 128
    per = chunk // TXT_LEN
    gain = line(gain_ref)
    sums_out[...] = jnp.zeros_like(sums_out)

    @pl.loop(0, rows // chunk)
    def _(k):
        at = pl.ds(pl.multiple_of(k * chunk, chunk), chunk)
        unit, scale = norm_parts(mid_ref[at, :])
        grad = out_ref[at, :]
        sums_out[:, :D] += jnp.sum(grad * unit, axis=0, keepdims=True)
        sums_out[:, D:] += jnp.sum(grad, axis=0, keepdims=True)
        row = row_ref[pl.ds(pl.multiple_of(k * per, per), per), :]
        row = jnp.broadcast_to(row[:, None, :], (per, TXT_LEN, D)).reshape(chunk, D)
        out_ref[at, :] = row + norm_back(unit, scale, gain, grad)


def mlp_back(given, weight_down, slope, weight_up, lhs, middle, gain):
    rows, count = slope.shape[0], given[-2].shape[0]
    with_loss = len(given) == 5
    shapes = [stays((D // 2, FF // 2), bf16)] * 4 + [stays((rows, D), f32), stays((1, 2 * D), f32)]
    scratch = []
    if with_loss:
        images = given[1].shape[0]
        wide = [(1, 128), (1, images), (1, images), (1, 128)]
        shapes += [jax.ShapeDtypeStruct(shape, f32) for shape in wide]
        scratch = [pltpu.VMEM((count, D), bf16), pltpu.VMEM((count, D), f32)]
    return pl.pallas_call(
        functools.partial(mlp_back_kernel, with_loss),
        out_shape=shapes,
        in_specs=in_vmem(6 + len(given)),
        out_specs=in_vmem(len(shapes)),
        scratch_shapes=scratch,
        compiler_params=params(16 << 20),
        cost_estimate=cost(4 * rows * D * FF, 4 * D * FF + 2 * rows * FF + 2 * D * FF, rows * FF),
        name="mlp_back",
    )(gain, *given, weight_down, slope, weight_up, lhs, middle)


def attention_back_kernel(first, grad_ref, wo_ref, qkv_ref, lse_ref, *refs):
    low_ref, out_ref = refs[-2:]
    chunk = 128
    mask = same_sequence(chunk, 0, chunk, 0, TXT_LEN)

    @pl.loop(0, low_ref.shape[0] // chunk)
    def _(step):
        here = pl.ds(pl.multiple_of((first + step) * chunk, chunk), chunk)
        there = pl.ds(pl.multiple_of(step * chunk, chunk), chunk)
        sums = lse_ref[pl.ds(pl.multiple_of((first + step) * 16, 16), 16), :]
        low = grad_ref[here, :].astype(bf16)
        low_ref[there, :] = low
        grad_att = mul_bt(low, wo_ref[...]).astype(bf16)
        for pair in range(HEADS // 2):
            queries = qkv_ref[here, pair_cols(0, pair)] * bf16(HEAD ** (-0.5))
            keys = two_heads(qkv_ref[here, pair_cols(1, pair)])
            vals = two_heads(qkv_ref[here, pair_cols(2, pair)])
            grads = grad_att[:, pair_cols(0, pair)]
            scores, grad_probs = mul_bt(keys, queries), mul_bt(vals, grads)
            probs, grad_scores = [], []
            for k in range(2):
                at = slice(k * chunk, (k + 1) * chunk)
                head = 2 * pair + k
                shifted = scores[at] - sums[head : head + 1, :]
                prob = jnp.where(mask, jnp.exp(jnp.where(mask, shifted, 0.0)), 0.0)
                along = jnp.sum(grad_probs[at] * prob, axis=0, keepdims=True)
                grad_scores.append((prob * (grad_probs[at] - along)).astype(bf16))
                probs.append(prob.astype(bf16))
            grad_q = mul_at(jnp.concatenate(grad_scores, axis=0), keys) * HEAD ** (-0.5)
            grad_k = mul(jnp.concatenate(grad_scores, axis=1), two_heads(queries))
            grad_v = mul(jnp.concatenate(probs, axis=1), two_heads(grads))
            out_ref[there, pair_cols(0, pair)] = grad_q.astype(bf16)
            out_ref[there, pair_cols(1, pair)] = grad_k.astype(bf16)
            out_ref[there, pair_cols(2, pair)] = grad_v.astype(bf16)


def attention_back(grad_middle, weight_out, project, log_sums, first, count, after=()):
    rows = count * 128
    return pl.pallas_call(
        functools.partial(attention_back_kernel, first),
        out_shape=[stays((rows, D), bf16), stays((rows, 3 * D), bf16)],
        in_specs=in_vmem(4) + anywhere(after),
        out_specs=in_vmem(2),
        compiler_params=params(16 << 20),
        cost_estimate=cost(10 * rows * D * D, 16 * rows * D + 2 * D * D, rows * 128 * HEADS),
        name="attention_back",
    )(grad_middle, weight_out, project, log_sums, *after)


def mul_rows(lhs, parts, cols):
    total, row = 0.0, 0
    for part in parts:
        total = total + mul(lhs[:, row : row + part.shape[0]], part[:, cols])
        row += part.shape[0]
    return total


def weight_back_kernel(factors, groups, lhs_ref, *refs):
    keep_a, send_a, keep_b, send_b = refs[-4:]
    half = D // 2
    for k, (factor, group, col) in enumerate(factors):
        parts = refs[sum(groups[:group]) : sum(groups[: group + 1])]
        weight = mul_rows(lhs_ref.at[factor], parts, slice(col * D, (col + 1) * D)).astype(bf16)
        at = slice(k % 2 * D, (k % 2 + 1) * D)
        (keep_b if k > 1 else keep_a)[:, at] = weight[:half]
        (send_b if k > 1 else send_a)[:, at] = weight[half:]


def weight_back(lhs, groups, factors, after=()):
    rows = lhs.shape[2]
    given = [part for group in groups for part in group]
    return pl.pallas_call(
        functools.partial(weight_back_kernel, factors, [len(group) for group in groups]),
        out_shape=[stays((D // 2, 2 * D), bf16)] * 4,
        in_specs=in_vmem(1 + len(given)) + anywhere(after),
        out_specs=in_vmem(4),
        compiler_params=params(16 << 20),
        cost_estimate=cost(8 * rows * D * D, 8 * rows * D + 14 * D * D),
        name="weight_back",
    )(lhs, *given, *after)


def input_back_kernel(count, *refs):
    projs = refs[:count]
    w_ref, x_ref, gain_ref, mid_ref, sums_ref = refs[count : count + 5]
    out_ref, sums_out = refs[-2:]
    rows, chunk = x_ref.shape[0], 128

    @pl.loop(0, D // 256)
    def _(step):
        at = pl.ds(pl.multiple_of(step * 256, 256), 256)
        row = 0
        for part in projs:
            there = slice(row, row + part.shape[0])
            out_ref[there, at] = mul_bt(part[...], w_ref[at, :])
            row += part.shape[0]

    gain = line(gain_ref)
    sums_out[...] = jnp.zeros_like(sums_out)
    sums_out[1:2, :] = sums_ref[...]

    @pl.loop(0, rows // chunk)
    def _(k):
        at = pl.ds(pl.multiple_of(k * chunk, chunk), chunk)
        unit, scale = norm_parts(x_ref[at, :].astype(f32))
        grad = out_ref[at, :]
        sums_out[0:1, :D] += jnp.sum(grad * unit, axis=0, keepdims=True)
        sums_out[0:1, D:] += jnp.sum(grad, axis=0, keepdims=True)
        out_ref[at, :] = mid_ref[at, :] + norm_back(unit, scale, gain, grad)


def input_back(grad_projs, weight, rows_in, gain, grad_middle, sums, after=()):
    rows = rows_in.shape[0]
    return pl.pallas_call(
        functools.partial(input_back_kernel, len(grad_projs)),
        out_shape=[jax.ShapeDtypeStruct((rows, D), f32), stays((8, 2 * D), f32)],
        in_specs=in_vmem(len(grad_projs) + 5) + anywhere(after),
        out_specs=in_vmem(2),
        compiler_params=params(16 << 20),
        cost_estimate=cost(6 * rows * D * D, 14 * rows * D + 6 * D * D),
        name="input_back",
    )(*grad_projs, weight, rows_in, gain, grad_middle, sums, *after)


def local(
    images,
    captions,
    img_gain1,
    img_bias1,
    img_qkv,
    img_out,
    img_gain2,
    img_bias2,
    img_up,
    img_down,
    txt_gain1,
    txt_bias1,
    txt_qkv,
    txt_out,
    txt_gain2,
    txt_bias2,
    txt_up,
    txt_down,
    counts,
    matches,
):
    peers = lax.axis_size(AXIS)
    own = lax.axis_index(AXIS)
    per = D // peers
    img_local = counts.shape[0]
    cap_local = matches.shape[0]
    total_images = matches.shape[1]

    up_rows = img_up.reshape(per, FF)
    whole = lax.all_gather(
        jnp.concatenate([img_down.reshape(per, FF), up_rows[:, EARLY:]], axis=1),
        AXIS,
        axis=0,
        tiled=True,
    )
    small = peers == 32
    shard = jnp.concatenate(
        [img_qkv.reshape(per, 3 * D), img_out.reshape(per, D), up_rows[:, :EARLY]], axis=1
    )
    if small:
        line, source = gathered_line(shard), row_order((1, 4, 2, 16, 8))
    else:
        line, source = lax.all_gather(shard, AXIS, axis=0, tiled=True), row_order(())

    normed1, project, attended, middle, normed2, middle_sum, log_sums = text_front(
        captions, txt_gain1, txt_bias1, txt_qkv, txt_out, txt_gain2, txt_bias2
    )
    middle_sum, line = in_turn(middle_sum, line)
    beside, above = (swapped(line, 2), swapped(line, 4)) if small else (line, line)
    slope, hidden_sum, text_unit, inverse = text_up(
        normed2, txt_up, txt_down, middle_sum, (line,)
    )
    text_unit, normed2, beside, above = lax.optimization_barrier(
        (text_unit, normed2, beside, above)
    )

    ends_at = jnp.cumsum(counts)
    slot_ids = lax.iota(jnp.int32, cap_local)
    owner = jnp.sum((ends_at[None, :] <= slot_ids[:, None]).astype(jnp.int32), axis=1)
    owner = owner + own * img_local
    live = slot_ids < ends_at[-1]
    columns = lax.iota(jnp.int32, total_images)
    positive = ((matches > 0) | (owner[:, None] == columns[None, :])) & live[:, None]

    order_a, order_b, tail = stage_orders()
    source_a, source_b = row_order(order_a + tail[::-1]), row_order(order_b + tail[::-1])
    own_pack = packed(text_unit, positive.astype(bf16), ())
    lhs_up = left_factors((source_a, normed2), (source_b, normed2))
    pieces = [line]
    if small:
        first, second = diagonal(beside, above)
        own_pack, first, second, lhs_up = lax.optimization_barrier(
            (own_pack, first, second, lhs_up)
        )
        held = own_pack[None]
        others = [swapped(held, mask) for mask in (8, 16, 24)]
        pieces = [line, beside, above, first, second]
        pieces = pieces + [swapped(piece, 1) for piece in pieces]

    normed_img, middle_img, early = image_front(
        images, pieces, source, img_gain1, img_bias1, img_gain2, img_bias2
    )
    if small:
        scaled_sum = (hidden_sum * inverse[:, :1]).astype(bf16)
        normed_img, scaled_sum, others = lax.optimization_barrier((normed_img, scaled_sum, others))
        held = joined(joined(held, others[0], 8), joined(others[1], others[2], 8), 16, 1)
        text_beside, text_above = swapped(held, 2), swapped(held, 4)
        hidden_cols = lax.all_to_all(scaled_sum, AXIS, split_axis=1, concat_axis=0, tiled=True)
        normed_img, text_beside, text_above = lax.optimization_barrier(
            (normed_img, text_beside, text_above)
        )
        halves = diagonal(text_beside, text_above)
    image_low = image_up(normed_img, whole, middle_img, early, peers)
    if small:
        image_low, halves, hidden_cols = lax.optimization_barrier((image_low, halves, hidden_cols))
        across = jnp.concatenate(halves, axis=0)
        held = joined(joined(held, text_beside, 2), joined(text_above, across, 2), 4, 4)
        other, slope = in_turn(swapped(held, 1), slope)
        heavy = loaded(txt_down, slope, txt_up, lhs_up, middle)
        other, heavy = in_turn(other, heavy)
        text_pack = joined(held, other, 1).reshape(-1, D + total_images)
    image_all = exchanged(image_low).reshape(total_images, D)
    if small:
        image_all, text_pack = in_turn(image_all, text_pack)

    if small:
        given = (text_pack, image_all, own_pack, text_unit, inverse)
    else:
        text_low, pos = own_pack[:, :D], own_pack[:, D:].astype(f32)
        totals = lax.psum(sums_over_captions(text_low, pos, image_all), AXIS)
        loss_value = loss_from(totals)
        grad = grad_of_unit(text_low, pos, image_all, totals[0], totals[1], totals[4])
        grad_row = inverse[:, :1] * turned(grad, text_unit) * (1.0 / TXT_LEN)
        row_low = grad_row.astype(bf16)
        given = (row_low, grad_row)
        heavy = (txt_down, slope, txt_up, lhs_up, middle)

    *up, grad_middle, sums = mlp_back(given, *heavy, txt_gain2)
    if small:
        *up, grad_middle, sums, loss_value, col_sum, col_count, live_total = (
            *up, grad_middle, sums
        )
    stages = len(order_a)
    low_one, proj_one = attention_back(grad_middle, txt_out, project, log_sums, 0, 2)
    for stage in range(stages - 2):
        up = fold(hand_on(up, stage), (proj_one,))
    low_two, proj_two = attention_back(grad_middle, txt_out, project, log_sums, 2, 3, up)
    proj_two, normed1 = in_turn(proj_two, normed1)
    lhs_rest = left_factors((source_a, normed1), (source_b, normed1), (source_b, attended))
    up = fold(hand_on(up, stages - 2), (proj_two, lhs_rest))
    projs, lows = (proj_one, proj_two), (low_one, low_two)
    rest = weight_back(lhs_rest, [projs, lows], [(0, 0, 0), (0, 0, 1), (1, 0, 2), (2, 1, 0)], up)
    up = hand_on(up, stages - 1)
    caption_grad, sums = input_back(
        projs, txt_qkv, captions, txt_gain1, grad_middle, sums, rest[:1]
    )
    caption_grad, up = in_turn(caption_grad, up)
    up = fold_last(up)
    if small:
        *rest, sums = fold(hand_on(rest, 0), up[:1], (sums, swapped(sums, 1)))
    else:
        norms = lax.psum(sums, AXIS)[:2].reshape(-1)
        for stage in range(stages - 2):
            rest = fold(hand_on(rest, stage), up[:1])
    up = hand_on_last(up)
    rest = hand_on(rest, stages - 2)
    if small:
        grad_down = grad_of_down(
            text_pack, image_all, col_sum, col_count, live_total, hidden_cols, (caption_grad,)
        )
    else:
        grad_down = lax.psum_scatter(
            mul_at(hidden_sum.astype(bf16), row_low), AXIS, scatter_dimension=0, tiled=True
        )
    grad_down, rest, up = lax.optimization_barrier((grad_down, rest, up))
    if small:
        *rest, sums = fold(rest, (), (sums,))
        rest = fold_last(hand_on(rest, stages - 1), (), (sums,))
    else:
        rest = fold_last(hand_on(fold(rest), stages - 1))
    up_share = sum_last(*up)
    rest_share = sum_last(*hand_on_last(rest))
    if small:
        norms = rest_share[per]
        rest_share = rest_share[:per]
    return (
        loss_value[0, 0],
        caption_grad,
        norms[:D],
        norms[D : 2 * D],
        rest_share[:, : 3 * D].reshape(-1),
        rest_share[:, 3 * D :].reshape(-1),
        norms[2 * D : 3 * D],
        norms[3 * D :],
        up_share.reshape(-1),
        grad_down.reshape(-1),
    )


def solution(mesh):
    split, flat, whole = P("blk", None), P("blk"), P()
    image_block = (whole, whole, flat, flat, whole, whole, flat, flat)
    return jax.shard_map(
        local,
        mesh=mesh,
        in_specs=(split, split) + image_block + (whole,) * 8 + (flat, split),
        out_specs=(whole, split, whole, whole, flat, flat, whole, whole, flat, flat),
        check_vma=False,
    )
```
